32 devices in a mesh: seq: 8 (over z, y), mp: 4 (over x, core).
Axes of the slice: x: 2, y: 2, z: 4, core: 2. Of those that a mesh axis runs over, the one named last changes fastest.
Arguments:
- tokens: bfloat16 [2, 2048, 2048], P(None, 'seq'), may hold values from -6 to 6
- lengths: int32 [2, 3], replicated, may hold values from 1 to 2046, as said below
- norm1_gain: float32 [2048], replicated, may hold values from 0.5 to 1.5
- q_down: bfloat16 [2048, 1024], P(None, 'mp'), may hold values from -0.125 to 0.125
- latent_gain: float32 [1024], replicated, may hold values from 0.5 to 1.5
- q_up: bfloat16 [1024, 4096], P(None, 'mp'), may hold values from -0.25 to 0.25
- kv_proj: bfloat16 [2048, 512], replicated, may hold values from -0.125 to 0.125
- out_proj: bfloat16 [4096, 2048], P('mp'), may hold values from -0.75 to 0.75
- norm2_gain: float32 [2048], replicated, may hold values from 0.5 to 1.5
- w_gate: bfloat16 [2048, 5632], P(None, 'mp'), may hold values from -0.125 to 0.125
- w_up: bfloat16 [2048, 5632], P(None, 'mp'), may hold values from -0.125 to 0.125
- w_down: bfloat16 [5632, 2048], P('mp'), may hold values from -0.078125 to 0.078125
- cotangent: bfloat16 [2, 2048, 2048], P(None, 'seq'), may hold values from -6 to 6
Outputs:
- layer_out: bfloat16 [2, 2048, 2048], P(None, 'seq')
- grad_tokens: bfloat16 [2, 2048, 2048], P(None, 'seq')
- grad_norm1_gain: float32 [2048], P('seq')
- grad_q_down: float32 [2048, 1024], P('seq', 'mp')
- grad_latent_gain: float32 [1024], P('seq')
- grad_q_up: float32 [1024, 4096], P('seq', 'mp')
- grad_kv_proj: float32 [2048, 512], P(('seq', 'mp'))
- grad_out_proj: float32 [4096, 2048], P('mp', 'seq')
- grad_norm2_gain: float32 [2048], P('seq')
- grad_w_gate: float32 [2048, 5632], P('seq', 'mp')
- grad_w_up: float32 [2048, 5632], P('seq', 'mp')
- grad_w_down: float32 [5632, 2048], P('mp', 'seq')
The draws below stay inside these ranges and needn't reach their ends.
Inputs may be any that keep to these rules, and one draw needn't show every extreme that they name: Row m holds the lengths of the three sequences of micro-batch m in order, summing to 2048; the first and the last are shorter than 256. In one micro-batch the first and the last both have length 1.
All inputs are finite; a program needn't handle non-finite values.
Results may differ from the reference program's by a relative error of at most 0.025.
Values may be sent and summed in bfloat16 or wider, within the bound.
A program may use at most 256 MiB of HBM per device.

```python
import math
import jax
import jax.numpy as jnp
from jax import lax

D = 2048
RANK = 1024
HEADS = 16
HDIM = 256
FF = 5632
TOK_MB = 256
MICRO = 2
MB_TOK = 2048


def draw_lengths(key, part):
    key = jax.random.fold_in(key, 7)
    first_key, last_key, pick_key = jax.random.split(key, 3)
    first = jax.random.randint(first_key, (MICRO,), 1, TOK_MB)
    last = jax.random.randint(last_key, (MICRO,), 1, TOK_MB)
    chosen = jax.random.randint(pick_key, (), 0, MICRO)
    marked = jnp.arange(MICRO, dtype=jnp.int32) == chosen
    first = jnp.where(marked, 1, first)
    last = jnp.where(marked, 1, last)
    middle = MB_TOK - first - last
    return jnp.stack([first, middle, last], axis=1).astype(jnp.int32)


def levels(stream_key, shape, pieces, low, high):
    gain, own = 1.0, jax.random.fold_in(stream_key, 6)
    for dim, blocks in pieces:
        draws = jnp.exp(jax.random.uniform(jax.random.fold_in(own, dim), (blocks,), jnp.float32, low / len(pieces), high / len(pieces)))
        gain = gain * jnp.repeat(draws, shape[dim] // blocks).reshape([-1 if axis == dim else 1 for axis in range(len(shape))])
    return gain


def centred(stream_key, extent, spread, bound, cuts=(), held_as=jnp.bfloat16):
    array = jax.random.normal(stream_key, extent, jnp.float32) * spread
    if len(cuts) > 0:
        array = levels(stream_key, extent, cuts, -0.22, 0.18) * array
    return jnp.clip(array, min=-bound, max=bound).astype(held_as)


def setup_inputs(seed: int = 0) -> dict:
    key_list = jax.random.split(jax.random.key(seed), 14)
    return {
        "tokens": centred(key_list[0], (MICRO, MB_TOK, D), 1.0, 6.0, ((1, 8),)),
        "lengths": draw_lengths(jax.random.fold_in(key_list[13], 71), 0),
        "norm1_gain": jnp.clip(1.0 + 0.1 * jax.random.normal(key_list[2], (D,), jnp.float32), 0.5, 1.5),
        "q_down": centred(key_list[3], (D, RANK), D ** -0.5, 0.125, ((1, 4),)),
        "latent_gain": jnp.clip(1.0 + 0.1 * jax.random.normal(key_list[4], (RANK,), jnp.float32), 0.5, 1.5),
        "q_up": centred(key_list[5], (RANK, HEADS * HDIM), (RANK // 2) ** -0.5, 0.25, ((1, 4),)),
        "kv_proj": centred(key_list[6], (D, 2 * HDIM), D ** -0.5, 0.125),
        "out_proj": centred(key_list[7], (HEADS * HDIM, D), (HEADS * HDIM // 64) ** -0.5, 0.75, ((0, 4),)),
        "norm2_gain": jnp.clip(1.0 + 0.1 * jax.random.normal(key_list[8], (D,), jnp.float32), 0.5, 1.5),
        "w_gate": centred(key_list[9], (D, FF), D ** -0.5, 0.125, ((1, 4),)),
        "w_up": centred(key_list[10], (D, FF), D ** -0.5, 0.125, ((1, 4),)),
        "w_down": centred(key_list[11], (FF, D), FF ** -0.5, 0.078125, ((0, 4),)),
        "cotangent": centred(key_list[12], (MICRO, MB_TOK, D), 1.0, 6.0, ((1, 8),)),
    }


EPS = 1e-06
BASE = 10000.0
NEG_LARGE = -1e+30

@jax.custom_vjp
def low(v):
    return lax.optimization_barrier(v.astype(jnp.bfloat16)).astype(jnp.float32)

@jax.custom_vjp
def low_back(v):
    return v

def low_keep(v):
    return (low(v), None)

def low_pass(kept, grad):
    return (grad,)

def back_keep(v):
    return (v, None)

def back_low(kept, grad):
    return (low(grad),)
low.defvjp(low_keep, low_pass)
low_back.defvjp(back_keep, back_low)

def normalize(values):
    return values * lax.rsqrt(lax.optimization_barrier(jnp.mean(values * values, axis=-1, keepdims=True)) + EPS)

def matmul(left, right):
    return jnp.dot(left, right, precision=lax.Precision.HIGHEST)

def documents(lengths_row, rows):
    first_end = lengths_row[0]
    second_end = first_end + lengths_row[1]
    doc_ids = (rows >= first_end).astype(jnp.int32) + (rows >= second_end).astype(jnp.int32)
    starts = jnp.where(rows >= second_end, second_end, jnp.where(rows >= first_end, first_end, 0))
    return (doc_ids, rows - starts)

def rotation(positions, head_dim):
    half = head_dim // 2
    freqs = BASE ** (-2.0 * jnp.arange(half, dtype=jnp.float32) / head_dim)
    angles = positions.astype(jnp.float32)[:, None] * freqs[None, :]
    return (jnp.cos(angles), jnp.sin(angles))

def rotate(values, cosine, sine):
    half = values.shape[-1] // 2
    first = values[..., :half]
    second = values[..., half:]
    return jnp.concatenate([first * cosine - second * sine, second * cosine + first * sine], axis=-1)

def micro_layer(inputs, lengths_row, params):
    norm1_gain, q_down, latent_gain, q_up, kv_proj, out_proj, norm2_gain, w_gate, w_up, w_down = params
    positions = jnp.arange(MB_TOK, dtype=jnp.int32)
    doc_ids, places = documents(lengths_row, positions)
    cosine, sine = rotation(places, HDIM)
    first_in = low(normalize(inputs) * norm1_gain)
    latent = low_back(low(matmul(first_in, q_down)))
    latent_in = low(normalize(latent) * latent_gain)
    query_pre = low_back(matmul(latent_in, q_up)).reshape(MB_TOK, HEADS, HDIM)
    queries = low(rotate(query_pre, cosine[:, None, :], sine[:, None, :]))
    key_value = matmul(first_in, kv_proj)
    keys = low(rotate(low_back(key_value[:, :HDIM]), cosine, sine))
    values = low_back(low(key_value[:, HDIM:]))
    block = math.gcd(MB_TOK, 512)
    scale = HDIM ** (-0.5)

    def attend(block_index):
        start = block_index * block
        query_block = lax.dynamic_slice_in_dim(queries, start, block, 0)
        query_rows = start + jnp.arange(block, dtype=jnp.int32)
        query_docs = lax.dynamic_slice_in_dim(doc_ids, start, block, 0)
        scores = low_back(jnp.einsum('thd,nd->thn', query_block, keys, precision=lax.Precision.HIGHEST) * scale)
        visible = (doc_ids[None, :] == query_docs[:, None]) & (positions[None, :] <= query_rows[:, None])
        probs = low(jax.nn.softmax(jnp.where(visible[:, None, :], scores, NEG_LARGE), axis=-1))
        return jnp.einsum('thn,nd->thd', probs, values, precision=lax.Precision.HIGHEST)
    attended = lax.map(jax.checkpoint(attend), jnp.arange(MB_TOK // block, dtype=jnp.int32))
    attn_out = low_back(low(attended.reshape(MB_TOK, HEADS * HDIM)))
    middle = inputs + low_back(matmul(attn_out, out_proj))
    second_in = low(normalize(middle) * norm2_gain)
    gate_pre = low_back(matmul(second_in, w_gate))
    up_pre = low_back(matmul(second_in, w_up))
    hidden = low(jax.nn.silu(gate_pre) * up_pre)
    return middle + matmul(hidden, w_down)

def reference(tokens, lengths, norm1_gain, q_down, latent_gain, q_up, kv_proj, out_proj, norm2_gain, w_gate, w_up, w_down, cotangent):
    inputs = tokens.astype(jnp.float32)
    params = tuple((p.astype(jnp.float32) for p in (norm1_gain, q_down, latent_gain, q_up, kv_proj, out_proj, norm2_gain, w_gate, w_up, w_down)))

    def whole(inputs_all, *weights):
        results = [micro_layer(inputs_all[index], lengths[index], weights) for index in range(MICRO)]
        return jnp.stack(results, axis=0)
    outputs, backward = jax.vjp(whole, inputs, *params)
    grads = backward(cotangent.astype(jnp.float32))
    return (outputs.astype(jnp.bfloat16), grads[0].astype(jnp.bfloat16), grads[1], grads[2], grads[3], grads[4], grads[5], grads[6], grads[7], grads[8], grads[9], grads[10])
```

```python
import jax
import jax.numpy as jnp
from jax import lax
from jax.sharding import PartitionSpec as P

EPS = 1e-06
BASE = 10000.0
NEG_LARGE = -1e30
LOW = jnp.bfloat16
F32 = jnp.float32
ORDER = (0, 2, 1, 3)
CORE = [(i, i ^ 1) for i in range(4)]
CROSS = [(i, i ^ 2) for i in range(4)]


def inverse_rms(values):
    return lax.rsqrt(jnp.mean(values * values, axis=-1, keepdims=True) + EPS)


def norm_backward(grad_hat, normed, inverse):
    return inverse * (grad_hat - normed * jnp.mean(grad_hat * normed, axis=-1, keepdims=True))


def dot(left, right):
    return jnp.dot(left, right, preferred_element_type=F32)


def inner_rows(left, right):
    return lax.dot_general(left, right, (((0,), (0,)), ((), ())), preferred_element_type=F32)


def inner_cols(left, right):
    return lax.dot_general(left, right, (((1,), (1,)), ((), ())), preferred_element_type=F32)


def documents(lengths_row, rows):
    first_end = lengths_row[0]
    second_end = first_end + lengths_row[1]
    doc_ids = (rows >= first_end).astype(jnp.int32) + (rows >= second_end).astype(jnp.int32)
    starts = jnp.where(rows >= second_end, second_end, jnp.where(rows >= first_end, first_end, 0))
    return (doc_ids, rows - starts)


def rotation(positions, head_dim):
    half = head_dim // 2
    freqs = BASE ** (-2.0 * jnp.arange(half, dtype=F32) / head_dim)
    angles = positions.astype(F32)[:, None] * freqs[None, :]
    return (jnp.cos(angles), jnp.sin(angles))


def rotate(values, cosine, sine):
    half = values.shape[-1] // 2
    first = values[..., :half]
    second = values[..., half:]
    return jnp.concatenate(
        [first * cosine - second * sine, second * cosine + first * sine], axis=-1
    )


def unrotate(grads, cosine, sine):
    return rotate(grads, cosine, -sine)


def local(
    tokens,
    lengths,
    norm1_gain,
    q_down,
    latent_gain,
    q_up,
    kv_proj,
    out_proj,
    norm2_gain,
    w_gate,
    w_up,
    w_down,
    cotangent,
):
    micro, rows, width = tokens.shape
    seq = lax.axis_size("seq")
    line = seq // 2
    at = lax.axis_index("seq")
    me = lax.axis_index("mp")
    place, side = at // 2, at % 2
    quarter = rows // 4
    head_dim = kv_proj.shape[1] // 2
    heads = q_up.shape[1] // head_dim
    part = q_down.shape[1]
    kv_part = kv_proj.shape[1] // 4
    scale = head_dim ** (-0.5)
    beside = [(i, i ^ 1) for i in range(seq)]

    def swap(index):
        return ((index & 1) << 1) | (index >> 1)

    def to_relative(array, axis):
        size = array.shape[axis] // 4
        return jnp.concatenate(
            [lax.dynamic_slice_in_dim(array, (me ^ k) * size, size, axis) for k in ORDER], axis
        )

    def to_natural(array, axis):
        size = array.shape[axis] // 4
        return jnp.concatenate(
            [lax.dynamic_slice_in_dim(array, swap(me ^ b) * size, size, axis) for b in range(4)],
            axis,
        )

    def sum_mp(partial):
        half = 2 * quarter
        got = lax.ppermute(partial[half:].astype(LOW), "mp", CORE)
        kept = partial[:half] + got.astype(F32)
        got = lax.ppermute(kept[quarter:].astype(LOW), "mp", CROSS)
        return kept[:quarter] + got.astype(F32)

    def gather_mp(piece, axis):
        pair = jnp.concatenate([piece, lax.ppermute(piece, "mp", CROSS)], axis)
        return jnp.concatenate([pair, lax.ppermute(pair, "mp", CORE)], axis)

    def gather_columns(piece):
        a, b, c, d = (lax.ppermute(piece, "mp", CROSS)[i * quarter : (i + 1) * quarter] for i in range(4))
        pair = jnp.concatenate([piece, jnp.concatenate([b, a, d, c], 0)], 1)
        got = lax.ppermute(pair, "mp", CORE)
        got = jnp.concatenate([got[2 * quarter :], got[: 2 * quarter]], 0)
        return jnp.concatenate([pair, got], 1)

    def halves(array):
        split = array.reshape(array.shape[0], line, 2, array.shape[1] // seq)
        mine = lax.dynamic_index_in_dim(split, side, 2, keepdims=False)
        theirs = lax.dynamic_index_in_dim(split, 1 - side, 2, keepdims=False)
        return jnp.swapaxes(mine, 0, 1), lax.ppermute(
            jnp.swapaxes(theirs, 0, 1), "seq", beside
        )

    def other(array):
        return lax.ppermute(array, "seq", beside)

    def reduce_line(block):
        up = down = None
        for step in range(1, line):
            goes_up = [(i, i + 2) for i in range(2 * step)]
            goes_down = [(seq - 1 - i, seq - 3 - i) for i in range(2 * step)]
            for_up, for_down = line - step + place, step - line + place
            if 2 * step < line + 1:
                which = jnp.where(
                    place <= step - 1, for_up, jnp.where(place >= line - step, for_down, 0)
                )
                term = block(which)
                if up is not None:
                    term = term + up.astype(F32) + down.astype(F32)
                term = term.astype(LOW)
                if step == 1 and line > 3:
                    up = lax.ppermute(term, "seq", goes_up + goes_down)
                    down = jnp.zeros_like(up)
                else:
                    up = lax.ppermute(term, "seq", goes_up)
                    down = lax.ppermute(term, "seq", goes_down)
            else:
                term_up = block(jnp.clip(for_up, 0, line - 1)) + up.astype(F32)
                term_down = block(jnp.clip(for_down, 0, line - 1)) + down.astype(F32)
                up = lax.ppermute(term_up.astype(LOW), "seq", goes_up)
                down = lax.ppermute(term_down.astype(LOW), "seq", goes_down)
        return block(place) + up.astype(F32) + down.astype(F32)

    def take(array, index):
        return lax.dynamic_index_in_dim(array, index, 0, keepdims=False)

    quarter_rows = jnp.arange(quarter, dtype=jnp.int32)
    row_ids = at * rows + jnp.concatenate([(me ^ k) * quarter + quarter_rows for k in ORDER])
    key_ids = (
        ((place - jnp.arange(line, dtype=jnp.int32)[None, None, :, None, None]) * 2
         + (side ^ jnp.arange(2, dtype=jnp.int32)[None, :, None, None, None])) * rows
        + (me ^ (jnp.arange(2, dtype=jnp.int32)[:, None, None, None, None]
                 + 2 * jnp.arange(2, dtype=jnp.int32)[None, None, None, :, None])) * quarter
        + quarter_rows[None, None, None, None, :]
    ).reshape(seq * rows)

    x_low = [to_relative(tokens[m], 0) for m in range(micro)]
    dz_low = [to_relative(cotangent[m], 0) for m in range(micro)]
    kv_cols = lax.dynamic_slice_in_dim(kv_proj, me * kv_part, kv_part, 1)
    first_weights = jnp.concatenate([q_down, kv_cols], axis=1)

    h1, kv, c_part, n1, inv1 = [], [], [], [], []
    tables, docs = [], []
    for m in range(micro):
        doc, places = documents(lengths[m], row_ids)
        docs.append(doc)
        cosine, sine = rotation(places, head_dim)
        tables.append((cosine, sine))
        x = x_low[m].astype(F32)
        inverse = inverse_rms(x)
        h1.append((x * inverse * norm1_gain).astype(LOW))
        inv1.append(inverse[:quarter])
        n1.append(x[:quarter] * inverse[:quarter])
        half = 2 * quarter
        pair = dot(h1[m][:half], kv_proj)
        packed = jnp.concatenate(
            [rotate(pair[:, :head_dim], cosine[:half], sine[:half]), pair[:, head_dim:]], axis=1
        ).astype(LOW)
        blocks = [packed] + [
            lax.ppermute(packed, "seq", [(i, i + 2 * d) for i in range(seq - 2 * d)])
            for d in range(1, line)
        ]
        near = jnp.stack(blocks, 0)
        near = jnp.stack([near, other(near)], 0)
        kv.append(
            jnp.stack([near, lax.ppermute(near, "mp", CORE)], 0).reshape(
                seq * rows, 2 * head_dim
            )
        )
        c_part.append(dot(h1[m], q_down).astype(LOW))

    dz_half, dz_half_other = halves(jnp.concatenate(dz_low, 0))
    h1_half, h1_half_other = halves(jnp.concatenate(h1, 0))

    state = []
    qn_list, o_list = [], []
    for m in range(micro):
        cosine, sine = tables[m]
        c = to_natural(gather_columns(c_part[m]), 1).astype(F32)
        inv_c = inverse_rms(c)
        chat = c * inv_c
        qn = (chat * latent_gain).astype(LOW)
        qp = dot(qn, q_up).reshape(rows, heads, head_dim)
        q = rotate(qp, cosine[:, None, :], sine[:, None, :]).astype(LOW)
        key_docs, _ = documents(lengths[m], key_ids)
        visible = (
            (key_docs[None, :] == docs[m][:, None])
            & (key_ids[None, :] <= row_ids[:, None])
            & (key_ids[None, :] >= 0)
        )
        keys, values = kv[m][:, :head_dim], kv[m][:, head_dim:]
        scores = jnp.einsum("thd,nd->thn", q, keys, preferred_element_type=F32) * scale
        scores = jnp.where(visible[:, None, :], scores, NEG_LARGE)
        top = jnp.max(scores, axis=-1, keepdims=True)
        probs = jnp.exp(scores - top)
        total = jnp.sum(probs, axis=-1, keepdims=True)
        attended = (
            jnp.einsum("thn,nd->thd", probs.astype(LOW), values, preferred_element_type=F32)
            / total
        )
        log_total = top + jnp.log(total)
        o = attended.astype(LOW).reshape(rows, heads * head_dim)
        branch = sum_mp(dot(o, out_proj))
        y = x_low[m][:quarter].astype(F32) + branch
        inv2 = inverse_rms(y)
        n2 = y * inv2
        h2 = gather_mp((n2 * norm2_gain).astype(LOW), 0)
        g = dot(h2, w_gate)
        u = dot(h2, w_up)
        sig = jax.nn.sigmoid(g)
        swish = g * sig
        hid = (swish * u).astype(LOW)
        dhid = inner_cols(dz_low[m], w_down)
        dg = (dhid * u * sig * (1.0 + g * (1.0 - sig))).astype(LOW)
        du = (dhid * swish).astype(LOW)
        qn_list.append(qn)
        o_list.append(o)
        state.append(
            dict(chat=chat, inv_c=inv_c, qn=qn, q=q, visible=visible, attended=attended,
                 log_total=log_total, o=o, y=y, n2=n2, inv2=inv2, h2=h2, hid=hid, dg=dg, du=du)
        )

    def tokens_of(name):
        own = [state[m][name] for m in range(micro)]
        return jnp.concatenate(own + [other(a) for a in own], 0)

    def halves_of(arrays):
        pairs = [halves(a) for a in arrays]
        return jnp.concatenate([p[0] for p in pairs] + [p[1] for p in pairs], 1)

    dz_all = jnp.concatenate([dz_half, dz_half_other], 1)
    h1_all = jnp.concatenate([h1_half, h1_half_other], 1)
    qn_all = halves_of(qn_list)
    o_all = tokens_of("o")
    hid_all = tokens_of("hid")
    h2_all = halves_of([st["h2"] for st in state])
    dg_all = tokens_of("dg")
    du_all = tokens_of("du")

    grad_down = reduce_line(lambda i: inner_rows(hid_all, take(dz_all, i)))
    grad_gate = reduce_line(lambda i: inner_rows(take(h2_all, i), dg_all))
    grad_up = reduce_line(lambda i: inner_rows(take(h2_all, i), du_all))

    dyl_list, gain2 = [], 0.0
    for m in range(micro):
        st = state[m]
        dh2 = sum_mp(inner_cols(st["dg"], w_gate) + inner_cols(st["du"], w_up))
        gain2 = gain2 + jnp.sum(dh2 * st["n2"], axis=0)
        dy = dz_low[m][:quarter].astype(F32) + norm_backward(
            dh2 * norm2_gain, st["n2"], st["inv2"]
        )
        st["dy"] = dy
        st["dyl"] = gather_mp(dy.astype(LOW), 0)
        dyl_list.append(st["dyl"])
    dyl_all = halves_of(dyl_list)
    grad_out = reduce_line(lambda i: inner_rows(o_all, take(dyl_all, i)))

    layer_out = []
    for m in range(micro):
        st = state[m]
        ffn = sum_mp(dot(st["hid"], w_down))
        layer_out.append(to_natural(gather_mp((st["y"] + ffn).astype(LOW), 0), 0))

    gain_c = 0.0
    for m in range(micro):
        st = state[m]
        cosine, sine = tables[m]
        keys, values = kv[m][:, :head_dim], kv[m][:, head_dim:]
        do = inner_cols(st["dyl"], out_proj).reshape(rows, heads, head_dim).astype(LOW)
        delta = jnp.sum(do.astype(F32) * st["attended"], axis=-1, keepdims=True)
        scores = jnp.einsum("thd,nd->thn", st["q"], keys, preferred_element_type=F32) * scale
        probs = jnp.exp(jnp.where(st["visible"][:, None, :], scores, NEG_LARGE) - st["log_total"])
        grad_probs = jnp.einsum("thd,nd->thn", do, values, preferred_element_type=F32)
        ds = (probs * (grad_probs - delta)).astype(LOW)
        dq = jnp.einsum("thn,nd->thd", ds, keys, preferred_element_type=F32) * scale
        dk = jnp.einsum("thn,thd->nd", ds, st["q"], preferred_element_type=F32) * scale
        dv = jnp.einsum("thn,thd->nd", probs.astype(LOW), do, preferred_element_type=F32)
        dkv = jnp.concatenate([dk, dv], 1).reshape(2, 2, line, 2, quarter, 2 * head_dim)
        mine = dkv[0] + lax.ppermute(dkv[1].astype(LOW), "mp", CORE).astype(F32)
        mine = mine[:, :, 0] + lax.ppermute(mine[:, :, 1].astype(LOW), "mp", CROSS).astype(F32)
        mine = mine[0] + other(mine[1].astype(LOW)).astype(F32)
        total = mine[0]
        for d in range(1, line):
            total = total + lax.ppermute(
                mine[d].astype(LOW), "seq", [(i + 2 * d, i) for i in range(seq - 2 * d)]
            ).astype(F32)
        dkv_low = jnp.concatenate(
            [
                unrotate(total[:, :head_dim], cosine[:quarter], sine[:quarter]),
                total[:, head_dim:],
            ],
            axis=1,
        ).astype(LOW)
        dkv_cols = lax.dynamic_slice_in_dim(gather_mp(dkv_low, 0), me * kv_part, kv_part, 1)
        dqp = (
            unrotate(dq, cosine[:, None, :], sine[:, None, :])
            .astype(LOW)
            .reshape(rows, heads * head_dim)
        )
        st["dqp"] = dqp
        dqn = sum_mp(inner_cols(dqp, q_up))
        chat, inv_c = st["chat"][:quarter], st["inv_c"][:quarter]
        gain_c = gain_c + jnp.sum(dqn * chat, axis=0)
        dc = norm_backward(dqn * latent_gain, chat, inv_c).astype(LOW)
        dc_cols = lax.dynamic_slice_in_dim(gather_mp(dc, 0), me * part, part, 1)
        st["dfirst"] = jnp.concatenate([dc_cols, dkv_cols], 1)

    dqp_all = tokens_of("dqp")
    grad_qup = reduce_line(lambda i: inner_rows(take(qn_all, i), dqp_all))
    dfirst_all = tokens_of("dfirst")
    grad_first = reduce_line(lambda i: inner_rows(take(h1_all, i), dfirst_all))
    grad_qdown = grad_first[:, :part]
    kv_cols_grad = grad_first[:, part:]
    pieces = []
    for k in ORDER:
        sent = lax.dynamic_slice_in_dim(
            kv_cols_grad, (me ^ k) * (kv_cols_grad.shape[0] // 4), kv_cols_grad.shape[0] // 4, 0
        )
        pieces.append(lax.ppermute(sent, "mp", [(i, i ^ k) for i in range(4)]) if k else sent)
    grad_kv = to_natural(jnp.concatenate(pieces, 1), 1)

    input_grads, gain1 = [], 0.0
    for m in range(micro):
        st = state[m]
        dh1 = sum_mp(inner_cols(st["dfirst"], first_weights))
        gain1 = gain1 + jnp.sum(dh1 * n1[m], axis=0)
        dx = (st["dy"] + norm_backward(dh1 * norm1_gain, n1[m], inv1[m])).astype(LOW)
        input_grads.append(to_natural(gather_mp(dx, 0), 0))

    gains = jnp.concatenate(
        [gain1.reshape(seq, -1), gain2.reshape(seq, -1), gain_c.reshape(seq, -1)], axis=1
    )
    gains = gains + lax.ppermute(gains, "mp", CORE)
    gains = gains + lax.ppermute(gains, "mp", CROSS)
    gain_sum = take(gains, at)
    for k in range(1, seq):
        gain_sum = gain_sum + lax.ppermute(
            take(gains, at ^ k), "seq", [(i, i ^ k) for i in range(seq)]
        )
    wide = width // seq
    return (
        jnp.stack(layer_out, axis=0),
        jnp.stack(input_grads, axis=0),
        gain_sum[:wide],
        grad_qdown,
        gain_sum[2 * wide :],
        grad_qup,
        grad_kv,
        grad_out,
        gain_sum[wide : 2 * wide],
        grad_gate,
        grad_up,
        grad_down,
    )


def solution(mesh):
    placed = (
        P(None, "seq", None),
        P(),
        P(),
        P(None, "mp"),
        P(),
        P(None, "mp"),
        P(),
        P("mp", None),
        P(),
        P(None, "mp"),
        P(None, "mp"),
        P("mp", None),
        P(None, "seq", None),
    )
    return jax.shard_map(
        local,
        mesh=mesh,
        in_specs=placed,
        out_specs=(
            P(None, "seq", None),
            P(None, "seq", None),
            P("seq"),
            P("seq", "mp"),
            P("seq"),
            P("seq", "mp"),
            P(("seq", "mp"), None),
            P("mp", "seq"),
            P("seq"),
            P("seq", "mp"),
            P("seq", "mp"),
            P("mp", "seq"),
        ),
        check_vma=False,
    )
```

```python
import jax
import jax.numpy as jnp
from jax import lax
from jax.experimental import pallas as pl
from jax.experimental.pallas import tpu as pltpu
from jax.sharding import PartitionSpec as P

EPS = 1e-06
BASE = 10000.0
NEG_LARGE = -1e30
LOW = jnp.bfloat16
F32 = jnp.float32
ORDER = (0, 2, 1, 3)
CORE = [(i, i ^ 1) for i in range(4)]
CROSS = [(i, i ^ 2) for i in range(4)]


def inverse_rms(values):
    return lax.rsqrt(jnp.mean(values * values, axis=-1, keepdims=True) + EPS)


def norm_backward(grad_hat, normed, inverse):
    return inverse * (grad_hat - normed * jnp.mean(grad_hat * normed, axis=-1, keepdims=True))


def dot(left, right):
    return jnp.dot(left, right, preferred_element_type=F32)


def inner_rows(left, right):
    return lax.dot_general(left, right, (((0,), (0,)), ((), ())), preferred_element_type=F32)


def inner_cols(left, right):
    return lax.dot_general(left, right, (((1,), (1,)), ((), ())), preferred_element_type=F32)


def documents(lengths_row, rows):
    first_end = lengths_row[0]
    second_end = first_end + lengths_row[1]
    doc_ids = (rows >= first_end).astype(jnp.int32) + (rows >= second_end).astype(jnp.int32)
    starts = jnp.where(rows >= second_end, second_end, jnp.where(rows >= first_end, first_end, 0))
    return (doc_ids, rows - starts)


def rotation(positions, head_dim):
    half = head_dim // 2
    freqs = BASE ** (-2.0 * jnp.arange(half, dtype=F32) / head_dim)
    angles = positions.astype(F32)[:, None] * freqs[None, :]
    return (jnp.cos(angles), jnp.sin(angles))


def rotate(values, cosine, sine):
    half = values.shape[-1] // 2
    first = values[..., :half]
    second = values[..., half:]
    return jnp.concatenate(
        [first * cosine - second * sine, second * cosine + first * sine], axis=-1
    )


def unrotate(grads, cosine, sine):
    return rotate(grads, cosine, -sine)


def in_vmem():
    return pl.BlockSpec(memory_space=pltpu.VMEM)


def whole(shape, dtype):
    return jax.ShapeDtypeStruct(shape, dtype)


def run(body, ids, args, outs, flops, scratch=(), name=None, limit=40):
    return pl.pallas_call(
        body,
        grid_spec=pltpu.PrefetchScalarGridSpec(
            num_scalar_prefetch=1,
            grid=(1,),
            in_specs=[in_vmem()] * len(args),
            out_specs=[in_vmem()] * len(outs),
            scratch_shapes=list(scratch),
        ),
        out_shape=list(outs),
        cost_estimate=pl.CostEstimate(flops=flops, bytes_accessed=1 << 20, transcendentals=0),
        compiler_params=pltpu.CompilerParams(vmem_limit_bytes=limit << 20),
        name=name,
    )(ids, *args)


def side_columns(source, mine, theirs, side):
    line, _, wide = mine.shape
    for z in range(line):
        mine[z] = source[:, pl.ds(pl.multiple_of((2 * z + side) * wide, wide), wide)]
        theirs[z] = source[:, pl.ds(pl.multiple_of((2 * z + 1 - side) * wide, wide), wide)]


def first_body(m, quarter, ids, x_ref, gain, q_down, kv_proj, cos, sin, c, kv, h1, mine, theirs):
    blocks = [
        x_ref[m, pl.ds(pl.multiple_of((ids[0] ^ k) * quarter, quarter), quarter), :] for k in ORDER
    ]
    x = jnp.concatenate(blocks, 0).astype(F32)
    low = (x * inverse_rms(x) * gain[...]).astype(LOW)
    h1[...] = low
    half = 2 * quarter
    pair = dot(low[:half], kv_proj[...])
    wide = kv_proj.shape[1] // 2
    kv[:, :wide] = rotate(pair[:, :wide], cos[:half], sin[:half]).astype(LOW)
    kv[:, wide:] = pair[:, wide:].astype(LOW)
    c[...] = dot(low, q_down[...]).astype(LOW)
    if mine is not None:
        side_columns(h1, mine, theirs, ids[1])


def cotangent_body(m, quarter, ids, z_ref, w_down, dhid, dz, mine, theirs):
    blocks = [
        z_ref[m, pl.ds(pl.multiple_of((ids[0] ^ k) * quarter, quarter), quarter), :] for k in ORDER
    ]
    dz[...] = jnp.concatenate(blocks, 0)
    if mine is not None:
        side_columns(dz, mine, theirs, ids[1])
    dhid[...] = inner_cols(dz[...], w_down[...])


def attend_body(
    scale, ids, c0, c1, c2, gain, q_up, cos, sin, kv, key_ids, row_ids, row_starts, out_proj,
    qn, q, o, lse, send, keep, mine, theirs,
):
    rows = qn.shape[0]
    quarter = rows // 4
    part = c0.shape[1]
    wide = q.shape[2]
    got = c1[...]
    pair = jnp.concatenate(
        [got[quarter : 2 * quarter], got[:quarter], got[3 * quarter :], got[2 * quarter : 3 * quarter]],
        0,
    )
    far = jnp.concatenate([c2[2 * quarter :], c2[: 2 * quarter]], 0)
    c = jnp.concatenate([c0[...], pair, far], 1).astype(F32)
    chat = c * inverse_rms(c)
    for k, xor in enumerate(ORDER):
        columns = pl.ds(pl.multiple_of((ids[0] ^ xor) * part, part), part)
        qn[:, columns] = (chat[:, k * part : (k + 1) * part] * gain[:, columns]).astype(LOW)
    if mine is not None:
        side_columns(qn, mine, theirs, ids[1])
    bias = jnp.where(
        (key_ids[...] >= row_starts[...]) & (key_ids[...] <= row_ids[...]), 0.0, NEG_LARGE
    )
    low = qn[...]
    keys, values = kv[:, :wide], kv[:, wide:]
    for h in range(q.shape[0]):
        pre = dot(low, q_up[:, h * wide : (h + 1) * wide])
        q_h = (rotate(pre, cos[...], sin[...]) * scale).astype(LOW)
        q[h] = q_h
        scores = inner_cols(q_h, keys) + bias
        top = jnp.max(scores, axis=-1, keepdims=True)
        probs = jnp.exp(scores - top)
        total = jnp.sum(probs, axis=-1, keepdims=True)
        out = dot(probs.astype(LOW), values) / total
        o[:, h * wide : (h + 1) * wide] = out.astype(LOW)
        log_total = jnp.broadcast_to(top + jnp.log(total), (rows, 128))
        lse[h : h + 1, :] = jnp.transpose(log_total)[:1]
    half = 2 * quarter
    send[...] = dot(o[half:, :], out_proj[...]).astype(LOW)
    keep[...] = dot(o[:half, :], out_proj[...])


def forward_body(ids, a0, a1, a2, w_gate, w_up, dhid, h2, hid, dgu, mine, theirs):
    h2[...] = jnp.concatenate([a0[...], a1[...], a2[...]], 0)
    if mine is not None:
        side_columns(h2, mine, theirs, ids[1])
    low = h2[...]
    wide = hid.shape[1]
    g = dot(low, w_gate[...])
    u = dot(low, w_up[...])
    sig = jax.nn.sigmoid(g)
    swish = g * sig
    hid[...] = (swish * u).astype(LOW)
    back = dhid[...]
    dgu[:, :wide] = (back * u * sig * (1.0 + g * (1.0 - sig))).astype(LOW)
    dgu[:, wide:] = (back * swish).astype(LOW)


def hidden_back_body(ids, dgu, w_gate, w_up, send, keep):
    wide = w_gate.shape[1]
    half = dgu.shape[0] // 2
    for rows, out in ((slice(half, None), send), (slice(0, half), keep)):
        out[...] = (
            inner_cols(dgu[rows, :wide], w_gate[...]) + inner_cols(dgu[rows, wide:], w_up[...])
        ).astype(out.dtype)


def block_body(count, extra, final, ids, *refs):
    lefts, rights = refs[:count], refs[count : 2 * count]
    added, outs = refs[2 * count : 2 * count + extra], refs[2 * count + extra :]
    total = None
    for a, b in zip(lefts, rights):
        term = inner_rows(a[ids[0]], b[...])
        total = term if total is None else total + term
    for ref in added:
        total = total + ref[...].astype(F32)
    if final == "turned":
        outs[0][...] = jnp.transpose(total)
    elif final == "split":
        wide = outs[0].shape[1]
        outs[0][...] = total[:, :wide]
        outs[1][...] = total[:, wide:]
    else:
        outs[0][...] = total.astype(outs[0].dtype)


def attend_back_body(
    scale, micro, chunk, ids, a0, a1, a2, out_proj, q_up, key_ids, *refs
):
    per = 7
    groups = [refs[m * per : (m + 1) * per] for m in range(micro)]
    dyl_out, dqp, send, keep, kv_send, kv_keep = refs[micro * per : micro * per + 6]
    dq_acc, do_acc, delta_acc = refs[-3:]
    sides = refs[micro * per + 6 : -3]
    for m in range(micro):
        q, kv, o, lse, row_ids, cos, sin = groups[m]
        heads, rows, wide = q.shape
        half_rows = rows // 2
        dyl = jnp.concatenate([a0[m], a1[m], a2[m]], 0)
        dyl_out[m] = dyl
        if sides:
            side_columns(dyl_out.at[m], sides[2 * m], sides[2 * m + 1], ids[1])
        for h in range(heads):
            do = inner_cols(dyl, out_proj[h * wide : (h + 1) * wide, :]).astype(LOW)
            do_acc[h] = do
            delta = jnp.sum(
                do.astype(F32) * o[:, h * wide : (h + 1) * wide].astype(F32), axis=-1, keepdims=True
            )
            delta_acc[h] = jnp.transpose(jnp.broadcast_to(delta, (rows, 128)))[:8]
            dq_acc[h] = jnp.zeros((rows, wide), F32)
        count = kv.shape[0] // 2 // chunk
        for part, out in ((0, kv_keep), (1, kv_send)):

            def one(i, carry):
                base = pl.multiple_of((part * count + i) * chunk, chunk)
                keys = kv[pl.ds(base, chunk), :wide]
                values = kv[pl.ds(base, chunk), wide:]
                at = key_ids[pl.ds(base, chunk), :]
                bias = jnp.where((at >= row_ids[1:2, :]) & (at <= row_ids[0:1, :]), 0.0, NEG_LARGE)

                def head(h, sums):
                    dk, dv = sums
                    q_h, do_h = q[h], do_acc[h]
                    probs = jnp.exp(inner_cols(keys, q_h) + bias - lse[pl.ds(h, 1), :])
                    back = inner_cols(values, do_h) - delta_acc[h][:1]
                    ds = (probs * back).astype(LOW)
                    dv = dv + dot(probs.astype(LOW), do_h)
                    dk = dk + dot(ds, q_h)
                    dq_acc[h] = dq_acc[h] + inner_rows(ds, keys)
                    return dk, dv

                zero = jnp.zeros((chunk, wide), F32)
                dk, dv = lax.fori_loop(0, heads, head, (zero, zero))
                place = pl.ds(pl.multiple_of(i * chunk, chunk), chunk)
                out[m, place, :wide] = dk.astype(out.dtype)
                out[m, place, wide:] = dv.astype(out.dtype)
                return carry

            if count == 1:
                one(0, 0)
            else:
                lax.fori_loop(0, count, one, 0)
        for h in range(heads):
            dq = unrotate(dq_acc[h] * scale, cos[...], sin[...])
            dqp[m, :, h * wide : (h + 1) * wide] = dq.astype(LOW)
        low = dqp[m]
        send[m] = inner_cols(low[half_rows:], q_up[...]).astype(LOW)
        keep[m] = inner_cols(low[:half_rows], q_up[...])


def natural_body(micro, quarter, ids, a0, a1, a2, out):
    for m in range(micro):
        pieces = (a0[m], a1[m], a2[m, :quarter, :], a2[m, quarter:, :])
        for k, piece in zip(ORDER, pieces):
            out[m, pl.ds(pl.multiple_of((ids[0] ^ k) * quarter, quarter), quarter), :] = piece


def local(
    tokens,
    lengths,
    norm1_gain,
    q_down,
    latent_gain,
    q_up,
    kv_proj,
    out_proj,
    norm2_gain,
    w_gate,
    w_up,
    w_down,
    cotangent,
):
    micro, rows, width = tokens.shape
    seq = lax.axis_size("seq")
    line = seq // 2
    at = lax.axis_index("seq").astype(jnp.int32)
    me = lax.axis_index("mp").astype(jnp.int32)
    place, side = at // 2, at % 2
    ids = jnp.stack([me, side])
    quarter, half = rows // 4, rows // 2
    head_dim = kv_proj.shape[1] // 2
    heads = q_up.shape[1] // head_dim
    part = q_down.shape[1]
    rank = q_up.shape[0]
    hidden = w_gate.shape[1]
    kv_part = kv_proj.shape[1] // 4
    wide = width // seq
    scale = head_dim ** (-0.5)
    key_count = seq * rows
    beside = [(i, i ^ 1) for i in range(seq)]

    def swap(index):
        return ((index & 1) << 1) | (index >> 1)

    def to_natural(array, axis):
        size = array.shape[axis] // 4
        return jnp.concatenate(
            [lax.dynamic_slice_in_dim(array, swap(me ^ b) * size, size, axis) for b in range(4)],
            axis,
        )

    def other(array):
        return lax.ppermute(array, "seq", beside)

    def sum_mp(send, keep):
        kept = keep + lax.ppermute(send, "mp", CORE).astype(F32)
        got = lax.ppermute(kept[..., quarter:, :].astype(LOW), "mp", CROSS)
        return kept[..., :quarter, :] + got.astype(F32)

    def gather_mp(piece):
        near = lax.ppermute(piece, "mp", CROSS)
        pair = jnp.concatenate([piece, near], -2)
        return piece, near, lax.ppermute(pair, "mp", CORE)

    def sides_shape(columns):
        if columns // seq % 128:
            return []
        return [whole((line, rows, columns // seq), LOW)] * 2

    def sides(made, full):
        if made:
            mine, theirs = made
        else:
            split = full.reshape(rows, line, 2, full.shape[1] // seq)
            mine = jnp.swapaxes(lax.dynamic_index_in_dim(split, side, 2, keepdims=False), 0, 1)
            theirs = jnp.swapaxes(
                lax.dynamic_index_in_dim(split, 1 - side, 2, keepdims=False), 0, 1
            )
        return mine, other(theirs)

    def without_sides(body, count):
        return body if count else lambda *refs: body(*refs, None, None)

    def reduce_line(lefts, rights, final):
        w, columns = lefts[0].shape[2], rights[0].shape[1]
        flops = 2 * w * columns * rows * len(lefts)

        def block(index, added, outs, kind):
            return run(
                lambda *refs: block_body(len(lefts), len(added), kind, *refs),
                index.reshape(1),
                [*lefts, *rights, *added],
                outs,
                flops,
                name="block",
            )

        low = [whole((w, columns), LOW)]
        up = down = None
        for step in range(1, line):
            goes_up = [(i, i + 2) for i in range(2 * step)]
            goes_down = [(seq - 1 - i, seq - 3 - i) for i in range(2 * step)]
            for_up, for_down = line - step + place, step - line + place
            if 2 * step < line + 1:
                which = jnp.where(
                    place <= step - 1, for_up, jnp.where(place >= line - step, for_down, 0)
                )
                (term,) = block(which, [a for a in (up, down) if a is not None], low, None)
                if step == 1 and line > 3:
                    up = lax.ppermute(term, "seq", goes_up + goes_down)
                else:
                    up = lax.ppermute(term, "seq", goes_up)
                    down = lax.ppermute(term, "seq", goes_down)
            else:
                (term_up,) = block(jnp.clip(for_up, 0, line - 1), [up], low, None)
                (term_down,) = block(jnp.clip(for_down, 0, line - 1), [down], low, None)
                up = lax.ppermute(term_up, "seq", goes_up)
                down = lax.ppermute(term_down, "seq", goes_down)
        if final == "turned":
            outs = [whole((columns, w), F32)]
        elif final == "split":
            outs = [whole((w, columns // 2), F32)] * 2
        else:
            outs = [whole((w, columns), F32)]
        return block(place, [up, down], outs, final)

    def with_other(arrays):
        return list(arrays) + [other(a) for a in arrays]

    def two_sides(pairs):
        return [p[0] for p in pairs] + [p[1] for p in pairs]

    quarter_rows = jnp.arange(quarter, dtype=jnp.int32)
    row_ids = at * rows + jnp.concatenate([(me ^ k) * quarter + quarter_rows for k in ORDER])
    key_ids = (
        ((place - jnp.arange(line, dtype=jnp.int32)[None, None, :, None, None]) * 2
         + (side ^ jnp.arange(2, dtype=jnp.int32)[None, :, None, None, None])) * rows
        + (me ^ (jnp.arange(2, dtype=jnp.int32)[:, None, None, None, None]
                 + 2 * jnp.arange(2, dtype=jnp.int32)[None, None, None, :, None])) * quarter
        + quarter_rows[None, None, None, None, :]
    ).reshape(key_count)

    gain1_row, gain2_row, gain_c_row = norm1_gain[None, :], norm2_gain[None, :], latent_gain[None, :]
    kv_cols = lax.dynamic_slice_in_dim(kv_proj, me * kv_part, kv_part, 1)
    first_weights = jnp.concatenate([q_down, kv_cols], axis=1)
    width_sides = sides_shape(width)
    rank_sides = sides_shape(rank)

    tables, starts, kv, c_part, h1_pairs = [], [], [], [], []
    for m in range(micro):
        _, places = documents(lengths[m], row_ids)
        starts.append(row_ids - places)
        tables.append(rotation(places, head_dim))
        c, packed, h1, *made = run(
            without_sides(lambda *refs: first_body(m, quarter, *refs), len(width_sides)),
            ids,
            [tokens, gain1_row, q_down, kv_proj, *tables[m]],
            [whole((rows, part), LOW), whole((half, 2 * head_dim), LOW), whole((rows, width), LOW),
             *width_sides],
            2 * width * (rows * part + half * 2 * head_dim),
            name="first",
        )
        blocks = [packed] + [
            lax.ppermute(packed, "seq", [(i, i + 2 * d) for i in range(seq - 2 * d)])
            for d in range(1, line)
        ]
        near = jnp.stack(blocks, 0)
        near = jnp.stack([near, other(near)], 0)
        kv.append(
            jnp.stack([near, lax.ppermute(near, "mp", CORE)], 0).reshape(key_count, 2 * head_dim)
        )
        c_part.append(c)
        h1_pairs.append(sides(made, h1))

    dhid, dz_pairs, dz_rows = [], [], []
    for m in range(micro):
        back, dz, *made = run(
            without_sides(lambda *refs: cotangent_body(m, quarter, *refs), len(width_sides)),
            ids,
            [cotangent, w_down],
            [whole((rows, hidden), F32), whole((rows, width), LOW), *width_sides],
            2 * rows * width * hidden,
            name="cotangent",
        )
        dhid.append(back)
        dz_rows.append(dz)
        dz_pairs.append(sides(made, dz))

    qn_pairs, h2_pairs, hid, dgu, qs, os, lses, state = [], [], [], [], [], [], [], []
    for m in range(micro):
        near = lax.ppermute(c_part[m], "mp", CROSS)
        swapped = jnp.concatenate(
            [near[quarter : 2 * quarter], near[:quarter], near[3 * quarter :], near[2 * quarter : 3 * quarter]], 0
        )
        far = lax.ppermute(jnp.concatenate([c_part[m], swapped], 1), "mp", CORE)
        qn, q, o, lse, send, keep, *made = run(
            without_sides(lambda *refs: attend_body(scale, *refs), len(rank_sides)),
            ids,
            [c_part[m], near, far, gain_c_row, q_up, *tables[m], kv[m], key_ids[None, :],
             row_ids[:, None], starts[m][:, None], out_proj],
            [whole((rows, rank), LOW), whole((heads, rows, head_dim), LOW),
             whole((rows, heads * head_dim), LOW), whole((heads, rows), F32),
             whole((half, width), LOW), whole((half, width), F32), *rank_sides],
            2 * rows * heads * head_dim * (rank + 2 * key_count + width),
            name="attend",
        )
        qn_pairs.append(sides(made, qn))
        x = lax.dynamic_slice_in_dim(tokens[m], me * quarter, quarter, 0).astype(F32)
        inv1 = inverse_rms(x)
        y = x + sum_mp(send, keep)
        inv2 = inverse_rms(y)
        n2 = y * inv2
        pieces = gather_mp((n2 * gain2_row).astype(LOW))
        h2, hid_m, dgu_m, *made = run(
            without_sides(forward_body, len(width_sides)),
            ids,
            [*pieces, w_gate, w_up, dhid[m]],
            [whole((rows, width), LOW), whole((rows, hidden), LOW), whole((rows, 2 * hidden), LOW),
             *width_sides],
            4 * rows * width * hidden,
            name="forward",
        )
        h2_pairs.append(sides(made, h2))
        hid.append(hid_m)
        dgu.append(dgu_m)
        qs.append(q)
        os.append(o)
        lses.append(lse)
        c_rows = jnp.concatenate(
            [c_part[m][:quarter], swapped[:quarter], far[half : half + quarter]], 1
        )
        state.append(dict(x=x, n1=x * inv1, inv1=inv1, y=y, n2=n2, inv2=inv2, c=c_rows))

    (grad_down,) = reduce_line(two_sides(dz_pairs), with_other(hid), "turned")
    grad_gate, grad_up = reduce_line(two_sides(h2_pairs), with_other(dgu), "split")

    def stacked(name):
        return jnp.stack([st[name] for st in state], 0)

    back = [
        run(
            hidden_back_body,
            ids,
            [dgu[m], w_gate, w_up],
            [whole((half, width), LOW), whole((half, width), F32)],
            4 * rows * width * hidden,
            name="hidden_back",
        )
        for m in range(micro)
    ]
    dh2 = sum_mp(jnp.stack([b[0] for b in back], 0), jnp.stack([b[1] for b in back], 0))
    y, n2, inv2, n1, inv1 = (stacked(k) for k in ("y", "n2", "inv2", "n1", "inv1"))
    dz_own = jnp.stack([dz[:quarter] for dz in dz_rows], 0).astype(F32)
    gain2 = jnp.sum(dh2 * n2, axis=(0, 1))
    dy = dz_own + norm_backward(dh2 * gain2_row, n2, inv2)

    def attend_back(which, pieces):
        args = [*pieces, out_proj, q_up, key_ids[:, None]]
        for m in which:
            args += [qs[m], kv[m], os[m], lses[m], jnp.stack([row_ids, starts[m]], 0), *tables[m]]
        n = len(which)
        return run(
            lambda *refs: attend_back_body(scale, n, min(1024, key_count // 2), *refs),
            ids,
            args,
            [whole((n, rows, width), LOW), whole((n, rows, heads * head_dim), LOW),
             whole((n, half, rank), LOW), whole((n, half, rank), F32),
             whole((n, key_count // 2, 2 * head_dim), LOW),
             whole((n, key_count // 2, 2 * head_dim), F32), *(width_sides * n)],
            2 * n * rows * heads * head_dim * (5 * key_count + width + rank),
            scratch=[pltpu.VMEM((heads, rows, head_dim), F32),
                     pltpu.VMEM((heads, rows, head_dim), LOW),
                     pltpu.VMEM((heads, 8, rows), F32)],
            name="attend_back",
            limit=56,
        )

    pieces = gather_mp(dy.astype(LOW))
    if key_count <= 2048:
        dyl, dqp, send, keep, kv_send, kv_keep, *made = attend_back(range(micro), pieces)
    else:
        each = [attend_back([m], [p[m : m + 1] for p in pieces]) for m in range(micro)]
        dyl, dqp, send, keep, kv_send, kv_keep = (
            jnp.concatenate([e[i] for e in each], 0) for i in range(6)
        )
        made = [a for e in each for a in e[6:]]
    dyl_pairs = [sides(made[2 * m : 2 * m + 2], dyl[m]) for m in range(micro)]
    (grad_out,) = reduce_line(two_sides(dyl_pairs), with_other(os), "turned")
    (grad_qup,) = reduce_line(two_sides(qn_pairs), with_other([dqp[m] for m in range(micro)]), None)

    dqn = sum_mp(send, keep)
    c = stacked("c").astype(F32)
    inv_c = inverse_rms(c)
    chat = c * inv_c
    chat = to_natural(chat, 2)
    gain_c = jnp.sum(dqn * chat, axis=(0, 1))
    dc = norm_backward(dqn * gain_c_row, chat, inv_c).astype(LOW)

    dkv = kv_keep + lax.ppermute(kv_send, "mp", CORE).astype(F32)
    dkv = dkv.reshape(micro, 2, line, 2, quarter, 2 * head_dim)
    dkv = dkv[:, :, :, 0] + lax.ppermute(dkv[:, :, :, 1].astype(LOW), "mp", CROSS).astype(F32)
    dkv = dkv[:, 0] + other(dkv[:, 1].astype(LOW)).astype(F32)
    total = dkv[:, 0]
    for d in range(1, line):
        total = total + lax.ppermute(
            dkv[:, d].astype(LOW), "seq", [(i + 2 * d, i) for i in range(seq - 2 * d)]
        ).astype(F32)
    cosine = jnp.stack([t[0][:quarter] for t in tables], 0)
    sine = jnp.stack([t[1][:quarter] for t in tables], 0)
    dkv_low = jnp.concatenate(
        [unrotate(total[..., :head_dim], cosine, sine), total[..., head_dim:]], axis=-1
    ).astype(LOW)
    both = jnp.concatenate(gather_mp(jnp.concatenate([dc, dkv_low], -1)), -2)
    dfirst = jnp.concatenate(
        [lax.dynamic_slice_in_dim(both, me * part, part, 2),
         lax.dynamic_slice_in_dim(both, rank + me * kv_part, kv_part, 2)], -1
    )
    dfirst_list = [dfirst[m] for m in range(micro)]
    (grad_first,) = reduce_line(two_sides(h1_pairs), with_other(dfirst_list), None)
    grad_qdown = grad_first[:, :part]
    kv_cols_grad = grad_first[:, part:]
    pieces = []
    for k in ORDER:
        size = kv_cols_grad.shape[0] // 4
        sent = lax.dynamic_slice_in_dim(kv_cols_grad, (me ^ k) * size, size, 0)
        pieces.append(lax.ppermute(sent, "mp", [(i, i ^ k) for i in range(4)]) if k else sent)
    grad_kv = to_natural(jnp.concatenate(pieces, 1), 1)

    def put_natural(pieces):
        return run(
            lambda *refs: natural_body(micro, quarter, *refs),
            ids,
            pieces,
            [whole((micro, rows, width), LOW)],
            0,
            name="natural",
        )[0]

    part_sum = inner_cols(dfirst.reshape(micro * rows, -1), first_weights).reshape(micro, rows, width)
    dh1 = sum_mp(part_sum[:, half:].astype(LOW), part_sum[:, :half])
    gain1 = jnp.sum(dh1 * n1, axis=(0, 1))
    dx = (dy + norm_backward(dh1 * gain1_row, n1, inv1)).astype(LOW)
    input_grads = put_natural(gather_mp(dx))

    ffn = [dot(hid[m], w_down) for m in range(micro)]
    ffn = sum_mp(
        jnp.stack([f[half:] for f in ffn], 0).astype(LOW), jnp.stack([f[:half] for f in ffn], 0)
    )
    layer_out = put_natural(gather_mp((y + ffn).astype(LOW)))

    gains = jnp.concatenate(
        [gain1.reshape(seq, -1), gain2.reshape(seq, -1), gain_c.reshape(seq, -1)], axis=1
    )
    gains = gains + lax.ppermute(gains, "mp", CORE)
    gains = gains + lax.ppermute(gains, "mp", CROSS)
    gain_sum = lax.dynamic_index_in_dim(gains, at, 0, keepdims=False)
    for k in range(1, seq):
        gain_sum = gain_sum + lax.ppermute(
            lax.dynamic_index_in_dim(gains, at ^ k, 0, keepdims=False),
            "seq",
            [(i, i ^ k) for i in range(seq)],
        )
    return (
        layer_out,
        input_grads,
        gain_sum[:wide],
        grad_qdown,
        gain_sum[2 * wide :],
        grad_qup,
        grad_kv,
        grad_out,
        gain_sum[wide : 2 * wide],
        grad_gate,
        grad_up,
        grad_down,
    )


def solution(mesh):
    placed = (
        P(None, "seq", None),
        P(),
        P(),
        P(None, "mp"),
        P(),
        P(None, "mp"),
        P(),
        P("mp", None),
        P(),
        P(None, "mp"),
        P(None, "mp"),
        P("mp", None),
        P(None, "seq", None),
    )
    return jax.shard_map(
        local,
        mesh=mesh,
        in_specs=placed,
        out_specs=(
            P(None, "seq", None),
            P(None, "seq", None),
            P("seq"),
            P("seq", "mp"),
            P("seq"),
            P("seq", "mp"),
            P(("seq", "mp"), None),
            P("mp", "seq"),
            P("seq"),
            P("seq", "mp"),
            P("seq", "mp"),
            P("mp", "seq"),
        ),
        check_vma=False,
    )
```

```python
import functools

import jax
import jax.numpy as jnp
from jax import lax
from jax.experimental import pallas as pl
from jax.experimental.pallas import tpu as pltpu
from jax.sharding import PartitionSpec as P

EPS = 1e-06
BASE = 10000.0
NEG_LARGE = -1e30
LOW = jnp.bfloat16
F32 = jnp.float32
ORDER = (0, 2, 1, 3)
CORE = [(i, i ^ 1) for i in range(4)]
CROSS = [(i, i ^ 2) for i in range(4)]


def inverse_rms(values):
    return lax.rsqrt(jnp.mean(values * values, axis=-1, keepdims=True) + EPS)


def norm_backward(grad_hat, normed, inverse):
    return inverse * (grad_hat - normed * jnp.mean(grad_hat * normed, axis=-1, keepdims=True))


def dot(left, right):
    return jnp.dot(left, right, preferred_element_type=F32)


def inner_rows(left, right):
    return lax.dot_general(left, right, (((0,), (0,)), ((), ())), preferred_element_type=F32)


def inner_cols(left, right):
    return lax.dot_general(left, right, (((1,), (1,)), ((), ())), preferred_element_type=F32)


def documents(lengths_row, rows):
    first_end = lengths_row[0]
    second_end = first_end + lengths_row[1]
    doc_ids = (rows >= first_end).astype(jnp.int32) + (rows >= second_end).astype(jnp.int32)
    starts = jnp.where(rows >= second_end, second_end, jnp.where(rows >= first_end, first_end, 0))
    return (doc_ids, rows - starts)


def rotation(positions, head_dim):
    half = head_dim // 2
    freqs = BASE ** (-2.0 * jnp.arange(half, dtype=F32) / head_dim)
    angles = positions.astype(F32)[:, None] * freqs[None, :]
    return (jnp.cos(angles), jnp.sin(angles))


def rotate(values, cosine, sine):
    half = values.shape[-1] // 2
    first = values[..., :half]
    second = values[..., half:]
    return jnp.concatenate(
        [first * cosine - second * sine, second * cosine + first * sine], axis=-1
    )


def unrotate(grads, cosine, sine):
    return rotate(grads, cosine, -sine)


def in_vmem():
    return pl.BlockSpec(memory_space=pltpu.VMEM)


def whole(shape, dtype):
    return jax.ShapeDtypeStruct(shape, dtype)


def run(body, ids, args, outs, after=(), scratch=(), name=None, limit=40):
    args, after = list(args), list(after)

    def without(*refs):
        body(*refs[: 1 + len(args)], *refs[1 + len(args) + len(after) :])

    return pl.pallas_call(
        without,
        grid_spec=pltpu.PrefetchScalarGridSpec(
            num_scalar_prefetch=1,
            grid=(1,),
            in_specs=[in_vmem()] * len(args) + [pl.BlockSpec(memory_space=pl.ANY)] * len(after),
            out_specs=[in_vmem()] * len(outs),
            scratch_shapes=list(scratch),
        ),
        out_shape=list(outs),
        cost_estimate=pl.CostEstimate(flops=1000, bytes_accessed=1000, transcendentals=0),
        compiler_params=pltpu.CompilerParams(vmem_limit_bytes=limit << 20),
        name=name,
    )(ids, *args, *after)


def side_columns(source, mine, theirs, side):
    line, _, wide = mine.shape
    rows = theirs.shape[1]
    for z in range(line):
        mine[z] = source[:, pl.ds(pl.multiple_of((2 * z + side) * wide, wide), wide)]
        theirs[z] = source[:rows, pl.ds(pl.multiple_of((2 * z + 1 - side) * wide, wide), wide)]


def first_body(m, quarter, ids, x_ref, gain, q_down, kv_proj, cos, sin, c, kv, h1, mine, theirs):
    blocks = [
        x_ref[m, pl.ds(pl.multiple_of((ids[0] ^ k) * quarter, quarter), quarter), :] for k in ORDER
    ]
    x = jnp.concatenate(blocks, 0).astype(F32)
    low = (x * inverse_rms(x) * gain[...]).astype(LOW)
    h1[...] = low
    half = 2 * quarter
    pair = dot(low[:half], kv_proj[...])
    wide = kv_proj.shape[1] // 2
    kv[:, :wide] = rotate(pair[:, :wide], cos[:half], sin[:half]).astype(LOW)
    kv[:, wide:] = pair[:, wide:].astype(LOW)
    c[...] = dot(low, q_down[...]).astype(LOW)
    if mine is not None:
        side_columns(h1, mine, theirs, ids[1])


def cotangent_body(micro, quarter, ids, z_ref, w_down, dhid, dz, *sides):
    for m in range(micro):
        blocks = [
            z_ref[m, pl.ds(pl.multiple_of((ids[0] ^ k) * quarter, quarter), quarter), :]
            for k in ORDER
        ]
        dz[m] = jnp.concatenate(blocks, 0)
        if sides:
            side_columns(dz.at[m], sides[0].at[m], sides[1].at[m], ids[1])
        dhid[m] = inner_cols(dz[m], w_down[...])


def attend_body(
    scale, ids, c0, c1, c2, gain, q_up, cos, sin, kv, key_ids, row_ids, row_starts, out_proj,
    qn, q, o, lse, send, keep, mine, theirs,
):
    rows = qn.shape[0]
    quarter = rows // 4
    part = c0.shape[1]
    wide = q.shape[2]
    got = c1[...]
    pair = jnp.concatenate(
        [got[quarter : 2 * quarter], got[:quarter], got[3 * quarter :], got[2 * quarter : 3 * quarter]],
        0,
    )
    far = jnp.concatenate([c2[2 * quarter :], c2[: 2 * quarter]], 0)
    c = jnp.concatenate([c0[...], pair, far], 1).astype(F32)
    chat = c * inverse_rms(c)
    for k, xor in enumerate(ORDER):
        columns = pl.ds(pl.multiple_of((ids[0] ^ xor) * part, part), part)
        qn[:, columns] = (chat[:, k * part : (k + 1) * part] * gain[:, columns]).astype(LOW)
    if mine is not None:
        side_columns(qn, mine, theirs, ids[1])
    bias = jnp.where(
        (key_ids[...] >= row_starts[...]) & (key_ids[...] <= row_ids[...]), 0.0, NEG_LARGE
    )
    low = qn[...]
    keys, values = kv[:, :wide], kv[:, wide:]
    for h in range(q.shape[0]):
        pre = dot(low, q_up[:, h * wide : (h + 1) * wide])
        q_h = (rotate(pre, cos[...], sin[...]) * scale).astype(LOW)
        q[h] = q_h
        scores = inner_cols(q_h, keys) + bias
        top = jnp.max(scores, axis=-1, keepdims=True)
        probs = jnp.exp(scores - top)
        total = jnp.sum(probs, axis=-1, keepdims=True)
        out = dot(probs.astype(LOW), values) / total
        o[:, h * wide : (h + 1) * wide] = out.astype(LOW)
        log_total = jnp.broadcast_to(top + jnp.log(total), (rows, 128))
        lse[h : h + 1, :] = jnp.transpose(log_total)[:1]
    half = 2 * quarter
    send[...] = dot(o[half:, :], out_proj[...]).astype(LOW)
    keep[...] = dot(o[:half, :], out_proj[...])


def forward_body(m, ids, a0, a1, a2, w_gate, w_up, dhid, h2, hid, dg, du, mine, theirs):
    h2[...] = jnp.concatenate([a0[...], a1[...], a2[...]], 0)
    if mine is not None:
        side_columns(h2, mine, theirs, ids[1])
    low = h2[...]
    g = dot(low, w_gate[...])
    u = dot(low, w_up[...])
    sig = jax.nn.sigmoid(g)
    swish = g * sig
    hid[...] = (swish * u).astype(LOW)
    back = dhid[m]
    dg[...] = (back * u * sig * (1.0 + g * (1.0 - sig))).astype(LOW)
    du[...] = (back * swish).astype(LOW)


def hidden_back_body(micro, ids, *refs):
    dgs, dus = refs[:micro], refs[micro : 2 * micro]
    w_gate, w_up, send, keep = refs[2 * micro :]
    half = send.shape[1]
    for m in range(micro):
        for rows, out in ((slice(half, None), send), (slice(0, half), keep)):
            out[m] = (
                inner_cols(dgs[m][rows, :], w_gate[...]) + inner_cols(dus[m][rows, :], w_up[...])
            ).astype(out.dtype)


def pick(ref, lead):
    return ref if lead is None else ref.at[lead]


def block_body(terms, lefts, rights, extra, from_side, turned, ids, *refs):
    left, refs = refs[:lefts], refs[lefts:]
    right, refs = refs[:rights], refs[rights:]
    added, out = refs[: extra + from_side], refs[-1]
    total = None
    for a, a_lead, b, b_lead, first, count in terms:
        rows = pick(right[b], b_lead)[first : first + count, :]
        term = inner_rows(pick(left[a], a_lead)[ids[0]], rows)
        total = term if total is None else total + term
    for i, ref in enumerate(added):
        total = total + (ref[ids[0]] if i >= extra else ref[...]).astype(F32)
    out[...] = jnp.transpose(total) if turned else total.astype(out.dtype)


def side_sum_body(terms, lefts, ids, *refs):
    left, right, out = refs[:lefts], refs[lefts:-1], refs[-1]
    for z in range(out.shape[0]):
        total = None
        for a, a_lead, b, b_lead, first, count in terms:
            rows = pick(right[b], b_lead)[first : first + count, :]
            term = inner_rows(pick(left[a], a_lead)[z], rows)
            total = term if total is None else total + term
        out[z] = total.astype(out.dtype)


def attend_back_body(
    scale, micro, chunk, ids, a0, a1, a2, out_proj, q_up, key_ids, *refs
):
    per = 7
    groups = [refs[m * per : (m + 1) * per] for m in range(micro)]
    dyl_out, dqp, send, keep, kv_send, kv_keep = refs[micro * per : micro * per + 6]
    dq_acc, do_acc, delta_acc = refs[-3:]
    sides = refs[micro * per + 6 : -3]
    for m in range(micro):
        q, kv, o, lse, row_ids, cos, sin = groups[m]
        heads, rows, wide = q.shape
        half_rows = rows // 2
        dyl = jnp.concatenate([a0[m], a1[m], a2[m]], 0)
        dyl_out[m] = dyl
        if sides:
            side_columns(dyl_out.at[m], sides[0].at[m], sides[1].at[m], ids[1])
        for h in range(heads):
            do = inner_cols(dyl, out_proj[h * wide : (h + 1) * wide, :]).astype(LOW)
            do_acc[h] = do
            delta = jnp.sum(
                do.astype(F32) * o[:, h * wide : (h + 1) * wide].astype(F32), axis=-1, keepdims=True
            )
            delta_acc[h] = jnp.transpose(jnp.broadcast_to(delta, (rows, 128)))[:8]
            dq_acc[h] = jnp.zeros((rows, wide), F32)
        count = kv.shape[0] // 2 // chunk
        for part, out in ((0, kv_keep), (1, kv_send)):

            def one(i, carry):
                base = pl.multiple_of((part * count + i) * chunk, chunk)
                keys = kv[pl.ds(base, chunk), :wide]
                values = kv[pl.ds(base, chunk), wide:]
                at = key_ids[pl.ds(base, chunk), :]
                bias = jnp.where((at >= row_ids[1:2, :]) & (at <= row_ids[0:1, :]), 0.0, NEG_LARGE)

                def head(h, sums):
                    dk, dv = sums
                    q_h, do_h = q[h], do_acc[h]
                    probs = jnp.exp(inner_cols(keys, q_h) + bias - lse[pl.ds(h, 1), :])
                    back = inner_cols(values, do_h) - delta_acc[h][:1]
                    ds = (probs * back).astype(LOW)
                    dv = dv + dot(probs.astype(LOW), do_h)
                    dk = dk + dot(ds, q_h)
                    dq_acc[h] = dq_acc[h] + inner_rows(ds, keys)
                    return dk, dv

                zero = jnp.zeros((chunk, wide), F32)
                dk, dv = lax.fori_loop(0, heads, head, (zero, zero))
                place = pl.ds(pl.multiple_of(i * chunk, chunk), chunk)
                out[m, place, :wide] = dk.astype(out.dtype)
                out[m, place, wide:] = dv.astype(out.dtype)
                return carry

            if count == 1:
                one(0, 0)
            else:
                lax.fori_loop(0, count, one, 0)
        for h in range(heads):
            dq = unrotate(dq_acc[h] * scale, cos[...], sin[...])
            dqp[m, :, h * wide : (h + 1) * wide] = dq.astype(LOW)
        low = dqp[m]
        send[m] = inner_cols(low[half_rows:], q_up[...]).astype(LOW)
        keep[m] = inner_cols(low[:half_rows], q_up[...])


def natural_body(micro, quarter, ids, a0, a1, a2, out):
    for m in range(micro):
        pieces = (a0[m], a1[m], a2[m, :quarter, :], a2[m, quarter:, :])
        for k, piece in zip(ORDER, pieces):
            out[m, pl.ds(pl.multiple_of((ids[0] ^ k) * quarter, quarter), quarter), :] = piece


def local(
    tokens,
    lengths,
    norm1_gain,
    q_down,
    latent_gain,
    q_up,
    kv_proj,
    out_proj,
    norm2_gain,
    w_gate,
    w_up,
    w_down,
    cotangent,
):
    micro, rows, width = tokens.shape
    seq = lax.axis_size("seq")
    line = seq // 2
    at = lax.axis_index("seq").astype(jnp.int32)
    me = lax.axis_index("mp").astype(jnp.int32)
    place, side = at // 2, at % 2
    ids = jnp.stack([me, side])
    quarter, half = rows // 4, rows // 2
    head_dim = kv_proj.shape[1] // 2
    heads = q_up.shape[1] // head_dim
    part = q_down.shape[1]
    rank = q_up.shape[0]
    hidden = w_gate.shape[1]
    kv_part = kv_proj.shape[1] // 4
    wide = width // seq
    scale = head_dim ** (-0.5)
    key_count = seq * rows
    beside = [(i, i ^ 1) for i in range(seq)]

    def swap(index):
        return ((index & 1) << 1) | (index >> 1)

    def to_natural(array, axis):
        size = array.shape[axis] // 4
        return jnp.concatenate(
            [lax.dynamic_slice_in_dim(array, swap(me ^ b) * size, size, axis) for b in range(4)],
            axis,
        )

    def other(array):
        return lax.ppermute(array, "seq", beside)

    def sum_mp(send, keep):
        kept = keep + lax.ppermute(send, "mp", CORE).astype(F32)
        got = lax.ppermute(kept[..., quarter:, :].astype(LOW), "mp", CROSS)
        return kept[..., :quarter, :] + got.astype(F32)

    def gather_mp(piece):
        near = lax.ppermute(piece, "mp", CROSS)
        pair = jnp.concatenate([piece, near], -2)
        return piece, near, lax.ppermute(pair, "mp", CORE)

    def sides_shape(columns, their_rows, lead=()):
        if columns // seq % 128:
            return []
        return [
            whole((*lead, line, n, columns // seq), LOW) for n in (rows, their_rows)
        ]

    def split_sides(made, full, their_rows):
        if made:
            return made
        split = full.reshape(*full.shape[:-1], line, 2, full.shape[-1] // seq)
        mine, theirs = (
            jnp.moveaxis(lax.dynamic_index_in_dim(split, i, split.ndim - 2, keepdims=False), -2, -3)
            for i in (side, 1 - side)
        )
        return mine, theirs[..., :their_rows, :]

    def from_other(theirs):
        got = other(theirs)
        return got, lax.ppermute(got, "mp", CORE)

    def without_sides(body, count):
        return body if count else lambda *refs: body(*refs, None, None)

    def both_sides(mine, got):
        lefts, spans = [], []
        for array, first, count, partner in (
            (mine, 0, rows, 0), (got[0], 0, half, 1), (got[1], half, half, 1)
        ):
            stacked_array = not isinstance(array, list)
            for m in range(micro):
                spans.append((len(lefts) if not stacked_array else len(lefts), m if stacked_array else None,
                              m, partner, first, count))
                if not stacked_array:
                    lefts.append(array[m])
            if stacked_array:
                lefts.append(array)
        return lefts, spans

    class Chain:
        def __init__(self, lefts, rights, terms, shape, turned=False, from_side=None):
            self.args = [*lefts, *rights]
            self.spec = (terms, len(lefts), len(rights))
            self.shape, self.turned = shape, turned
            self.from_side = [] if from_side is None else [from_side]
            self.step, self.up, self.down = 0, None, None

        def block(self, index, added, after, last=False):
            turned = last and self.turned
            body = functools.partial(
                block_body, *self.spec, len(added), len(self.from_side), turned
            )
            shape = self.shape[::-1] if turned else self.shape
            return run(
                body, index.reshape(1), [*self.args, *added, *self.from_side],
                [whole(shape, F32 if last else LOW)], after, name="block",
            )[0]

        def advance(self, after):
            self.step += 1
            step = self.step
            goes_up = [(i, i + 2) for i in range(2 * step)]
            goes_down = [(seq - 1 - i, seq - 3 - i) for i in range(2 * step)]
            for_up, for_down = line - step + place, step - line + place
            if 2 * step < line + 1:
                which = jnp.where(
                    place <= step - 1, for_up, jnp.where(place >= line - step, for_down, 0)
                )
                term = self.block(which, [a for a in (self.up, self.down) if a is not None], after)
                if step == 1 and line > 3:
                    self.up = lax.ppermute(term, "seq", goes_up + goes_down)
                else:
                    self.up = lax.ppermute(term, "seq", goes_up)
                    self.down = lax.ppermute(term, "seq", goes_down)
                return [term]
            term_up = self.block(jnp.clip(for_up, 0, line - 1), [self.up], after)
            term_down = self.block(jnp.clip(for_down, 0, line - 1), [self.down], [term_up])
            self.up = lax.ppermute(term_up, "seq", goes_up)
            self.down = lax.ppermute(term_down, "seq", goes_down)
            return [term_down]

        def finish(self, after):
            while self.step < line - 1:
                after = self.advance(after)
            result = self.block(place, [self.up, self.down], after, last=True)
            return result, [result]

    quarter_rows = jnp.arange(quarter, dtype=jnp.int32)
    row_ids = at * rows + jnp.concatenate([(me ^ k) * quarter + quarter_rows for k in ORDER])
    key_ids = (
        ((place - jnp.arange(line, dtype=jnp.int32)[None, None, :, None, None]) * 2
         + (side ^ jnp.arange(2, dtype=jnp.int32)[None, :, None, None, None])) * rows
        + (me ^ (jnp.arange(2, dtype=jnp.int32)[:, None, None, None, None]
                 + 2 * jnp.arange(2, dtype=jnp.int32)[None, None, None, :, None])) * quarter
        + quarter_rows[None, None, None, None, :]
    ).reshape(key_count)

    gain1_row, gain2_row, gain_c_row = norm1_gain[None, :], norm2_gain[None, :], latent_gain[None, :]
    kv_cols = lax.dynamic_slice_in_dim(kv_proj, me * kv_part, kv_part, 1)
    first_weights = jnp.concatenate([q_down, kv_cols], axis=1)
    both_rows = sides_shape(width, rows)
    half_rows = sides_shape(width, half)
    rank_sides = sides_shape(rank, rows)

    tables, starts, kv, c_part, h1_sides = [], [], [], [], []
    order = []
    for m in range(micro):
        _, places = documents(lengths[m], row_ids)
        starts.append(row_ids - places)
        tables.append(rotation(places, head_dim))
        c, packed, h1, *made = run(
            without_sides(functools.partial(first_body, m, quarter), len(both_rows)),
            ids,
            [tokens, gain1_row, q_down, kv_proj, *tables[m]],
            [whole((rows, part), LOW), whole((half, 2 * head_dim), LOW), whole((rows, width), LOW),
             *both_rows],
            order,
            name="first",
        )
        order = [c]
        blocks = [packed] + [
            lax.ppermute(packed, "seq", [(i, i + 2 * d) for i in range(seq - 2 * d)])
            for d in range(1, line)
        ]
        near = jnp.stack(blocks, 0)
        near = jnp.stack([near, other(near)], 0)
        kv.append(
            jnp.stack([near, lax.ppermute(near, "mp", CORE)], 0).reshape(key_count, 2 * head_dim)
        )
        c_part.append(c)
        h1_sides.append(split_sides(made, h1, rows))

    dhid, dz, *made = run(
        functools.partial(cotangent_body, micro, quarter),
        ids,
        [cotangent, w_down],
        [whole((micro, rows, hidden), F32), whole((micro, rows, width), LOW),
         *sides_shape(width, half, (micro,))],
        order,
        name="cotangent",
    )
    order = [dz]
    dz_mine, dz_theirs = split_sides(made, dz, half)
    dz_got = from_other(dz_theirs)

    qn_sides, qs, os, lses, sums, c_rows = [], [], [], [], [], []
    for m in range(micro):
        near = lax.ppermute(c_part[m], "mp", CROSS)
        swapped = jnp.concatenate(
            [near[quarter : 2 * quarter], near[:quarter], near[3 * quarter :],
             near[2 * quarter : 3 * quarter]], 0
        )
        far = lax.ppermute(jnp.concatenate([c_part[m], swapped], 1), "mp", CORE)
        qn, q, o, lse, send, keep, *made = run(
            without_sides(functools.partial(attend_body, scale), len(rank_sides)),
            ids,
            [c_part[m], near, far, gain_c_row, q_up, *tables[m], kv[m], key_ids[None, :],
             row_ids[:, None], starts[m][:, None], out_proj],
            [whole((rows, rank), LOW), whole((heads, rows, head_dim), LOW),
             whole((rows, heads * head_dim), LOW), whole((heads, rows), F32),
             whole((half, width), LOW), whole((half, width), F32), *rank_sides],
            order,
            name="attend",
        )
        order = [o]
        qn_sides.append(split_sides(made, qn, rows))
        qs.append(q)
        os.append(o)
        lses.append(lse)
        sums.append(sum_mp(send, keep))
        c_rows.append(
            jnp.concatenate([c_part[m][:quarter], swapped[:quarter], far[half : half + quarter]], 1)
        )

    h2_mine, h2_got, hid, dg, du, state = [], [], [], [], [], []
    for m in range(micro):
        x = lax.dynamic_slice_in_dim(tokens[m], me * quarter, quarter, 0).astype(F32)
        inv1 = inverse_rms(x)
        y = x + sums[m]
        inv2 = inverse_rms(y)
        n2 = y * inv2
        pieces = gather_mp((n2 * gain2_row).astype(LOW))
        h2, hid_m, dg_m, du_m, *made = run(
            without_sides(functools.partial(forward_body, m), len(half_rows)),
            ids,
            [*pieces, w_gate, w_up, dhid],
            [whole((rows, width), LOW), *[whole((rows, hidden), LOW)] * 3, *half_rows],
            order,
            name="forward",
        )
        order = [hid_m]
        mine, theirs = split_sides(made, h2, half)
        h2_mine.append(mine)
        h2_got.append(from_other(theirs))
        hid.append(hid_m)
        dg.append(dg_m)
        du.append(du_m)
        state.append(dict(x=x, n1=x * inv1, inv1=inv1, y=y, n2=n2, inv2=inv2, c=c_rows[m]))

    def stacked(name):
        return jnp.stack([st[name] for st in state], 0)

    def with_other(arrays):
        return [*arrays, *[other(a) for a in arrays]]

    def terms_of(spans):
        return [(a, lead, m + micro * partner, None, first, count)
                for a, lead, m, partner, first, count in spans]

    lefts, spans = both_sides(dz_mine, dz_got)
    chain_down = Chain(lefts, with_other(hid), terms_of(spans), (wide, hidden), turned=True)
    lefts, spans = both_sides(h2_mine, [list(p) for p in zip(*h2_got)])
    chain_gate = Chain(lefts, with_other(dg), terms_of(spans), (wide, hidden))
    chain_up = Chain(lefts, with_other(du), terms_of(spans), (wide, hidden))

    send, keep = run(
        functools.partial(hidden_back_body, micro),
        ids,
        [*dg, *du, w_gate, w_up],
        [whole((micro, half, width), LOW), whole((micro, half, width), F32)],
        order,
        name="hidden_back",
    )
    order = chain_down.advance([send])
    dh2 = sum_mp(send, keep)
    y, n2, inv2, n1, inv1 = (stacked(k) for k in ("y", "n2", "inv2", "n1", "inv1"))
    dz_own = dz[:, :quarter].astype(F32)
    gain2 = jnp.sum(dh2 * n2, axis=(0, 1))
    dy = dz_own + norm_backward(dh2 * gain2_row, n2, inv2)
    for _ in range(2):
        order = chain_down.advance(order)
    order = chain_gate.advance(order)

    def attend_back(which, pieces):
        args = [*pieces, out_proj, q_up, key_ids[:, None]]
        for m in which:
            args += [qs[m], kv[m], os[m], lses[m], jnp.stack([row_ids, starts[m]], 0), *tables[m]]
        n = len(which)
        return run(
            functools.partial(attend_back_body, scale, n, min(1024, key_count // 2)),
            ids,
            args,
            [whole((n, rows, width), LOW), whole((n, rows, heads * head_dim), LOW),
             whole((n, half, rank), LOW), whole((n, half, rank), F32),
             whole((n, key_count // 2, 2 * head_dim), LOW),
             whole((n, key_count // 2, 2 * head_dim), F32), *sides_shape(width, half, (n,))],
            order,
            scratch=[pltpu.VMEM((heads, rows, head_dim), F32),
                     pltpu.VMEM((heads, rows, head_dim), LOW),
                     pltpu.VMEM((heads, 8, rows), F32)],
            name="attend_back",
            limit=56,
        )

    pieces = gather_mp(dy.astype(LOW))
    if key_count <= 2048:
        made = attend_back(range(micro), pieces)
    else:
        each = [attend_back([m], [p[m : m + 1] for p in pieces]) for m in range(micro)]
        made = [jnp.concatenate(parts, 0) for parts in zip(*each)]
    dyl, dqp, send, keep, kv_send, kv_keep, *made = made
    order = [send]
    dyl_mine, dyl_theirs = split_sides(made, dyl, half)
    lefts, spans = both_sides(dyl_mine, from_other(dyl_theirs))
    chain_out = Chain(lefts, with_other(os), terms_of(spans), (wide, heads * head_dim), turned=True)

    def side_sum(lefts, rights, shape, after):
        terms = [(m, None, 0, m, 0, rows) for m in range(micro)]
        (made,) = run(
            functools.partial(side_sum_body, terms, len(lefts)),
            ids,
            [*lefts, *rights],
            [whole((line, *shape), LOW)],
            after,
            name="side_sum",
        )
        return other(made), [made]

    def own_chain(side_pairs, right, shape, after):
        from_side, after = side_sum([p[1] for p in side_pairs], [right], shape, after)
        terms = [(m, None, 0, m, 0, rows) for m in range(micro)]
        return Chain([p[0] for p in side_pairs], [right], terms, shape, from_side=from_side), after

    shape = (rank // seq, heads * head_dim)
    chain_qup, order = own_chain(qn_sides, dqp, shape, order)
    order = chain_gate.advance(order)
    order = chain_up.advance(order)

    dqn = sum_mp(send, keep)
    c = stacked("c").astype(F32)
    inv_c = inverse_rms(c)
    chat = c * inv_c
    chat = to_natural(chat, 2)
    gain_c = jnp.sum(dqn * chat, axis=(0, 1))
    dc = norm_backward(dqn * gain_c_row, chat, inv_c).astype(LOW)

    dkv = kv_keep + lax.ppermute(kv_send, "mp", CORE).astype(F32)
    dkv = dkv.reshape(micro, 2, line, 2, quarter, 2 * head_dim)
    dkv = dkv[:, :, :, 0] + lax.ppermute(dkv[:, :, :, 1].astype(LOW), "mp", CROSS).astype(F32)
    dkv = dkv[:, 0] + other(dkv[:, 1].astype(LOW)).astype(F32)
    total = dkv[:, 0]
    for d in range(1, line):
        total = total + lax.ppermute(
            dkv[:, d].astype(LOW), "seq", [(i + 2 * d, i) for i in range(seq - 2 * d)]
        ).astype(F32)
    cosine = jnp.stack([t[0][:quarter] for t in tables], 0)
    sine = jnp.stack([t[1][:quarter] for t in tables], 0)
    dkv_low = jnp.concatenate(
        [unrotate(total[..., :head_dim], cosine, sine), total[..., head_dim:]], axis=-1
    ).astype(LOW)
    both = jnp.concatenate(gather_mp(jnp.concatenate([dc, dkv_low], -1)), -2)
    dfirst = jnp.concatenate(
        [lax.dynamic_slice_in_dim(both, me * part, part, 2),
         lax.dynamic_slice_in_dim(both, rank + me * kv_part, kv_part, 2)], -1
    )

    grad_down, order = chain_down.finish(order)
    order = chain_gate.advance(order)
    order = chain_up.advance(order)
    order = chain_out.advance(order)
    grad_gate, order = chain_gate.finish(order)
    order = chain_up.advance(order)
    order = chain_out.advance(order)
    grad_up, order = chain_up.finish(order)
    order = chain_qup.advance(order)
    order = chain_out.advance(order)
    chain_first, order = own_chain(h1_sides, dfirst, (wide, part + kv_part), order)
    order = chain_qup.advance(order)
    grad_out, order = chain_out.finish(order)
    order = chain_first.advance(order)
    order = chain_qup.advance(order)
    order = chain_first.advance(order)
    grad_qup, order = chain_qup.finish(order)
    order = chain_first.advance(order)
    grad_first, order = chain_first.finish(order)

    grad_qdown = grad_first[:, :part]
    kv_cols_grad = grad_first[:, part:]
    pieces = []
    for k in ORDER:
        size = kv_cols_grad.shape[0] // 4
        sent = lax.dynamic_slice_in_dim(kv_cols_grad, (me ^ k) * size, size, 0)
        pieces.append(lax.ppermute(sent, "mp", [(i, i ^ k) for i in range(4)]) if k else sent)
    grad_kv = to_natural(jnp.concatenate(pieces, 1), 1)

    def put_natural(pieces):
        return run(
            functools.partial(natural_body, micro, quarter),
            ids,
            pieces,
            [whole((micro, rows, width), LOW)],
            name="natural",
        )[0]

    part_sum = inner_cols(dfirst.reshape(micro * rows, -1), first_weights).reshape(micro, rows, width)
    dh1 = sum_mp(part_sum[:, half:].astype(LOW), part_sum[:, :half])
    gain1 = jnp.sum(dh1 * n1, axis=(0, 1))
    dx = (dy + norm_backward(dh1 * gain1_row, n1, inv1)).astype(LOW)
    input_grads = put_natural(gather_mp(dx))

    ffn = [dot(hid[m], w_down) for m in range(micro)]
    ffn = sum_mp(
        jnp.stack([f[half:] for f in ffn], 0).astype(LOW), jnp.stack([f[:half] for f in ffn], 0)
    )
    layer_out = put_natural(gather_mp((y + ffn).astype(LOW)))

    gains = jnp.concatenate(
        [gain1.reshape(seq, -1), gain2.reshape(seq, -1), gain_c.reshape(seq, -1)], axis=1
    )
    gains = gains + lax.ppermute(gains, "mp", CORE)
    gains = gains + lax.ppermute(gains, "mp", CROSS)
    gain_sum = lax.dynamic_index_in_dim(gains, at, 0, keepdims=False)
    for k in range(1, seq):
        gain_sum = gain_sum + lax.ppermute(
            lax.dynamic_index_in_dim(gains, at ^ k, 0, keepdims=False),
            "seq",
            [(i, i ^ k) for i in range(seq)],
        )
    return (
        layer_out,
        input_grads,
        gain_sum[:wide],
        grad_qdown,
        gain_sum[2 * wide :],
        grad_qup,
        grad_kv,
        grad_out,
        gain_sum[wide : 2 * wide],
        grad_gate,
        grad_up,
        grad_down,
    )


def solution(mesh):
    placed = (
        P(None, "seq", None),
        P(),
        P(),
        P(None, "mp"),
        P(),
        P(None, "mp"),
        P(),
        P("mp", None),
        P(),
        P(None, "mp"),
        P(None, "mp"),
        P("mp", None),
        P(None, "seq", None),
    )
    return jax.shard_map(
        local,
        mesh=mesh,
        in_specs=placed,
        out_specs=(
            P(None, "seq", None),
            P(None, "seq", None),
            P("seq"),
            P("seq", "mp"),
            P("seq"),
            P("seq", "mp"),
            P(("seq", "mp"), None),
            P("mp", "seq"),
            P("seq"),
            P("seq", "mp"),
            P("seq", "mp"),
            P("mp", "seq"),
        ),
        check_vma=False,
    )
```

```python
import functools

import jax
import jax.numpy as jnp
from jax import lax
from jax.experimental import pallas as pl
from jax.experimental.pallas import tpu as pltpu
from jax.sharding import PartitionSpec as P

EPS = 1e-06
BASE = 10000.0
NEG_LARGE = -1e30
LOW = jnp.bfloat16
F32 = jnp.float32
ORDER = (0, 2, 1, 3)
CORE = [(i, i ^ 1) for i in range(4)]
CROSS = [(i, i ^ 2) for i in range(4)]


def inverse_rms(values):
    return lax.rsqrt(jnp.mean(values * values, axis=-1, keepdims=True) + EPS)


def norm_backward(grad_hat, normed, inverse):
    return inverse * (grad_hat - normed * jnp.mean(grad_hat * normed, axis=-1, keepdims=True))


def dot(left, right):
    return jnp.dot(left, right, preferred_element_type=F32)


def inner_rows(left, right):
    return lax.dot_general(left, right, (((0,), (0,)), ((), ())), preferred_element_type=F32)


def inner_cols(left, right):
    return lax.dot_general(left, right, (((1,), (1,)), ((), ())), preferred_element_type=F32)


def documents(lengths_row, rows):
    first_end = lengths_row[0]
    second_end = first_end + lengths_row[1]
    doc_ids = (rows >= first_end).astype(jnp.int32) + (rows >= second_end).astype(jnp.int32)
    starts = jnp.where(rows >= second_end, second_end, jnp.where(rows >= first_end, first_end, 0))
    return (doc_ids, rows - starts)


def rotation(positions, head_dim):
    half = head_dim // 2
    freqs = BASE ** (-2.0 * jnp.arange(half, dtype=F32) / head_dim)
    angles = positions.astype(F32)[:, None] * freqs[None, :]
    return (jnp.cos(angles), jnp.sin(angles))


def rotate(values, cosine, sine):
    half = values.shape[-1] // 2
    first = values[..., :half]
    second = values[..., half:]
    return jnp.concatenate(
        [first * cosine - second * sine, second * cosine + first * sine], axis=-1
    )


def unrotate(grads, cosine, sine):
    return rotate(grads, cosine, -sine)


def in_vmem():
    return pl.BlockSpec(memory_space=pltpu.VMEM)


def whole(shape, dtype):
    return jax.ShapeDtypeStruct(shape, dtype)


def run(body, ids, args, outs, after=(), scratch=(), name=None, limit=40):
    args, after = list(args), list(after)

    def without(*refs):
        body(*refs[: 1 + len(args)], *refs[1 + len(args) + len(after) :])

    return pl.pallas_call(
        without,
        grid_spec=pltpu.PrefetchScalarGridSpec(
            num_scalar_prefetch=1,
            grid=(1,),
            in_specs=[in_vmem()] * len(args) + [pl.BlockSpec(memory_space=pl.ANY)] * len(after),
            out_specs=[in_vmem()] * len(outs),
            scratch_shapes=list(scratch),
        ),
        out_shape=list(outs),
        cost_estimate=pl.CostEstimate(flops=1000, bytes_accessed=1000, transcendentals=0),
        compiler_params=pltpu.CompilerParams(vmem_limit_bytes=limit << 20),
        name=name,
    )(ids, *args, *after)


def side_columns(source, mine, theirs, side):
    line, _, wide = mine.shape
    rows = theirs.shape[1]
    for z in range(line):
        mine[z] = source[:, pl.ds(pl.multiple_of((2 * z + side) * wide, wide), wide)]
        theirs[z] = source[:rows, pl.ds(pl.multiple_of((2 * z + 1 - side) * wide, wide), wide)]


def first_body(m, quarter, ids, x_ref, gain, q_down, kv_proj, cos, sin, c, kv, h1, mine, theirs):
    blocks = [
        x_ref[m, pl.ds(pl.multiple_of((ids[0] ^ k) * quarter, quarter), quarter), :] for k in ORDER
    ]
    x = jnp.concatenate(blocks, 0).astype(F32)
    low = (x * inverse_rms(x) * gain[...]).astype(LOW)
    h1[...] = low
    half = 2 * quarter
    pair = dot(low[:half], kv_proj[...])
    wide = kv_proj.shape[1] // 2
    kv[:, :wide] = rotate(pair[:, :wide], cos[:half], sin[:half]).astype(LOW)
    kv[:, wide:] = pair[:, wide:].astype(LOW)
    c[...] = dot(low, q_down[...]).astype(LOW)
    if mine is not None:
        side_columns(h1, mine, theirs, ids[1])


def cotangent_body(micro, quarter, ids, z_ref, w_down, dhid, dz, *sides):
    for m in range(micro):
        blocks = [
            z_ref[m, pl.ds(pl.multiple_of((ids[0] ^ k) * quarter, quarter), quarter), :]
            for k in ORDER
        ]
        dz[m] = jnp.concatenate(blocks, 0)
        if sides:
            side_columns(dz.at[m], sides[0].at[m], sides[1].at[m], ids[1])
        dhid[m] = inner_cols(dz[m], w_down[...])


def attend_body(
    scale, ids, c0, c1, c2, gain, q_up, cos, sin, kv, key_ids, row_ids, row_starts, out_proj,
    qn, q, o, lse, send, keep, mine, theirs,
):
    rows = qn.shape[0]
    quarter = rows // 4
    part = c0.shape[1]
    wide = q.shape[2]
    got = c1[...]
    pair = jnp.concatenate(
        [got[quarter : 2 * quarter], got[:quarter], got[3 * quarter :], got[2 * quarter : 3 * quarter]],
        0,
    )
    far = jnp.concatenate([c2[2 * quarter :], c2[: 2 * quarter]], 0)
    c = jnp.concatenate([c0[...], pair, far], 1).astype(F32)
    chat = c * inverse_rms(c)
    for k, xor in enumerate(ORDER):
        columns = pl.ds(pl.multiple_of((ids[0] ^ xor) * part, part), part)
        qn[:, columns] = (chat[:, k * part : (k + 1) * part] * gain[:, columns]).astype(LOW)
    if mine is not None:
        side_columns(qn, mine, theirs, ids[1])
    bias = jnp.where(
        (key_ids[...] >= row_starts[...]) & (key_ids[...] <= row_ids[...]), 0.0, NEG_LARGE
    )
    low = qn[...]
    keys, values = kv[:, :wide], kv[:, wide:]
    for h in range(q.shape[0]):
        pre = dot(low, q_up[:, h * wide : (h + 1) * wide])
        q_h = (rotate(pre, cos[...], sin[...]) * scale).astype(LOW)
        q[h] = q_h
        scores = inner_cols(q_h, keys) + bias
        top = jnp.max(scores, axis=-1, keepdims=True)
        probs = jnp.exp(scores - top)
        total = jnp.sum(probs, axis=-1, keepdims=True)
        out = dot(probs.astype(LOW), values) / total
        o[:, h * wide : (h + 1) * wide] = out.astype(LOW)
        log_total = jnp.broadcast_to(top + jnp.log(total), (rows, 128))
        lse[h : h + 1, :] = jnp.transpose(log_total)[:1]
    half = 2 * quarter
    send[...] = dot(o[half:, :], out_proj[...]).astype(LOW)
    keep[...] = dot(o[:half, :], out_proj[...])


def forward_body(m, ids, a0, a1, a2, w_gate, w_up, dhid, h2, hid, dg, du, mine, theirs):
    h2[...] = jnp.concatenate([a0[...], a1[...], a2[...]], 0)
    if mine is not None:
        side_columns(h2, mine, theirs, ids[1])
    low = h2[...]
    g = dot(low, w_gate[...])
    u = dot(low, w_up[...])
    sig = jax.nn.sigmoid(g)
    swish = g * sig
    hid[...] = (swish * u).astype(LOW)
    back = dhid[m]
    dg[...] = (back * u * sig * (1.0 + g * (1.0 - sig))).astype(LOW)
    du[...] = (back * swish).astype(LOW)


def hidden_back_body(micro, ids, *refs):
    dgs, dus = refs[:micro], refs[micro : 2 * micro]
    w_gate, w_up, send, keep = refs[2 * micro :]
    half = send.shape[1]
    for m in range(micro):
        for rows, out in ((slice(half, None), send), (slice(0, half), keep)):
            out[m] = (
                inner_cols(dgs[m][rows, :], w_gate[...]) + inner_cols(dus[m][rows, :], w_up[...])
            ).astype(out.dtype)


def pick(ref, lead):
    return ref if lead is None else ref.at[lead]


def block_body(terms, lefts, rights, extra, from_side, turned, ids, *refs):
    left, refs = refs[:lefts], refs[lefts:]
    right, refs = refs[:rights], refs[rights:]
    added, out = refs[: extra + from_side], refs[-1]
    total = None
    for a, a_lead, b, b_lead, first, count in terms:
        rows = pick(right[b], b_lead)[first : first + count, :]
        term = inner_rows(pick(left[a], a_lead)[ids[0]], rows)
        total = term if total is None else total + term
    for i, ref in enumerate(added):
        total = total + (ref[ids[0]] if i >= extra else ref[...]).astype(F32)
    out[...] = jnp.transpose(total) if turned else total.astype(out.dtype)


def side_sum_body(terms, lefts, ids, *refs):
    left, right, out = refs[:lefts], refs[lefts:-1], refs[-1]
    for z in range(out.shape[0]):
        total = None
        for a, a_lead, b, b_lead, first, count in terms:
            rows = pick(right[b], b_lead)[first : first + count, :]
            term = inner_rows(pick(left[a], a_lead)[z], rows)
            total = term if total is None else total + term
        out[z] = total.astype(out.dtype)


def attend_back_body(
    scale, micro, chunk, ids, a0, a1, a2, out_proj, q_up, key_ids, *refs
):
    per = 7
    groups = [refs[m * per : (m + 1) * per] for m in range(micro)]
    dyl_out, dqp, send, keep, kv_send, kv_keep = refs[micro * per : micro * per + 6]
    dq_acc, do_acc, delta_acc = refs[-3:]
    sides = refs[micro * per + 6 : -3]
    for m in range(micro):
        q, kv, o, lse, row_ids, cos, sin = groups[m]
        heads, rows, wide = q.shape
        half_rows = rows // 2
        dyl = jnp.concatenate([a0[m], a1[m], a2[m]], 0)
        dyl_out[m] = dyl
        if sides:
            side_columns(dyl_out.at[m], sides[0].at[m], sides[1].at[m], ids[1])
        for h in range(heads):
            do = inner_cols(dyl, out_proj[h * wide : (h + 1) * wide, :]).astype(LOW)
            do_acc[h] = do
            delta = jnp.sum(
                do.astype(F32) * o[:, h * wide : (h + 1) * wide].astype(F32), axis=-1, keepdims=True
            )
            delta_acc[h] = jnp.transpose(jnp.broadcast_to(delta, (rows, 128)))[:8]
            dq_acc[h] = jnp.zeros((rows, wide), F32)
        count = kv.shape[0] // 2 // chunk
        for part, out in ((0, kv_keep), (1, kv_send)):

            def one(i, carry):
                base = pl.multiple_of((part * count + i) * chunk, chunk)
                keys = kv[pl.ds(base, chunk), :wide]
                values = kv[pl.ds(base, chunk), wide:]
                at = key_ids[pl.ds(base, chunk), :]
                bias = jnp.where((at >= row_ids[1:2, :]) & (at <= row_ids[0:1, :]), 0.0, NEG_LARGE)

                def head(h, sums):
                    dk, dv = sums
                    q_h, do_h = q[h], do_acc[h]
                    probs = jnp.exp(inner_cols(keys, q_h) + bias - lse[pl.ds(h, 1), :])
                    back = inner_cols(values, do_h) - delta_acc[h][:1]
                    ds = (probs * back).astype(LOW)
                    dv = dv + dot(probs.astype(LOW), do_h)
                    dk = dk + dot(ds, q_h)
                    dq_acc[h] = dq_acc[h] + inner_rows(ds, keys)
                    return dk, dv

                zero = jnp.zeros((chunk, wide), F32)
                dk, dv = lax.fori_loop(0, heads, head, (zero, zero))
                place = pl.ds(pl.multiple_of(i * chunk, chunk), chunk)
                out[m, place, :wide] = dk.astype(out.dtype)
                out[m, place, wide:] = dv.astype(out.dtype)
                return carry

            if count == 1:
                one(0, 0)
            else:
                lax.fori_loop(0, count, one, 0)
        for h in range(heads):
            dq = unrotate(dq_acc[h] * scale, cos[...], sin[...])
            dqp[m, :, h * wide : (h + 1) * wide] = dq.astype(LOW)
        low = dqp[m]
        send[m] = inner_cols(low[half_rows:], q_up[...]).astype(LOW)
        keep[m] = inner_cols(low[:half_rows], q_up[...])


def natural_body(micro, quarter, ids, a0, a1, a2, out):
    for m in range(micro):
        pieces = (a0[m], a1[m], a2[m, :quarter, :], a2[m, quarter:, :])
        for k, piece in zip(ORDER, pieces):
            out[m, pl.ds(pl.multiple_of((ids[0] ^ k) * quarter, quarter), quarter), :] = piece


class Wire:
    def __init__(self, sends, recvs):
        self.sends, self.recvs, self.used = sends, recvs, 0
        self.seq, self.mp = lax.axis_index("seq"), lax.axis_index("mp")
        self.place, self.side = self.seq // 2, self.seq % 2
        core, cross = self.mp % 2, self.mp // 2
        self.blocks = (
            self.mp, 2 * (1 - cross) + core, 2 * cross + 1 - core, 2 * (1 - cross) + 1 - core
        )
        self.core, self.cross = {"mp": self.blocks[2]}, {"mp": self.blocks[1]}
        self.beside = {"seq": self.seq + 1 - 2 * self.side}
        self.up, self.down = {"seq": self.seq + 2}, {"seq": self.seq - 2}

    def copy(self, source, target, device):
        at = self.used
        self.used += 1
        return pltpu.make_async_remote_copy(
            src_ref=source, dst_ref=target, send_sem=self.sends.at[at], recv_sem=self.recvs.at[at],
            device_id=device, device_id_type=pl.DeviceIdType.MESH,
        )

    def send(self, source, target, device):
        made = self.copy(source, target, device)
        made.start()
        return made

    def greet(self, line, far=1):
        barrier = pltpu.get_barrier_semaphore()
        for device in (self.core, self.cross, self.beside):
            pl.semaphore_signal(barrier, 1, device_id=device, device_id_type=pl.DeviceIdType.MESH)
        for d in range(1, far + 1):
            for way, there in ((1, self.place < line - d), (-1, self.place >= d)):

                @pl.when(there)
                def _():
                    pl.semaphore_signal(
                        barrier, 1, device_id={"seq": self.seq + 2 * way * d},
                        device_id_type=pl.DeviceIdType.MESH,
                    )
        below, above = jnp.minimum(self.place, far), jnp.minimum(line - 1 - self.place, far)
        pl.semaphore_wait(barrier, 3 + below + above)


class LineSum:
    def __init__(self, wire, term, room, rows, columns, keep):
        got, out = room
        view = lambda ref, i: ref.at[i, :rows, :columns]
        self.place, self.term, self.keep = wire.place, term, keep
        self.got = [view(got, i) for i in range(5)]
        self.out = [view(out, i) for i in range(3)]
        one, two_up, two_down, three_up, three_down = self.got
        a, b, c = self.out
        self.one = wire.copy(a, one, wire.up), wire.copy(a, one, wire.down)
        self.two = wire.copy(b, two_up, wire.up), wire.copy(b, two_down, wire.down)
        self.three = wire.copy(a, three_up, wire.up), wire.copy(c, three_down, wire.down)

    def clear(self):
        place = self.place
        for ref, empty in zip(
            self.got, ((place == 0) | (place == 3),) * 3 + (place == 0, place == 3)
        ):

            @pl.when(empty)
            def _(ref=ref):
                ref[...] = jnp.zeros(ref.shape, ref.dtype)

    def step1(self):
        place = self.place

        @pl.when((place == 0) | (place == 3))
        def _():
            self.out[0][...] = self.term(3 - place).astype(LOW)

        pl.when(place == 0)(self.one[0].start)
        pl.when(place == 3)(self.one[1].start)

    def step2(self):
        place = self.place
        pl.when(place == 1)(self.one[0].wait_recv)
        pl.when(place == 2)(self.one[1].wait_recv)
        self.out[1][...] = (
            self.term((place + 2) % 4) + self.got[0][...].astype(F32)
        ).astype(LOW)
        pl.when(place <= 1)(self.two[0].start)
        pl.when(place >= 2)(self.two[1].start)

    def step3(self):
        place = self.place

        @pl.when((place == 1) | (place == 2))
        def _():
            self.two[0].wait_recv()
            self.two[1].wait_recv()

        pl.when(place == 0)(self.one[0].wait_send)
        pl.when(place == 3)(self.one[1].wait_send)

        @pl.when(place <= 2)
        def _():
            self.out[0][...] = (self.term(place + 1) + self.got[1][...].astype(F32)).astype(LOW)
            self.three[0].start()

        @pl.when(place >= 1)
        def _():
            self.out[2][...] = (self.term(place - 1) + self.got[2][...].astype(F32)).astype(LOW)
            self.three[1].start()

    def finish(self):
        place = self.place
        pl.when(place >= 1)(self.three[0].wait_recv)
        pl.when(place <= 2)(self.three[1].wait_recv)
        self.keep(
            self.term(place) + self.got[3][...].astype(F32) + self.got[4][...].astype(F32)
        )

    def settle(self):
        place = self.place
        pl.when(place <= 1)(self.two[0].wait_send)
        pl.when(place >= 2)(self.two[1].wait_send)
        pl.when(place <= 2)(self.three[0].wait_send)
        pl.when(place >= 1)(self.three[1].wait_send)


def mesh_run(body, args, outs, scratch, number, name, limit, sends):
    return pl.pallas_call(
        body,
        in_specs=[in_vmem() if kind else pl.BlockSpec(memory_space=pl.ANY) for kind, _ in args],
        out_specs=[in_vmem() if kind else pl.BlockSpec(memory_space=pl.ANY) for kind, _ in outs],
        out_shape=[shape for _, shape in outs],
        scratch_shapes=[
            *scratch, pltpu.SemaphoreType.DMA((sends,)), pltpu.SemaphoreType.DMA((sends,))
        ],
        cost_estimate=pl.CostEstimate(flops=1000, bytes_accessed=1000, transcendentals=0),
        compiler_params=pltpu.CompilerParams(
            collective_id=number, has_side_effects=True, vmem_limit_bytes=limit << 20
        ),
        name=name,
    )(*[array for _, array in args])


def attend_back_one(
    scale, chunk, dyl, out_proj, q_up, key_ids, q, kv, o, lse, row_ids, cos, sin,
    dqp, send, keep, kv_send, kv_keep, dq_acc, do_acc, delta_acc,
):
    heads, rows, wide = q.shape
    half_rows = rows // 2
    low = dyl[...]
    for h in range(heads):
        do = inner_cols(low, out_proj[h * wide : (h + 1) * wide, :]).astype(LOW)
        do_acc[h] = do
        delta = jnp.sum(
            do.astype(F32) * o[:, h * wide : (h + 1) * wide].astype(F32), axis=-1, keepdims=True
        )
        delta_acc[h] = jnp.transpose(jnp.broadcast_to(delta, (rows, 128)))[:8]
        dq_acc[h] = jnp.zeros((rows, wide), F32)
    count = kv.shape[0] // 2 // chunk
    for part, out in ((0, kv_keep), (1, kv_send)):
        for i in range(count):
            base = (part * count + i) * chunk
            keys = kv[base : base + chunk, :wide]
            values = kv[base : base + chunk, wide:]
            at = key_ids[base : base + chunk, :]
            bias = jnp.where((at >= row_ids[1:2, :]) & (at <= row_ids[0:1, :]), 0.0, NEG_LARGE)

            def head(h, sums):
                dk, dv = sums
                q_h, do_h = q[h], do_acc[h]
                probs = jnp.exp(inner_cols(keys, q_h) + bias - lse[pl.ds(h, 1), :])
                back = inner_cols(values, do_h) - delta_acc[h][:1]
                ds = (probs * back).astype(LOW)
                dv = dv + dot(probs.astype(LOW), do_h)
                dk = dk + dot(ds, q_h)
                dq_acc[h] = dq_acc[h] + inner_rows(ds, keys)
                return dk, dv

            zero = jnp.zeros((chunk, wide), F32)
            dk, dv = lax.fori_loop(0, heads, head, (zero, zero))
            out[i * chunk : (i + 1) * chunk, :wide] = dk.astype(out.dtype)
            out[i * chunk : (i + 1) * chunk, wide:] = dv.astype(out.dtype)
    for h in range(heads):
        dq = unrotate(dq_acc[h] * scale, cos[...], sin[...])
        dqp[:, h * wide : (h + 1) * wide] = dq.astype(LOW)
    low = dqp[...]
    send[...] = inner_cols(low[half_rows:], q_up[...]).astype(LOW)
    keep[...] = inner_cols(low[:half_rows], q_up[...])


def mean_of(values):
    return jnp.mean(values, axis=-1, keepdims=True)


def terms_sum(pairs):
    total = None
    for left, right in pairs:
        term = inner_rows(left, right)
        total = term if total is None else total + term
    return total


def back1_body(quarter, scale, chunk, *refs):
    refs = list(refs)
    take = lambda n: [refs.pop(0) for _ in range(n)]
    hid, (hid_other0, dz_mine, dz_got, dz_far) = take(2), take(4)
    h2_theirs, dg = take(2), take(2)
    dh2_send, dh2_keep, n2, inv2, dz, gain2, out_proj, q_up, key_ids = take(9)
    groups = [take(7) for _ in range(2)]
    grad, dy, gain_sum, dyl_mine, dyl_theirs, dqp, dqn_send, dqn_keep, kv_send, kv_keep = take(10)
    h2_got, h2_far, dg_other = take(2), take(2), take(2)
    hid_other1, got, out, core_got, cross_out, cross_got, dyl, dq_acc, do_acc, delta_acc = take(10)
    wire = Wire(*take(2))
    half, rows = 2 * quarter, 4 * quarter
    wire.greet(4)
    y_hid = wire.send(hid[1], hid_other1, wire.beside)
    core_dh2 = wire.send(dh2_send, core_got, wire.core)
    hid_all = (hid[0], hid[1], hid_other0, hid_other1)

    def term(z):
        pairs = [(dz_mine[m, z], hid_all[m][...]) for m in range(2)]
        for m in range(2):
            pairs.append((dz_got[m, z], hid_all[2 + m][:half, :]))
            pairs.append((dz_far[m, z], hid_all[2 + m][half:, :]))
        return terms_sum(pairs)

    def keep(total):
        grad[...] = jnp.transpose(total)

    chain = LineSum(wire, term, (got, out), grad.shape[1], grad.shape[0], keep)
    chain.clear()

    core_dh2.wait_recv()
    cross_out[...] = (
        dh2_keep[:, quarter:, :] + core_got[:, quarter:, :].astype(F32)
    ).astype(LOW)
    cross_dh2 = wire.send(cross_out, cross_got, wire.cross)

    y_hid.wait_recv()
    y_next = [wire.send(h2_theirs[m], h2_got[m], wire.beside) for m in range(2)]
    y_next += [wire.send(dg[m], dg_other[m], wire.beside) for m in range(2)]
    chain.step1()

    cross_dh2.wait_recv()
    dh2 = (
        dh2_keep[:, :quarter, :] + core_got[:, :quarter, :].astype(F32) + cross_got[...].astype(F32)
    )
    gain_sum[...] = jnp.sum(jnp.sum(dh2 * n2[...], axis=0), axis=0, keepdims=True)
    back = dh2 * gain2[...]
    grad_y = dz[:, :quarter, :].astype(F32) + inv2[...] * (
        back - n2[...] * mean_of(back * n2[...])
    )
    dy[...] = grad_y
    dyl[:, :quarter, :] = grad_y.astype(LOW)
    cross_dyl = wire.send(dyl.at[:, :quarter, :], dyl.at[:, quarter:half, :], wire.cross)
    chain.step2()
    cross_dyl.wait_recv()
    core_dyl = wire.send(dyl.at[:, :half, :], dyl.at[:, half:, :], wire.core)
    core_dyl.wait_recv()

    for m in range(2):
        side_columns(dyl.at[m], dyl_mine.at[m], dyl_theirs.at[m], wire.side)
        q, kv, o, lse, row_ids, cos, sin = groups[m]
        attend_back_one(
            scale, chunk, dyl.at[m], out_proj, q_up, key_ids, q, kv, o, lse, row_ids, cos, sin,
            dqp.at[m], dqn_send.at[m], dqn_keep.at[m], kv_send.at[m], kv_keep.at[m],
            dq_acc, do_acc, delta_acc,
        )
        if m == 0:
            chain.step3()
            core_h2 = []
            for i in range(2):
                y_next[i].wait_recv()
                core_h2.append(wire.send(h2_got[i], h2_far[i], wire.core))
    chain.finish()
    for made in y_next[2:] + core_h2:
        made.wait_recv()
    for made in [y_hid, core_dh2, cross_dh2, cross_dyl, core_dyl, *y_next, *core_h2]:
        made.wait_send()
    chain.settle()


def local(
    tokens,
    lengths,
    norm1_gain,
    q_down,
    latent_gain,
    q_up,
    kv_proj,
    out_proj,
    norm2_gain,
    w_gate,
    w_up,
    w_down,
    cotangent,
):
    micro, rows, width = tokens.shape
    seq = lax.axis_size("seq")
    line = seq // 2
    at = lax.axis_index("seq").astype(jnp.int32)
    me = lax.axis_index("mp").astype(jnp.int32)
    place, side = at // 2, at % 2
    ids = jnp.stack([me, side])
    quarter, half = rows // 4, rows // 2
    head_dim = kv_proj.shape[1] // 2
    heads = q_up.shape[1] // head_dim
    part = q_down.shape[1]
    rank = q_up.shape[0]
    hidden = w_gate.shape[1]
    kv_part = kv_proj.shape[1] // 4
    wide = width // seq
    scale = head_dim ** (-0.5)
    key_count = seq * rows
    beside = [(i, i ^ 1) for i in range(seq)]
    narrow = line == 4 and micro == 2 and key_count <= 2048 and not wide % 128

    def swap(index):
        return ((index & 1) << 1) | (index >> 1)

    def to_natural(array, axis):
        size = array.shape[axis] // 4
        return jnp.concatenate(
            [lax.dynamic_slice_in_dim(array, swap(me ^ b) * size, size, axis) for b in range(4)],
            axis,
        )

    def other(array):
        return lax.ppermute(array, "seq", beside)

    def sum_mp(send, keep):
        kept = keep + lax.ppermute(send, "mp", CORE).astype(F32)
        got = lax.ppermute(kept[..., quarter:, :].astype(LOW), "mp", CROSS)
        return kept[..., :quarter, :] + got.astype(F32)

    def gather_mp(piece):
        near = lax.ppermute(piece, "mp", CROSS)
        pair = jnp.concatenate([piece, near], -2)
        return piece, near, lax.ppermute(pair, "mp", CORE)

    def sides_shape(columns, their_rows, lead=()):
        if columns // seq % 128:
            return []
        return [
            whole((*lead, line, n, columns // seq), LOW) for n in (rows, their_rows)
        ]

    def split_sides(made, full, their_rows):
        if made:
            return made
        split = full.reshape(*full.shape[:-1], line, 2, full.shape[-1] // seq)
        mine, theirs = (
            jnp.moveaxis(lax.dynamic_index_in_dim(split, i, split.ndim - 2, keepdims=False), -2, -3)
            for i in (side, 1 - side)
        )
        return mine, theirs[..., :their_rows, :]

    def from_other(theirs):
        got = other(theirs)
        return got, lax.ppermute(got, "mp", CORE)

    def without_sides(body, count):
        return body if count else lambda *refs: body(*refs, None, None)

    def both_sides(mine, got):
        lefts, spans = [], []
        for array, first, count, partner in (
            (mine, 0, rows, 0), (got[0], 0, half, 1), (got[1], half, half, 1)
        ):
            stacked_array = not isinstance(array, list)
            for m in range(micro):
                spans.append((len(lefts) if not stacked_array else len(lefts), m if stacked_array else None,
                              m, partner, first, count))
                if not stacked_array:
                    lefts.append(array[m])
            if stacked_array:
                lefts.append(array)
        return lefts, spans

    class Chain:
        def __init__(self, lefts, rights, terms, shape, turned=False, from_side=None):
            self.args = [*lefts, *rights]
            self.spec = (terms, len(lefts), len(rights))
            self.shape, self.turned = shape, turned
            self.from_side = [] if from_side is None else [from_side]
            self.step, self.up, self.down = 0, None, None

        def block(self, index, added, after, last=False):
            turned = last and self.turned
            body = functools.partial(
                block_body, *self.spec, len(added), len(self.from_side), turned
            )
            shape = self.shape[::-1] if turned else self.shape
            return run(
                body, index.reshape(1), [*self.args, *added, *self.from_side],
                [whole(shape, F32 if last else LOW)], after, name="block",
            )[0]

        def advance(self, after):
            self.step += 1
            step = self.step
            goes_up = [(i, i + 2) for i in range(2 * step)]
            goes_down = [(seq - 1 - i, seq - 3 - i) for i in range(2 * step)]
            for_up, for_down = line - step + place, step - line + place
            if 2 * step < line + 1:
                which = jnp.where(
                    place <= step - 1, for_up, jnp.where(place >= line - step, for_down, 0)
                )
                term = self.block(which, [a for a in (self.up, self.down) if a is not None], after)
                if step == 1 and line > 3:
                    self.up = lax.ppermute(term, "seq", goes_up + goes_down)
                else:
                    self.up = lax.ppermute(term, "seq", goes_up)
                    self.down = lax.ppermute(term, "seq", goes_down)
                return [term]
            term_up = self.block(jnp.clip(for_up, 0, line - 1), [self.up], after)
            term_down = self.block(jnp.clip(for_down, 0, line - 1), [self.down], [term_up])
            self.up = lax.ppermute(term_up, "seq", goes_up)
            self.down = lax.ppermute(term_down, "seq", goes_down)
            return [term_down]

        def finish(self, after):
            while self.step < line - 1:
                after = self.advance(after)
            result = self.block(place, [self.up, self.down], after, last=True)
            return result, [result]

    quarter_rows = jnp.arange(quarter, dtype=jnp.int32)
    row_ids = at * rows + jnp.concatenate([(me ^ k) * quarter + quarter_rows for k in ORDER])
    key_ids = (
        ((place - jnp.arange(line, dtype=jnp.int32)[None, None, :, None, None]) * 2
         + (side ^ jnp.arange(2, dtype=jnp.int32)[None, :, None, None, None])) * rows
        + (me ^ (jnp.arange(2, dtype=jnp.int32)[:, None, None, None, None]
                 + 2 * jnp.arange(2, dtype=jnp.int32)[None, None, None, :, None])) * quarter
        + quarter_rows[None, None, None, None, :]
    ).reshape(key_count)

    gain1_row, gain2_row, gain_c_row = norm1_gain[None, :], norm2_gain[None, :], latent_gain[None, :]
    kv_cols = lax.dynamic_slice_in_dim(kv_proj, me * kv_part, kv_part, 1)
    first_weights = jnp.concatenate([q_down, kv_cols], axis=1)
    both_rows = sides_shape(width, rows)
    half_rows = sides_shape(width, half)
    rank_sides = sides_shape(rank, rows)

    tables, starts, kv, c_part, h1_sides = [], [], [], [], []
    order = []
    for m in range(micro):
        _, places = documents(lengths[m], row_ids)
        starts.append(row_ids - places)
        tables.append(rotation(places, head_dim))
        c, packed, h1, *made = run(
            without_sides(functools.partial(first_body, m, quarter), len(both_rows)),
            ids,
            [tokens, gain1_row, q_down, kv_proj, *tables[m]],
            [whole((rows, part), LOW), whole((half, 2 * head_dim), LOW), whole((rows, width), LOW),
             *both_rows],
            order,
            name="first",
        )
        order = [c]
        blocks = [packed] + [
            lax.ppermute(packed, "seq", [(i, i + 2 * d) for i in range(seq - 2 * d)])
            for d in range(1, line)
        ]
        near = jnp.stack(blocks, 0)
        near = jnp.stack([near, other(near)], 0)
        kv.append(
            jnp.stack([near, lax.ppermute(near, "mp", CORE)], 0).reshape(key_count, 2 * head_dim)
        )
        c_part.append(c)
        h1_sides.append(split_sides(made, h1, rows))

    dhid, dz, *made = run(
        functools.partial(cotangent_body, micro, quarter),
        ids,
        [cotangent, w_down],
        [whole((micro, rows, hidden), F32), whole((micro, rows, width), LOW),
         *sides_shape(width, half, (micro,))],
        order,
        name="cotangent",
    )
    order = [dz]
    dz_mine, dz_theirs = split_sides(made, dz, half)
    dz_got = from_other(dz_theirs)

    qn_sides, qs, os, lses, sums, c_rows = [], [], [], [], [], []
    for m in range(micro):
        near = lax.ppermute(c_part[m], "mp", CROSS)
        swapped = jnp.concatenate(
            [near[quarter : 2 * quarter], near[:quarter], near[3 * quarter :],
             near[2 * quarter : 3 * quarter]], 0
        )
        far = lax.ppermute(jnp.concatenate([c_part[m], swapped], 1), "mp", CORE)
        qn, q, o, lse, send, keep, *made = run(
            without_sides(functools.partial(attend_body, scale), len(rank_sides)),
            ids,
            [c_part[m], near, far, gain_c_row, q_up, *tables[m], kv[m], key_ids[None, :],
             row_ids[:, None], starts[m][:, None], out_proj],
            [whole((rows, rank), LOW), whole((heads, rows, head_dim), LOW),
             whole((rows, heads * head_dim), LOW), whole((heads, rows), F32),
             whole((half, width), LOW), whole((half, width), F32), *rank_sides],
            order,
            name="attend",
        )
        order = [o]
        qn_sides.append(split_sides(made, qn, rows))
        qs.append(q)
        os.append(o)
        lses.append(lse)
        sums.append(sum_mp(send, keep))
        c_rows.append(
            jnp.concatenate([c_part[m][:quarter], swapped[:quarter], far[half : half + quarter]], 1)
        )

    h2_mine, h2_theirs, hid, dg, du, state = [], [], [], [], [], []
    for m in range(micro):
        x = lax.dynamic_slice_in_dim(tokens[m], me * quarter, quarter, 0).astype(F32)
        inv1 = inverse_rms(x)
        y = x + sums[m]
        inv2 = inverse_rms(y)
        n2 = y * inv2
        pieces = gather_mp((n2 * gain2_row).astype(LOW))
        h2, hid_m, dg_m, du_m, *made = run(
            without_sides(functools.partial(forward_body, m), len(half_rows)),
            ids,
            [*pieces, w_gate, w_up, dhid],
            [whole((rows, width), LOW), *[whole((rows, hidden), LOW)] * 3, *half_rows],
            order,
            name="forward",
        )
        order = [hid_m]
        mine, theirs = split_sides(made, h2, half)
        h2_mine.append(mine)
        h2_theirs.append(theirs)
        hid.append(hid_m)
        dg.append(dg_m)
        du.append(du_m)
        state.append(dict(x=x, n1=x * inv1, inv1=inv1, y=y, n2=n2, inv2=inv2, c=c_rows[m]))

    def stacked(name):
        return jnp.stack([st[name] for st in state], 0)

    def with_other(arrays):
        return [*arrays, *[other(a) for a in arrays]]

    def terms_of(spans):
        return [(a, lead, m + micro * partner, None, first, count)
                for a, lead, m, partner, first, count in spans]

    send, keep = run(
        functools.partial(hidden_back_body, micro),
        ids,
        [*dg, *du, w_gate, w_up],
        [whole((micro, half, width), LOW), whole((micro, half, width), F32)],
        order,
        name="hidden_back",
    )
    if narrow:
        y, n2, inv2, n1, inv1 = (stacked(k) for k in ("y", "n2", "inv2", "n1", "inv1"))
        args = [(1, a) for a in (*hid, other(hid[0]), dz_mine, *dz_got)]
        args += [(0, a) for a in (*h2_theirs, *dg)]
        args += [(1, a) for a in (send, keep, n2, inv2, dz, gain2_row, out_proj, q_up,
                                  key_ids[:, None])]
        for m in range(micro):
            args += [(1, a) for a in (qs[m], kv[m], os[m], lses[m],
                                      jnp.stack([row_ids, starts[m]], 0), *tables[m])]
        outs = [(1, whole(shape, dtype)) for shape, dtype in (
            ((hidden, wide), F32), ((micro, quarter, width), F32), ((1, width), F32),
            ((micro, line, rows, wide), LOW), ((micro, line, half, wide), LOW),
            ((micro, rows, heads * head_dim), LOW), ((micro, half, rank), LOW),
            ((micro, half, rank), F32), ((micro, key_count // 2, 2 * head_dim), LOW),
            ((micro, key_count // 2, 2 * head_dim), F32))]
        outs += [(0, whole((line, half, wide), LOW))] * 4 + [(0, whole((rows, hidden), LOW))] * 2
        low = lambda *shape: pltpu.VMEM(shape, LOW)
        (grad_down, dy, gain2, dyl_mine, dyl_theirs, dqp, send, keep, kv_send, kv_keep,
         *exchanged) = mesh_run(
            functools.partial(back1_body, quarter, scale, 1024),
            args,
            outs,
            [low(rows, hidden), low(5, wide, hidden), low(3, wide, hidden),
             low(micro, half, width), low(micro, quarter, width), low(micro, quarter, width),
             low(micro, rows, width), pltpu.VMEM((heads, rows, head_dim), F32),
             low(heads, rows, head_dim), pltpu.VMEM((heads, 8, rows), F32)],
            1,
            "back1",
            60,
            24,
        )
        gain2 = gain2[0]
        order = [send]
        h2_parts = [exchanged[0:2], exchanged[2:4]]
        lefts, spans = both_sides(h2_mine, h2_parts)
        chain_gate = Chain(lefts, [*dg, *exchanged[4:6]], terms_of(spans), (wide, hidden))
        chain_up = Chain(lefts, with_other(du), terms_of(spans), (wide, hidden))
        lefts, spans = both_sides(dyl_mine, from_other(dyl_theirs))
        chain_out = Chain(
            lefts, with_other(os), terms_of(spans), (wide, heads * head_dim), turned=True
        )
    else:
        lefts, spans = both_sides(dz_mine, dz_got)
        chain_down = Chain(lefts, with_other(hid), terms_of(spans), (wide, hidden), turned=True)
        lefts, spans = both_sides(h2_mine, [list(p) for p in zip(*[from_other(t) for t in h2_theirs])])
        chain_gate = Chain(lefts, with_other(dg), terms_of(spans), (wide, hidden))
        chain_up = Chain(lefts, with_other(du), terms_of(spans), (wide, hidden))
        order = chain_down.advance([send])
        dh2 = sum_mp(send, keep)
        y, n2, inv2, n1, inv1 = (stacked(k) for k in ("y", "n2", "inv2", "n1", "inv1"))
        dz_own = dz[:, :quarter].astype(F32)
        gain2 = jnp.sum(dh2 * n2, axis=(0, 1))
        dy = dz_own + norm_backward(dh2 * gain2_row, n2, inv2)
        for _ in range(2):
            order = chain_down.advance(order)
        order = chain_gate.advance(order)

        def attend_back(which, pieces):
            args = [*pieces, out_proj, q_up, key_ids[:, None]]
            for m in which:
                args += [qs[m], kv[m], os[m], lses[m], jnp.stack([row_ids, starts[m]], 0), *tables[m]]
            n = len(which)
            return run(
                functools.partial(attend_back_body, scale, n, min(1024, key_count // 2)),
                ids,
                args,
                [whole((n, rows, width), LOW), whole((n, rows, heads * head_dim), LOW),
                 whole((n, half, rank), LOW), whole((n, half, rank), F32),
                 whole((n, key_count // 2, 2 * head_dim), LOW),
                 whole((n, key_count // 2, 2 * head_dim), F32), *sides_shape(width, half, (n,))],
                order,
                scratch=[pltpu.VMEM((heads, rows, head_dim), F32),
                         pltpu.VMEM((heads, rows, head_dim), LOW),
                         pltpu.VMEM((heads, 8, rows), F32)],
                name="attend_back",
                limit=56,
            )

        pieces = gather_mp(dy.astype(LOW))
        if key_count <= 2048:
            made = attend_back(range(micro), pieces)
        else:
            each = [attend_back([m], [p[m : m + 1] for p in pieces]) for m in range(micro)]
            made = [jnp.concatenate(parts, 0) for parts in zip(*each)]
        dyl, dqp, send, keep, kv_send, kv_keep, *made = made
        order = [send]
        dyl_mine, dyl_theirs = split_sides(made, dyl, half)
        lefts, spans = both_sides(dyl_mine, from_other(dyl_theirs))
        chain_out = Chain(lefts, with_other(os), terms_of(spans), (wide, heads * head_dim), turned=True)

    def side_sum(lefts, rights, shape, after):
        terms = [(m, None, 0, m, 0, rows) for m in range(micro)]
        (made,) = run(
            functools.partial(side_sum_body, terms, len(lefts)),
            ids,
            [*lefts, *rights],
            [whole((line, *shape), LOW)],
            after,
            name="side_sum",
        )
        return other(made), [made]

    def own_chain(side_pairs, right, shape, after):
        from_side, after = side_sum([p[1] for p in side_pairs], [right], shape, after)
        terms = [(m, None, 0, m, 0, rows) for m in range(micro)]
        return Chain([p[0] for p in side_pairs], [right], terms, shape, from_side=from_side), after

    shape = (rank // seq, heads * head_dim)
    chain_qup, order = own_chain(qn_sides, dqp, shape, order)
    order = chain_gate.advance(order)
    order = chain_up.advance(order)

    dqn = sum_mp(send, keep)
    c = stacked("c").astype(F32)
    inv_c = inverse_rms(c)
    chat = c * inv_c
    chat = to_natural(chat, 2)
    gain_c = jnp.sum(dqn * chat, axis=(0, 1))
    dc = norm_backward(dqn * gain_c_row, chat, inv_c).astype(LOW)

    dkv = kv_keep + lax.ppermute(kv_send, "mp", CORE).astype(F32)
    dkv = dkv.reshape(micro, 2, line, 2, quarter, 2 * head_dim)
    dkv = dkv[:, :, :, 0] + lax.ppermute(dkv[:, :, :, 1].astype(LOW), "mp", CROSS).astype(F32)
    dkv = dkv[:, 0] + other(dkv[:, 1].astype(LOW)).astype(F32)
    total = dkv[:, 0]
    for d in range(1, line):
        total = total + lax.ppermute(
            dkv[:, d].astype(LOW), "seq", [(i + 2 * d, i) for i in range(seq - 2 * d)]
        ).astype(F32)
    cosine = jnp.stack([t[0][:quarter] for t in tables], 0)
    sine = jnp.stack([t[1][:quarter] for t in tables], 0)
    dkv_low = jnp.concatenate(
        [unrotate(total[..., :head_dim], cosine, sine), total[..., head_dim:]], axis=-1
    ).astype(LOW)
    both = jnp.concatenate(gather_mp(jnp.concatenate([dc, dkv_low], -1)), -2)
    dfirst = jnp.concatenate(
        [lax.dynamic_slice_in_dim(both, me * part, part, 2),
         lax.dynamic_slice_in_dim(both, rank + me * kv_part, kv_part, 2)], -1
    )

    if not narrow:
        grad_down, order = chain_down.finish(order)
    order = chain_gate.advance(order)
    order = chain_up.advance(order)
    order = chain_out.advance(order)
    grad_gate, order = chain_gate.finish(order)
    order = chain_up.advance(order)
    order = chain_out.advance(order)
    grad_up, order = chain_up.finish(order)
    order = chain_qup.advance(order)
    order = chain_out.advance(order)
    chain_first, order = own_chain(h1_sides, dfirst, (wide, part + kv_part), order)
    order = chain_qup.advance(order)
    grad_out, order = chain_out.finish(order)
    order = chain_first.advance(order)
    order = chain_qup.advance(order)
    order = chain_first.advance(order)
    grad_qup, order = chain_qup.finish(order)
    order = chain_first.advance(order)
    grad_first, order = chain_first.finish(order)

    grad_qdown = grad_first[:, :part]
    kv_cols_grad = grad_first[:, part:]
    pieces = []
    for k in ORDER:
        size = kv_cols_grad.shape[0] // 4
        sent = lax.dynamic_slice_in_dim(kv_cols_grad, (me ^ k) * size, size, 0)
        pieces.append(lax.ppermute(sent, "mp", [(i, i ^ k) for i in range(4)]) if k else sent)
    grad_kv = to_natural(jnp.concatenate(pieces, 1), 1)

    def put_natural(pieces):
        return run(
            functools.partial(natural_body, micro, quarter),
            ids,
            pieces,
            [whole((micro, rows, width), LOW)],
            name="natural",
        )[0]

    part_sum = inner_cols(dfirst.reshape(micro * rows, -1), first_weights).reshape(micro, rows, width)
    dh1 = sum_mp(part_sum[:, half:].astype(LOW), part_sum[:, :half])
    gain1 = jnp.sum(dh1 * n1, axis=(0, 1))
    dx = (dy + norm_backward(dh1 * gain1_row, n1, inv1)).astype(LOW)
    input_grads = put_natural(gather_mp(dx))

    ffn = [dot(hid[m], w_down) for m in range(micro)]
    ffn = sum_mp(
        jnp.stack([f[half:] for f in ffn], 0).astype(LOW), jnp.stack([f[:half] for f in ffn], 0)
    )
    layer_out = put_natural(gather_mp((y + ffn).astype(LOW)))

    gains = jnp.concatenate(
        [gain1.reshape(seq, -1), gain2.reshape(seq, -1), gain_c.reshape(seq, -1)], axis=1
    )
    gains = gains + lax.ppermute(gains, "mp", CORE)
    gains = gains + lax.ppermute(gains, "mp", CROSS)
    gain_sum = lax.dynamic_index_in_dim(gains, at, 0, keepdims=False)
    for k in range(1, seq):
        gain_sum = gain_sum + lax.ppermute(
            lax.dynamic_index_in_dim(gains, at ^ k, 0, keepdims=False),
            "seq",
            [(i, i ^ k) for i in range(seq)],
        )
    return (
        layer_out,
        input_grads,
        gain_sum[:wide],
        grad_qdown,
        gain_sum[2 * wide :],
        grad_qup,
        grad_kv,
        grad_out,
        gain_sum[wide : 2 * wide],
        grad_gate,
        grad_up,
        grad_down,
    )


def solution(mesh):
    placed = (
        P(None, "seq", None),
        P(),
        P(),
        P(None, "mp"),
        P(),
        P(None, "mp"),
        P(),
        P("mp", None),
        P(),
        P(None, "mp"),
        P(None, "mp"),
        P("mp", None),
        P(None, "seq", None),
    )
    return jax.shard_map(
        local,
        mesh=mesh,
        in_specs=placed,
        out_specs=(
            P(None, "seq", None),
            P(None, "seq", None),
            P("seq"),
            P("seq", "mp"),
            P("seq"),
            P("seq", "mp"),
            P(("seq", "mp"), None),
            P("mp", "seq"),
            P("seq"),
            P("seq", "mp"),
            P("seq", "mp"),
            P("mp", "seq"),
        ),
        check_vma=False,
    )
```

```python
import functools

import jax
import jax.numpy as jnp
from jax import lax
from jax.experimental import pallas as pl
from jax.experimental.pallas import tpu as pltpu
from jax.sharding import PartitionSpec as P

EPS = 1e-06
BASE = 10000.0
NEG_LARGE = -1e30
LOW = jnp.bfloat16
F32 = jnp.float32
ORDER = (0, 2, 1, 3)
CORE = [(i, i ^ 1) for i in range(4)]
CROSS = [(i, i ^ 2) for i in range(4)]


def inverse_rms(values):
    return lax.rsqrt(jnp.mean(values * values, axis=-1, keepdims=True) + EPS)


def norm_backward(grad_hat, normed, inverse):
    return inverse * (grad_hat - normed * jnp.mean(grad_hat * normed, axis=-1, keepdims=True))


def dot(left, right):
    return jnp.dot(left, right, preferred_element_type=F32)


def inner_rows(left, right):
    return lax.dot_general(left, right, (((0,), (0,)), ((), ())), preferred_element_type=F32)


def inner_cols(left, right):
    return lax.dot_general(left, right, (((1,), (1,)), ((), ())), preferred_element_type=F32)


def documents(lengths_row, rows):
    first_end = lengths_row[0]
    second_end = first_end + lengths_row[1]
    doc_ids = (rows >= first_end).astype(jnp.int32) + (rows >= second_end).astype(jnp.int32)
    starts = jnp.where(rows >= second_end, second_end, jnp.where(rows >= first_end, first_end, 0))
    return (doc_ids, rows - starts)


def rotation(positions, head_dim):
    half = head_dim // 2
    freqs = BASE ** (-2.0 * jnp.arange(half, dtype=F32) / head_dim)
    angles = positions.astype(F32)[:, None] * freqs[None, :]
    return (jnp.cos(angles), jnp.sin(angles))


def rotate(values, cosine, sine):
    half = values.shape[-1] // 2
    first = values[..., :half]
    second = values[..., half:]
    return jnp.concatenate(
        [first * cosine - second * sine, second * cosine + first * sine], axis=-1
    )


def unrotate(grads, cosine, sine):
    return rotate(grads, cosine, -sine)


def in_vmem():
    return pl.BlockSpec(memory_space=pltpu.VMEM)


def whole(shape, dtype):
    return jax.ShapeDtypeStruct(shape, dtype)


def run(body, ids, args, outs, after=(), scratch=(), name=None, limit=40):
    args, after = list(args), list(after)

    def without(*refs):
        body(*refs[: 1 + len(args)], *refs[1 + len(args) + len(after) :])

    return pl.pallas_call(
        without,
        grid_spec=pltpu.PrefetchScalarGridSpec(
            num_scalar_prefetch=1,
            grid=(1,),
            in_specs=[in_vmem()] * len(args) + [pl.BlockSpec(memory_space=pl.ANY)] * len(after),
            out_specs=[in_vmem()] * len(outs),
            scratch_shapes=list(scratch),
        ),
        out_shape=list(outs),
        cost_estimate=pl.CostEstimate(flops=1000, bytes_accessed=1000, transcendentals=0),
        compiler_params=pltpu.CompilerParams(vmem_limit_bytes=limit << 20),
        name=name,
    )(ids, *args, *after)


def side_columns(source, mine, theirs, side):
    line, _, wide = mine.shape
    rows = theirs.shape[1]
    for z in range(line):
        mine[z] = source[:, pl.ds(pl.multiple_of((2 * z + side) * wide, wide), wide)]
        theirs[z] = source[:rows, pl.ds(pl.multiple_of((2 * z + 1 - side) * wide, wide), wide)]


def first_body(m, quarter, ids, x_ref, gain, q_down, kv_proj, cos, sin, c, kv, h1, mine, theirs):
    blocks = [
        x_ref[m, pl.ds(pl.multiple_of((ids[0] ^ k) * quarter, quarter), quarter), :] for k in ORDER
    ]
    x = jnp.concatenate(blocks, 0).astype(F32)
    low = (x * inverse_rms(x) * gain[...]).astype(LOW)
    h1[...] = low
    half = 2 * quarter
    pair = dot(low[:half], kv_proj[...])
    wide = kv_proj.shape[1] // 2
    kv[:, :wide] = rotate(pair[:, :wide], cos[:half], sin[:half]).astype(LOW)
    kv[:, wide:] = pair[:, wide:].astype(LOW)
    c[...] = dot(low, q_down[...]).astype(LOW)
    if mine is not None:
        side_columns(h1, mine, theirs, ids[1])


def cotangent_body(micro, quarter, ids, z_ref, w_down, dhid, dz, *sides):
    for m in range(micro):
        blocks = [
            z_ref[m, pl.ds(pl.multiple_of((ids[0] ^ k) * quarter, quarter), quarter), :]
            for k in ORDER
        ]
        dz[m] = jnp.concatenate(blocks, 0)
        if sides:
            side_columns(dz.at[m], sides[0].at[m], sides[1].at[m], ids[1])
        dhid[m] = inner_cols(dz[m], w_down[...])


def attend_body(
    scale, ids, c0, c1, c2, gain, q_up, cos, sin, kv, key_ids, row_ids, row_starts, out_proj,
    qn, q, o, lse, send, keep, mine, theirs,
):
    rows = qn.shape[0]
    quarter = rows // 4
    part = c0.shape[1]
    wide = q.shape[2]
    got = c1[...]
    pair = jnp.concatenate(
        [got[quarter : 2 * quarter], got[:quarter], got[3 * quarter :], got[2 * quarter : 3 * quarter]],
        0,
    )
    far = jnp.concatenate([c2[2 * quarter :], c2[: 2 * quarter]], 0)
    c = jnp.concatenate([c0[...], pair, far], 1).astype(F32)
    chat = c * inverse_rms(c)
    for k, xor in enumerate(ORDER):
        columns = pl.ds(pl.multiple_of((ids[0] ^ xor) * part, part), part)
        qn[:, columns] = (chat[:, k * part : (k + 1) * part] * gain[:, columns]).astype(LOW)
    if mine is not None:
        side_columns(qn, mine, theirs, ids[1])
    bias = jnp.where(
        (key_ids[...] >= row_starts[...]) & (key_ids[...] <= row_ids[...]), 0.0, NEG_LARGE
    )
    low = qn[...]
    keys, values = kv[:, :wide], kv[:, wide:]
    for h in range(q.shape[0]):
        pre = dot(low, q_up[:, h * wide : (h + 1) * wide])
        q_h = (rotate(pre, cos[...], sin[...]) * scale).astype(LOW)
        q[h] = q_h
        scores = inner_cols(q_h, keys) + bias
        top = jnp.max(scores, axis=-1, keepdims=True)
        probs = jnp.exp(scores - top)
        total = jnp.sum(probs, axis=-1, keepdims=True)
        out = dot(probs.astype(LOW), values) / total
        o[:, h * wide : (h + 1) * wide] = out.astype(LOW)
        log_total = jnp.broadcast_to(top + jnp.log(total), (rows, 128))
        lse[h : h + 1, :] = jnp.transpose(log_total)[:1]
    half = 2 * quarter
    send[...] = dot(o[half:, :], out_proj[...]).astype(LOW)
    keep[...] = dot(o[:half, :], out_proj[...])


def forward_body(m, ids, a0, a1, a2, w_gate, w_up, dhid, h2, hid, dg, du, mine, theirs):
    h2[...] = jnp.concatenate([a0[...], a1[...], a2[...]], 0)
    if mine is not None:
        side_columns(h2, mine, theirs, ids[1])
    low = h2[...]
    g = dot(low, w_gate[...])
    u = dot(low, w_up[...])
    sig = jax.nn.sigmoid(g)
    swish = g * sig
    hid[...] = (swish * u).astype(LOW)
    back = dhid[m]
    dg[...] = (back * u * sig * (1.0 + g * (1.0 - sig))).astype(LOW)
    du[...] = (back * swish).astype(LOW)


def hidden_back_body(micro, ids, *refs):
    dgs, dus = refs[:micro], refs[micro : 2 * micro]
    hids = refs[2 * micro : 3 * micro]
    w_gate, w_up, w_down, send, keep, out_send, out_keep = refs[3 * micro :]
    half = send.shape[1]
    for m in range(micro):
        for rows, out in ((slice(half, None), send), (slice(0, half), keep)):
            out[m] = (
                inner_cols(dgs[m][rows, :], w_gate[...]) + inner_cols(dus[m][rows, :], w_up[...])
            ).astype(out.dtype)
    for m in range(micro):
        for rows, out in ((slice(half, None), out_send), (slice(0, half), out_keep)):
            out[m] = dot(hids[m][rows, :], w_down[...]).astype(out.dtype)


def pick(ref, lead):
    return ref if lead is None else ref.at[lead]


def block_body(terms, lefts, rights, extra, from_side, turned, ids, *refs):
    left, refs = refs[:lefts], refs[lefts:]
    right, refs = refs[:rights], refs[rights:]
    added, out = refs[: extra + from_side], refs[-1]
    total = None
    for a, a_lead, b, b_lead, first, count in terms:
        rows = pick(right[b], b_lead)[first : first + count, :]
        term = inner_rows(pick(left[a], a_lead)[ids[0]], rows)
        total = term if total is None else total + term
    for i, ref in enumerate(added):
        total = total + (ref[ids[0]] if i >= extra else ref[...]).astype(F32)
    out[...] = jnp.transpose(total) if turned else total.astype(out.dtype)


def side_sum_body(terms, lefts, ids, *refs):
    left, right, out = refs[:lefts], refs[lefts:-1], refs[-1]
    for z in range(out.shape[0]):
        total = None
        for a, a_lead, b, b_lead, first, count in terms:
            rows = pick(right[b], b_lead)[first : first + count, :]
            term = inner_rows(pick(left[a], a_lead)[z], rows)
            total = term if total is None else total + term
        out[z] = total.astype(out.dtype)


def attend_back_body(
    scale, micro, chunk, ids, a0, a1, a2, out_proj, q_up, key_ids, *refs
):
    per = 7
    groups = [refs[m * per : (m + 1) * per] for m in range(micro)]
    dyl_out, dqp, send, keep, kv_send, kv_keep = refs[micro * per : micro * per + 6]
    dq_acc, do_acc, delta_acc = refs[-3:]
    sides = refs[micro * per + 6 : -3]
    for m in range(micro):
        q, kv, o, lse, row_ids, cos, sin = groups[m]
        heads, rows, wide = q.shape
        half_rows = rows // 2
        dyl = jnp.concatenate([a0[m], a1[m], a2[m]], 0)
        dyl_out[m] = dyl
        if sides:
            side_columns(dyl_out.at[m], sides[0].at[m], sides[1].at[m], ids[1])
        for h in range(heads):
            do = inner_cols(dyl, out_proj[h * wide : (h + 1) * wide, :]).astype(LOW)
            do_acc[h] = do
            delta = jnp.sum(
                do.astype(F32) * o[:, h * wide : (h + 1) * wide].astype(F32), axis=-1, keepdims=True
            )
            delta_acc[h] = jnp.transpose(jnp.broadcast_to(delta, (rows, 128)))[:8]
            dq_acc[h] = jnp.zeros((rows, wide), F32)
        count = kv.shape[0] // 2 // chunk
        for part, out in ((0, kv_keep), (1, kv_send)):

            def one(i, carry):
                base = pl.multiple_of((part * count + i) * chunk, chunk)
                keys = kv[pl.ds(base, chunk), :wide]
                values = kv[pl.ds(base, chunk), wide:]
                at = key_ids[pl.ds(base, chunk), :]
                bias = jnp.where((at >= row_ids[1:2, :]) & (at <= row_ids[0:1, :]), 0.0, NEG_LARGE)

                def head(h, sums):
                    dk, dv = sums
                    q_h, do_h = q[h], do_acc[h]
                    probs = jnp.exp(inner_cols(keys, q_h) + bias - lse[pl.ds(h, 1), :])
                    back = inner_cols(values, do_h) - delta_acc[h][:1]
                    ds = (probs * back).astype(LOW)
                    dv = dv + dot(probs.astype(LOW), do_h)
                    dk = dk + dot(ds, q_h)
                    dq_acc[h] = dq_acc[h] + inner_rows(ds, keys)
                    return dk, dv

                zero = jnp.zeros((chunk, wide), F32)
                dk, dv = lax.fori_loop(0, heads, head, (zero, zero))
                place = pl.ds(pl.multiple_of(i * chunk, chunk), chunk)
                out[m, place, :wide] = dk.astype(out.dtype)
                out[m, place, wide:] = dv.astype(out.dtype)
                return carry

            if count == 1:
                one(0, 0)
            else:
                lax.fori_loop(0, count, one, 0)
        for h in range(heads):
            dq = unrotate(dq_acc[h] * scale, cos[...], sin[...])
            dqp[m, :, h * wide : (h + 1) * wide] = dq.astype(LOW)
        low = dqp[m]
        send[m] = inner_cols(low[half_rows:], q_up[...]).astype(LOW)
        keep[m] = inner_cols(low[:half_rows], q_up[...])


def natural_body(micro, quarter, ids, a0, a1, a2, out):
    for m in range(micro):
        pieces = (a0[m], a1[m], a2[m, :quarter, :], a2[m, quarter:, :])
        for k, piece in zip(ORDER, pieces):
            out[m, pl.ds(pl.multiple_of((ids[0] ^ k) * quarter, quarter), quarter), :] = piece


class Wire:
    def __init__(self, sends, recvs):
        self.sends, self.recvs, self.used = sends, recvs, 0
        self.seq, self.mp = lax.axis_index("seq"), lax.axis_index("mp")
        self.place, self.side = self.seq // 2, self.seq % 2
        core, cross = self.mp % 2, self.mp // 2
        self.blocks = (
            self.mp, 2 * (1 - cross) + core, 2 * cross + 1 - core, 2 * (1 - cross) + 1 - core
        )
        self.core, self.cross = {"mp": self.blocks[2]}, {"mp": self.blocks[1]}
        self.beside = {"seq": self.seq + 1 - 2 * self.side}
        self.up, self.down = {"seq": self.seq + 2}, {"seq": self.seq - 2}

    def copy(self, source, target, device):
        at = self.used
        self.used += 1
        return pltpu.make_async_remote_copy(
            src_ref=source, dst_ref=target, send_sem=self.sends.at[at], recv_sem=self.recvs.at[at],
            device_id=device, device_id_type=pl.DeviceIdType.MESH,
        )

    def send(self, source, target, device):
        made = self.copy(source, target, device)
        made.start()
        return made

    def greet(self, line, far=1, diagonal=False):
        barrier = pltpu.get_barrier_semaphore()
        devices = [self.core, self.cross, self.beside]
        if diagonal:
            devices.append({"mp": self.blocks[3]})
        for device in devices:
            pl.semaphore_signal(barrier, 1, device_id=device, device_id_type=pl.DeviceIdType.MESH)
        for d in range(1, far + 1):
            for way, there in ((1, self.place < line - d), (-1, self.place >= d)):

                @pl.when(there)
                def _():
                    pl.semaphore_signal(
                        barrier, 1, device_id={"seq": self.seq + 2 * way * d},
                        device_id_type=pl.DeviceIdType.MESH,
                    )
        below, above = jnp.minimum(self.place, far), jnp.minimum(line - 1 - self.place, far)
        pl.semaphore_wait(barrier, len(devices) + below + above)


class LineSum:
    def __init__(self, wire, term, room, rows, columns, keep):
        got, out = room
        view = lambda ref, i: ref.at[i, :rows, :columns]
        self.place, self.term, self.keep = wire.place, term, keep
        self.got = [view(got, i) for i in range(5)]
        self.out = [view(out, i) for i in range(3)]
        one, two_up, two_down, three_up, three_down = self.got
        a, b, c = self.out
        self.one = wire.copy(a, one, wire.up), wire.copy(a, one, wire.down)
        self.two = wire.copy(b, two_up, wire.up), wire.copy(b, two_down, wire.down)
        self.three = wire.copy(a, three_up, wire.up), wire.copy(c, three_down, wire.down)

    def clear(self):
        place = self.place
        for ref, empty in zip(
            self.got, ((place == 0) | (place == 3),) * 3 + (place == 0, place == 3)
        ):

            @pl.when(empty)
            def _(ref=ref):
                ref[...] = jnp.zeros(ref.shape, ref.dtype)

    def step1(self):
        place = self.place

        @pl.when((place == 0) | (place == 3))
        def _():
            self.out[0][...] = self.term(3 - place).astype(LOW)

        pl.when(place == 0)(self.one[0].start)
        pl.when(place == 3)(self.one[1].start)

    def step2(self):
        place = self.place
        pl.when(place == 1)(self.one[0].wait_recv)
        pl.when(place == 2)(self.one[1].wait_recv)
        self.out[1][...] = (
            self.term((place + 2) % 4) + self.got[0][...].astype(F32)
        ).astype(LOW)
        pl.when(place <= 1)(self.two[0].start)
        pl.when(place >= 2)(self.two[1].start)

    def step3(self):
        place = self.place

        @pl.when((place == 1) | (place == 2))
        def _():
            self.two[0].wait_recv()
            self.two[1].wait_recv()

        pl.when(place == 0)(self.one[0].wait_send)
        pl.when(place == 3)(self.one[1].wait_send)

        @pl.when(place <= 2)
        def _():
            self.out[0][...] = (self.term(place + 1) + self.got[1][...].astype(F32)).astype(LOW)
            self.three[0].start()

        @pl.when(place >= 1)
        def _():
            self.out[2][...] = (self.term(place - 1) + self.got[2][...].astype(F32)).astype(LOW)
            self.three[1].start()

    def finish(self):
        place = self.place
        pl.when(place >= 1)(self.three[0].wait_recv)
        pl.when(place <= 2)(self.three[1].wait_recv)
        self.keep(
            self.term(place) + self.got[3][...].astype(F32) + self.got[4][...].astype(F32)
        )

    def settle(self):
        place = self.place
        pl.when(place <= 1)(self.two[0].wait_send)
        pl.when(place >= 2)(self.two[1].wait_send)
        pl.when(place <= 2)(self.three[0].wait_send)
        pl.when(place >= 1)(self.three[1].wait_send)


def mesh_run(body, args, outs, scratch, number, name, limit, sends):
    return pl.pallas_call(
        body,
        in_specs=[in_vmem() if kind else pl.BlockSpec(memory_space=pl.ANY) for kind, _ in args],
        out_specs=[in_vmem() if kind else pl.BlockSpec(memory_space=pl.ANY) for kind, _ in outs],
        out_shape=[shape for _, shape in outs],
        scratch_shapes=[
            *scratch, pltpu.SemaphoreType.DMA((sends,)), pltpu.SemaphoreType.DMA((sends,))
        ],
        cost_estimate=pl.CostEstimate(flops=1000, bytes_accessed=1000, transcendentals=0),
        compiler_params=pltpu.CompilerParams(
            collective_id=number, has_side_effects=True, vmem_limit_bytes=limit << 20
        ),
        name=name,
    )(*[array for _, array in args])


def attend_back_one(
    scale, chunk, dyl, out_proj, q_up, key_ids, q, kv, o, lse, row_ids, cos, sin,
    dqp, send, keep, kv_send, kv_keep, dq_acc, do_acc, delta_acc,
):
    heads, rows, wide = q.shape
    half_rows = rows // 2
    low = dyl[...]
    for h in range(heads):
        do = inner_cols(low, out_proj[h * wide : (h + 1) * wide, :]).astype(LOW)
        do_acc[h] = do
        delta = jnp.sum(
            do.astype(F32) * o[:, h * wide : (h + 1) * wide].astype(F32), axis=-1, keepdims=True
        )
        delta_acc[h] = jnp.transpose(jnp.broadcast_to(delta, (rows, 128)))[:8]
        dq_acc[h] = jnp.zeros((rows, wide), F32)
    count = kv.shape[0] // 2 // chunk
    for part, out in ((0, kv_keep), (1, kv_send)):
        for i in range(count):
            base = (part * count + i) * chunk
            keys = kv[base : base + chunk, :wide]
            values = kv[base : base + chunk, wide:]
            at = key_ids[base : base + chunk, :]
            bias = jnp.where((at >= row_ids[1:2, :]) & (at <= row_ids[0:1, :]), 0.0, NEG_LARGE)

            def head(h, sums):
                dk, dv = sums
                q_h, do_h = q[h], do_acc[h]
                probs = jnp.exp(inner_cols(keys, q_h) + bias - lse[pl.ds(h, 1), :])
                back = inner_cols(values, do_h) - delta_acc[h][:1]
                ds = (probs * back).astype(LOW)
                dv = dv + dot(probs.astype(LOW), do_h)
                dk = dk + dot(ds, q_h)
                dq_acc[h] = dq_acc[h] + inner_rows(ds, keys)
                return dk, dv

            zero = jnp.zeros((chunk, wide), F32)
            dk, dv = lax.fori_loop(0, heads, head, (zero, zero))
            out[i * chunk : (i + 1) * chunk, :wide] = dk.astype(out.dtype)
            out[i * chunk : (i + 1) * chunk, wide:] = dv.astype(out.dtype)
    for h in range(heads):
        dq = unrotate(dq_acc[h] * scale, cos[...], sin[...])
        dqp[:, h * wide : (h + 1) * wide] = dq.astype(LOW)
    low = dqp[...]
    send[...] = inner_cols(low[half_rows:], q_up[...]).astype(LOW)
    keep[...] = inner_cols(low[:half_rows], q_up[...])


def mean_of(values):
    return jnp.mean(values, axis=-1, keepdims=True)


def terms_sum(pairs):
    total = None
    for left, right in pairs:
        term = inner_rows(left, right)
        total = term if total is None else total + term
    return total


def back1_body(quarter, scale, chunk, *refs):
    refs = list(refs)
    take = lambda n: [refs.pop(0) for _ in range(n)]
    hid, (hid_other0, dz_mine, dz_got, dz_far) = take(2), take(4)
    h2_theirs, dg = take(2), take(2)
    dh2_send, dh2_keep, n2, inv2, dz, gain2, out_proj, q_up, key_ids = take(9)
    groups = [take(7) for _ in range(2)]
    grad, dy, gain_sum, dyl_mine, dyl_theirs, dqp, dqn_send, dqn_keep, kv_send, kv_keep = take(10)
    h2_got, h2_far, dg_other = take(2), take(2), take(2)
    hid_other1, got, out, core_got, cross_out, cross_got, dyl, dq_acc, do_acc, delta_acc = take(10)
    wire = Wire(*take(2))
    half, rows = 2 * quarter, 4 * quarter
    wire.greet(4)
    y_hid = wire.send(hid[1], hid_other1, wire.beside)
    core_dh2 = wire.send(dh2_send, core_got, wire.core)
    hid_all = (hid[0], hid[1], hid_other0, hid_other1)

    def term(z):
        pairs = [(dz_mine[m, z], hid_all[m][...]) for m in range(2)]
        for m in range(2):
            pairs.append((dz_got[m, z], hid_all[2 + m][:half, :]))
            pairs.append((dz_far[m, z], hid_all[2 + m][half:, :]))
        return terms_sum(pairs)

    def keep(total):
        grad[...] = jnp.transpose(total)

    chain = LineSum(wire, term, (got, out), grad.shape[1], grad.shape[0], keep)
    chain.clear()

    core_dh2.wait_recv()
    cross_out[...] = (
        dh2_keep[:, quarter:, :] + core_got[:, quarter:, :].astype(F32)
    ).astype(LOW)
    cross_dh2 = wire.send(cross_out, cross_got, wire.cross)

    y_hid.wait_recv()
    y_next = [wire.send(h2_theirs[m], h2_got[m], wire.beside) for m in range(2)]
    y_next += [wire.send(dg[m], dg_other[m], wire.beside) for m in range(2)]
    chain.step1()

    cross_dh2.wait_recv()
    dh2 = (
        dh2_keep[:, :quarter, :] + core_got[:, :quarter, :].astype(F32) + cross_got[...].astype(F32)
    )
    gain_sum[...] = jnp.sum(jnp.sum(dh2 * n2[...], axis=0), axis=0, keepdims=True)
    back = dh2 * gain2[...]
    grad_y = dz[:, :quarter, :].astype(F32) + inv2[...] * (
        back - n2[...] * mean_of(back * n2[...])
    )
    dy[...] = grad_y
    dyl[:, :quarter, :] = grad_y.astype(LOW)
    cross_dyl = wire.send(dyl.at[:, :quarter, :], dyl.at[:, quarter:half, :], wire.cross)
    chain.step2()
    cross_dyl.wait_recv()
    core_dyl = wire.send(dyl.at[:, :half, :], dyl.at[:, half:, :], wire.core)
    core_dyl.wait_recv()

    for m in range(2):
        side_columns(dyl.at[m], dyl_mine.at[m], dyl_theirs.at[m], wire.side)
        q, kv, o, lse, row_ids, cos, sin = groups[m]
        attend_back_one(
            scale, chunk, dyl.at[m], out_proj, q_up, key_ids, q, kv, o, lse, row_ids, cos, sin,
            dqp.at[m], dqn_send.at[m], dqn_keep.at[m], kv_send.at[m], kv_keep.at[m],
            dq_acc, do_acc, delta_acc,
        )
        if m == 0:
            chain.step3()
            core_h2 = []
            for i in range(2):
                y_next[i].wait_recv()
                core_h2.append(wire.send(h2_got[i], h2_far[i], wire.core))
    chain.finish()
    for made in y_next[2:] + core_h2:
        made.wait_recv()
    for made in [y_hid, core_dh2, cross_dh2, cross_dyl, core_dyl, *y_next, *core_h2]:
        made.wait_send()
    chain.settle()


class Share:
    def __init__(self, wire, out, quarter):
        spot = lambda block: out.at[:, pl.ds(pl.multiple_of(block * quarter, quarter), quarter), :]
        own, near = spot(wire.blocks[0]), spot(wire.blocks[1])
        self.own = own
        self.first = wire.copy(own, own, wire.cross)
        self.rest = wire.copy(own, own, wire.core), wire.copy(near, near, wire.core)

    def begin(self, value):
        self.own[...] = value
        self.first.start()
        self.rest[0].start()

    def forward(self):
        self.first.wait_recv()
        self.rest[1].start()

    def end(self):
        for made in self.rest:
            made.wait_recv()
        for made in (self.first, *self.rest):
            made.wait_send()


class RowSum:
    def __init__(self, wire, send, kept, got, cross_out, cross_got, quarter):
        self.kept, self.got, self.quarter = kept, got, quarter
        self.out, self.back = cross_out, cross_got
        self.core = wire.copy(send, got, wire.core)
        self.cross = wire.copy(cross_out, cross_got, wire.cross)

    def pass_on(self):
        self.core.wait_recv()
        rest = slice(self.quarter, None)
        self.out[...] = (self.kept[:, rest, :] + self.got[:, rest, :].astype(F32)).astype(LOW)
        self.cross.start()

    def result(self):
        self.cross.wait_recv()
        own = slice(0, self.quarter)
        return (
            self.kept[:, own, :] + self.got[:, own, :].astype(F32) + self.back[...].astype(F32)
        )

    def end(self):
        self.core.wait_send()
        self.cross.wait_send()


def halves_terms(mine, got, far, rights, half):
    pairs = [(mine[m], rights[m][...]) for m in range(2)]
    for m in range(2):
        pairs.append((got[m], rights[2 + m][:half, :]))
        pairs.append((far[m], rights[2 + m][half:, :]))
    return pairs


def back2_body(quarter, *refs):
    refs = list(refs)
    take = lambda n: [refs.pop(0) for _ in range(n)]
    dg, dg_other, du, h2_mine, h2_got, h2_far = (take(2) for _ in range(6))
    kv_send, kv_keep, dqn_send, dqn_keep, chat, inv_c, gain_c, cos, sin = take(9)
    qn_theirs = take(2)
    dqp, dyl_theirs, o0, o1, ffn_send, ffn_keep, y = take(7)
    grad_gate, grad_up, dfirst, gain_sum, qup_side, dyl_got, dyl_far, oo0, oo1, layer_out = take(10)
    du_other = take(2)
    got_a, out_a, got_b, out_b = take(4)
    dqn_got, dqn_out, dqn_back = take(3)
    kv_got, kv_out, kv_back, side_out, side_got, line_out, line_got, kv_own = take(8)
    both, side_sums = take(2)
    ffn_got, ffn_out, ffn_back = take(3)
    wire = Wire(*take(2))
    half, rows = 2 * quarter, 4 * quarter
    wide = kv_own.shape[2] // 2
    place = wire.place
    wire.greet(4, 3)

    y_du = [wire.send(du[m], du_other[m], wire.beside) for m in range(2)]
    dqn_sum = RowSum(wire, dqn_send, dqn_keep, dqn_got, dqn_out, dqn_back, quarter)
    dqn_sum.core.start()
    core_kv = wire.send(kv_send, kv_got, wire.core)
    ffn_sum = RowSum(wire, ffn_send, ffn_keep, ffn_got, ffn_out, ffn_back, quarter)
    ffn_sum.core.start()

    def gate_term(z):
        return terms_sum(halves_terms(
            [a.at[z][...] for a in h2_mine], [a.at[z][...] for a in h2_got],
            [a.at[z][...] for a in h2_far], (*dg, *dg_other), half))

    def up_term(z):
        return terms_sum(halves_terms(
            [a.at[z][...] for a in h2_mine], [a.at[z][...] for a in h2_got],
            [a.at[z][...] for a in h2_far], (*du, *du_other), half))

    def keep_gate(total):
        grad_gate[...] = total

    def keep_up(total):
        grad_up[...] = total

    gate = LineSum(wire, gate_term, (got_a, out_a), *grad_gate.shape, keep_gate)
    up = LineSum(wire, up_term, (got_b, out_b), *grad_up.shape, keep_up)
    gate.clear()
    up.clear()
    line_kv = []
    for d in range(1, 4):
        line_kv.append(wire.copy(line_out.at[d - 1], line_got.at[d - 1],
                                 {"seq": wire.seq - 2 * d}))

        @pl.when(place > 3 - d)
        def _(d=d):
            line_got[d - 1] = jnp.zeros(line_got.shape[1:], LOW)

    gate.step1()
    dqn_sum.pass_on()
    core_kv.wait_recv()
    kv_out[...] = (kv_keep[:, :, 1] + kv_got[:, :, 1].astype(F32)).astype(LOW)
    cross_kv = wire.send(kv_out, kv_back, wire.cross)
    for z in range(4):
        side_sums[z] = terms_sum([(qn_theirs[m][z], dqp[m]) for m in range(2)]).astype(LOW)
    dqn = dqn_sum.result()
    gain_sum[...] = jnp.sum(jnp.sum(dqn * chat[...], axis=0), axis=0, keepdims=True)
    back = dqn * gain_c[...]
    rank = chat.shape[2]
    both[:, :quarter, :rank] = (
        inv_c[...] * (back - chat[...] * mean_of(back * chat[...]))
    ).astype(LOW)
    gate.step2()

    cross_kv.wait_recv()
    for part in range(2):
        span = slice(4 * part, 4 * part + 4)
        total = kv_keep[:, span, 0] + kv_got[:, span, 0].astype(F32) + kv_back[:, span].astype(F32)
        if part:
            side_out[...] = total.astype(LOW)
    for made in y_du:
        made.wait_recv()
    side_kv = wire.send(side_out, side_got, wire.beside)
    y_rest = [wire.send(side_sums, qup_side, wire.beside)]
    up.step1()
    gate.step3()
    ffn_sum.pass_on()
    side_kv.wait_recv()
    y_rest.append(wire.send(dyl_theirs, dyl_got, wire.beside))
    y_rest += [wire.send(a, b, wire.beside) for a, b in ((o0, oo0), (o1, oo1))]
    own = kv_keep[:, :4, 0] + kv_got[:, :4, 0].astype(F32) + kv_back[:, :4].astype(F32)
    own = own + side_got[...].astype(F32)
    kv_own[...] = own[:, 0]
    for d in range(1, 4):
        line_out[d - 1] = own[:, d].astype(LOW)
        pl.when(place >= d)(line_kv[d - 1].start)
    up.step2()
    gate.finish()
    share = Share(wire, layer_out, quarter)
    share.begin((y[...] + ffn_sum.result()).astype(LOW))
    for d in range(1, 4):
        pl.when(place <= 3 - d)(line_kv[d - 1].wait_recv)
    total = kv_own[...]
    for d in range(1, 4):
        total = total + line_got[d - 1].astype(F32)
    both[:, :quarter, rank : rank + wide] = unrotate(
        total[:, :, :wide], cos[...], sin[...]
    ).astype(LOW)
    both[:, :quarter, rank + wide :] = total[:, :, wide:].astype(LOW)
    cross_both = wire.send(both.at[:, :quarter, :], both.at[:, quarter:half, :], wire.cross)
    share.forward()
    cross_both.wait_recv()
    core_both = wire.send(both.at[:, :half, :], both.at[:, half:, :], wire.core)
    up.step3()
    core_both.wait_recv()
    part = rank // 4
    kv_part = wide // 2
    dfirst[:, :, :part] = both[:, :, pl.ds(pl.multiple_of(wire.mp * part, part), part)]
    dfirst[:, :, part:] = both[
        :, :, pl.ds(pl.multiple_of(rank + wire.mp * kv_part, kv_part), kv_part)
    ]
    y_rest[1].wait_recv()
    core_dyl = wire.send(dyl_got, dyl_far, wire.core)
    up.finish()
    share.end()
    core_dyl.wait_recv()
    for made in (y_rest[0], y_rest[2], y_rest[3]):
        made.wait_recv()
    for made in [*y_du, core_kv, cross_kv, side_kv, cross_both, core_both, *y_rest, core_dyl]:
        made.wait_send()
    for d in range(1, 4):
        pl.when(place >= d)(line_kv[d - 1].wait_send)
    dqn_sum.end()
    ffn_sum.end()
    gate.settle()
    up.settle()


def back3_body(quarter, *refs):
    refs = list(refs)
    take = lambda n: [refs.pop(0) for _ in range(n)]
    dfirst, weights = take(2)
    h1_mine, h1_theirs, o, oo = (take(2) for _ in range(4))
    dyl_mine, dyl_got, dyl_far = take(3)
    qn_mine = take(2)
    dqp, qup_side, n1, inv1, dy, gain1, gain2_sum, gain_c_sum = take(8)
    grad_out, grad_qup, grad_qdown, grad_kv, grad_tokens, gains = take(6)
    got_a, out_a, got_b, out_b, got_c, out_c = take(6)
    side_sums, side_got = take(2)
    send, kept, row_got, row_out, row_back = take(5)
    kv_out, kv_got = take(2)
    sums, sums_core, sums_cross, sums_side, sums_line = take(5)
    wire = Wire(*take(2))
    half, rows = 2 * quarter, 4 * quarter
    place = wire.place
    wire.greet(4, 3, diagonal=True)

    for z in range(4):
        side_sums[z] = terms_sum([(h1_theirs[m][z], dfirst[m]) for m in range(2)]).astype(LOW)
    side_first = wire.send(side_sums, side_got, wire.beside)

    def out_term(z):
        return terms_sum(halves_terms(
            [dyl_mine[m, z] for m in range(2)], [dyl_got[m, z] for m in range(2)],
            [dyl_far[m, z] for m in range(2)], (*o, *oo), half))

    def qup_term(z):
        return terms_sum([(qn_mine[m][z], dqp[m]) for m in range(2)]) + qup_side[z].astype(F32)

    def first_term(z):
        return terms_sum([(h1_mine[m][z], dfirst[m]) for m in range(2)]) + side_got[z].astype(F32)

    def keep_out(total):
        grad_out[...] = jnp.transpose(total)

    def keep_qup(total):
        grad_qup[...] = total

    part = grad_qdown.shape[1]

    def keep_first(total):
        grad_qdown[...] = total[:, :part]
        kv_out[...] = total[:, part:]

    out = LineSum(wire, out_term, (got_a, out_a), *grad_out.shape[::-1], keep_out)
    qup = LineSum(wire, qup_term, (got_b, out_b), *grad_qup.shape, keep_qup)
    first = LineSum(wire, first_term, (got_c, out_c), kv_out.shape[0], dfirst.shape[2], keep_first)
    for chain in (out, qup, first):
        chain.clear()
    row_sum = RowSum(wire, send, kept, row_got, row_out, row_back, quarter)
    out.step1()
    for m in range(2):
        send[m] = inner_cols(dfirst[m, half:, :], weights[...]).astype(LOW)
    row_sum.core.start()
    for m in range(2):
        kept[m] = inner_cols(dfirst[m, :half, :], weights[...])
    row_sum.pass_on()
    qup.step1()
    out.step2()
    qup.step2()
    dh1 = row_sum.result()
    gain1_sum = jnp.sum(jnp.sum(dh1 * n1[...], axis=0), axis=0, keepdims=True)
    back = dh1 * gain1[...]
    share = Share(wire, grad_tokens, quarter)
    share.begin(
        (dy[...] + inv1[...] * (back - n1[...] * mean_of(back * n1[...]))).astype(LOW)
    )
    w, r = gain1_sum.shape[1] // 8, gain_c_sum.shape[1] // 8
    for s in range(8):
        sums[s] = jnp.concatenate(
            [gain1_sum[:, s * w : (s + 1) * w], gain2_sum[:, s * w : (s + 1) * w],
             gain_c_sum[:, s * r : (s + 1) * r]], axis=1
        )
    core_sums = wire.send(sums, sums_core, wire.core)
    side_first.wait_recv()
    first.step1()
    out.step3()
    core_sums.wait_recv()
    core_sums.wait_send()
    sums[...] = sums[...] + sums_core[...]
    cross_sums = wire.send(sums, sums_cross, wire.cross)
    qup.step3()
    share.forward()
    first.step2()
    cross_sums.wait_recv()
    cross_sums.wait_send()
    sums[...] = sums[...] + sums_cross[...]
    side_of = lambda p, s: sums.at[2 * p + s]
    side_sends = [
        wire.send(side_of(p, 1 - wire.side), sums_side.at[p], wire.beside) for p in range(4)
    ]
    out.finish()
    first.step3()
    for made in side_sends:
        made.wait_recv()
        made.wait_send()
    line_sends = []
    for d in range(1, 4):
        for way, there in ((1, place + d <= 3), (-1, place - d >= 0)):
            index = 2 * (d - 1) + (way < 0)
            line_sends.append(
                (wire.copy(sums_line.at[6 + index], sums_line.at[index],
                           {"seq": wire.seq + 2 * way * d}), d, way, there)
            )

            @pl.when(there)
            def _(index=index, d=d, way=way):
                to = place + way * d
                sums_line[6 + index] = sums[2 * to + wire.side] + sums_side[to]
                line_sends[-1][0].start()

            @pl.when((place - way * d < 0) | (place - way * d > 3))
            def _(index=index):
                sums_line[index] = jnp.zeros(sums_line.shape[1:], F32)

    qup.finish()
    first.finish()
    cores = []
    size = kv_out.shape[0] // 4
    for k in range(4):
        rows_of = pl.ds(pl.multiple_of(wire.blocks[k] * size, size), size)
        if k:
            device = {"mp": wire.blocks[k]}
            cores.append(wire.send(kv_out.at[rows_of], kv_got.at[k], device))
        else:
            kv_got[0] = kv_out[rows_of]
    total = sums[2 * place + wire.side] + sums_side[place]
    for made, d, way, there in line_sends:
        pl.when((place - way * d >= 0) & (place - way * d <= 3))(made.wait_recv)
    for index in range(6):
        total = total + sums_line[index]
    gains[...] = total
    for made in cores:
        made.wait_recv()
    columns = kv_out.shape[1]
    for k in range(4):
        at = pl.ds(pl.multiple_of(wire.blocks[k] * columns, columns), columns)
        grad_kv[:, at] = kv_got[k]
    share.end()
    for made in (side_first, *cores):
        made.wait_send()
    for made, d, way, there in line_sends:
        pl.when(there)(made.wait_send)
    row_sum.end()
    for chain in (out, qup, first):
        chain.settle()


def local(
    tokens,
    lengths,
    norm1_gain,
    q_down,
    latent_gain,
    q_up,
    kv_proj,
    out_proj,
    norm2_gain,
    w_gate,
    w_up,
    w_down,
    cotangent,
):
    micro, rows, width = tokens.shape
    seq = lax.axis_size("seq")
    line = seq // 2
    at = lax.axis_index("seq").astype(jnp.int32)
    me = lax.axis_index("mp").astype(jnp.int32)
    place, side = at // 2, at % 2
    ids = jnp.stack([me, side])
    quarter, half = rows // 4, rows // 2
    head_dim = kv_proj.shape[1] // 2
    heads = q_up.shape[1] // head_dim
    part = q_down.shape[1]
    rank = q_up.shape[0]
    hidden = w_gate.shape[1]
    kv_part = kv_proj.shape[1] // 4
    wide = width // seq
    scale = head_dim ** (-0.5)
    key_count = seq * rows
    beside = [(i, i ^ 1) for i in range(seq)]
    narrow = line == 4 and micro == 2 and key_count <= 2048 and not wide % 128

    def swap(index):
        return ((index & 1) << 1) | (index >> 1)

    def to_natural(array, axis):
        size = array.shape[axis] // 4
        return jnp.concatenate(
            [lax.dynamic_slice_in_dim(array, swap(me ^ b) * size, size, axis) for b in range(4)],
            axis,
        )

    def other(array):
        return lax.ppermute(array, "seq", beside)

    def sum_mp(send, keep):
        kept = keep + lax.ppermute(send, "mp", CORE).astype(F32)
        got = lax.ppermute(kept[..., quarter:, :].astype(LOW), "mp", CROSS)
        return kept[..., :quarter, :] + got.astype(F32)

    def gather_mp(piece):
        near = lax.ppermute(piece, "mp", CROSS)
        pair = jnp.concatenate([piece, near], -2)
        return piece, near, lax.ppermute(pair, "mp", CORE)

    def sides_shape(columns, their_rows, lead=()):
        if columns // seq % 128:
            return []
        return [
            whole((*lead, line, n, columns // seq), LOW) for n in (rows, their_rows)
        ]

    def split_sides(made, full, their_rows):
        if made:
            return made
        split = full.reshape(*full.shape[:-1], line, 2, full.shape[-1] // seq)
        mine, theirs = (
            jnp.moveaxis(lax.dynamic_index_in_dim(split, i, split.ndim - 2, keepdims=False), -2, -3)
            for i in (side, 1 - side)
        )
        return mine, theirs[..., :their_rows, :]

    def from_other(theirs):
        got = other(theirs)
        return got, lax.ppermute(got, "mp", CORE)

    def without_sides(body, count):
        return body if count else lambda *refs: body(*refs, None, None)

    def both_sides(mine, got):
        lefts, spans = [], []
        for array, first, count, partner in (
            (mine, 0, rows, 0), (got[0], 0, half, 1), (got[1], half, half, 1)
        ):
            stacked_array = not isinstance(array, list)
            for m in range(micro):
                spans.append((len(lefts) if not stacked_array else len(lefts), m if stacked_array else None,
                              m, partner, first, count))
                if not stacked_array:
                    lefts.append(array[m])
            if stacked_array:
                lefts.append(array)
        return lefts, spans

    class Chain:
        def __init__(self, lefts, rights, terms, shape, turned=False, from_side=None):
            self.args = [*lefts, *rights]
            self.spec = (terms, len(lefts), len(rights))
            self.shape, self.turned = shape, turned
            self.from_side = [] if from_side is None else [from_side]
            self.step, self.up, self.down = 0, None, None

        def block(self, index, added, after, last=False):
            turned = last and self.turned
            body = functools.partial(
                block_body, *self.spec, len(added), len(self.from_side), turned
            )
            shape = self.shape[::-1] if turned else self.shape
            return run(
                body, index.reshape(1), [*self.args, *added, *self.from_side],
                [whole(shape, F32 if last else LOW)], after, name="block",
            )[0]

        def advance(self, after):
            self.step += 1
            step = self.step
            goes_up = [(i, i + 2) for i in range(2 * step)]
            goes_down = [(seq - 1 - i, seq - 3 - i) for i in range(2 * step)]
            for_up, for_down = line - step + place, step - line + place
            if 2 * step < line + 1:
                which = jnp.where(
                    place <= step - 1, for_up, jnp.where(place >= line - step, for_down, 0)
                )
                term = self.block(which, [a for a in (self.up, self.down) if a is not None], after)
                if step == 1 and line > 3:
                    self.up = lax.ppermute(term, "seq", goes_up + goes_down)
                else:
                    self.up = lax.ppermute(term, "seq", goes_up)
                    self.down = lax.ppermute(term, "seq", goes_down)
                return [term]
            term_up = self.block(jnp.clip(for_up, 0, line - 1), [self.up], after)
            term_down = self.block(jnp.clip(for_down, 0, line - 1), [self.down], [term_up])
            self.up = lax.ppermute(term_up, "seq", goes_up)
            self.down = lax.ppermute(term_down, "seq", goes_down)
            return [term_down]

        def finish(self, after):
            while self.step < line - 1:
                after = self.advance(after)
            result = self.block(place, [self.up, self.down], after, last=True)
            return result, [result]

    quarter_rows = jnp.arange(quarter, dtype=jnp.int32)
    row_ids = at * rows + jnp.concatenate([(me ^ k) * quarter + quarter_rows for k in ORDER])
    key_ids = (
        ((place - jnp.arange(line, dtype=jnp.int32)[None, None, :, None, None]) * 2
         + (side ^ jnp.arange(2, dtype=jnp.int32)[None, :, None, None, None])) * rows
        + (me ^ (jnp.arange(2, dtype=jnp.int32)[:, None, None, None, None]
                 + 2 * jnp.arange(2, dtype=jnp.int32)[None, None, None, :, None])) * quarter
        + quarter_rows[None, None, None, None, :]
    ).reshape(key_count)

    gain1_row, gain2_row, gain_c_row = norm1_gain[None, :], norm2_gain[None, :], latent_gain[None, :]
    kv_cols = lax.dynamic_slice_in_dim(kv_proj, me * kv_part, kv_part, 1)
    first_weights = jnp.concatenate([q_down, kv_cols], axis=1)
    both_rows = sides_shape(width, rows)
    half_rows = sides_shape(width, half)
    rank_sides = sides_shape(rank, rows)

    tables, starts, kv, c_part, h1_sides = [], [], [], [], []
    order = []
    for m in range(micro):
        _, places = documents(lengths[m], row_ids)
        starts.append(row_ids - places)
        tables.append(rotation(places, head_dim))
        c, packed, h1, *made = run(
            without_sides(functools.partial(first_body, m, quarter), len(both_rows)),
            ids,
            [tokens, gain1_row, q_down, kv_proj, *tables[m]],
            [whole((rows, part), LOW), whole((half, 2 * head_dim), LOW), whole((rows, width), LOW),
             *both_rows],
            order,
            name="first",
        )
        order = [c]
        blocks = [packed] + [
            lax.ppermute(packed, "seq", [(i, i + 2 * d) for i in range(seq - 2 * d)])
            for d in range(1, line)
        ]
        near = jnp.stack(blocks, 0)
        near = jnp.stack([near, other(near)], 0)
        kv.append(
            jnp.stack([near, lax.ppermute(near, "mp", CORE)], 0).reshape(key_count, 2 * head_dim)
        )
        c_part.append(c)
        h1_sides.append(split_sides(made, h1, rows))

    dhid, dz, *made = run(
        functools.partial(cotangent_body, micro, quarter),
        ids,
        [cotangent, w_down],
        [whole((micro, rows, hidden), F32), whole((micro, rows, width), LOW),
         *sides_shape(width, half, (micro,))],
        order,
        name="cotangent",
    )
    order = [dz]
    dz_mine, dz_theirs = split_sides(made, dz, half)
    dz_got = from_other(dz_theirs)

    qn_sides, qs, os, lses, sums, c_rows = [], [], [], [], [], []
    for m in range(micro):
        near = lax.ppermute(c_part[m], "mp", CROSS)
        swapped = jnp.concatenate(
            [near[quarter : 2 * quarter], near[:quarter], near[3 * quarter :],
             near[2 * quarter : 3 * quarter]], 0
        )
        far = lax.ppermute(jnp.concatenate([c_part[m], swapped], 1), "mp", CORE)
        qn, q, o, lse, send, keep, *made = run(
            without_sides(functools.partial(attend_body, scale), len(rank_sides)),
            ids,
            [c_part[m], near, far, gain_c_row, q_up, *tables[m], kv[m], key_ids[None, :],
             row_ids[:, None], starts[m][:, None], out_proj],
            [whole((rows, rank), LOW), whole((heads, rows, head_dim), LOW),
             whole((rows, heads * head_dim), LOW), whole((heads, rows), F32),
             whole((half, width), LOW), whole((half, width), F32), *rank_sides],
            order,
            name="attend",
        )
        order = [o]
        qn_sides.append(split_sides(made, qn, rows))
        qs.append(q)
        os.append(o)
        lses.append(lse)
        sums.append(sum_mp(send, keep))
        c_rows.append(
            jnp.concatenate([c_part[m][:quarter], swapped[:quarter], far[half : half + quarter]], 1)
        )

    h2_mine, h2_theirs, hid, dg, du, state = [], [], [], [], [], []
    for m in range(micro):
        x = lax.dynamic_slice_in_dim(tokens[m], me * quarter, quarter, 0).astype(F32)
        inv1 = inverse_rms(x)
        y = x + sums[m]
        inv2 = inverse_rms(y)
        n2 = y * inv2
        pieces = gather_mp((n2 * gain2_row).astype(LOW))
        h2, hid_m, dg_m, du_m, *made = run(
            without_sides(functools.partial(forward_body, m), len(half_rows)),
            ids,
            [*pieces, w_gate, w_up, dhid],
            [whole((rows, width), LOW), *[whole((rows, hidden), LOW)] * 3, *half_rows],
            order,
            name="forward",
        )
        order = [hid_m]
        mine, theirs = split_sides(made, h2, half)
        h2_mine.append(mine)
        h2_theirs.append(theirs)
        hid.append(hid_m)
        dg.append(dg_m)
        du.append(du_m)
        state.append(dict(x=x, n1=x * inv1, inv1=inv1, y=y, n2=n2, inv2=inv2, c=c_rows[m]))

    def stacked(name):
        return jnp.stack([st[name] for st in state], 0)

    def with_other(arrays):
        return [*arrays, *[other(a) for a in arrays]]

    def terms_of(spans):
        return [(a, lead, m + micro * partner, None, first, count)
                for a, lead, m, partner, first, count in spans]

    send, keep, ffn_send, ffn_keep = run(
        functools.partial(hidden_back_body, micro),
        ids,
        [*dg, *du, *hid, w_gate, w_up, w_down],
        [whole((micro, half, width), LOW), whole((micro, half, width), F32)] * 2,
        order,
        name="hidden_back",
    )
    if narrow:
        y, n2, inv2, n1, inv1 = (stacked(k) for k in ("y", "n2", "inv2", "n1", "inv1"))
        low = lambda *shape: pltpu.VMEM(shape, LOW)
        full = lambda *shape: pltpu.VMEM(shape, F32)
        near = lambda *arrays: [(1, a) for a in arrays]
        far = lambda *arrays: [(0, a) for a in arrays]
        columns = heads * head_dim
        both_columns = rank + 2 * head_dim
        first_columns = part + kv_part

        args = near(*hid, other(hid[0]), dz_mine, *dz_got) + far(*h2_theirs, *dg)
        args += near(send, keep, n2, inv2, dz, gain2_row, out_proj, q_up, key_ids[:, None])
        for m in range(micro):
            args += near(qs[m], kv[m], os[m], lses[m], jnp.stack([row_ids, starts[m]], 0),
                         *tables[m])
        outs = near(
            whole((hidden, wide), F32), whole((micro, quarter, width), F32),
            whole((1, width), F32), whole((micro, line, rows, wide), LOW),
            whole((micro, line, half, wide), LOW), whole((micro, rows, columns), LOW),
            whole((micro, half, rank), LOW), whole((micro, half, rank), F32),
            whole((micro, key_count // 2, 2 * head_dim), LOW),
            whole((micro, key_count // 2, 2 * head_dim), F32),
        ) + far(*[whole((line, half, wide), LOW)] * 4, *[whole((rows, hidden), LOW)] * 2)
        (grad_down, dy, gain2, dyl_mine, dyl_theirs, dqp, send, keep, kv_send, kv_keep,
         *exchanged) = mesh_run(
            functools.partial(back1_body, quarter, scale, 1024), args, outs,
            [low(rows, hidden), low(5, wide, hidden), low(3, wide, hidden),
             low(micro, half, width), low(micro, quarter, width), low(micro, quarter, width),
             low(micro, rows, width), full(heads, rows, head_dim), low(heads, rows, head_dim),
             full(heads, 8, rows)],
            1, "back1", 60, 24,
        )

        c = stacked("c").astype(F32)
        inv_c = inverse_rms(c)
        chat = to_natural(c * inv_c, 2)
        kv_shape = (micro, 2 * line, 2, quarter, 2 * head_dim)
        args = near(*dg, *exchanged[4:6], *du, *h2_mine, *exchanged[0:4])
        args += far(kv_send.reshape(kv_shape)) + near(kv_keep.reshape(kv_shape)) + far(send)
        args += near(keep, chat, inv_c, gain_c_row,
                     jnp.stack([t[0][:quarter] for t in tables], 0),
                     jnp.stack([t[1][:quarter] for t in tables], 0),
                     *[pair[1] for pair in qn_sides], dqp)
        args += far(dyl_theirs, *os, ffn_send) + near(ffn_keep, y)
        side_rows = rank // seq
        outs = near(whole((wide, hidden), F32), whole((wide, hidden), F32),
                    whole((micro, rows, first_columns), LOW), whole((1, rank), F32))
        outs += far(whole((line, side_rows, columns), LOW),
                    *[whole((micro, line, half, wide), LOW)] * 2,
                    *[whole((rows, columns), LOW)] * 2)
        outs += near(whole((micro, rows, width), LOW))
        kv_low = lambda *lead: low(*lead, quarter, 2 * head_dim)
        (grad_gate, grad_up, dfirst, gain_c, qup_side, dyl_got, dyl_far, *o_other,
         layer_out) = mesh_run(
            functools.partial(back2_body, quarter), args, outs,
            [low(rows, hidden), low(rows, hidden), low(5, wide, hidden), low(3, wide, hidden),
             low(5, wide, hidden), low(3, wide, hidden), low(micro, half, rank),
             low(micro, quarter, rank), low(micro, quarter, rank), kv_low(micro, 2 * line, 2),
             kv_low(micro, 2 * line), kv_low(micro, 2 * line), kv_low(micro, line),
             kv_low(micro, line), kv_low(3, micro), kv_low(3, micro),
             full(micro, quarter, 2 * head_dim), low(micro, rows, both_columns),
             low(line, side_rows, columns), low(micro, half, width), low(micro, quarter, width),
             low(micro, quarter, width)],
            2, "back2", 60, 40,
        )

        args = near(dfirst, first_weights, *[pair[0] for pair in h1_sides],
                    *[pair[1] for pair in h1_sides], *os, *o_other, dyl_mine, dyl_got, dyl_far,
                    *[pair[0] for pair in qn_sides], dqp, qup_side, n1, inv1, dy, gain1_row,
                    gain2, gain_c)
        block = width // 4 // seq
        gain_columns = 2 * wide + side_rows
        outs = near(whole((columns, wide), F32), whole((side_rows, columns), F32),
                    whole((wide, part), F32), whole((block, 2 * head_dim), F32),
                    whole((micro, rows, width), LOW), whole((1, gain_columns), F32))
        grad_out, grad_qup, grad_qdown, grad_kv, input_grads, gains = mesh_run(
            functools.partial(back3_body, quarter), args, outs,
            [low(5, wide, columns), low(3, wide, columns), low(5, side_rows, columns),
             low(3, side_rows, columns), low(5, wide, first_columns),
             low(3, wide, first_columns), low(line, wide, first_columns),
             low(line, wide, first_columns), low(micro, half, width), full(micro, half, width),
             low(micro, half, width), low(micro, quarter, width), low(micro, quarter, width),
             full(wide, kv_part), full(4, block, kv_part), full(seq, 1, gain_columns),
             full(seq, 1, gain_columns), full(seq, 1, gain_columns), full(line, 1, gain_columns),
             full(12, 1, gain_columns)],
            3, "back3", 60, 44,
        )
        return (
            layer_out, input_grads, gains[0, :wide], grad_qdown, gains[0, 2 * wide :], grad_qup,
            grad_kv, grad_out, gains[0, wide : 2 * wide], grad_gate, grad_up, grad_down,
        )

    lefts, spans = both_sides(dz_mine, dz_got)
    chain_down = Chain(lefts, with_other(hid), terms_of(spans), (wide, hidden), turned=True)
    lefts, spans = both_sides(h2_mine, [list(p) for p in zip(*[from_other(t) for t in h2_theirs])])
    chain_gate = Chain(lefts, with_other(dg), terms_of(spans), (wide, hidden))
    chain_up = Chain(lefts, with_other(du), terms_of(spans), (wide, hidden))

    order = chain_down.advance([send])
    dh2 = sum_mp(send, keep)
    y, n2, inv2, n1, inv1 = (stacked(k) for k in ("y", "n2", "inv2", "n1", "inv1"))
    dz_own = dz[:, :quarter].astype(F32)
    gain2 = jnp.sum(dh2 * n2, axis=(0, 1))
    dy = dz_own + norm_backward(dh2 * gain2_row, n2, inv2)
    for _ in range(2):
        order = chain_down.advance(order)
    order = chain_gate.advance(order)

    def attend_back(which, pieces):
        args = [*pieces, out_proj, q_up, key_ids[:, None]]
        for m in which:
            args += [qs[m], kv[m], os[m], lses[m], jnp.stack([row_ids, starts[m]], 0), *tables[m]]
        n = len(which)
        return run(
            functools.partial(attend_back_body, scale, n, min(1024, key_count // 2)),
            ids,
            args,
            [whole((n, rows, width), LOW), whole((n, rows, heads * head_dim), LOW),
             whole((n, half, rank), LOW), whole((n, half, rank), F32),
             whole((n, key_count // 2, 2 * head_dim), LOW),
             whole((n, key_count // 2, 2 * head_dim), F32), *sides_shape(width, half, (n,))],
            order,
            scratch=[pltpu.VMEM((heads, rows, head_dim), F32),
                     pltpu.VMEM((heads, rows, head_dim), LOW),
                     pltpu.VMEM((heads, 8, rows), F32)],
            name="attend_back",
            limit=56,
        )

    pieces = gather_mp(dy.astype(LOW))
    if key_count <= 2048:
        made = attend_back(range(micro), pieces)
    else:
        each = [attend_back([m], [p[m : m + 1] for p in pieces]) for m in range(micro)]
        made = [jnp.concatenate(parts, 0) for parts in zip(*each)]
    dyl, dqp, send, keep, kv_send, kv_keep, *made = made
    order = [send]
    dyl_mine, dyl_theirs = split_sides(made, dyl, half)
    lefts, spans = both_sides(dyl_mine, from_other(dyl_theirs))
    chain_out = Chain(lefts, with_other(os), terms_of(spans), (wide, heads * head_dim), turned=True)

    def side_sum(lefts, rights, shape, after):
        terms = [(m, None, 0, m, 0, rows) for m in range(micro)]
        (made,) = run(
            functools.partial(side_sum_body, terms, len(lefts)),
            ids,
            [*lefts, *rights],
            [whole((line, *shape), LOW)],
            after,
            name="side_sum",
        )
        return other(made), [made]

    def own_chain(side_pairs, right, shape, after):
        from_side, after = side_sum([p[1] for p in side_pairs], [right], shape, after)
        terms = [(m, None, 0, m, 0, rows) for m in range(micro)]
        return Chain([p[0] for p in side_pairs], [right], terms, shape, from_side=from_side), after

    shape = (rank // seq, heads * head_dim)
    chain_qup, order = own_chain(qn_sides, dqp, shape, order)
    order = chain_gate.advance(order)
    order = chain_up.advance(order)

    dqn = sum_mp(send, keep)
    c = stacked("c").astype(F32)
    inv_c = inverse_rms(c)
    chat = c * inv_c
    chat = to_natural(chat, 2)
    gain_c = jnp.sum(dqn * chat, axis=(0, 1))
    dc = norm_backward(dqn * gain_c_row, chat, inv_c).astype(LOW)

    dkv = kv_keep + lax.ppermute(kv_send, "mp", CORE).astype(F32)
    dkv = dkv.reshape(micro, 2, line, 2, quarter, 2 * head_dim)
    dkv = dkv[:, :, :, 0] + lax.ppermute(dkv[:, :, :, 1].astype(LOW), "mp", CROSS).astype(F32)
    dkv = dkv[:, 0] + other(dkv[:, 1].astype(LOW)).astype(F32)
    total = dkv[:, 0]
    for d in range(1, line):
        total = total + lax.ppermute(
            dkv[:, d].astype(LOW), "seq", [(i + 2 * d, i) for i in range(seq - 2 * d)]
        ).astype(F32)
    cosine = jnp.stack([t[0][:quarter] for t in tables], 0)
    sine = jnp.stack([t[1][:quarter] for t in tables], 0)
    dkv_low = jnp.concatenate(
        [unrotate(total[..., :head_dim], cosine, sine), total[..., head_dim:]], axis=-1
    ).astype(LOW)
    both = jnp.concatenate(gather_mp(jnp.concatenate([dc, dkv_low], -1)), -2)
    dfirst = jnp.concatenate(
        [lax.dynamic_slice_in_dim(both, me * part, part, 2),
         lax.dynamic_slice_in_dim(both, rank + me * kv_part, kv_part, 2)], -1
    )

    grad_down, order = chain_down.finish(order)
    order = chain_gate.advance(order)
    order = chain_up.advance(order)
    order = chain_out.advance(order)
    grad_gate, order = chain_gate.finish(order)
    order = chain_up.advance(order)
    order = chain_out.advance(order)
    grad_up, order = chain_up.finish(order)
    order = chain_qup.advance(order)
    order = chain_out.advance(order)
    chain_first, order = own_chain(h1_sides, dfirst, (wide, part + kv_part), order)
    order = chain_qup.advance(order)
    grad_out, order = chain_out.finish(order)
    order = chain_first.advance(order)
    order = chain_qup.advance(order)
    order = chain_first.advance(order)
    grad_qup, order = chain_qup.finish(order)
    order = chain_first.advance(order)
    grad_first, order = chain_first.finish(order)

    grad_qdown = grad_first[:, :part]
    kv_cols_grad = grad_first[:, part:]
    pieces = []
    for k in ORDER:
        size = kv_cols_grad.shape[0] // 4
        sent = lax.dynamic_slice_in_dim(kv_cols_grad, (me ^ k) * size, size, 0)
        pieces.append(lax.ppermute(sent, "mp", [(i, i ^ k) for i in range(4)]) if k else sent)
    grad_kv = to_natural(jnp.concatenate(pieces, 1), 1)

    def put_natural(pieces):
        return run(
            functools.partial(natural_body, micro, quarter),
            ids,
            pieces,
            [whole((micro, rows, width), LOW)],
            name="natural",
        )[0]

    part_sum = inner_cols(dfirst.reshape(micro * rows, -1), first_weights).reshape(micro, rows, width)
    dh1 = sum_mp(part_sum[:, half:].astype(LOW), part_sum[:, :half])
    gain1 = jnp.sum(dh1 * n1, axis=(0, 1))
    dx = (dy + norm_backward(dh1 * gain1_row, n1, inv1)).astype(LOW)
    input_grads = put_natural(gather_mp(dx))

    ffn = sum_mp(ffn_send, ffn_keep)
    layer_out = put_natural(gather_mp((y + ffn).astype(LOW)))

    gains = jnp.concatenate(
        [gain1.reshape(seq, -1), gain2.reshape(seq, -1), gain_c.reshape(seq, -1)], axis=1
    )
    gains = gains + lax.ppermute(gains, "mp", CORE)
    gains = gains + lax.ppermute(gains, "mp", CROSS)
    gain_sum = lax.dynamic_index_in_dim(gains, at, 0, keepdims=False)
    for k in range(1, seq):
        gain_sum = gain_sum + lax.ppermute(
            lax.dynamic_index_in_dim(gains, at ^ k, 0, keepdims=False),
            "seq",
            [(i, i ^ k) for i in range(seq)],
        )
    return (
        layer_out,
        input_grads,
        gain_sum[:wide],
        grad_qdown,
        gain_sum[2 * wide :],
        grad_qup,
        grad_kv,
        grad_out,
        gain_sum[wide : 2 * wide],
        grad_gate,
        grad_up,
        grad_down,
    )


def solution(mesh):
    placed = (
        P(None, "seq", None),
        P(),
        P(),
        P(None, "mp"),
        P(),
        P(None, "mp"),
        P(),
        P("mp", None),
        P(),
        P(None, "mp"),
        P(None, "mp"),
        P("mp", None),
        P(None, "seq", None),
    )
    return jax.shard_map(
        local,
        mesh=mesh,
        in_specs=placed,
        out_specs=(
            P(None, "seq", None),
            P(None, "seq", None),
            P("seq"),
            P("seq", "mp"),
            P("seq"),
            P("seq", "mp"),
            P(("seq", "mp"), None),
            P("mp", "seq"),
            P("seq"),
            P("seq", "mp"),
            P("seq", "mp"),
            P("mp", "seq"),
        ),
        check_vma=False,
    )
```

```python
import functools

import jax
import jax.numpy as jnp
from jax import lax
from jax.experimental import pallas as pl
from jax.experimental.pallas import tpu as pltpu
from jax.sharding import PartitionSpec as P

EPS = 1e-06
BASE = 10000.0
NEG_LARGE = -1e30
LOW = jnp.bfloat16
F32 = jnp.float32
ORDER = (0, 2, 1, 3)
CORE = [(i, i ^ 1) for i in range(4)]
CROSS = [(i, i ^ 2) for i in range(4)]


def inverse_rms(values):
    return lax.rsqrt(jnp.mean(values * values, axis=-1, keepdims=True) + EPS)


def norm_backward(grad_hat, normed, inverse):
    return inverse * (grad_hat - normed * jnp.mean(grad_hat * normed, axis=-1, keepdims=True))


def dot(left, right):
    return jnp.dot(left, right, preferred_element_type=F32)


def inner_rows(left, right):
    return lax.dot_general(left, right, (((0,), (0,)), ((), ())), preferred_element_type=F32)


def inner_cols(left, right):
    return lax.dot_general(left, right, (((1,), (1,)), ((), ())), preferred_element_type=F32)


def documents(lengths_row, rows):
    first_end = lengths_row[0]
    second_end = first_end + lengths_row[1]
    doc_ids = (rows >= first_end).astype(jnp.int32) + (rows >= second_end).astype(jnp.int32)
    starts = jnp.where(rows >= second_end, second_end, jnp.where(rows >= first_end, first_end, 0))
    return (doc_ids, rows - starts)


def rotation(positions, head_dim):
    half = head_dim // 2
    freqs = BASE ** (-2.0 * jnp.arange(half, dtype=F32) / head_dim)
    angles = positions.astype(F32)[:, None] * freqs[None, :]
    return (jnp.cos(angles), jnp.sin(angles))


def rotate(values, cosine, sine):
    half = values.shape[-1] // 2
    first = values[..., :half]
    second = values[..., half:]
    return jnp.concatenate(
        [first * cosine - second * sine, second * cosine + first * sine], axis=-1
    )


def unrotate(grads, cosine, sine):
    return rotate(grads, cosine, -sine)


def in_vmem():
    return pl.BlockSpec(memory_space=pltpu.VMEM)


def whole(shape, dtype):
    return jax.ShapeDtypeStruct(shape, dtype)


def run(body, ids, args, outs, after=(), scratch=(), name=None, limit=40):
    args, after = list(args), list(after)

    def without(*refs):
        body(*refs[: 1 + len(args)], *refs[1 + len(args) + len(after) :])

    return pl.pallas_call(
        without,
        grid_spec=pltpu.PrefetchScalarGridSpec(
            num_scalar_prefetch=1,
            grid=(1,),
            in_specs=[in_vmem()] * len(args) + [pl.BlockSpec(memory_space=pl.ANY)] * len(after),
            out_specs=[in_vmem()] * len(outs),
            scratch_shapes=list(scratch),
        ),
        out_shape=list(outs),
        cost_estimate=pl.CostEstimate(flops=1000, bytes_accessed=1000, transcendentals=0),
        compiler_params=pltpu.CompilerParams(vmem_limit_bytes=limit << 20),
        name=name,
    )(ids, *args, *after)


def side_columns(source, mine, theirs, side):
    line, _, wide = mine.shape
    rows = theirs.shape[1]
    for z in range(line):
        mine[z] = source[:, pl.ds(pl.multiple_of((2 * z + side) * wide, wide), wide)]
        theirs[z] = source[:rows, pl.ds(pl.multiple_of((2 * z + 1 - side) * wide, wide), wide)]


def first_body(m, quarter, ids, x_ref, gain, q_down, kv_proj, cos, sin, c, kv, h1, mine, theirs):
    blocks = [
        x_ref[m, pl.ds(pl.multiple_of((ids[0] ^ k) * quarter, quarter), quarter), :] for k in ORDER
    ]
    x = jnp.concatenate(blocks, 0).astype(F32)
    low = (x * inverse_rms(x) * gain[...]).astype(LOW)
    h1[...] = low
    half = 2 * quarter
    pair = dot(low[:half], kv_proj[...])
    wide = kv_proj.shape[1] // 2
    kv[:, :wide] = rotate(pair[:, :wide], cos[:half], sin[:half]).astype(LOW)
    kv[:, wide:] = pair[:, wide:].astype(LOW)
    c[...] = dot(low, q_down[...]).astype(LOW)
    if mine is not None:
        side_columns(h1, mine, theirs, ids[1])


def cotangent_body(micro, quarter, ids, z_ref, w_down, dhid, dz, *sides):
    for m in range(micro):
        blocks = [
            z_ref[m, pl.ds(pl.multiple_of((ids[0] ^ k) * quarter, quarter), quarter), :]
            for k in ORDER
        ]
        dz[m] = jnp.concatenate(blocks, 0)
        if sides:
            side_columns(dz.at[m], sides[0].at[m], sides[1].at[m], ids[1])
        dhid[m] = inner_cols(dz[m], w_down[...])


def attend_body(
    scale, ids, c0, c1, c2, gain, q_up, cos, sin, kv, key_ids, row_ids, row_starts, out_proj,
    qn, q, o, lse, send, keep, mine, theirs,
):
    rows = qn.shape[0]
    quarter = rows // 4
    part = c0.shape[1]
    wide = q.shape[2]
    got = c1[...]
    pair = jnp.concatenate(
        [got[quarter : 2 * quarter], got[:quarter], got[3 * quarter :], got[2 * quarter : 3 * quarter]],
        0,
    )
    far = jnp.concatenate([c2[2 * quarter :], c2[: 2 * quarter]], 0)
    c = jnp.concatenate([c0[...], pair, far], 1).astype(F32)
    chat = c * inverse_rms(c)
    for k, xor in enumerate(ORDER):
        columns = pl.ds(pl.multiple_of((ids[0] ^ xor) * part, part), part)
        qn[:, columns] = (chat[:, k * part : (k + 1) * part] * gain[:, columns]).astype(LOW)
    if mine is not None:
        side_columns(qn, mine, theirs, ids[1])
    bias = jnp.where(
        (key_ids[...] >= row_starts[...]) & (key_ids[...] <= row_ids[...]), 0.0, NEG_LARGE
    )
    low = qn[...]
    keys, values = kv[:, :wide], kv[:, wide:]
    for h in range(q.shape[0]):
        pre = dot(low, q_up[:, h * wide : (h + 1) * wide])
        q_h = (rotate(pre, cos[...], sin[...]) * scale).astype(LOW)
        q[h] = q_h
        scores = inner_cols(q_h, keys) + bias
        top = jnp.max(scores, axis=-1, keepdims=True)
        probs = jnp.exp(scores - top)
        total = jnp.sum(probs, axis=-1, keepdims=True)
        out = dot(probs.astype(LOW), values) / total
        o[:, h * wide : (h + 1) * wide] = out.astype(LOW)
        log_total = jnp.broadcast_to(top + jnp.log(total), (rows, 128))
        lse[h : h + 1, :] = jnp.transpose(log_total)[:1]
    half = 2 * quarter
    send[...] = dot(o[half:, :], out_proj[...]).astype(LOW)
    keep[...] = dot(o[:half, :], out_proj[...])


def forward_body(m, ids, a0, a1, a2, w_gate, w_up, dhid, h2, hid, dg, du, mine, theirs):
    h2[...] = jnp.concatenate([a0[...], a1[...], a2[...]], 0)
    if mine is not None:
        side_columns(h2, mine, theirs, ids[1])
    low = h2[...]
    g = dot(low, w_gate[...])
    u = dot(low, w_up[...])
    sig = jax.nn.sigmoid(g)
    swish = g * sig
    hid[...] = (swish * u).astype(LOW)
    back = dhid[m]
    dg[...] = (back * u * sig * (1.0 + g * (1.0 - sig))).astype(LOW)
    du[...] = (back * swish).astype(LOW)


def forward_whole_body(m, ids, h2, w_gate, w_up, dhid, hid, dg, du, mine, theirs):
    side_columns(h2.at[m], mine, theirs, ids[1])
    low = h2[m]
    g = dot(low, w_gate[...])
    u = dot(low, w_up[...])
    sig = jax.nn.sigmoid(g)
    swish = g * sig
    hid[...] = (swish * u).astype(LOW)
    back = dhid[m]
    dg[...] = (back * u * sig * (1.0 + g * (1.0 - sig))).astype(LOW)
    du[...] = (back * swish).astype(LOW)


def hidden_back_body(micro, ids, *refs):
    dgs, dus = refs[:micro], refs[micro : 2 * micro]
    hids = refs[2 * micro : 3 * micro]
    w_gate, w_up, w_down, send, keep, out_send, out_keep = refs[3 * micro :]
    half = send.shape[1]
    every = lambda parts: jnp.concatenate([part[...] for part in parts], 0)
    rows = 2 * half
    total = inner_cols(every(dgs), w_gate[...]) + inner_cols(every(dus), w_up[...])
    for m in range(micro):
        send[m] = total[m * rows + half : (m + 1) * rows].astype(LOW)
        keep[m] = total[m * rows : m * rows + half]
    total = dot(every(hids), w_down[...])
    for m in range(micro):
        out_send[m] = total[m * rows + half : (m + 1) * rows].astype(LOW)
        out_keep[m] = total[m * rows : m * rows + half]


def pick(ref, lead):
    return ref if lead is None else ref.at[lead]


def block_body(terms, lefts, rights, extra, from_side, turned, ids, *refs):
    left, refs = refs[:lefts], refs[lefts:]
    right, refs = refs[:rights], refs[rights:]
    added, out = refs[: extra + from_side], refs[-1]
    total = None
    for a, a_lead, b, b_lead, first, count in terms:
        rows = pick(right[b], b_lead)[first : first + count, :]
        term = inner_rows(pick(left[a], a_lead)[ids[0]], rows)
        total = term if total is None else total + term
    for i, ref in enumerate(added):
        total = total + (ref[ids[0]] if i >= extra else ref[...]).astype(F32)
    out[...] = jnp.transpose(total) if turned else total.astype(out.dtype)


def side_sum_body(terms, lefts, ids, *refs):
    left, right, out = refs[:lefts], refs[lefts:-1], refs[-1]
    for z in range(out.shape[0]):
        total = None
        for a, a_lead, b, b_lead, first, count in terms:
            rows = pick(right[b], b_lead)[first : first + count, :]
            term = inner_rows(pick(left[a], a_lead)[z], rows)
            total = term if total is None else total + term
        out[z] = total.astype(out.dtype)


def attend_back_body(
    scale, micro, chunk, ids, a0, a1, a2, out_proj, q_up, key_ids, *refs
):
    per = 7
    groups = [refs[m * per : (m + 1) * per] for m in range(micro)]
    dyl_out, dqp, send, keep, kv_send, kv_keep = refs[micro * per : micro * per + 6]
    dq_acc, do_acc, delta_acc = refs[-3:]
    sides = refs[micro * per + 6 : -3]
    for m in range(micro):
        q, kv, o, lse, row_ids, cos, sin = groups[m]
        heads, rows, wide = q.shape
        half_rows = rows // 2
        dyl = jnp.concatenate([a0[m], a1[m], a2[m]], 0)
        dyl_out[m] = dyl
        if sides:
            side_columns(dyl_out.at[m], sides[0].at[m], sides[1].at[m], ids[1])
        for h in range(heads):
            do = inner_cols(dyl, out_proj[h * wide : (h + 1) * wide, :]).astype(LOW)
            do_acc[h] = do
            delta = jnp.sum(
                do.astype(F32) * o[:, h * wide : (h + 1) * wide].astype(F32), axis=-1, keepdims=True
            )
            delta_acc[h] = jnp.transpose(jnp.broadcast_to(delta, (rows, 128)))[:8]
            dq_acc[h] = jnp.zeros((rows, wide), F32)
        count = kv.shape[0] // 2 // chunk
        for part, out in ((0, kv_keep), (1, kv_send)):

            def one(i, carry):
                base = pl.multiple_of((part * count + i) * chunk, chunk)
                keys = kv[pl.ds(base, chunk), :wide]
                values = kv[pl.ds(base, chunk), wide:]
                at = key_ids[pl.ds(base, chunk), :]
                bias = jnp.where((at >= row_ids[1:2, :]) & (at <= row_ids[0:1, :]), 0.0, NEG_LARGE)

                def head(h, sums):
                    dk, dv = sums
                    q_h, do_h = q[h], do_acc[h]
                    probs = jnp.exp(inner_cols(keys, q_h) + bias - lse[pl.ds(h, 1), :])
                    back = inner_cols(values, do_h) - delta_acc[h][:1]
                    ds = (probs * back).astype(LOW)
                    dv = dv + dot(probs.astype(LOW), do_h)
                    dk = dk + dot(ds, q_h)
                    dq_acc[h] = dq_acc[h] + inner_rows(ds, keys)
                    return dk, dv

                zero = jnp.zeros((chunk, wide), F32)
                dk, dv = lax.fori_loop(0, heads, head, (zero, zero))
                place = pl.ds(pl.multiple_of(i * chunk, chunk), chunk)
                out[m, place, :wide] = dk.astype(out.dtype)
                out[m, place, wide:] = dv.astype(out.dtype)
                return carry

            if count == 1:
                one(0, 0)
            else:
                lax.fori_loop(0, count, one, 0)
        for h in range(heads):
            dq = unrotate(dq_acc[h] * scale, cos[...], sin[...])
            dqp[m, :, h * wide : (h + 1) * wide] = dq.astype(LOW)
        low = dqp[m]
        send[m] = inner_cols(low[half_rows:], q_up[...]).astype(LOW)
        keep[m] = inner_cols(low[:half_rows], q_up[...])


def natural_body(micro, quarter, ids, a0, a1, a2, out):
    for m in range(micro):
        pieces = (a0[m], a1[m], a2[m, :quarter, :], a2[m, quarter:, :])
        for k, piece in zip(ORDER, pieces):
            out[m, pl.ds(pl.multiple_of((ids[0] ^ k) * quarter, quarter), quarter), :] = piece


class Wire:
    def __init__(self, sends, recvs):
        self.sends, self.recvs, self.used = sends, recvs, 0
        self.seq, self.mp = lax.axis_index("seq"), lax.axis_index("mp")
        self.place, self.side = self.seq // 2, self.seq % 2
        core, cross = self.mp % 2, self.mp // 2
        self.blocks = (
            self.mp, 2 * (1 - cross) + core, 2 * cross + 1 - core, 2 * (1 - cross) + 1 - core
        )
        self.core, self.cross = {"mp": self.blocks[2]}, {"mp": self.blocks[1]}
        self.beside = {"seq": self.seq + 1 - 2 * self.side}
        self.up, self.down = {"seq": self.seq + 2}, {"seq": self.seq - 2}

    def copy(self, source, target, device):
        at = self.used
        self.used += 1
        return pltpu.make_async_remote_copy(
            src_ref=source, dst_ref=target, send_sem=self.sends.at[at], recv_sem=self.recvs.at[at],
            device_id=device, device_id_type=pl.DeviceIdType.MESH,
        )

    def send(self, source, target, device):
        made = self.copy(source, target, device)
        made.start()
        return made

    def greet(self, line, far=1, diagonal=False):
        barrier = pltpu.get_barrier_semaphore()
        devices = [self.core, self.cross, self.beside]
        if diagonal:
            devices.append({"mp": self.blocks[3]})
        for device in devices:
            pl.semaphore_signal(barrier, 1, device_id=device, device_id_type=pl.DeviceIdType.MESH)
        for d in range(1, far + 1):
            for way, there in ((1, self.place < line - d), (-1, self.place >= d)):

                @pl.when(there)
                def _():
                    pl.semaphore_signal(
                        barrier, 1, device_id={"seq": self.seq + 2 * way * d},
                        device_id_type=pl.DeviceIdType.MESH,
                    )
        below, above = jnp.minimum(self.place, far), jnp.minimum(line - 1 - self.place, far)
        pl.semaphore_wait(barrier, len(devices) + below + above)


class LineSum:
    def __init__(self, wire, term, room, rows, columns, keep):
        got, out = room
        view = lambda ref, i: ref.at[i, :rows, :columns]
        self.place, self.term, self.keep = wire.place, term, keep
        self.got = [view(got, i) for i in range(5)]
        self.out = [view(out, i) for i in range(3)]
        one, two_up, two_down, three_up, three_down = self.got
        a, b, c = self.out
        self.one = wire.copy(a, one, wire.up), wire.copy(a, one, wire.down)
        self.two = wire.copy(b, two_up, wire.up), wire.copy(b, two_down, wire.down)
        self.three = wire.copy(a, three_up, wire.up), wire.copy(c, three_down, wire.down)

    def clear(self):
        place = self.place
        for ref, empty in zip(
            self.got, ((place == 0) | (place == 3),) * 3 + (place == 0, place == 3)
        ):

            @pl.when(empty)
            def _(ref=ref):
                ref[...] = jnp.zeros(ref.shape, ref.dtype)

    def step1(self):
        place = self.place

        @pl.when((place == 0) | (place == 3))
        def _():
            self.out[0][...] = self.term(3 - place).astype(LOW)

        pl.when(place == 0)(self.one[0].start)
        pl.when(place == 3)(self.one[1].start)

    def step2(self):
        place = self.place
        pl.when(place == 1)(self.one[0].wait_recv)
        pl.when(place == 2)(self.one[1].wait_recv)
        self.out[1][...] = (
            self.term((place + 2) % 4) + self.got[0][...].astype(F32)
        ).astype(LOW)
        pl.when(place <= 1)(self.two[0].start)
        pl.when(place >= 2)(self.two[1].start)

    def step3(self):
        place = self.place

        @pl.when((place == 1) | (place == 2))
        def _():
            self.two[0].wait_recv()
            self.two[1].wait_recv()

        pl.when(place == 0)(self.one[0].wait_send)
        pl.when(place == 3)(self.one[1].wait_send)

        @pl.when(place <= 2)
        def _():
            self.out[0][...] = (self.term(place + 1) + self.got[1][...].astype(F32)).astype(LOW)
            self.three[0].start()

        @pl.when(place >= 1)
        def _():
            self.out[2][...] = (self.term(place - 1) + self.got[2][...].astype(F32)).astype(LOW)
            self.three[1].start()

    def finish(self):
        place = self.place
        pl.when(place >= 1)(self.three[0].wait_recv)
        pl.when(place <= 2)(self.three[1].wait_recv)
        self.keep(
            self.term(place) + self.got[3][...].astype(F32) + self.got[4][...].astype(F32)
        )

    def settle(self):
        place = self.place
        pl.when(place <= 1)(self.two[0].wait_send)
        pl.when(place >= 2)(self.two[1].wait_send)
        pl.when(place <= 2)(self.three[0].wait_send)
        pl.when(place >= 1)(self.three[1].wait_send)


def mesh_run(body, args, outs, scratch, number, name, limit, sends):
    return pl.pallas_call(
        body,
        in_specs=[in_vmem() if kind else pl.BlockSpec(memory_space=pl.ANY) for kind, _ in args],
        out_specs=[in_vmem() if kind else pl.BlockSpec(memory_space=pl.ANY) for kind, _ in outs],
        out_shape=[shape for _, shape in outs],
        scratch_shapes=[
            *scratch, pltpu.SemaphoreType.DMA((sends,)), pltpu.SemaphoreType.DMA((sends,))
        ],
        cost_estimate=pl.CostEstimate(flops=1000, bytes_accessed=1000, transcendentals=0),
        compiler_params=pltpu.CompilerParams(
            collective_id=number, has_side_effects=True, vmem_limit_bytes=limit << 20
        ),
        name=name,
    )(*[array for _, array in args])


def attend_back_one(
    scale, chunk, dyl, out_proj, q_up, key_ids, q, kv, o, lse, row_ids, cos, sin,
    dqp, send, keep, kv_send, kv_keep, dq_acc, do_acc, delta_acc,
):
    heads, rows, wide = q.shape
    half_rows = rows // 2
    low = dyl[...]
    for h in range(heads):
        do = inner_cols(low, out_proj[h * wide : (h + 1) * wide, :]).astype(LOW)
        do_acc[h] = do
        delta = jnp.sum(
            do.astype(F32) * o[:, h * wide : (h + 1) * wide].astype(F32), axis=-1, keepdims=True
        )
        delta_acc[h] = jnp.transpose(jnp.broadcast_to(delta, (rows, 128)))[:8]
        dq_acc[h] = jnp.zeros((rows, wide), F32)
    count = kv.shape[0] // 2 // chunk
    for part, out in ((0, kv_keep), (1, kv_send)):
        for i in range(count):
            base = (part * count + i) * chunk
            keys = kv[base : base + chunk, :wide]
            values = kv[base : base + chunk, wide:]
            at = key_ids[base : base + chunk, :]
            bias = jnp.where((at >= row_ids[1:2, :]) & (at <= row_ids[0:1, :]), 0.0, NEG_LARGE)

            def head(h, sums):
                dk, dv = sums
                q_h, do_h = q[h], do_acc[h]
                probs = jnp.exp(inner_cols(keys, q_h) + bias - lse[pl.ds(h, 1), :])
                back = inner_cols(values, do_h) - delta_acc[h][:1]
                ds = (probs * back).astype(LOW)
                dv = dv + dot(probs.astype(LOW), do_h)
                dk = dk + dot(ds, q_h)
                dq_acc[h] = dq_acc[h] + inner_rows(ds, keys)
                return dk, dv

            zero = jnp.zeros((chunk, wide), F32)
            dk, dv = lax.fori_loop(0, heads, head, (zero, zero))
            out[i * chunk : (i + 1) * chunk, :wide] = dk.astype(out.dtype)
            out[i * chunk : (i + 1) * chunk, wide:] = dv.astype(out.dtype)
    for h in range(heads):
        dq = unrotate(dq_acc[h] * scale, cos[...], sin[...])
        dqp[:, h * wide : (h + 1) * wide] = dq.astype(LOW)
    low = dqp[...]
    send[...] = inner_cols(low[half_rows:], q_up[...]).astype(LOW)
    keep[...] = inner_cols(low[:half_rows], q_up[...])


def mean_of(values):
    return jnp.mean(values, axis=-1, keepdims=True)


def terms_sum(pairs):
    total = None
    for left, right in pairs:
        term = inner_rows(left, right)
        total = term if total is None else total + term
    return total


def back1_body(quarter, scale, chunk, *refs):
    refs = list(refs)
    take = lambda n: [refs.pop(0) for _ in range(n)]
    hid, (hid_other0, dz_mine, dz_got, dz_far) = take(2), take(4)
    h2_theirs, dg = take(2), take(2)
    dh2_send, dh2_keep, n2, inv2, dz, gain2, out_proj, q_up, key_ids = take(9)
    groups = [take(7) for _ in range(2)]
    grad, dy, gain_sum, dyl_mine, dyl_theirs, dqp, dqn_send, dqn_keep, kv_send, kv_keep = take(10)
    h2_got, h2_far, dg_other = take(2), take(2), take(2)
    hid_other1, got, out, core_got, cross_out, cross_got, dyl, dq_acc, do_acc, delta_acc = take(10)
    wire = Wire(*take(2))
    half, rows = 2 * quarter, 4 * quarter
    wire.greet(4)
    y_hid = wire.send(hid[1], hid_other1, wire.beside)
    core_dh2 = wire.send(dh2_send, core_got, wire.core)
    hid_all = (hid[0], hid[1], hid_other0, hid_other1)

    def term(z):
        pairs = [(dz_mine[m, z], hid_all[m][...]) for m in range(2)]
        for m in range(2):
            pairs.append((dz_got[m, z], hid_all[2 + m][:half, :]))
            pairs.append((dz_far[m, z], hid_all[2 + m][half:, :]))
        return terms_sum(pairs)

    def keep(total):
        grad[...] = jnp.transpose(total)

    chain = LineSum(wire, term, (got, out), grad.shape[1], grad.shape[0], keep)
    chain.clear()

    core_dh2.wait_recv()
    cross_out[...] = (
        dh2_keep[:, quarter:, :] + core_got[:, quarter:, :].astype(F32)
    ).astype(LOW)
    cross_dh2 = wire.send(cross_out, cross_got, wire.cross)

    y_hid.wait_recv()
    y_next = [wire.send(h2_theirs[m], h2_got[m], wire.beside) for m in range(2)]
    y_next += [wire.send(dg[m], dg_other[m], wire.beside) for m in range(2)]
    chain.step1()

    cross_dh2.wait_recv()
    dh2 = (
        dh2_keep[:, :quarter, :] + core_got[:, :quarter, :].astype(F32) + cross_got[...].astype(F32)
    )
    gain_sum[...] = jnp.sum(jnp.sum(dh2 * n2[...], axis=0), axis=0, keepdims=True)
    back = dh2 * gain2[...]
    grad_y = dz[:, :quarter, :].astype(F32) + inv2[...] * (
        back - n2[...] * mean_of(back * n2[...])
    )
    dy[...] = grad_y
    dyl[:, :quarter, :] = grad_y.astype(LOW)
    cross_dyl = wire.send(dyl.at[:, :quarter, :], dyl.at[:, quarter:half, :], wire.cross)
    chain.step2()
    cross_dyl.wait_recv()
    core_dyl = wire.send(dyl.at[:, :half, :], dyl.at[:, half:, :], wire.core)
    core_dyl.wait_recv()

    for m in range(2):
        side_columns(dyl.at[m], dyl_mine.at[m], dyl_theirs.at[m], wire.side)
        q, kv, o, lse, row_ids, cos, sin = groups[m]
        attend_back_one(
            scale, chunk, dyl.at[m], out_proj, q_up, key_ids, q, kv, o, lse, row_ids, cos, sin,
            dqp.at[m], dqn_send.at[m], dqn_keep.at[m], kv_send.at[m], kv_keep.at[m],
            dq_acc, do_acc, delta_acc,
        )
        if m == 0:
            chain.step3()
            core_h2 = []
            for i in range(2):
                y_next[i].wait_recv()
                core_h2.append(wire.send(h2_got[i], h2_far[i], wire.core))
    chain.finish()
    for made in y_next[2:] + core_h2:
        made.wait_recv()
    for made in [y_hid, core_dh2, cross_dh2, cross_dyl, core_dyl, *y_next, *core_h2]:
        made.wait_send()
    chain.settle()


class Share:
    def __init__(self, wire, out, quarter):
        spot = lambda block: out.at[:, pl.ds(pl.multiple_of(block * quarter, quarter), quarter), :]
        own, near = spot(wire.blocks[0]), spot(wire.blocks[1])
        self.own = own
        self.first = wire.copy(own, own, wire.cross)
        self.rest = wire.copy(own, own, wire.core), wire.copy(near, near, wire.core)

    def begin(self, value):
        self.own[...] = value
        self.first.start()
        self.rest[0].start()

    def forward(self):
        self.first.wait_recv()
        self.rest[1].start()

    def end(self):
        for made in self.rest:
            made.wait_recv()
        for made in (self.first, *self.rest):
            made.wait_send()


class RowSum:
    def __init__(self, wire, send, kept, got, cross_out, cross_got, quarter):
        self.kept, self.got, self.quarter = kept, got, quarter
        self.out, self.back = cross_out, cross_got
        self.core = wire.copy(send, got, wire.core)
        self.cross = wire.copy(cross_out, cross_got, wire.cross)

    def pass_on(self):
        self.core.wait_recv()
        rest = slice(self.quarter, None)
        self.out[...] = (self.kept[:, rest, :] + self.got[:, rest, :].astype(F32)).astype(LOW)
        self.cross.start()

    def result(self):
        self.cross.wait_recv()
        own = slice(0, self.quarter)
        return (
            self.kept[:, own, :] + self.got[:, own, :].astype(F32) + self.back[...].astype(F32)
        )

    def end(self):
        self.core.wait_send()
        self.cross.wait_send()


def halves_terms(mine, got, far, rights, half):
    pairs = [(mine[m], rights[m][...]) for m in range(2)]
    for m in range(2):
        pairs.append((got[m], rights[2 + m][:half, :]))
        pairs.append((far[m], rights[2 + m][half:, :]))
    return pairs


def back2_body(quarter, *refs):
    refs = list(refs)
    take = lambda n: [refs.pop(0) for _ in range(n)]
    dg, dg_other, du, h2_mine, h2_got, h2_far = (take(2) for _ in range(6))
    kv_send, kv_keep, dqn_send, dqn_keep, chat, inv_c, gain_c, cos, sin = take(9)
    qn_theirs = take(2)
    dqp, dyl_theirs, ffn_send, ffn_keep, y = take(5)
    grad_gate, grad_up, dfirst, gain_sum, qup_side, dyl_got, dyl_far, layer_out = take(8)
    du_other = take(2)
    got_a, out_a, got_b, out_b = take(4)
    dqn_got, dqn_out, dqn_back = take(3)
    kv_got, kv_out, kv_back, side_out, side_got, line_out, line_got, kv_own = take(8)
    both, side_sums = take(2)
    ffn_got, ffn_out, ffn_back = take(3)
    wire = Wire(*take(2))
    half, rows = 2 * quarter, 4 * quarter
    wide = kv_own.shape[2] // 2
    place = wire.place
    wire.greet(4, 3)

    y_du = [wire.send(du[m], du_other[m], wire.beside) for m in range(2)]
    dqn_sum = RowSum(wire, dqn_send, dqn_keep, dqn_got, dqn_out, dqn_back, quarter)
    dqn_sum.core.start()
    core_kv = wire.send(kv_send, kv_got, wire.core)
    ffn_sum = RowSum(wire, ffn_send, ffn_keep, ffn_got, ffn_out, ffn_back, quarter)
    ffn_sum.core.start()

    def gate_term(z):
        return terms_sum(halves_terms(
            [a.at[z][...] for a in h2_mine], [a.at[z][...] for a in h2_got],
            [a.at[z][...] for a in h2_far], (*dg, *dg_other), half))

    def up_term(z):
        return terms_sum(halves_terms(
            [a.at[z][...] for a in h2_mine], [a.at[z][...] for a in h2_got],
            [a.at[z][...] for a in h2_far], (*du, *du_other), half))

    def keep_gate(total):
        grad_gate[...] = total

    def keep_up(total):
        grad_up[...] = total

    gate = LineSum(wire, gate_term, (got_a, out_a), *grad_gate.shape, keep_gate)
    up = LineSum(wire, up_term, (got_b, out_b), *grad_up.shape, keep_up)
    gate.clear()
    up.clear()
    line_kv = []
    for d in range(1, 4):
        line_kv.append(wire.copy(line_out.at[d - 1], line_got.at[d - 1],
                                 {"seq": wire.seq - 2 * d}))

        @pl.when(place > 3 - d)
        def _(d=d):
            line_got[d - 1] = jnp.zeros(line_got.shape[1:], LOW)

    gate.step1()
    dqn_sum.pass_on()
    core_kv.wait_recv()
    kv_out[...] = (kv_keep[:, :, 1] + kv_got[:, :, 1].astype(F32)).astype(LOW)
    cross_kv = wire.send(kv_out, kv_back, wire.cross)
    for z in range(4):
        side_sums[z] = terms_sum([(qn_theirs[m][z], dqp[m]) for m in range(2)]).astype(LOW)
    dqn = dqn_sum.result()
    gain_sum[...] = jnp.sum(jnp.sum(dqn * chat[...], axis=0), axis=0, keepdims=True)
    back = dqn * gain_c[...]
    rank = chat.shape[2]
    both[:, :quarter, :rank] = (
        inv_c[...] * (back - chat[...] * mean_of(back * chat[...]))
    ).astype(LOW)
    gate.step2()

    cross_kv.wait_recv()
    for part in range(2):
        span = slice(4 * part, 4 * part + 4)
        total = kv_keep[:, span, 0] + kv_got[:, span, 0].astype(F32) + kv_back[:, span].astype(F32)
        if part:
            side_out[...] = total.astype(LOW)
    for made in y_du:
        made.wait_recv()
    side_kv = wire.send(side_out, side_got, wire.beside)
    y_rest = [wire.send(side_sums, qup_side, wire.beside)]
    up.step1()
    gate.step3()
    ffn_sum.pass_on()
    side_kv.wait_recv()
    y_rest.append(wire.send(dyl_theirs, dyl_got, wire.beside))
    own = kv_keep[:, :4, 0] + kv_got[:, :4, 0].astype(F32) + kv_back[:, :4].astype(F32)
    own = own + side_got[...].astype(F32)
    kv_own[...] = own[:, 0]
    for d in range(1, 4):
        line_out[d - 1] = own[:, d].astype(LOW)
        pl.when(place >= d)(line_kv[d - 1].start)
    up.step2()
    gate.finish()
    share = Share(wire, layer_out, quarter)
    share.begin((y[...] + ffn_sum.result()).astype(LOW))
    for d in range(1, 4):
        pl.when(place <= 3 - d)(line_kv[d - 1].wait_recv)
    total = kv_own[...]
    for d in range(1, 4):
        total = total + line_got[d - 1].astype(F32)
    both[:, :quarter, rank : rank + wide] = unrotate(
        total[:, :, :wide], cos[...], sin[...]
    ).astype(LOW)
    both[:, :quarter, rank + wide :] = total[:, :, wide:].astype(LOW)
    cross_both = wire.send(both.at[:, :quarter, :], both.at[:, quarter:half, :], wire.cross)
    share.forward()
    cross_both.wait_recv()
    core_both = wire.send(both.at[:, :half, :], both.at[:, half:, :], wire.core)
    up.step3()
    core_both.wait_recv()
    part = rank // 4
    kv_part = wide // 2
    dfirst[:, :, :part] = both[:, :, pl.ds(pl.multiple_of(wire.mp * part, part), part)]
    dfirst[:, :, part:] = both[
        :, :, pl.ds(pl.multiple_of(rank + wire.mp * kv_part, kv_part), kv_part)
    ]
    y_rest[1].wait_recv()
    core_dyl = wire.send(dyl_got, dyl_far, wire.core)
    up.finish()
    share.end()
    core_dyl.wait_recv()
    y_rest[0].wait_recv()
    for made in [*y_du, core_kv, cross_kv, side_kv, cross_both, core_both, *y_rest, core_dyl]:
        made.wait_send()
    for d in range(1, 4):
        pl.when(place >= d)(line_kv[d - 1].wait_send)
    dqn_sum.end()
    ffn_sum.end()
    gate.settle()
    up.settle()


def back3_body(quarter, *refs):
    refs = list(refs)
    take = lambda n: [refs.pop(0) for _ in range(n)]
    dfirst, weights = take(2)
    h1_mine, h1_theirs, o, oo = (take(2) for _ in range(4))
    dyl_mine, dyl_got, dyl_far = take(3)
    qn_mine = take(2)
    dqp, qup_side, n1, inv1, dy, gain1, gain2_sum, gain_c_sum = take(8)
    grad_out, grad_qup, grad_qdown, grad_kv, grad_tokens, gains = take(6)
    got_a, out_a, got_b, out_b, got_c, out_c = take(6)
    side_sums, side_got = take(2)
    send, kept, row_got, row_out, row_back = take(5)
    kv_out, kv_got = take(2)
    sums, sums_core, sums_cross, sums_side, sums_line = take(5)
    wire = Wire(*take(2))
    half, rows = 2 * quarter, 4 * quarter
    place = wire.place
    wire.greet(4, 3, diagonal=True)

    for z in range(4):
        side_sums[z] = terms_sum([(h1_theirs[m][z], dfirst[m]) for m in range(2)]).astype(LOW)
    side_first = wire.send(side_sums, side_got, wire.beside)

    def out_term(z):
        return terms_sum(halves_terms(
            [dyl_mine[m, z] for m in range(2)], [dyl_got[m, z] for m in range(2)],
            [dyl_far[m, z] for m in range(2)], (*o, *oo), half))

    def qup_term(z):
        return terms_sum([(qn_mine[m][z], dqp[m]) for m in range(2)]) + qup_side[z].astype(F32)

    def first_term(z):
        return terms_sum([(h1_mine[m][z], dfirst[m]) for m in range(2)]) + side_got[z].astype(F32)

    def keep_out(total):
        grad_out[...] = jnp.transpose(total)

    def keep_qup(total):
        grad_qup[...] = total

    part = grad_qdown.shape[1]

    def keep_first(total):
        grad_qdown[...] = total[:, :part]
        kv_out[...] = total[:, part:]

    out = LineSum(wire, out_term, (got_a, out_a), *grad_out.shape[::-1], keep_out)
    qup = LineSum(wire, qup_term, (got_b, out_b), *grad_qup.shape, keep_qup)
    first = LineSum(wire, first_term, (got_c, out_c), kv_out.shape[0], dfirst.shape[2], keep_first)
    for chain in (out, qup, first):
        chain.clear()
    row_sum = RowSum(wire, send, kept, row_got, row_out, row_back, quarter)
    out.step1()
    for m in range(2):
        send[m] = inner_cols(dfirst[m, half:, :], weights[...]).astype(LOW)
    row_sum.core.start()
    for m in range(2):
        kept[m] = inner_cols(dfirst[m, :half, :], weights[...])
    row_sum.pass_on()
    qup.step1()
    out.step2()
    qup.step2()
    dh1 = row_sum.result()
    gain1_sum = jnp.sum(jnp.sum(dh1 * n1[...], axis=0), axis=0, keepdims=True)
    back = dh1 * gain1[...]
    share = Share(wire, grad_tokens, quarter)
    share.begin(
        (dy[...] + inv1[...] * (back - n1[...] * mean_of(back * n1[...]))).astype(LOW)
    )
    w, r = gain1_sum.shape[1] // 8, gain_c_sum.shape[1] // 8
    for s in range(8):
        sums[s] = jnp.concatenate(
            [gain1_sum[:, s * w : (s + 1) * w], gain2_sum[:, s * w : (s + 1) * w],
             gain_c_sum[:, s * r : (s + 1) * r]], axis=1
        )
    core_sums = wire.send(sums, sums_core, wire.core)
    side_first.wait_recv()
    first.step1()
    out.step3()
    core_sums.wait_recv()
    core_sums.wait_send()
    sums[...] = sums[...] + sums_core[...]
    cross_sums = wire.send(sums, sums_cross, wire.cross)
    qup.step3()
    share.forward()
    first.step2()
    cross_sums.wait_recv()
    cross_sums.wait_send()
    sums[...] = sums[...] + sums_cross[...]
    side_of = lambda p, s: sums.at[2 * p + s]
    side_sends = [
        wire.send(side_of(p, 1 - wire.side), sums_side.at[p], wire.beside) for p in range(4)
    ]
    out.finish()
    first.step3()
    for made in side_sends:
        made.wait_recv()
        made.wait_send()
    line_sends = []
    for d in range(1, 4):
        for way, there in ((1, place + d <= 3), (-1, place - d >= 0)):
            index = 2 * (d - 1) + (way < 0)
            line_sends.append(
                (wire.copy(sums_line.at[6 + index], sums_line.at[index],
                           {"seq": wire.seq + 2 * way * d}), d, way, there)
            )

            @pl.when(there)
            def _(index=index, d=d, way=way):
                to = place + way * d
                sums_line[6 + index] = sums[2 * to + wire.side] + sums_side[to]
                line_sends[-1][0].start()

            @pl.when((place - way * d < 0) | (place - way * d > 3))
            def _(index=index):
                sums_line[index] = jnp.zeros(sums_line.shape[1:], F32)

    qup.finish()
    first.finish()
    cores = []
    size = kv_out.shape[0] // 4
    for k in range(4):
        rows_of = pl.ds(pl.multiple_of(wire.blocks[k] * size, size), size)
        if k:
            device = {"mp": wire.blocks[k]}
            cores.append(wire.send(kv_out.at[rows_of], kv_got.at[k], device))
        else:
            kv_got[0] = kv_out[rows_of]
    total = sums[2 * place + wire.side] + sums_side[place]
    for made, d, way, there in line_sends:
        pl.when((place - way * d >= 0) & (place - way * d <= 3))(made.wait_recv)
    for index in range(6):
        total = total + sums_line[index]
    gains[...] = total
    for made in cores:
        made.wait_recv()
    columns = kv_out.shape[1]
    for k in range(4):
        at = pl.ds(pl.multiple_of(wire.blocks[k] * columns, columns), columns)
        grad_kv[:, at] = kv_got[k]
    share.end()
    for made in (side_first, *cores):
        made.wait_send()
    for made, d, way, there in line_sends:
        pl.when(there)(made.wait_send)
    row_sum.end()
    for chain in (out, qup, first):
        chain.settle()


def attend_one(
    scale, mp_blocks, c, gain, q_up, cos, sin, kv, key_ids, row_ids, row_starts, out_proj,
    qn, q, o, lse, send, keep, chat_out, inverse_out,
):
    rows = qn.shape[0]
    half, quarter = rows // 2, rows // 4
    part = c.shape[2]
    wide = q.shape[2]
    cut = lambda k, i: c[k, i * quarter : (i + 1) * quarter, :]
    pieces = [jnp.concatenate([cut(k, i ^ k) for i in range(4)], 0) for k in range(4)]
    latent = jnp.concatenate(pieces, 1).astype(F32)
    inverse = inverse_rms(latent)
    chat = latent * inverse
    inverse_out[...] = inverse[:quarter]
    for k in range(4):
        columns = pl.ds(pl.multiple_of(mp_blocks[k] * part, part), part)
        chat_out[:, columns] = chat[:quarter, k * part : (k + 1) * part]
        qn[:, columns] = (chat[:, k * part : (k + 1) * part] * gain[:, columns]).astype(LOW)
    bias = jnp.where((key_ids >= row_starts[...]) & (key_ids <= row_ids[...]), 0.0, NEG_LARGE)
    low = qn[...]
    for h in range(q.shape[0]):
        pre = dot(low, q_up[:, h * wide : (h + 1) * wide])
        q_h = (rotate(pre, cos[...], sin[...]) * scale).astype(LOW)
        q[h] = q_h
        scores = inner_cols(q_h, kv[:, :wide]) + bias
        top = jnp.max(scores, axis=-1, keepdims=True)
        probs = jnp.exp(scores - top)
        total = jnp.sum(probs, axis=-1, keepdims=True)
        out = dot(probs.astype(LOW), kv[:, wide:]) / total
        o[:, h * wide : (h + 1) * wide] = out.astype(LOW)
        log_total = jnp.broadcast_to(top + jnp.log(total), (rows, 128))
        lse[h : h + 1, :] = jnp.transpose(log_total)[:1]
    keep[...] = dot(o[:half, :], out_proj[...])
    send[...] = dot(o[half:, :], out_proj[...]).astype(LOW)


def fore1_body(scale, *refs):
    refs = list(refs)
    take = lambda n: [refs.pop(0) for _ in range(n)]
    tokens, cotangent, q_down, kv_proj, q_up, out_proj, w_down = take(7)
    gain1, gain_c, gain2, key_ids, row_ids = take(5)
    groups = [take(3) for _ in range(2)]
    h1_mine, h1_theirs, qn_mine, qn_theirs = (take(2) for _ in range(4))
    qs, os, lses, kvs, oo, dz_got = (take(2) for _ in range(6))
    dz, dz_mine, dhid, chat, inv_c, y_out, n2_out, inv2_out, n1_out, inv1_out, h2 = take(11)
    x, down_w, kv_w, up_w, out_w, back_w, h1, c, qn, dz_theirs = take(10)
    send, kept, got, cross_out, cross_got = take(5)
    loads = take(1)[0]
    wire = Wire(*take(2))
    place, blocks = wire.place, wire.blocks
    rows = x.shape[1]
    half, quarter = rows // 2, rows // 4
    wide = kv_proj.shape[1] // 2

    started = []

    def load(source, target):
        made = pltpu.make_async_copy(source, target, loads.at[len(started)])
        made.start()
        started.append(made)
        return made

    def load_rows(source, target):
        return [
            load(source.at[pl.ds(pl.multiple_of(blocks[k] * quarter, quarter), quarter), :],
                 target.at[k * quarter : (k + 1) * quarter, :])
            for k in range(4)
        ]

    in_x = [load_rows(tokens.at[0], x.at[0])]
    in_kv = load(kv_proj, kv_w)
    in_x.append(load_rows(tokens.at[1], x.at[1]))
    in_down = load(q_down, down_w)
    in_dz = [load_rows(cotangent.at[m], dz.at[m]) for m in range(2)]
    in_back, in_up, in_out = load(w_down, back_w), load(q_up, up_w), load(out_proj, out_w)

    line_kv, side_kv, core_kv, cross_c, core_c = [], [], [], [], []
    for m in range(2):
        for d in range(1, 4):

            @pl.when(place < d)
            def _(m=m, d=d):
                kvs[m][0, :, d] = jnp.zeros(kvs[m].shape[1:2] + kvs[m].shape[3:], LOW)
                kvs[m][1, :, d] = jnp.zeros(kvs[m].shape[1:2] + kvs[m].shape[3:], LOW)

        own = kvs[m].at[0, 0, 0]
        line_kv.append([
            wire.copy(own, kvs[m].at[0, 0, d], {"seq": wire.seq + 2 * d}) for d in range(1, 4)
        ])
        side_kv.append([
            wire.copy(kvs[m].at[0, 0, d], kvs[m].at[0, 1, d], wire.beside) for d in range(4)
        ])
        core_kv.append([
            wire.copy(kvs[m].at[0, :, d], kvs[m].at[1, :, d], wire.core) for d in range(4)
        ])
        cross_c.append(wire.copy(c.at[m, 0], c.at[m, 1], wire.cross))
        core_c.append([
            wire.copy(c.at[m, 0], c.at[m, 2], wire.core),
            wire.copy(c.at[m, 1], c.at[m, 3], wire.core),
        ])
    wire.greet(4, 3)

    for m in range(2):
        cos, sin, _ = groups[m]
        for made in in_x[m]:
            made.wait()
        if m == 0:
            in_kv.wait()
        values = x[m].astype(F32)
        inverse = inverse_rms(values)
        normed = values * inverse
        n1_out[m], inv1_out[m] = normed[:quarter], inverse[:quarter]
        low = (normed * gain1[...]).astype(LOW)
        h1[...] = low
        pair = dot(low[:half], kv_w[...])
        own = kvs[m].at[0, 0, 0]
        own[:, :wide] = rotate(pair[:, :wide], cos[:half], sin[:half]).astype(LOW)
        own[:, wide:] = pair[:, wide:].astype(LOW)
        for d in (3, 2, 1):
            pl.when(place + d <= 3)(line_kv[m][d - 1].start)
        side_kv[m][0].start()
        if m == 0:
            in_down.wait()
        c[m, 0] = dot(low, down_w[...]).astype(LOW)
        cross_c[m].start()
        core_c[m][0].start()
        side_columns(h1, h1_mine[m], h1_theirs[m], wire.side)

    def pass_kv(m, d):
        @pl.when(place >= d)
        def _():
            line_kv[m][d - 1].wait_recv()
            side_kv[m][d].start()

    def pass_core(m, d):
        @pl.when(place >= d)
        def _():
            side_kv[m][d].wait_recv()
            core_kv[m][d].start()

    in_back.wait()
    for m in range(2):
        for made in in_dz[m]:
            made.wait()
    dhid[0] = inner_cols(dz[0], back_w[...])
    for d in (1, 2, 3):
        pass_kv(0, d)
    pass_core(0, 0)
    for m in range(2):
        cross_c[m].wait_recv()
        core_c[m][1].start()
    dhid[1] = inner_cols(dz[1], back_w[...])
    for d in (1, 2, 3):
        pass_kv(1, d)
    for m in range(2):
        side_columns(dz.at[m], dz_mine.at[m], dz_theirs.at[m], wire.side)
    for d in (1, 2, 3):
        pass_core(0, d)
    in_up.wait()
    in_out.wait()
    sums = [
        RowSum(wire, send.at[m : m + 1], kept.at[m : m + 1], got.at[m : m + 1],
               cross_out.at[m : m + 1], cross_got.at[m : m + 1], quarter)
        for m in range(2)
    ]
    side_o, shares = [], []

    def after_sum(m):
        value = x[m, :quarter, :].astype(F32) + sums[m].result()[0]
        inverse = inverse_rms(value)
        normed = value * inverse
        y_out[m], n2_out[m], inv2_out[m] = value, normed, inverse
        h2[m, :quarter, :] = (normed * gain2[...]).astype(LOW)
        spot = lambda k: h2.at[m, k * quarter : (k + 1) * quarter, :]
        shares.append((
            wire.send(spot(0), spot(1), wire.cross), wire.send(spot(0), spot(2), wire.core),
            wire.copy(spot(1), spot(3), wire.core),
        ))

    for m in range(2):
        if m == 1:
            for d in range(4):
                pass_core(1, d)
        for d in range(4):
            pl.when(place >= d)(core_kv[m][d].wait_recv)
        for made in core_c[m]:
            made.wait_recv()
        cos, sin, row_starts = groups[m]
        attend_one(
            scale, blocks, c.at[m], gain_c, up_w, cos, sin,
            kvs[m][...].reshape(2 * 2 * 4 * half, 2 * wide), key_ids[...], row_ids[...],
            row_starts, out_w, qn, qs[m], os[m], lses[m], send.at[m], kept.at[m],
            chat.at[m], inv_c.at[m],
        )
        sums[m].core.start()
        if m == 0:
            side_dz = wire.send(dz_theirs, dz_got[0], wire.beside)
        side_o.append(wire.send(os[m], oo[m], wire.beside))
        side_columns(qn, qn_mine[m], qn_theirs[m], wire.side)
        if m == 1:
            after_sum(0)
        sums[m].pass_on()
    after_sum(1)
    side_dz.wait_recv()
    core_dz = wire.send(dz_got[0], dz_got[1], wire.core)
    for near, _, far in shares:
        near.wait_recv()
        far.start()
    for _, first, far in shares:
        first.wait_recv()
        far.wait_recv()
    core_dz.wait_recv()
    for made in side_o:
        made.wait_recv()
    for made in [side_dz, core_dz, *side_o, *cross_c, *(a for p in core_c for a in p),
                 *(a for p in shares for a in p)]:
        made.wait_send()
    for m in range(2):
        sums[m].end()
        for d in range(4):

            @pl.when(place >= d)
            def _(m=m, d=d):
                side_kv[m][d].wait_send()
                core_kv[m][d].wait_send()

        for d in range(1, 4):
            pl.when(place + d <= 3)(line_kv[m][d - 1].wait_send)


def local(
    tokens,
    lengths,
    norm1_gain,
    q_down,
    latent_gain,
    q_up,
    kv_proj,
    out_proj,
    norm2_gain,
    w_gate,
    w_up,
    w_down,
    cotangent,
):
    micro, rows, width = tokens.shape
    seq = lax.axis_size("seq")
    line = seq // 2
    at = lax.axis_index("seq").astype(jnp.int32)
    me = lax.axis_index("mp").astype(jnp.int32)
    place, side = at // 2, at % 2
    ids = jnp.stack([me, side])
    quarter, half = rows // 4, rows // 2
    head_dim = kv_proj.shape[1] // 2
    heads = q_up.shape[1] // head_dim
    part = q_down.shape[1]
    rank = q_up.shape[0]
    hidden = w_gate.shape[1]
    kv_part = kv_proj.shape[1] // 4
    wide = width // seq
    scale = head_dim ** (-0.5)
    key_count = seq * rows
    beside = [(i, i ^ 1) for i in range(seq)]
    narrow = line == 4 and micro == 2 and key_count <= 2048 and not wide % 128

    def swap(index):
        return ((index & 1) << 1) | (index >> 1)

    def to_natural(array, axis):
        size = array.shape[axis] // 4
        return jnp.concatenate(
            [lax.dynamic_slice_in_dim(array, swap(me ^ b) * size, size, axis) for b in range(4)],
            axis,
        )

    def other(array):
        return lax.ppermute(array, "seq", beside)

    def sum_mp(send, keep):
        kept = keep + lax.ppermute(send, "mp", CORE).astype(F32)
        got = lax.ppermute(kept[..., quarter:, :].astype(LOW), "mp", CROSS)
        return kept[..., :quarter, :] + got.astype(F32)

    def gather_mp(piece):
        near = lax.ppermute(piece, "mp", CROSS)
        pair = jnp.concatenate([piece, near], -2)
        return piece, near, lax.ppermute(pair, "mp", CORE)

    def sides_shape(columns, their_rows, lead=()):
        if columns // seq % 128:
            return []
        return [
            whole((*lead, line, n, columns // seq), LOW) for n in (rows, their_rows)
        ]

    def split_sides(made, full, their_rows):
        if made:
            return made
        split = full.reshape(*full.shape[:-1], line, 2, full.shape[-1] // seq)
        mine, theirs = (
            jnp.moveaxis(lax.dynamic_index_in_dim(split, i, split.ndim - 2, keepdims=False), -2, -3)
            for i in (side, 1 - side)
        )
        return mine, theirs[..., :their_rows, :]

    def from_other(theirs):
        got = other(theirs)
        return got, lax.ppermute(got, "mp", CORE)

    def without_sides(body, count):
        return body if count else lambda *refs: body(*refs, None, None)

    def both_sides(mine, got):
        lefts, spans = [], []
        for array, first, count, partner in (
            (mine, 0, rows, 0), (got[0], 0, half, 1), (got[1], half, half, 1)
        ):
            stacked_array = not isinstance(array, list)
            for m in range(micro):
                spans.append((len(lefts) if not stacked_array else len(lefts), m if stacked_array else None,
                              m, partner, first, count))
                if not stacked_array:
                    lefts.append(array[m])
            if stacked_array:
                lefts.append(array)
        return lefts, spans

    class Chain:
        def __init__(self, lefts, rights, terms, shape, turned=False, from_side=None):
            self.args = [*lefts, *rights]
            self.spec = (terms, len(lefts), len(rights))
            self.shape, self.turned = shape, turned
            self.from_side = [] if from_side is None else [from_side]
            self.step, self.up, self.down = 0, None, None

        def block(self, index, added, after, last=False):
            turned = last and self.turned
            body = functools.partial(
                block_body, *self.spec, len(added), len(self.from_side), turned
            )
            shape = self.shape[::-1] if turned else self.shape
            return run(
                body, index.reshape(1), [*self.args, *added, *self.from_side],
                [whole(shape, F32 if last else LOW)], after, name="block",
            )[0]

        def advance(self, after):
            self.step += 1
            step = self.step
            goes_up = [(i, i + 2) for i in range(2 * step)]
            goes_down = [(seq - 1 - i, seq - 3 - i) for i in range(2 * step)]
            for_up, for_down = line - step + place, step - line + place
            if 2 * step < line + 1:
                which = jnp.where(
                    place <= step - 1, for_up, jnp.where(place >= line - step, for_down, 0)
                )
                term = self.block(which, [a for a in (self.up, self.down) if a is not None], after)
                if step == 1 and line > 3:
                    self.up = lax.ppermute(term, "seq", goes_up + goes_down)
                else:
                    self.up = lax.ppermute(term, "seq", goes_up)
                    self.down = lax.ppermute(term, "seq", goes_down)
                return [term]
            term_up = self.block(jnp.clip(for_up, 0, line - 1), [self.up], after)
            term_down = self.block(jnp.clip(for_down, 0, line - 1), [self.down], [term_up])
            self.up = lax.ppermute(term_up, "seq", goes_up)
            self.down = lax.ppermute(term_down, "seq", goes_down)
            return [term_down]

        def finish(self, after):
            while self.step < line - 1:
                after = self.advance(after)
            result = self.block(place, [self.up, self.down], after, last=True)
            return result, [result]

    quarter_rows = jnp.arange(quarter, dtype=jnp.int32)
    row_ids = at * rows + jnp.concatenate([(me ^ k) * quarter + quarter_rows for k in ORDER])
    key_ids = (
        ((place - jnp.arange(line, dtype=jnp.int32)[None, None, :, None, None]) * 2
         + (side ^ jnp.arange(2, dtype=jnp.int32)[None, :, None, None, None])) * rows
        + (me ^ (jnp.arange(2, dtype=jnp.int32)[:, None, None, None, None]
                 + 2 * jnp.arange(2, dtype=jnp.int32)[None, None, None, :, None])) * quarter
        + quarter_rows[None, None, None, None, :]
    ).reshape(key_count)

    gain1_row, gain2_row, gain_c_row = norm1_gain[None, :], norm2_gain[None, :], latent_gain[None, :]
    kv_cols = lax.dynamic_slice_in_dim(kv_proj, me * kv_part, kv_part, 1)
    first_weights = jnp.concatenate([q_down, kv_cols], axis=1)
    low = lambda *shape: pltpu.VMEM(shape, LOW)
    full = lambda *shape: pltpu.VMEM(shape, F32)
    near = lambda *arrays: [(1, a) for a in arrays]
    far = lambda *arrays: [(0, a) for a in arrays]
    columns = heads * head_dim
    side_rows = rank // seq
    first_columns = part + kv_part

    def narrow_layer():
        tables, starts = [], []
        for m in range(micro):
            _, places = documents(lengths[m], row_ids)
            starts.append(row_ids - places)
            tables.append(rotation(places, head_dim))
        row_shape = whole((micro, quarter, width), F32)
        one_shape = whole((micro, quarter, 1), F32)
        args = far(tokens, cotangent, q_down, kv_proj, q_up, out_proj, w_down)
        args += near(gain1_row, gain_c_row, gain2_row, key_ids[None, :], row_ids[:, None])
        for m in range(micro):
            args += near(*tables[m], starts[m][:, None])
        outs = near(*[whole((line, rows, wide), LOW)] * 4, *[whole((line, rows, side_rows), LOW)] * 4)
        outs += near(*[whole((heads, rows, head_dim), LOW)] * 2, *[whole((rows, columns), LOW)] * 2)
        outs += near(*[whole((heads, rows), F32)] * 2)
        outs += near(*[whole((2, 2, line, half, 2 * head_dim), LOW)] * 2)
        outs += far(*[whole((rows, columns), LOW)] * 2, *[whole((micro, line, half, wide), LOW)] * 2)
        outs += near(
            whole((micro, rows, width), LOW), whole((micro, line, rows, wide), LOW),
            whole((micro, rows, hidden), F32), whole((micro, quarter, rank), F32), one_shape,
            row_shape, row_shape, one_shape, row_shape, one_shape,
            whole((micro, rows, width), LOW),
        )
        made = list(mesh_run(
            functools.partial(fore1_body, scale), args, outs,
            [low(micro, rows, width), low(width, part), low(width, 2 * head_dim),
             low(rank, columns), low(columns, width), low(hidden, width), low(rows, width),
             low(micro, 4, rows, part), low(rows, rank), low(micro, line, half, wide),
             low(micro, half, width), full(micro, half, width), low(micro, half, width),
             low(micro, quarter, width), low(micro, quarter, width),
             pltpu.SemaphoreType.DMA((24,))],
            4, "fore1", 60, 60,
        ))
        give = lambda n: [made.pop(0) for _ in range(n)]
        h1_mine, h1_theirs, qn_mine, qn_theirs = (give(2) for _ in range(4))
        qs, os, lses, kv, o_other, dz_got = (give(2) for _ in range(6))
        kv = [a.reshape(key_count, 2 * head_dim) for a in kv]
        dz, dz_mine, dhid, chat, inv_c, y, n2, inv2, n1, inv1, h2 = give(11)

        h2_mine, h2_theirs, hid, dg, du = [], [], [], [], []
        order = []
        for m in range(micro):
            made = run(
                functools.partial(forward_whole_body, m),
                ids,
                [h2, w_gate, w_up, dhid],
                [whole((rows, hidden), LOW)] * 3
                + [whole((line, rows, wide), LOW), whole((line, half, wide), LOW)],
                order,
                name="forward",
            )
            order = [made[0]]
            for kept, a in zip((hid, dg, du, h2_mine, h2_theirs), made):
                kept.append(a)
        send, keep, ffn_send, ffn_keep = run(
            functools.partial(hidden_back_body, micro),
            ids,
            [*dg, *du, *hid, w_gate, w_up, w_down],
            [whole((micro, half, width), LOW), whole((micro, half, width), F32)] * 2,
            order,
            name="hidden_back",
            limit=56,
        )

        args = near(*hid, other(hid[0]), dz_mine, *dz_got) + far(*h2_theirs, *dg)
        args += near(send, keep, n2, inv2, dz, gain2_row, out_proj, q_up, key_ids[:, None])
        for m in range(micro):
            args += near(qs[m], kv[m], os[m], lses[m], jnp.stack([row_ids, starts[m]], 0),
                         *tables[m])
        outs = near(
            whole((hidden, wide), F32), row_shape,
            whole((1, width), F32), whole((micro, line, rows, wide), LOW),
            whole((micro, line, half, wide), LOW), whole((micro, rows, columns), LOW),
            whole((micro, half, rank), LOW), whole((micro, half, rank), F32),
            whole((micro, key_count // 2, 2 * head_dim), LOW),
            whole((micro, key_count // 2, 2 * head_dim), F32),
        ) + far(*[whole((line, half, wide), LOW)] * 4, *[whole((rows, hidden), LOW)] * 2)
        (grad_down, dy, gain2, dyl_mine, dyl_theirs, dqp, send, keep, kv_send, kv_keep,
         *exchanged) = mesh_run(
            functools.partial(back1_body, quarter, scale, 1024), args, outs,
            [low(rows, hidden), low(5, wide, hidden), low(3, wide, hidden),
             low(micro, half, width), low(micro, quarter, width), low(micro, quarter, width),
             low(micro, rows, width), full(heads, rows, head_dim), low(heads, rows, head_dim),
             full(heads, 8, rows)],
            1, "back1", 60, 24,
        )

        kv_shape = (micro, 2 * line, 2, quarter, 2 * head_dim)
        args = near(*dg, *exchanged[4:6], *du, *h2_mine, *exchanged[0:4])
        args += far(kv_send.reshape(kv_shape)) + near(kv_keep.reshape(kv_shape)) + far(send)
        args += near(keep, chat, inv_c, gain_c_row,
                     jnp.stack([t[0][:quarter] for t in tables], 0),
                     jnp.stack([t[1][:quarter] for t in tables], 0), *qn_theirs, dqp)
        args += far(dyl_theirs, ffn_send) + near(ffn_keep, y)
        outs = near(whole((wide, hidden), F32), whole((wide, hidden), F32),
                    whole((micro, rows, first_columns), LOW), whole((1, rank), F32))
        outs += far(whole((line, side_rows, columns), LOW),
                    *[whole((micro, line, half, wide), LOW)] * 2)
        outs += near(whole((micro, rows, width), LOW))
        kv_low = lambda *lead: low(*lead, quarter, 2 * head_dim)
        grad_gate, grad_up, dfirst, gain_c, qup_side, dyl_got, dyl_far, layer_out = mesh_run(
            functools.partial(back2_body, quarter), args, outs,
            [low(rows, hidden), low(rows, hidden), low(5, wide, hidden), low(3, wide, hidden),
             low(5, wide, hidden), low(3, wide, hidden), low(micro, half, rank),
             low(micro, quarter, rank), low(micro, quarter, rank), kv_low(micro, 2 * line, 2),
             kv_low(micro, 2 * line), kv_low(micro, 2 * line), kv_low(micro, line),
             kv_low(micro, line), kv_low(3, micro), kv_low(3, micro),
             full(micro, quarter, 2 * head_dim), low(micro, rows, rank + 2 * head_dim),
             low(line, side_rows, columns), low(micro, half, width), low(micro, quarter, width),
             low(micro, quarter, width)],
            2, "back2", 60, 40,
        )

        kv_cols = lax.dynamic_slice_in_dim(kv_proj, me * kv_part, kv_part, 1)
        first_weights = jnp.concatenate([q_down, kv_cols], axis=1)
        args = near(dfirst, first_weights, *h1_mine, *h1_theirs, *os, *o_other, dyl_mine, dyl_got,
                    dyl_far, *qn_mine, dqp, qup_side, n1, inv1, dy, gain1_row, gain2, gain_c)
        block = width // 4 // seq
        gain_columns = 2 * wide + side_rows
        outs = near(whole((columns, wide), F32), whole((side_rows, columns), F32),
                    whole((wide, part), F32), whole((block, 2 * head_dim), F32),
                    whole((micro, rows, width), LOW), whole((1, gain_columns), F32))
        grad_out, grad_qup, grad_qdown, grad_kv, input_grads, gains = mesh_run(
            functools.partial(back3_body, quarter), args, outs,
            [low(5, wide, columns), low(3, wide, columns), low(5, side_rows, columns),
             low(3, side_rows, columns), low(5, wide, first_columns),
             low(3, wide, first_columns), low(line, wide, first_columns),
             low(line, wide, first_columns), low(micro, half, width), full(micro, half, width),
             low(micro, half, width), low(micro, quarter, width), low(micro, quarter, width),
             full(wide, kv_part), full(4, block, kv_part), full(seq, 1, gain_columns),
             full(seq, 1, gain_columns), full(seq, 1, gain_columns), full(line, 1, gain_columns),
             full(12, 1, gain_columns)],
            3, "back3", 60, 44,
        )
        return (
            layer_out, input_grads, gains[0, :wide], grad_qdown, gains[0, 2 * wide :], grad_qup,
            grad_kv, grad_out, gains[0, wide : 2 * wide], grad_gate, grad_up, grad_down,
        )

    if narrow:
        return narrow_layer()

    both_rows = sides_shape(width, rows)
    half_rows = sides_shape(width, half)
    rank_sides = sides_shape(rank, rows)

    tables, starts, kv, c_part, h1_sides = [], [], [], [], []
    order = []
    for m in range(micro):
        _, places = documents(lengths[m], row_ids)
        starts.append(row_ids - places)
        tables.append(rotation(places, head_dim))
        c, packed, h1, *made = run(
            without_sides(functools.partial(first_body, m, quarter), len(both_rows)),
            ids,
            [tokens, gain1_row, q_down, kv_proj, *tables[m]],
            [whole((rows, part), LOW), whole((half, 2 * head_dim), LOW), whole((rows, width), LOW),
             *both_rows],
            order,
            name="first",
        )
        order = [c]
        blocks = [packed] + [
            lax.ppermute(packed, "seq", [(i, i + 2 * d) for i in range(seq - 2 * d)])
            for d in range(1, line)
        ]
        near = jnp.stack(blocks, 0)
        near = jnp.stack([near, other(near)], 0)
        kv.append(
            jnp.stack([near, lax.ppermute(near, "mp", CORE)], 0).reshape(key_count, 2 * head_dim)
        )
        c_part.append(c)
        h1_sides.append(split_sides(made, h1, rows))

    dhid, dz, *made = run(
        functools.partial(cotangent_body, micro, quarter),
        ids,
        [cotangent, w_down],
        [whole((micro, rows, hidden), F32), whole((micro, rows, width), LOW),
         *sides_shape(width, half, (micro,))],
        order,
        name="cotangent",
    )
    order = [dz]
    dz_mine, dz_theirs = split_sides(made, dz, half)
    dz_got = from_other(dz_theirs)

    qn_sides, qs, os, lses, sums, c_rows = [], [], [], [], [], []
    for m in range(micro):
        near = lax.ppermute(c_part[m], "mp", CROSS)
        swapped = jnp.concatenate(
            [near[quarter : 2 * quarter], near[:quarter], near[3 * quarter :],
             near[2 * quarter : 3 * quarter]], 0
        )
        far = lax.ppermute(jnp.concatenate([c_part[m], swapped], 1), "mp", CORE)
        qn, q, o, lse, send, keep, *made = run(
            without_sides(functools.partial(attend_body, scale), len(rank_sides)),
            ids,
            [c_part[m], near, far, gain_c_row, q_up, *tables[m], kv[m], key_ids[None, :],
             row_ids[:, None], starts[m][:, None], out_proj],
            [whole((rows, rank), LOW), whole((heads, rows, head_dim), LOW),
             whole((rows, heads * head_dim), LOW), whole((heads, rows), F32),
             whole((half, width), LOW), whole((half, width), F32), *rank_sides],
            order,
            name="attend",
        )
        order = [o]
        qn_sides.append(split_sides(made, qn, rows))
        qs.append(q)
        os.append(o)
        lses.append(lse)
        sums.append(sum_mp(send, keep))
        c_rows.append(
            jnp.concatenate([c_part[m][:quarter], swapped[:quarter], far[half : half + quarter]], 1)
        )

    h2_mine, h2_theirs, hid, dg, du, state = [], [], [], [], [], []
    for m in range(micro):
        x = lax.dynamic_slice_in_dim(tokens[m], me * quarter, quarter, 0).astype(F32)
        inv1 = inverse_rms(x)
        y = x + sums[m]
        inv2 = inverse_rms(y)
        n2 = y * inv2
        pieces = gather_mp((n2 * gain2_row).astype(LOW))
        h2, hid_m, dg_m, du_m, *made = run(
            without_sides(functools.partial(forward_body, m), len(half_rows)),
            ids,
            [*pieces, w_gate, w_up, dhid],
            [whole((rows, width), LOW), *[whole((rows, hidden), LOW)] * 3, *half_rows],
            order,
            name="forward",
        )
        order = [hid_m]
        mine, theirs = split_sides(made, h2, half)
        h2_mine.append(mine)
        h2_theirs.append(theirs)
        hid.append(hid_m)
        dg.append(dg_m)
        du.append(du_m)
        state.append(dict(x=x, n1=x * inv1, inv1=inv1, y=y, n2=n2, inv2=inv2, c=c_rows[m]))

    def stacked(name):
        return jnp.stack([st[name] for st in state], 0)

    def with_other(arrays):
        return [*arrays, *[other(a) for a in arrays]]

    def terms_of(spans):
        return [(a, lead, m + micro * partner, None, first, count)
                for a, lead, m, partner, first, count in spans]

    send, keep, ffn_send, ffn_keep = run(
        functools.partial(hidden_back_body, micro),
        ids,
        [*dg, *du, *hid, w_gate, w_up, w_down],
        [whole((micro, half, width), LOW), whole((micro, half, width), F32)] * 2,
        order,
        name="hidden_back",
    )
    lefts, spans = both_sides(dz_mine, dz_got)
    chain_down = Chain(lefts, with_other(hid), terms_of(spans), (wide, hidden), turned=True)
    lefts, spans = both_sides(h2_mine, [list(p) for p in zip(*[from_other(t) for t in h2_theirs])])
    chain_gate = Chain(lefts, with_other(dg), terms_of(spans), (wide, hidden))
    chain_up = Chain(lefts, with_other(du), terms_of(spans), (wide, hidden))

    order = chain_down.advance([send])
    dh2 = sum_mp(send, keep)
    y, n2, inv2, n1, inv1 = (stacked(k) for k in ("y", "n2", "inv2", "n1", "inv1"))
    dz_own = dz[:, :quarter].astype(F32)
    gain2 = jnp.sum(dh2 * n2, axis=(0, 1))
    dy = dz_own + norm_backward(dh2 * gain2_row, n2, inv2)
    for _ in range(2):
        order = chain_down.advance(order)
    order = chain_gate.advance(order)

    def attend_back(which, pieces):
        args = [*pieces, out_proj, q_up, key_ids[:, None]]
        for m in which:
            args += [qs[m], kv[m], os[m], lses[m], jnp.stack([row_ids, starts[m]], 0), *tables[m]]
        n = len(which)
        return run(
            functools.partial(attend_back_body, scale, n, min(1024, key_count // 2)),
            ids,
            args,
            [whole((n, rows, width), LOW), whole((n, rows, heads * head_dim), LOW),
             whole((n, half, rank), LOW), whole((n, half, rank), F32),
             whole((n, key_count // 2, 2 * head_dim), LOW),
             whole((n, key_count // 2, 2 * head_dim), F32), *sides_shape(width, half, (n,))],
            order,
            scratch=[pltpu.VMEM((heads, rows, head_dim), F32),
                     pltpu.VMEM((heads, rows, head_dim), LOW),
                     pltpu.VMEM((heads, 8, rows), F32)],
            name="attend_back",
            limit=56,
        )

    pieces = gather_mp(dy.astype(LOW))
    if key_count <= 2048:
        made = attend_back(range(micro), pieces)
    else:
        each = [attend_back([m], [p[m : m + 1] for p in pieces]) for m in range(micro)]
        made = [jnp.concatenate(parts, 0) for parts in zip(*each)]
    dyl, dqp, send, keep, kv_send, kv_keep, *made = made
    order = [send]
    dyl_mine, dyl_theirs = split_sides(made, dyl, half)
    lefts, spans = both_sides(dyl_mine, from_other(dyl_theirs))
    chain_out = Chain(lefts, with_other(os), terms_of(spans), (wide, heads * head_dim), turned=True)

    def side_sum(lefts, rights, shape, after):
        terms = [(m, None, 0, m, 0, rows) for m in range(micro)]
        (made,) = run(
            functools.partial(side_sum_body, terms, len(lefts)),
            ids,
            [*lefts, *rights],
            [whole((line, *shape), LOW)],
            after,
            name="side_sum",
        )
        return other(made), [made]

    def own_chain(side_pairs, right, shape, after):
        from_side, after = side_sum([p[1] for p in side_pairs], [right], shape, after)
        terms = [(m, None, 0, m, 0, rows) for m in range(micro)]
        return Chain([p[0] for p in side_pairs], [right], terms, shape, from_side=from_side), after

    shape = (rank // seq, heads * head_dim)
    chain_qup, order = own_chain(qn_sides, dqp, shape, order)
    order = chain_gate.advance(order)
    order = chain_up.advance(order)

    dqn = sum_mp(send, keep)
    c = stacked("c").astype(F32)
    inv_c = inverse_rms(c)
    chat = c * inv_c
    chat = to_natural(chat, 2)
    gain_c = jnp.sum(dqn * chat, axis=(0, 1))
    dc = norm_backward(dqn * gain_c_row, chat, inv_c).astype(LOW)

    dkv = kv_keep + lax.ppermute(kv_send, "mp", CORE).astype(F32)
    dkv = dkv.reshape(micro, 2, line, 2, quarter, 2 * head_dim)
    dkv = dkv[:, :, :, 0] + lax.ppermute(dkv[:, :, :, 1].astype(LOW), "mp", CROSS).astype(F32)
    dkv = dkv[:, 0] + other(dkv[:, 1].astype(LOW)).astype(F32)
    total = dkv[:, 0]
    for d in range(1, line):
        total = total + lax.ppermute(
            dkv[:, d].astype(LOW), "seq", [(i + 2 * d, i) for i in range(seq - 2 * d)]
        ).astype(F32)
    cosine = jnp.stack([t[0][:quarter] for t in tables], 0)
    sine = jnp.stack([t[1][:quarter] for t in tables], 0)
    dkv_low = jnp.concatenate(
        [unrotate(total[..., :head_dim], cosine, sine), total[..., head_dim:]], axis=-1
    ).astype(LOW)
    both = jnp.concatenate(gather_mp(jnp.concatenate([dc, dkv_low], -1)), -2)
    dfirst = jnp.concatenate(
        [lax.dynamic_slice_in_dim(both, me * part, part, 2),
         lax.dynamic_slice_in_dim(both, rank + me * kv_part, kv_part, 2)], -1
    )

    grad_down, order = chain_down.finish(order)
    order = chain_gate.advance(order)
    order = chain_up.advance(order)
    order = chain_out.advance(order)
    grad_gate, order = chain_gate.finish(order)
    order = chain_up.advance(order)
    order = chain_out.advance(order)
    grad_up, order = chain_up.finish(order)
    order = chain_qup.advance(order)
    order = chain_out.advance(order)
    chain_first, order = own_chain(h1_sides, dfirst, (wide, part + kv_part), order)
    order = chain_qup.advance(order)
    grad_out, order = chain_out.finish(order)
    order = chain_first.advance(order)
    order = chain_qup.advance(order)
    order = chain_first.advance(order)
    grad_qup, order = chain_qup.finish(order)
    order = chain_first.advance(order)
    grad_first, order = chain_first.finish(order)

    grad_qdown = grad_first[:, :part]
    kv_cols_grad = grad_first[:, part:]
    pieces = []
    for k in ORDER:
        size = kv_cols_grad.shape[0] // 4
        sent = lax.dynamic_slice_in_dim(kv_cols_grad, (me ^ k) * size, size, 0)
        pieces.append(lax.ppermute(sent, "mp", [(i, i ^ k) for i in range(4)]) if k else sent)
    grad_kv = to_natural(jnp.concatenate(pieces, 1), 1)

    def put_natural(pieces):
        return run(
            functools.partial(natural_body, micro, quarter),
            ids,
            pieces,
            [whole((micro, rows, width), LOW)],
            name="natural",
        )[0]

    part_sum = inner_cols(dfirst.reshape(micro * rows, -1), first_weights).reshape(micro, rows, width)
    dh1 = sum_mp(part_sum[:, half:].astype(LOW), part_sum[:, :half])
    gain1 = jnp.sum(dh1 * n1, axis=(0, 1))
    dx = (dy + norm_backward(dh1 * gain1_row, n1, inv1)).astype(LOW)
    input_grads = put_natural(gather_mp(dx))

    ffn = sum_mp(ffn_send, ffn_keep)
    layer_out = put_natural(gather_mp((y + ffn).astype(LOW)))

    gains = jnp.concatenate(
        [gain1.reshape(seq, -1), gain2.reshape(seq, -1), gain_c.reshape(seq, -1)], axis=1
    )
    gains = gains + lax.ppermute(gains, "mp", CORE)
    gains = gains + lax.ppermute(gains, "mp", CROSS)
    gain_sum = lax.dynamic_index_in_dim(gains, at, 0, keepdims=False)
    for k in range(1, seq):
        gain_sum = gain_sum + lax.ppermute(
            lax.dynamic_index_in_dim(gains, at ^ k, 0, keepdims=False),
            "seq",
            [(i, i ^ k) for i in range(seq)],
        )
    return (
        layer_out,
        input_grads,
        gain_sum[:wide],
        grad_qdown,
        gain_sum[2 * wide :],
        grad_qup,
        grad_kv,
        grad_out,
        gain_sum[wide : 2 * wide],
        grad_gate,
        grad_up,
        grad_down,
    )


def solution(mesh):
    placed = (
        P(None, "seq", None),
        P(),
        P(),
        P(None, "mp"),
        P(),
        P(None, "mp"),
        P(),
        P("mp", None),
        P(),
        P(None, "mp"),
        P(None, "mp"),
        P("mp", None),
        P(None, "seq", None),
    )
    return jax.shard_map(
        local,
        mesh=mesh,
        in_specs=placed,
        out_specs=(
            P(None, "seq", None),
            P(None, "seq", None),
            P("seq"),
            P("seq", "mp"),
            P("seq"),
            P("seq", "mp"),
            P(("seq", "mp"), None),
            P("mp", "seq"),
            P("seq"),
            P("seq", "mp"),
            P("seq", "mp"),
            P("mp", "seq"),
        ),
        check_vma=False,
    )
```

```python
import functools

import jax
import jax.numpy as jnp
from jax import lax
from jax.experimental import pallas as pl
from jax.experimental.pallas import tpu as pltpu
from jax.sharding import PartitionSpec as P

EPS = 1e-06
BASE = 10000.0
NEG_LARGE = -1e30
LOW = jnp.bfloat16
F32 = jnp.float32
ORDER = (0, 2, 1, 3)
CORE = [(i, i ^ 1) for i in range(4)]
CROSS = [(i, i ^ 2) for i in range(4)]


def inverse_rms(values):
    return lax.rsqrt(jnp.mean(values * values, axis=-1, keepdims=True) + EPS)


def norm_backward(grad_hat, normed, inverse):
    return inverse * (grad_hat - normed * jnp.mean(grad_hat * normed, axis=-1, keepdims=True))


def dot(left, right):
    return jnp.dot(left, right, preferred_element_type=F32)


def inner_rows(left, right):
    return lax.dot_general(left, right, (((0,), (0,)), ((), ())), preferred_element_type=F32)


def inner_cols(left, right):
    return lax.dot_general(left, right, (((1,), (1,)), ((), ())), preferred_element_type=F32)


def documents(lengths_row, rows):
    first_end = lengths_row[0]
    second_end = first_end + lengths_row[1]
    doc_ids = (rows >= first_end).astype(jnp.int32) + (rows >= second_end).astype(jnp.int32)
    starts = jnp.where(rows >= second_end, second_end, jnp.where(rows >= first_end, first_end, 0))
    return (doc_ids, rows - starts)


def rotation(positions, head_dim):
    half = head_dim // 2
    freqs = BASE ** (-2.0 * jnp.arange(half, dtype=F32) / head_dim)
    angles = positions.astype(F32)[:, None] * freqs[None, :]
    return (jnp.cos(angles), jnp.sin(angles))


def rotate(values, cosine, sine):
    half = values.shape[-1] // 2
    first = values[..., :half]
    second = values[..., half:]
    return jnp.concatenate(
        [first * cosine - second * sine, second * cosine + first * sine], axis=-1
    )


def unrotate(grads, cosine, sine):
    return rotate(grads, cosine, -sine)


def in_vmem():
    return pl.BlockSpec(memory_space=pltpu.VMEM)


def whole(shape, dtype):
    return jax.ShapeDtypeStruct(shape, dtype)


def run(body, ids, args, outs, after=(), scratch=(), name=None, limit=40):
    args, after = list(args), list(after)

    def without(*refs):
        body(*refs[: 1 + len(args)], *refs[1 + len(args) + len(after) :])

    return pl.pallas_call(
        without,
        grid_spec=pltpu.PrefetchScalarGridSpec(
            num_scalar_prefetch=1,
            grid=(1,),
            in_specs=[in_vmem()] * len(args) + [pl.BlockSpec(memory_space=pl.ANY)] * len(after),
            out_specs=[in_vmem()] * len(outs),
            scratch_shapes=list(scratch),
        ),
        out_shape=list(outs),
        cost_estimate=pl.CostEstimate(flops=1000, bytes_accessed=1000, transcendentals=0),
        compiler_params=pltpu.CompilerParams(vmem_limit_bytes=limit << 20),
        name=name,
    )(ids, *args, *after)


def side_columns(source, mine, theirs, side):
    line, _, wide = mine.shape
    rows = theirs.shape[1]
    for z in range(line):
        mine[z] = source[:, pl.ds(pl.multiple_of((2 * z + side) * wide, wide), wide)]
        theirs[z] = source[:rows, pl.ds(pl.multiple_of((2 * z + 1 - side) * wide, wide), wide)]


def first_body(m, quarter, ids, x_ref, gain, q_down, kv_proj, cos, sin, c, kv, h1, mine, theirs):
    blocks = [
        x_ref[m, pl.ds(pl.multiple_of((ids[0] ^ k) * quarter, quarter), quarter), :] for k in ORDER
    ]
    x = jnp.concatenate(blocks, 0).astype(F32)
    low = (x * inverse_rms(x) * gain[...]).astype(LOW)
    h1[...] = low
    half = 2 * quarter
    pair = dot(low[:half], kv_proj[...])
    wide = kv_proj.shape[1] // 2
    kv[:, :wide] = rotate(pair[:, :wide], cos[:half], sin[:half]).astype(LOW)
    kv[:, wide:] = pair[:, wide:].astype(LOW)
    c[...] = dot(low, q_down[...]).astype(LOW)
    if mine is not None:
        side_columns(h1, mine, theirs, ids[1])


def cotangent_body(micro, quarter, ids, z_ref, w_down, dhid, dz, *sides):
    for m in range(micro):
        blocks = [
            z_ref[m, pl.ds(pl.multiple_of((ids[0] ^ k) * quarter, quarter), quarter), :]
            for k in ORDER
        ]
        dz[m] = jnp.concatenate(blocks, 0)
        if sides:
            side_columns(dz.at[m], sides[0].at[m], sides[1].at[m], ids[1])
        dhid[m] = inner_cols(dz[m], w_down[...])


def attend_body(
    scale, ids, c0, c1, c2, gain, q_up, cos, sin, kv, key_ids, row_ids, row_starts, out_proj,
    qn, q, o, lse, send, keep, mine, theirs,
):
    rows = qn.shape[0]
    quarter = rows // 4
    part = c0.shape[1]
    wide = q.shape[2]
    got = c1[...]
    pair = jnp.concatenate(
        [got[quarter : 2 * quarter], got[:quarter], got[3 * quarter :], got[2 * quarter : 3 * quarter]],
        0,
    )
    far = jnp.concatenate([c2[2 * quarter :], c2[: 2 * quarter]], 0)
    c = jnp.concatenate([c0[...], pair, far], 1).astype(F32)
    chat = c * inverse_rms(c)
    for k, xor in enumerate(ORDER):
        columns = pl.ds(pl.multiple_of((ids[0] ^ xor) * part, part), part)
        qn[:, columns] = (chat[:, k * part : (k + 1) * part] * gain[:, columns]).astype(LOW)
    if mine is not None:
        side_columns(qn, mine, theirs, ids[1])
    bias = jnp.where(
        (key_ids[...] >= row_starts[...]) & (key_ids[...] <= row_ids[...]), 0.0, NEG_LARGE
    )
    low = qn[...]
    keys, values = kv[:, :wide], kv[:, wide:]
    for h in range(q.shape[0]):
        pre = dot(low, q_up[:, h * wide : (h + 1) * wide])
        q_h = (rotate(pre, cos[...], sin[...]) * scale).astype(LOW)
        q[h] = q_h
        scores = inner_cols(q_h, keys) + bias
        top = jnp.max(scores, axis=-1, keepdims=True)
        probs = jnp.exp(scores - top)
        total = jnp.sum(probs, axis=-1, keepdims=True)
        out = dot(probs.astype(LOW), values) / total
        o[:, h * wide : (h + 1) * wide] = out.astype(LOW)
        log_total = jnp.broadcast_to(top + jnp.log(total), (rows, 128))
        lse[h : h + 1, :] = jnp.transpose(log_total)[:1]
    half = 2 * quarter
    send[...] = dot(o[half:, :], out_proj[...]).astype(LOW)
    keep[...] = dot(o[:half, :], out_proj[...])


def forward_body(m, ids, a0, a1, a2, w_gate, w_up, dhid, h2, hid, dg, du, mine, theirs):
    h2[...] = jnp.concatenate([a0[...], a1[...], a2[...]], 0)
    if mine is not None:
        side_columns(h2, mine, theirs, ids[1])
    low = h2[...]
    g = dot(low, w_gate[...])
    u = dot(low, w_up[...])
    sig = jax.nn.sigmoid(g)
    swish = g * sig
    hid[...] = (swish * u).astype(LOW)
    back = dhid[m]
    dg[...] = (back * u * sig * (1.0 + g * (1.0 - sig))).astype(LOW)
    du[...] = (back * swish).astype(LOW)


def hidden_back_body(micro, ids, *refs):
    dgs, dus = refs[:micro], refs[micro : 2 * micro]
    hids = refs[2 * micro : 3 * micro]
    w_gate, w_up, w_down, send, keep, out_send, out_keep = refs[3 * micro :]
    half = send.shape[1]
    every = lambda parts: jnp.concatenate([part[...] for part in parts], 0)
    rows = 2 * half
    total = inner_cols(every(dgs), w_gate[...]) + inner_cols(every(dus), w_up[...])
    for m in range(micro):
        send[m] = total[m * rows + half : (m + 1) * rows].astype(LOW)
        keep[m] = total[m * rows : m * rows + half]
    total = dot(every(hids), w_down[...])
    for m in range(micro):
        out_send[m] = total[m * rows + half : (m + 1) * rows].astype(LOW)
        out_keep[m] = total[m * rows : m * rows + half]


def pick(ref, lead):
    return ref if lead is None else ref.at[lead]


def block_body(terms, lefts, rights, extra, from_side, turned, ids, *refs):
    left, refs = refs[:lefts], refs[lefts:]
    right, refs = refs[:rights], refs[rights:]
    added, out = refs[: extra + from_side], refs[-1]
    total = None
    for a, a_lead, b, b_lead, first, count in terms:
        rows = pick(right[b], b_lead)[first : first + count, :]
        term = inner_rows(pick(left[a], a_lead)[ids[0]], rows)
        total = term if total is None else total + term
    for i, ref in enumerate(added):
        total = total + (ref[ids[0]] if i >= extra else ref[...]).astype(F32)
    out[...] = jnp.transpose(total) if turned else total.astype(out.dtype)


def side_sum_body(terms, lefts, ids, *refs):
    left, right, out = refs[:lefts], refs[lefts:-1], refs[-1]
    for z in range(out.shape[0]):
        total = None
        for a, a_lead, b, b_lead, first, count in terms:
            rows = pick(right[b], b_lead)[first : first + count, :]
            term = inner_rows(pick(left[a], a_lead)[z], rows)
            total = term if total is None else total + term
        out[z] = total.astype(out.dtype)


def attend_back_body(
    scale, micro, chunk, ids, a0, a1, a2, out_proj, q_up, key_ids, *refs
):
    per = 7
    groups = [refs[m * per : (m + 1) * per] for m in range(micro)]
    dyl_out, dqp, send, keep, kv_send, kv_keep = refs[micro * per : micro * per + 6]
    dq_acc, do_acc, delta_acc = refs[-3:]
    sides = refs[micro * per + 6 : -3]
    for m in range(micro):
        q, kv, o, lse, row_ids, cos, sin = groups[m]
        heads, rows, wide = q.shape
        half_rows = rows // 2
        dyl = jnp.concatenate([a0[m], a1[m], a2[m]], 0)
        dyl_out[m] = dyl
        if sides:
            side_columns(dyl_out.at[m], sides[0].at[m], sides[1].at[m], ids[1])
        for h in range(heads):
            do = inner_cols(dyl, out_proj[h * wide : (h + 1) * wide, :]).astype(LOW)
            do_acc[h] = do
            delta = jnp.sum(
                do.astype(F32) * o[:, h * wide : (h + 1) * wide].astype(F32), axis=-1, keepdims=True
            )
            delta_acc[h] = jnp.transpose(jnp.broadcast_to(delta, (rows, 128)))[:8]
            dq_acc[h] = jnp.zeros((rows, wide), F32)
        count = kv.shape[0] // 2 // chunk
        for part, out in ((0, kv_keep), (1, kv_send)):

            def one(i, carry):
                base = pl.multiple_of((part * count + i) * chunk, chunk)
                keys = kv[pl.ds(base, chunk), :wide]
                values = kv[pl.ds(base, chunk), wide:]
                at = key_ids[pl.ds(base, chunk), :]
                bias = jnp.where((at >= row_ids[1:2, :]) & (at <= row_ids[0:1, :]), 0.0, NEG_LARGE)

                def head(h, sums):
                    dk, dv = sums
                    q_h, do_h = q[h], do_acc[h]
                    probs = jnp.exp(inner_cols(keys, q_h) + bias - lse[pl.ds(h, 1), :])
                    back = inner_cols(values, do_h) - delta_acc[h][:1]
                    ds = (probs * back).astype(LOW)
                    dv = dv + dot(probs.astype(LOW), do_h)
                    dk = dk + dot(ds, q_h)
                    dq_acc[h] = dq_acc[h] + inner_rows(ds, keys)
                    return dk, dv

                zero = jnp.zeros((chunk, wide), F32)
                dk, dv = lax.fori_loop(0, heads, head, (zero, zero))
                place = pl.ds(pl.multiple_of(i * chunk, chunk), chunk)
                out[m, place, :wide] = dk.astype(out.dtype)
                out[m, place, wide:] = dv.astype(out.dtype)
                return carry

            if count == 1:
                one(0, 0)
            else:
                lax.fori_loop(0, count, one, 0)
        for h in range(heads):
            dq = unrotate(dq_acc[h] * scale, cos[...], sin[...])
            dqp[m, :, h * wide : (h + 1) * wide] = dq.astype(LOW)
        low = dqp[m]
        send[m] = inner_cols(low[half_rows:], q_up[...]).astype(LOW)
        keep[m] = inner_cols(low[:half_rows], q_up[...])


def natural_body(micro, quarter, ids, a0, a1, a2, out):
    for m in range(micro):
        pieces = (a0[m], a1[m], a2[m, :quarter, :], a2[m, quarter:, :])
        for k, piece in zip(ORDER, pieces):
            out[m, pl.ds(pl.multiple_of((ids[0] ^ k) * quarter, quarter), quarter), :] = piece


class Wire:
    def __init__(self, sends, recvs):
        self.sends, self.recvs, self.used = sends, recvs, 0
        self.seq, self.mp = lax.axis_index("seq"), lax.axis_index("mp")
        self.place, self.side = self.seq // 2, self.seq % 2
        core, cross = self.mp % 2, self.mp // 2
        self.blocks = (
            self.mp, 2 * (1 - cross) + core, 2 * cross + 1 - core, 2 * (1 - cross) + 1 - core
        )
        self.core, self.cross = {"mp": self.blocks[2]}, {"mp": self.blocks[1]}
        self.beside = {"seq": self.seq + 1 - 2 * self.side}
        self.up, self.down = {"seq": self.seq + 2}, {"seq": self.seq - 2}

    def copy(self, source, target, device):
        at = self.used
        self.used += 1
        return pltpu.make_async_remote_copy(
            src_ref=source, dst_ref=target, send_sem=self.sends.at[at], recv_sem=self.recvs.at[at],
            device_id=device, device_id_type=pl.DeviceIdType.MESH,
        )

    def send(self, source, target, device):
        made = self.copy(source, target, device)
        made.start()
        return made

    def greet(self, line, far=1, diagonal=False):
        barrier = pltpu.get_barrier_semaphore()
        devices = [self.core, self.cross, self.beside]
        if diagonal:
            devices.append({"mp": self.blocks[3]})
        for device in devices:
            pl.semaphore_signal(barrier, 1, device_id=device, device_id_type=pl.DeviceIdType.MESH)
        for d in range(1, far + 1):
            for way, there in ((1, self.place < line - d), (-1, self.place >= d)):

                @pl.when(there)
                def _():
                    pl.semaphore_signal(
                        barrier, 1, device_id={"seq": self.seq + 2 * way * d},
                        device_id_type=pl.DeviceIdType.MESH,
                    )
        below, above = jnp.minimum(self.place, far), jnp.minimum(line - 1 - self.place, far)
        pl.semaphore_wait(barrier, len(devices) + below + above)


def along(pieces, axis):
    return pieces[0] if len(pieces) == 1 else jnp.concatenate(pieces, axis)


def pair_places(first, second, quarter, axis):
    shape = (2 * quarter, 1) if axis == 0 else (1, 2 * quarter)
    index = lax.broadcasted_iota(jnp.int32, shape, axis)
    return jnp.where(index < quarter, first * quarter + index, (second - 1) * quarter + index)


def row_places(wire, quarter, axis):
    b = wire.blocks
    pieces = [pair_places(b[i], b[i + 1], quarter, axis) for i in (0, 2)]
    return wire.seq * (4 * quarter) + along(pieces, axis)


def key_places(wire, quarter, line, axis, cores):
    pieces = []
    for core in cores:
        for side in (wire.side, 1 - wire.side):
            for d in range(line):
                base = ((wire.place - d) * 2 + side) * (4 * quarter)
                b = wire.blocks[2 * core : 2 * core + 2]
                pieces.append(base + pair_places(b[0], b[1], quarter, axis))
    return along(pieces, axis)


def sequence_starts(lengths, m, places):
    first_end = lengths[m, 0]
    second_end = first_end + lengths[m, 1]
    return jnp.where(
        places >= second_end, second_end, jnp.where(places >= first_end, first_end, 0)
    )


class LineSum:
    def __init__(self, wire, term, room, rows, columns, keep):
        got, out = room
        view = lambda ref, i: ref.at[i, :rows, :columns]
        self.place, self.term, self.keep = wire.place, term, keep
        self.got = [view(got, i) for i in range(5)]
        self.out = [view(out, i) for i in range(2)]
        one, two_up, two_down, three_up, three_down = self.got
        a, b = self.out
        self.one = wire.copy(a, one, wire.up), wire.copy(a, one, wire.down)
        self.two = wire.copy(b, two_up, wire.up), wire.copy(b, two_down, wire.down)
        self.three = wire.copy(a, three_up, wire.up), wire.copy(b, three_down, wire.down)

    def clear(self):
        place = self.place
        for ref, empty in zip(
            self.got, ((place == 0) | (place == 3),) * 3 + (place == 0, place == 3)
        ):

            @pl.when(empty)
            def _(ref=ref):
                ref[...] = jnp.zeros(ref.shape, ref.dtype)

    def step1(self):
        place = self.place

        @pl.when((place == 0) | (place == 3))
        def _():
            self.out[0][...] = self.term(3 - place).astype(LOW)

        pl.when(place == 0)(self.one[0].start)
        pl.when(place == 3)(self.one[1].start)

    def step2(self):
        place = self.place
        pl.when(place == 1)(self.one[0].wait_recv)
        pl.when(place == 2)(self.one[1].wait_recv)
        self.out[1][...] = (
            self.term((place + 2) % 4) + self.got[0][...].astype(F32)
        ).astype(LOW)
        pl.when(place <= 1)(self.two[0].start)
        pl.when(place >= 2)(self.two[1].start)

    def step3(self):
        place = self.place

        @pl.when((place == 1) | (place == 2))
        def _():
            self.two[0].wait_recv()
            self.two[1].wait_recv()

        pl.when(place == 0)(self.one[0].wait_send)
        pl.when(place == 3)(self.one[1].wait_send)

        @pl.when(place <= 2)
        def _():
            self.out[0][...] = (self.term(place + 1) + self.got[1][...].astype(F32)).astype(LOW)
            self.three[0].start()

        pl.when(place <= 1)(self.two[0].wait_send)
        pl.when(place >= 2)(self.two[1].wait_send)

        @pl.when(place >= 1)
        def _():
            self.out[1][...] = (self.term(place - 1) + self.got[2][...].astype(F32)).astype(LOW)
            self.three[1].start()

    def finish(self):
        place = self.place
        pl.when(place >= 1)(self.three[0].wait_recv)
        pl.when(place <= 2)(self.three[1].wait_recv)
        self.keep(
            self.term(place) + self.got[3][...].astype(F32) + self.got[4][...].astype(F32)
        )

    def settle(self):
        place = self.place
        pl.when(place <= 2)(self.three[0].wait_send)
        pl.when(place >= 1)(self.three[1].wait_send)


SPACES = (pl.ANY, pltpu.VMEM, pltpu.SMEM)


def mesh_run(body, args, outs, scratch, number, name, limit, sends):
    return pl.pallas_call(
        body,
        in_specs=[pl.BlockSpec(memory_space=SPACES[kind]) for kind, _ in args],
        out_specs=[pl.BlockSpec(memory_space=SPACES[kind]) for kind, _ in outs],
        out_shape=[shape for _, shape in outs],
        scratch_shapes=[
            *scratch, pltpu.SemaphoreType.DMA((sends,)), pltpu.SemaphoreType.DMA((sends,))
        ],
        cost_estimate=pl.CostEstimate(flops=1000, bytes_accessed=1000, transcendentals=0),
        compiler_params=pltpu.CompilerParams(
            collective_id=number, has_side_effects=True, vmem_limit_bytes=limit << 20
        ),
        name=name,
    )(*[array for _, array in args])


def attend_back_one(
    scale, keys_at, rows_at, starts, dyl, out_proj, q_up, q, kv, o, lse, cos, sin,
    dqp, send, keep, kv_send, kv_keep, dq_acc, do_acc, delta_acc,
):
    heads, rows, wide = q.shape
    half_rows = rows // 2
    low = dyl[...]
    for h in range(heads):
        do = inner_cols(low, out_proj[h * wide : (h + 1) * wide, :]).astype(LOW)
        do_acc[h] = do
        delta = jnp.sum(
            do.astype(F32) * o[:, h * wide : (h + 1) * wide].astype(F32), axis=-1, keepdims=True
        )
        delta_acc[h] = jnp.transpose(jnp.broadcast_to(delta, (rows, 128)))[:8]
        dq_acc[h] = jnp.zeros((rows, wide), F32)
    chunk = kv.shape[0] // 4
    for part, out in ((2, kv_send), (3, kv_send), (0, kv_keep), (1, kv_keep)):
        keys = kv[part * chunk : (part + 1) * chunk, :wide]
        values = kv[part * chunk : (part + 1) * chunk, wide:]
        at = keys_at[part // 2][part % 2 * chunk : (part % 2 + 1) * chunk]
        bias = jnp.where((at >= starts) & (at <= rows_at), 0.0, NEG_LARGE)

        def head(h, sums):
            dk, dv = sums
            q_h, do_h = q[h], do_acc[h]
            probs = jnp.exp(inner_cols(keys, q_h) + bias - lse[pl.ds(h, 1), :])
            back = inner_cols(values, do_h) - delta_acc[h][:1]
            ds = (probs * back).astype(LOW)
            dv = dv + dot(probs.astype(LOW), do_h)
            dk = dk + dot(ds, q_h)
            dq_acc[h] = dq_acc[h] + inner_rows(ds, keys)
            return dk, dv

        zero = jnp.zeros((chunk, wide), F32)
        dk, dv = lax.fori_loop(0, heads, head, (zero, zero))
        spot = slice(part % 2 * chunk, (part % 2 + 1) * chunk)
        out[spot, :wide] = dk.astype(out.dtype)
        out[spot, wide:] = dv.astype(out.dtype)
    for h in range(heads):
        dq = unrotate(dq_acc[h] * scale, cos[...], sin[...])
        dqp[:, h * wide : (h + 1) * wide] = dq.astype(LOW)
    low = dqp[...]
    send[...] = inner_cols(low[half_rows:], q_up[...]).astype(LOW)
    keep[...] = inner_cols(low[:half_rows], q_up[...])


def mean_of(values):
    return jnp.mean(values, axis=-1, keepdims=True)


def terms_sum(pairs):
    total = None
    for left, right in pairs:
        term = inner_rows(left, right)
        total = term if total is None else total + term
    return total


def back1_body(quarter, *refs):
    refs = list(refs)
    take = lambda n: [refs.pop(0) for _ in range(n)]
    w_gate, w_up, h2, dhid, n2, inv2, dz, gain2, dz_mine, dz_got, dz_far = take(11)
    grad, dy, gain_sum, dyl, dyl_mine, dyl_theirs = take(6)
    hid, dg, du, h2_mine = (take(2) for _ in range(4))
    h2_got, h2_far, dg_other = take(2), take(2), take(2)
    gate_w, up_w, hid_other0, hid_other1, h2_theirs, got, out = take(7)
    send, kept, core_got, cross_out, cross_got, loads = take(6)
    wire = Wire(*take(2))
    half, rows = 2 * quarter, 4 * quarter
    in_gate = pltpu.make_async_copy(w_gate, gate_w, loads.at[0])
    in_up = pltpu.make_async_copy(w_up, up_w, loads.at[1])
    in_gate.start()
    in_up.start()
    hid_other = (hid_other0, hid_other1)
    hid_all = (*hid, *hid_other)

    def term(z):
        return terms_sum(halves_terms(
            [dz_mine[m, z] for m in range(2)], [dz_got[m, z] for m in range(2)],
            [dz_far[m, z] for m in range(2)], hid_all, half))

    def keep(total):
        grad[...] = jnp.transpose(total)

    chain = LineSum(wire, term, (got, out), grad.shape[1], grad.shape[0], keep)
    chain.clear()
    wire.greet(4)
    y_hid = []
    for m in range(2):
        low = h2[m]
        if m == 0:
            in_gate.wait()
        g = dot(low, gate_w[...])
        if m == 0:
            in_up.wait()
        u = dot(low, up_w[...])
        sig = jax.nn.sigmoid(g)
        swish = g * sig
        hid[m][...] = (swish * u).astype(LOW)
        y_hid.append(wire.send(hid[m], hid_other[m], wire.beside))
        back = dhid[m]
        dg[m][...] = (back * u * sig * (1.0 + g * (1.0 - sig))).astype(LOW)
        du[m][...] = (back * swish).astype(LOW)
    both = lambda pair: jnp.concatenate([pair[0][...], pair[1][...]], 0)
    total = inner_cols(both(dg), gate_w[...]) + inner_cols(both(du), up_w[...])
    for m in range(2):
        send[m] = total[m * rows + half : (m + 1) * rows].astype(LOW)
        kept[m] = total[m * rows : m * rows + half]
    sums = RowSum(wire, send, kept, core_got, cross_out, cross_got, quarter)
    sums.core.start()
    for m in range(2):
        side_columns(h2.at[m], h2_mine[m], h2_theirs.at[m], wire.side)
    sums.pass_on()
    for made in y_hid:
        made.wait_recv()
    y_next = [wire.send(h2_theirs.at[m], h2_got[m], wire.beside) for m in range(2)]
    y_next += [wire.send(dg[m], dg_other[m], wire.beside) for m in range(2)]
    chain.step1()
    dh2 = sums.result()
    gain_sum[...] = jnp.sum(jnp.sum(dh2 * n2[...], axis=0), axis=0, keepdims=True)
    back = dh2 * gain2[...]
    grad_y = dz[:, :quarter, :].astype(F32) + inv2[...] * (
        back - n2[...] * mean_of(back * n2[...])
    )
    dy[...] = grad_y
    dyl[:, :quarter, :] = grad_y.astype(LOW)
    cross_dyl = wire.send(dyl.at[:, :quarter, :], dyl.at[:, quarter:half, :], wire.cross)
    chain.step2()
    cross_dyl.wait_recv()
    core_dyl = wire.send(dyl.at[:, :half, :], dyl.at[:, half:, :], wire.core)
    core_h2 = []
    for i in range(2):
        y_next[i].wait_recv()
        core_h2.append(wire.send(h2_got[i], h2_far[i], wire.core))
    core_dyl.wait_recv()
    for m in range(2):
        side_columns(dyl.at[m], dyl_mine.at[m], dyl_theirs.at[m], wire.side)
    chain.step3()
    for made in y_next[2:] + core_h2:
        made.wait_recv()
    chain.finish()
    for made in [*y_hid, cross_dyl, core_dyl, *y_next, *core_h2]:
        made.wait_send()
    sums.end()
    chain.settle()


class Share:
    def __init__(self, wire, out, quarter):
        spot = lambda block: out.at[:, pl.ds(pl.multiple_of(block * quarter, quarter), quarter), :]
        own, near = spot(wire.blocks[0]), spot(wire.blocks[1])
        self.own = own
        self.first = wire.copy(own, own, wire.cross)
        self.rest = wire.copy(own, own, wire.core), wire.copy(near, near, wire.core)

    def begin(self, value):
        self.own[...] = value
        self.first.start()
        self.rest[0].start()

    def forward(self):
        self.first.wait_recv()
        self.rest[1].start()

    def end(self):
        for made in self.rest:
            made.wait_recv()
        for made in (self.first, *self.rest):
            made.wait_send()


class RowSum:
    def __init__(self, wire, send, kept, got, cross_out, cross_got, quarter):
        self.kept, self.got, self.quarter = kept, got, quarter
        self.out, self.back = cross_out, cross_got
        self.core = wire.copy(send, got, wire.core)
        self.cross = wire.copy(cross_out, cross_got, wire.cross)

    def pass_on(self):
        self.core.wait_recv()
        rest = slice(self.quarter, None)
        self.out[...] = (self.kept[:, rest, :] + self.got[:, rest, :].astype(F32)).astype(LOW)
        self.cross.start()

    def result(self):
        self.cross.wait_recv()
        own = slice(0, self.quarter)
        return (
            self.kept[:, own, :] + self.got[:, own, :].astype(F32) + self.back[...].astype(F32)
        )

    def end(self):
        self.core.wait_send()
        self.cross.wait_send()


def halves_terms(mine, got, far, rights, half):
    pairs = [(mine[m], rights[m][...]) for m in range(2)]
    for m in range(2):
        pairs.append((got[m], rights[2 + m][:half, :]))
        pairs.append((far[m], rights[2 + m][half:, :]))
    return pairs


def back2_body(quarter, scale, *refs):
    refs = list(refs)
    take = lambda n: [refs.pop(0) for _ in range(n)]
    (lengths,) = take(1)
    dg, dg_other, du, h2_mine, h2_got, h2_far = (take(2) for _ in range(6))
    dyl, out_proj, q_up = take(3)
    q, kv, o, lse = (take(2) for _ in range(4))
    cos, sin, chat, inv_c, gain_c, dyl_theirs = take(6)
    grad_gate, grad_up, dfirst, gain_sum, dqp, dyl_got, dyl_far = take(7)
    du_other = take(2)
    got_a, out_a, got_b, out_b = take(4)
    dq_acc, do_acc, delta_acc, dqn_send, dqn_keep, kv_send, kv_keep = take(7)
    dqn_got, dqn_out, dqn_back = take(3)
    kv_got, kv_out, kv_back, side_out, side_got, line_out, line_got, kv_own = take(8)
    (both,) = take(1)
    wire = Wire(*take(2))
    half, rows = 2 * quarter, 4 * quarter
    wide = kv_own.shape[2] // 2
    rank = chat.shape[2]
    place = wire.place

    y_du = [wire.copy(du[m], du_other[m], wire.beside) for m in range(2)]

    def chain(rights, grad, room):
        def term(z):
            return terms_sum(halves_terms(
                [a[z] for a in h2_mine], [a[z] for a in h2_got], [a[z] for a in h2_far], rights,
                half))

        def keep(total):
            grad[...] = total

        made = LineSum(wire, term, room, *grad.shape, keep)
        made.clear()
        return made

    gate = chain((*dg, *dg_other), grad_gate, (got_a, out_a))
    up = chain((*du, *du_other), grad_up, (got_b, out_b))
    dqn_sum, core_kv, cross_kv, side_kv, line_kv = [], [], [], [], []
    for m in range(2):
        one = lambda ref: ref.at[m : m + 1]
        dqn_sum.append(RowSum(wire, one(dqn_send), one(dqn_keep), one(dqn_got), one(dqn_out),
                              one(dqn_back), quarter))
        core_kv.append(wire.copy(kv_send.at[m], kv_got.at[m], wire.core))
        cross_kv.append(wire.copy(kv_out.at[m], kv_back.at[m], wire.cross))
        side_kv.append(wire.copy(side_out.at[m], side_got.at[m], wire.beside))
        line_kv.append([
            wire.copy(line_out.at[m, d - 1], line_got.at[m, d - 1], {"seq": wire.seq - 2 * d})
            for d in range(1, 4)
        ])
        for d in range(1, 4):

            @pl.when(place > 3 - d)
            def _(m=m, d=d):
                line_got[m, d - 1] = jnp.zeros(line_got.shape[2:], LOW)

    wire.greet(4, 3)
    for made in y_du:
        made.start()
    gate.step1()

    def attend(m):
        rows_at = row_places(wire, quarter, 1)
        attend_back_one(
            scale, [key_places(wire, quarter, 4, 0, (core,)) for core in range(2)], rows_at,
            sequence_starts(lengths, m, rows_at), dyl.at[m], out_proj, q_up, q[m], kv[m], o[m],
            lse[m], cos[m], sin[m], dqp.at[m], dqn_send.at[m], dqn_keep.at[m], kv_send.at[m],
            kv_keep.at[m], dq_acc, do_acc, delta_acc,
        )
        core_kv[m].start()
        dqn_sum[m].core.start()

    split = lambda ref, m: ref[m].reshape(8, 2, quarter, 2 * wide)

    def kv_cross(m):
        dqn_sum[m].pass_on()
        core_kv[m].wait_recv()
        kv_out[m] = (
            split(kv_keep, m)[:, 1].astype(F32) + split(kv_got, m)[:, 1].astype(F32)
        ).astype(LOW)
        cross_kv[m].start()

    def kv_sum(m, span):
        return (
            split(kv_keep, m)[span, 0].astype(F32) + split(kv_got, m)[span, 0].astype(F32)
            + kv_back[m, span].astype(F32)
        )

    def kv_side(m):
        cross_kv[m].wait_recv()
        side_out[m] = kv_sum(m, slice(4, 8)).astype(LOW)
        side_kv[m].start()

    def kv_line(m):
        side_kv[m].wait_recv()
        own = kv_sum(m, slice(0, 4)) + side_got[m].astype(F32)
        kv_own[m] = own[0]
        for d in range(1, 4):
            line_out[m, d - 1] = own[d].astype(LOW)
            pl.when(place >= d)(line_kv[m][d - 1].start)

    def latent(m):
        dqn = dqn_sum[m].result()[0]
        gain = jnp.sum(dqn * chat[m], axis=0, keepdims=True)
        gain_sum[...] = gain if m == 0 else gain_sum[...] + gain
        back = dqn * gain_c[...]
        both[m, :quarter, :rank] = (
            inv_c[m] * (back - chat[m] * mean_of(back * chat[m]))
        ).astype(LOW)

    attend(0)
    kv_cross(0)
    gate.step2()
    attend(1)
    kv_cross(1)
    for made in y_du:
        made.wait_recv()
    up.step1()
    kv_side(0)
    gate.step3()
    latent(0)
    latent(1)
    kv_side(1)
    side_dyl = wire.send(dyl_theirs, dyl_got, wire.beside)
    kv_line(0)
    kv_line(1)
    up.step2()
    gate.finish()
    for m in range(2):
        for d in range(1, 4):
            pl.when(place <= 3 - d)(line_kv[m][d - 1].wait_recv)
        total = kv_own[m]
        for d in range(1, 4):
            total = total + line_got[m, d - 1].astype(F32)
        both[m, :quarter, rank : rank + wide] = unrotate(
            total[:, :wide], cos[m, :quarter], sin[m, :quarter]
        ).astype(LOW)
        both[m, :quarter, rank + wide :] = total[:, wide:].astype(LOW)
    cross_both = wire.send(both.at[:, :quarter, :], both.at[:, quarter:half, :], wire.cross)
    up.step3()
    cross_both.wait_recv()
    core_both = wire.send(both.at[:, :half, :], both.at[:, half:, :], wire.core)
    side_dyl.wait_recv()
    core_dyl = wire.send(dyl_got, dyl_far, wire.core)
    core_both.wait_recv()
    part = rank // 4
    kv_part = wide // 2
    dfirst[:, :, :part] = both[:, :, pl.ds(pl.multiple_of(wire.mp * part, part), part)]
    dfirst[:, :, part:] = both[
        :, :, pl.ds(pl.multiple_of(rank + wire.mp * kv_part, kv_part), kv_part)
    ]
    up.finish()
    core_dyl.wait_recv()
    for made in [*y_du, *core_kv, *cross_kv, *side_kv, cross_both, core_both, side_dyl, core_dyl]:
        made.wait_send()
    for m in range(2):
        dqn_sum[m].end()
        for d in range(1, 4):
            pl.when(place >= d)(line_kv[m][d - 1].wait_send)
    gate.settle()
    up.settle()


def back3_body(quarter, *refs):
    refs = list(refs)
    take = lambda n: [refs.pop(0) for _ in range(n)]
    dfirst, weights = take(2)
    h1_mine, h1_theirs, o, oo = (take(2) for _ in range(4))
    dyl_mine, dyl_got, dyl_far = take(3)
    qn_mine, qn_theirs = take(2), take(2)
    dqp, n1, inv1, dy, gain1, gain2_sum, gain_c_sum = take(7)
    hid0, hid1, w_down, y = take(4)
    grad_out, grad_qup, grad_qdown, grad_kv, grad_tokens, gains, layer_out = take(7)
    got_a, out_a, got_b, out_b, got_c, out_c = take(6)
    side_sums, side_got = take(2)
    send, kept, row_got, row_out, row_back = take(5)
    kv_out, kv_got = take(2)
    sums, sums_core, sums_cross, sums_side, sums_line = take(5)
    ffn_send, ffn_keep, ffn_got, ffn_out, ffn_back, qup_sums, qup_side = take(7)
    wire = Wire(*take(2))
    half, rows = 2 * quarter, 4 * quarter
    place = wire.place
    wire.greet(4, 3, diagonal=True)

    for z in range(4):
        qup_sums[z] = terms_sum([(qn_theirs[m][z], dqp[m]) for m in range(2)]).astype(LOW)
    side_qup = wire.send(qup_sums, qup_side, wire.beside)

    def out_term(z):
        return terms_sum(halves_terms(
            [dyl_mine[m, z] for m in range(2)], [dyl_got[m, z] for m in range(2)],
            [dyl_far[m, z] for m in range(2)], (*o, *oo), half))

    def qup_term(z):
        return terms_sum([(qn_mine[m][z], dqp[m]) for m in range(2)]) + qup_side[z].astype(F32)

    def first_term(z):
        return terms_sum([(h1_mine[m][z], dfirst[m]) for m in range(2)]) + side_got[z].astype(F32)

    def keep_out(total):
        grad_out[...] = jnp.transpose(total)

    def keep_qup(total):
        grad_qup[...] = total

    part = grad_qdown.shape[1]

    def keep_first(total):
        grad_qdown[...] = total[:, :part]
        kv_out[...] = total[:, part:]

    out = LineSum(wire, out_term, (got_a, out_a), *grad_out.shape[::-1], keep_out)
    qup = LineSum(wire, qup_term, (got_b, out_b), *grad_qup.shape, keep_qup)
    first = LineSum(wire, first_term, (got_c, out_c), kv_out.shape[0], dfirst.shape[2], keep_first)
    for chain in (out, qup, first):
        chain.clear()
    row_sum = RowSum(wire, send, kept, row_got, row_out, row_back, quarter)
    out.step1()
    for m in range(2):
        send[m] = inner_cols(dfirst[m, half:, :], weights[...]).astype(LOW)
    row_sum.core.start()
    for m in range(2):
        kept[m] = inner_cols(dfirst[m, :half, :], weights[...])
    for z in range(4):
        side_sums[z] = terms_sum([(h1_theirs[m][z], dfirst[m]) for m in range(2)]).astype(LOW)
    row_sum.pass_on()
    ffn_sum = RowSum(wire, ffn_send, ffn_keep, ffn_got, ffn_out, ffn_back, quarter)
    ffn = dot(jnp.concatenate([hid0[...], hid1[...]], 0), w_down[...])
    for m in range(2):
        ffn_send[m] = ffn[m * rows + half : (m + 1) * rows].astype(LOW)
        ffn_keep[m] = ffn[m * rows : m * rows + half]
    ffn_sum.core.start()
    out.step2()
    dh1 = row_sum.result()
    gain1_sum = jnp.sum(jnp.sum(dh1 * n1[...], axis=0), axis=0, keepdims=True)
    back = dh1 * gain1[...]
    share = Share(wire, grad_tokens, quarter)
    share.begin(
        (dy[...] + inv1[...] * (back - n1[...] * mean_of(back * n1[...]))).astype(LOW)
    )
    w, r = gain1_sum.shape[1] // 8, gain_c_sum.shape[1] // 8
    for s in range(8):
        sums[s] = jnp.concatenate(
            [gain1_sum[:, s * w : (s + 1) * w], gain2_sum[:, s * w : (s + 1) * w],
             gain_c_sum[:, s * r : (s + 1) * r]], axis=1
        )
    core_sums = wire.send(sums, sums_core, wire.core)
    ffn_sum.pass_on()
    side_qup.wait_recv()
    side_first = wire.send(side_sums, side_got, wire.beside)
    qup.step1()
    out.step3()
    core_sums.wait_recv()
    core_sums.wait_send()
    sums[...] = sums[...] + sums_core[...]
    cross_sums = wire.send(sums, sums_cross, wire.cross)
    qup.step2()
    share.forward()
    layer_share = Share(wire, layer_out, quarter)
    layer_share.begin((y[...] + ffn_sum.result()).astype(LOW))
    side_first.wait_recv()
    first.step1()
    cross_sums.wait_recv()
    cross_sums.wait_send()
    sums[...] = sums[...] + sums_cross[...]
    side_of = lambda p, s: sums.at[2 * p + s]
    side_sends = [
        wire.send(side_of(p, 1 - wire.side), sums_side.at[p], wire.beside) for p in range(4)
    ]
    out.finish()
    qup.step3()
    first.step2()
    for made in side_sends:
        made.wait_recv()
        made.wait_send()
    line_sends = []
    for d in range(1, 4):
        for way, there in ((1, place + d <= 3), (-1, place - d >= 0)):
            index = 2 * (d - 1) + (way < 0)
            line_sends.append(
                (wire.copy(sums_line.at[6 + index], sums_line.at[index],
                           {"seq": wire.seq + 2 * way * d}), d, way, there)
            )

            @pl.when(there)
            def _(index=index, d=d, way=way):
                to = place + way * d
                sums_line[6 + index] = sums[2 * to + wire.side] + sums_side[to]
                line_sends[-1][0].start()

            @pl.when((place - way * d < 0) | (place - way * d > 3))
            def _(index=index):
                sums_line[index] = jnp.zeros(sums_line.shape[1:], F32)

    layer_share.forward()
    first.step3()
    qup.finish()
    first.finish()
    cores = []
    size = kv_out.shape[0] // 4
    for k in range(4):
        rows_of = pl.ds(pl.multiple_of(wire.blocks[k] * size, size), size)
        if k:
            device = {"mp": wire.blocks[k]}
            cores.append(wire.send(kv_out.at[rows_of], kv_got.at[k], device))
        else:
            kv_got[0] = kv_out[rows_of]
    total = sums[2 * place + wire.side] + sums_side[place]
    for made, d, way, there in line_sends:
        pl.when((place - way * d >= 0) & (place - way * d <= 3))(made.wait_recv)
    for index in range(6):
        total = total + sums_line[index]
    gains[...] = total
    for made in cores:
        made.wait_recv()
    columns = kv_out.shape[1]
    for k in range(4):
        at = pl.ds(pl.multiple_of(wire.blocks[k] * columns, columns), columns)
        grad_kv[:, at] = kv_got[k]
    share.end()
    layer_share.end()
    ffn_sum.end()
    for made in (side_first, side_qup, *cores):
        made.wait_send()
    for made, d, way, there in line_sends:
        pl.when(there)(made.wait_send)
    row_sum.end()
    for chain in (out, qup, first):
        chain.settle()


def attend_one(
    scale, mp_blocks, c, gain, q_up, cos, sin, kv, key_ids, row_ids, row_starts, out_proj,
    qn, q, o, lse, send, keep, chat_out, inverse_out,
):
    rows = qn.shape[0]
    half, quarter = rows // 2, rows // 4
    part = c.shape[2]
    wide = q.shape[2]
    cut = lambda k, i: c[k, i * quarter : (i + 1) * quarter, :]
    pieces = [jnp.concatenate([cut(k, i ^ k) for i in range(4)], 0) for k in range(4)]
    latent = jnp.concatenate(pieces, 1).astype(F32)
    inverse = inverse_rms(latent)
    chat = latent * inverse
    inverse_out[...] = inverse[:quarter]
    for k in range(4):
        columns = pl.ds(pl.multiple_of(mp_blocks[k] * part, part), part)
        chat_out[:, columns] = chat[:quarter, k * part : (k + 1) * part]
        qn[:, columns] = (chat[:, k * part : (k + 1) * part] * gain[:, columns]).astype(LOW)
    bias = jnp.where((key_ids >= row_starts) & (key_ids <= row_ids), 0.0, NEG_LARGE)
    low = qn[...]
    for h in range(q.shape[0]):
        pre = dot(low, q_up[:, h * wide : (h + 1) * wide])
        q_h = (rotate(pre, cos, sin) * scale).astype(LOW)
        q[h] = q_h
        scores = inner_cols(q_h, kv[:, :wide]) + bias
        top = jnp.max(scores, axis=-1, keepdims=True)
        probs = jnp.exp(scores - top)
        total = jnp.sum(probs, axis=-1, keepdims=True)
        out = dot(probs.astype(LOW), kv[:, wide:]) / total
        o[:, h * wide : (h + 1) * wide] = out.astype(LOW)
        log_total = jnp.broadcast_to(top + jnp.log(total), (rows, 128))
        lse[h : h + 1, :] = jnp.transpose(log_total)[:1]
    keep[...] = dot(o[:half, :], out_proj[...])
    send[...] = dot(o[half:, :], out_proj[...]).astype(LOW)


def fore1_body(scale, *refs):
    refs = list(refs)
    take = lambda n: [refs.pop(0) for _ in range(n)]
    tokens, cotangent, q_down, kv_proj, q_up, out_proj, w_down = take(7)
    lengths, gain1, gain_c, gain2, cosine, sine = take(6)
    h1_mine, h1_theirs, qn_mine, qn_theirs = (take(2) for _ in range(4))
    qs, os, lses, kvs, oo, dz_got = (take(2) for _ in range(6))
    dz, dz_mine, dhid, chat, inv_c, y_out, n2_out, inv2_out, n1_out, inv1_out, h2 = take(11)
    x, down_w, kv_w, up_w, out_w, back_w, h1, c, qn, dz_theirs = take(10)
    send, kept, got, cross_out, cross_got = take(5)
    loads = take(1)[0]
    wire = Wire(*take(2))
    place, blocks = wire.place, wire.blocks
    rows = x.shape[1]
    half, quarter = rows // 2, rows // 4
    wide = kv_proj.shape[1] // 2

    started = []

    def load(source, target):
        made = pltpu.make_async_copy(source, target, loads.at[len(started)])
        made.start()
        started.append(made)
        return made

    def load_rows(source, target):
        return [
            load(source.at[pl.ds(pl.multiple_of(blocks[k] * quarter, quarter), quarter), :],
                 target.at[k * quarter : (k + 1) * quarter, :])
            for k in range(4)
        ]

    in_x = [load_rows(tokens.at[0], x.at[0])]
    in_kv = load(kv_proj, kv_w)
    in_x.append(load_rows(tokens.at[1], x.at[1]))
    in_down = load(q_down, down_w)
    in_dz = [load_rows(cotangent.at[m], dz.at[m]) for m in range(2)]
    in_back, in_up, in_out = load(w_down, back_w), load(q_up, up_w), load(out_proj, out_w)

    line_kv, side_kv, core_kv, cross_c, core_c = [], [], [], [], []
    for m in range(2):
        for d in range(1, 4):

            @pl.when(place < d)
            def _(m=m, d=d):
                kvs[m][0, :, d] = jnp.zeros(kvs[m].shape[1:2] + kvs[m].shape[3:], LOW)
                kvs[m][1, :, d] = jnp.zeros(kvs[m].shape[1:2] + kvs[m].shape[3:], LOW)

        own = kvs[m].at[0, 0, 0]
        line_kv.append([
            wire.copy(own, kvs[m].at[0, 0, d], {"seq": wire.seq + 2 * d}) for d in range(1, 4)
        ])
        side_kv.append([
            wire.copy(kvs[m].at[0, 0, d], kvs[m].at[0, 1, d], wire.beside) for d in range(4)
        ])
        core_kv.append([
            wire.copy(kvs[m].at[0, :, d], kvs[m].at[1, :, d], wire.core) for d in range(4)
        ])
        cross_c.append(wire.copy(c.at[m, 0], c.at[m, 1], wire.cross))
        core_c.append([
            wire.copy(c.at[m, 0], c.at[m, 2], wire.core),
            wire.copy(c.at[m, 1], c.at[m, 3], wire.core),
        ])
    wire.greet(4, 3)

    for m in range(2):
        cos, sin = cosine[m], sine[m]
        for made in in_x[m]:
            made.wait()
        if m == 0:
            in_kv.wait()
        values = x[m].astype(F32)
        inverse = inverse_rms(values)
        normed = values * inverse
        n1_out[m], inv1_out[m] = normed[:quarter], inverse[:quarter]
        low = (normed * gain1[...]).astype(LOW)
        h1[...] = low
        pair = dot(low[:half], kv_w[...])
        own = kvs[m].at[0, 0, 0]
        own[:, :wide] = rotate(pair[:, :wide], cos[:half], sin[:half]).astype(LOW)
        own[:, wide:] = pair[:, wide:].astype(LOW)
        for d in (3, 2, 1):
            pl.when(place + d <= 3)(line_kv[m][d - 1].start)
        side_kv[m][0].start()
        if m == 0:
            in_down.wait()
        c[m, 0] = dot(low, down_w[...]).astype(LOW)
        cross_c[m].start()
        core_c[m][0].start()
        side_columns(h1, h1_mine[m], h1_theirs[m], wire.side)

    def pass_kv(m, d):
        @pl.when(place >= d)
        def _():
            line_kv[m][d - 1].wait_recv()
            side_kv[m][d].start()

    def pass_core(m, d):
        @pl.when(place >= d)
        def _():
            side_kv[m][d].wait_recv()
            core_kv[m][d].start()

    in_back.wait()
    for m in range(2):
        for made in in_dz[m]:
            made.wait()
    dhid[0] = inner_cols(dz[0], back_w[...])
    for d in (1, 2, 3):
        pass_kv(0, d)
    pass_core(0, 0)
    for m in range(2):
        cross_c[m].wait_recv()
        core_c[m][1].start()
    dhid[1] = inner_cols(dz[1], back_w[...])
    for d in (1, 2, 3):
        pass_kv(1, d)
    for m in range(2):
        side_columns(dz.at[m], dz_mine.at[m], dz_theirs.at[m], wire.side)
    for d in (1, 2, 3):
        pass_core(0, d)
    in_up.wait()
    in_out.wait()
    sums = [
        RowSum(wire, send.at[m : m + 1], kept.at[m : m + 1], got.at[m : m + 1],
               cross_out.at[m : m + 1], cross_got.at[m : m + 1], quarter)
        for m in range(2)
    ]
    side_o, shares = [], []

    def after_sum(m):
        value = x[m, :quarter, :].astype(F32) + sums[m].result()[0]
        inverse = inverse_rms(value)
        normed = value * inverse
        y_out[m], n2_out[m], inv2_out[m] = value, normed, inverse
        h2[m, :quarter, :] = (normed * gain2[...]).astype(LOW)
        spot = lambda k: h2.at[m, k * quarter : (k + 1) * quarter, :]
        shares.append((
            wire.send(spot(0), spot(1), wire.cross), wire.send(spot(0), spot(2), wire.core),
            wire.copy(spot(1), spot(3), wire.core),
        ))

    for m in range(2):
        if m == 1:
            for d in range(4):
                pass_core(1, d)
        for d in range(4):
            pl.when(place >= d)(core_kv[m][d].wait_recv)
        for made in core_c[m]:
            made.wait_recv()
        rows_at = row_places(wire, quarter, 0)
        attend_one(
            scale, blocks, c.at[m], gain_c, up_w, cosine[m], sine[m],
            kvs[m][...].reshape(2 * 2 * 4 * half, 2 * wide),
            key_places(wire, quarter, 4, 1, (0, 1)), rows_at,
            sequence_starts(lengths, m, rows_at), out_w, qn, qs[m], os[m], lses[m], send.at[m], kept.at[m],
            chat.at[m], inv_c.at[m],
        )
        sums[m].core.start()
        if m == 0:
            side_dz = wire.send(dz_theirs, dz_got[0], wire.beside)
        side_o.append(wire.send(os[m], oo[m], wire.beside))
        side_columns(qn, qn_mine[m], qn_theirs[m], wire.side)
        if m == 1:
            after_sum(0)
        sums[m].pass_on()
    after_sum(1)
    side_dz.wait_recv()
    core_dz = wire.send(dz_got[0], dz_got[1], wire.core)
    for near, _, far in shares:
        near.wait_recv()
        far.start()
    for _, first, far in shares:
        first.wait_recv()
        far.wait_recv()
    core_dz.wait_recv()
    for made in side_o:
        made.wait_recv()
    for made in [side_dz, core_dz, *side_o, *cross_c, *(a for p in core_c for a in p),
                 *(a for p in shares for a in p)]:
        made.wait_send()
    for m in range(2):
        sums[m].end()
        for d in range(4):

            @pl.when(place >= d)
            def _(m=m, d=d):
                side_kv[m][d].wait_send()
                core_kv[m][d].wait_send()

        for d in range(1, 4):
            pl.when(place + d <= 3)(line_kv[m][d - 1].wait_send)


def local(
    tokens,
    lengths,
    norm1_gain,
    q_down,
    latent_gain,
    q_up,
    kv_proj,
    out_proj,
    norm2_gain,
    w_gate,
    w_up,
    w_down,
    cotangent,
):
    micro, rows, width = tokens.shape
    seq = lax.axis_size("seq")
    line = seq // 2
    at = lax.axis_index("seq").astype(jnp.int32)
    me = lax.axis_index("mp").astype(jnp.int32)
    place, side = at // 2, at % 2
    ids = jnp.stack([me, side])
    quarter, half = rows // 4, rows // 2
    head_dim = kv_proj.shape[1] // 2
    heads = q_up.shape[1] // head_dim
    part = q_down.shape[1]
    rank = q_up.shape[0]
    hidden = w_gate.shape[1]
    kv_part = kv_proj.shape[1] // 4
    wide = width // seq
    scale = head_dim ** (-0.5)
    key_count = seq * rows
    beside = [(i, i ^ 1) for i in range(seq)]
    narrow = line == 4 and micro == 2 and key_count <= 2048 and not wide % 128

    def swap(index):
        return ((index & 1) << 1) | (index >> 1)

    def to_natural(array, axis):
        size = array.shape[axis] // 4
        return jnp.concatenate(
            [lax.dynamic_slice_in_dim(array, swap(me ^ b) * size, size, axis) for b in range(4)],
            axis,
        )

    def other(array):
        return lax.ppermute(array, "seq", beside)

    def sum_mp(send, keep):
        kept = keep + lax.ppermute(send, "mp", CORE).astype(F32)
        got = lax.ppermute(kept[..., quarter:, :].astype(LOW), "mp", CROSS)
        return kept[..., :quarter, :] + got.astype(F32)

    def gather_mp(piece):
        near = lax.ppermute(piece, "mp", CROSS)
        pair = jnp.concatenate([piece, near], -2)
        return piece, near, lax.ppermute(pair, "mp", CORE)

    def sides_shape(columns, their_rows, lead=()):
        if columns // seq % 128:
            return []
        return [
            whole((*lead, line, n, columns // seq), LOW) for n in (rows, their_rows)
        ]

    def split_sides(made, full, their_rows):
        if made:
            return made
        split = full.reshape(*full.shape[:-1], line, 2, full.shape[-1] // seq)
        mine, theirs = (
            jnp.moveaxis(lax.dynamic_index_in_dim(split, i, split.ndim - 2, keepdims=False), -2, -3)
            for i in (side, 1 - side)
        )
        return mine, theirs[..., :their_rows, :]

    def from_other(theirs):
        got = other(theirs)
        return got, lax.ppermute(got, "mp", CORE)

    def without_sides(body, count):
        return body if count else lambda *refs: body(*refs, None, None)

    def both_sides(mine, got):
        lefts, spans = [], []
        for array, first, count, partner in (
            (mine, 0, rows, 0), (got[0], 0, half, 1), (got[1], half, half, 1)
        ):
            stacked_array = not isinstance(array, list)
            for m in range(micro):
                spans.append((len(lefts) if not stacked_array else len(lefts), m if stacked_array else None,
                              m, partner, first, count))
                if not stacked_array:
                    lefts.append(array[m])
            if stacked_array:
                lefts.append(array)
        return lefts, spans

    class Chain:
        def __init__(self, lefts, rights, terms, shape, turned=False, from_side=None):
            self.args = [*lefts, *rights]
            self.spec = (terms, len(lefts), len(rights))
            self.shape, self.turned = shape, turned
            self.from_side = [] if from_side is None else [from_side]
            self.step, self.up, self.down = 0, None, None

        def block(self, index, added, after, last=False):
            turned = last and self.turned
            body = functools.partial(
                block_body, *self.spec, len(added), len(self.from_side), turned
            )
            shape = self.shape[::-1] if turned else self.shape
            return run(
                body, index.reshape(1), [*self.args, *added, *self.from_side],
                [whole(shape, F32 if last else LOW)], after, name="block",
            )[0]

        def advance(self, after):
            self.step += 1
            step = self.step
            goes_up = [(i, i + 2) for i in range(2 * step)]
            goes_down = [(seq - 1 - i, seq - 3 - i) for i in range(2 * step)]
            for_up, for_down = line - step + place, step - line + place
            if 2 * step < line + 1:
                which = jnp.where(
                    place <= step - 1, for_up, jnp.where(place >= line - step, for_down, 0)
                )
                term = self.block(which, [a for a in (self.up, self.down) if a is not None], after)
                if step == 1 and line > 3:
                    self.up = lax.ppermute(term, "seq", goes_up + goes_down)
                else:
                    self.up = lax.ppermute(term, "seq", goes_up)
                    self.down = lax.ppermute(term, "seq", goes_down)
                return [term]
            term_up = self.block(jnp.clip(for_up, 0, line - 1), [self.up], after)
            term_down = self.block(jnp.clip(for_down, 0, line - 1), [self.down], [term_up])
            self.up = lax.ppermute(term_up, "seq", goes_up)
            self.down = lax.ppermute(term_down, "seq", goes_down)
            return [term_down]

        def finish(self, after):
            while self.step < line - 1:
                after = self.advance(after)
            result = self.block(place, [self.up, self.down], after, last=True)
            return result, [result]

    quarter_rows = jnp.arange(quarter, dtype=jnp.int32)
    row_ids = at * rows + jnp.concatenate([(me ^ k) * quarter + quarter_rows for k in ORDER])
    key_ids = (
        ((place - jnp.arange(line, dtype=jnp.int32)[None, None, :, None, None]) * 2
         + (side ^ jnp.arange(2, dtype=jnp.int32)[None, :, None, None, None])) * rows
        + (me ^ (jnp.arange(2, dtype=jnp.int32)[:, None, None, None, None]
                 + 2 * jnp.arange(2, dtype=jnp.int32)[None, None, None, :, None])) * quarter
        + quarter_rows[None, None, None, None, :]
    ).reshape(key_count)

    gain1_row, gain2_row, gain_c_row = norm1_gain[None, :], norm2_gain[None, :], latent_gain[None, :]
    kv_cols = lax.dynamic_slice_in_dim(kv_proj, me * kv_part, kv_part, 1)
    first_weights = jnp.concatenate([q_down, kv_cols], axis=1)
    low = lambda *shape: pltpu.VMEM(shape, LOW)
    full = lambda *shape: pltpu.VMEM(shape, F32)
    near = lambda *arrays: [(1, a) for a in arrays]
    far = lambda *arrays: [(0, a) for a in arrays]
    columns = heads * head_dim
    side_rows = rank // seq
    first_columns = part + kv_part

    def narrow_layer():
        numbers = lambda array: [(2, array)]
        ends = jnp.cumsum(lengths, axis=1)
        first_end, second_end = ends[:, 0:1], ends[:, 1:2]
        places = row_ids[None, :] - jnp.where(
            row_ids >= second_end, second_end, jnp.where(row_ids >= first_end, first_end, 0)
        )
        freqs = BASE ** (-2.0 * jnp.arange(head_dim // 2, dtype=F32) / head_dim)
        angles = places.astype(F32)[:, :, None] * freqs
        cosine, sine = jnp.cos(angles), jnp.sin(angles)
        row_shape = whole((micro, quarter, width), F32)
        one_shape = whole((micro, quarter, 1), F32)
        side_shape = whole((micro, line, half, wide), LOW)
        args = far(tokens, cotangent, q_down, kv_proj, q_up, out_proj, w_down)
        args += numbers(lengths) + near(gain1_row, gain_c_row, gain2_row, cosine, sine)
        outs = near(*[whole((line, rows, wide), LOW)] * 4, *[whole((line, rows, side_rows), LOW)] * 4)
        outs += near(*[whole((heads, rows, head_dim), LOW)] * 2, *[whole((rows, columns), LOW)] * 2)
        outs += near(*[whole((heads, rows), F32)] * 2)
        outs += near(*[whole((2, 2, line, half, 2 * head_dim), LOW)] * 2)
        outs += far(*[whole((rows, columns), LOW)] * 2, *[side_shape] * 2)
        outs += near(
            whole((micro, rows, width), LOW), whole((micro, line, rows, wide), LOW),
            whole((micro, rows, hidden), F32), whole((micro, quarter, rank), F32), one_shape,
            row_shape, row_shape, one_shape, row_shape, one_shape,
            whole((micro, rows, width), LOW),
        )
        made = list(mesh_run(
            functools.partial(fore1_body, scale), args, outs,
            [low(micro, rows, width), low(width, part), low(width, 2 * head_dim),
             low(rank, columns), low(columns, width), low(hidden, width), low(rows, width),
             low(micro, 4, rows, part), low(rows, rank), low(micro, line, half, wide),
             low(micro, half, width), full(micro, half, width), low(micro, half, width),
             low(micro, quarter, width), low(micro, quarter, width),
             pltpu.SemaphoreType.DMA((24,))],
            4, "fore1", 60, 60,
        ))
        give = lambda n: [made.pop(0) for _ in range(n)]
        h1_mine, h1_theirs, qn_mine, qn_theirs = (give(2) for _ in range(4))
        qs, os, lses, kv, o_other, dz_got = (give(2) for _ in range(6))
        kv = [a.reshape(key_count, 2 * head_dim) for a in kv]
        dz, dz_mine, dhid, chat, inv_c, y, n2, inv2, n1, inv1, h2 = give(11)

        args = far(w_gate, w_up) + near(h2, dhid, n2, inv2, dz, gain2_row, dz_mine, *dz_got)
        outs = near(
            whole((hidden, wide), F32), row_shape, whole((1, width), F32),
            whole((micro, rows, width), LOW), whole((micro, line, rows, wide), LOW), side_shape,
            *[whole((rows, hidden), LOW)] * 6, *[whole((line, rows, wide), LOW)] * 2,
        ) + far(*[whole((line, half, wide), LOW)] * 4, *[whole((rows, hidden), LOW)] * 2)
        made = list(mesh_run(
            functools.partial(back1_body, quarter), args, outs,
            [low(width, hidden), low(width, hidden), low(rows, hidden), low(rows, hidden),
             low(micro, line, half, wide), low(5, wide, hidden), low(2, wide, hidden),
             low(micro, half, width), full(micro, half, width), low(micro, half, width),
             low(micro, quarter, width), low(micro, quarter, width),
             pltpu.SemaphoreType.DMA((2,))],
            1, "back1", 60, 24,
        ))
        grad_down, dy, gain2, dyl, dyl_mine, dyl_theirs = give(6)
        hid, dg, du, h2_mine, h2_got, h2_far, dg_other = (give(2) for _ in range(7))

        args = numbers(lengths) + near(*dg, *dg_other, *du, *h2_mine, *h2_got, *h2_far)
        args += near(dyl, out_proj, q_up, *qs, *kv, *os, *lses, cosine, sine, chat, inv_c,
                     gain_c_row) + far(dyl_theirs)
        outs = near(whole((wide, hidden), F32), whole((wide, hidden), F32),
                    whole((micro, rows, first_columns), LOW), whole((1, rank), F32),
                    whole((micro, rows, columns), LOW))
        outs += far(side_shape, side_shape)
        kv_low = lambda *lead: low(*lead, quarter, 2 * head_dim)
        key_half = key_count // 2
        grad_gate, grad_up, dfirst, gain_c, dqp, dyl_got, dyl_far = mesh_run(
            functools.partial(back2_body, quarter, scale), args, outs,
            [low(rows, hidden), low(rows, hidden), low(5, wide, hidden), low(2, wide, hidden),
             low(5, wide, hidden), low(2, wide, hidden), full(heads, rows, head_dim),
             low(heads, rows, head_dim), full(heads, 8, rows), low(micro, half, rank),
             full(micro, half, rank), low(micro, key_half, 2 * head_dim),
             low(micro, key_half, 2 * head_dim), low(micro, half, rank),
             low(micro, quarter, rank), low(micro, quarter, rank),
             low(micro, key_half, 2 * head_dim), kv_low(micro, 2 * line), kv_low(micro, 2 * line),
             kv_low(micro, line), kv_low(micro, line), kv_low(micro, 3), kv_low(micro, 3),
             full(micro, quarter, 2 * head_dim), low(micro, rows, rank + 2 * head_dim)],
            2, "back2", 62, 44,
        )

        kv_cols = lax.dynamic_slice_in_dim(kv_proj, me * kv_part, kv_part, 1)
        first_weights = jnp.concatenate([q_down, kv_cols], axis=1)
        args = near(dfirst, first_weights, *h1_mine, *h1_theirs, *os, *o_other, dyl_mine, dyl_got,
                    dyl_far, *qn_mine, *qn_theirs, dqp, n1, inv1, dy, gain1_row, gain2, gain_c,
                    *hid, w_down, y)
        block = width // 4 // seq
        gain_columns = 2 * wide + side_rows
        outs = near(whole((columns, wide), F32), whole((side_rows, columns), F32),
                    whole((wide, part), F32), whole((block, 2 * head_dim), F32),
                    whole((micro, rows, width), LOW), whole((1, gain_columns), F32),
                    whole((micro, rows, width), LOW))
        grad_out, grad_qup, grad_qdown, grad_kv, input_grads, gains, layer_out = mesh_run(
            functools.partial(back3_body, quarter), args, outs,
            [low(5, wide, columns), low(2, wide, columns), low(5, side_rows, columns),
             low(2, side_rows, columns), low(5, wide, first_columns),
             low(2, wide, first_columns), low(line, wide, first_columns),
             low(line, wide, first_columns), low(micro, half, width), full(micro, half, width),
             low(micro, half, width), low(micro, quarter, width), low(micro, quarter, width),
             full(wide, kv_part), full(4, block, kv_part), full(seq, 1, gain_columns),
             full(seq, 1, gain_columns), full(seq, 1, gain_columns), full(line, 1, gain_columns),
             full(12, 1, gain_columns), low(micro, half, width), full(micro, half, width),
             low(micro, half, width), low(micro, quarter, width), low(micro, quarter, width),
             low(line, side_rows, columns), low(line, side_rows, columns)],
            3, "back3", 60, 50,
        )
        return (
            layer_out, input_grads, gains[0, :wide], grad_qdown, gains[0, 2 * wide :], grad_qup,
            grad_kv, grad_out, gains[0, wide : 2 * wide], grad_gate, grad_up, grad_down,
        )

    if narrow:
        return narrow_layer()

    both_rows = sides_shape(width, rows)
    half_rows = sides_shape(width, half)
    rank_sides = sides_shape(rank, rows)

    tables, starts, kv, c_part, h1_sides = [], [], [], [], []
    order = []
    for m in range(micro):
        _, places = documents(lengths[m], row_ids)
        starts.append(row_ids - places)
        tables.append(rotation(places, head_dim))
        c, packed, h1, *made = run(
            without_sides(functools.partial(first_body, m, quarter), len(both_rows)),
            ids,
            [tokens, gain1_row, q_down, kv_proj, *tables[m]],
            [whole((rows, part), LOW), whole((half, 2 * head_dim), LOW), whole((rows, width), LOW),
             *both_rows],
            order,
            name="first",
        )
        order = [c]
        blocks = [packed] + [
            lax.ppermute(packed, "seq", [(i, i + 2 * d) for i in range(seq - 2 * d)])
            for d in range(1, line)
        ]
        near = jnp.stack(blocks, 0)
        near = jnp.stack([near, other(near)], 0)
        kv.append(
            jnp.stack([near, lax.ppermute(near, "mp", CORE)], 0).reshape(key_count, 2 * head_dim)
        )
        c_part.append(c)
        h1_sides.append(split_sides(made, h1, rows))

    dhid, dz, *made = run(
        functools.partial(cotangent_body, micro, quarter),
        ids,
        [cotangent, w_down],
        [whole((micro, rows, hidden), F32), whole((micro, rows, width), LOW),
         *sides_shape(width, half, (micro,))],
        order,
        name="cotangent",
    )
    order = [dz]
    dz_mine, dz_theirs = split_sides(made, dz, half)
    dz_got = from_other(dz_theirs)

    qn_sides, qs, os, lses, sums, c_rows = [], [], [], [], [], []
    for m in range(micro):
        near = lax.ppermute(c_part[m], "mp", CROSS)
        swapped = jnp.concatenate(
            [near[quarter : 2 * quarter], near[:quarter], near[3 * quarter :],
             near[2 * quarter : 3 * quarter]], 0
        )
        far = lax.ppermute(jnp.concatenate([c_part[m], swapped], 1), "mp", CORE)
        qn, q, o, lse, send, keep, *made = run(
            without_sides(functools.partial(attend_body, scale), len(rank_sides)),
            ids,
            [c_part[m], near, far, gain_c_row, q_up, *tables[m], kv[m], key_ids[None, :],
             row_ids[:, None], starts[m][:, None], out_proj],
            [whole((rows, rank), LOW), whole((heads, rows, head_dim), LOW),
             whole((rows, heads * head_dim), LOW), whole((heads, rows), F32),
             whole((half, width), LOW), whole((half, width), F32), *rank_sides],
            order,
            name="attend",
        )
        order = [o]
        qn_sides.append(split_sides(made, qn, rows))
        qs.append(q)
        os.append(o)
        lses.append(lse)
        sums.append(sum_mp(send, keep))
        c_rows.append(
            jnp.concatenate([c_part[m][:quarter], swapped[:quarter], far[half : half + quarter]], 1)
        )

    h2_mine, h2_theirs, hid, dg, du, state = [], [], [], [], [], []
    for m in range(micro):
        x = lax.dynamic_slice_in_dim(tokens[m], me * quarter, quarter, 0).astype(F32)
        inv1 = inverse_rms(x)
        y = x + sums[m]
        inv2 = inverse_rms(y)
        n2 = y * inv2
        pieces = gather_mp((n2 * gain2_row).astype(LOW))
        h2, hid_m, dg_m, du_m, *made = run(
            without_sides(functools.partial(forward_body, m), len(half_rows)),
            ids,
            [*pieces, w_gate, w_up, dhid],
            [whole((rows, width), LOW), *[whole((rows, hidden), LOW)] * 3, *half_rows],
            order,
            name="forward",
        )
        order = [hid_m]
        mine, theirs = split_sides(made, h2, half)
        h2_mine.append(mine)
        h2_theirs.append(theirs)
        hid.append(hid_m)
        dg.append(dg_m)
        du.append(du_m)
        state.append(dict(x=x, n1=x * inv1, inv1=inv1, y=y, n2=n2, inv2=inv2, c=c_rows[m]))

    def stacked(name):
        return jnp.stack([st[name] for st in state], 0)

    def with_other(arrays):
        return [*arrays, *[other(a) for a in arrays]]

    def terms_of(spans):
        return [(a, lead, m + micro * partner, None, first, count)
                for a, lead, m, partner, first, count in spans]

    send, keep, ffn_send, ffn_keep = run(
        functools.partial(hidden_back_body, micro),
        ids,
        [*dg, *du, *hid, w_gate, w_up, w_down],
        [whole((micro, half, width), LOW), whole((micro, half, width), F32)] * 2,
        order,
        name="hidden_back",
    )
    lefts, spans = both_sides(dz_mine, dz_got)
    chain_down = Chain(lefts, with_other(hid), terms_of(spans), (wide, hidden), turned=True)
    lefts, spans = both_sides(h2_mine, [list(p) for p in zip(*[from_other(t) for t in h2_theirs])])
    chain_gate = Chain(lefts, with_other(dg), terms_of(spans), (wide, hidden))
    chain_up = Chain(lefts, with_other(du), terms_of(spans), (wide, hidden))

    order = chain_down.advance([send])
    dh2 = sum_mp(send, keep)
    y, n2, inv2, n1, inv1 = (stacked(k) for k in ("y", "n2", "inv2", "n1", "inv1"))
    dz_own = dz[:, :quarter].astype(F32)
    gain2 = jnp.sum(dh2 * n2, axis=(0, 1))
    dy = dz_own + norm_backward(dh2 * gain2_row, n2, inv2)
    for _ in range(2):
        order = chain_down.advance(order)
    order = chain_gate.advance(order)

    def attend_back(which, pieces):
        args = [*pieces, out_proj, q_up, key_ids[:, None]]
        for m in which:
            args += [qs[m], kv[m], os[m], lses[m], jnp.stack([row_ids, starts[m]], 0), *tables[m]]
        n = len(which)
        return run(
            functools.partial(attend_back_body, scale, n, min(1024, key_count // 2)),
            ids,
            args,
            [whole((n, rows, width), LOW), whole((n, rows, heads * head_dim), LOW),
             whole((n, half, rank), LOW), whole((n, half, rank), F32),
             whole((n, key_count // 2, 2 * head_dim), LOW),
             whole((n, key_count // 2, 2 * head_dim), F32), *sides_shape(width, half, (n,))],
            order,
            scratch=[pltpu.VMEM((heads, rows, head_dim), F32),
                     pltpu.VMEM((heads, rows, head_dim), LOW),
                     pltpu.VMEM((heads, 8, rows), F32)],
            name="attend_back",
            limit=56,
        )

    pieces = gather_mp(dy.astype(LOW))
    if key_count <= 2048:
        made = attend_back(range(micro), pieces)
    else:
        each = [attend_back([m], [p[m : m + 1] for p in pieces]) for m in range(micro)]
        made = [jnp.concatenate(parts, 0) for parts in zip(*each)]
    dyl, dqp, send, keep, kv_send, kv_keep, *made = made
    order = [send]
    dyl_mine, dyl_theirs = split_sides(made, dyl, half)
    lefts, spans = both_sides(dyl_mine, from_other(dyl_theirs))
    chain_out = Chain(lefts, with_other(os), terms_of(spans), (wide, heads * head_dim), turned=True)

    def side_sum(lefts, rights, shape, after):
        terms = [(m, None, 0, m, 0, rows) for m in range(micro)]
        (made,) = run(
            functools.partial(side_sum_body, terms, len(lefts)),
            ids,
            [*lefts, *rights],
            [whole((line, *shape), LOW)],
            after,
            name="side_sum",
        )
        return other(made), [made]

    def own_chain(side_pairs, right, shape, after):
        from_side, after = side_sum([p[1] for p in side_pairs], [right], shape, after)
        terms = [(m, None, 0, m, 0, rows) for m in range(micro)]
        return Chain([p[0] for p in side_pairs], [right], terms, shape, from_side=from_side), after

    shape = (rank // seq, heads * head_dim)
    chain_qup, order = own_chain(qn_sides, dqp, shape, order)
    order = chain_gate.advance(order)
    order = chain_up.advance(order)

    dqn = sum_mp(send, keep)
    c = stacked("c").astype(F32)
    inv_c = inverse_rms(c)
    chat = c * inv_c
    chat = to_natural(chat, 2)
    gain_c = jnp.sum(dqn * chat, axis=(0, 1))
    dc = norm_backward(dqn * gain_c_row, chat, inv_c).astype(LOW)

    dkv = kv_keep + lax.ppermute(kv_send, "mp", CORE).astype(F32)
    dkv = dkv.reshape(micro, 2, line, 2, quarter, 2 * head_dim)
    dkv = dkv[:, :, :, 0] + lax.ppermute(dkv[:, :, :, 1].astype(LOW), "mp", CROSS).astype(F32)
    dkv = dkv[:, 0] + other(dkv[:, 1].astype(LOW)).astype(F32)
    total = dkv[:, 0]
    for d in range(1, line):
        total = total + lax.ppermute(
            dkv[:, d].astype(LOW), "seq", [(i + 2 * d, i) for i in range(seq - 2 * d)]
        ).astype(F32)
    cosine = jnp.stack([t[0][:quarter] for t in tables], 0)
    sine = jnp.stack([t[1][:quarter] for t in tables], 0)
    dkv_low = jnp.concatenate(
        [unrotate(total[..., :head_dim], cosine, sine), total[..., head_dim:]], axis=-1
    ).astype(LOW)
    both = jnp.concatenate(gather_mp(jnp.concatenate([dc, dkv_low], -1)), -2)
    dfirst = jnp.concatenate(
        [lax.dynamic_slice_in_dim(both, me * part, part, 2),
         lax.dynamic_slice_in_dim(both, rank + me * kv_part, kv_part, 2)], -1
    )

    grad_down, order = chain_down.finish(order)
    order = chain_gate.advance(order)
    order = chain_up.advance(order)
    order = chain_out.advance(order)
    grad_gate, order = chain_gate.finish(order)
    order = chain_up.advance(order)
    order = chain_out.advance(order)
    grad_up, order = chain_up.finish(order)
    order = chain_qup.advance(order)
    order = chain_out.advance(order)
    chain_first, order = own_chain(h1_sides, dfirst, (wide, part + kv_part), order)
    order = chain_qup.advance(order)
    grad_out, order = chain_out.finish(order)
    order = chain_first.advance(order)
    order = chain_qup.advance(order)
    order = chain_first.advance(order)
    grad_qup, order = chain_qup.finish(order)
    order = chain_first.advance(order)
    grad_first, order = chain_first.finish(order)

    grad_qdown = grad_first[:, :part]
    kv_cols_grad = grad_first[:, part:]
    pieces = []
    for k in ORDER:
        size = kv_cols_grad.shape[0] // 4
        sent = lax.dynamic_slice_in_dim(kv_cols_grad, (me ^ k) * size, size, 0)
        pieces.append(lax.ppermute(sent, "mp", [(i, i ^ k) for i in range(4)]) if k else sent)
    grad_kv = to_natural(jnp.concatenate(pieces, 1), 1)

    def put_natural(pieces):
        return run(
            functools.partial(natural_body, micro, quarter),
            ids,
            pieces,
            [whole((micro, rows, width), LOW)],
            name="natural",
        )[0]

    part_sum = inner_cols(dfirst.reshape(micro * rows, -1), first_weights).reshape(micro, rows, width)
    dh1 = sum_mp(part_sum[:, half:].astype(LOW), part_sum[:, :half])
    gain1 = jnp.sum(dh1 * n1, axis=(0, 1))
    dx = (dy + norm_backward(dh1 * gain1_row, n1, inv1)).astype(LOW)
    input_grads = put_natural(gather_mp(dx))

    ffn = sum_mp(ffn_send, ffn_keep)
    layer_out = put_natural(gather_mp((y + ffn).astype(LOW)))

    gains = jnp.concatenate(
        [gain1.reshape(seq, -1), gain2.reshape(seq, -1), gain_c.reshape(seq, -1)], axis=1
    )
    gains = gains + lax.ppermute(gains, "mp", CORE)
    gains = gains + lax.ppermute(gains, "mp", CROSS)
    gain_sum = lax.dynamic_index_in_dim(gains, at, 0, keepdims=False)
    for k in range(1, seq):
        gain_sum = gain_sum + lax.ppermute(
            lax.dynamic_index_in_dim(gains, at ^ k, 0, keepdims=False),
            "seq",
            [(i, i ^ k) for i in range(seq)],
        )
    return (
        layer_out,
        input_grads,
        gain_sum[:wide],
        grad_qdown,
        gain_sum[2 * wide :],
        grad_qup,
        grad_kv,
        grad_out,
        gain_sum[wide : 2 * wide],
        grad_gate,
        grad_up,
        grad_down,
    )


def solution(mesh):
    placed = (
        P(None, "seq", None),
        P(),
        P(),
        P(None, "mp"),
        P(),
        P(None, "mp"),
        P(),
        P("mp", None),
        P(),
        P(None, "mp"),
        P(None, "mp"),
        P("mp", None),
        P(None, "seq", None),
    )
    return jax.shard_map(
        local,
        mesh=mesh,
        in_specs=placed,
        out_specs=(
            P(None, "seq", None),
            P(None, "seq", None),
            P("seq"),
            P("seq", "mp"),
            P("seq"),
            P("seq", "mp"),
            P(("seq", "mp"), None),
            P("mp", "seq"),
            P("seq"),
            P("seq", "mp"),
            P("seq", "mp"),
            P("mp", "seq"),
        ),
        check_vma=False,
    )
```

```python
import functools

import jax
import jax.numpy as jnp
from jax import lax
from jax.experimental import pallas as pl
from jax.experimental.pallas import tpu as pltpu
from jax.sharding import PartitionSpec as P

EPS = 1e-06
BASE = 10000.0
NEG_LARGE = -1e30
LOW = jnp.bfloat16
F32 = jnp.float32
ORDER = (0, 2, 1, 3)
CORE = [(i, i ^ 1) for i in range(4)]
CROSS = [(i, i ^ 2) for i in range(4)]


def inverse_rms(values):
    return lax.rsqrt(jnp.mean(values * values, axis=-1, keepdims=True) + EPS)


def norm_backward(grad_hat, normed, inverse):
    return inverse * (grad_hat - normed * jnp.mean(grad_hat * normed, axis=-1, keepdims=True))


def dot(left, right):
    return jnp.dot(left, right, preferred_element_type=F32)


def inner_rows(left, right):
    return lax.dot_general(left, right, (((0,), (0,)), ((), ())), preferred_element_type=F32)


def inner_cols(left, right):
    return lax.dot_general(left, right, (((1,), (1,)), ((), ())), preferred_element_type=F32)


def documents(lengths_row, rows):
    first_end = lengths_row[0]
    second_end = first_end + lengths_row[1]
    doc_ids = (rows >= first_end).astype(jnp.int32) + (rows >= second_end).astype(jnp.int32)
    starts = jnp.where(rows >= second_end, second_end, jnp.where(rows >= first_end, first_end, 0))
    return (doc_ids, rows - starts)


def rotation(positions, head_dim):
    half = head_dim // 2
    freqs = BASE ** (-2.0 * jnp.arange(half, dtype=F32) / head_dim)
    angles = positions.astype(F32)[:, None] * freqs[None, :]
    return (jnp.cos(angles), jnp.sin(angles))


def rotate(values, cosine, sine):
    half = values.shape[-1] // 2
    first = values[..., :half]
    second = values[..., half:]
    return jnp.concatenate(
        [first * cosine - second * sine, second * cosine + first * sine], axis=-1
    )


def unrotate(grads, cosine, sine):
    return rotate(grads, cosine, -sine)


def in_vmem():
    return pl.BlockSpec(memory_space=pltpu.VMEM)


def whole(shape, dtype):
    return jax.ShapeDtypeStruct(shape, dtype)


def run(body, ids, args, outs, after=(), scratch=(), name=None, limit=40):
    args, after = list(args), list(after)

    def without(*refs):
        body(*refs[: 1 + len(args)], *refs[1 + len(args) + len(after) :])

    return pl.pallas_call(
        without,
        grid_spec=pltpu.PrefetchScalarGridSpec(
            num_scalar_prefetch=1,
            grid=(1,),
            in_specs=[in_vmem()] * len(args) + [pl.BlockSpec(memory_space=pl.ANY)] * len(after),
            out_specs=[in_vmem()] * len(outs),
            scratch_shapes=list(scratch),
        ),
        out_shape=list(outs),
        cost_estimate=pl.CostEstimate(flops=1000, bytes_accessed=1000, transcendentals=0),
        compiler_params=pltpu.CompilerParams(vmem_limit_bytes=limit << 20),
        name=name,
    )(ids, *args, *after)


def side_columns(source, mine, theirs, side):
    line, _, wide = mine.shape
    rows = theirs.shape[1]
    for z in range(line):
        mine[z] = source[:, pl.ds(pl.multiple_of((2 * z + side) * wide, wide), wide)]
        theirs[z] = source[:rows, pl.ds(pl.multiple_of((2 * z + 1 - side) * wide, wide), wide)]


def first_body(m, quarter, ids, x_ref, gain, q_down, kv_proj, cos, sin, c, kv, h1, mine, theirs):
    blocks = [
        x_ref[m, pl.ds(pl.multiple_of((ids[0] ^ k) * quarter, quarter), quarter), :] for k in ORDER
    ]
    x = jnp.concatenate(blocks, 0).astype(F32)
    low = (x * inverse_rms(x) * gain[...]).astype(LOW)
    h1[...] = low
    half = 2 * quarter
    pair = dot(low[:half], kv_proj[...])
    wide = kv_proj.shape[1] // 2
    kv[:, :wide] = rotate(pair[:, :wide], cos[:half], sin[:half]).astype(LOW)
    kv[:, wide:] = pair[:, wide:].astype(LOW)
    c[...] = dot(low, q_down[...]).astype(LOW)
    if mine is not None:
        side_columns(h1, mine, theirs, ids[1])


def cotangent_body(micro, quarter, ids, z_ref, w_down, dhid, dz, *sides):
    for m in range(micro):
        blocks = [
            z_ref[m, pl.ds(pl.multiple_of((ids[0] ^ k) * quarter, quarter), quarter), :]
            for k in ORDER
        ]
        dz[m] = jnp.concatenate(blocks, 0)
        if sides:
            side_columns(dz.at[m], sides[0].at[m], sides[1].at[m], ids[1])
        dhid[m] = inner_cols(dz[m], w_down[...])


def attend_body(
    scale, ids, c0, c1, c2, gain, q_up, cos, sin, kv, key_ids, row_ids, row_starts, out_proj,
    qn, q, o, lse, send, keep, mine, theirs,
):
    rows = qn.shape[0]
    quarter = rows // 4
    part = c0.shape[1]
    wide = q.shape[2]
    got = c1[...]
    pair = jnp.concatenate(
        [got[quarter : 2 * quarter], got[:quarter], got[3 * quarter :], got[2 * quarter : 3 * quarter]],
        0,
    )
    far = jnp.concatenate([c2[2 * quarter :], c2[: 2 * quarter]], 0)
    c = jnp.concatenate([c0[...], pair, far], 1).astype(F32)
    chat = c * inverse_rms(c)
    for k, xor in enumerate(ORDER):
        columns = pl.ds(pl.multiple_of((ids[0] ^ xor) * part, part), part)
        qn[:, columns] = (chat[:, k * part : (k + 1) * part] * gain[:, columns]).astype(LOW)
    if mine is not None:
        side_columns(qn, mine, theirs, ids[1])
    bias = jnp.where(
        (key_ids[...] >= row_starts[...]) & (key_ids[...] <= row_ids[...]), 0.0, NEG_LARGE
    )
    low = qn[...]
    keys, values = kv[:, :wide], kv[:, wide:]
    for h in range(q.shape[0]):
        pre = dot(low, q_up[:, h * wide : (h + 1) * wide])
        q_h = (rotate(pre, cos[...], sin[...]) * scale).astype(LOW)
        q[h] = q_h
        scores = inner_cols(q_h, keys) + bias
        top = jnp.max(scores, axis=-1, keepdims=True)
        probs = jnp.exp(scores - top)
        total = jnp.sum(probs, axis=-1, keepdims=True)
        out = dot(probs.astype(LOW), values) / total
        o[:, h * wide : (h + 1) * wide] = out.astype(LOW)
        log_total = jnp.broadcast_to(top + jnp.log(total), (rows, 128))
        lse[h : h + 1, :] = jnp.transpose(log_total)[:1]
    half = 2 * quarter
    send[...] = dot(o[half:, :], out_proj[...]).astype(LOW)
    keep[...] = dot(o[:half, :], out_proj[...])


def forward_body(m, ids, a0, a1, a2, w_gate, w_up, dhid, h2, hid, dg, du, mine, theirs):
    h2[...] = jnp.concatenate([a0[...], a1[...], a2[...]], 0)
    if mine is not None:
        side_columns(h2, mine, theirs, ids[1])
    low = h2[...]
    g = dot(low, w_gate[...])
    u = dot(low, w_up[...])
    sig = jax.nn.sigmoid(g)
    swish = g * sig
    hid[...] = (swish * u).astype(LOW)
    back = dhid[m]
    dg[...] = (back * u * sig * (1.0 + g * (1.0 - sig))).astype(LOW)
    du[...] = (back * swish).astype(LOW)


def hidden_back_body(micro, ids, *refs):
    dgs, dus = refs[:micro], refs[micro : 2 * micro]
    hids = refs[2 * micro : 3 * micro]
    w_gate, w_up, w_down, send, keep, out_send, out_keep = refs[3 * micro :]
    half = send.shape[1]
    every = lambda parts: jnp.concatenate([part[...] for part in parts], 0)
    rows = 2 * half
    total = inner_cols(every(dgs), w_gate[...]) + inner_cols(every(dus), w_up[...])
    for m in range(micro):
        send[m] = total[m * rows + half : (m + 1) * rows].astype(LOW)
        keep[m] = total[m * rows : m * rows + half]
    total = dot(every(hids), w_down[...])
    for m in range(micro):
        out_send[m] = total[m * rows + half : (m + 1) * rows].astype(LOW)
        out_keep[m] = total[m * rows : m * rows + half]


def pick(ref, lead):
    return ref if lead is None else ref.at[lead]


def block_body(terms, lefts, rights, extra, from_side, turned, ids, *refs):
    left, refs = refs[:lefts], refs[lefts:]
    right, refs = refs[:rights], refs[rights:]
    added, out = refs[: extra + from_side], refs[-1]
    total = None
    for a, a_lead, b, b_lead, first, count in terms:
        rows = pick(right[b], b_lead)[first : first + count, :]
        term = inner_rows(pick(left[a], a_lead)[ids[0]], rows)
        total = term if total is None else total + term
    for i, ref in enumerate(added):
        total = total + (ref[ids[0]] if i >= extra else ref[...]).astype(F32)
    out[...] = jnp.transpose(total) if turned else total.astype(out.dtype)


def side_sum_body(terms, lefts, ids, *refs):
    left, right, out = refs[:lefts], refs[lefts:-1], refs[-1]
    for z in range(out.shape[0]):
        total = None
        for a, a_lead, b, b_lead, first, count in terms:
            rows = pick(right[b], b_lead)[first : first + count, :]
            term = inner_rows(pick(left[a], a_lead)[z], rows)
            total = term if total is None else total + term
        out[z] = total.astype(out.dtype)


def attend_back_body(
    scale, micro, chunk, ids, a0, a1, a2, out_proj, q_up, key_ids, *refs
):
    per = 7
    groups = [refs[m * per : (m + 1) * per] for m in range(micro)]
    dyl_out, dqp, send, keep, kv_send, kv_keep = refs[micro * per : micro * per + 6]
    dq_acc, do_acc, delta_acc = refs[-3:]
    sides = refs[micro * per + 6 : -3]
    for m in range(micro):
        q, kv, o, lse, row_ids, cos, sin = groups[m]
        heads, rows, wide = q.shape
        half_rows = rows // 2
        dyl = jnp.concatenate([a0[m], a1[m], a2[m]], 0)
        dyl_out[m] = dyl
        if sides:
            side_columns(dyl_out.at[m], sides[0].at[m], sides[1].at[m], ids[1])
        for h in range(heads):
            do = inner_cols(dyl, out_proj[h * wide : (h + 1) * wide, :]).astype(LOW)
            do_acc[h] = do
            delta = jnp.sum(
                do.astype(F32) * o[:, h * wide : (h + 1) * wide].astype(F32), axis=-1, keepdims=True
            )
            delta_acc[h] = jnp.transpose(jnp.broadcast_to(delta, (rows, 128)))[:8]
            dq_acc[h] = jnp.zeros((rows, wide), F32)
        count = kv.shape[0] // 2 // chunk
        for part, out in ((0, kv_keep), (1, kv_send)):

            def one(i, carry):
                base = pl.multiple_of((part * count + i) * chunk, chunk)
                keys = kv[pl.ds(base, chunk), :wide]
                values = kv[pl.ds(base, chunk), wide:]
                at = key_ids[pl.ds(base, chunk), :]
                bias = jnp.where((at >= row_ids[1:2, :]) & (at <= row_ids[0:1, :]), 0.0, NEG_LARGE)

                def head(h, sums):
                    dk, dv = sums
                    q_h, do_h = q[h], do_acc[h]
                    probs = jnp.exp(inner_cols(keys, q_h) + bias - lse[pl.ds(h, 1), :])
                    back = inner_cols(values, do_h) - delta_acc[h][:1]
                    ds = (probs * back).astype(LOW)
                    dv = dv + dot(probs.astype(LOW), do_h)
                    dk = dk + dot(ds, q_h)
                    dq_acc[h] = dq_acc[h] + inner_rows(ds, keys)
                    return dk, dv

                zero = jnp.zeros((chunk, wide), F32)
                dk, dv = lax.fori_loop(0, heads, head, (zero, zero))
                place = pl.ds(pl.multiple_of(i * chunk, chunk), chunk)
                out[m, place, :wide] = dk.astype(out.dtype)
                out[m, place, wide:] = dv.astype(out.dtype)
                return carry

            if count == 1:
                one(0, 0)
            else:
                lax.fori_loop(0, count, one, 0)
        for h in range(heads):
            dq = unrotate(dq_acc[h] * scale, cos[...], sin[...])
            dqp[m, :, h * wide : (h + 1) * wide] = dq.astype(LOW)
        low = dqp[m]
        send[m] = inner_cols(low[half_rows:], q_up[...]).astype(LOW)
        keep[m] = inner_cols(low[:half_rows], q_up[...])


def natural_body(micro, quarter, ids, a0, a1, a2, out):
    for m in range(micro):
        pieces = (a0[m], a1[m], a2[m, :quarter, :], a2[m, quarter:, :])
        for k, piece in zip(ORDER, pieces):
            out[m, pl.ds(pl.multiple_of((ids[0] ^ k) * quarter, quarter), quarter), :] = piece


class Wire:
    def __init__(self, sends, recvs):
        self.sends, self.recvs, self.used = sends, recvs, 0
        self.seq, self.mp = lax.axis_index("seq"), lax.axis_index("mp")
        self.place, self.side = self.seq // 2, self.seq % 2
        core, cross = self.mp % 2, self.mp // 2
        self.blocks = (
            self.mp, 2 * (1 - cross) + core, 2 * cross + 1 - core, 2 * (1 - cross) + 1 - core
        )
        self.core, self.cross = {"mp": self.blocks[2]}, {"mp": self.blocks[1]}
        self.beside = {"seq": self.seq + 1 - 2 * self.side}
        self.up, self.down = {"seq": self.seq + 2}, {"seq": self.seq - 2}

    def copy(self, source, target, device):
        at = self.used
        self.used += 1
        return pltpu.make_async_remote_copy(
            src_ref=source, dst_ref=target, send_sem=self.sends.at[at], recv_sem=self.recvs.at[at],
            device_id=device, device_id_type=pl.DeviceIdType.MESH,
        )

    def send(self, source, target, device):
        made = self.copy(source, target, device)
        made.start()
        return made

    def greet(self, line, far=1, diagonal=False):
        barrier = pltpu.get_barrier_semaphore()
        devices = [self.core, self.cross, self.beside]
        if diagonal:
            devices.append({"mp": self.blocks[3]})
        for device in devices:
            pl.semaphore_signal(barrier, 1, device_id=device, device_id_type=pl.DeviceIdType.MESH)
        for d in range(1, far + 1):
            for way, there in ((1, self.place < line - d), (-1, self.place >= d)):

                @pl.when(there)
                def _():
                    pl.semaphore_signal(
                        barrier, 1, device_id={"seq": self.seq + 2 * way * d},
                        device_id_type=pl.DeviceIdType.MESH,
                    )
        below, above = jnp.minimum(self.place, far), jnp.minimum(line - 1 - self.place, far)
        pl.semaphore_wait(barrier, len(devices) + below + above)


def along(pieces, axis):
    return pieces[0] if len(pieces) == 1 else jnp.concatenate(pieces, axis)


def pair_places(first, second, quarter, axis):
    shape = (2 * quarter, 1) if axis == 0 else (1, 2 * quarter)
    index = lax.broadcasted_iota(jnp.int32, shape, axis)
    return jnp.where(index < quarter, first * quarter + index, (second - 1) * quarter + index)


def row_places(wire, quarter, axis):
    b = wire.blocks
    pieces = [pair_places(b[i], b[i + 1], quarter, axis) for i in (0, 2)]
    return wire.seq * (4 * quarter) + along(pieces, axis)


def key_places(wire, quarter, line, axis, cores):
    pieces = []
    for core in cores:
        for side in (wire.side, 1 - wire.side):
            for d in range(line):
                base = ((wire.place - d) * 2 + side) * (4 * quarter)
                b = wire.blocks[2 * core : 2 * core + 2]
                pieces.append(base + pair_places(b[0], b[1], quarter, axis))
    return along(pieces, axis)


def sequence_starts(lengths, m, places):
    first_end = lengths[m, 0]
    second_end = first_end + lengths[m, 1]
    return jnp.where(
        places >= second_end, second_end, jnp.where(places >= first_end, first_end, 0)
    )


class LineSum:
    def __init__(self, wire, term, room, rows, columns, keep):
        got, out = room
        view = lambda ref, i: ref.at[i, :rows, :columns]
        self.place, self.term, self.keep = wire.place, term, keep
        self.got = [view(got, i) for i in range(5)]
        self.out = [view(out, i) for i in range(2)]
        one, two_up, two_down, three_up, three_down = self.got
        a, b = self.out
        self.one = wire.copy(a, one, wire.up), wire.copy(a, one, wire.down)
        self.two = wire.copy(b, two_up, wire.up), wire.copy(b, two_down, wire.down)
        self.three = wire.copy(a, three_up, wire.up), wire.copy(b, three_down, wire.down)

    def clear(self):
        place = self.place
        for ref, empty in zip(
            self.got, ((place == 0) | (place == 3),) * 3 + (place == 0, place == 3)
        ):

            @pl.when(empty)
            def _(ref=ref):
                ref[...] = jnp.zeros(ref.shape, ref.dtype)

    def step1(self):
        place = self.place

        @pl.when((place == 0) | (place == 3))
        def _():
            self.out[0][...] = self.term(3 - place).astype(LOW)

        pl.when(place == 0)(self.one[0].start)
        pl.when(place == 3)(self.one[1].start)

    def step2(self):
        place = self.place
        pl.when(place == 1)(self.one[0].wait_recv)
        pl.when(place == 2)(self.one[1].wait_recv)
        self.out[1][...] = (
            self.term((place + 2) % 4) + self.got[0][...].astype(F32)
        ).astype(LOW)
        pl.when(place <= 1)(self.two[0].start)
        pl.when(place >= 2)(self.two[1].start)

    def step3(self):
        place = self.place

        @pl.when((place == 1) | (place == 2))
        def _():
            self.two[0].wait_recv()
            self.two[1].wait_recv()

        pl.when(place == 0)(self.one[0].wait_send)
        pl.when(place == 3)(self.one[1].wait_send)

        @pl.when(place <= 2)
        def _():
            self.out[0][...] = (self.term(place + 1) + self.got[1][...].astype(F32)).astype(LOW)
            self.three[0].start()

        pl.when(place <= 1)(self.two[0].wait_send)
        pl.when(place >= 2)(self.two[1].wait_send)

        @pl.when(place >= 1)
        def _():
            self.out[1][...] = (self.term(place - 1) + self.got[2][...].astype(F32)).astype(LOW)
            self.three[1].start()

    def finish(self):
        place = self.place
        pl.when(place >= 1)(self.three[0].wait_recv)
        pl.when(place <= 2)(self.three[1].wait_recv)
        self.keep(
            self.term(place) + self.got[3][...].astype(F32) + self.got[4][...].astype(F32)
        )

    def settle(self):
        place = self.place
        pl.when(place <= 2)(self.three[0].wait_send)
        pl.when(place >= 1)(self.three[1].wait_send)


SPACES = (pl.ANY, pltpu.VMEM, pltpu.SMEM)


def mesh_run(body, args, outs, scratch, number, name, limit, sends):
    return pl.pallas_call(
        body,
        in_specs=[pl.BlockSpec(memory_space=SPACES[kind]) for kind, _ in args],
        out_specs=[pl.BlockSpec(memory_space=SPACES[kind]) for kind, _ in outs],
        out_shape=[shape for _, shape in outs],
        scratch_shapes=[
            *scratch, pltpu.SemaphoreType.DMA((sends,)), pltpu.SemaphoreType.DMA((sends,))
        ],
        cost_estimate=pl.CostEstimate(flops=1000, bytes_accessed=1000, transcendentals=0),
        compiler_params=pltpu.CompilerParams(
            collective_id=number, has_side_effects=True, vmem_limit_bytes=limit << 20
        ),
        name=name,
    )(*[array for _, array in args])


def attend_back_one(
    scale, keys_at, rows_at, starts, dyl, out_proj, q_up, q, kv, o, lse, cos, sin,
    dqp, send, keep, kv_send, kv_keep, dq_acc, between=None,
):
    heads, rows, wide = q.shape
    half_rows = rows // 2
    low = dyl[...]
    grads, deltas = [], []
    for h in range(heads):
        columns = slice(h * wide, (h + 1) * wide)
        do = inner_cols(low, out_proj[columns, :]).astype(LOW)
        grads.append(do)
        delta = jnp.sum(do.astype(F32) * o[:, columns].astype(F32), axis=-1, keepdims=True)
        deltas.append(jnp.transpose(jnp.broadcast_to(delta, (rows, 128)))[:1])
    do_all, delta_all = jnp.concatenate(grads, 0), jnp.concatenate(deltas, 1)
    q_all = q[...].reshape(heads * rows, wide)
    lse_all = jnp.concatenate([lse[h : h + 1, :] for h in range(heads)], 1)
    dq_acc[...] = jnp.zeros(dq_acc.shape, F32)
    count = kv.shape[0] // 2
    chunk = min(256, count)
    for part, out in ((1, kv_send), (0, kv_keep)):
        for first in range(0, count, chunk):
            span = slice(part * count + first, part * count + first + chunk)
            keys, values = kv[span, :wide], kv[span, wide:]
            at = keys_at[part][first : first + chunk]
            bias = jnp.where((at >= starts) & (at <= rows_at), 0.0, NEG_LARGE)
            scores = inner_cols(keys, q_all) + jnp.concatenate([bias] * heads, 1)
            probs = jnp.exp(scores - lse_all)
            ds = (probs * (inner_cols(values, do_all) - delta_all)).astype(LOW)
            spot = slice(first, first + chunk)
            out[spot, :wide] = dot(ds, q_all).astype(out.dtype)
            out[spot, wide:] = dot(probs.astype(LOW), do_all).astype(out.dtype)
            dq_acc[...] += inner_rows(ds, keys)
        if part and between is not None:
            between()
    for h in range(heads):
        dq = unrotate(dq_acc[h * rows : (h + 1) * rows, :] * scale, cos, sin)
        dqp[:, h * wide : (h + 1) * wide] = dq.astype(LOW)
    total = inner_cols(dqp[...], q_up[...])
    send[...] = total[half_rows:].astype(LOW)
    keep[...] = total[:half_rows]


def mean_of(values):
    return jnp.mean(values, axis=-1, keepdims=True)


def terms_sum(pairs):
    total = None
    for left, right in pairs:
        term = inner_rows(left, right)
        total = term if total is None else total + term
    return total


def back1_body(quarter, *refs):
    refs = list(refs)
    take = lambda n: [refs.pop(0) for _ in range(n)]
    w_gate, w_up, w_down, h2, dhid, n2, inv2, dz, gain2, dz_mine, dz_got, dz_far, y = take(13)
    grad, dy, gain_sum, dyl, dyl_mine, dyl_theirs, layer_out = take(7)
    hid, dg, du, h2_mine = (take(2) for _ in range(4))
    h2_got, h2_far, dg_other = take(2), take(2), take(2)
    gate_w, up_w, hid_other0, hid_other1, h2_theirs, got, out = take(7)
    send, kept, core_got, cross_out, cross_got, loads = take(6)
    ffn_send, ffn_kept, ffn_got, ffn_out, ffn_back = take(5)
    wire = Wire(*take(2))
    half, rows = 2 * quarter, 4 * quarter
    in_gate = pltpu.make_async_copy(w_gate, gate_w, loads.at[0])
    in_up = pltpu.make_async_copy(w_up, up_w, loads.at[1])
    in_gate.start()
    in_up.start()
    hid_other = (hid_other0, hid_other1)
    hid_all = (*hid, *hid_other)

    def term(z):
        return terms_sum(halves_terms(
            [dz_mine[m, z] for m in range(2)], [dz_got[m, z] for m in range(2)],
            [dz_far[m, z] for m in range(2)], hid_all, half))

    def keep(total):
        grad[...] = jnp.transpose(total)

    chain = LineSum(wire, term, (got, out), grad.shape[1], grad.shape[0], keep)
    chain.clear()
    wire.greet(4)
    y_hid = []
    for m in range(2):
        low = h2[m]
        if m == 0:
            in_gate.wait()
        g = dot(low, gate_w[...])
        if m == 0:
            in_up.wait()
        u = dot(low, up_w[...])
        sig = jax.nn.sigmoid(g)
        swish = g * sig
        hid[m][...] = (swish * u).astype(LOW)
        y_hid.append(wire.send(hid[m], hid_other[m], wire.beside))
        back = dhid[m]
        dg[m][...] = (back * u * sig * (1.0 + g * (1.0 - sig))).astype(LOW)
        du[m][...] = (back * swish).astype(LOW)
    both = lambda pair: jnp.concatenate([pair[0][...], pair[1][...]], 0)
    total = inner_cols(both(dg), gate_w[...]) + inner_cols(both(du), up_w[...])
    for m in range(2):
        send[m] = total[m * rows + half : (m + 1) * rows].astype(LOW)
        kept[m] = total[m * rows : m * rows + half]
    sums = RowSum(wire, send, kept, core_got, cross_out, cross_got, quarter)
    sums.core.start()
    wide = gate_w.shape[1]
    rest = w_down.shape[1] - wide
    downs = [gate_w.at[:wide, :], up_w.at[:wide, :rest]]
    in_down = [
        pltpu.make_async_copy(w_down.at[:, :wide], downs[0], loads.at[0]),
        pltpu.make_async_copy(w_down.at[:, wide:], downs[1], loads.at[1]),
    ]
    for made in in_down:
        made.start()
    for m in range(2):
        side_columns(h2.at[m], h2_mine[m], h2_theirs.at[m], wire.side)
    sums.pass_on()
    for made in in_down:
        made.wait()
    low = both(hid)
    ffn_sum = RowSum(wire, ffn_send, ffn_kept, ffn_got, ffn_out, ffn_back, quarter)
    for columns, part in ((slice(0, wide), downs[0]), (slice(wide, None), downs[1])):
        total = dot(low, part[...])
        for m in range(2):
            ffn_send[m, :, columns] = total[m * rows + half : (m + 1) * rows].astype(LOW)
            ffn_kept[m, :, columns] = total[m * rows : m * rows + half]
    ffn_sum.core.start()
    for made in y_hid:
        made.wait_recv()
    y_next = [wire.send(h2_theirs.at[m], h2_got[m], wire.beside) for m in range(2)]
    y_next += [wire.send(dg[m], dg_other[m], wire.beside) for m in range(2)]
    chain.step1()
    ffn_sum.pass_on()
    dh2 = sums.result()
    gain_sum[...] = jnp.sum(jnp.sum(dh2 * n2[...], axis=0), axis=0, keepdims=True)
    back = dh2 * gain2[...]
    grad_y = dz[:, :quarter, :].astype(F32) + inv2[...] * (
        back - n2[...] * mean_of(back * n2[...])
    )
    dy[...] = grad_y
    dyl[:, :quarter, :] = grad_y.astype(LOW)
    cross_dyl = wire.send(dyl.at[:, :quarter, :], dyl.at[:, quarter:half, :], wire.cross)
    chain.step2()
    cross_dyl.wait_recv()
    core_dyl = wire.send(dyl.at[:, :half, :], dyl.at[:, half:, :], wire.core)
    share = Share(wire, layer_out, quarter)
    share.begin((y[...] + ffn_sum.result()).astype(LOW))
    core_h2 = []
    for i in range(2):
        y_next[i].wait_recv()
        core_h2.append(wire.send(h2_got[i], h2_far[i], wire.core))
    core_dyl.wait_recv()
    for m in range(2):
        side_columns(dyl.at[m], dyl_mine.at[m], dyl_theirs.at[m], wire.side)
    chain.step3()
    for made in y_next[2:] + core_h2:
        made.wait_recv()
    share.forward()
    chain.finish()
    for made in [*y_hid, cross_dyl, core_dyl, *y_next, *core_h2]:
        made.wait_send()
    share.end()
    sums.end()
    ffn_sum.end()
    chain.settle()


class Share:
    def __init__(self, wire, out, quarter):
        spot = lambda block: out.at[:, pl.ds(pl.multiple_of(block * quarter, quarter), quarter), :]
        own, near = spot(wire.blocks[0]), spot(wire.blocks[1])
        self.own = own
        self.first = wire.copy(own, own, wire.cross)
        self.rest = wire.copy(own, own, wire.core), wire.copy(near, near, wire.core)

    def begin(self, value):
        self.own[...] = value
        self.first.start()
        self.rest[0].start()

    def forward(self):
        self.first.wait_recv()
        self.rest[1].start()

    def end(self):
        for made in self.rest:
            made.wait_recv()
        for made in (self.first, *self.rest):
            made.wait_send()


class RowSum:
    def __init__(self, wire, send, kept, got, cross_out, cross_got, quarter):
        self.kept, self.got, self.quarter = kept, got, quarter
        self.out, self.back = cross_out, cross_got
        self.core = wire.copy(send, got, wire.core)
        self.cross = wire.copy(cross_out, cross_got, wire.cross)

    def pass_on(self):
        self.core.wait_recv()
        rest = slice(self.quarter, None)
        self.out[...] = (self.kept[:, rest, :] + self.got[:, rest, :].astype(F32)).astype(LOW)
        self.cross.start()

    def result(self):
        self.cross.wait_recv()
        own = slice(0, self.quarter)
        return (
            self.kept[:, own, :] + self.got[:, own, :].astype(F32) + self.back[...].astype(F32)
        )

    def end(self):
        self.core.wait_send()
        self.cross.wait_send()


def halves_terms(mine, got, far, rights, half):
    pairs = [(mine[m], rights[m][...]) for m in range(2)]
    for m in range(2):
        pairs.append((got[m], rights[2 + m][:half, :]))
        pairs.append((far[m], rights[2 + m][half:, :]))
    return pairs


def back2_body(quarter, scale, *refs):
    refs = list(refs)
    take = lambda n: [refs.pop(0) for _ in range(n)]
    (lengths,) = take(1)
    dg, dg_other, du, h2_mine, h2_got, h2_far = (take(2) for _ in range(6))
    dyl, out_proj, q_up = take(3)
    q, kv, o, lse = (take(2) for _ in range(4))
    cos, sin, chat, inv_c, gain_c, dyl_theirs = take(6)
    qn_theirs = take(2)
    grad_gate, grad_up, dfirst, gain_sum, dqp, dyl_got, dyl_far, qup_side = take(8)
    du_other = take(2)
    got_a, out_a, got_b, out_b = take(4)
    dq_acc, dqn_send, dqn_keep, kv_send, kv_keep = take(5)
    dqn_got, dqn_out, dqn_back = take(3)
    kv_got, kv_out, kv_back, side_out, side_got, line_out, line_got, kv_own = take(8)
    both, side_sums = take(2)
    wire = Wire(*take(2))
    half, rows = 2 * quarter, 4 * quarter
    wide = kv_own.shape[2] // 2
    rank = chat.shape[2]
    place = wire.place

    y_du = [wire.copy(du[m], du_other[m], wire.beside) for m in range(2)]

    def chain(rights, grad, room):
        def term(z):
            return terms_sum(halves_terms(
                [a[z] for a in h2_mine], [a[z] for a in h2_got], [a[z] for a in h2_far], rights,
                half))

        def keep(total):
            grad[...] = total

        made = LineSum(wire, term, room, *grad.shape, keep)
        made.clear()
        return made

    gate = chain((*dg, *dg_other), grad_gate, (got_a, out_a))
    up = chain((*du, *du_other), grad_up, (got_b, out_b))
    dqn_sum, core_kv, cross_kv, side_kv, line_kv = [], [], [], [], []
    for m in range(2):
        one = lambda ref: ref.at[m : m + 1]
        dqn_sum.append(RowSum(wire, one(dqn_send), one(dqn_keep), one(dqn_got), one(dqn_out),
                              one(dqn_back), quarter))
        core_kv.append(wire.copy(kv_send.at[m], kv_got.at[m], wire.core))
        cross_kv.append(wire.copy(kv_out.at[m], kv_back.at[m], wire.cross))
        side_kv.append(wire.copy(side_out.at[m], side_got.at[m], wire.beside))
        line_kv.append([
            wire.copy(line_out.at[m, d - 1], line_got.at[m, d - 1], {"seq": wire.seq - 2 * d})
            for d in range(1, 4)
        ])
        for d in range(1, 4):

            @pl.when(place > 3 - d)
            def _(m=m, d=d):
                line_got[m, d - 1] = jnp.zeros(line_got.shape[2:], LOW)

    wire.greet(4, 3)
    for made in y_du:
        made.start()
    gate.step1()

    def attend(m, between=None):
        rows_at = row_places(wire, quarter, 1)
        attend_back_one(
            scale, [key_places(wire, quarter, 4, 0, (core,)) for core in range(2)], rows_at,
            sequence_starts(lengths, m, rows_at), dyl.at[m], out_proj, q_up, q[m], kv[m], o[m],
            lse[m], cos[m], sin[m], dqp.at[m], dqn_send.at[m], dqn_keep.at[m], kv_send.at[m],
            kv_keep.at[m], dq_acc, between,
        )
        core_kv[m].start()
        dqn_sum[m].core.start()

    split = lambda ref, m: ref[m].reshape(8, 2, quarter, 2 * wide)

    def kv_cross(m):
        dqn_sum[m].pass_on()
        core_kv[m].wait_recv()
        kv_out[m] = (
            split(kv_keep, m)[:, 1].astype(F32) + split(kv_got, m)[:, 1].astype(F32)
        ).astype(LOW)
        cross_kv[m].start()

    def kv_sum(m, span):
        return (
            split(kv_keep, m)[span, 0].astype(F32) + split(kv_got, m)[span, 0].astype(F32)
            + kv_back[m, span].astype(F32)
        )

    def kv_side(m):
        cross_kv[m].wait_recv()
        side_out[m] = kv_sum(m, slice(4, 8)).astype(LOW)
        side_kv[m].start()

    def kv_line(m):
        side_kv[m].wait_recv()
        own = kv_sum(m, slice(0, 4)) + side_got[m].astype(F32)
        kv_own[m] = own[0]
        for d in range(1, 4):
            line_out[m, d - 1] = own[d].astype(LOW)
            pl.when(place >= d)(line_kv[m][d - 1].start)

    def latent(m):
        dqn = dqn_sum[m].result()[0]
        gain = jnp.sum(dqn * chat[m], axis=0, keepdims=True)
        gain_sum[...] = gain if m == 0 else gain_sum[...] + gain
        back = dqn * gain_c[...]
        both[m, :quarter, :rank] = (
            inv_c[m] * (back - chat[m] * mean_of(back * chat[m]))
        ).astype(LOW)

    def start_up():
        for made in y_du:
            made.wait_recv()
        up.step1()

    attend(0)
    kv_cross(0)
    gate.step2()
    attend(1, start_up)
    gate.step3()
    kv_cross(1)
    kv_side(0)
    latent(0)
    up.step2()
    latent(1)
    for z in range(4):
        side_sums[z] = terms_sum([(qn_theirs[m][z], dqp[m]) for m in range(2)]).astype(LOW)
    kv_side(1)
    side_dyl = wire.send(dyl_theirs, dyl_got, wire.beside)
    side_qup = wire.send(side_sums, qup_side, wire.beside)
    kv_line(0)
    kv_line(1)
    gate.finish()
    for m in range(2):
        for d in range(1, 4):
            pl.when(place <= 3 - d)(line_kv[m][d - 1].wait_recv)
        total = kv_own[m]
        for d in range(1, 4):
            total = total + line_got[m, d - 1].astype(F32)
        both[m, :quarter, rank : rank + wide] = unrotate(
            total[:, :wide], cos[m, :quarter], sin[m, :quarter]
        ).astype(LOW)
        both[m, :quarter, rank + wide :] = total[:, wide:].astype(LOW)
    cross_both = wire.send(both.at[:, :quarter, :], both.at[:, quarter:half, :], wire.cross)
    up.step3()
    cross_both.wait_recv()
    core_both = wire.send(both.at[:, :half, :], both.at[:, half:, :], wire.core)
    side_dyl.wait_recv()
    core_dyl = wire.send(dyl_got, dyl_far, wire.core)
    core_both.wait_recv()
    part = rank // 4
    kv_part = wide // 2
    dfirst[:, :, :part] = both[:, :, pl.ds(pl.multiple_of(wire.mp * part, part), part)]
    dfirst[:, :, part:] = both[
        :, :, pl.ds(pl.multiple_of(rank + wire.mp * kv_part, kv_part), kv_part)
    ]
    up.finish()
    core_dyl.wait_recv()
    side_qup.wait_recv()
    for made in [*y_du, *core_kv, *cross_kv, *side_kv, cross_both, core_both, side_dyl, core_dyl,
                 side_qup]:
        made.wait_send()
    for m in range(2):
        dqn_sum[m].end()
        for d in range(1, 4):
            pl.when(place >= d)(line_kv[m][d - 1].wait_send)
    gate.settle()
    up.settle()


def back3_body(quarter, *refs):
    refs = list(refs)
    take = lambda n: [refs.pop(0) for _ in range(n)]
    dfirst, weights = take(2)
    h1_mine, h1_theirs, o, oo = (take(2) for _ in range(4))
    dyl_mine, dyl_got, dyl_far = take(3)
    qn_mine = take(2)
    dqp, qup_side, n1, inv1, dy, gain1, gain2_sum, gain_c_sum = take(8)
    grad_out, grad_qup, grad_qdown, grad_kv, grad_tokens, gains = take(6)
    got_a, out_a, got_b, out_b, got_c, out_c = take(6)
    side_sums, side_got = take(2)
    send, kept, row_got, row_out, row_back = take(5)
    kv_out, kv_got = take(2)
    sums, sums_core, sums_cross, sums_side, sums_line = take(5)
    wire = Wire(*take(2))
    half, rows = 2 * quarter, 4 * quarter
    place = wire.place
    wire.greet(4, 3, diagonal=True)

    for z in range(4):
        side_sums[z] = terms_sum([(h1_theirs[m][z], dfirst[m]) for m in range(2)]).astype(LOW)
    side_first = wire.send(side_sums, side_got, wire.beside)

    def out_term(z):
        return terms_sum(halves_terms(
            [dyl_mine[m, z] for m in range(2)], [dyl_got[m, z] for m in range(2)],
            [dyl_far[m, z] for m in range(2)], (*o, *oo), half))

    def qup_term(z):
        return terms_sum([(qn_mine[m][z], dqp[m]) for m in range(2)]) + qup_side[z].astype(F32)

    def first_term(z):
        return terms_sum([(h1_mine[m][z], dfirst[m]) for m in range(2)]) + side_got[z].astype(F32)

    def keep_out(total):
        grad_out[...] = jnp.transpose(total)

    def keep_qup(total):
        grad_qup[...] = total

    part = grad_qdown.shape[1]

    def keep_first(total):
        grad_qdown[...] = total[:, :part]
        kv_out[...] = total[:, part:]

    out = LineSum(wire, out_term, (got_a, out_a), *grad_out.shape[::-1], keep_out)
    qup = LineSum(wire, qup_term, (got_b, out_b), *grad_qup.shape, keep_qup)
    first = LineSum(wire, first_term, (got_c, out_c), kv_out.shape[0], dfirst.shape[2], keep_first)
    for chain in (out, qup, first):
        chain.clear()
    row_sum = RowSum(wire, send, kept, row_got, row_out, row_back, quarter)
    out.step1()
    term = inner_cols(dfirst[...].reshape(2 * rows, dfirst.shape[2]), weights[...])
    for m in range(2):
        send[m] = term[m * rows + half : (m + 1) * rows].astype(LOW)
        kept[m] = term[m * rows : m * rows + half]
    row_sum.core.start()
    qup.step1()
    row_sum.pass_on()
    out.step2()
    side_first.wait_recv()
    first.step1()
    qup.step2()
    dh1 = row_sum.result()
    gain1_sum = jnp.sum(jnp.sum(dh1 * n1[...], axis=0), axis=0, keepdims=True)
    back = dh1 * gain1[...]
    share = Share(wire, grad_tokens, quarter)
    share.begin(
        (dy[...] + inv1[...] * (back - n1[...] * mean_of(back * n1[...]))).astype(LOW)
    )
    w, r = gain1_sum.shape[1] // 8, gain_c_sum.shape[1] // 8
    for s in range(8):
        sums[s] = jnp.concatenate(
            [gain1_sum[:, s * w : (s + 1) * w], gain2_sum[:, s * w : (s + 1) * w],
             gain_c_sum[:, s * r : (s + 1) * r]], axis=1
        )
    core_sums = wire.send(sums, sums_core, wire.core)
    out.step3()
    core_sums.wait_recv()
    core_sums.wait_send()
    sums[...] = sums[...] + sums_core[...]
    cross_sums = wire.send(sums, sums_cross, wire.cross)
    qup.step3()
    first.step2()
    cross_sums.wait_recv()
    cross_sums.wait_send()
    sums[...] = sums[...] + sums_cross[...]
    side_of = lambda p, s: sums.at[2 * p + s]
    side_sends = [
        wire.send(side_of(p, 1 - wire.side), sums_side.at[p], wire.beside) for p in range(4)
    ]
    share.forward()
    first.step3()
    for made in side_sends:
        made.wait_recv()
        made.wait_send()
    line_sends = []
    for d in range(1, 4):
        for way, there in ((1, place + d <= 3), (-1, place - d >= 0)):
            index = 2 * (d - 1) + (way < 0)
            line_sends.append(
                (wire.copy(sums_line.at[6 + index], sums_line.at[index],
                           {"seq": wire.seq + 2 * way * d}), d, way, there)
            )

            @pl.when(there)
            def _(index=index, d=d, way=way):
                to = place + way * d
                sums_line[6 + index] = sums[2 * to + wire.side] + sums_side[to]
                line_sends[-1][0].start()

            @pl.when((place - way * d < 0) | (place - way * d > 3))
            def _(index=index):
                sums_line[index] = jnp.zeros(sums_line.shape[1:], F32)

    out.finish()
    qup.finish()
    first.finish()
    cores = []
    size = kv_out.shape[0] // 4
    for k in range(4):
        rows_of = pl.ds(pl.multiple_of(wire.blocks[k] * size, size), size)
        if k:
            device = {"mp": wire.blocks[k]}
            cores.append(wire.send(kv_out.at[rows_of], kv_got.at[k], device))
        else:
            kv_got[0] = kv_out[rows_of]
    total = sums[2 * place + wire.side] + sums_side[place]
    for made, d, way, there in line_sends:
        pl.when((place - way * d >= 0) & (place - way * d <= 3))(made.wait_recv)
    for index in range(6):
        total = total + sums_line[index]
    gains[...] = total
    for made in cores:
        made.wait_recv()
    columns = kv_out.shape[1]
    for k in range(4):
        at = pl.ds(pl.multiple_of(wire.blocks[k] * columns, columns), columns)
        grad_kv[:, at] = kv_got[k]
    share.end()
    for made in (side_first, *cores):
        made.wait_send()
    for made, d, way, there in line_sends:
        pl.when(there)(made.wait_send)
    row_sum.end()
    for chain in (out, qup, first):
        chain.settle()


def attend_one(
    scale, mp_blocks, c, gain, q_up, cos, sin, kv, key_ids, row_ids, row_starts, out_proj,
    qn, q, o, lse, send, keep, chat_out, inverse_out,
):
    rows = qn.shape[0]
    half, quarter = rows // 2, rows // 4
    part = c.shape[2]
    wide = q.shape[2]
    cut = lambda k, i: c[k, i * quarter : (i + 1) * quarter, :]
    pieces = [jnp.concatenate([cut(k, i ^ k) for i in range(4)], 0) for k in range(4)]
    latent = jnp.concatenate(pieces, 1).astype(F32)
    inverse = inverse_rms(latent)
    chat = latent * inverse
    inverse_out[...] = inverse[:quarter]
    for k in range(4):
        columns = pl.ds(pl.multiple_of(mp_blocks[k] * part, part), part)
        chat_out[:, columns] = chat[:quarter, k * part : (k + 1) * part]
        qn[:, columns] = (chat[:, k * part : (k + 1) * part] * gain[:, columns]).astype(LOW)
    bias = jnp.where((key_ids >= row_starts) & (key_ids <= row_ids), 0.0, NEG_LARGE)
    low = qn[...]
    for h in range(q.shape[0]):
        pre = dot(low, q_up[:, h * wide : (h + 1) * wide])
        q_h = (rotate(pre, cos, sin) * scale).astype(LOW)
        q[h] = q_h
        scores = inner_cols(q_h, kv[:, :wide]) + bias
        top = jnp.max(scores, axis=-1, keepdims=True)
        probs = jnp.exp(scores - top)
        total = jnp.sum(probs, axis=-1, keepdims=True)
        out = dot(probs.astype(LOW), kv[:, wide:]) / total
        o[:, h * wide : (h + 1) * wide] = out.astype(LOW)
        log_total = jnp.broadcast_to(top + jnp.log(total), (rows, 128))
        lse[h : h + 1, :] = jnp.transpose(log_total)[:1]
    keep[...] = dot(o[:half, :], out_proj[...])
    send[...] = dot(o[half:, :], out_proj[...]).astype(LOW)


def fore1_body(scale, *refs):
    refs = list(refs)
    take = lambda n: [refs.pop(0) for _ in range(n)]
    tokens, cotangent, q_down, kv_proj, q_up, out_proj, w_down = take(7)
    lengths, gain1, gain_c, gain2, cosine, sine = take(6)
    h1_mine, h1_theirs, qn_mine, qn_theirs = (take(2) for _ in range(4))
    qs, os, lses, kvs, oo, dz_got = (take(2) for _ in range(6))
    dz, dz_mine, dhid, chat, inv_c, y_out, n2_out, inv2_out, n1_out, inv1_out, h2 = take(11)
    x, down_w, kv_w, up_w, out_w, back_w, h1, c, qn, dz_theirs = take(10)
    send, kept, got, cross_out, cross_got = take(5)
    loads = take(1)[0]
    wire = Wire(*take(2))
    place, blocks = wire.place, wire.blocks
    rows = x.shape[1]
    half, quarter = rows // 2, rows // 4
    wide = kv_proj.shape[1] // 2

    started = []

    def load(source, target):
        made = pltpu.make_async_copy(source, target, loads.at[len(started)])
        made.start()
        started.append(made)
        return made

    def load_rows(source, target):
        return [
            load(source.at[pl.ds(pl.multiple_of(blocks[k] * quarter, quarter), quarter), :],
                 target.at[k * quarter : (k + 1) * quarter, :])
            for k in range(4)
        ]

    in_x = [load_rows(tokens.at[0], x.at[0])]
    in_kv = load(kv_proj, kv_w)
    in_x.append(load_rows(tokens.at[1], x.at[1]))
    in_down = load(q_down, down_w)
    in_dz = [load_rows(cotangent.at[m], dz.at[m]) for m in range(2)]
    in_back, in_up, in_out = load(w_down, back_w), load(q_up, up_w), load(out_proj, out_w)

    line_kv, side_kv, core_kv, cross_c, core_c = [], [], [], [], []
    for m in range(2):
        for d in range(1, 4):

            @pl.when(place < d)
            def _(m=m, d=d):
                kvs[m][0, :, d] = jnp.zeros(kvs[m].shape[1:2] + kvs[m].shape[3:], LOW)
                kvs[m][1, :, d] = jnp.zeros(kvs[m].shape[1:2] + kvs[m].shape[3:], LOW)

        own = kvs[m].at[0, 0, 0]
        line_kv.append([
            wire.copy(own, kvs[m].at[0, 0, d], {"seq": wire.seq + 2 * d}) for d in range(1, 4)
        ])
        side_kv.append([
            wire.copy(kvs[m].at[0, 0, d], kvs[m].at[0, 1, d], wire.beside) for d in range(4)
        ])
        core_kv.append([
            wire.copy(kvs[m].at[0, :, d], kvs[m].at[1, :, d], wire.core) for d in range(4)
        ])
        cross_c.append(wire.copy(c.at[m, 0], c.at[m, 1], wire.cross))
        core_c.append([
            wire.copy(c.at[m, 0], c.at[m, 2], wire.core),
            wire.copy(c.at[m, 1], c.at[m, 3], wire.core),
        ])
    wire.greet(4, 3)

    for m in range(2):
        cos, sin = cosine[m], sine[m]
        for made in in_x[m]:
            made.wait()
        if m == 0:
            in_kv.wait()
        values = x[m].astype(F32)
        inverse = inverse_rms(values)
        normed = values * inverse
        n1_out[m], inv1_out[m] = normed[:quarter], inverse[:quarter]
        low = (normed * gain1[...]).astype(LOW)
        h1[...] = low
        pair = dot(low[:half], kv_w[...])
        own = kvs[m].at[0, 0, 0]
        own[:, :wide] = rotate(pair[:, :wide], cos[:half], sin[:half]).astype(LOW)
        own[:, wide:] = pair[:, wide:].astype(LOW)
        for d in (3, 2, 1):
            pl.when(place + d <= 3)(line_kv[m][d - 1].start)
        side_kv[m][0].start()
        if m == 0:
            in_down.wait()
        c[m, 0] = dot(low, down_w[...]).astype(LOW)
        cross_c[m].start()
        core_c[m][0].start()
        side_columns(h1, h1_mine[m], h1_theirs[m], wire.side)

    def pass_kv(m, d):
        @pl.when(place >= d)
        def _():
            line_kv[m][d - 1].wait_recv()
            side_kv[m][d].start()

    def pass_core(m, d):
        @pl.when(place >= d)
        def _():
            side_kv[m][d].wait_recv()
            core_kv[m][d].start()

    in_back.wait()
    for m in range(2):
        for made in in_dz[m]:
            made.wait()
    dhid[0] = inner_cols(dz[0], back_w[...])
    for d in (1, 2, 3):
        pass_kv(0, d)
    pass_core(0, 0)
    for m in range(2):
        cross_c[m].wait_recv()
        core_c[m][1].start()
    dhid[1] = inner_cols(dz[1], back_w[...])
    for d in (1, 2, 3):
        pass_kv(1, d)
    for m in range(2):
        side_columns(dz.at[m], dz_mine.at[m], dz_theirs.at[m], wire.side)
    for d in (1, 2, 3):
        pass_core(0, d)
    in_up.wait()
    in_out.wait()
    sums = [
        RowSum(wire, send.at[m : m + 1], kept.at[m : m + 1], got.at[m : m + 1],
               cross_out.at[m : m + 1], cross_got.at[m : m + 1], quarter)
        for m in range(2)
    ]
    side_o, shares = [], []

    def after_sum(m):
        value = x[m, :quarter, :].astype(F32) + sums[m].result()[0]
        inverse = inverse_rms(value)
        normed = value * inverse
        y_out[m], n2_out[m], inv2_out[m] = value, normed, inverse
        h2[m, :quarter, :] = (normed * gain2[...]).astype(LOW)
        spot = lambda k: h2.at[m, k * quarter : (k + 1) * quarter, :]
        shares.append((
            wire.send(spot(0), spot(1), wire.cross), wire.send(spot(0), spot(2), wire.core),
            wire.copy(spot(1), spot(3), wire.core),
        ))

    for m in range(2):
        if m == 1:
            for d in range(4):
                pass_core(1, d)
        for d in range(4):
            pl.when(place >= d)(core_kv[m][d].wait_recv)
        for made in core_c[m]:
            made.wait_recv()
        rows_at = row_places(wire, quarter, 0)
        attend_one(
            scale, blocks, c.at[m], gain_c, up_w, cosine[m], sine[m],
            kvs[m][...].reshape(2 * 2 * 4 * half, 2 * wide),
            key_places(wire, quarter, 4, 1, (0, 1)), rows_at,
            sequence_starts(lengths, m, rows_at), out_w, qn, qs[m], os[m], lses[m], send.at[m], kept.at[m],
            chat.at[m], inv_c.at[m],
        )
        sums[m].core.start()
        if m == 0:
            side_dz = wire.send(dz_theirs, dz_got[0], wire.beside)
        side_o.append(wire.send(os[m], oo[m], wire.beside))
        side_columns(qn, qn_mine[m], qn_theirs[m], wire.side)
        if m == 1:
            after_sum(0)
        sums[m].pass_on()
    after_sum(1)
    side_dz.wait_recv()
    core_dz = wire.send(dz_got[0], dz_got[1], wire.core)
    for near, _, far in shares:
        near.wait_recv()
        far.start()
    for _, first, far in shares:
        first.wait_recv()
        far.wait_recv()
    core_dz.wait_recv()
    for made in side_o:
        made.wait_recv()
    for made in [side_dz, core_dz, *side_o, *cross_c, *(a for p in core_c for a in p),
                 *(a for p in shares for a in p)]:
        made.wait_send()
    for m in range(2):
        sums[m].end()
        for d in range(4):

            @pl.when(place >= d)
            def _(m=m, d=d):
                side_kv[m][d].wait_send()
                core_kv[m][d].wait_send()

        for d in range(1, 4):
            pl.when(place + d <= 3)(line_kv[m][d - 1].wait_send)


def deliver_body(*refs):
    sems = refs[-1]
    count = sems.shape[0]
    gains, outs = refs[count], refs[count + 1 : -1]
    copies = [
        pltpu.make_async_copy(refs[i], outs[i], sems.at[i]) for i in range(count)
    ]
    for made in copies:
        made.start()
    at = 0
    for ref in outs[count:]:
        ref[...] = gains[0, at : at + ref.shape[0]]
        at += ref.shape[0]
    for made in copies:
        made.wait()


def local(
    tokens,
    lengths,
    norm1_gain,
    q_down,
    latent_gain,
    q_up,
    kv_proj,
    out_proj,
    norm2_gain,
    w_gate,
    w_up,
    w_down,
    cotangent,
):
    micro, rows, width = tokens.shape
    seq = lax.axis_size("seq")
    line = seq // 2
    at = lax.axis_index("seq").astype(jnp.int32)
    me = lax.axis_index("mp").astype(jnp.int32)
    place, side = at // 2, at % 2
    ids = jnp.stack([me, side])
    quarter, half = rows // 4, rows // 2
    head_dim = kv_proj.shape[1] // 2
    heads = q_up.shape[1] // head_dim
    part = q_down.shape[1]
    rank = q_up.shape[0]
    hidden = w_gate.shape[1]
    kv_part = kv_proj.shape[1] // 4
    wide = width // seq
    scale = head_dim ** (-0.5)
    key_count = seq * rows
    beside = [(i, i ^ 1) for i in range(seq)]
    narrow = line == 4 and micro == 2 and key_count <= 2048 and not wide % 128

    def swap(index):
        return ((index & 1) << 1) | (index >> 1)

    def to_natural(array, axis):
        size = array.shape[axis] // 4
        return jnp.concatenate(
            [lax.dynamic_slice_in_dim(array, swap(me ^ b) * size, size, axis) for b in range(4)],
            axis,
        )

    def other(array):
        return lax.ppermute(array, "seq", beside)

    def sum_mp(send, keep):
        kept = keep + lax.ppermute(send, "mp", CORE).astype(F32)
        got = lax.ppermute(kept[..., quarter:, :].astype(LOW), "mp", CROSS)
        return kept[..., :quarter, :] + got.astype(F32)

    def gather_mp(piece):
        near = lax.ppermute(piece, "mp", CROSS)
        pair = jnp.concatenate([piece, near], -2)
        return piece, near, lax.ppermute(pair, "mp", CORE)

    def sides_shape(columns, their_rows, lead=()):
        if columns // seq % 128:
            return []
        return [
            whole((*lead, line, n, columns // seq), LOW) for n in (rows, their_rows)
        ]

    def split_sides(made, full, their_rows):
        if made:
            return made
        split = full.reshape(*full.shape[:-1], line, 2, full.shape[-1] // seq)
        mine, theirs = (
            jnp.moveaxis(lax.dynamic_index_in_dim(split, i, split.ndim - 2, keepdims=False), -2, -3)
            for i in (side, 1 - side)
        )
        return mine, theirs[..., :their_rows, :]

    def from_other(theirs):
        got = other(theirs)
        return got, lax.ppermute(got, "mp", CORE)

    def without_sides(body, count):
        return body if count else lambda *refs: body(*refs, None, None)

    def both_sides(mine, got):
        lefts, spans = [], []
        for array, first, count, partner in (
            (mine, 0, rows, 0), (got[0], 0, half, 1), (got[1], half, half, 1)
        ):
            stacked_array = not isinstance(array, list)
            for m in range(micro):
                spans.append((len(lefts) if not stacked_array else len(lefts), m if stacked_array else None,
                              m, partner, first, count))
                if not stacked_array:
                    lefts.append(array[m])
            if stacked_array:
                lefts.append(array)
        return lefts, spans

    class Chain:
        def __init__(self, lefts, rights, terms, shape, turned=False, from_side=None):
            self.args = [*lefts, *rights]
            self.spec = (terms, len(lefts), len(rights))
            self.shape, self.turned = shape, turned
            self.from_side = [] if from_side is None else [from_side]
            self.step, self.up, self.down = 0, None, None

        def block(self, index, added, after, last=False):
            turned = last and self.turned
            body = functools.partial(
                block_body, *self.spec, len(added), len(self.from_side), turned
            )
            shape = self.shape[::-1] if turned else self.shape
            return run(
                body, index.reshape(1), [*self.args, *added, *self.from_side],
                [whole(shape, F32 if last else LOW)], after, name="block",
            )[0]

        def advance(self, after):
            self.step += 1
            step = self.step
            goes_up = [(i, i + 2) for i in range(2 * step)]
            goes_down = [(seq - 1 - i, seq - 3 - i) for i in range(2 * step)]
            for_up, for_down = line - step + place, step - line + place
            if 2 * step < line + 1:
                which = jnp.where(
                    place <= step - 1, for_up, jnp.where(place >= line - step, for_down, 0)
                )
                term = self.block(which, [a for a in (self.up, self.down) if a is not None], after)
                if step == 1 and line > 3:
                    self.up = lax.ppermute(term, "seq", goes_up + goes_down)
                else:
                    self.up = lax.ppermute(term, "seq", goes_up)
                    self.down = lax.ppermute(term, "seq", goes_down)
                return [term]
            term_up = self.block(jnp.clip(for_up, 0, line - 1), [self.up], after)
            term_down = self.block(jnp.clip(for_down, 0, line - 1), [self.down], [term_up])
            self.up = lax.ppermute(term_up, "seq", goes_up)
            self.down = lax.ppermute(term_down, "seq", goes_down)
            return [term_down]

        def finish(self, after):
            while self.step < line - 1:
                after = self.advance(after)
            result = self.block(place, [self.up, self.down], after, last=True)
            return result, [result]

    quarter_rows = jnp.arange(quarter, dtype=jnp.int32)
    row_ids = at * rows + jnp.concatenate([(me ^ k) * quarter + quarter_rows for k in ORDER])
    key_ids = (
        ((place - jnp.arange(line, dtype=jnp.int32)[None, None, :, None, None]) * 2
         + (side ^ jnp.arange(2, dtype=jnp.int32)[None, :, None, None, None])) * rows
        + (me ^ (jnp.arange(2, dtype=jnp.int32)[:, None, None, None, None]
                 + 2 * jnp.arange(2, dtype=jnp.int32)[None, None, None, :, None])) * quarter
        + quarter_rows[None, None, None, None, :]
    ).reshape(key_count)

    gain1_row, gain2_row, gain_c_row = norm1_gain[None, :], norm2_gain[None, :], latent_gain[None, :]
    kv_cols = lax.dynamic_slice_in_dim(kv_proj, me * kv_part, kv_part, 1)
    first_weights = jnp.concatenate([q_down, kv_cols], axis=1)
    low = lambda *shape: pltpu.VMEM(shape, LOW)
    full = lambda *shape: pltpu.VMEM(shape, F32)
    near = lambda *arrays: [(1, a) for a in arrays]
    far = lambda *arrays: [(0, a) for a in arrays]
    columns = heads * head_dim
    side_rows = rank // seq
    first_columns = part + kv_part

    def narrow_layer():
        numbers = lambda array: [(2, array)]
        ends = jnp.cumsum(lengths, axis=1)
        first_end, second_end = ends[:, 0:1], ends[:, 1:2]
        places = row_ids[None, :] - jnp.where(
            row_ids >= second_end, second_end, jnp.where(row_ids >= first_end, first_end, 0)
        )
        freqs = BASE ** (-2.0 * jnp.arange(head_dim // 2, dtype=F32) / head_dim)
        angles = places.astype(F32)[:, :, None] * freqs
        cosine, sine = jnp.cos(angles), jnp.sin(angles)
        row_shape = whole((micro, quarter, width), F32)
        one_shape = whole((micro, quarter, 1), F32)
        side_shape = whole((micro, line, half, wide), LOW)
        args = far(tokens, cotangent, q_down, kv_proj, q_up, out_proj, w_down)
        args += numbers(lengths) + near(gain1_row, gain_c_row, gain2_row, cosine, sine)
        outs = near(*[whole((line, rows, wide), LOW)] * 4, *[whole((line, rows, side_rows), LOW)] * 4)
        outs += near(*[whole((heads, rows, head_dim), LOW)] * 2, *[whole((rows, columns), LOW)] * 2)
        outs += near(*[whole((heads, rows), F32)] * 2)
        outs += near(*[whole((2, 2, line, half, 2 * head_dim), LOW)] * 2)
        outs += far(*[whole((rows, columns), LOW)] * 2, *[side_shape] * 2)
        outs += near(
            whole((micro, rows, width), LOW), whole((micro, line, rows, wide), LOW),
            whole((micro, rows, hidden), F32), whole((micro, quarter, rank), F32), one_shape,
            row_shape, row_shape, one_shape, row_shape, one_shape,
            whole((micro, rows, width), LOW),
        )
        made = list(mesh_run(
            functools.partial(fore1_body, scale), args, outs,
            [low(micro, rows, width), low(width, part), low(width, 2 * head_dim),
             low(rank, columns), low(columns, width), low(hidden, width), low(rows, width),
             low(micro, 4, rows, part), low(rows, rank), low(micro, line, half, wide),
             low(micro, half, width), full(micro, half, width), low(micro, half, width),
             low(micro, quarter, width), low(micro, quarter, width),
             pltpu.SemaphoreType.DMA((24,))],
            4, "fore1", 60, 60,
        ))
        give = lambda n: [made.pop(0) for _ in range(n)]
        h1_mine, h1_theirs, qn_mine, qn_theirs = (give(2) for _ in range(4))
        qs, os, lses, kv, o_other, dz_got = (give(2) for _ in range(6))
        kv = [a.reshape(key_count, 2 * head_dim) for a in kv]
        dz, dz_mine, dhid, chat, inv_c, y, n2, inv2, n1, inv1, h2 = give(11)

        args = far(w_gate, w_up, w_down) + near(h2, dhid, n2, inv2, dz, gain2_row, dz_mine)
        args += near(*dz_got, y)
        outs = near(
            whole((hidden, wide), F32), row_shape, whole((1, width), F32),
            whole((micro, rows, width), LOW), whole((micro, line, rows, wide), LOW), side_shape,
            whole((micro, rows, width), LOW), *[whole((rows, hidden), LOW)] * 6, *[whole((line, rows, wide), LOW)] * 2,
        ) + far(*[whole((line, half, wide), LOW)] * 4, *[whole((rows, hidden), LOW)] * 2)
        made = list(mesh_run(
            functools.partial(back1_body, quarter), args, outs,
            [low(width, hidden), low(width, hidden), low(rows, hidden), low(rows, hidden),
             low(micro, line, half, wide), low(5, wide, hidden), low(2, wide, hidden),
             low(micro, half, width), full(micro, half, width), low(micro, half, width),
             low(micro, quarter, width), low(micro, quarter, width),
             pltpu.SemaphoreType.DMA((2,)), low(micro, half, width), full(micro, half, width),
             low(micro, half, width), low(micro, quarter, width), low(micro, quarter, width)],
            1, "back1", 62, 30,
        ))
        grad_down, dy, gain2, dyl, dyl_mine, dyl_theirs, layer_out = give(7)
        hid, dg, du, h2_mine, h2_got, h2_far, dg_other = (give(2) for _ in range(7))

        args = numbers(lengths) + near(*dg, *dg_other, *du, *h2_mine, *h2_got, *h2_far)
        args += near(dyl, out_proj, q_up, *qs, *kv, *os, *lses, cosine, sine, chat, inv_c,
                     gain_c_row) + far(dyl_theirs) + near(*qn_theirs)
        outs = near(whole((wide, hidden), F32), whole((wide, hidden), F32),
                    whole((micro, rows, first_columns), LOW), whole((1, rank), F32),
                    whole((micro, rows, columns), LOW))
        outs += far(side_shape, side_shape, whole((line, side_rows, columns), LOW))
        kv_low = lambda *lead: low(*lead, quarter, 2 * head_dim)
        key_half = key_count // 2
        grad_gate, grad_up, dfirst, gain_c, dqp, dyl_got, dyl_far, qup_side = mesh_run(
            functools.partial(back2_body, quarter, scale), args, outs,
            [low(rows, hidden), low(rows, hidden), low(5, wide, hidden), low(2, wide, hidden),
             low(5, wide, hidden), low(2, wide, hidden), full(heads * rows, head_dim),
             low(micro, half, rank),
             full(micro, half, rank), low(micro, key_half, 2 * head_dim),
             low(micro, key_half, 2 * head_dim), low(micro, half, rank),
             low(micro, quarter, rank), low(micro, quarter, rank),
             low(micro, key_half, 2 * head_dim), kv_low(micro, 2 * line), kv_low(micro, 2 * line),
             kv_low(micro, line), kv_low(micro, line), kv_low(micro, 3), kv_low(micro, 3),
             full(micro, quarter, 2 * head_dim), low(micro, rows, rank + 2 * head_dim),
             low(line, side_rows, columns)],
            2, "back2", 62, 44,
        )

        kv_cols = lax.dynamic_slice_in_dim(kv_proj, me * kv_part, kv_part, 1)
        first_weights = jnp.concatenate([q_down, kv_cols], axis=1)
        args = near(dfirst, first_weights, *h1_mine, *h1_theirs, *os, *o_other, dyl_mine, dyl_got,
                    dyl_far, *qn_mine, dqp, qup_side, n1, inv1, dy, gain1_row, gain2, gain_c)
        block = width // 4 // seq
        gain_columns = 2 * wide + side_rows
        outs = near(whole((columns, wide), F32), whole((side_rows, columns), F32),
                    whole((wide, part), F32), whole((block, 2 * head_dim), F32),
                    whole((micro, rows, width), LOW), whole((1, gain_columns), F32))
        grad_out, grad_qup, grad_qdown, grad_kv, input_grads, gains = mesh_run(
            functools.partial(back3_body, quarter), args, outs,
            [low(5, wide, columns), low(2, wide, columns), low(5, side_rows, columns),
             low(2, side_rows, columns), low(5, wide, first_columns),
             low(2, wide, first_columns), low(line, wide, first_columns),
             low(line, wide, first_columns), low(micro, half, width), full(micro, half, width),
             low(micro, half, width), low(micro, quarter, width), low(micro, quarter, width),
             full(wide, kv_part), full(4, block, kv_part), full(seq, 1, gain_columns),
             full(seq, 1, gain_columns), full(seq, 1, gain_columns), full(line, 1, gain_columns),
             full(12, 1, gain_columns)],
            3, "back3", 60, 44,
        )
        results = [layer_out, input_grads, grad_qdown, grad_qup, grad_kv, grad_out, grad_gate,
                   grad_up, grad_down]
        made = pl.pallas_call(
            deliver_body,
            in_specs=[pl.BlockSpec(memory_space=pl.ANY)] * len(results) + [in_vmem()],
            out_specs=[pl.BlockSpec(memory_space=pl.ANY)] * len(results) + [in_vmem()] * 3,
            out_shape=[whole(a.shape, a.dtype) for a in results]
            + [whole((n,), F32) for n in (wide, wide, side_rows)],
            scratch_shapes=[pltpu.SemaphoreType.DMA((len(results),))],
            name="deliver",
        )(*results, gains)
        (layer_out, input_grads, grad_qdown, grad_qup, grad_kv, grad_out, grad_gate, grad_up,
         grad_down, grad_n1, grad_n2, grad_c) = made
        return (
            layer_out, input_grads, grad_n1, grad_qdown, grad_c, grad_qup, grad_kv, grad_out,
            grad_n2, grad_gate, grad_up, grad_down,
        )

    if narrow:
        return narrow_layer()

    both_rows = sides_shape(width, rows)
    half_rows = sides_shape(width, half)
    rank_sides = sides_shape(rank, rows)

    tables, starts, kv, c_part, h1_sides = [], [], [], [], []
    order = []
    for m in range(micro):
        _, places = documents(lengths[m], row_ids)
        starts.append(row_ids - places)
        tables.append(rotation(places, head_dim))
        c, packed, h1, *made = run(
            without_sides(functools.partial(first_body, m, quarter), len(both_rows)),
            ids,
            [tokens, gain1_row, q_down, kv_proj, *tables[m]],
            [whole((rows, part), LOW), whole((half, 2 * head_dim), LOW), whole((rows, width), LOW),
             *both_rows],
            order,
            name="first",
        )
        order = [c]
        blocks = [packed] + [
            lax.ppermute(packed, "seq", [(i, i + 2 * d) for i in range(seq - 2 * d)])
            for d in range(1, line)
        ]
        near = jnp.stack(blocks, 0)
        near = jnp.stack([near, other(near)], 0)
        kv.append(
            jnp.stack([near, lax.ppermute(near, "mp", CORE)], 0).reshape(key_count, 2 * head_dim)
        )
        c_part.append(c)
        h1_sides.append(split_sides(made, h1, rows))

    dhid, dz, *made = run(
        functools.partial(cotangent_body, micro, quarter),
        ids,
        [cotangent, w_down],
        [whole((micro, rows, hidden), F32), whole((micro, rows, width), LOW),
         *sides_shape(width, half, (micro,))],
        order,
        name="cotangent",
    )
    order = [dz]
    dz_mine, dz_theirs = split_sides(made, dz, half)
    dz_got = from_other(dz_theirs)

    qn_sides, qs, os, lses, sums, c_rows = [], [], [], [], [], []
    for m in range(micro):
        near = lax.ppermute(c_part[m], "mp", CROSS)
        swapped = jnp.concatenate(
            [near[quarter : 2 * quarter], near[:quarter], near[3 * quarter :],
             near[2 * quarter : 3 * quarter]], 0
        )
        far = lax.ppermute(jnp.concatenate([c_part[m], swapped], 1), "mp", CORE)
        qn, q, o, lse, send, keep, *made = run(
            without_sides(functools.partial(attend_body, scale), len(rank_sides)),
            ids,
            [c_part[m], near, far, gain_c_row, q_up, *tables[m], kv[m], key_ids[None, :],
             row_ids[:, None], starts[m][:, None], out_proj],
            [whole((rows, rank), LOW), whole((heads, rows, head_dim), LOW),
             whole((rows, heads * head_dim), LOW), whole((heads, rows), F32),
             whole((half, width), LOW), whole((half, width), F32), *rank_sides],
            order,
            name="attend",
        )
        order = [o]
        qn_sides.append(split_sides(made, qn, rows))
        qs.append(q)
        os.append(o)
        lses.append(lse)
        sums.append(sum_mp(send, keep))
        c_rows.append(
            jnp.concatenate([c_part[m][:quarter], swapped[:quarter], far[half : half + quarter]], 1)
        )

    h2_mine, h2_theirs, hid, dg, du, state = [], [], [], [], [], []
    for m in range(micro):
        x = lax.dynamic_slice_in_dim(tokens[m], me * quarter, quarter, 0).astype(F32)
        inv1 = inverse_rms(x)
        y = x + sums[m]
        inv2 = inverse_rms(y)
        n2 = y * inv2
        pieces = gather_mp((n2 * gain2_row).astype(LOW))
        h2, hid_m, dg_m, du_m, *made = run(
            without_sides(functools.partial(forward_body, m), len(half_rows)),
            ids,
            [*pieces, w_gate, w_up, dhid],
            [whole((rows, width), LOW), *[whole((rows, hidden), LOW)] * 3, *half_rows],
            order,
            name="forward",
        )
        order = [hid_m]
        mine, theirs = split_sides(made, h2, half)
        h2_mine.append(mine)
        h2_theirs.append(theirs)
        hid.append(hid_m)
        dg.append(dg_m)
        du.append(du_m)
        state.append(dict(x=x, n1=x * inv1, inv1=inv1, y=y, n2=n2, inv2=inv2, c=c_rows[m]))

    def stacked(name):
        return jnp.stack([st[name] for st in state], 0)

    def with_other(arrays):
        return [*arrays, *[other(a) for a in arrays]]

    def terms_of(spans):
        return [(a, lead, m + micro * partner, None, first, count)
                for a, lead, m, partner, first, count in spans]

    send, keep, ffn_send, ffn_keep = run(
        functools.partial(hidden_back_body, micro),
        ids,
        [*dg, *du, *hid, w_gate, w_up, w_down],
        [whole((micro, half, width), LOW), whole((micro, half, width), F32)] * 2,
        order,
        name="hidden_back",
    )
    lefts, spans = both_sides(dz_mine, dz_got)
    chain_down = Chain(lefts, with_other(hid), terms_of(spans), (wide, hidden), turned=True)
    lefts, spans = both_sides(h2_mine, [list(p) for p in zip(*[from_other(t) for t in h2_theirs])])
    chain_gate = Chain(lefts, with_other(dg), terms_of(spans), (wide, hidden))
    chain_up = Chain(lefts, with_other(du), terms_of(spans), (wide, hidden))

    order = chain_down.advance([send])
    dh2 = sum_mp(send, keep)
    y, n2, inv2, n1, inv1 = (stacked(k) for k in ("y", "n2", "inv2", "n1", "inv1"))
    dz_own = dz[:, :quarter].astype(F32)
    gain2 = jnp.sum(dh2 * n2, axis=(0, 1))
    dy = dz_own + norm_backward(dh2 * gain2_row, n2, inv2)
    for _ in range(2):
        order = chain_down.advance(order)
    order = chain_gate.advance(order)

    def attend_back(which, pieces):
        args = [*pieces, out_proj, q_up, key_ids[:, None]]
        for m in which:
            args += [qs[m], kv[m], os[m], lses[m], jnp.stack([row_ids, starts[m]], 0), *tables[m]]
        n = len(which)
        return run(
            functools.partial(attend_back_body, scale, n, min(1024, key_count // 2)),
            ids,
            args,
            [whole((n, rows, width), LOW), whole((n, rows, heads * head_dim), LOW),
             whole((n, half, rank), LOW), whole((n, half, rank), F32),
             whole((n, key_count // 2, 2 * head_dim), LOW),
             whole((n, key_count // 2, 2 * head_dim), F32), *sides_shape(width, half, (n,))],
            order,
            scratch=[pltpu.VMEM((heads, rows, head_dim), F32),
                     pltpu.VMEM((heads, rows, head_dim), LOW),
                     pltpu.VMEM((heads, 8, rows), F32)],
            name="attend_back",
            limit=56,
        )

    pieces = gather_mp(dy.astype(LOW))
    if key_count <= 2048:
        made = attend_back(range(micro), pieces)
    else:
        each = [attend_back([m], [p[m : m + 1] for p in pieces]) for m in range(micro)]
        made = [jnp.concatenate(parts, 0) for parts in zip(*each)]
    dyl, dqp, send, keep, kv_send, kv_keep, *made = made
    order = [send]
    dyl_mine, dyl_theirs = split_sides(made, dyl, half)
    lefts, spans = both_sides(dyl_mine, from_other(dyl_theirs))
    chain_out = Chain(lefts, with_other(os), terms_of(spans), (wide, heads * head_dim), turned=True)

    def side_sum(lefts, rights, shape, after):
        terms = [(m, None, 0, m, 0, rows) for m in range(micro)]
        (made,) = run(
            functools.partial(side_sum_body, terms, len(lefts)),
            ids,
            [*lefts, *rights],
            [whole((line, *shape), LOW)],
            after,
            name="side_sum",
        )
        return other(made), [made]

    def own_chain(side_pairs, right, shape, after):
        from_side, after = side_sum([p[1] for p in side_pairs], [right], shape, after)
        terms = [(m, None, 0, m, 0, rows) for m in range(micro)]
        return Chain([p[0] for p in side_pairs], [right], terms, shape, from_side=from_side), after

    shape = (rank // seq, heads * head_dim)
    chain_qup, order = own_chain(qn_sides, dqp, shape, order)
    order = chain_gate.advance(order)
    order = chain_up.advance(order)

    dqn = sum_mp(send, keep)
    c = stacked("c").astype(F32)
    inv_c = inverse_rms(c)
    chat = c * inv_c
    chat = to_natural(chat, 2)
    gain_c = jnp.sum(dqn * chat, axis=(0, 1))
    dc = norm_backward(dqn * gain_c_row, chat, inv_c).astype(LOW)

    dkv = kv_keep + lax.ppermute(kv_send, "mp", CORE).astype(F32)
    dkv = dkv.reshape(micro, 2, line, 2, quarter, 2 * head_dim)
    dkv = dkv[:, :, :, 0] + lax.ppermute(dkv[:, :, :, 1].astype(LOW), "mp", CROSS).astype(F32)
    dkv = dkv[:, 0] + other(dkv[:, 1].astype(LOW)).astype(F32)
    total = dkv[:, 0]
    for d in range(1, line):
        total = total + lax.ppermute(
            dkv[:, d].astype(LOW), "seq", [(i + 2 * d, i) for i in range(seq - 2 * d)]
        ).astype(F32)
    cosine = jnp.stack([t[0][:quarter] for t in tables], 0)
    sine = jnp.stack([t[1][:quarter] for t in tables], 0)
    dkv_low = jnp.concatenate(
        [unrotate(total[..., :head_dim], cosine, sine), total[..., head_dim:]], axis=-1
    ).astype(LOW)
    both = jnp.concatenate(gather_mp(jnp.concatenate([dc, dkv_low], -1)), -2)
    dfirst = jnp.concatenate(
        [lax.dynamic_slice_in_dim(both, me * part, part, 2),
         lax.dynamic_slice_in_dim(both, rank + me * kv_part, kv_part, 2)], -1
    )

    grad_down, order = chain_down.finish(order)
    order = chain_gate.advance(order)
    order = chain_up.advance(order)
    order = chain_out.advance(order)
    grad_gate, order = chain_gate.finish(order)
    order = chain_up.advance(order)
    order = chain_out.advance(order)
    grad_up, order = chain_up.finish(order)
    order = chain_qup.advance(order)
    order = chain_out.advance(order)
    chain_first, order = own_chain(h1_sides, dfirst, (wide, part + kv_part), order)
    order = chain_qup.advance(order)
    grad_out, order = chain_out.finish(order)
    order = chain_first.advance(order)
    order = chain_qup.advance(order)
    order = chain_first.advance(order)
    grad_qup, order = chain_qup.finish(order)
    order = chain_first.advance(order)
    grad_first, order = chain_first.finish(order)

    grad_qdown = grad_first[:, :part]
    kv_cols_grad = grad_first[:, part:]
    pieces = []
    for k in ORDER:
        size = kv_cols_grad.shape[0] // 4
        sent = lax.dynamic_slice_in_dim(kv_cols_grad, (me ^ k) * size, size, 0)
        pieces.append(lax.ppermute(sent, "mp", [(i, i ^ k) for i in range(4)]) if k else sent)
    grad_kv = to_natural(jnp.concatenate(pieces, 1), 1)

    def put_natural(pieces):
        return run(
            functools.partial(natural_body, micro, quarter),
            ids,
            pieces,
            [whole((micro, rows, width), LOW)],
            name="natural",
        )[0]

    part_sum = inner_cols(dfirst.reshape(micro * rows, -1), first_weights).reshape(micro, rows, width)
    dh1 = sum_mp(part_sum[:, half:].astype(LOW), part_sum[:, :half])
    gain1 = jnp.sum(dh1 * n1, axis=(0, 1))
    dx = (dy + norm_backward(dh1 * gain1_row, n1, inv1)).astype(LOW)
    input_grads = put_natural(gather_mp(dx))

    ffn = sum_mp(ffn_send, ffn_keep)
    layer_out = put_natural(gather_mp((y + ffn).astype(LOW)))

    gains = jnp.concatenate(
        [gain1.reshape(seq, -1), gain2.reshape(seq, -1), gain_c.reshape(seq, -1)], axis=1
    )
    gains = gains + lax.ppermute(gains, "mp", CORE)
    gains = gains + lax.ppermute(gains, "mp", CROSS)
    gain_sum = lax.dynamic_index_in_dim(gains, at, 0, keepdims=False)
    for k in range(1, seq):
        gain_sum = gain_sum + lax.ppermute(
            lax.dynamic_index_in_dim(gains, at ^ k, 0, keepdims=False),
            "seq",
            [(i, i ^ k) for i in range(seq)],
        )
    return (
        layer_out,
        input_grads,
        gain_sum[:wide],
        grad_qdown,
        gain_sum[2 * wide :],
        grad_qup,
        grad_kv,
        grad_out,
        gain_sum[wide : 2 * wide],
        grad_gate,
        grad_up,
        grad_down,
    )


def solution(mesh):
    placed = (
        P(None, "seq", None),
        P(),
        P(),
        P(None, "mp"),
        P(),
        P(None, "mp"),
        P(),
        P("mp", None),
        P(),
        P(None, "mp"),
        P(None, "mp"),
        P("mp", None),
        P(None, "seq", None),
    )
    return jax.shard_map(
        local,
        mesh=mesh,
        in_specs=placed,
        out_specs=(
            P(None, "seq", None),
            P(None, "seq", None),
            P("seq"),
            P("seq", "mp"),
            P("seq"),
            P("seq", "mp"),
            P(("seq", "mp"), None),
            P("mp", "seq"),
            P("seq"),
            P("seq", "mp"),
            P("seq", "mp"),
            P("mp", "seq"),
        ),
        check_vma=False,
    )
```

```python
import functools

import jax
import jax.numpy as jnp
from jax import lax
from jax.experimental import pallas as pl
from jax.experimental.pallas import tpu as pltpu
from jax.sharding import PartitionSpec as P

EPS = 1e-06
BASE = 10000.0
NEG_LARGE = -1e30
LOW = jnp.bfloat16
F32 = jnp.float32
ORDER = (0, 2, 1, 3)
CORE = [(i, i ^ 1) for i in range(4)]
CROSS = [(i, i ^ 2) for i in range(4)]


def inverse_rms(values):
    return lax.rsqrt(jnp.mean(values * values, axis=-1, keepdims=True) + EPS)


def norm_backward(grad_hat, normed, inverse):
    return inverse * (grad_hat - normed * jnp.mean(grad_hat * normed, axis=-1, keepdims=True))


def dot(left, right):
    return jnp.dot(left, right, preferred_element_type=F32)


def inner_rows(left, right):
    return lax.dot_general(left, right, (((0,), (0,)), ((), ())), preferred_element_type=F32)


def inner_cols(left, right):
    return lax.dot_general(left, right, (((1,), (1,)), ((), ())), preferred_element_type=F32)


def documents(lengths_row, rows):
    first_end = lengths_row[0]
    second_end = first_end + lengths_row[1]
    doc_ids = (rows >= first_end).astype(jnp.int32) + (rows >= second_end).astype(jnp.int32)
    starts = jnp.where(rows >= second_end, second_end, jnp.where(rows >= first_end, first_end, 0))
    return (doc_ids, rows - starts)


def rotation(positions, head_dim):
    half = head_dim // 2
    freqs = BASE ** (-2.0 * jnp.arange(half, dtype=F32) / head_dim)
    angles = positions.astype(F32)[:, None] * freqs[None, :]
    return (jnp.cos(angles), jnp.sin(angles))


def rotate(values, cosine, sine):
    half = values.shape[-1] // 2
    first = values[..., :half]
    second = values[..., half:]
    return jnp.concatenate(
        [first * cosine - second * sine, second * cosine + first * sine], axis=-1
    )


def unrotate(grads, cosine, sine):
    return rotate(grads, cosine, -sine)


def in_vmem():
    return pl.BlockSpec(memory_space=pltpu.VMEM)


def whole(shape, dtype):
    return jax.ShapeDtypeStruct(shape, dtype)


def run(body, ids, args, outs, after=(), scratch=(), name=None, limit=40):
    args, after = list(args), list(after)

    def without(*refs):
        body(*refs[: 1 + len(args)], *refs[1 + len(args) + len(after) :])

    return pl.pallas_call(
        without,
        grid_spec=pltpu.PrefetchScalarGridSpec(
            num_scalar_prefetch=1,
            grid=(1,),
            in_specs=[in_vmem()] * len(args) + [pl.BlockSpec(memory_space=pl.ANY)] * len(after),
            out_specs=[in_vmem()] * len(outs),
            scratch_shapes=list(scratch),
        ),
        out_shape=list(outs),
        cost_estimate=pl.CostEstimate(flops=1000, bytes_accessed=1000, transcendentals=0),
        compiler_params=pltpu.CompilerParams(vmem_limit_bytes=limit << 20),
        name=name,
    )(ids, *args, *after)


def side_columns(source, mine, theirs, side):
    line, _, wide = mine.shape
    rows = theirs.shape[1]
    for z in range(line):
        mine[z] = source[:, pl.ds(pl.multiple_of((2 * z + side) * wide, wide), wide)]
        theirs[z] = source[:rows, pl.ds(pl.multiple_of((2 * z + 1 - side) * wide, wide), wide)]


def first_body(m, quarter, ids, x_ref, gain, q_down, kv_proj, cos, sin, c, kv, h1, mine, theirs):
    blocks = [
        x_ref[m, pl.ds(pl.multiple_of((ids[0] ^ k) * quarter, quarter), quarter), :] for k in ORDER
    ]
    x = jnp.concatenate(blocks, 0).astype(F32)
    low = (x * inverse_rms(x) * gain[...]).astype(LOW)
    h1[...] = low
    half = 2 * quarter
    pair = dot(low[:half], kv_proj[...])
    wide = kv_proj.shape[1] // 2
    kv[:, :wide] = rotate(pair[:, :wide], cos[:half], sin[:half]).astype(LOW)
    kv[:, wide:] = pair[:, wide:].astype(LOW)
    c[...] = dot(low, q_down[...]).astype(LOW)
    if mine is not None:
        side_columns(h1, mine, theirs, ids[1])


def cotangent_body(micro, quarter, ids, z_ref, w_down, dhid, dz, *sides):
    for m in range(micro):
        blocks = [
            z_ref[m, pl.ds(pl.multiple_of((ids[0] ^ k) * quarter, quarter), quarter), :]
            for k in ORDER
        ]
        dz[m] = jnp.concatenate(blocks, 0)
        if sides:
            side_columns(dz.at[m], sides[0].at[m], sides[1].at[m], ids[1])
        dhid[m] = inner_cols(dz[m], w_down[...])


def attend_body(
    scale, ids, c0, c1, c2, gain, q_up, cos, sin, kv, key_ids, row_ids, row_starts, out_proj,
    qn, q, o, lse, send, keep, mine, theirs,
):
    rows = qn.shape[0]
    quarter = rows // 4
    part = c0.shape[1]
    wide = q.shape[2]
    got = c1[...]
    pair = jnp.concatenate(
        [got[quarter : 2 * quarter], got[:quarter], got[3 * quarter :], got[2 * quarter : 3 * quarter]],
        0,
    )
    far = jnp.concatenate([c2[2 * quarter :], c2[: 2 * quarter]], 0)
    c = jnp.concatenate([c0[...], pair, far], 1).astype(F32)
    chat = c * inverse_rms(c)
    for k, xor in enumerate(ORDER):
        columns = pl.ds(pl.multiple_of((ids[0] ^ xor) * part, part), part)
        qn[:, columns] = (chat[:, k * part : (k + 1) * part] * gain[:, columns]).astype(LOW)
    if mine is not None:
        side_columns(qn, mine, theirs, ids[1])
    bias = jnp.where(
        (key_ids[...] >= row_starts[...]) & (key_ids[...] <= row_ids[...]), 0.0, NEG_LARGE
    )
    low = qn[...]
    keys, values = kv[:, :wide], kv[:, wide:]
    for h in range(q.shape[0]):
        pre = dot(low, q_up[:, h * wide : (h + 1) * wide])
        q_h = (rotate(pre, cos[...], sin[...]) * scale).astype(LOW)
        q[h] = q_h
        scores = inner_cols(q_h, keys) + bias
        top = jnp.max(scores, axis=-1, keepdims=True)
        probs = jnp.exp(scores - top)
        total = jnp.sum(probs, axis=-1, keepdims=True)
        out = dot(probs.astype(LOW), values) / total
        o[:, h * wide : (h + 1) * wide] = out.astype(LOW)
        log_total = jnp.broadcast_to(top + jnp.log(total), (rows, 128))
        lse[h : h + 1, :] = jnp.transpose(log_total)[:1]
    half = 2 * quarter
    send[...] = dot(o[half:, :], out_proj[...]).astype(LOW)
    keep[...] = dot(o[:half, :], out_proj[...])


def forward_body(m, ids, a0, a1, a2, w_gate, w_up, dhid, h2, hid, dg, du, mine, theirs):
    h2[...] = jnp.concatenate([a0[...], a1[...], a2[...]], 0)
    if mine is not None:
        side_columns(h2, mine, theirs, ids[1])
    low = h2[...]
    g = dot(low, w_gate[...])
    u = dot(low, w_up[...])
    sig = jax.nn.sigmoid(g)
    swish = g * sig
    hid[...] = (swish * u).astype(LOW)
    back = dhid[m]
    dg[...] = (back * u * sig * (1.0 + g * (1.0 - sig))).astype(LOW)
    du[...] = (back * swish).astype(LOW)


def hidden_back_body(micro, ids, *refs):
    dgs, dus = refs[:micro], refs[micro : 2 * micro]
    hids = refs[2 * micro : 3 * micro]
    w_gate, w_up, w_down, send, keep, out_send, out_keep = refs[3 * micro :]
    half = send.shape[1]
    every = lambda parts: jnp.concatenate([part[...] for part in parts], 0)
    rows = 2 * half
    total = inner_cols(every(dgs), w_gate[...]) + inner_cols(every(dus), w_up[...])
    for m in range(micro):
        send[m] = total[m * rows + half : (m + 1) * rows].astype(LOW)
        keep[m] = total[m * rows : m * rows + half]
    total = dot(every(hids), w_down[...])
    for m in range(micro):
        out_send[m] = total[m * rows + half : (m + 1) * rows].astype(LOW)
        out_keep[m] = total[m * rows : m * rows + half]


def pick(ref, lead):
    return ref if lead is None else ref.at[lead]


def block_body(terms, lefts, rights, extra, from_side, turned, ids, *refs):
    left, refs = refs[:lefts], refs[lefts:]
    right, refs = refs[:rights], refs[rights:]
    added, out = refs[: extra + from_side], refs[-1]
    total = None
    for a, a_lead, b, b_lead, first, count in terms:
        rows = pick(right[b], b_lead)[first : first + count, :]
        term = inner_rows(pick(left[a], a_lead)[ids[0]], rows)
        total = term if total is None else total + term
    for i, ref in enumerate(added):
        total = total + (ref[ids[0]] if i >= extra else ref[...]).astype(F32)
    out[...] = jnp.transpose(total) if turned else total.astype(out.dtype)


def side_sum_body(terms, lefts, ids, *refs):
    left, right, out = refs[:lefts], refs[lefts:-1], refs[-1]
    for z in range(out.shape[0]):
        total = None
        for a, a_lead, b, b_lead, first, count in terms:
            rows = pick(right[b], b_lead)[first : first + count, :]
            term = inner_rows(pick(left[a], a_lead)[z], rows)
            total = term if total is None else total + term
        out[z] = total.astype(out.dtype)


def attend_back_body(
    scale, micro, chunk, ids, a0, a1, a2, out_proj, q_up, key_ids, *refs
):
    per = 7
    groups = [refs[m * per : (m + 1) * per] for m in range(micro)]
    dyl_out, dqp, send, keep, kv_send, kv_keep = refs[micro * per : micro * per + 6]
    dq_acc, do_acc, delta_acc = refs[-3:]
    sides = refs[micro * per + 6 : -3]
    for m in range(micro):
        q, kv, o, lse, row_ids, cos, sin = groups[m]
        heads, rows, wide = q.shape
        half_rows = rows // 2
        dyl = jnp.concatenate([a0[m], a1[m], a2[m]], 0)
        dyl_out[m] = dyl
        if sides:
            side_columns(dyl_out.at[m], sides[0].at[m], sides[1].at[m], ids[1])
        for h in range(heads):
            do = inner_cols(dyl, out_proj[h * wide : (h + 1) * wide, :]).astype(LOW)
            do_acc[h] = do
            delta = jnp.sum(
                do.astype(F32) * o[:, h * wide : (h + 1) * wide].astype(F32), axis=-1, keepdims=True
            )
            delta_acc[h] = jnp.transpose(jnp.broadcast_to(delta, (rows, 128)))[:8]
            dq_acc[h] = jnp.zeros((rows, wide), F32)
        count = kv.shape[0] // 2 // chunk
        for part, out in ((0, kv_keep), (1, kv_send)):

            def one(i, carry):
                base = pl.multiple_of((part * count + i) * chunk, chunk)
                keys = kv[pl.ds(base, chunk), :wide]
                values = kv[pl.ds(base, chunk), wide:]
                at = key_ids[pl.ds(base, chunk), :]
                bias = jnp.where((at >= row_ids[1:2, :]) & (at <= row_ids[0:1, :]), 0.0, NEG_LARGE)

                def head(h, sums):
                    dk, dv = sums
                    q_h, do_h = q[h], do_acc[h]
                    probs = jnp.exp(inner_cols(keys, q_h) + bias - lse[pl.ds(h, 1), :])
                    back = inner_cols(values, do_h) - delta_acc[h][:1]
                    ds = (probs * back).astype(LOW)
                    dv = dv + dot(probs.astype(LOW), do_h)
                    dk = dk + dot(ds, q_h)
                    dq_acc[h] = dq_acc[h] + inner_rows(ds, keys)
                    return dk, dv

                zero = jnp.zeros((chunk, wide), F32)
                dk, dv = lax.fori_loop(0, heads, head, (zero, zero))
                place = pl.ds(pl.multiple_of(i * chunk, chunk), chunk)
                out[m, place, :wide] = dk.astype(out.dtype)
                out[m, place, wide:] = dv.astype(out.dtype)
                return carry

            if count == 1:
                one(0, 0)
            else:
                lax.fori_loop(0, count, one, 0)
        for h in range(heads):
            dq = unrotate(dq_acc[h] * scale, cos[...], sin[...])
            dqp[m, :, h * wide : (h + 1) * wide] = dq.astype(LOW)
        low = dqp[m]
        send[m] = inner_cols(low[half_rows:], q_up[...]).astype(LOW)
        keep[m] = inner_cols(low[:half_rows], q_up[...])


def natural_body(micro, quarter, ids, a0, a1, a2, out):
    for m in range(micro):
        pieces = (a0[m], a1[m], a2[m, :quarter, :], a2[m, quarter:, :])
        for k, piece in zip(ORDER, pieces):
            out[m, pl.ds(pl.multiple_of((ids[0] ^ k) * quarter, quarter), quarter), :] = piece


class Wire:
    def __init__(self, sends, recvs):
        self.sends, self.recvs, self.used = sends, recvs, 0
        self.seq, self.mp = lax.axis_index("seq"), lax.axis_index("mp")
        self.place, self.side = self.seq // 2, self.seq % 2
        core, cross = self.mp % 2, self.mp // 2
        self.blocks = (
            self.mp, 2 * (1 - cross) + core, 2 * cross + 1 - core, 2 * (1 - cross) + 1 - core
        )
        self.core, self.cross = {"mp": self.blocks[2]}, {"mp": self.blocks[1]}
        self.beside = {"seq": self.seq + 1 - 2 * self.side}
        self.up, self.down = {"seq": self.seq + 2}, {"seq": self.seq - 2}

    def copy(self, source, target, device):
        at = self.used
        self.used += 1
        return pltpu.make_async_remote_copy(
            src_ref=source, dst_ref=target, send_sem=self.sends.at[at], recv_sem=self.recvs.at[at],
            device_id=device, device_id_type=pl.DeviceIdType.MESH,
        )

    def send(self, source, target, device):
        made = self.copy(source, target, device)
        made.start()
        return made

    def greet(self, line, far=1, diagonal=False):
        barrier = pltpu.get_barrier_semaphore()
        devices = [self.core, self.cross, self.beside]
        if diagonal:
            devices.append({"mp": self.blocks[3]})
        for device in devices:
            pl.semaphore_signal(barrier, 1, device_id=device, device_id_type=pl.DeviceIdType.MESH)
        for d in range(1, far + 1):
            for way, there in ((1, self.place < line - d), (-1, self.place >= d)):

                @pl.when(there)
                def _():
                    pl.semaphore_signal(
                        barrier, 1, device_id={"seq": self.seq + 2 * way * d},
                        device_id_type=pl.DeviceIdType.MESH,
                    )
        below, above = jnp.minimum(self.place, far), jnp.minimum(line - 1 - self.place, far)
        pl.semaphore_wait(barrier, len(devices) + below + above)


def along(pieces, axis):
    return pieces[0] if len(pieces) == 1 else jnp.concatenate(pieces, axis)


def pair_places(first, second, quarter, axis):
    shape = (2 * quarter, 1) if axis == 0 else (1, 2 * quarter)
    index = lax.broadcasted_iota(jnp.int32, shape, axis)
    return jnp.where(index < quarter, first * quarter + index, (second - 1) * quarter + index)


def row_places(wire, quarter, axis):
    b = wire.blocks
    pieces = [pair_places(b[i], b[i + 1], quarter, axis) for i in (0, 2)]
    return wire.seq * (4 * quarter) + along(pieces, axis)


def key_places(wire, quarter, line, axis, cores):
    pieces = []
    for core in cores:
        for side in (wire.side, 1 - wire.side):
            for d in range(line):
                base = ((wire.place - d) * 2 + side) * (4 * quarter)
                b = wire.blocks[2 * core : 2 * core + 2]
                pieces.append(base + pair_places(b[0], b[1], quarter, axis))
    return along(pieces, axis)


def sequence_starts(lengths, m, places):
    first_end = lengths[m, 0]
    second_end = first_end + lengths[m, 1]
    return jnp.where(
        places >= second_end, second_end, jnp.where(places >= first_end, first_end, 0)
    )


class LineSum:
    def __init__(self, wire, term, room, rows, columns, keep):
        got, out = room
        view = lambda ref, i: ref.at[i, :rows, :columns]
        self.place, self.term, self.keep = wire.place, term, keep
        self.got = [view(got, i) for i in range(5)]
        self.out = [view(out, i) for i in range(2)]
        one, two_up, two_down, three_up, three_down = self.got
        a, b = self.out
        self.one = wire.copy(a, one, wire.up), wire.copy(a, one, wire.down)
        self.two = wire.copy(b, two_up, wire.up), wire.copy(b, two_down, wire.down)
        self.three = wire.copy(a, three_up, wire.up), wire.copy(b, three_down, wire.down)

    def clear(self):
        place = self.place
        for ref, empty in zip(
            self.got, ((place == 0) | (place == 3),) * 3 + (place == 0, place == 3)
        ):

            @pl.when(empty)
            def _(ref=ref):
                ref[...] = jnp.zeros(ref.shape, ref.dtype)

    def step1(self):
        place = self.place

        @pl.when((place == 0) | (place == 3))
        def _():
            self.out[0][...] = self.term(3 - place).astype(LOW)

        pl.when(place == 0)(self.one[0].start)
        pl.when(place == 3)(self.one[1].start)

    def step2(self):
        place = self.place
        pl.when(place == 1)(self.one[0].wait_recv)
        pl.when(place == 2)(self.one[1].wait_recv)
        self.out[1][...] = (
            self.term((place + 2) % 4) + self.got[0][...].astype(F32)
        ).astype(LOW)
        pl.when(place <= 1)(self.two[0].start)
        pl.when(place >= 2)(self.two[1].start)

    def step3(self):
        place = self.place

        @pl.when((place == 1) | (place == 2))
        def _():
            self.two[0].wait_recv()
            self.two[1].wait_recv()

        pl.when(place == 0)(self.one[0].wait_send)
        pl.when(place == 3)(self.one[1].wait_send)

        @pl.when(place <= 2)
        def _():
            self.out[0][...] = (self.term(place + 1) + self.got[1][...].astype(F32)).astype(LOW)
            self.three[0].start()

        pl.when(place <= 1)(self.two[0].wait_send)
        pl.when(place >= 2)(self.two[1].wait_send)

        @pl.when(place >= 1)
        def _():
            self.out[1][...] = (self.term(place - 1) + self.got[2][...].astype(F32)).astype(LOW)
            self.three[1].start()

    def finish(self):
        place = self.place
        pl.when(place >= 1)(self.three[0].wait_recv)
        pl.when(place <= 2)(self.three[1].wait_recv)
        self.keep(
            self.term(place) + self.got[3][...].astype(F32) + self.got[4][...].astype(F32)
        )

    def settle(self):
        place = self.place
        pl.when(place <= 2)(self.three[0].wait_send)
        pl.when(place >= 1)(self.three[1].wait_send)


SPACES = (pl.ANY, pltpu.VMEM, pltpu.SMEM)


def mesh_run(body, args, outs, scratch, number, name, limit, sends):
    return pl.pallas_call(
        body,
        in_specs=[pl.BlockSpec(memory_space=SPACES[kind]) for kind, _ in args],
        out_specs=[pl.BlockSpec(memory_space=SPACES[kind]) for kind, _ in outs],
        out_shape=[shape for _, shape in outs],
        scratch_shapes=[
            *scratch, pltpu.SemaphoreType.DMA((sends,)), pltpu.SemaphoreType.DMA((sends,))
        ],
        cost_estimate=pl.CostEstimate(flops=1000, bytes_accessed=1000, transcendentals=0),
        compiler_params=pltpu.CompilerParams(
            collective_id=number, has_side_effects=True, vmem_limit_bytes=limit << 20
        ),
        name=name,
    )(*[array for _, array in args])


def attend_back_one(
    scale, keys_at, rows_at, starts, dyl, out_proj, q_up, q, kv, o, lse, cos, sin,
    dqp, send, keep, kv_send, kv_keep, dq_acc, between=None,
):
    heads, rows, wide = q.shape
    half_rows = rows // 2
    low = dyl[...]
    grads, deltas = [], []
    for h in range(heads):
        columns = slice(h * wide, (h + 1) * wide)
        do = inner_cols(low, out_proj[columns, :]).astype(LOW)
        grads.append(do)
        delta = jnp.sum(do.astype(F32) * o[:, columns].astype(F32), axis=-1, keepdims=True)
        deltas.append(jnp.transpose(jnp.broadcast_to(delta, (rows, 128)))[:1])
    do_all, delta_all = jnp.concatenate(grads, 0), jnp.concatenate(deltas, 1)
    q_all = q[...].reshape(heads * rows, wide)
    lse_all = jnp.concatenate([lse[h : h + 1, :] for h in range(heads)], 1)
    dq_acc[...] = jnp.zeros(dq_acc.shape, F32)
    count = kv.shape[0] // 2
    chunk = min(256, count)
    for part, out in ((1, kv_send), (0, kv_keep)):
        for first in range(0, count, chunk):
            span = slice(part * count + first, part * count + first + chunk)
            keys, values = kv[span, :wide], kv[span, wide:]
            at = keys_at[part][first : first + chunk]
            bias = jnp.where((at >= starts) & (at <= rows_at), 0.0, NEG_LARGE)
            scores = inner_cols(keys, q_all) + jnp.concatenate([bias] * heads, 1)
            probs = jnp.exp(scores - lse_all)
            ds = (probs * (inner_cols(values, do_all) - delta_all)).astype(LOW)
            spot = slice(first, first + chunk)
            out[spot, :wide] = dot(ds, q_all).astype(out.dtype)
            out[spot, wide:] = dot(probs.astype(LOW), do_all).astype(out.dtype)
            dq_acc[...] += inner_rows(ds, keys)
        if part and between is not None:
            between()
    for h in range(heads):
        dq = unrotate(dq_acc[h * rows : (h + 1) * rows, :] * scale, cos, sin)
        dqp[:, h * wide : (h + 1) * wide] = dq.astype(LOW)
    total = inner_cols(dqp[...], q_up[...])
    send[...] = total[half_rows:].astype(LOW)
    keep[...] = total[:half_rows]


def mean_of(values):
    return jnp.mean(values, axis=-1, keepdims=True)


def terms_sum(pairs):
    total = None
    for left, right in pairs:
        term = inner_rows(left, right)
        total = term if total is None else total + term
    return total


def back1_body(quarter, *refs):
    refs = list(refs)
    take = lambda n: [refs.pop(0) for _ in range(n)]
    w_gate, w_up, w_down, h2, dhid, n2, inv2, dz, gain2, dz_mine, dz_got, dz_far, y = take(13)
    grad, dy, gain_sum, dyl, dyl_mine, dyl_theirs, layer_own = take(7)
    hid, dg, du, h2_mine = (take(2) for _ in range(4))
    h2_got, h2_far, dg_other = take(2), take(2), take(2)
    gate_w, up_w, hid_other0, hid_other1, h2_theirs, got, out = take(7)
    send, kept, core_got, cross_out, cross_got, loads = take(6)
    ffn_send, ffn_kept, ffn_got, ffn_out, ffn_back = take(5)
    early_got, early_out, early_sum, early_send, early_back = take(5)
    wire = Wire(*take(2))
    half, rows = 2 * quarter, 4 * quarter
    ahead = early_send.shape[1]
    block = early_send.shape[0]
    in_gate = pltpu.make_async_copy(w_gate, gate_w, loads.at[0])
    in_up = pltpu.make_async_copy(w_up, up_w, loads.at[1])
    in_gate.start()
    in_up.start()
    hid_other = (hid_other0, hid_other1)
    hid_all = (*(a.at[:, ahead:] for a in hid), *hid_other)

    def term(z):
        return terms_sum(halves_terms(
            [dz_mine[m, z] for m in range(2)], [dz_got[m, z] for m in range(2)],
            [dz_far[m, z] for m in range(2)], hid_all, half))

    def early_term(z):
        columns = pl.ds(pl.multiple_of(z * 2 * block, 2 * block), 2 * block)
        return terms_sum([(dz[m, :, columns], hid[m][:, :ahead]) for m in range(2)])

    def keep(total):
        grad[ahead:, :] = jnp.transpose(total)

    def early_keep(total):
        early_sum[0], early_sum[1] = total[:block], total[block:]

    chain = LineSum(wire, term, (got, out), block, grad.shape[0] - ahead, keep)
    early = LineSum(wire, early_term, (early_got, early_out), 2 * block, ahead, early_keep)
    chain.clear()
    early.clear()
    wire.greet(4)
    y_hid = []
    for m in range(2):
        low = h2[m]
        if m == 0:
            in_gate.wait()
        g = dot(low, gate_w[...])
        if m == 0:
            in_up.wait()
        u = dot(low, up_w[...])
        sig = jax.nn.sigmoid(g)
        swish = g * sig
        hid[m][...] = (swish * u).astype(LOW)
        y_hid.append(wire.send(hid[m].at[:, ahead:], hid_other[m], wire.beside))
        back = dhid[m]
        dg[m][...] = (back * u * sig * (1.0 + g * (1.0 - sig))).astype(LOW)
        du[m][...] = (back * swish).astype(LOW)
    early.step1()
    both = lambda pair: jnp.concatenate([pair[0][...], pair[1][...]], 0)
    total = inner_cols(both(dg), gate_w[...]) + inner_cols(both(du), up_w[...])
    for m in range(2):
        send[m] = total[m * rows + half : (m + 1) * rows].astype(LOW)
        kept[m] = total[m * rows : m * rows + half]
    sums = RowSum(wire, send, kept, core_got, cross_out, cross_got, quarter)
    sums.core.start()
    wide = gate_w.shape[1]
    rest = w_down.shape[1] - wide
    downs = [gate_w.at[:wide, :], up_w.at[:wide, :rest]]
    in_down = [
        pltpu.make_async_copy(w_down.at[:, :wide], downs[0], loads.at[0]),
        pltpu.make_async_copy(w_down.at[:, wide:], downs[1], loads.at[1]),
    ]
    for made in in_down:
        made.start()
    for m in range(2):
        side_columns(h2.at[m], h2_mine[m], h2_theirs.at[m], wire.side)
    sums.pass_on()
    early.step2()
    for made in in_down:
        made.wait()
    low = both(hid)
    ffn_sum = RowSum(wire, ffn_send, ffn_kept, ffn_got, ffn_out, ffn_back, quarter)
    for columns, part in ((slice(0, wide), downs[0]), (slice(wide, None), downs[1])):
        total = dot(low, part[...])
        for m in range(2):
            ffn_send[m, :, columns] = total[m * rows + half : (m + 1) * rows].astype(LOW)
            ffn_kept[m, :, columns] = total[m * rows : m * rows + half]
    ffn_sum.core.start()
    for made in y_hid:
        made.wait_recv()
    y_next = [wire.send(h2_theirs.at[m], h2_got[m], wire.beside) for m in range(2)]
    y_next += [wire.send(dg[m], dg_other[m], wire.beside) for m in range(2)]
    chain.step1()
    early.step3()
    dh2 = sums.result()
    gain_sum[...] = jnp.sum(jnp.sum(dh2 * n2[...], axis=0), axis=0, keepdims=True)
    back = dh2 * gain2[...]
    grad_y = dz[:, :quarter, :].astype(F32) + inv2[...] * (
        back - n2[...] * mean_of(back * n2[...])
    )
    dy[...] = grad_y
    dyl[:, :quarter, :] = grad_y.astype(LOW)
    cross_dyl = wire.send(dyl.at[:, :quarter, :], dyl.at[:, quarter:half, :], wire.cross)
    ffn_sum.pass_on()
    chain.step2()
    early.finish()
    early_send[...] = early_sum[1 - wire.side].astype(LOW)
    y_early = wire.send(early_send, early_back, wire.beside)
    cross_dyl.wait_recv()
    core_dyl = wire.send(dyl.at[:, :half, :], dyl.at[:, half:, :], wire.core)
    core_h2 = []
    for i in range(2):
        y_next[i].wait_recv()
        core_h2.append(wire.send(h2_got[i], h2_far[i], wire.core))
    core_dyl.wait_recv()
    for m in range(2):
        side_columns(dyl.at[m], dyl_mine.at[m], dyl_theirs.at[m], wire.side)
    chain.step3()
    layer_own[...] = (y[...] + ffn_sum.result()).astype(LOW)
    y_early.wait_recv()
    grad[:ahead, :] = jnp.transpose(early_sum[wire.side] + early_back[...].astype(F32))
    for made in y_next[2:] + core_h2:
        made.wait_recv()
    chain.finish()
    for made in [*y_hid, cross_dyl, core_dyl, *y_next, *core_h2, y_early]:
        made.wait_send()
    sums.end()
    ffn_sum.end()
    early.settle()
    chain.settle()


class Share:
    def __init__(self, wire, out, quarter):
        spot = lambda block: out.at[:, pl.ds(pl.multiple_of(block * quarter, quarter), quarter), :]
        own, near = spot(wire.blocks[0]), spot(wire.blocks[1])
        self.own = own
        self.first = wire.copy(own, own, wire.cross)
        self.rest = wire.copy(own, own, wire.core), wire.copy(near, near, wire.core)

    def begin(self, value):
        self.own[...] = value
        self.first.start()
        self.rest[0].start()

    def forward(self):
        self.first.wait_recv()
        self.rest[1].start()

    def end(self):
        for made in self.rest:
            made.wait_recv()
        for made in (self.first, *self.rest):
            made.wait_send()


class RowSum:
    def __init__(self, wire, send, kept, got, cross_out, cross_got, quarter):
        self.kept, self.got, self.quarter = kept, got, quarter
        self.out, self.back = cross_out, cross_got
        self.core = wire.copy(send, got, wire.core)
        self.cross = wire.copy(cross_out, cross_got, wire.cross)

    def pass_on(self):
        self.core.wait_recv()
        rest = slice(self.quarter, None)
        self.out[...] = (self.kept[:, rest, :] + self.got[:, rest, :].astype(F32)).astype(LOW)
        self.cross.start()

    def result(self):
        self.cross.wait_recv()
        own = slice(0, self.quarter)
        return (
            self.kept[:, own, :] + self.got[:, own, :].astype(F32) + self.back[...].astype(F32)
        )

    def end(self):
        self.core.wait_send()
        self.cross.wait_send()


def halves_terms(mine, got, far, rights, half):
    pairs = [(mine[m], rights[m][...]) for m in range(2)]
    for m in range(2):
        pairs.append((got[m], rights[2 + m][:half, :]))
        pairs.append((far[m], rights[2 + m][half:, :]))
    return pairs


def back2_body(quarter, scale, *refs):
    refs = list(refs)
    take = lambda n: [refs.pop(0) for _ in range(n)]
    (lengths,) = take(1)
    dg, dg_other, du, h2_mine, h2_got, h2_far = (take(2) for _ in range(6))
    dyl, out_proj, q_up = take(3)
    q, kv, o, lse = (take(2) for _ in range(4))
    cos, sin, chat, inv_c, gain_c, dyl_theirs = take(6)
    qn_theirs = take(2)
    grad_gate, grad_up, dfirst, gain_sum, dqp, dyl_got, dyl_far, qup_side = take(8)
    du_other = take(2)
    got_a, out_a, got_b, out_b = take(4)
    dq_acc, dqn_send, dqn_keep, kv_send, kv_keep = take(5)
    dqn_got, dqn_out, dqn_back = take(3)
    kv_got, kv_out, kv_back, side_out, side_got, line_out, line_got, kv_own = take(8)
    both, side_sums = take(2)
    wire = Wire(*take(2))
    half, rows = 2 * quarter, 4 * quarter
    wide = kv_own.shape[2] // 2
    rank = chat.shape[2]
    place = wire.place

    y_du = [wire.copy(du[m], du_other[m], wire.beside) for m in range(2)]

    def chain(rights, grad, room):
        def term(z):
            return terms_sum(halves_terms(
                [a[z] for a in h2_mine], [a[z] for a in h2_got], [a[z] for a in h2_far], rights,
                half))

        def keep(total):
            grad[...] = total

        made = LineSum(wire, term, room, *grad.shape, keep)
        made.clear()
        return made

    gate = chain((*dg, *dg_other), grad_gate, (got_a, out_a))
    up = chain((*du, *du_other), grad_up, (got_b, out_b))
    dqn_sum, core_kv, cross_kv, side_kv, line_kv = [], [], [], [], []
    for m in range(2):
        one = lambda ref: ref.at[m : m + 1]
        dqn_sum.append(RowSum(wire, one(dqn_send), one(dqn_keep), one(dqn_got), one(dqn_out),
                              one(dqn_back), quarter))
        core_kv.append(wire.copy(kv_send.at[m], kv_got.at[m], wire.core))
        cross_kv.append(wire.copy(kv_out.at[m], kv_back.at[m], wire.cross))
        side_kv.append(wire.copy(side_out.at[m], side_got.at[m], wire.beside))
        line_kv.append([
            wire.copy(line_out.at[m, d - 1], line_got.at[m, d - 1], {"seq": wire.seq - 2 * d})
            for d in range(1, 4)
        ])
        for d in range(1, 4):

            @pl.when(place > 3 - d)
            def _(m=m, d=d):
                line_got[m, d - 1] = jnp.zeros(line_got.shape[2:], LOW)

    wire.greet(4, 3)
    for made in y_du:
        made.start()
    gate.step1()

    def attend(m, between=None):
        rows_at = row_places(wire, quarter, 1)
        attend_back_one(
            scale, [key_places(wire, quarter, 4, 0, (core,)) for core in range(2)], rows_at,
            sequence_starts(lengths, m, rows_at), dyl.at[m], out_proj, q_up, q[m], kv[m], o[m],
            lse[m], cos[m], sin[m], dqp.at[m], dqn_send.at[m], dqn_keep.at[m], kv_send.at[m],
            kv_keep.at[m], dq_acc, between,
        )
        core_kv[m].start()
        dqn_sum[m].core.start()

    split = lambda ref, m: ref[m].reshape(8, 2, quarter, 2 * wide)

    def kv_cross(m):
        dqn_sum[m].pass_on()
        core_kv[m].wait_recv()
        kv_out[m] = (
            split(kv_keep, m)[:, 1].astype(F32) + split(kv_got, m)[:, 1].astype(F32)
        ).astype(LOW)
        cross_kv[m].start()

    def kv_sum(m, span):
        return (
            split(kv_keep, m)[span, 0].astype(F32) + split(kv_got, m)[span, 0].astype(F32)
            + kv_back[m, span].astype(F32)
        )

    def kv_side(m):
        cross_kv[m].wait_recv()
        side_out[m] = kv_sum(m, slice(4, 8)).astype(LOW)
        side_kv[m].start()

    def kv_line(m):
        side_kv[m].wait_recv()
        own = kv_sum(m, slice(0, 4)) + side_got[m].astype(F32)
        kv_own[m] = own[0]
        for d in range(1, 4):
            line_out[m, d - 1] = own[d].astype(LOW)
            pl.when(place >= d)(line_kv[m][d - 1].start)

    def latent(m):
        dqn = dqn_sum[m].result()[0]
        gain = jnp.sum(dqn * chat[m], axis=0, keepdims=True)
        gain_sum[...] = gain if m == 0 else gain_sum[...] + gain
        back = dqn * gain_c[...]
        both[m, :quarter, :rank] = (
            inv_c[m] * (back - chat[m] * mean_of(back * chat[m]))
        ).astype(LOW)

    def start_up():
        for made in y_du:
            made.wait_recv()
        up.step1()

    attend(0)
    kv_cross(0)
    gate.step2()
    attend(1, start_up)
    gate.step3()
    kv_cross(1)
    kv_side(0)
    latent(0)
    up.step2()
    latent(1)
    for z in range(4):
        side_sums[z] = terms_sum([(qn_theirs[m][z], dqp[m]) for m in range(2)]).astype(LOW)
    kv_side(1)
    side_dyl = wire.send(dyl_theirs, dyl_got, wire.beside)
    side_qup = wire.send(side_sums, qup_side, wire.beside)
    kv_line(0)
    kv_line(1)
    gate.finish()
    for m in range(2):
        for d in range(1, 4):
            pl.when(place <= 3 - d)(line_kv[m][d - 1].wait_recv)
        total = kv_own[m]
        for d in range(1, 4):
            total = total + line_got[m, d - 1].astype(F32)
        both[m, :quarter, rank : rank + wide] = unrotate(
            total[:, :wide], cos[m, :quarter], sin[m, :quarter]
        ).astype(LOW)
        both[m, :quarter, rank + wide :] = total[:, wide:].astype(LOW)
    cross_both = wire.send(both.at[:, :quarter, :], both.at[:, quarter:half, :], wire.cross)
    up.step3()
    cross_both.wait_recv()
    core_both = wire.send(both.at[:, :half, :], both.at[:, half:, :], wire.core)
    side_dyl.wait_recv()
    core_dyl = wire.send(dyl_got, dyl_far, wire.core)
    core_both.wait_recv()
    part = rank // 4
    kv_part = wide // 2
    dfirst[:, :, :part] = both[:, :, pl.ds(pl.multiple_of(wire.mp * part, part), part)]
    dfirst[:, :, part:] = both[
        :, :, pl.ds(pl.multiple_of(rank + wire.mp * kv_part, kv_part), kv_part)
    ]
    up.finish()
    core_dyl.wait_recv()
    side_qup.wait_recv()
    for made in [*y_du, *core_kv, *cross_kv, *side_kv, cross_both, core_both, side_dyl, core_dyl,
                 side_qup]:
        made.wait_send()
    for m in range(2):
        dqn_sum[m].end()
        for d in range(1, 4):
            pl.when(place >= d)(line_kv[m][d - 1].wait_send)
    gate.settle()
    up.settle()


def back3_body(quarter, *refs):
    refs = list(refs)
    take = lambda n: [refs.pop(0) for _ in range(n)]
    dfirst, weights = take(2)
    h1_mine, h1_theirs, o, oo = (take(2) for _ in range(4))
    dyl_mine, dyl_got, dyl_far = take(3)
    qn_mine = take(2)
    dqp, qup_side, n1, inv1, dy, gain1, gain2_sum, gain_c_sum, layer_own = take(9)
    grad_out, grad_qup, grad_qdown, grad_kv, grad_tokens, gains, layer_out = take(7)
    got_a, out_a, got_b, out_b, got_c, out_c = take(6)
    side_sums, side_got = take(2)
    send, kept, row_got, row_out, row_back = take(5)
    kv_out, kv_got = take(2)
    sums, sums_core, sums_cross, sums_side, sums_line = take(5)
    wire = Wire(*take(2))
    half, rows = 2 * quarter, 4 * quarter
    place = wire.place
    wire.greet(4, 3, diagonal=True)

    for z in range(4):
        side_sums[z] = terms_sum([(h1_theirs[m][z], dfirst[m]) for m in range(2)]).astype(LOW)
    side_first = wire.send(side_sums, side_got, wire.beside)

    def out_term(z):
        return terms_sum(halves_terms(
            [dyl_mine[m, z] for m in range(2)], [dyl_got[m, z] for m in range(2)],
            [dyl_far[m, z] for m in range(2)], (*o, *oo), half))

    def qup_term(z):
        return terms_sum([(qn_mine[m][z], dqp[m]) for m in range(2)]) + qup_side[z].astype(F32)

    def first_term(z):
        return terms_sum([(h1_mine[m][z], dfirst[m]) for m in range(2)]) + side_got[z].astype(F32)

    def keep_out(total):
        grad_out[...] = jnp.transpose(total)

    def keep_qup(total):
        grad_qup[...] = total

    part = grad_qdown.shape[1]

    def keep_first(total):
        grad_qdown[...] = total[:, :part]
        kv_out[...] = total[:, part:]

    out = LineSum(wire, out_term, (got_a, out_a), *grad_out.shape[::-1], keep_out)
    qup = LineSum(wire, qup_term, (got_b, out_b), *grad_qup.shape, keep_qup)
    first = LineSum(wire, first_term, (got_c, out_c), kv_out.shape[0], dfirst.shape[2], keep_first)
    for chain in (out, qup, first):
        chain.clear()
    row_sum = RowSum(wire, send, kept, row_got, row_out, row_back, quarter)
    out.step1()
    term = inner_cols(dfirst[...].reshape(2 * rows, dfirst.shape[2]), weights[...])
    for m in range(2):
        send[m] = term[m * rows + half : (m + 1) * rows].astype(LOW)
        kept[m] = term[m * rows : m * rows + half]
    row_sum.core.start()
    qup.step1()
    row_sum.pass_on()
    layer_share = Share(wire, layer_out, quarter)
    layer_share.begin(layer_own[...])
    out.step2()
    side_first.wait_recv()
    first.step1()
    qup.step2()
    dh1 = row_sum.result()
    gain1_sum = jnp.sum(jnp.sum(dh1 * n1[...], axis=0), axis=0, keepdims=True)
    back = dh1 * gain1[...]
    share = Share(wire, grad_tokens, quarter)
    share.begin(
        (dy[...] + inv1[...] * (back - n1[...] * mean_of(back * n1[...]))).astype(LOW)
    )
    w, r = gain1_sum.shape[1] // 8, gain_c_sum.shape[1] // 8
    for s in range(8):
        sums[s] = jnp.concatenate(
            [gain1_sum[:, s * w : (s + 1) * w], gain2_sum[:, s * w : (s + 1) * w],
             gain_c_sum[:, s * r : (s + 1) * r]], axis=1
        )
    core_sums = wire.send(sums, sums_core, wire.core)
    out.step3()
    core_sums.wait_recv()
    core_sums.wait_send()
    sums[...] = sums[...] + sums_core[...]
    cross_sums = wire.send(sums, sums_cross, wire.cross)
    qup.step3()
    first.step2()
    cross_sums.wait_recv()
    cross_sums.wait_send()
    sums[...] = sums[...] + sums_cross[...]
    side_of = lambda p, s: sums.at[2 * p + s]
    side_sends = [
        wire.send(side_of(p, 1 - wire.side), sums_side.at[p], wire.beside) for p in range(4)
    ]
    layer_share.forward()
    share.forward()
    first.step3()
    for made in side_sends:
        made.wait_recv()
        made.wait_send()
    line_sends = []
    for d in range(1, 4):
        for way, there in ((1, place + d <= 3), (-1, place - d >= 0)):
            index = 2 * (d - 1) + (way < 0)
            line_sends.append(
                (wire.copy(sums_line.at[6 + index], sums_line.at[index],
                           {"seq": wire.seq + 2 * way * d}), d, way, there)
            )

            @pl.when(there)
            def _(index=index, d=d, way=way):
                to = place + way * d
                sums_line[6 + index] = sums[2 * to + wire.side] + sums_side[to]
                line_sends[-1][0].start()

            @pl.when((place - way * d < 0) | (place - way * d > 3))
            def _(index=index):
                sums_line[index] = jnp.zeros(sums_line.shape[1:], F32)

    out.finish()
    qup.finish()
    first.finish()
    cores = []
    size = kv_out.shape[0] // 4
    for k in range(4):
        rows_of = pl.ds(pl.multiple_of(wire.blocks[k] * size, size), size)
        if k:
            device = {"mp": wire.blocks[k]}
            cores.append(wire.send(kv_out.at[rows_of], kv_got.at[k], device))
        else:
            kv_got[0] = kv_out[rows_of]
    total = sums[2 * place + wire.side] + sums_side[place]
    for made, d, way, there in line_sends:
        pl.when((place - way * d >= 0) & (place - way * d <= 3))(made.wait_recv)
    for index in range(6):
        total = total + sums_line[index]
    gains[...] = total
    for made in cores:
        made.wait_recv()
    columns = kv_out.shape[1]
    for k in range(4):
        at = pl.ds(pl.multiple_of(wire.blocks[k] * columns, columns), columns)
        grad_kv[:, at] = kv_got[k]
    share.end()
    layer_share.end()
    for made in (side_first, *cores):
        made.wait_send()
    for made, d, way, there in line_sends:
        pl.when(there)(made.wait_send)
    row_sum.end()
    for chain in (out, qup, first):
        chain.settle()


def attend_one(
    scale, mp_blocks, c, gain, q_up, cos, sin, kv, key_ids, row_ids, row_starts, out_proj,
    qn, q, o, lse, send, keep, chat_out, inverse_out,
):
    rows = qn.shape[0]
    half, quarter = rows // 2, rows // 4
    part = c.shape[2]
    wide = q.shape[2]
    cut = lambda k, i: c[k, i * quarter : (i + 1) * quarter, :]
    pieces = [jnp.concatenate([cut(k, i ^ k) for i in range(4)], 0) for k in range(4)]
    latent = jnp.concatenate(pieces, 1).astype(F32)
    inverse = inverse_rms(latent)
    chat = latent * inverse
    inverse_out[...] = inverse[:quarter]
    for k in range(4):
        columns = pl.ds(pl.multiple_of(mp_blocks[k] * part, part), part)
        chat_out[:, columns] = chat[:quarter, k * part : (k + 1) * part]
        qn[:, columns] = (chat[:, k * part : (k + 1) * part] * gain[:, columns]).astype(LOW)
    bias = jnp.where((key_ids >= row_starts) & (key_ids <= row_ids), 0.0, NEG_LARGE)
    low = qn[...]
    for h in range(q.shape[0]):
        pre = dot(low, q_up[:, h * wide : (h + 1) * wide])
        q_h = (rotate(pre, cos, sin) * scale).astype(LOW)
        q[h] = q_h
        scores = inner_cols(q_h, kv[:, :wide]) + bias
        top = jnp.max(scores, axis=-1, keepdims=True)
        probs = jnp.exp(scores - top)
        total = jnp.sum(probs, axis=-1, keepdims=True)
        out = dot(probs.astype(LOW), kv[:, wide:]) / total
        o[:, h * wide : (h + 1) * wide] = out.astype(LOW)
        log_total = jnp.broadcast_to(top + jnp.log(total), (rows, 128))
        lse[h : h + 1, :] = jnp.transpose(log_total)[:1]
    keep[...] = dot(o[:half, :], out_proj[...])
    send[...] = dot(o[half:, :], out_proj[...]).astype(LOW)


def fore1_body(scale, *refs):
    refs = list(refs)
    take = lambda n: [refs.pop(0) for _ in range(n)]
    tokens, cotangent, q_down, kv_proj, q_up, out_proj, w_down = take(7)
    lengths, gain1, gain_c, gain2, cosine, sine = take(6)
    h1_mine, h1_theirs, qn_mine, qn_theirs = (take(2) for _ in range(4))
    qs, os, lses, kvs, oo, dz_got = (take(2) for _ in range(6))
    dz, dz_mine, dhid, chat, inv_c, y_out, n2_out, inv2_out, n1_out, inv1_out, h2 = take(11)
    x, down_w, kv_w, up_w, out_w, back_w, h1, c, qn, dz_theirs = take(10)
    send, kept, got, cross_out, cross_got = take(5)
    loads = take(1)[0]
    wire = Wire(*take(2))
    place, blocks = wire.place, wire.blocks
    rows = x.shape[1]
    half, quarter = rows // 2, rows // 4
    wide = kv_proj.shape[1] // 2

    started = []

    def load(source, target):
        made = pltpu.make_async_copy(source, target, loads.at[len(started)])
        made.start()
        started.append(made)
        return made

    def load_rows(source, target):
        return [
            load(source.at[pl.ds(pl.multiple_of(blocks[k] * quarter, quarter), quarter), :],
                 target.at[k * quarter : (k + 1) * quarter, :])
            for k in range(4)
        ]

    in_x = [load_rows(tokens.at[0], x.at[0])]
    in_kv = load(kv_proj, kv_w)
    in_x.append(load_rows(tokens.at[1], x.at[1]))
    in_down = load(q_down, down_w)
    in_dz = [load_rows(cotangent.at[m], dz.at[m]) for m in range(2)]
    in_back, in_up, in_out = load(w_down, back_w), load(q_up, up_w), load(out_proj, out_w)

    line_kv, side_kv, core_kv, cross_c, core_c = [], [], [], [], []
    for m in range(2):
        for d in range(1, 4):

            @pl.when(place < d)
            def _(m=m, d=d):
                kvs[m][0, :, d] = jnp.zeros(kvs[m].shape[1:2] + kvs[m].shape[3:], LOW)
                kvs[m][1, :, d] = jnp.zeros(kvs[m].shape[1:2] + kvs[m].shape[3:], LOW)

        own = kvs[m].at[0, 0, 0]
        line_kv.append([
            wire.copy(own, kvs[m].at[0, 0, d], {"seq": wire.seq + 2 * d}) for d in range(1, 4)
        ])
        side_kv.append([
            wire.copy(kvs[m].at[0, 0, d], kvs[m].at[0, 1, d], wire.beside) for d in range(4)
        ])
        core_kv.append([
            wire.copy(kvs[m].at[0, :, d], kvs[m].at[1, :, d], wire.core) for d in range(4)
        ])
        cross_c.append(wire.copy(c.at[m, 0], c.at[m, 1], wire.cross))
        core_c.append([
            wire.copy(c.at[m, 0], c.at[m, 2], wire.core),
            wire.copy(c.at[m, 1], c.at[m, 3], wire.core),
        ])
    wire.greet(4, 3)

    for m in range(2):
        cos, sin = cosine[m], sine[m]
        for made in in_x[m]:
            made.wait()
        if m == 0:
            in_kv.wait()
        values = x[m].astype(F32)
        inverse = inverse_rms(values)
        normed = values * inverse
        n1_out[m], inv1_out[m] = normed[:quarter], inverse[:quarter]
        low = (normed * gain1[...]).astype(LOW)
        h1[...] = low
        pair = dot(low[:half], kv_w[...])
        own = kvs[m].at[0, 0, 0]
        own[:, :wide] = rotate(pair[:, :wide], cos[:half], sin[:half]).astype(LOW)
        own[:, wide:] = pair[:, wide:].astype(LOW)
        for d in (3, 2, 1):
            pl.when(place + d <= 3)(line_kv[m][d - 1].start)
        side_kv[m][0].start()
        if m == 0:
            in_down.wait()
        c[m, 0] = dot(low, down_w[...]).astype(LOW)
        cross_c[m].start()
        core_c[m][0].start()
        side_columns(h1, h1_mine[m], h1_theirs[m], wire.side)

    def pass_kv(m, d):
        @pl.when(place >= d)
        def _():
            line_kv[m][d - 1].wait_recv()
            side_kv[m][d].start()

    def pass_core(m, d):
        @pl.when(place >= d)
        def _():
            side_kv[m][d].wait_recv()
            core_kv[m][d].start()

    in_back.wait()
    for m in range(2):
        for made in in_dz[m]:
            made.wait()
    dhid[0] = inner_cols(dz[0], back_w[...])
    for d in (1, 2, 3):
        pass_kv(0, d)
    pass_core(0, 0)
    for m in range(2):
        cross_c[m].wait_recv()
        core_c[m][1].start()
    dhid[1] = inner_cols(dz[1], back_w[...])
    for d in (1, 2, 3):
        pass_kv(1, d)
    for m in range(2):
        side_columns(dz.at[m], dz_mine.at[m], dz_theirs.at[m], wire.side)
    for d in (1, 2, 3):
        pass_core(0, d)
    in_up.wait()
    in_out.wait()
    sums = [
        RowSum(wire, send.at[m : m + 1], kept.at[m : m + 1], got.at[m : m + 1],
               cross_out.at[m : m + 1], cross_got.at[m : m + 1], quarter)
        for m in range(2)
    ]
    side_o, shares = [], []

    def after_sum(m):
        value = x[m, :quarter, :].astype(F32) + sums[m].result()[0]
        inverse = inverse_rms(value)
        normed = value * inverse
        y_out[m], n2_out[m], inv2_out[m] = value, normed, inverse
        h2[m, :quarter, :] = (normed * gain2[...]).astype(LOW)
        spot = lambda k: h2.at[m, k * quarter : (k + 1) * quarter, :]
        shares.append((
            wire.send(spot(0), spot(1), wire.cross), wire.send(spot(0), spot(2), wire.core),
            wire.copy(spot(1), spot(3), wire.core),
        ))

    for m in range(2):
        if m == 1:
            for d in range(4):
                pass_core(1, d)
        for d in range(4):
            pl.when(place >= d)(core_kv[m][d].wait_recv)
        for made in core_c[m]:
            made.wait_recv()
        rows_at = row_places(wire, quarter, 0)
        attend_one(
            scale, blocks, c.at[m], gain_c, up_w, cosine[m], sine[m],
            kvs[m][...].reshape(2 * 2 * 4 * half, 2 * wide),
            key_places(wire, quarter, 4, 1, (0, 1)), rows_at,
            sequence_starts(lengths, m, rows_at), out_w, qn, qs[m], os[m], lses[m], send.at[m], kept.at[m],
            chat.at[m], inv_c.at[m],
        )
        sums[m].core.start()
        if m == 0:
            side_dz = wire.send(dz_theirs, dz_got[0], wire.beside)
        side_o.append(wire.send(os[m], oo[m], wire.beside))
        side_columns(qn, qn_mine[m], qn_theirs[m], wire.side)
        if m == 1:
            after_sum(0)
        sums[m].pass_on()
    after_sum(1)
    side_dz.wait_recv()
    core_dz = wire.send(dz_got[0], dz_got[1], wire.core)
    for near, _, far in shares:
        near.wait_recv()
        far.start()
    for _, first, far in shares:
        first.wait_recv()
        far.wait_recv()
    core_dz.wait_recv()
    for made in side_o:
        made.wait_recv()
    for made in [side_dz, core_dz, *side_o, *cross_c, *(a for p in core_c for a in p),
                 *(a for p in shares for a in p)]:
        made.wait_send()
    for m in range(2):
        sums[m].end()
        for d in range(4):

            @pl.when(place >= d)
            def _(m=m, d=d):
                side_kv[m][d].wait_send()
                core_kv[m][d].wait_send()

        for d in range(1, 4):
            pl.when(place + d <= 3)(line_kv[m][d - 1].wait_send)


def deliver_body(count, *refs):
    results, gains = refs[:count], refs[count]
    outs, rooms, sems = refs[count + 1 : -count - 1], refs[-count - 1 : -1], refs[-1]
    loads = [pltpu.make_async_copy(results[i], rooms[i], sems.at[i]) for i in range(count)]
    stores = [
        pltpu.make_async_copy(rooms[i], outs[i], sems.at[count + i]) for i in range(count)
    ]
    for made in loads:
        made.start()
    at = 0
    for ref in outs[count:]:
        ref[...] = gains[0, at : at + ref.shape[0]]
        at += ref.shape[0]
    for load, store in zip(loads, stores):
        load.wait()
        store.start()
    for made in stores:
        made.wait()


def local(
    tokens,
    lengths,
    norm1_gain,
    q_down,
    latent_gain,
    q_up,
    kv_proj,
    out_proj,
    norm2_gain,
    w_gate,
    w_up,
    w_down,
    cotangent,
):
    micro, rows, width = tokens.shape
    seq = lax.axis_size("seq")
    line = seq // 2
    at = lax.axis_index("seq").astype(jnp.int32)
    me = lax.axis_index("mp").astype(jnp.int32)
    place, side = at // 2, at % 2
    ids = jnp.stack([me, side])
    quarter, half = rows // 4, rows // 2
    head_dim = kv_proj.shape[1] // 2
    heads = q_up.shape[1] // head_dim
    part = q_down.shape[1]
    rank = q_up.shape[0]
    hidden = w_gate.shape[1]
    kv_part = kv_proj.shape[1] // 4
    wide = width // seq
    scale = head_dim ** (-0.5)
    key_count = seq * rows
    beside = [(i, i ^ 1) for i in range(seq)]
    narrow = line == 4 and micro == 2 and key_count <= 2048 and not wide % 128

    def swap(index):
        return ((index & 1) << 1) | (index >> 1)

    def to_natural(array, axis):
        size = array.shape[axis] // 4
        return jnp.concatenate(
            [lax.dynamic_slice_in_dim(array, swap(me ^ b) * size, size, axis) for b in range(4)],
            axis,
        )

    def other(array):
        return lax.ppermute(array, "seq", beside)

    def sum_mp(send, keep):
        kept = keep + lax.ppermute(send, "mp", CORE).astype(F32)
        got = lax.ppermute(kept[..., quarter:, :].astype(LOW), "mp", CROSS)
        return kept[..., :quarter, :] + got.astype(F32)

    def gather_mp(piece):
        near = lax.ppermute(piece, "mp", CROSS)
        pair = jnp.concatenate([piece, near], -2)
        return piece, near, lax.ppermute(pair, "mp", CORE)

    def sides_shape(columns, their_rows, lead=()):
        if columns // seq % 128:
            return []
        return [
            whole((*lead, line, n, columns // seq), LOW) for n in (rows, their_rows)
        ]

    def split_sides(made, full, their_rows):
        if made:
            return made
        split = full.reshape(*full.shape[:-1], line, 2, full.shape[-1] // seq)
        mine, theirs = (
            jnp.moveaxis(lax.dynamic_index_in_dim(split, i, split.ndim - 2, keepdims=False), -2, -3)
            for i in (side, 1 - side)
        )
        return mine, theirs[..., :their_rows, :]

    def from_other(theirs):
        got = other(theirs)
        return got, lax.ppermute(got, "mp", CORE)

    def without_sides(body, count):
        return body if count else lambda *refs: body(*refs, None, None)

    def both_sides(mine, got):
        lefts, spans = [], []
        for array, first, count, partner in (
            (mine, 0, rows, 0), (got[0], 0, half, 1), (got[1], half, half, 1)
        ):
            stacked_array = not isinstance(array, list)
            for m in range(micro):
                spans.append((len(lefts) if not stacked_array else len(lefts), m if stacked_array else None,
                              m, partner, first, count))
                if not stacked_array:
                    lefts.append(array[m])
            if stacked_array:
                lefts.append(array)
        return lefts, spans

    class Chain:
        def __init__(self, lefts, rights, terms, shape, turned=False, from_side=None):
            self.args = [*lefts, *rights]
            self.spec = (terms, len(lefts), len(rights))
            self.shape, self.turned = shape, turned
            self.from_side = [] if from_side is None else [from_side]
            self.step, self.up, self.down = 0, None, None

        def block(self, index, added, after, last=False):
            turned = last and self.turned
            body = functools.partial(
                block_body, *self.spec, len(added), len(self.from_side), turned
            )
            shape = self.shape[::-1] if turned else self.shape
            return run(
                body, index.reshape(1), [*self.args, *added, *self.from_side],
                [whole(shape, F32 if last else LOW)], after, name="block",
            )[0]

        def advance(self, after):
            self.step += 1
            step = self.step
            goes_up = [(i, i + 2) for i in range(2 * step)]
            goes_down = [(seq - 1 - i, seq - 3 - i) for i in range(2 * step)]
            for_up, for_down = line - step + place, step - line + place
            if 2 * step < line + 1:
                which = jnp.where(
                    place <= step - 1, for_up, jnp.where(place >= line - step, for_down, 0)
                )
                term = self.block(which, [a for a in (self.up, self.down) if a is not None], after)
                if step == 1 and line > 3:
                    self.up = lax.ppermute(term, "seq", goes_up + goes_down)
                else:
                    self.up = lax.ppermute(term, "seq", goes_up)
                    self.down = lax.ppermute(term, "seq", goes_down)
                return [term]
            term_up = self.block(jnp.clip(for_up, 0, line - 1), [self.up], after)
            term_down = self.block(jnp.clip(for_down, 0, line - 1), [self.down], [term_up])
            self.up = lax.ppermute(term_up, "seq", goes_up)
            self.down = lax.ppermute(term_down, "seq", goes_down)
            return [term_down]

        def finish(self, after):
            while self.step < line - 1:
                after = self.advance(after)
            result = self.block(place, [self.up, self.down], after, last=True)
            return result, [result]

    quarter_rows = jnp.arange(quarter, dtype=jnp.int32)
    row_ids = at * rows + jnp.concatenate([(me ^ k) * quarter + quarter_rows for k in ORDER])
    key_ids = (
        ((place - jnp.arange(line, dtype=jnp.int32)[None, None, :, None, None]) * 2
         + (side ^ jnp.arange(2, dtype=jnp.int32)[None, :, None, None, None])) * rows
        + (me ^ (jnp.arange(2, dtype=jnp.int32)[:, None, None, None, None]
                 + 2 * jnp.arange(2, dtype=jnp.int32)[None, None, None, :, None])) * quarter
        + quarter_rows[None, None, None, None, :]
    ).reshape(key_count)

    gain1_row, gain2_row, gain_c_row = norm1_gain[None, :], norm2_gain[None, :], latent_gain[None, :]
    kv_cols = lax.dynamic_slice_in_dim(kv_proj, me * kv_part, kv_part, 1)
    first_weights = jnp.concatenate([q_down, kv_cols], axis=1)
    low = lambda *shape: pltpu.VMEM(shape, LOW)
    full = lambda *shape: pltpu.VMEM(shape, F32)
    near = lambda *arrays: [(1, a) for a in arrays]
    far = lambda *arrays: [(0, a) for a in arrays]
    columns = heads * head_dim
    side_rows = rank // seq
    first_columns = part + kv_part

    def narrow_layer():
        numbers = lambda array: [(2, array)]
        ends = jnp.cumsum(lengths, axis=1)
        first_end, second_end = ends[:, 0:1], ends[:, 1:2]
        places = row_ids[None, :] - jnp.where(
            row_ids >= second_end, second_end, jnp.where(row_ids >= first_end, first_end, 0)
        )
        freqs = BASE ** (-2.0 * jnp.arange(head_dim // 2, dtype=F32) / head_dim)
        angles = places.astype(F32)[:, :, None] * freqs
        cosine, sine = jnp.cos(angles), jnp.sin(angles)
        row_shape = whole((micro, quarter, width), F32)
        one_shape = whole((micro, quarter, 1), F32)
        side_shape = whole((micro, line, half, wide), LOW)
        args = far(tokens, cotangent, q_down, kv_proj, q_up, out_proj, w_down)
        args += numbers(lengths) + near(gain1_row, gain_c_row, gain2_row, cosine, sine)
        outs = near(*[whole((line, rows, wide), LOW)] * 4, *[whole((line, rows, side_rows), LOW)] * 4)
        outs += near(*[whole((heads, rows, head_dim), LOW)] * 2, *[whole((rows, columns), LOW)] * 2)
        outs += near(*[whole((heads, rows), F32)] * 2)
        outs += near(*[whole((2, 2, line, half, 2 * head_dim), LOW)] * 2)
        outs += far(*[whole((rows, columns), LOW)] * 2, *[side_shape] * 2)
        outs += near(
            whole((micro, rows, width), LOW), whole((micro, line, rows, wide), LOW),
            whole((micro, rows, hidden), F32), whole((micro, quarter, rank), F32), one_shape,
            row_shape, row_shape, one_shape, row_shape, one_shape,
            whole((micro, rows, width), LOW),
        )
        made = list(mesh_run(
            functools.partial(fore1_body, scale), args, outs,
            [low(micro, rows, width), low(width, part), low(width, 2 * head_dim),
             low(rank, columns), low(columns, width), low(hidden, width), low(rows, width),
             low(micro, 4, rows, part), low(rows, rank), low(micro, line, half, wide),
             low(micro, half, width), full(micro, half, width), low(micro, half, width),
             low(micro, quarter, width), low(micro, quarter, width),
             pltpu.SemaphoreType.DMA((24,))],
            4, "fore1", 60, 60,
        ))
        give = lambda n: [made.pop(0) for _ in range(n)]
        h1_mine, h1_theirs, qn_mine, qn_theirs = (give(2) for _ in range(4))
        qs, os, lses, kv, o_other, dz_got = (give(2) for _ in range(6))
        kv = [a.reshape(key_count, 2 * head_dim) for a in kv]
        dz, dz_mine, dhid, chat, inv_c, y, n2, inv2, n1, inv1, h2 = give(11)

        ahead = hidden * 3 // 11 // 128 * 128
        args = far(w_gate, w_up, w_down) + near(h2, dhid, n2, inv2, dz, gain2_row, dz_mine)
        args += near(*dz_got, y)
        outs = near(
            whole((hidden, wide), F32), row_shape, whole((1, width), F32),
            whole((micro, rows, width), LOW), whole((micro, line, rows, wide), LOW), side_shape,
            whole((micro, quarter, width), LOW), *[whole((rows, hidden), LOW)] * 6, *[whole((line, rows, wide), LOW)] * 2,
        ) + far(*[whole((line, half, wide), LOW)] * 4, *[whole((rows, hidden), LOW)] * 2)
        made = list(mesh_run(
            functools.partial(back1_body, quarter), args, outs,
            [low(width, hidden), low(width, hidden), low(rows, hidden - ahead),
             low(rows, hidden - ahead), low(micro, line, half, wide),
             low(5, wide, hidden - ahead), low(2, wide, hidden - ahead),
             low(micro, half, width), full(micro, half, width), low(micro, half, width),
             low(micro, quarter, width), low(micro, quarter, width),
             pltpu.SemaphoreType.DMA((2,)), low(micro, half, width), full(micro, half, width),
             low(micro, half, width), low(micro, quarter, width), low(micro, quarter, width),
             low(5, 2 * wide, ahead), low(2, 2 * wide, ahead), full(2, wide, ahead),
             low(wide, ahead), low(wide, ahead)],
            1, "back1", 62, 40,
        ))
        grad_down, dy, gain2, dyl, dyl_mine, dyl_theirs, layer_own = give(7)
        hid, dg, du, h2_mine, h2_got, h2_far, dg_other = (give(2) for _ in range(7))

        args = numbers(lengths) + near(*dg, *dg_other, *du, *h2_mine, *h2_got, *h2_far)
        args += near(dyl, out_proj, q_up, *qs, *kv, *os, *lses, cosine, sine, chat, inv_c,
                     gain_c_row) + far(dyl_theirs) + near(*qn_theirs)
        outs = near(whole((wide, hidden), F32), whole((wide, hidden), F32),
                    whole((micro, rows, first_columns), LOW), whole((1, rank), F32),
                    whole((micro, rows, columns), LOW))
        outs += far(side_shape, side_shape, whole((line, side_rows, columns), LOW))
        kv_low = lambda *lead: low(*lead, quarter, 2 * head_dim)
        key_half = key_count // 2
        grad_gate, grad_up, dfirst, gain_c, dqp, dyl_got, dyl_far, qup_side = mesh_run(
            functools.partial(back2_body, quarter, scale), args, outs,
            [low(rows, hidden), low(rows, hidden), low(5, wide, hidden), low(2, wide, hidden),
             low(5, wide, hidden), low(2, wide, hidden), full(heads * rows, head_dim),
             low(micro, half, rank),
             full(micro, half, rank), low(micro, key_half, 2 * head_dim),
             low(micro, key_half, 2 * head_dim), low(micro, half, rank),
             low(micro, quarter, rank), low(micro, quarter, rank),
             low(micro, key_half, 2 * head_dim), kv_low(micro, 2 * line), kv_low(micro, 2 * line),
             kv_low(micro, line), kv_low(micro, line), kv_low(micro, 3), kv_low(micro, 3),
             full(micro, quarter, 2 * head_dim), low(micro, rows, rank + 2 * head_dim),
             low(line, side_rows, columns)],
            2, "back2", 62, 44,
        )

        kv_cols = lax.dynamic_slice_in_dim(kv_proj, me * kv_part, kv_part, 1)
        first_weights = jnp.concatenate([q_down, kv_cols], axis=1)
        args = near(dfirst, first_weights, *h1_mine, *h1_theirs, *os, *o_other, dyl_mine, dyl_got,
                    dyl_far, *qn_mine, dqp, qup_side, n1, inv1, dy, gain1_row, gain2, gain_c,
                    layer_own)
        block = width // 4 // seq
        gain_columns = 2 * wide + side_rows
        outs = near(whole((columns, wide), F32), whole((side_rows, columns), F32),
                    whole((wide, part), F32), whole((block, 2 * head_dim), F32),
                    whole((micro, rows, width), LOW), whole((1, gain_columns), F32),
                    whole((micro, rows, width), LOW))
        grad_out, grad_qup, grad_qdown, grad_kv, input_grads, gains, layer_out = mesh_run(
            functools.partial(back3_body, quarter), args, outs,
            [low(5, wide, columns), low(2, wide, columns), low(5, side_rows, columns),
             low(2, side_rows, columns), low(5, wide, first_columns),
             low(2, wide, first_columns), low(line, wide, first_columns),
             low(line, wide, first_columns), low(micro, half, width), full(micro, half, width),
             low(micro, half, width), low(micro, quarter, width), low(micro, quarter, width),
             full(wide, kv_part), full(4, block, kv_part), full(seq, 1, gain_columns),
             full(seq, 1, gain_columns), full(seq, 1, gain_columns), full(line, 1, gain_columns),
             full(12, 1, gain_columns)],
            3, "back3", 60, 44,
        )
        results = [layer_out, input_grads, grad_qdown, grad_qup, grad_kv, grad_out, grad_gate,
                   grad_up, grad_down]
        made = pl.pallas_call(
            functools.partial(deliver_body, len(results)),
            in_specs=[pl.BlockSpec(memory_space=pl.ANY)] * len(results) + [in_vmem()],
            out_specs=[pl.BlockSpec(memory_space=pl.ANY)] * len(results) + [in_vmem()] * 3,
            out_shape=[whole(a.shape, a.dtype) for a in results]
            + [whole((n,), F32) for n in (wide, wide, side_rows)],
            scratch_shapes=[pltpu.VMEM(a.shape, a.dtype) for a in results]
            + [pltpu.SemaphoreType.DMA((2 * len(results),))],
            compiler_params=pltpu.CompilerParams(vmem_limit_bytes=40 << 20),
            name="deliver",
        )(*results, gains)
        (layer_out, input_grads, grad_qdown, grad_qup, grad_kv, grad_out, grad_gate, grad_up,
         grad_down, grad_n1, grad_n2, grad_c) = made
        return (
            layer_out, input_grads, grad_n1, grad_qdown, grad_c, grad_qup, grad_kv, grad_out,
            grad_n2, grad_gate, grad_up, grad_down,
        )

    if narrow:
        return narrow_layer()

    both_rows = sides_shape(width, rows)
    half_rows = sides_shape(width, half)
    rank_sides = sides_shape(rank, rows)

    tables, starts, kv, c_part, h1_sides = [], [], [], [], []
    order = []
    for m in range(micro):
        _, places = documents(lengths[m], row_ids)
        starts.append(row_ids - places)
        tables.append(rotation(places, head_dim))
        c, packed, h1, *made = run(
            without_sides(functools.partial(first_body, m, quarter), len(both_rows)),
            ids,
            [tokens, gain1_row, q_down, kv_proj, *tables[m]],
            [whole((rows, part), LOW), whole((half, 2 * head_dim), LOW), whole((rows, width), LOW),
             *both_rows],
            order,
            name="first",
        )
        order = [c]
        blocks = [packed] + [
            lax.ppermute(packed, "seq", [(i, i + 2 * d) for i in range(seq - 2 * d)])
            for d in range(1, line)
        ]
        near = jnp.stack(blocks, 0)
        near = jnp.stack([near, other(near)], 0)
        kv.append(
            jnp.stack([near, lax.ppermute(near, "mp", CORE)], 0).reshape(key_count, 2 * head_dim)
        )
        c_part.append(c)
        h1_sides.append(split_sides(made, h1, rows))

    dhid, dz, *made = run(
        functools.partial(cotangent_body, micro, quarter),
        ids,
        [cotangent, w_down],
        [whole((micro, rows, hidden), F32), whole((micro, rows, width), LOW),
         *sides_shape(width, half, (micro,))],
        order,
        name="cotangent",
    )
    order = [dz]
    dz_mine, dz_theirs = split_sides(made, dz, half)
    dz_got = from_other(dz_theirs)

    qn_sides, qs, os, lses, sums, c_rows = [], [], [], [], [], []
    for m in range(micro):
        near = lax.ppermute(c_part[m], "mp", CROSS)
        swapped = jnp.concatenate(
            [near[quarter : 2 * quarter], near[:quarter], near[3 * quarter :],
             near[2 * quarter : 3 * quarter]], 0
        )
        far = lax.ppermute(jnp.concatenate([c_part[m], swapped], 1), "mp", CORE)
        qn, q, o, lse, send, keep, *made = run(
            without_sides(functools.partial(attend_body, scale), len(rank_sides)),
            ids,
            [c_part[m], near, far, gain_c_row, q_up, *tables[m], kv[m], key_ids[None, :],
             row_ids[:, None], starts[m][:, None], out_proj],
            [whole((rows, rank), LOW), whole((heads, rows, head_dim), LOW),
             whole((rows, heads * head_dim), LOW), whole((heads, rows), F32),
             whole((half, width), LOW), whole((half, width), F32), *rank_sides],
            order,
            name="attend",
        )
        order = [o]
        qn_sides.append(split_sides(made, qn, rows))
        qs.append(q)
        os.append(o)
        lses.append(lse)
        sums.append(sum_mp(send, keep))
        c_rows.append(
            jnp.concatenate([c_part[m][:quarter], swapped[:quarter], far[half : half + quarter]], 1)
        )

    h2_mine, h2_theirs, hid, dg, du, state = [], [], [], [], [], []
    for m in range(micro):
        x = lax.dynamic_slice_in_dim(tokens[m], me * quarter, quarter, 0).astype(F32)
        inv1 = inverse_rms(x)
        y = x + sums[m]
        inv2 = inverse_rms(y)
        n2 = y * inv2
        pieces = gather_mp((n2 * gain2_row).astype(LOW))
        h2, hid_m, dg_m, du_m, *made = run(
            without_sides(functools.partial(forward_body, m), len(half_rows)),
            ids,
            [*pieces, w_gate, w_up, dhid],
            [whole((rows, width), LOW), *[whole((rows, hidden), LOW)] * 3, *half_rows],
            order,
            name="forward",
        )
        order = [hid_m]
        mine, theirs = split_sides(made, h2, half)
        h2_mine.append(mine)
        h2_theirs.append(theirs)
        hid.append(hid_m)
        dg.append(dg_m)
        du.append(du_m)
        state.append(dict(x=x, n1=x * inv1, inv1=inv1, y=y, n2=n2, inv2=inv2, c=c_rows[m]))

    def stacked(name):
        return jnp.stack([st[name] for st in state], 0)

    def with_other(arrays):
        return [*arrays, *[other(a) for a in arrays]]

    def terms_of(spans):
        return [(a, lead, m + micro * partner, None, first, count)
                for a, lead, m, partner, first, count in spans]

    send, keep, ffn_send, ffn_keep = run(
        functools.partial(hidden_back_body, micro),
        ids,
        [*dg, *du, *hid, w_gate, w_up, w_down],
        [whole((micro, half, width), LOW), whole((micro, half, width), F32)] * 2,
        order,
        name="hidden_back",
    )
    lefts, spans = both_sides(dz_mine, dz_got)
    chain_down = Chain(lefts, with_other(hid), terms_of(spans), (wide, hidden), turned=True)
    lefts, spans = both_sides(h2_mine, [list(p) for p in zip(*[from_other(t) for t in h2_theirs])])
    chain_gate = Chain(lefts, with_other(dg), terms_of(spans), (wide, hidden))
    chain_up = Chain(lefts, with_other(du), terms_of(spans), (wide, hidden))

    order = chain_down.advance([send])
    dh2 = sum_mp(send, keep)
    y, n2, inv2, n1, inv1 = (stacked(k) for k in ("y", "n2", "inv2", "n1", "inv1"))
    dz_own = dz[:, :quarter].astype(F32)
    gain2 = jnp.sum(dh2 * n2, axis=(0, 1))
    dy = dz_own + norm_backward(dh2 * gain2_row, n2, inv2)
    for _ in range(2):
        order = chain_down.advance(order)
    order = chain_gate.advance(order)

    def attend_back(which, pieces):
        args = [*pieces, out_proj, q_up, key_ids[:, None]]
        for m in which:
            args += [qs[m], kv[m], os[m], lses[m], jnp.stack([row_ids, starts[m]], 0), *tables[m]]
        n = len(which)
        return run(
            functools.partial(attend_back_body, scale, n, min(1024, key_count // 2)),
            ids,
            args,
            [whole((n, rows, width), LOW), whole((n, rows, heads * head_dim), LOW),
             whole((n, half, rank), LOW), whole((n, half, rank), F32),
             whole((n, key_count // 2, 2 * head_dim), LOW),
             whole((n, key_count // 2, 2 * head_dim), F32), *sides_shape(width, half, (n,))],
            order,
            scratch=[pltpu.VMEM((heads, rows, head_dim), F32),
                     pltpu.VMEM((heads, rows, head_dim), LOW),
                     pltpu.VMEM((heads, 8, rows), F32)],
            name="attend_back",
            limit=56,
        )

    pieces = gather_mp(dy.astype(LOW))
    if key_count <= 2048:
        made = attend_back(range(micro), pieces)
    else:
        each = [attend_back([m], [p[m : m + 1] for p in pieces]) for m in range(micro)]
        made = [jnp.concatenate(parts, 0) for parts in zip(*each)]
    dyl, dqp, send, keep, kv_send, kv_keep, *made = made
    order = [send]
    dyl_mine, dyl_theirs = split_sides(made, dyl, half)
    lefts, spans = both_sides(dyl_mine, from_other(dyl_theirs))
    chain_out = Chain(lefts, with_other(os), terms_of(spans), (wide, heads * head_dim), turned=True)

    def side_sum(lefts, rights, shape, after):
        terms = [(m, None, 0, m, 0, rows) for m in range(micro)]
        (made,) = run(
            functools.partial(side_sum_body, terms, len(lefts)),
            ids,
            [*lefts, *rights],
            [whole((line, *shape), LOW)],
            after,
            name="side_sum",
        )
        return other(made), [made]

    def own_chain(side_pairs, right, shape, after):
        from_side, after = side_sum([p[1] for p in side_pairs], [right], shape, after)
        terms = [(m, None, 0, m, 0, rows) for m in range(micro)]
        return Chain([p[0] for p in side_pairs], [right], terms, shape, from_side=from_side), after

    shape = (rank // seq, heads * head_dim)
    chain_qup, order = own_chain(qn_sides, dqp, shape, order)
    order = chain_gate.advance(order)
    order = chain_up.advance(order)

    dqn = sum_mp(send, keep)
    c = stacked("c").astype(F32)
    inv_c = inverse_rms(c)
    chat = c * inv_c
    chat = to_natural(chat, 2)
    gain_c = jnp.sum(dqn * chat, axis=(0, 1))
    dc = norm_backward(dqn * gain_c_row, chat, inv_c).astype(LOW)

    dkv = kv_keep + lax.ppermute(kv_send, "mp", CORE).astype(F32)
    dkv = dkv.reshape(micro, 2, line, 2, quarter, 2 * head_dim)
    dkv = dkv[:, :, :, 0] + lax.ppermute(dkv[:, :, :, 1].astype(LOW), "mp", CROSS).astype(F32)
    dkv = dkv[:, 0] + other(dkv[:, 1].astype(LOW)).astype(F32)
    total = dkv[:, 0]
    for d in range(1, line):
        total = total + lax.ppermute(
            dkv[:, d].astype(LOW), "seq", [(i + 2 * d, i) for i in range(seq - 2 * d)]
        ).astype(F32)
    cosine = jnp.stack([t[0][:quarter] for t in tables], 0)
    sine = jnp.stack([t[1][:quarter] for t in tables], 0)
    dkv_low = jnp.concatenate(
        [unrotate(total[..., :head_dim], cosine, sine), total[..., head_dim:]], axis=-1
    ).astype(LOW)
    both = jnp.concatenate(gather_mp(jnp.concatenate([dc, dkv_low], -1)), -2)
    dfirst = jnp.concatenate(
        [lax.dynamic_slice_in_dim(both, me * part, part, 2),
         lax.dynamic_slice_in_dim(both, rank + me * kv_part, kv_part, 2)], -1
    )

    grad_down, order = chain_down.finish(order)
    order = chain_gate.advance(order)
    order = chain_up.advance(order)
    order = chain_out.advance(order)
    grad_gate, order = chain_gate.finish(order)
    order = chain_up.advance(order)
    order = chain_out.advance(order)
    grad_up, order = chain_up.finish(order)
    order = chain_qup.advance(order)
    order = chain_out.advance(order)
    chain_first, order = own_chain(h1_sides, dfirst, (wide, part + kv_part), order)
    order = chain_qup.advance(order)
    grad_out, order = chain_out.finish(order)
    order = chain_first.advance(order)
    order = chain_qup.advance(order)
    order = chain_first.advance(order)
    grad_qup, order = chain_qup.finish(order)
    order = chain_first.advance(order)
    grad_first, order = chain_first.finish(order)

    grad_qdown = grad_first[:, :part]
    kv_cols_grad = grad_first[:, part:]
    pieces = []
    for k in ORDER:
        size = kv_cols_grad.shape[0] // 4
        sent = lax.dynamic_slice_in_dim(kv_cols_grad, (me ^ k) * size, size, 0)
        pieces.append(lax.ppermute(sent, "mp", [(i, i ^ k) for i in range(4)]) if k else sent)
    grad_kv = to_natural(jnp.concatenate(pieces, 1), 1)

    def put_natural(pieces):
        return run(
            functools.partial(natural_body, micro, quarter),
            ids,
            pieces,
            [whole((micro, rows, width), LOW)],
            name="natural",
        )[0]

    part_sum = inner_cols(dfirst.reshape(micro * rows, -1), first_weights).reshape(micro, rows, width)
    dh1 = sum_mp(part_sum[:, half:].astype(LOW), part_sum[:, :half])
    gain1 = jnp.sum(dh1 * n1, axis=(0, 1))
    dx = (dy + norm_backward(dh1 * gain1_row, n1, inv1)).astype(LOW)
    input_grads = put_natural(gather_mp(dx))

    ffn = sum_mp(ffn_send, ffn_keep)
    layer_out = put_natural(gather_mp((y + ffn).astype(LOW)))

    gains = jnp.concatenate(
        [gain1.reshape(seq, -1), gain2.reshape(seq, -1), gain_c.reshape(seq, -1)], axis=1
    )
    gains = gains + lax.ppermute(gains, "mp", CORE)
    gains = gains + lax.ppermute(gains, "mp", CROSS)
    gain_sum = lax.dynamic_index_in_dim(gains, at, 0, keepdims=False)
    for k in range(1, seq):
        gain_sum = gain_sum + lax.ppermute(
            lax.dynamic_index_in_dim(gains, at ^ k, 0, keepdims=False),
            "seq",
            [(i, i ^ k) for i in range(seq)],
        )
    return (
        layer_out,
        input_grads,
        gain_sum[:wide],
        grad_qdown,
        gain_sum[2 * wide :],
        grad_qup,
        grad_kv,
        grad_out,
        gain_sum[wide : 2 * wide],
        grad_gate,
        grad_up,
        grad_down,
    )


def solution(mesh):
    placed = (
        P(None, "seq", None),
        P(),
        P(),
        P(None, "mp"),
        P(),
        P(None, "mp"),
        P(),
        P("mp", None),
        P(),
        P(None, "mp"),
        P(None, "mp"),
        P("mp", None),
        P(None, "seq", None),
    )
    return jax.shard_map(
        local,
        mesh=mesh,
        in_specs=placed,
        out_specs=(
            P(None, "seq", None),
            P(None, "seq", None),
            P("seq"),
            P("seq", "mp"),
            P("seq"),
            P("seq", "mp"),
            P(("seq", "mp"), None),
            P("mp", "seq"),
            P("seq"),
            P("seq", "mp"),
            P("seq", "mp"),
            P("mp", "seq"),
        ),
        check_vma=False,
    )
```

```python
import functools

import jax
import jax.numpy as jnp
from jax import lax
from jax.experimental import pallas as pl
from jax.experimental.pallas import tpu as pltpu
from jax.sharding import PartitionSpec as P

EPS = 1e-06
BASE = 10000.0
NEG_LARGE = -1e30
LOW = jnp.bfloat16
F32 = jnp.float32
ORDER = (0, 2, 1, 3)
CORE = [(i, i ^ 1) for i in range(4)]
CROSS = [(i, i ^ 2) for i in range(4)]


def inverse_rms(values):
    return lax.rsqrt(jnp.mean(values * values, axis=-1, keepdims=True) + EPS)


def norm_backward(grad_hat, normed, inverse):
    return inverse * (grad_hat - normed * jnp.mean(grad_hat * normed, axis=-1, keepdims=True))


def dot(left, right):
    return jnp.dot(left, right, preferred_element_type=F32)


def inner_rows(left, right):
    return lax.dot_general(left, right, (((0,), (0,)), ((), ())), preferred_element_type=F32)


def inner_cols(left, right):
    return lax.dot_general(left, right, (((1,), (1,)), ((), ())), preferred_element_type=F32)


def documents(lengths_row, rows):
    first_end = lengths_row[0]
    second_end = first_end + lengths_row[1]
    doc_ids = (rows >= first_end).astype(jnp.int32) + (rows >= second_end).astype(jnp.int32)
    starts = jnp.where(rows >= second_end, second_end, jnp.where(rows >= first_end, first_end, 0))
    return (doc_ids, rows - starts)


def rotation(positions, head_dim):
    half = head_dim // 2
    freqs = BASE ** (-2.0 * jnp.arange(half, dtype=F32) / head_dim)
    angles = positions.astype(F32)[:, None] * freqs[None, :]
    return (jnp.cos(angles), jnp.sin(angles))


def rotate(values, cosine, sine):
    half = values.shape[-1] // 2
    first = values[..., :half]
    second = values[..., half:]
    return jnp.concatenate(
        [first * cosine - second * sine, second * cosine + first * sine], axis=-1
    )


def unrotate(grads, cosine, sine):
    return rotate(grads, cosine, -sine)


def in_vmem():
    return pl.BlockSpec(memory_space=pltpu.VMEM)


def whole(shape, dtype):
    return jax.ShapeDtypeStruct(shape, dtype)


def run(body, ids, args, outs, after=(), scratch=(), name=None, limit=40):
    args, after = list(args), list(after)

    def without(*refs):
        body(*refs[: 1 + len(args)], *refs[1 + len(args) + len(after) :])

    return pl.pallas_call(
        without,
        grid_spec=pltpu.PrefetchScalarGridSpec(
            num_scalar_prefetch=1,
            grid=(1,),
            in_specs=[in_vmem()] * len(args) + [pl.BlockSpec(memory_space=pl.ANY)] * len(after),
            out_specs=[in_vmem()] * len(outs),
            scratch_shapes=list(scratch),
        ),
        out_shape=list(outs),
        cost_estimate=pl.CostEstimate(flops=1000, bytes_accessed=1000, transcendentals=0),
        compiler_params=pltpu.CompilerParams(vmem_limit_bytes=limit << 20),
        name=name,
    )(ids, *args, *after)


def side_columns(source, mine, theirs, side):
    line, _, wide = mine.shape
    rows = theirs.shape[1]
    for z in range(line):
        mine[z] = source[:, pl.ds(pl.multiple_of((2 * z + side) * wide, wide), wide)]
        theirs[z] = source[:rows, pl.ds(pl.multiple_of((2 * z + 1 - side) * wide, wide), wide)]


def first_body(m, quarter, ids, x_ref, gain, q_down, kv_proj, cos, sin, c, kv, h1, mine, theirs):
    blocks = [
        x_ref[m, pl.ds(pl.multiple_of((ids[0] ^ k) * quarter, quarter), quarter), :] for k in ORDER
    ]
    x = jnp.concatenate(blocks, 0).astype(F32)
    low = (x * inverse_rms(x) * gain[...]).astype(LOW)
    h1[...] = low
    half = 2 * quarter
    pair = dot(low[:half], kv_proj[...])
    wide = kv_proj.shape[1] // 2
    kv[:, :wide] = rotate(pair[:, :wide], cos[:half], sin[:half]).astype(LOW)
    kv[:, wide:] = pair[:, wide:].astype(LOW)
    c[...] = dot(low, q_down[...]).astype(LOW)
    if mine is not None:
        side_columns(h1, mine, theirs, ids[1])


def cotangent_body(micro, quarter, ids, z_ref, w_down, dhid, dz, *sides):
    for m in range(micro):
        blocks = [
            z_ref[m, pl.ds(pl.multiple_of((ids[0] ^ k) * quarter, quarter), quarter), :]
            for k in ORDER
        ]
        dz[m] = jnp.concatenate(blocks, 0)
        if sides:
            side_columns(dz.at[m], sides[0].at[m], sides[1].at[m], ids[1])
        dhid[m] = inner_cols(dz[m], w_down[...])


def attend_body(
    scale, ids, c0, c1, c2, gain, q_up, cos, sin, kv, key_ids, row_ids, row_starts, out_proj,
    qn, q, o, lse, send, keep, mine, theirs,
):
    rows = qn.shape[0]
    quarter = rows // 4
    part = c0.shape[1]
    wide = q.shape[2]
    got = c1[...]
    pair = jnp.concatenate(
        [got[quarter : 2 * quarter], got[:quarter], got[3 * quarter :], got[2 * quarter : 3 * quarter]],
        0,
    )
    far = jnp.concatenate([c2[2 * quarter :], c2[: 2 * quarter]], 0)
    c = jnp.concatenate([c0[...], pair, far], 1).astype(F32)
    chat = c * inverse_rms(c)
    for k, xor in enumerate(ORDER):
        columns = pl.ds(pl.multiple_of((ids[0] ^ xor) * part, part), part)
        qn[:, columns] = (chat[:, k * part : (k + 1) * part] * gain[:, columns]).astype(LOW)
    if mine is not None:
        side_columns(qn, mine, theirs, ids[1])
    bias = jnp.where(
        (key_ids[...] >= row_starts[...]) & (key_ids[...] <= row_ids[...]), 0.0, NEG_LARGE
    )
    low = qn[...]
    keys, values = kv[:, :wide], kv[:, wide:]
    for h in range(q.shape[0]):
        pre = dot(low, q_up[:, h * wide : (h + 1) * wide])
        q_h = (rotate(pre, cos[...], sin[...]) * scale).astype(LOW)
        q[h] = q_h
        scores = inner_cols(q_h, keys) + bias
        top = jnp.max(scores, axis=-1, keepdims=True)
        probs = jnp.exp(scores - top)
        total = jnp.sum(probs, axis=-1, keepdims=True)
        out = dot(probs.astype(LOW), values) / total
        o[:, h * wide : (h + 1) * wide] = out.astype(LOW)
        log_total = jnp.broadcast_to(top + jnp.log(total), (rows, 128))
        lse[h : h + 1, :] = jnp.transpose(log_total)[:1]
    half = 2 * quarter
    send[...] = dot(o[half:, :], out_proj[...]).astype(LOW)
    keep[...] = dot(o[:half, :], out_proj[...])


def forward_body(m, ids, a0, a1, a2, w_gate, w_up, dhid, h2, hid, dg, du, mine, theirs):
    h2[...] = jnp.concatenate([a0[...], a1[...], a2[...]], 0)
    if mine is not None:
        side_columns(h2, mine, theirs, ids[1])
    low = h2[...]
    g = dot(low, w_gate[...])
    u = dot(low, w_up[...])
    sig = jax.nn.sigmoid(g)
    swish = g * sig
    hid[...] = (swish * u).astype(LOW)
    back = dhid[m]
    dg[...] = (back * u * sig * (1.0 + g * (1.0 - sig))).astype(LOW)
    du[...] = (back * swish).astype(LOW)


def hidden_back_body(micro, ids, *refs):
    dgs, dus = refs[:micro], refs[micro : 2 * micro]
    hids = refs[2 * micro : 3 * micro]
    w_gate, w_up, w_down, send, keep, out_send, out_keep = refs[3 * micro :]
    half = send.shape[1]
    every = lambda parts: jnp.concatenate([part[...] for part in parts], 0)
    rows = 2 * half
    total = inner_cols(every(dgs), w_gate[...]) + inner_cols(every(dus), w_up[...])
    for m in range(micro):
        send[m] = total[m * rows + half : (m + 1) * rows].astype(LOW)
        keep[m] = total[m * rows : m * rows + half]
    total = dot(every(hids), w_down[...])
    for m in range(micro):
        out_send[m] = total[m * rows + half : (m + 1) * rows].astype(LOW)
        out_keep[m] = total[m * rows : m * rows + half]


def pick(ref, lead):
    return ref if lead is None else ref.at[lead]


def block_body(terms, lefts, rights, extra, from_side, turned, ids, *refs):
    left, refs = refs[:lefts], refs[lefts:]
    right, refs = refs[:rights], refs[rights:]
    added, out = refs[: extra + from_side], refs[-1]
    total = None
    for a, a_lead, b, b_lead, first, count in terms:
        rows = pick(right[b], b_lead)[first : first + count, :]
        term = inner_rows(pick(left[a], a_lead)[ids[0]], rows)
        total = term if total is None else total + term
    for i, ref in enumerate(added):
        total = total + (ref[ids[0]] if i >= extra else ref[...]).astype(F32)
    out[...] = jnp.transpose(total) if turned else total.astype(out.dtype)


def side_sum_body(terms, lefts, ids, *refs):
    left, right, out = refs[:lefts], refs[lefts:-1], refs[-1]
    for z in range(out.shape[0]):
        total = None
        for a, a_lead, b, b_lead, first, count in terms:
            rows = pick(right[b], b_lead)[first : first + count, :]
            term = inner_rows(pick(left[a], a_lead)[z], rows)
            total = term if total is None else total + term
        out[z] = total.astype(out.dtype)


def attend_back_body(
    scale, micro, chunk, ids, a0, a1, a2, out_proj, q_up, key_ids, *refs
):
    per = 7
    groups = [refs[m * per : (m + 1) * per] for m in range(micro)]
    dyl_out, dqp, send, keep, kv_send, kv_keep = refs[micro * per : micro * per + 6]
    dq_acc, do_acc, delta_acc = refs[-3:]
    sides = refs[micro * per + 6 : -3]
    for m in range(micro):
        q, kv, o, lse, row_ids, cos, sin = groups[m]
        heads, rows, wide = q.shape
        half_rows = rows // 2
        dyl = jnp.concatenate([a0[m], a1[m], a2[m]], 0)
        dyl_out[m] = dyl
        if sides:
            side_columns(dyl_out.at[m], sides[0].at[m], sides[1].at[m], ids[1])
        for h in range(heads):
            do = inner_cols(dyl, out_proj[h * wide : (h + 1) * wide, :]).astype(LOW)
            do_acc[h] = do
            delta = jnp.sum(
                do.astype(F32) * o[:, h * wide : (h + 1) * wide].astype(F32), axis=-1, keepdims=True
            )
            delta_acc[h] = jnp.transpose(jnp.broadcast_to(delta, (rows, 128)))[:8]
            dq_acc[h] = jnp.zeros((rows, wide), F32)
        count = kv.shape[0] // 2 // chunk
        for part, out in ((0, kv_keep), (1, kv_send)):

            def one(i, carry):
                base = pl.multiple_of((part * count + i) * chunk, chunk)
                keys = kv[pl.ds(base, chunk), :wide]
                values = kv[pl.ds(base, chunk), wide:]
                at = key_ids[pl.ds(base, chunk), :]
                bias = jnp.where((at >= row_ids[1:2, :]) & (at <= row_ids[0:1, :]), 0.0, NEG_LARGE)

                def head(h, sums):
                    dk, dv = sums
                    q_h, do_h = q[h], do_acc[h]
                    probs = jnp.exp(inner_cols(keys, q_h) + bias - lse[pl.ds(h, 1), :])
                    back = inner_cols(values, do_h) - delta_acc[h][:1]
                    ds = (probs * back).astype(LOW)
                    dv = dv + dot(probs.astype(LOW), do_h)
                    dk = dk + dot(ds, q_h)
                    dq_acc[h] = dq_acc[h] + inner_rows(ds, keys)
                    return dk, dv

                zero = jnp.zeros((chunk, wide), F32)
                dk, dv = lax.fori_loop(0, heads, head, (zero, zero))
                place = pl.ds(pl.multiple_of(i * chunk, chunk), chunk)
                out[m, place, :wide] = dk.astype(out.dtype)
                out[m, place, wide:] = dv.astype(out.dtype)
                return carry

            if count == 1:
                one(0, 0)
            else:
                lax.fori_loop(0, count, one, 0)
        for h in range(heads):
            dq = unrotate(dq_acc[h] * scale, cos[...], sin[...])
            dqp[m, :, h * wide : (h + 1) * wide] = dq.astype(LOW)
        low = dqp[m]
        send[m] = inner_cols(low[half_rows:], q_up[...]).astype(LOW)
        keep[m] = inner_cols(low[:half_rows], q_up[...])


def natural_body(micro, quarter, ids, a0, a1, a2, out):
    for m in range(micro):
        pieces = (a0[m], a1[m], a2[m, :quarter, :], a2[m, quarter:, :])
        for k, piece in zip(ORDER, pieces):
            out[m, pl.ds(pl.multiple_of((ids[0] ^ k) * quarter, quarter), quarter), :] = piece


class Wire:
    def __init__(self, sends, recvs):
        self.sends, self.recvs, self.used = sends, recvs, 0
        self.seq, self.mp = lax.axis_index("seq"), lax.axis_index("mp")
        self.place, self.side = self.seq // 2, self.seq % 2
        core, cross = self.mp % 2, self.mp // 2
        self.blocks = (
            self.mp, 2 * (1 - cross) + core, 2 * cross + 1 - core, 2 * (1 - cross) + 1 - core
        )
        self.core, self.cross = {"mp": self.blocks[2]}, {"mp": self.blocks[1]}
        self.beside = {"seq": self.seq + 1 - 2 * self.side}
        self.up, self.down = {"seq": self.seq + 2}, {"seq": self.seq - 2}

    def copy(self, source, target, device):
        at = self.used
        self.used += 1
        return pltpu.make_async_remote_copy(
            src_ref=source, dst_ref=target, send_sem=self.sends.at[at], recv_sem=self.recvs.at[at],
            device_id=device, device_id_type=pl.DeviceIdType.MESH,
        )

    def send(self, source, target, device):
        made = self.copy(source, target, device)
        made.start()
        return made

    def greet(self, line, far=1, diagonal=False):
        barrier = pltpu.get_barrier_semaphore()
        devices = [self.core, self.cross, self.beside]
        if diagonal:
            devices.append({"mp": self.blocks[3]})
        for device in devices:
            pl.semaphore_signal(barrier, 1, device_id=device, device_id_type=pl.DeviceIdType.MESH)
        for d in range(1, far + 1):
            for way, there in ((1, self.place < line - d), (-1, self.place >= d)):

                @pl.when(there)
                def _():
                    pl.semaphore_signal(
                        barrier, 1, device_id={"seq": self.seq + 2 * way * d},
                        device_id_type=pl.DeviceIdType.MESH,
                    )
        below, above = jnp.minimum(self.place, far), jnp.minimum(line - 1 - self.place, far)
        pl.semaphore_wait(barrier, len(devices) + below + above)


def along(pieces, axis):
    return pieces[0] if len(pieces) == 1 else jnp.concatenate(pieces, axis)


def pair_places(first, second, quarter, axis):
    shape = (2 * quarter, 1) if axis == 0 else (1, 2 * quarter)
    index = lax.broadcasted_iota(jnp.int32, shape, axis)
    return jnp.where(index < quarter, first * quarter + index, (second - 1) * quarter + index)


def row_places(wire, quarter, axis):
    b = wire.blocks
    pieces = [pair_places(b[i], b[i + 1], quarter, axis) for i in (0, 2)]
    return wire.seq * (4 * quarter) + along(pieces, axis)


def key_places(wire, quarter, line, axis, cores):
    pieces = []
    for core in cores:
        for side in (wire.side, 1 - wire.side):
            for d in range(line):
                base = ((wire.place - d) * 2 + side) * (4 * quarter)
                b = wire.blocks[2 * core : 2 * core + 2]
                pieces.append(base + pair_places(b[0], b[1], quarter, axis))
    return along(pieces, axis)


def sequence_starts(lengths, m, places):
    first_end = lengths[m, 0]
    second_end = first_end + lengths[m, 1]
    return jnp.where(
        places >= second_end, second_end, jnp.where(places >= first_end, first_end, 0)
    )


class LineSum:
    def __init__(self, wire, term, room, rows, columns, keep):
        got, out = room
        view = lambda ref, i: ref.at[i, :rows, :columns]
        self.place, self.term, self.keep = wire.place, term, keep
        self.got = [view(got, i) for i in range(5)]
        self.out = [view(out, i) for i in range(2)]
        one, two_up, two_down, three_up, three_down = self.got
        a, b = self.out
        self.one = wire.copy(a, one, wire.up), wire.copy(a, one, wire.down)
        self.two = wire.copy(b, two_up, wire.up), wire.copy(b, two_down, wire.down)
        self.three = wire.copy(a, three_up, wire.up), wire.copy(b, three_down, wire.down)

    def clear(self):
        place = self.place
        for ref, empty in zip(
            self.got, ((place == 0) | (place == 3),) * 3 + (place == 0, place == 3)
        ):

            @pl.when(empty)
            def _(ref=ref):
                ref[...] = jnp.zeros(ref.shape, ref.dtype)

    def step1(self):
        place = self.place

        @pl.when((place == 0) | (place == 3))
        def _():
            self.out[0][...] = self.term(3 - place).astype(LOW)

        pl.when(place == 0)(self.one[0].start)
        pl.when(place == 3)(self.one[1].start)

    def step2(self):
        place = self.place
        pl.when(place == 1)(self.one[0].wait_recv)
        pl.when(place == 2)(self.one[1].wait_recv)
        self.out[1][...] = (
            self.term((place + 2) % 4) + self.got[0][...].astype(F32)
        ).astype(LOW)
        pl.when(place <= 1)(self.two[0].start)
        pl.when(place >= 2)(self.two[1].start)

    def step3(self):
        place = self.place

        @pl.when((place == 1) | (place == 2))
        def _():
            self.two[0].wait_recv()
            self.two[1].wait_recv()

        pl.when(place == 0)(self.one[0].wait_send)
        pl.when(place == 3)(self.one[1].wait_send)

        @pl.when(place <= 2)
        def _():
            self.out[0][...] = (self.term(place + 1) + self.got[1][...].astype(F32)).astype(LOW)
            self.three[0].start()

        pl.when(place <= 1)(self.two[0].wait_send)
        pl.when(place >= 2)(self.two[1].wait_send)

        @pl.when(place >= 1)
        def _():
            self.out[1][...] = (self.term(place - 1) + self.got[2][...].astype(F32)).astype(LOW)
            self.three[1].start()

    def finish(self):
        place = self.place
        pl.when(place >= 1)(self.three[0].wait_recv)
        pl.when(place <= 2)(self.three[1].wait_recv)
        self.keep(
            self.term(place) + self.got[3][...].astype(F32) + self.got[4][...].astype(F32)
        )

    def settle(self):
        place = self.place
        pl.when(place <= 2)(self.three[0].wait_send)
        pl.when(place >= 1)(self.three[1].wait_send)


class Desk:
    def __init__(self, loads, stores):
        self.loads, self.stores, self.stored = loads, stores, []
        for _, made in loads:
            made.start()
        self.waiting = list(loads)

    def arrive(self, *refs):
        rest = []
        for ref, made in self.waiting:
            if not refs or any(ref is other for other in refs):
                made.wait()
            else:
                rest.append((ref, made))
        self.waiting = rest

    def flush(self, *refs):
        rest = []
        for ref, made in self.stores:
            if not refs or any(ref is other for other in refs):
                made.start()
                self.stored.append(made)
            else:
                rest.append((ref, made))
        self.stores = rest

    def close(self):
        self.flush()
        for made in self.stored:
            made.wait()


SPACES = (pl.ANY, pltpu.VMEM, pltpu.SMEM, pl.ANY)


def mesh_run(body, args, outs, scratch, number, name, limit, sends):
    late_in = [i for i, (kind, _) in enumerate(args) if kind == 3]
    late_out = [i for i, (kind, _) in enumerate(outs) if kind == 3]

    def whole_body(*refs):
        refs = list(refs)
        take = lambda n: [refs.pop(0) for _ in range(n)]
        given, results, rooms_in, rooms_out = (
            take(len(args)), take(len(outs)), take(len(late_in)), take(len(late_out))
        )
        load_sems, store_sems = take(2)
        loads, stores = [], []
        for n, (i, room) in enumerate(zip(late_in, rooms_in)):
            loads.append((room, pltpu.make_async_copy(given[i], room, load_sems.at[n])))
            given[i] = room
        for n, (i, room) in enumerate(zip(late_out, rooms_out)):
            stores.append((room, pltpu.make_async_copy(room, results[i], store_sems.at[n])))
            results[i] = room
        desk = Desk(loads, stores)
        body(desk, *given, *results, *refs)
        desk.close()

    room = lambda a: pltpu.VMEM(a.shape, a.dtype)
    return pl.pallas_call(
        whole_body,
        in_specs=[pl.BlockSpec(memory_space=SPACES[kind]) for kind, _ in args],
        out_specs=[pl.BlockSpec(memory_space=SPACES[kind]) for kind, _ in outs],
        out_shape=[shape for _, shape in outs],
        scratch_shapes=[
            *[room(args[i][1]) for i in late_in], *[room(outs[i][1]) for i in late_out],
            pltpu.SemaphoreType.DMA((max(1, len(late_in)),)),
            pltpu.SemaphoreType.DMA((max(1, len(late_out)),)),
            *scratch, pltpu.SemaphoreType.DMA((sends,)), pltpu.SemaphoreType.DMA((sends,)),
        ],
        cost_estimate=pl.CostEstimate(flops=1000, bytes_accessed=1000, transcendentals=0),
        compiler_params=pltpu.CompilerParams(
            collective_id=number, has_side_effects=True, vmem_limit_bytes=limit << 20
        ),
        name=name,
    )(*[array for _, array in args])


def attend_back_one(
    scale, keys_at, rows_at, starts, dyl, out_proj, q_up, q, kv, o, lse, cos, sin,
    dqp, send, keep, kv_send, kv_keep, dq_acc, between=None,
):
    heads, rows, wide = q.shape
    half_rows = rows // 2
    low = dyl[...]
    grads, deltas = [], []
    for h in range(heads):
        columns = slice(h * wide, (h + 1) * wide)
        do = inner_cols(low, out_proj[columns, :]).astype(LOW)
        grads.append(do)
        delta = jnp.sum(do.astype(F32) * o[:, columns].astype(F32), axis=-1, keepdims=True)
        deltas.append(jnp.transpose(jnp.broadcast_to(delta, (rows, 128)))[:1])
    do_all, delta_all = jnp.concatenate(grads, 0), jnp.concatenate(deltas, 1)
    q_all = q[...].reshape(heads * rows, wide)
    lse_all = jnp.concatenate([lse[h : h + 1, :] for h in range(heads)], 1)
    dq_acc[...] = jnp.zeros(dq_acc.shape, F32)
    count = kv.shape[0] // 2
    chunk = min(256, count)
    for part, out in ((1, kv_send), (0, kv_keep)):
        for first in range(0, count, chunk):
            span = slice(part * count + first, part * count + first + chunk)
            keys, values = kv[span, :wide], kv[span, wide:]
            at = keys_at[part][first : first + chunk]
            bias = jnp.where((at >= starts) & (at <= rows_at), 0.0, NEG_LARGE)
            scores = inner_cols(keys, q_all) + jnp.concatenate([bias] * heads, 1)
            probs = jnp.exp(scores - lse_all)
            ds = (probs * (inner_cols(values, do_all) - delta_all)).astype(LOW)
            spot = slice(first, first + chunk)
            out[spot, :wide] = dot(ds, q_all).astype(out.dtype)
            out[spot, wide:] = dot(probs.astype(LOW), do_all).astype(out.dtype)
            dq_acc[...] += inner_rows(ds, keys)
        if part and between is not None:
            between()
    for h in range(heads):
        dq = unrotate(dq_acc[h * rows : (h + 1) * rows, :] * scale, cos, sin)
        dqp[:, h * wide : (h + 1) * wide] = dq.astype(LOW)
    total = inner_cols(dqp[...], q_up[...])
    send[...] = total[half_rows:].astype(LOW)
    keep[...] = total[:half_rows]


def mean_of(values):
    return jnp.mean(values, axis=-1, keepdims=True)


def terms_sum(pairs):
    total = None
    for left, right in pairs:
        term = inner_rows(left, right)
        total = term if total is None else total + term
    return total


def back1_body(quarter, desk, *refs):
    refs = list(refs)
    take = lambda n: [refs.pop(0) for _ in range(n)]
    w_gate, w_up, w_down, cotangent, h2, dhid, n2, inv2, gain2, dz_got, dz_far, y = take(12)
    grad, dy, gain_sum, dyl, dyl_mine, dyl_theirs, layer_own = take(7)
    hid, dg, du, h2_mine = (take(2) for _ in range(4))
    h2_got, h2_far, dg_other = take(2), take(2), take(2)
    gate_w, up_w, hid_other0, hid_other1, h2_theirs, got, out = take(7)
    send, kept, core_got, cross_out, cross_got, loads = take(6)
    ffn_send, ffn_kept, ffn_got, ffn_out, ffn_back = take(5)
    early_got, early_out, early_sum, early_send, early_back, dz, row_loads = take(7)
    wire = Wire(*take(2))
    half, rows = 2 * quarter, 4 * quarter
    ahead = early_send.shape[1]
    block = early_send.shape[0]
    in_gate = pltpu.make_async_copy(w_gate, gate_w, loads.at[0])
    in_up = pltpu.make_async_copy(w_up, up_w, loads.at[1])
    in_gate.start()
    in_up.start()
    in_dz = []
    for m in range(2):
        for k in range(4):
            at = pl.ds(pl.multiple_of(wire.blocks[k] * quarter, quarter), quarter)
            in_dz.append(pltpu.make_async_copy(
                cotangent.at[m, at, :], dz.at[m, k * quarter : (k + 1) * quarter, :],
                row_loads.at[4 * m + k],
            ))
            in_dz[-1].start()
    hid_other = (hid_other0, hid_other1)
    hid_all = (*(a.at[:, ahead:] for a in hid), *hid_other)

    def term(z):
        columns = pl.ds(pl.multiple_of((2 * z + wire.side) * block, block), block)
        return terms_sum(halves_terms(
            [dz[m, :, columns] for m in range(2)], [dz_got[m, z] for m in range(2)],
            [dz_far[m, z] for m in range(2)], hid_all, half))

    def early_term(z):
        columns = pl.ds(pl.multiple_of(z * 2 * block, 2 * block), 2 * block)
        return terms_sum([(dz[m, :, columns], hid[m][:, :ahead]) for m in range(2)])

    def keep(total):
        grad[ahead:, :] = jnp.transpose(total)

    def early_keep(total):
        early_sum[0], early_sum[1] = total[:block], total[block:]

    chain = LineSum(wire, term, (got, out), block, grad.shape[0] - ahead, keep)
    early = LineSum(wire, early_term, (early_got, early_out), 2 * block, ahead, early_keep)
    chain.clear()
    early.clear()
    wire.greet(4)
    y_hid = []
    desk.arrive(h2)
    for m in range(2):
        low = h2[m]
        if m == 0:
            in_gate.wait()
        g = dot(low, gate_w[...])
        if m == 0:
            in_up.wait()
        u = dot(low, up_w[...])
        sig = jax.nn.sigmoid(g)
        swish = g * sig
        hid[m][...] = (swish * u).astype(LOW)
        y_hid.append(wire.send(hid[m].at[:, ahead:], hid_other[m], wire.beside))
        if m == 0:
            desk.arrive()
        back = dhid[m]
        dg[m][...] = (back * u * sig * (1.0 + g * (1.0 - sig))).astype(LOW)
        du[m][...] = (back * swish).astype(LOW)
        desk.flush(dg[m], du[m], hid[m])
    for made in in_dz:
        made.wait()
    early.step1()
    both = lambda pair: jnp.concatenate([pair[0][...], pair[1][...]], 0)
    total = inner_cols(both(dg), gate_w[...]) + inner_cols(both(du), up_w[...])
    for m in range(2):
        send[m] = total[m * rows + half : (m + 1) * rows].astype(LOW)
        kept[m] = total[m * rows : m * rows + half]
    sums = RowSum(wire, send, kept, core_got, cross_out, cross_got, quarter)
    sums.core.start()
    wide = gate_w.shape[1]
    rest = w_down.shape[1] - wide
    downs = [gate_w.at[:wide, :], up_w.at[:wide, :rest]]
    in_down = [
        pltpu.make_async_copy(w_down.at[:, :wide], downs[0], loads.at[0]),
        pltpu.make_async_copy(w_down.at[:, wide:], downs[1], loads.at[1]),
    ]
    for made in in_down:
        made.start()
    for m in range(2):
        side_columns(h2.at[m], h2_mine[m], h2_theirs.at[m], wire.side)
        desk.flush(h2_mine[m])
    sums.pass_on()
    early.step2()
    for made in in_down:
        made.wait()
    low = both(hid)
    ffn_sum = RowSum(wire, ffn_send, ffn_kept, ffn_got, ffn_out, ffn_back, quarter)
    for columns, part in ((slice(0, wide), downs[0]), (slice(wide, None), downs[1])):
        total = dot(low, part[...])
        for m in range(2):
            ffn_send[m, :, columns] = total[m * rows + half : (m + 1) * rows].astype(LOW)
            ffn_kept[m, :, columns] = total[m * rows : m * rows + half].astype(LOW)
    ffn_sum.core.start()
    for made in y_hid:
        made.wait_recv()
    y_next = [wire.send(h2_theirs.at[m], h2_got[m], wire.beside) for m in range(2)]
    y_next += [wire.send(dg[m], dg_other[m], wire.beside) for m in range(2)]
    chain.step1()
    early.step3()
    dh2 = sums.result()
    gain_sum[...] = jnp.sum(jnp.sum(dh2 * n2[...], axis=0), axis=0, keepdims=True)
    back = dh2 * gain2[...]
    grad_y = dz[:, :quarter, :].astype(F32) + inv2[...] * (
        back - n2[...] * mean_of(back * n2[...])
    )
    dy[...] = grad_y
    dyl[:, :quarter, :] = grad_y.astype(LOW)
    cross_dyl = wire.send(dyl.at[:, :quarter, :], dyl.at[:, quarter:half, :], wire.cross)
    ffn_sum.pass_on()
    chain.step2()
    early.finish()
    early_send[...] = early_sum[1 - wire.side].astype(LOW)
    y_early = wire.send(early_send, early_back, wire.beside)
    cross_dyl.wait_recv()
    core_dyl = wire.send(dyl.at[:, :half, :], dyl.at[:, half:, :], wire.core)
    core_h2 = []
    for i in range(2):
        y_next[i].wait_recv()
        core_h2.append(wire.send(h2_got[i], h2_far[i], wire.core))
    core_dyl.wait_recv()
    for m in range(2):
        side_columns(dyl.at[m], dyl_mine.at[m], dyl_theirs.at[m], wire.side)
    desk.flush(dy, dyl, dyl_mine, dyl_theirs)
    chain.step3()
    layer_own[...] = (y[...] + ffn_sum.result()).astype(LOW)
    y_early.wait_recv()
    grad[:ahead, :] = jnp.transpose(early_sum[wire.side] + early_back[...].astype(F32))
    for made in y_next[2:] + core_h2:
        made.wait_recv()
    chain.finish()
    for made in [*y_hid, cross_dyl, core_dyl, *y_next, *core_h2, y_early]:
        made.wait_send()
    sums.end()
    ffn_sum.end()
    early.settle()
    chain.settle()


class Share:
    def __init__(self, wire, out, quarter):
        spot = lambda block: out.at[:, pl.ds(pl.multiple_of(block * quarter, quarter), quarter), :]
        own, near = spot(wire.blocks[0]), spot(wire.blocks[1])
        self.own = own
        self.first = wire.copy(own, own, wire.cross)
        self.rest = wire.copy(own, own, wire.core), wire.copy(near, near, wire.core)

    def begin(self, value):
        self.own[...] = value
        self.first.start()
        self.rest[0].start()

    def forward(self):
        self.first.wait_recv()
        self.rest[1].start()

    def end(self):
        for made in self.rest:
            made.wait_recv()
        for made in (self.first, *self.rest):
            made.wait_send()


class RowSum:
    def __init__(self, wire, send, kept, got, cross_out, cross_got, quarter):
        self.kept, self.got, self.quarter = kept, got, quarter
        self.out, self.back = cross_out, cross_got
        self.core = wire.copy(send, got, wire.core)
        self.cross = wire.copy(cross_out, cross_got, wire.cross)

    def pass_on(self):
        self.core.wait_recv()
        rest = slice(self.quarter, None)
        self.out[...] = (self.kept[:, rest, :] + self.got[:, rest, :].astype(F32)).astype(LOW)
        self.cross.start()

    def result(self):
        self.cross.wait_recv()
        own = slice(0, self.quarter)
        return (
            self.kept[:, own, :] + self.got[:, own, :].astype(F32) + self.back[...].astype(F32)
        )

    def end(self):
        self.core.wait_send()
        self.cross.wait_send()


def halves_terms(mine, got, far, rights, half):
    pairs = [(mine[m], rights[m][...]) for m in range(2)]
    for m in range(2):
        pairs.append((got[m], rights[2 + m][:half, :]))
        pairs.append((far[m], rights[2 + m][half:, :]))
    return pairs


def back2_body(quarter, scale, desk, *refs):
    refs = list(refs)
    take = lambda n: [refs.pop(0) for _ in range(n)]
    (lengths,) = take(1)
    dg, dg_other, du, h2_mine, h2_got, h2_far = (take(2) for _ in range(6))
    dyl, out_proj, q_up = take(3)
    q, kv, o, lse = (take(2) for _ in range(4))
    cos, sin, chat, inv_c, gain_c, dyl_theirs = take(6)
    qn_theirs, os_far = take(2), take(2)
    grad_gate, grad_up, dfirst, gain_sum, dqp, dyl_got, dyl_far, qup_side = take(8)
    oo = take(2)
    du_other = take(2)
    got_a, out_a, got_b, out_b = take(4)
    dq_acc, dqn_send, dqn_keep, kv_send, kv_keep = take(5)
    dqn_got, dqn_out, dqn_back = take(3)
    kv_got, kv_out, kv_back, side_out, side_got, line_out, line_got, kv_own = take(8)
    both, side_sums = take(2)
    wire = Wire(*take(2))
    half, rows = 2 * quarter, 4 * quarter
    wide = kv_own.shape[2] // 2
    rank = chat.shape[2]
    place = wire.place

    y_du = [wire.copy(du[m], du_other[m], wire.beside) for m in range(2)]

    def chain(rights, grad, room):
        def term(z):
            return terms_sum(halves_terms(
                [a[z] for a in h2_mine], [a[z] for a in h2_got], [a[z] for a in h2_far], rights,
                half))

        def keep(total):
            grad[...] = total

        made = LineSum(wire, term, room, *grad.shape, keep)
        made.clear()
        return made

    gate = chain((*dg, *dg_other), grad_gate, (got_a, out_a))
    up = chain((*du, *du_other), grad_up, (got_b, out_b))
    dqn_sum, core_kv, cross_kv, side_kv, line_kv = [], [], [], [], []
    for m in range(2):
        one = lambda ref: ref.at[m : m + 1]
        dqn_sum.append(RowSum(wire, one(dqn_send), one(dqn_keep), one(dqn_got), one(dqn_out),
                              one(dqn_back), quarter))
        core_kv.append(wire.copy(kv_send.at[m], kv_got.at[m], wire.core))
        cross_kv.append(wire.copy(kv_out.at[m], kv_back.at[m], wire.cross))
        side_kv.append(wire.copy(side_out.at[m], side_got.at[m], wire.beside))
        line_kv.append([
            wire.copy(line_out.at[m, d - 1], line_got.at[m, d - 1], {"seq": wire.seq - 2 * d})
            for d in range(1, 4)
        ])
        for d in range(1, 4):

            @pl.when(place > 3 - d)
            def _(m=m, d=d):
                line_got[m, d - 1] = jnp.zeros(line_got.shape[2:], LOW)

    wire.greet(4, 3)
    desk.arrive(*du)
    for made in y_du:
        made.start()
    desk.arrive(*dg, *dg_other, *h2_mine, *h2_got, *h2_far)
    gate.step1()
    desk.arrive()

    def attend(m, between=None):
        rows_at = row_places(wire, quarter, 1)
        attend_back_one(
            scale, [key_places(wire, quarter, 4, 0, (core,)) for core in range(2)], rows_at,
            sequence_starts(lengths, m, rows_at), dyl.at[m], out_proj, q_up, q[m], kv[m], o[m],
            lse[m], cos[m], sin[m], dqp.at[m], dqn_send.at[m], dqn_keep.at[m], kv_send.at[m],
            kv_keep.at[m], dq_acc, between,
        )
        core_kv[m].start()
        dqn_sum[m].core.start()

    split = lambda ref, m: ref[m].reshape(8, 2, quarter, 2 * wide)

    def kv_cross(m):
        dqn_sum[m].pass_on()
        core_kv[m].wait_recv()
        kv_out[m] = (
            split(kv_keep, m)[:, 1].astype(F32) + split(kv_got, m)[:, 1].astype(F32)
        ).astype(LOW)
        cross_kv[m].start()

    def kv_sum(m, span):
        return (
            split(kv_keep, m)[span, 0].astype(F32) + split(kv_got, m)[span, 0].astype(F32)
            + kv_back[m, span].astype(F32)
        )

    def kv_side(m):
        cross_kv[m].wait_recv()
        side_out[m] = kv_sum(m, slice(4, 8)).astype(LOW)
        side_kv[m].start()

    def kv_line(m):
        side_kv[m].wait_recv()
        own = kv_sum(m, slice(0, 4)) + side_got[m].astype(F32)
        kv_own[m] = own[0]
        for d in range(1, 4):
            line_out[m, d - 1] = own[d].astype(LOW)
            pl.when(place >= d)(line_kv[m][d - 1].start)

    def latent(m):
        dqn = dqn_sum[m].result()[0]
        gain = jnp.sum(dqn * chat[m], axis=0, keepdims=True)
        gain_sum[...] = gain if m == 0 else gain_sum[...] + gain
        back = dqn * gain_c[...]
        both[m, :quarter, :rank] = (
            inv_c[m] * (back - chat[m] * mean_of(back * chat[m]))
        ).astype(LOW)

    y_late = []

    def start_up():
        for made in y_du:
            made.wait_recv()
        y_late.append(wire.send(dyl_theirs, dyl_got, wire.beside))
        y_late.extend(wire.send(os_far[m], oo[m], wire.beside) for m in range(2))
        up.step1()

    attend(0)
    kv_cross(0)
    gate.step2()
    attend(1, start_up)
    gate.step3()
    kv_cross(1)
    kv_side(0)
    latent(0)
    up.step2()
    latent(1)
    for z in range(4):
        side_sums[z] = terms_sum([(qn_theirs[m][z], dqp[m]) for m in range(2)]).astype(LOW)
    kv_side(1)
    side_qup = wire.send(side_sums, qup_side, wire.beside)
    side_dyl, *side_o = y_late
    desk.flush(dqp)
    kv_line(0)
    kv_line(1)
    gate.finish()
    desk.flush(grad_gate)
    for m in range(2):
        for d in range(1, 4):
            pl.when(place <= 3 - d)(line_kv[m][d - 1].wait_recv)
        total = kv_own[m]
        for d in range(1, 4):
            total = total + line_got[m, d - 1].astype(F32)
        both[m, :quarter, rank : rank + wide] = unrotate(
            total[:, :wide], cos[m, :quarter], sin[m, :quarter]
        ).astype(LOW)
        both[m, :quarter, rank + wide :] = total[:, wide:].astype(LOW)
    cross_both = wire.send(both.at[:, :quarter, :], both.at[:, quarter:half, :], wire.cross)
    up.step3()
    cross_both.wait_recv()
    core_both = wire.send(both.at[:, :half, :], both.at[:, half:, :], wire.core)
    side_dyl.wait_recv()
    core_dyl = wire.send(dyl_got, dyl_far, wire.core)
    core_both.wait_recv()
    part = rank // 4
    kv_part = wide // 2
    dfirst[:, :, :part] = both[:, :, pl.ds(pl.multiple_of(wire.mp * part, part), part)]
    dfirst[:, :, part:] = both[
        :, :, pl.ds(pl.multiple_of(rank + wire.mp * kv_part, kv_part), kv_part)
    ]
    up.finish()
    core_dyl.wait_recv()
    for made in (side_qup, *side_o):
        made.wait_recv()
    for made in [*y_du, *core_kv, *cross_kv, *side_kv, cross_both, core_both, side_dyl, core_dyl,
                 side_qup, *side_o]:
        made.wait_send()
    for m in range(2):
        dqn_sum[m].end()
        for d in range(1, 4):
            pl.when(place >= d)(line_kv[m][d - 1].wait_send)
    gate.settle()
    up.settle()


def back3_body(quarter, desk, *refs):
    refs = list(refs)
    take = lambda n: [refs.pop(0) for _ in range(n)]
    dfirst, weights = take(2)
    h1_mine, h1_theirs, o, oo = (take(2) for _ in range(4))
    dyl_mine, dyl_got, dyl_far = take(3)
    qn_mine = take(2)
    dqp, qup_side, n1, inv1, dy, gain1, gain2_sum, gain_c_sum, layer_own = take(9)
    grad_out, grad_qup, grad_qdown, grad_kv, grad_tokens, gains, layer_out = take(7)
    got_a, out_a, got_b, out_b, got_c, out_c = take(6)
    side_sums, side_got = take(2)
    send, kept, row_got, row_out, row_back = take(5)
    kv_out, kv_got = take(2)
    sums, sums_core, sums_cross, sums_side, sums_line = take(5)
    wire = Wire(*take(2))
    half, rows = 2 * quarter, 4 * quarter
    place = wire.place
    wire.greet(4, 3, diagonal=True)


    def out_term(z):
        return terms_sum(halves_terms(
            [dyl_mine[m, z] for m in range(2)], [dyl_got[m, z] for m in range(2)],
            [dyl_far[m, z] for m in range(2)], (*o, *oo), half))

    def qup_term(z):
        return terms_sum([(qn_mine[m][z], dqp[m]) for m in range(2)]) + qup_side[z].astype(F32)

    def first_term(z):
        return terms_sum([(h1_mine[m][z], dfirst[m]) for m in range(2)]) + side_got[z].astype(F32)

    def keep_out(total):
        grad_out[...] = jnp.transpose(total)

    def keep_qup(total):
        grad_qup[...] = total

    part = grad_qdown.shape[1]

    def keep_first(total):
        grad_qdown[...] = total[:, :part]
        kv_out[...] = total[:, part:]

    out = LineSum(wire, out_term, (got_a, out_a), *grad_out.shape[::-1], keep_out)
    qup = LineSum(wire, qup_term, (got_b, out_b), *grad_qup.shape, keep_qup)
    first = LineSum(wire, first_term, (got_c, out_c), kv_out.shape[0], dfirst.shape[2], keep_first)
    for chain in (out, qup, first):
        chain.clear()
    row_sum = RowSum(wire, send, kept, row_got, row_out, row_back, quarter)
    desk.arrive(*o, *oo, dyl_mine, dyl_got, dyl_far)
    out.step1()
    desk.arrive()
    for z in range(4):
        side_sums[z] = terms_sum([(h1_theirs[m][z], dfirst[m]) for m in range(2)]).astype(LOW)
    side_first = wire.send(side_sums, side_got, wire.beside)
    term = inner_cols(dfirst[...].reshape(2 * rows, dfirst.shape[2]), weights[...])
    for m in range(2):
        send[m] = term[m * rows + half : (m + 1) * rows].astype(LOW)
        kept[m] = term[m * rows : m * rows + half]
    row_sum.core.start()
    qup.step1()
    row_sum.pass_on()
    layer_share = Share(wire, layer_out, quarter)
    layer_share.begin(layer_own[...])
    out.step2()
    side_first.wait_recv()
    first.step1()
    qup.step2()
    dh1 = row_sum.result()
    gain1_sum = jnp.sum(jnp.sum(dh1 * n1[...], axis=0), axis=0, keepdims=True)
    back = dh1 * gain1[...]
    share = Share(wire, grad_tokens, quarter)
    share.begin(
        (dy[...] + inv1[...] * (back - n1[...] * mean_of(back * n1[...]))).astype(LOW)
    )
    w, r = gain1_sum.shape[1] // 8, gain_c_sum.shape[1] // 8
    for s in range(8):
        sums[s] = jnp.concatenate(
            [gain1_sum[:, s * w : (s + 1) * w], gain2_sum[:, s * w : (s + 1) * w],
             gain_c_sum[:, s * r : (s + 1) * r]], axis=1
        )
    core_sums = wire.send(sums, sums_core, wire.core)
    out.step3()
    core_sums.wait_recv()
    core_sums.wait_send()
    sums[...] = sums[...] + sums_core[...]
    cross_sums = wire.send(sums, sums_cross, wire.cross)
    qup.step3()
    first.step2()
    cross_sums.wait_recv()
    cross_sums.wait_send()
    sums[...] = sums[...] + sums_cross[...]
    side_of = lambda p, s: sums.at[2 * p + s]
    side_sends = [
        wire.send(side_of(p, 1 - wire.side), sums_side.at[p], wire.beside) for p in range(4)
    ]
    layer_share.forward()
    share.forward()
    first.step3()
    for made in side_sends:
        made.wait_recv()
        made.wait_send()
    line_sends = []
    for d in range(1, 4):
        for way, there in ((1, place + d <= 3), (-1, place - d >= 0)):
            index = 2 * (d - 1) + (way < 0)
            line_sends.append(
                (wire.copy(sums_line.at[6 + index], sums_line.at[index],
                           {"seq": wire.seq + 2 * way * d}), d, way, there)
            )

            @pl.when(there)
            def _(index=index, d=d, way=way):
                to = place + way * d
                sums_line[6 + index] = sums[2 * to + wire.side] + sums_side[to]
                line_sends[-1][0].start()

            @pl.when((place - way * d < 0) | (place - way * d > 3))
            def _(index=index):
                sums_line[index] = jnp.zeros(sums_line.shape[1:], F32)

    out.finish()
    desk.flush(grad_out)
    qup.finish()
    desk.flush(grad_qup)
    first.finish()
    cores = []
    size = kv_out.shape[0] // 4
    for k in range(4):
        rows_of = pl.ds(pl.multiple_of(wire.blocks[k] * size, size), size)
        if k:
            device = {"mp": wire.blocks[k]}
            cores.append(wire.send(kv_out.at[rows_of], kv_got.at[k], device))
        else:
            kv_got[0] = kv_out[rows_of]
    total = sums[2 * place + wire.side] + sums_side[place]
    for made, d, way, there in line_sends:
        pl.when((place - way * d >= 0) & (place - way * d <= 3))(made.wait_recv)
    for index in range(6):
        total = total + sums_line[index]
    gains[...] = total
    for made in cores:
        made.wait_recv()
    columns = kv_out.shape[1]
    for k in range(4):
        at = pl.ds(pl.multiple_of(wire.blocks[k] * columns, columns), columns)
        grad_kv[:, at] = kv_got[k]
    share.end()
    layer_share.end()
    for made in (side_first, *cores):
        made.wait_send()
    for made, d, way, there in line_sends:
        pl.when(there)(made.wait_send)
    row_sum.end()
    for chain in (out, qup, first):
        chain.settle()


def attend_one(
    scale, mp_blocks, c, gain, q_up, cos, sin, kv, key_ids, row_ids, row_starts, out_proj,
    qn, q, o, lse, send, keep, chat_out, inverse_out,
):
    rows = qn.shape[0]
    half, quarter = rows // 2, rows // 4
    part = c.shape[2]
    wide = q.shape[2]
    cut = lambda k, i: c[k, i * quarter : (i + 1) * quarter, :]
    pieces = [jnp.concatenate([cut(k, i ^ k) for i in range(4)], 0) for k in range(4)]
    latent = jnp.concatenate(pieces, 1).astype(F32)
    inverse = inverse_rms(latent)
    chat = latent * inverse
    inverse_out[...] = inverse[:quarter]
    for k in range(4):
        columns = pl.ds(pl.multiple_of(mp_blocks[k] * part, part), part)
        chat_out[:, columns] = chat[:quarter, k * part : (k + 1) * part]
        qn[:, columns] = (chat[:, k * part : (k + 1) * part] * gain[:, columns]).astype(LOW)
    bias = jnp.where((key_ids >= row_starts) & (key_ids <= row_ids), 0.0, NEG_LARGE)
    low = qn[...]
    for h in range(q.shape[0]):
        pre = dot(low, q_up[:, h * wide : (h + 1) * wide])
        q_h = (rotate(pre, cos, sin) * scale).astype(LOW)
        q[h] = q_h
        scores = inner_cols(q_h, kv[:, :wide]) + bias
        top = jnp.max(scores, axis=-1, keepdims=True)
        probs = jnp.exp(scores - top)
        total = jnp.sum(probs, axis=-1, keepdims=True)
        out = dot(probs.astype(LOW), kv[:, wide:]) / total
        o[:, h * wide : (h + 1) * wide] = out.astype(LOW)
        log_total = jnp.broadcast_to(top + jnp.log(total), (rows, 128))
        lse[h : h + 1, :] = jnp.transpose(log_total)[:1]
    keep[...] = dot(o[:half, :], out_proj[...])
    send[...] = dot(o[half:, :], out_proj[...]).astype(LOW)


def fore1_body(scale, desk, *refs):
    refs = list(refs)
    take = lambda n: [refs.pop(0) for _ in range(n)]
    tokens, cotangent, q_down, kv_proj, q_up, out_proj, w_down = take(7)
    lengths, gain1, gain_c, gain2, cosine, sine = take(6)
    h1_mine, h1_theirs, qn_mine, qn_theirs = (take(2) for _ in range(4))
    qs, os, lses, kvs, dz_got = (take(2) for _ in range(5))
    dhid, chat, inv_c, y_out, n2_out, inv2_out, n1_out, inv1_out, h2 = take(9)
    dz, x, down_w, kv_w, up_w, out_w, back_w, h1, c, qn, dz_theirs = take(11)
    send, kept, got, cross_out, cross_got = take(5)
    loads = take(1)[0]
    wire = Wire(*take(2))
    place, blocks = wire.place, wire.blocks
    rows = x.shape[1]
    half, quarter = rows // 2, rows // 4
    wide = kv_proj.shape[1] // 2

    started = []

    def load(source, target):
        made = pltpu.make_async_copy(source, target, loads.at[len(started)])
        made.start()
        started.append(made)
        return made

    def load_rows(source, target):
        return [
            load(source.at[pl.ds(pl.multiple_of(blocks[k] * quarter, quarter), quarter), :],
                 target.at[k * quarter : (k + 1) * quarter, :])
            for k in range(4)
        ]

    in_x = [load_rows(tokens.at[0], x.at[0])]
    in_kv = load(kv_proj, kv_w)
    in_x.append(load_rows(tokens.at[1], x.at[1]))
    in_down = load(q_down, down_w)
    in_dz = [load_rows(cotangent.at[m], dz.at[m]) for m in range(2)]
    in_back, in_up, in_out = load(w_down, back_w), load(q_up, up_w), load(out_proj, out_w)

    line_kv, side_kv, core_kv, cross_c, core_c = [], [], [], [], []
    for m in range(2):
        for d in range(1, 4):

            @pl.when(place < d)
            def _(m=m, d=d):
                kvs[m][0, :, d] = jnp.zeros(kvs[m].shape[1:2] + kvs[m].shape[3:], LOW)
                kvs[m][1, :, d] = jnp.zeros(kvs[m].shape[1:2] + kvs[m].shape[3:], LOW)

        own = kvs[m].at[0, 0, 0]
        line_kv.append([
            wire.copy(own, kvs[m].at[0, 0, d], {"seq": wire.seq + 2 * d}) for d in range(1, 4)
        ])
        side_kv.append([
            wire.copy(kvs[m].at[0, 0, d], kvs[m].at[0, 1, d], wire.beside) for d in range(4)
        ])
        core_kv.append([
            wire.copy(kvs[m].at[0, :, d], kvs[m].at[1, :, d], wire.core) for d in range(4)
        ])
        cross_c.append(wire.copy(c.at[m, 0], c.at[m, 1], wire.cross))
        core_c.append([
            wire.copy(c.at[m, 0], c.at[m, 2], wire.core),
            wire.copy(c.at[m, 1], c.at[m, 3], wire.core),
        ])
    wire.greet(4, 3)

    for m in range(2):
        cos, sin = cosine[m], sine[m]
        for made in in_x[m]:
            made.wait()
        if m == 0:
            in_kv.wait()
        values = x[m].astype(F32)
        inverse = inverse_rms(values)
        normed = values * inverse
        n1_out[m], inv1_out[m] = normed[:quarter], inverse[:quarter]
        low = (normed * gain1[...]).astype(LOW)
        h1[...] = low
        pair = dot(low[:half], kv_w[...])
        own = kvs[m].at[0, 0, 0]
        own[:, :wide] = rotate(pair[:, :wide], cos[:half], sin[:half]).astype(LOW)
        own[:, wide:] = pair[:, wide:].astype(LOW)
        for d in (3, 2, 1):
            pl.when(place + d <= 3)(line_kv[m][d - 1].start)
        side_kv[m][0].start()
        if m == 0:
            in_down.wait()
        c[m, 0] = dot(low, down_w[...]).astype(LOW)
        cross_c[m].start()
        core_c[m][0].start()
        side_columns(h1, h1_mine[m], h1_theirs[m], wire.side)
        desk.flush(h1_mine[m], h1_theirs[m])

    def pass_kv(m, d):
        @pl.when(place >= d)
        def _():
            line_kv[m][d - 1].wait_recv()
            side_kv[m][d].start()

    def pass_core(m, d):
        @pl.when(place >= d)
        def _():
            side_kv[m][d].wait_recv()
            core_kv[m][d].start()

    in_back.wait()
    for m in range(2):
        for made in in_dz[m]:
            made.wait()
    dhid[0] = inner_cols(dz[0], back_w[...])
    for d in (1, 2, 3):
        pass_kv(0, d)
    pass_core(0, 0)
    for m in range(2):
        cross_c[m].wait_recv()
        core_c[m][1].start()
    dhid[1] = inner_cols(dz[1], back_w[...])
    for d in (1, 2, 3):
        pass_kv(1, d)
    for m in range(2):
        for z in range(4):
            block = dz_theirs.shape[3]
            columns = pl.ds(pl.multiple_of((2 * z + 1 - wire.side) * block, block), block)
            dz_theirs[m, z] = dz[m, :half, columns]
    desk.flush(dhid, n1_out)
    for d in (1, 2, 3):
        pass_core(0, d)
    in_up.wait()
    in_out.wait()
    sums = [
        RowSum(wire, send.at[m : m + 1], kept.at[m : m + 1], got.at[m : m + 1],
               cross_out.at[m : m + 1], cross_got.at[m : m + 1], quarter)
        for m in range(2)
    ]
    shares = []

    def after_sum(m):
        value = x[m, :quarter, :].astype(F32) + sums[m].result()[0]
        inverse = inverse_rms(value)
        normed = value * inverse
        y_out[m], n2_out[m], inv2_out[m] = value, normed, inverse
        h2[m, :quarter, :] = (normed * gain2[...]).astype(LOW)
        spot = lambda k: h2.at[m, k * quarter : (k + 1) * quarter, :]
        shares.append((
            wire.send(spot(0), spot(1), wire.cross), wire.send(spot(0), spot(2), wire.core),
            wire.copy(spot(1), spot(3), wire.core),
        ))

    for m in range(2):
        if m == 1:
            for d in range(4):
                pass_core(1, d)
        for d in range(4):
            pl.when(place >= d)(core_kv[m][d].wait_recv)
        for made in core_c[m]:
            made.wait_recv()
        desk.flush(kvs[m])
        rows_at = row_places(wire, quarter, 0)
        attend_one(
            scale, blocks, c.at[m], gain_c, up_w, cosine[m], sine[m],
            kvs[m][...].reshape(2 * 2 * 4 * half, 2 * wide),
            key_places(wire, quarter, 4, 1, (0, 1)), rows_at,
            sequence_starts(lengths, m, rows_at), out_w, qn, qs[m], os[m], lses[m], send.at[m], kept.at[m],
            chat.at[m], inv_c.at[m],
        )
        sums[m].core.start()
        if m == 0:
            side_dz = wire.send(dz_theirs, dz_got[0], wire.beside)
        side_columns(qn, qn_mine[m], qn_theirs[m], wire.side)
        desk.flush(qs[m], os[m], qn_mine[m], qn_theirs[m])
        if m == 1:
            after_sum(0)
        sums[m].pass_on()
    after_sum(1)
    desk.flush(chat, y_out, n2_out)
    side_dz.wait_recv()
    core_dz = wire.send(dz_got[0], dz_got[1], wire.core)
    for near, _, far in shares:
        near.wait_recv()
        far.start()
    for _, first, far in shares:
        first.wait_recv()
        far.wait_recv()
    core_dz.wait_recv()
    for made in [side_dz, core_dz, *cross_c, *(a for p in core_c for a in p),
                 *(a for p in shares for a in p)]:
        made.wait_send()
    for m in range(2):
        sums[m].end()
        for d in range(4):

            @pl.when(place >= d)
            def _(m=m, d=d):
                side_kv[m][d].wait_send()
                core_kv[m][d].wait_send()

        for d in range(1, 4):
            pl.when(place + d <= 3)(line_kv[m][d - 1].wait_send)


def deliver_body(count, *refs):
    results, gains = refs[:count], refs[count]
    outs, rooms, sems = refs[count + 1 : -count - 1], refs[-count - 1 : -1], refs[-1]
    loads = [pltpu.make_async_copy(results[i], rooms[i], sems.at[i]) for i in range(count)]
    stores = [
        pltpu.make_async_copy(rooms[i], outs[i], sems.at[count + i]) for i in range(count)
    ]
    for made in loads:
        made.start()
    at = 0
    for ref in outs[count:]:
        ref[...] = gains[0, at : at + ref.shape[0]]
        at += ref.shape[0]
    for load, store in zip(loads, stores):
        load.wait()
        store.start()
    for made in stores:
        made.wait()


def local(
    tokens,
    lengths,
    norm1_gain,
    q_down,
    latent_gain,
    q_up,
    kv_proj,
    out_proj,
    norm2_gain,
    w_gate,
    w_up,
    w_down,
    cotangent,
):
    micro, rows, width = tokens.shape
    seq = lax.axis_size("seq")
    line = seq // 2
    at = lax.axis_index("seq").astype(jnp.int32)
    me = lax.axis_index("mp").astype(jnp.int32)
    place, side = at // 2, at % 2
    ids = jnp.stack([me, side])
    quarter, half = rows // 4, rows // 2
    head_dim = kv_proj.shape[1] // 2
    heads = q_up.shape[1] // head_dim
    part = q_down.shape[1]
    rank = q_up.shape[0]
    hidden = w_gate.shape[1]
    kv_part = kv_proj.shape[1] // 4
    wide = width // seq
    scale = head_dim ** (-0.5)
    key_count = seq * rows
    beside = [(i, i ^ 1) for i in range(seq)]
    narrow = line == 4 and micro == 2 and key_count <= 2048 and not wide % 128

    def swap(index):
        return ((index & 1) << 1) | (index >> 1)

    def to_natural(array, axis):
        size = array.shape[axis] // 4
        return jnp.concatenate(
            [lax.dynamic_slice_in_dim(array, swap(me ^ b) * size, size, axis) for b in range(4)],
            axis,
        )

    def other(array):
        return lax.ppermute(array, "seq", beside)

    def sum_mp(send, keep):
        kept = keep + lax.ppermute(send, "mp", CORE).astype(F32)
        got = lax.ppermute(kept[..., quarter:, :].astype(LOW), "mp", CROSS)
        return kept[..., :quarter, :] + got.astype(F32)

    def gather_mp(piece):
        near = lax.ppermute(piece, "mp", CROSS)
        pair = jnp.concatenate([piece, near], -2)
        return piece, near, lax.ppermute(pair, "mp", CORE)

    def sides_shape(columns, their_rows, lead=()):
        if columns // seq % 128:
            return []
        return [
            whole((*lead, line, n, columns // seq), LOW) for n in (rows, their_rows)
        ]

    def split_sides(made, full, their_rows):
        if made:
            return made
        split = full.reshape(*full.shape[:-1], line, 2, full.shape[-1] // seq)
        mine, theirs = (
            jnp.moveaxis(lax.dynamic_index_in_dim(split, i, split.ndim - 2, keepdims=False), -2, -3)
            for i in (side, 1 - side)
        )
        return mine, theirs[..., :their_rows, :]

    def from_other(theirs):
        got = other(theirs)
        return got, lax.ppermute(got, "mp", CORE)

    def without_sides(body, count):
        return body if count else lambda *refs: body(*refs, None, None)

    def both_sides(mine, got):
        lefts, spans = [], []
        for array, first, count, partner in (
            (mine, 0, rows, 0), (got[0], 0, half, 1), (got[1], half, half, 1)
        ):
            stacked_array = not isinstance(array, list)
            for m in range(micro):
                spans.append((len(lefts) if not stacked_array else len(lefts), m if stacked_array else None,
                              m, partner, first, count))
                if not stacked_array:
                    lefts.append(array[m])
            if stacked_array:
                lefts.append(array)
        return lefts, spans

    class Chain:
        def __init__(self, lefts, rights, terms, shape, turned=False, from_side=None):
            self.args = [*lefts, *rights]
            self.spec = (terms, len(lefts), len(rights))
            self.shape, self.turned = shape, turned
            self.from_side = [] if from_side is None else [from_side]
            self.step, self.up, self.down = 0, None, None

        def block(self, index, added, after, last=False):
            turned = last and self.turned
            body = functools.partial(
                block_body, *self.spec, len(added), len(self.from_side), turned
            )
            shape = self.shape[::-1] if turned else self.shape
            return run(
                body, index.reshape(1), [*self.args, *added, *self.from_side],
                [whole(shape, F32 if last else LOW)], after, name="block",
            )[0]

        def advance(self, after):
            self.step += 1
            step = self.step
            goes_up = [(i, i + 2) for i in range(2 * step)]
            goes_down = [(seq - 1 - i, seq - 3 - i) for i in range(2 * step)]
            for_up, for_down = line - step + place, step - line + place
            if 2 * step < line + 1:
                which = jnp.where(
                    place <= step - 1, for_up, jnp.where(place >= line - step, for_down, 0)
                )
                term = self.block(which, [a for a in (self.up, self.down) if a is not None], after)
                if step == 1 and line > 3:
                    self.up = lax.ppermute(term, "seq", goes_up + goes_down)
                else:
                    self.up = lax.ppermute(term, "seq", goes_up)
                    self.down = lax.ppermute(term, "seq", goes_down)
                return [term]
            term_up = self.block(jnp.clip(for_up, 0, line - 1), [self.up], after)
            term_down = self.block(jnp.clip(for_down, 0, line - 1), [self.down], [term_up])
            self.up = lax.ppermute(term_up, "seq", goes_up)
            self.down = lax.ppermute(term_down, "seq", goes_down)
            return [term_down]

        def finish(self, after):
            while self.step < line - 1:
                after = self.advance(after)
            result = self.block(place, [self.up, self.down], after, last=True)
            return result, [result]

    quarter_rows = jnp.arange(quarter, dtype=jnp.int32)
    row_ids = at * rows + jnp.concatenate([(me ^ k) * quarter + quarter_rows for k in ORDER])
    key_ids = (
        ((place - jnp.arange(line, dtype=jnp.int32)[None, None, :, None, None]) * 2
         + (side ^ jnp.arange(2, dtype=jnp.int32)[None, :, None, None, None])) * rows
        + (me ^ (jnp.arange(2, dtype=jnp.int32)[:, None, None, None, None]
                 + 2 * jnp.arange(2, dtype=jnp.int32)[None, None, None, :, None])) * quarter
        + quarter_rows[None, None, None, None, :]
    ).reshape(key_count)

    gain1_row, gain2_row, gain_c_row = norm1_gain[None, :], norm2_gain[None, :], latent_gain[None, :]
    kv_cols = lax.dynamic_slice_in_dim(kv_proj, me * kv_part, kv_part, 1)
    first_weights = jnp.concatenate([q_down, kv_cols], axis=1)
    low = lambda *shape: pltpu.VMEM(shape, LOW)
    full = lambda *shape: pltpu.VMEM(shape, F32)
    near = lambda *arrays: [(1, a) for a in arrays]
    far = lambda *arrays: [(0, a) for a in arrays]
    columns = heads * head_dim
    side_rows = rank // seq
    first_columns = part + kv_part

    def narrow_layer():
        numbers = lambda array: [(2, array)]
        late = lambda *arrays: [(3, a) for a in arrays]
        ends = jnp.cumsum(lengths, axis=1)
        first_end, second_end = ends[:, 0:1], ends[:, 1:2]
        places = row_ids[None, :] - jnp.where(
            row_ids >= second_end, second_end, jnp.where(row_ids >= first_end, first_end, 0)
        )
        freqs = BASE ** (-2.0 * jnp.arange(head_dim // 2, dtype=F32) / head_dim)
        angles = places.astype(F32)[:, :, None] * freqs
        cosine, sine = jnp.cos(angles), jnp.sin(angles)
        row_shape = whole((micro, quarter, width), F32)
        one_shape = whole((micro, quarter, 1), F32)
        side_shape = whole((micro, line, half, wide), LOW)
        args = far(tokens, cotangent, q_down, kv_proj, q_up, out_proj, w_down)
        args += numbers(lengths) + near(gain1_row, gain_c_row, gain2_row, cosine, sine)
        outs = late(*[whole((line, rows, wide), LOW)] * 4, *[whole((line, rows, side_rows), LOW)] * 4)
        outs += late(*[whole((heads, rows, head_dim), LOW)] * 2, *[whole((rows, columns), LOW)] * 2)
        outs += near(*[whole((heads, rows), F32)] * 2)
        outs += late(*[whole((2, 2, line, half, 2 * head_dim), LOW)] * 2)
        outs += far(*[side_shape] * 2)
        outs += late(
            whole((micro, rows, hidden), F32), whole((micro, quarter, rank), F32))
        outs += near(one_shape) + late(row_shape, row_shape) + near(one_shape) + late(row_shape)
        outs += near(one_shape) + late(whole((micro, rows, width), LOW))
        made = list(mesh_run(
            functools.partial(fore1_body, scale), args, outs,
            [low(micro, rows, width), low(micro, rows, width), low(width, part),
             low(width, 2 * head_dim),
             low(rank, columns), low(columns, width), low(hidden, width), low(rows, width),
             low(micro, 4, rows, part), low(rows, rank), low(micro, line, half, wide),
             low(micro, half, width), full(micro, half, width), low(micro, half, width),
             low(micro, quarter, width), low(micro, quarter, width),
             pltpu.SemaphoreType.DMA((24,))],
            4, "fore1", 60, 60,
        ))
        give = lambda n: [made.pop(0) for _ in range(n)]
        h1_mine, h1_theirs, qn_mine, qn_theirs = (give(2) for _ in range(4))
        qs, os, lses, kv, dz_got = (give(2) for _ in range(5))
        kv = [a.reshape(key_count, 2 * head_dim) for a in kv]
        dhid, chat, inv_c, y, n2, inv2, n1, inv1, h2 = give(9)

        ahead = hidden * 3 // 11 // 128 * 128
        args = far(w_gate, w_up, w_down, cotangent) + late(h2, dhid, n2)
        args += near(inv2, gain2_row) + late(*dz_got, y)
        outs = near(whole((hidden, wide), F32)) + late(row_shape) + near(whole((1, width), F32))
        outs += late(whole((micro, rows, width), LOW), whole((micro, line, rows, wide), LOW), side_shape)
        outs += near(whole((micro, quarter, width), LOW))
        outs += late(*[whole((rows, hidden), LOW)] * 6, *[whole((line, rows, wide), LOW)] * 2)
        outs += far(*[whole((line, half, wide), LOW)] * 4, *[whole((rows, hidden), LOW)] * 2)
        made = list(mesh_run(
            functools.partial(back1_body, quarter), args, outs,
            [low(width, hidden), low(width, hidden), low(rows, hidden - ahead),
             low(rows, hidden - ahead), low(micro, line, half, wide),
             low(5, wide, hidden - ahead), low(2, wide, hidden - ahead),
             low(micro, half, width), full(micro, half, width), low(micro, half, width),
             low(micro, quarter, width), low(micro, quarter, width),
             pltpu.SemaphoreType.DMA((2,)), low(micro, half, width), low(micro, half, width),
             low(micro, half, width), low(micro, quarter, width), low(micro, quarter, width),
             low(5, 2 * wide, ahead), low(2, 2 * wide, ahead), full(2, wide, ahead),
             low(wide, ahead), low(wide, ahead), low(micro, rows, width),
             pltpu.SemaphoreType.DMA((8,))],
            1, "back1", 62, 40,
        ))
        grad_down, dy, gain2, dyl, dyl_mine, dyl_theirs, layer_own = give(7)
        hid, dg, du, h2_mine, h2_got, h2_far, dg_other = (give(2) for _ in range(7))

        args = numbers(lengths) + late(*dg, *dg_other, *du, *h2_mine, *h2_got, *h2_far)
        args += late(dyl, out_proj, q_up, *qs, *kv, *os) + near(*lses)
        args += late(cosine, sine, chat) + near(inv_c, gain_c_row) + far(dyl_theirs)
        args += late(*qn_theirs) + far(*os)
        outs = late(whole((wide, hidden), F32), whole((wide, hidden), F32))
        outs += near(whole((micro, rows, first_columns), LOW), whole((1, rank), F32))
        outs += late(whole((micro, rows, columns), LOW))
        outs += far(side_shape, side_shape, whole((line, side_rows, columns), LOW),
                    *[whole((rows, columns), LOW)] * 2)
        kv_low = lambda *lead: low(*lead, quarter, 2 * head_dim)
        key_half = key_count // 2
        (grad_gate, grad_up, dfirst, gain_c, dqp, dyl_got, dyl_far, qup_side,
         *o_other) = mesh_run(
            functools.partial(back2_body, quarter, scale), args, outs,
            [low(rows, hidden), low(rows, hidden), low(5, wide, hidden), low(2, wide, hidden),
             low(5, wide, hidden), low(2, wide, hidden), full(heads * rows, head_dim),
             low(micro, half, rank),
             full(micro, half, rank), low(micro, key_half, 2 * head_dim),
             low(micro, key_half, 2 * head_dim), low(micro, half, rank),
             low(micro, quarter, rank), low(micro, quarter, rank),
             low(micro, key_half, 2 * head_dim), kv_low(micro, 2 * line), kv_low(micro, 2 * line),
             kv_low(micro, line), kv_low(micro, line), kv_low(micro, 3), kv_low(micro, 3),
             full(micro, quarter, 2 * head_dim), low(micro, rows, rank + 2 * head_dim),
             low(line, side_rows, columns)],
            2, "back2", 62, 44,
        )

        kv_cols = lax.dynamic_slice_in_dim(kv_proj, me * kv_part, kv_part, 1)
        first_weights = jnp.concatenate([q_down, kv_cols], axis=1)
        args = late(dfirst, first_weights, *h1_mine, *h1_theirs, *os, *o_other, dyl_mine, dyl_got,
                    dyl_far, *qn_mine, dqp, qup_side, n1)
        args += near(inv1) + late(dy) + near(gain1_row, gain2, gain_c, layer_own)
        block = width // 4 // seq
        gain_columns = 2 * wide + side_rows
        outs = late(whole((columns, wide), F32), whole((side_rows, columns), F32))
        outs += near(whole((wide, part), F32), whole((block, 2 * head_dim), F32),
                    whole((micro, rows, width), LOW), whole((1, gain_columns), F32),
                    whole((micro, rows, width), LOW))
        grad_out, grad_qup, grad_qdown, grad_kv, input_grads, gains, layer_out = mesh_run(
            functools.partial(back3_body, quarter), args, outs,
            [low(5, wide, columns), low(2, wide, columns), low(5, side_rows, columns),
             low(2, side_rows, columns), low(5, wide, first_columns),
             low(2, wide, first_columns), low(line, wide, first_columns),
             low(line, wide, first_columns), low(micro, half, width), full(micro, half, width),
             low(micro, half, width), low(micro, quarter, width), low(micro, quarter, width),
             full(wide, kv_part), full(4, block, kv_part), full(seq, 1, gain_columns),
             full(seq, 1, gain_columns), full(seq, 1, gain_columns), full(line, 1, gain_columns),
             full(12, 1, gain_columns)],
            3, "back3", 60, 44,
        )
        results = [layer_out, input_grads, grad_qdown, grad_qup, grad_kv, grad_out, grad_gate,
                   grad_up, grad_down]
        made = pl.pallas_call(
            functools.partial(deliver_body, len(results)),
            in_specs=[pl.BlockSpec(memory_space=pl.ANY)] * len(results) + [in_vmem()],
            out_specs=[pl.BlockSpec(memory_space=pl.ANY)] * len(results) + [in_vmem()] * 3,
            out_shape=[whole(a.shape, a.dtype) for a in results]
            + [whole((n,), F32) for n in (wide, wide, side_rows)],
            scratch_shapes=[pltpu.VMEM(a.shape, a.dtype) for a in results]
            + [pltpu.SemaphoreType.DMA((2 * len(results),))],
            compiler_params=pltpu.CompilerParams(vmem_limit_bytes=60 << 20),
            name="deliver",
        )(*results, gains)
        (layer_out, input_grads, grad_qdown, grad_qup, grad_kv, grad_out, grad_gate, grad_up,
         grad_down, grad_n1, grad_n2, grad_c) = made
        return (
            layer_out, input_grads, grad_n1, grad_qdown, grad_c, grad_qup, grad_kv, grad_out,
            grad_n2, grad_gate, grad_up, grad_down,
        )

    if narrow:
        return narrow_layer()

    both_rows = sides_shape(width, rows)
    half_rows = sides_shape(width, half)
    rank_sides = sides_shape(rank, rows)

    tables, starts, kv, c_part, h1_sides = [], [], [], [], []
    order = []
    for m in range(micro):
        _, places = documents(lengths[m], row_ids)
        starts.append(row_ids - places)
        tables.append(rotation(places, head_dim))
        c, packed, h1, *made = run(
            without_sides(functools.partial(first_body, m, quarter), len(both_rows)),
            ids,
            [tokens, gain1_row, q_down, kv_proj, *tables[m]],
            [whole((rows, part), LOW), whole((half, 2 * head_dim), LOW), whole((rows, width), LOW),
             *both_rows],
            order,
            name="first",
        )
        order = [c]
        blocks = [packed] + [
            lax.ppermute(packed, "seq", [(i, i + 2 * d) for i in range(seq - 2 * d)])
            for d in range(1, line)
        ]
        near = jnp.stack(blocks, 0)
        near = jnp.stack([near, other(near)], 0)
        kv.append(
            jnp.stack([near, lax.ppermute(near, "mp", CORE)], 0).reshape(key_count, 2 * head_dim)
        )
        c_part.append(c)
        h1_sides.append(split_sides(made, h1, rows))

    dhid, dz, *made = run(
        functools.partial(cotangent_body, micro, quarter),
        ids,
        [cotangent, w_down],
        [whole((micro, rows, hidden), F32), whole((micro, rows, width), LOW),
         *sides_shape(width, half, (micro,))],
        order,
        name="cotangent",
    )
    order = [dz]
    dz_mine, dz_theirs = split_sides(made, dz, half)
    dz_got = from_other(dz_theirs)

    qn_sides, qs, os, lses, sums, c_rows = [], [], [], [], [], []
    for m in range(micro):
        near = lax.ppermute(c_part[m], "mp", CROSS)
        swapped = jnp.concatenate(
            [near[quarter : 2 * quarter], near[:quarter], near[3 * quarter :],
             near[2 * quarter : 3 * quarter]], 0
        )
        far = lax.ppermute(jnp.concatenate([c_part[m], swapped], 1), "mp", CORE)
        qn, q, o, lse, send, keep, *made = run(
            without_sides(functools.partial(attend_body, scale), len(rank_sides)),
            ids,
            [c_part[m], near, far, gain_c_row, q_up, *tables[m], kv[m], key_ids[None, :],
             row_ids[:, None], starts[m][:, None], out_proj],
            [whole((rows, rank), LOW), whole((heads, rows, head_dim), LOW),
             whole((rows, heads * head_dim), LOW), whole((heads, rows), F32),
             whole((half, width), LOW), whole((half, width), F32), *rank_sides],
            order,
            name="attend",
        )
        order = [o]
        qn_sides.append(split_sides(made, qn, rows))
        qs.append(q)
        os.append(o)
        lses.append(lse)
        sums.append(sum_mp(send, keep))
        c_rows.append(
            jnp.concatenate([c_part[m][:quarter], swapped[:quarter], far[half : half + quarter]], 1)
        )

    h2_mine, h2_theirs, hid, dg, du, state = [], [], [], [], [], []
    for m in range(micro):
        x = lax.dynamic_slice_in_dim(tokens[m], me * quarter, quarter, 0).astype(F32)
        inv1 = inverse_rms(x)
        y = x + sums[m]
        inv2 = inverse_rms(y)
        n2 = y * inv2
        pieces = gather_mp((n2 * gain2_row).astype(LOW))
        h2, hid_m, dg_m, du_m, *made = run(
            without_sides(functools.partial(forward_body, m), len(half_rows)),
            ids,
            [*pieces, w_gate, w_up, dhid],
            [whole((rows, width), LOW), *[whole((rows, hidden), LOW)] * 3, *half_rows],
            order,
            name="forward",
        )
        order = [hid_m]
        mine, theirs = split_sides(made, h2, half)
        h2_mine.append(mine)
        h2_theirs.append(theirs)
        hid.append(hid_m)
        dg.append(dg_m)
        du.append(du_m)
        state.append(dict(x=x, n1=x * inv1, inv1=inv1, y=y, n2=n2, inv2=inv2, c=c_rows[m]))

    def stacked(name):
        return jnp.stack([st[name] for st in state], 0)

    def with_other(arrays):
        return [*arrays, *[other(a) for a in arrays]]

    def terms_of(spans):
        return [(a, lead, m + micro * partner, None, first, count)
                for a, lead, m, partner, first, count in spans]

    send, keep, ffn_send, ffn_keep = run(
        functools.partial(hidden_back_body, micro),
        ids,
        [*dg, *du, *hid, w_gate, w_up, w_down],
        [whole((micro, half, width), LOW), whole((micro, half, width), F32)] * 2,
        order,
        name="hidden_back",
    )
    lefts, spans = both_sides(dz_mine, dz_got)
    chain_down = Chain(lefts, with_other(hid), terms_of(spans), (wide, hidden), turned=True)
    lefts, spans = both_sides(h2_mine, [list(p) for p in zip(*[from_other(t) for t in h2_theirs])])
    chain_gate = Chain(lefts, with_other(dg), terms_of(spans), (wide, hidden))
    chain_up = Chain(lefts, with_other(du), terms_of(spans), (wide, hidden))

    order = chain_down.advance([send])
    dh2 = sum_mp(send, keep)
    y, n2, inv2, n1, inv1 = (stacked(k) for k in ("y", "n2", "inv2", "n1", "inv1"))
    dz_own = dz[:, :quarter].astype(F32)
    gain2 = jnp.sum(dh2 * n2, axis=(0, 1))
    dy = dz_own + norm_backward(dh2 * gain2_row, n2, inv2)
    for _ in range(2):
        order = chain_down.advance(order)
    order = chain_gate.advance(order)

    def attend_back(which, pieces):
        args = [*pieces, out_proj, q_up, key_ids[:, None]]
        for m in which:
            args += [qs[m], kv[m], os[m], lses[m], jnp.stack([row_ids, starts[m]], 0), *tables[m]]
        n = len(which)
        return run(
            functools.partial(attend_back_body, scale, n, min(1024, key_count // 2)),
            ids,
            args,
            [whole((n, rows, width), LOW), whole((n, rows, heads * head_dim), LOW),
             whole((n, half, rank), LOW), whole((n, half, rank), F32),
             whole((n, key_count // 2, 2 * head_dim), LOW),
             whole((n, key_count // 2, 2 * head_dim), F32), *sides_shape(width, half, (n,))],
            order,
            scratch=[pltpu.VMEM((heads, rows, head_dim), F32),
                     pltpu.VMEM((heads, rows, head_dim), LOW),
                     pltpu.VMEM((heads, 8, rows), F32)],
            name="attend_back",
            limit=56,
        )

    pieces = gather_mp(dy.astype(LOW))
    if key_count <= 2048:
        made = attend_back(range(micro), pieces)
    else:
        each = [attend_back([m], [p[m : m + 1] for p in pieces]) for m in range(micro)]
        made = [jnp.concatenate(parts, 0) for parts in zip(*each)]
    dyl, dqp, send, keep, kv_send, kv_keep, *made = made
    order = [send]
    dyl_mine, dyl_theirs = split_sides(made, dyl, half)
    lefts, spans = both_sides(dyl_mine, from_other(dyl_theirs))
    chain_out = Chain(lefts, with_other(os), terms_of(spans), (wide, heads * head_dim), turned=True)

    def side_sum(lefts, rights, shape, after):
        terms = [(m, None, 0, m, 0, rows) for m in range(micro)]
        (made,) = run(
            functools.partial(side_sum_body, terms, len(lefts)),
            ids,
            [*lefts, *rights],
            [whole((line, *shape), LOW)],
            after,
            name="side_sum",
        )
        return other(made), [made]

    def own_chain(side_pairs, right, shape, after):
        from_side, after = side_sum([p[1] for p in side_pairs], [right], shape, after)
        terms = [(m, None, 0, m, 0, rows) for m in range(micro)]
        return Chain([p[0] for p in side_pairs], [right], terms, shape, from_side=from_side), after

    shape = (rank // seq, heads * head_dim)
    chain_qup, order = own_chain(qn_sides, dqp, shape, order)
    order = chain_gate.advance(order)
    order = chain_up.advance(order)

    dqn = sum_mp(send, keep)
    c = stacked("c").astype(F32)
    inv_c = inverse_rms(c)
    chat = c * inv_c
    chat = to_natural(chat, 2)
    gain_c = jnp.sum(dqn * chat, axis=(0, 1))
    dc = norm_backward(dqn * gain_c_row, chat, inv_c).astype(LOW)

    dkv = kv_keep + lax.ppermute(kv_send, "mp", CORE).astype(F32)
    dkv = dkv.reshape(micro, 2, line, 2, quarter, 2 * head_dim)
    dkv = dkv[:, :, :, 0] + lax.ppermute(dkv[:, :, :, 1].astype(LOW), "mp", CROSS).astype(F32)
    dkv = dkv[:, 0] + other(dkv[:, 1].astype(LOW)).astype(F32)
    total = dkv[:, 0]
    for d in range(1, line):
        total = total + lax.ppermute(
            dkv[:, d].astype(LOW), "seq", [(i + 2 * d, i) for i in range(seq - 2 * d)]
        ).astype(F32)
    cosine = jnp.stack([t[0][:quarter] for t in tables], 0)
    sine = jnp.stack([t[1][:quarter] for t in tables], 0)
    dkv_low = jnp.concatenate(
        [unrotate(total[..., :head_dim], cosine, sine), total[..., head_dim:]], axis=-1
    ).astype(LOW)
    both = jnp.concatenate(gather_mp(jnp.concatenate([dc, dkv_low], -1)), -2)
    dfirst = jnp.concatenate(
        [lax.dynamic_slice_in_dim(both, me * part, part, 2),
         lax.dynamic_slice_in_dim(both, rank + me * kv_part, kv_part, 2)], -1
    )

    grad_down, order = chain_down.finish(order)
    order = chain_gate.advance(order)
    order = chain_up.advance(order)
    order = chain_out.advance(order)
    grad_gate, order = chain_gate.finish(order)
    order = chain_up.advance(order)
    order = chain_out.advance(order)
    grad_up, order = chain_up.finish(order)
    order = chain_qup.advance(order)
    order = chain_out.advance(order)
    chain_first, order = own_chain(h1_sides, dfirst, (wide, part + kv_part), order)
    order = chain_qup.advance(order)
    grad_out, order = chain_out.finish(order)
    order = chain_first.advance(order)
    order = chain_qup.advance(order)
    order = chain_first.advance(order)
    grad_qup, order = chain_qup.finish(order)
    order = chain_first.advance(order)
    grad_first, order = chain_first.finish(order)

    grad_qdown = grad_first[:, :part]
    kv_cols_grad = grad_first[:, part:]
    pieces = []
    for k in ORDER:
        size = kv_cols_grad.shape[0] // 4
        sent = lax.dynamic_slice_in_dim(kv_cols_grad, (me ^ k) * size, size, 0)
        pieces.append(lax.ppermute(sent, "mp", [(i, i ^ k) for i in range(4)]) if k else sent)
    grad_kv = to_natural(jnp.concatenate(pieces, 1), 1)

    def put_natural(pieces):
        return run(
            functools.partial(natural_body, micro, quarter),
            ids,
            pieces,
            [whole((micro, rows, width), LOW)],
            name="natural",
        )[0]

    part_sum = inner_cols(dfirst.reshape(micro * rows, -1), first_weights).reshape(micro, rows, width)
    dh1 = sum_mp(part_sum[:, half:].astype(LOW), part_sum[:, :half])
    gain1 = jnp.sum(dh1 * n1, axis=(0, 1))
    dx = (dy + norm_backward(dh1 * gain1_row, n1, inv1)).astype(LOW)
    input_grads = put_natural(gather_mp(dx))

    ffn = sum_mp(ffn_send, ffn_keep)
    layer_out = put_natural(gather_mp((y + ffn).astype(LOW)))

    gains = jnp.concatenate(
        [gain1.reshape(seq, -1), gain2.reshape(seq, -1), gain_c.reshape(seq, -1)], axis=1
    )
    gains = gains + lax.ppermute(gains, "mp", CORE)
    gains = gains + lax.ppermute(gains, "mp", CROSS)
    gain_sum = lax.dynamic_index_in_dim(gains, at, 0, keepdims=False)
    for k in range(1, seq):
        gain_sum = gain_sum + lax.ppermute(
            lax.dynamic_index_in_dim(gains, at ^ k, 0, keepdims=False),
            "seq",
            [(i, i ^ k) for i in range(seq)],
        )
    return (
        layer_out,
        input_grads,
        gain_sum[:wide],
        grad_qdown,
        gain_sum[2 * wide :],
        grad_qup,
        grad_kv,
        grad_out,
        gain_sum[wide : 2 * wide],
        grad_gate,
        grad_up,
        grad_down,
    )


def solution(mesh):
    placed = (
        P(None, "seq", None),
        P(),
        P(),
        P(None, "mp"),
        P(),
        P(None, "mp"),
        P(),
        P("mp", None),
        P(),
        P(None, "mp"),
        P(None, "mp"),
        P("mp", None),
        P(None, "seq", None),
    )
    return jax.shard_map(
        local,
        mesh=mesh,
        in_specs=placed,
        out_specs=(
            P(None, "seq", None),
            P(None, "seq", None),
            P("seq"),
            P("seq", "mp"),
            P("seq"),
            P("seq", "mp"),
            P(("seq", "mp"), None),
            P("mp", "seq"),
            P("seq"),
            P("seq", "mp"),
            P("seq", "mp"),
            P("mp", "seq"),
        ),
        check_vma=False,
    )
```

```python
import functools

import jax
import jax.numpy as jnp
from jax import lax
from jax.experimental import pallas as pl
from jax.experimental.pallas import tpu as pltpu
from jax.sharding import PartitionSpec as P

EPS = 1e-06
BASE = 10000.0
NEG_LARGE = -1e30
LOW = jnp.bfloat16
F32 = jnp.float32
ORDER = (0, 2, 1, 3)
CORE = [(i, i ^ 1) for i in range(4)]
CROSS = [(i, i ^ 2) for i in range(4)]


def inverse_rms(values):
    return lax.rsqrt(jnp.mean(values * values, axis=-1, keepdims=True) + EPS)


def norm_backward(grad_hat, normed, inverse):
    return inverse * (grad_hat - normed * jnp.mean(grad_hat * normed, axis=-1, keepdims=True))


def dot(left, right):
    return jnp.dot(left, right, preferred_element_type=F32)


def inner_rows(left, right):
    return lax.dot_general(left, right, (((0,), (0,)), ((), ())), preferred_element_type=F32)


def inner_cols(left, right):
    return lax.dot_general(left, right, (((1,), (1,)), ((), ())), preferred_element_type=F32)


def documents(lengths_row, rows):
    first_end = lengths_row[0]
    second_end = first_end + lengths_row[1]
    doc_ids = (rows >= first_end).astype(jnp.int32) + (rows >= second_end).astype(jnp.int32)
    starts = jnp.where(rows >= second_end, second_end, jnp.where(rows >= first_end, first_end, 0))
    return (doc_ids, rows - starts)


def rotation(positions, head_dim):
    half = head_dim // 2
    freqs = BASE ** (-2.0 * jnp.arange(half, dtype=F32) / head_dim)
    angles = positions.astype(F32)[:, None] * freqs[None, :]
    return (jnp.cos(angles), jnp.sin(angles))


def rotate(values, cosine, sine):
    half = values.shape[-1] // 2
    first = values[..., :half]
    second = values[..., half:]
    return jnp.concatenate(
        [first * cosine - second * sine, second * cosine + first * sine], axis=-1
    )


def unrotate(grads, cosine, sine):
    return rotate(grads, cosine, -sine)


def in_vmem():
    return pl.BlockSpec(memory_space=pltpu.VMEM)


def whole(shape, dtype):
    return jax.ShapeDtypeStruct(shape, dtype)


def run(body, ids, args, outs, after=(), scratch=(), name=None, limit=40):
    args, after = list(args), list(after)

    def without(*refs):
        body(*refs[: 1 + len(args)], *refs[1 + len(args) + len(after) :])

    return pl.pallas_call(
        without,
        grid_spec=pltpu.PrefetchScalarGridSpec(
            num_scalar_prefetch=1,
            grid=(1,),
            in_specs=[in_vmem()] * len(args) + [pl.BlockSpec(memory_space=pl.ANY)] * len(after),
            out_specs=[in_vmem()] * len(outs),
            scratch_shapes=list(scratch),
        ),
        out_shape=list(outs),
        cost_estimate=pl.CostEstimate(flops=1000, bytes_accessed=1000, transcendentals=0),
        compiler_params=pltpu.CompilerParams(vmem_limit_bytes=limit << 20),
        name=name,
    )(ids, *args, *after)


def side_columns(source, mine, theirs, side):
    line, _, wide = mine.shape
    rows = theirs.shape[1]
    for z in range(line):
        mine[z] = source[:, pl.ds(pl.multiple_of((2 * z + side) * wide, wide), wide)]
        theirs[z] = source[:rows, pl.ds(pl.multiple_of((2 * z + 1 - side) * wide, wide), wide)]


def first_body(m, quarter, ids, x_ref, gain, q_down, kv_proj, cos, sin, c, kv, h1, mine, theirs):
    blocks = [
        x_ref[m, pl.ds(pl.multiple_of((ids[0] ^ k) * quarter, quarter), quarter), :] for k in ORDER
    ]
    x = jnp.concatenate(blocks, 0).astype(F32)
    low = (x * inverse_rms(x) * gain[...]).astype(LOW)
    h1[...] = low
    half = 2 * quarter
    pair = dot(low[:half], kv_proj[...])
    wide = kv_proj.shape[1] // 2
    kv[:, :wide] = rotate(pair[:, :wide], cos[:half], sin[:half]).astype(LOW)
    kv[:, wide:] = pair[:, wide:].astype(LOW)
    c[...] = dot(low, q_down[...]).astype(LOW)
    if mine is not None:
        side_columns(h1, mine, theirs, ids[1])


def cotangent_body(micro, quarter, ids, z_ref, w_down, dhid, dz, *sides):
    for m in range(micro):
        blocks = [
            z_ref[m, pl.ds(pl.multiple_of((ids[0] ^ k) * quarter, quarter), quarter), :]
            for k in ORDER
        ]
        dz[m] = jnp.concatenate(blocks, 0)
        if sides:
            side_columns(dz.at[m], sides[0].at[m], sides[1].at[m], ids[1])
        dhid[m] = inner_cols(dz[m], w_down[...])


def attend_body(
    scale, ids, c0, c1, c2, gain, q_up, cos, sin, kv, key_ids, row_ids, row_starts, out_proj,
    qn, q, o, lse, send, keep, mine, theirs,
):
    rows = qn.shape[0]
    quarter = rows // 4
    part = c0.shape[1]
    wide = q.shape[2]
    got = c1[...]
    pair = jnp.concatenate(
        [got[quarter : 2 * quarter], got[:quarter], got[3 * quarter :], got[2 * quarter : 3 * quarter]],
        0,
    )
    far = jnp.concatenate([c2[2 * quarter :], c2[: 2 * quarter]], 0)
    c = jnp.concatenate([c0[...], pair, far], 1).astype(F32)
    chat = c * inverse_rms(c)
    for k, xor in enumerate(ORDER):
        columns = pl.ds(pl.multiple_of((ids[0] ^ xor) * part, part), part)
        qn[:, columns] = (chat[:, k * part : (k + 1) * part] * gain[:, columns]).astype(LOW)
    if mine is not None:
        side_columns(qn, mine, theirs, ids[1])
    bias = jnp.where(
        (key_ids[...] >= row_starts[...]) & (key_ids[...] <= row_ids[...]), 0.0, NEG_LARGE
    )
    low = qn[...]
    keys, values = kv[:, :wide], kv[:, wide:]
    for h in range(q.shape[0]):
        pre = dot(low, q_up[:, h * wide : (h + 1) * wide])
        q_h = (rotate(pre, cos[...], sin[...]) * scale).astype(LOW)
        q[h] = q_h
        scores = inner_cols(q_h, keys) + bias
        top = jnp.max(scores, axis=-1, keepdims=True)
        probs = jnp.exp(scores - top)
        total = jnp.sum(probs, axis=-1, keepdims=True)
        out = dot(probs.astype(LOW), values) / total
        o[:, h * wide : (h + 1) * wide] = out.astype(LOW)
        log_total = jnp.broadcast_to(top + jnp.log(total), (rows, 128))
        lse[h : h + 1, :] = jnp.transpose(log_total)[:1]
    half = 2 * quarter
    send[...] = dot(o[half:, :], out_proj[...]).astype(LOW)
    keep[...] = dot(o[:half, :], out_proj[...])


def forward_body(m, ids, a0, a1, a2, w_gate, w_up, dhid, h2, hid, dg, du, mine, theirs):
    h2[...] = jnp.concatenate([a0[...], a1[...], a2[...]], 0)
    if mine is not None:
        side_columns(h2, mine, theirs, ids[1])
    low = h2[...]
    g = dot(low, w_gate[...])
    u = dot(low, w_up[...])
    sig = jax.nn.sigmoid(g)
    swish = g * sig
    hid[...] = (swish * u).astype(LOW)
    back = dhid[m]
    dg[...] = (back * u * sig * (1.0 + g * (1.0 - sig))).astype(LOW)
    du[...] = (back * swish).astype(LOW)


def hidden_back_body(micro, ids, *refs):
    dgs, dus = refs[:micro], refs[micro : 2 * micro]
    hids = refs[2 * micro : 3 * micro]
    w_gate, w_up, w_down, send, keep, out_send, out_keep = refs[3 * micro :]
    half = send.shape[1]
    every = lambda parts: jnp.concatenate([part[...] for part in parts], 0)
    rows = 2 * half
    total = inner_cols(every(dgs), w_gate[...]) + inner_cols(every(dus), w_up[...])
    for m in range(micro):
        send[m] = total[m * rows + half : (m + 1) * rows].astype(LOW)
        keep[m] = total[m * rows : m * rows + half]
    total = dot(every(hids), w_down[...])
    for m in range(micro):
        out_send[m] = total[m * rows + half : (m + 1) * rows].astype(LOW)
        out_keep[m] = total[m * rows : m * rows + half]


def pick(ref, lead):
    return ref if lead is None else ref.at[lead]


def block_body(terms, lefts, rights, extra, from_side, turned, ids, *refs):
    left, refs = refs[:lefts], refs[lefts:]
    right, refs = refs[:rights], refs[rights:]
    added, out = refs[: extra + from_side], refs[-1]
    total = None
    for a, a_lead, b, b_lead, first, count in terms:
        rows = pick(right[b], b_lead)[first : first + count, :]
        term = inner_rows(pick(left[a], a_lead)[ids[0]], rows)
        total = term if total is None else total + term
    for i, ref in enumerate(added):
        total = total + (ref[ids[0]] if i >= extra else ref[...]).astype(F32)
    out[...] = jnp.transpose(total) if turned else total.astype(out.dtype)


def side_sum_body(terms, lefts, ids, *refs):
    left, right, out = refs[:lefts], refs[lefts:-1], refs[-1]
    for z in range(out.shape[0]):
        total = None
        for a, a_lead, b, b_lead, first, count in terms:
            rows = pick(right[b], b_lead)[first : first + count, :]
            term = inner_rows(pick(left[a], a_lead)[z], rows)
            total = term if total is None else total + term
        out[z] = total.astype(out.dtype)


def attend_back_body(
    scale, micro, chunk, ids, a0, a1, a2, out_proj, q_up, key_ids, *refs
):
    per = 7
    groups = [refs[m * per : (m + 1) * per] for m in range(micro)]
    dyl_out, dqp, send, keep, kv_send, kv_keep = refs[micro * per : micro * per + 6]
    dq_acc, do_acc, delta_acc = refs[-3:]
    sides = refs[micro * per + 6 : -3]
    for m in range(micro):
        q, kv, o, lse, row_ids, cos, sin = groups[m]
        heads, rows, wide = q.shape
        half_rows = rows // 2
        dyl = jnp.concatenate([a0[m], a1[m], a2[m]], 0)
        dyl_out[m] = dyl
        if sides:
            side_columns(dyl_out.at[m], sides[0].at[m], sides[1].at[m], ids[1])
        for h in range(heads):
            do = inner_cols(dyl, out_proj[h * wide : (h + 1) * wide, :]).astype(LOW)
            do_acc[h] = do
            delta = jnp.sum(
                do.astype(F32) * o[:, h * wide : (h + 1) * wide].astype(F32), axis=-1, keepdims=True
            )
            delta_acc[h] = jnp.transpose(jnp.broadcast_to(delta, (rows, 128)))[:8]
            dq_acc[h] = jnp.zeros((rows, wide), F32)
        count = kv.shape[0] // 2 // chunk
        for part, out in ((0, kv_keep), (1, kv_send)):

            def one(i, carry):
                base = pl.multiple_of((part * count + i) * chunk, chunk)
                keys = kv[pl.ds(base, chunk), :wide]
                values = kv[pl.ds(base, chunk), wide:]
                at = key_ids[pl.ds(base, chunk), :]
                bias = jnp.where((at >= row_ids[1:2, :]) & (at <= row_ids[0:1, :]), 0.0, NEG_LARGE)

                def head(h, sums):
                    dk, dv = sums
                    q_h, do_h = q[h], do_acc[h]
                    probs = jnp.exp(inner_cols(keys, q_h) + bias - lse[pl.ds(h, 1), :])
                    back = inner_cols(values, do_h) - delta_acc[h][:1]
                    ds = (probs * back).astype(LOW)
                    dv = dv + dot(probs.astype(LOW), do_h)
                    dk = dk + dot(ds, q_h)
                    dq_acc[h] = dq_acc[h] + inner_rows(ds, keys)
                    return dk, dv

                zero = jnp.zeros((chunk, wide), F32)
                dk, dv = lax.fori_loop(0, heads, head, (zero, zero))
                place = pl.ds(pl.multiple_of(i * chunk, chunk), chunk)
                out[m, place, :wide] = dk.astype(out.dtype)
                out[m, place, wide:] = dv.astype(out.dtype)
                return carry

            if count == 1:
                one(0, 0)
            else:
                lax.fori_loop(0, count, one, 0)
        for h in range(heads):
            dq = unrotate(dq_acc[h] * scale, cos[...], sin[...])
            dqp[m, :, h * wide : (h + 1) * wide] = dq.astype(LOW)
        low = dqp[m]
        send[m] = inner_cols(low[half_rows:], q_up[...]).astype(LOW)
        keep[m] = inner_cols(low[:half_rows], q_up[...])


def natural_body(micro, quarter, ids, a0, a1, a2, out):
    for m in range(micro):
        pieces = (a0[m], a1[m], a2[m, :quarter, :], a2[m, quarter:, :])
        for k, piece in zip(ORDER, pieces):
            out[m, pl.ds(pl.multiple_of((ids[0] ^ k) * quarter, quarter), quarter), :] = piece


class Wire:
    def __init__(self, sends, recvs):
        self.sends, self.recvs, self.used = sends, recvs, 0
        self.seq, self.mp = lax.axis_index("seq"), lax.axis_index("mp")
        self.place, self.side = self.seq // 2, self.seq % 2
        core, cross = self.mp % 2, self.mp // 2
        self.blocks = (
            self.mp, 2 * (1 - cross) + core, 2 * cross + 1 - core, 2 * (1 - cross) + 1 - core
        )
        self.core, self.cross = {"mp": self.blocks[2]}, {"mp": self.blocks[1]}
        self.beside = {"seq": self.seq + 1 - 2 * self.side}
        self.up, self.down = {"seq": self.seq + 2}, {"seq": self.seq - 2}

    def copy(self, source, target, device):
        at = self.used
        self.used += 1
        return pltpu.make_async_remote_copy(
            src_ref=source, dst_ref=target, send_sem=self.sends.at[at], recv_sem=self.recvs.at[at],
            device_id=device, device_id_type=pl.DeviceIdType.MESH,
        )

    def send(self, source, target, device):
        made = self.copy(source, target, device)
        made.start()
        return made

    def greet(self, line, far=1, diagonal=False):
        barrier = pltpu.get_barrier_semaphore()
        devices = [self.core, self.cross, self.beside]
        if diagonal:
            devices.append({"mp": self.blocks[3]})
        for device in devices:
            pl.semaphore_signal(barrier, 1, device_id=device, device_id_type=pl.DeviceIdType.MESH)
        for d in range(1, far + 1):
            for way, there in ((1, self.place < line - d), (-1, self.place >= d)):

                @pl.when(there)
                def _():
                    pl.semaphore_signal(
                        barrier, 1, device_id={"seq": self.seq + 2 * way * d},
                        device_id_type=pl.DeviceIdType.MESH,
                    )
        below, above = jnp.minimum(self.place, far), jnp.minimum(line - 1 - self.place, far)
        pl.semaphore_wait(barrier, len(devices) + below + above)


def along(pieces, axis):
    return pieces[0] if len(pieces) == 1 else jnp.concatenate(pieces, axis)


def pair_places(first, second, quarter, axis):
    shape = (2 * quarter, 1) if axis == 0 else (1, 2 * quarter)
    index = lax.broadcasted_iota(jnp.int32, shape, axis)
    return jnp.where(index < quarter, first * quarter + index, (second - 1) * quarter + index)


def row_places(wire, quarter, axis):
    b = wire.blocks
    pieces = [pair_places(b[i], b[i + 1], quarter, axis) for i in (0, 2)]
    return wire.seq * (4 * quarter) + along(pieces, axis)


def key_places(wire, quarter, line, axis, cores):
    pieces = []
    for core in cores:
        for side in (wire.side, 1 - wire.side):
            for d in range(line):
                base = ((wire.place - d) * 2 + side) * (4 * quarter)
                b = wire.blocks[2 * core : 2 * core + 2]
                pieces.append(base + pair_places(b[0], b[1], quarter, axis))
    return along(pieces, axis)


def sequence_starts(lengths, m, places):
    first_end = lengths[m, 0]
    second_end = first_end + lengths[m, 1]
    return jnp.where(
        places >= second_end, second_end, jnp.where(places >= first_end, first_end, 0)
    )


class LineSum:
    def __init__(self, wire, term, room, rows, columns, keep):
        got, out = room
        view = lambda ref, i: ref.at[i, :rows, :columns]
        self.place, self.term, self.keep = wire.place, term, keep
        self.got = [view(got, i) for i in range(5)]
        self.out = [view(out, i) for i in range(2)]
        one, two_up, two_down, three_up, three_down = self.got
        a, b = self.out
        self.one = wire.copy(a, one, wire.up), wire.copy(a, one, wire.down)
        self.two = wire.copy(b, two_up, wire.up), wire.copy(b, two_down, wire.down)
        self.three = wire.copy(a, three_up, wire.up), wire.copy(b, three_down, wire.down)

    def clear(self):
        place = self.place
        for ref, empty in zip(
            self.got, ((place == 0) | (place == 3),) * 3 + (place == 0, place == 3)
        ):

            @pl.when(empty)
            def _(ref=ref):
                ref[...] = jnp.zeros(ref.shape, ref.dtype)

    def step1(self):
        place = self.place

        @pl.when((place == 0) | (place == 3))
        def _():
            self.out[0][...] = self.term(3 - place).astype(LOW)

        pl.when(place == 0)(self.one[0].start)
        pl.when(place == 3)(self.one[1].start)

    def step2(self):
        place = self.place
        pl.when(place == 1)(self.one[0].wait_recv)
        pl.when(place == 2)(self.one[1].wait_recv)
        self.out[1][...] = (
            self.term((place + 2) % 4) + self.got[0][...].astype(F32)
        ).astype(LOW)
        pl.when(place <= 1)(self.two[0].start)
        pl.when(place >= 2)(self.two[1].start)

    def step3(self):
        place = self.place

        @pl.when((place == 1) | (place == 2))
        def _():
            self.two[0].wait_recv()
            self.two[1].wait_recv()

        pl.when(place == 0)(self.one[0].wait_send)
        pl.when(place == 3)(self.one[1].wait_send)

        @pl.when(place <= 2)
        def _():
            self.out[0][...] = (self.term(place + 1) + self.got[1][...].astype(F32)).astype(LOW)
            self.three[0].start()

        pl.when(place <= 1)(self.two[0].wait_send)
        pl.when(place >= 2)(self.two[1].wait_send)

        @pl.when(place >= 1)
        def _():
            self.out[1][...] = (self.term(place - 1) + self.got[2][...].astype(F32)).astype(LOW)
            self.three[1].start()

    def finish(self):
        place = self.place
        pl.when(place >= 1)(self.three[0].wait_recv)
        pl.when(place <= 2)(self.three[1].wait_recv)
        self.keep(
            self.term(place) + self.got[3][...].astype(F32) + self.got[4][...].astype(F32)
        )

    def settle(self):
        place = self.place
        pl.when(place <= 2)(self.three[0].wait_send)
        pl.when(place >= 1)(self.three[1].wait_send)


class Desk:
    def __init__(self, first, loads, stores):
        self.loads, self.stores, self.stored = loads, stores, []
        for _, made in first:
            made.start()
        self.waiting = list(first)

    def more(self):
        for _, made in self.loads:
            made.start()
        self.waiting += self.loads

    def arrive(self, *refs):
        rest = []
        for ref, made in self.waiting:
            if not refs or any(ref is other for other in refs):
                made.wait()
            else:
                rest.append((ref, made))
        self.waiting = rest

    def flush(self, *refs):
        rest = []
        for ref, made in self.stores:
            if not refs or any(ref is other for other in refs):
                made.start()
                self.stored.append(made)
            else:
                rest.append((ref, made))
        self.stores = rest

    def close(self):
        self.flush()
        for made in self.stored:
            made.wait()


SPACES = (pl.ANY, pltpu.VMEM, pltpu.SMEM, pl.ANY, pl.ANY)


def mesh_run(body, args, outs, scratch, number, name, limit, sends):
    late_in = [i for i, (kind, _) in enumerate(args) if kind >= 3]
    late_out = [i for i, (kind, _) in enumerate(outs) if kind == 3]

    def whole_body(*refs):
        refs = list(refs)
        take = lambda n: [refs.pop(0) for _ in range(n)]
        given, results, rooms_in, rooms_out = (
            take(len(args)), take(len(outs)), take(len(late_in)), take(len(late_out))
        )
        load_sems, store_sems = take(2)
        first, loads, stores = [], [], []
        for n, (i, room) in enumerate(zip(late_in, rooms_in)):
            made = pltpu.make_async_copy(given[i], room, load_sems.at[n])
            (first if args[i][0] == 3 else loads).append((room, made))
            given[i] = room
        for n, (i, room) in enumerate(zip(late_out, rooms_out)):
            stores.append((room, pltpu.make_async_copy(room, results[i], store_sems.at[n])))
            results[i] = room
        desk = Desk(first, loads, stores)
        body(desk, *given, *results, *refs)
        desk.close()

    room = lambda a: pltpu.VMEM(a.shape, a.dtype)
    return pl.pallas_call(
        whole_body,
        in_specs=[pl.BlockSpec(memory_space=SPACES[kind]) for kind, _ in args],
        out_specs=[pl.BlockSpec(memory_space=SPACES[kind]) for kind, _ in outs],
        out_shape=[shape for _, shape in outs],
        scratch_shapes=[
            *[room(args[i][1]) for i in late_in], *[room(outs[i][1]) for i in late_out],
            pltpu.SemaphoreType.DMA((max(1, len(late_in)),)),
            pltpu.SemaphoreType.DMA((max(1, len(late_out)),)),
            *scratch, pltpu.SemaphoreType.DMA((sends,)), pltpu.SemaphoreType.DMA((sends,)),
        ],
        cost_estimate=pl.CostEstimate(flops=1000, bytes_accessed=1000, transcendentals=0),
        compiler_params=pltpu.CompilerParams(
            collective_id=number, has_side_effects=True, vmem_limit_bytes=limit << 20
        ),
        name=name,
    )(*[array for _, array in args])


def attend_back_one(
    scale, keys_at, rows_at, starts, dyl, out_proj, q_up, q, kv, o, lse, cos, sin,
    dqp, send, keep, kv_send, kv_keep, dq_acc, between=None,
):
    heads, rows, wide = q.shape
    half_rows = rows // 2
    low = dyl[...]
    grads, deltas = [], []
    for h in range(heads):
        columns = slice(h * wide, (h + 1) * wide)
        do = inner_cols(low, out_proj[columns, :]).astype(LOW)
        grads.append(do)
        delta = jnp.sum(do.astype(F32) * o[:, columns].astype(F32), axis=-1, keepdims=True)
        deltas.append(jnp.transpose(jnp.broadcast_to(delta, (rows, 128)))[:1])
    do_all, delta_all = jnp.concatenate(grads, 0), jnp.concatenate(deltas, 1)
    q_all = q[...].reshape(heads * rows, wide)
    lse_all = jnp.concatenate([lse[h : h + 1, :] for h in range(heads)], 1)
    dq_acc[...] = jnp.zeros(dq_acc.shape, F32)
    count = kv.shape[0] // 2
    chunk = min(256, count)
    for part, out in ((1, kv_send), (0, kv_keep)):
        for first in range(0, count, chunk):
            span = slice(part * count + first, part * count + first + chunk)
            keys, values = kv[span, :wide], kv[span, wide:]
            at = keys_at[part][first : first + chunk]
            bias = jnp.where((at >= starts) & (at <= rows_at), 0.0, NEG_LARGE)
            scores = inner_cols(keys, q_all) + jnp.concatenate([bias] * heads, 1)
            probs = jnp.exp(scores - lse_all)
            ds = (probs * (inner_cols(values, do_all) - delta_all)).astype(LOW)
            spot = slice(first, first + chunk)
            out[spot, :wide] = dot(ds, q_all).astype(out.dtype)
            out[spot, wide:] = dot(probs.astype(LOW), do_all).astype(out.dtype)
            dq_acc[...] += inner_rows(ds, keys)
        if part and between is not None:
            between()
    for h in range(heads):
        dq = unrotate(dq_acc[h * rows : (h + 1) * rows, :] * scale, cos, sin)
        dqp[:, h * wide : (h + 1) * wide] = dq.astype(LOW)
    total = inner_cols(dqp[...], q_up[...])
    send[...] = total[half_rows:].astype(LOW)
    keep[...] = total[:half_rows]


def mean_of(values):
    return jnp.mean(values, axis=-1, keepdims=True)


def terms_sum(pairs):
    total = None
    for left, right in pairs:
        term = inner_rows(left, right)
        total = term if total is None else total + term
    return total


def back1_body(quarter, desk, *refs):
    refs = list(refs)
    take = lambda n: [refs.pop(0) for _ in range(n)]
    w_gate, w_up, w_down, cotangent, h2, dhid, n2, inv2, gain2, dz_got, dz_far, y = take(12)
    grad, dy, gain_sum, dyl, dyl_mine, dyl_theirs, layer_own = take(7)
    hid, dg, du, h2_mine = (take(2) for _ in range(4))
    h2_got, h2_far, dg_other = take(2), take(2), take(2)
    gate_w, up_w, hid_other0, hid_other1, h2_theirs, got, out = take(7)
    send, kept, core_got, cross_out, cross_got, loads = take(6)
    ffn_send, ffn_kept, ffn_got, ffn_out, ffn_back = take(5)
    early_got, early_out, early_sum, early_send, early_back, dz, row_loads = take(7)
    wire = Wire(*take(2))
    half, rows = 2 * quarter, 4 * quarter
    ahead = early_send.shape[1]
    block = early_send.shape[0]
    middle = ahead + (gate_w.shape[1] - ahead) // 2
    columns_of = [slice(0, ahead), slice(ahead, middle), slice(middle, gate_w.shape[1])]
    in_weights = []
    for i, columns in enumerate(columns_of):
        for j, (source, target) in enumerate(((w_gate, gate_w), (w_up, up_w))):
            in_weights.append(pltpu.make_async_copy(
                source.at[:, columns], target.at[:, columns], loads.at[2 * i + j]
            ))
    for made in in_weights[:2]:
        made.start()
    hid_other = (hid_other0, hid_other1)
    hid_all = (*(a.at[:, ahead:] for a in hid), *hid_other)

    def term(z):
        columns = pl.ds(pl.multiple_of((2 * z + wire.side) * block, block), block)
        return terms_sum(halves_terms(
            [dz[m, :, columns] for m in range(2)], [dz_got[m, z] for m in range(2)],
            [dz_far[m, z] for m in range(2)], hid_all, half))

    def early_term(z):
        columns = pl.ds(pl.multiple_of(z * 2 * block, 2 * block), 2 * block)
        return terms_sum([(dz[m, :, columns], hid[m][:, :ahead]) for m in range(2)])

    def keep(total):
        grad[ahead:, :] = jnp.transpose(total)

    def early_keep(total):
        early_sum[0], early_sum[1] = total[:block], total[block:]

    chain = LineSum(wire, term, (got, out), block, grad.shape[0] - ahead, keep)
    early = LineSum(wire, early_term, (early_got, early_out), 2 * block, ahead, early_keep)
    chain.clear()
    early.clear()
    wire.greet(4)
    desk.arrive(h2)
    for made in in_weights[2:]:
        made.start()
    desk.more()
    in_dz = []
    for m in range(2):
        for k in range(4):
            at = pl.ds(pl.multiple_of(wire.blocks[k] * quarter, quarter), quarter)
            in_dz.append(pltpu.make_async_copy(
                cotangent.at[m, at, :], dz.at[m, k * quarter : (k + 1) * quarter, :],
                row_loads.at[4 * m + k],
            ))
            in_dz[-1].start()
    for m in range(2):
        side_columns(h2.at[m], h2_mine[m], h2_theirs.at[m], wire.side)
    y_h2 = [wire.send(h2_theirs.at[m], h2_got[m], wire.beside) for m in range(2)]
    y_hid = []

    def columns_forward(m, i):
        columns = columns_of[i]
        if m == 0:
            for made in in_weights[2 * i : 2 * i + 2]:
                made.wait()
        g = dot(h2[m], gate_w[:, columns])
        u = dot(h2[m], up_w[:, columns])
        sig = jax.nn.sigmoid(g)
        swish = g * sig
        hid[m][:, columns] = (swish * u).astype(LOW)
        if i:
            there = hid_other[m].at[:, columns.start - ahead : columns.stop - ahead]
            y_hid.append(wire.send(hid[m].at[:, columns], there, wire.beside))
        if m == 0 and i == 0:
            desk.arrive()
        back = dhid[m, :, columns]
        dg[m][:, columns] = (back * u * sig * (1.0 + g * (1.0 - sig))).astype(LOW)
        du[m][:, columns] = (back * swish).astype(LOW)

    for m in range(2):
        columns_forward(m, 0)
    for made in in_dz:
        made.wait()
    early.step1()
    for m in range(2):
        columns_forward(m, 1)
        if m == 1:
            early.step2()
        columns_forward(m, 2)
        desk.flush(dg[m], du[m], hid[m], h2_mine[m])
    both = lambda pair: jnp.concatenate([pair[0][...], pair[1][...]], 0)
    total = inner_cols(both(dg), gate_w[...]) + inner_cols(both(du), up_w[...])
    for m in range(2):
        send[m] = total[m * rows + half : (m + 1) * rows].astype(LOW)
        kept[m] = total[m * rows : m * rows + half]
    sums = RowSum(wire, send, kept, core_got, cross_out, cross_got, quarter)
    sums.core.start()
    wide = gate_w.shape[1]
    rest = w_down.shape[1] - wide
    downs = [gate_w.at[:wide, :], up_w.at[:wide, :rest]]
    in_down = [
        pltpu.make_async_copy(w_down.at[:, :wide], downs[0], loads.at[0]),
        pltpu.make_async_copy(w_down.at[:, wide:], downs[1], loads.at[1]),
    ]
    for made in in_down:
        made.start()
    early.step3()
    sums.pass_on()
    for made in y_hid:
        made.wait_recv()
    y_next = y_h2 + [wire.send(dg[m], dg_other[m], wire.beside) for m in range(2)]
    chain.step1()
    for made in in_down:
        made.wait()
    low = both(hid)
    ffn_sum = RowSum(wire, ffn_send, ffn_kept, ffn_got, ffn_out, ffn_back, quarter)
    for columns, part in ((slice(0, wide), downs[0]), (slice(wide, None), downs[1])):
        total = dot(low, part[...])
        for m in range(2):
            ffn_send[m, :, columns] = total[m * rows + half : (m + 1) * rows].astype(LOW)
            ffn_kept[m, :, columns] = total[m * rows : m * rows + half].astype(LOW)
    ffn_sum.core.start()
    early.finish()
    early_send[...] = early_sum[1 - wire.side].astype(LOW)
    y_early = wire.send(early_send, early_back, wire.beside)
    dh2 = sums.result()
    gain_sum[...] = jnp.sum(jnp.sum(dh2 * n2[...], axis=0), axis=0, keepdims=True)
    back = dh2 * gain2[...]
    grad_y = dz[:, :quarter, :].astype(F32) + inv2[...] * (
        back - n2[...] * mean_of(back * n2[...])
    )
    dy[...] = grad_y
    dyl[:, :quarter, :] = grad_y.astype(LOW)
    cross_dyl = wire.send(dyl.at[:, :quarter, :], dyl.at[:, quarter:half, :], wire.cross)
    ffn_sum.pass_on()
    chain.step2()
    cross_dyl.wait_recv()
    core_dyl = wire.send(dyl.at[:, :half, :], dyl.at[:, half:, :], wire.core)
    core_h2 = []
    for i in range(2):
        y_next[i].wait_recv()
        core_h2.append(wire.send(h2_got[i], h2_far[i], wire.core))
    core_dyl.wait_recv()
    for m in range(2):
        side_columns(dyl.at[m], dyl_mine.at[m], dyl_theirs.at[m], wire.side)
    desk.flush(dy, dyl, dyl_mine, dyl_theirs)
    chain.step3()
    layer_own[...] = (y[...] + ffn_sum.result()).astype(LOW)
    y_early.wait_recv()
    grad[:ahead, :] = jnp.transpose(early_sum[wire.side] + early_back[...].astype(F32))
    for made in y_next[2:] + core_h2:
        made.wait_recv()
    chain.finish()
    for made in [*y_hid, cross_dyl, core_dyl, *y_next, *core_h2, y_early]:
        made.wait_send()
    sums.end()
    ffn_sum.end()
    early.settle()
    chain.settle()


class Share:
    def __init__(self, wire, out, quarter):
        spot = lambda block: out.at[:, pl.ds(pl.multiple_of(block * quarter, quarter), quarter), :]
        own, near = spot(wire.blocks[0]), spot(wire.blocks[1])
        self.own = own
        self.first = wire.copy(own, own, wire.cross)
        self.rest = wire.copy(own, own, wire.core), wire.copy(near, near, wire.core)

    def begin(self, value):
        self.own[...] = value
        self.first.start()
        self.rest[0].start()

    def forward(self):
        self.first.wait_recv()
        self.rest[1].start()

    def end(self):
        for made in self.rest:
            made.wait_recv()
        for made in (self.first, *self.rest):
            made.wait_send()


class RowSum:
    def __init__(self, wire, send, kept, got, cross_out, cross_got, quarter):
        self.kept, self.got, self.quarter = kept, got, quarter
        self.out, self.back = cross_out, cross_got
        self.core = wire.copy(send, got, wire.core)
        self.cross = wire.copy(cross_out, cross_got, wire.cross)

    def pass_on(self):
        self.core.wait_recv()
        rest = slice(self.quarter, None)
        self.out[...] = (self.kept[:, rest, :] + self.got[:, rest, :].astype(F32)).astype(LOW)
        self.cross.start()

    def result(self):
        self.cross.wait_recv()
        own = slice(0, self.quarter)
        return (
            self.kept[:, own, :] + self.got[:, own, :].astype(F32) + self.back[...].astype(F32)
        )

    def end(self):
        self.core.wait_send()
        self.cross.wait_send()


def halves_terms(mine, got, far, rights, half):
    pairs = [(mine[m], rights[m][...]) for m in range(2)]
    for m in range(2):
        pairs.append((got[m], rights[2 + m][:half, :]))
        pairs.append((far[m], rights[2 + m][half:, :]))
    return pairs


def back2_body(quarter, scale, desk, *refs):
    refs = list(refs)
    take = lambda n: [refs.pop(0) for _ in range(n)]
    (lengths,) = take(1)
    dg, dg_other, du, h2_mine, h2_got, h2_far = (take(2) for _ in range(6))
    dyl, out_proj, q_up = take(3)
    q, kv, o, lse = (take(2) for _ in range(4))
    cos, sin, chat, inv_c, gain_c, dyl_theirs = take(6)
    qn_theirs, os_far = take(2), take(2)
    grad_gate, grad_up, dfirst, gain_sum, dqp, dyl_got, dyl_far, qup_side = take(8)
    oo = take(2)
    du_other = take(2)
    got_a, out_a, got_b, out_b = take(4)
    dq_acc, dqn_send, dqn_keep, kv_send, kv_keep = take(5)
    dqn_got, dqn_out, dqn_back = take(3)
    kv_got, kv_out, kv_back, side_out, side_got, line_out, line_got, kv_own = take(8)
    both, side_sums = take(2)
    wire = Wire(*take(2))
    half, rows = 2 * quarter, 4 * quarter
    wide = kv_own.shape[2] // 2
    rank = chat.shape[2]
    place = wire.place

    y_du = [wire.copy(du[m], du_other[m], wire.beside) for m in range(2)]

    def chain(rights, grad, room):
        def term(z):
            return terms_sum(halves_terms(
                [a[z] for a in h2_mine], [a[z] for a in h2_got], [a[z] for a in h2_far], rights,
                half))

        def keep(total):
            grad[...] = total

        made = LineSum(wire, term, room, *grad.shape, keep)
        made.clear()
        return made

    gate = chain((*dg, *dg_other), grad_gate, (got_a, out_a))
    up = chain((*du, *du_other), grad_up, (got_b, out_b))
    dqn_sum, core_kv, cross_kv, side_kv, line_kv = [], [], [], [], []
    for m in range(2):
        one = lambda ref: ref.at[m : m + 1]
        dqn_sum.append(RowSum(wire, one(dqn_send), one(dqn_keep), one(dqn_got), one(dqn_out),
                              one(dqn_back), quarter))
        core_kv.append(wire.copy(kv_send.at[m], kv_got.at[m], wire.core))
        cross_kv.append(wire.copy(kv_out.at[m], kv_back.at[m], wire.cross))
        side_kv.append(wire.copy(side_out.at[m], side_got.at[m], wire.beside))
        line_kv.append([
            wire.copy(line_out.at[m, d - 1], line_got.at[m, d - 1], {"seq": wire.seq - 2 * d})
            for d in range(1, 4)
        ])
        for d in range(1, 4):

            @pl.when(place > 3 - d)
            def _(m=m, d=d):
                line_got[m, d - 1] = jnp.zeros(line_got.shape[2:], LOW)

    wire.greet(4, 3)
    desk.arrive(*du)
    for made in y_du:
        made.start()
    desk.arrive(*dg, *dg_other, *h2_mine, *h2_got, *h2_far)
    gate.step1()
    desk.arrive()

    def attend(m, between=None):
        rows_at = row_places(wire, quarter, 1)
        attend_back_one(
            scale, [key_places(wire, quarter, 4, 0, (core,)) for core in range(2)], rows_at,
            sequence_starts(lengths, m, rows_at), dyl.at[m], out_proj, q_up, q[m], kv[m], o[m],
            lse[m], cos[m], sin[m], dqp.at[m], dqn_send.at[m], dqn_keep.at[m], kv_send.at[m],
            kv_keep.at[m], dq_acc, between,
        )
        core_kv[m].start()
        dqn_sum[m].core.start()

    split = lambda ref, m: ref[m].reshape(8, 2, quarter, 2 * wide)

    def kv_cross(m):
        dqn_sum[m].pass_on()
        core_kv[m].wait_recv()
        kv_out[m] = (
            split(kv_keep, m)[:, 1].astype(F32) + split(kv_got, m)[:, 1].astype(F32)
        ).astype(LOW)
        cross_kv[m].start()

    def kv_sum(m, span):
        return (
            split(kv_keep, m)[span, 0].astype(F32) + split(kv_got, m)[span, 0].astype(F32)
            + kv_back[m, span].astype(F32)
        )

    def kv_side(m):
        cross_kv[m].wait_recv()
        side_out[m] = kv_sum(m, slice(4, 8)).astype(LOW)
        side_kv[m].start()

    def kv_line(m):
        side_kv[m].wait_recv()
        own = kv_sum(m, slice(0, 4)) + side_got[m].astype(F32)
        kv_own[m] = own[0]
        for d in range(1, 4):
            line_out[m, d - 1] = own[d].astype(LOW)
            pl.when(place >= d)(line_kv[m][d - 1].start)

    def latent(m):
        dqn = dqn_sum[m].result()[0]
        gain = jnp.sum(dqn * chat[m], axis=0, keepdims=True)
        gain_sum[...] = gain if m == 0 else gain_sum[...] + gain
        back = dqn * gain_c[...]
        both[m, :quarter, :rank] = (
            inv_c[m] * (back - chat[m] * mean_of(back * chat[m]))
        ).astype(LOW)

    y_late = []

    def start_up():
        for made in y_du:
            made.wait_recv()
        y_late.append(wire.send(dyl_theirs, dyl_got, wire.beside))
        y_late.extend(wire.send(os_far[m], oo[m], wire.beside) for m in range(2))
        up.step1()

    attend(0)
    kv_cross(0)
    gate.step2()
    attend(1, start_up)
    gate.step3()
    kv_cross(1)
    kv_side(0)
    latent(0)
    up.step2()
    latent(1)
    for z in range(4):
        side_sums[z] = terms_sum([(qn_theirs[m][z], dqp[m]) for m in range(2)]).astype(LOW)
    kv_side(1)
    side_qup = wire.send(side_sums, qup_side, wire.beside)
    side_dyl, *side_o = y_late
    desk.flush(dqp)
    kv_line(0)
    kv_line(1)
    gate.finish()
    desk.flush(grad_gate)
    for m in range(2):
        for d in range(1, 4):
            pl.when(place <= 3 - d)(line_kv[m][d - 1].wait_recv)
        total = kv_own[m]
        for d in range(1, 4):
            total = total + line_got[m, d - 1].astype(F32)
        both[m, :quarter, rank : rank + wide] = unrotate(
            total[:, :wide], cos[m, :quarter], sin[m, :quarter]
        ).astype(LOW)
        both[m, :quarter, rank + wide :] = total[:, wide:].astype(LOW)
    cross_both = wire.send(both.at[:, :quarter, :], both.at[:, quarter:half, :], wire.cross)
    up.step3()
    cross_both.wait_recv()
    core_both = wire.send(both.at[:, :half, :], both.at[:, half:, :], wire.core)
    side_dyl.wait_recv()
    core_dyl = wire.send(dyl_got, dyl_far, wire.core)
    core_both.wait_recv()
    part = rank // 4
    kv_part = wide // 2
    dfirst[:, :, :part] = both[:, :, pl.ds(pl.multiple_of(wire.mp * part, part), part)]
    dfirst[:, :, part:] = both[
        :, :, pl.ds(pl.multiple_of(rank + wire.mp * kv_part, kv_part), kv_part)
    ]
    up.finish()
    core_dyl.wait_recv()
    for made in (side_qup, *side_o):
        made.wait_recv()
    for made in [*y_du, *core_kv, *cross_kv, *side_kv, cross_both, core_both, side_dyl, core_dyl,
                 side_qup, *side_o]:
        made.wait_send()
    for m in range(2):
        dqn_sum[m].end()
        for d in range(1, 4):
            pl.when(place >= d)(line_kv[m][d - 1].wait_send)
    gate.settle()
    up.settle()


def back3_body(quarter, desk, *refs):
    refs = list(refs)
    take = lambda n: [refs.pop(0) for _ in range(n)]
    dfirst, q_down, kv_proj = take(3)
    h1_mine, h1_theirs, o, oo = (take(2) for _ in range(4))
    dyl_mine, dyl_got, dyl_far = take(3)
    qn_mine = take(2)
    dqp, qup_side, n1, inv1, dy, gain1, gain2_sum, gain_c_sum, layer_own = take(9)
    grad_out, grad_qup, grad_qdown, grad_kv, grad_tokens, gains, layer_out = take(7)
    got_a, out_a, got_b, out_b, got_c, out_c = take(6)
    side_sums, side_got = take(2)
    send, kept, row_got, row_out, row_back = take(5)
    kv_out, kv_got = take(2)
    sums, sums_core, sums_cross, sums_side, sums_line, weights, weight_loads = take(7)
    wire = Wire(*take(2))
    half, rows = 2 * quarter, 4 * quarter
    place = wire.place
    part, kv_part = grad_qdown.shape[1], kv_out.shape[1]
    wire.greet(4, 3, diagonal=True)


    def out_term(z):
        return terms_sum(halves_terms(
            [dyl_mine[m, z] for m in range(2)], [dyl_got[m, z] for m in range(2)],
            [dyl_far[m, z] for m in range(2)], (*o, *oo), half))

    def qup_term(z):
        return terms_sum([(qn_mine[m][z], dqp[m]) for m in range(2)]) + qup_side[z].astype(F32)

    def first_term(z):
        return terms_sum([(h1_mine[m][z], dfirst[m]) for m in range(2)]) + side_got[z].astype(F32)

    def keep_out(total):
        grad_out[...] = jnp.transpose(total)

    def keep_qup(total):
        grad_qup[...] = total

    def keep_first(total):
        grad_qdown[...] = total[:, :part]
        kv_out[...] = total[:, part:]

    out = LineSum(wire, out_term, (got_a, out_a), *grad_out.shape[::-1], keep_out)
    qup = LineSum(wire, qup_term, (got_b, out_b), *grad_qup.shape, keep_qup)
    first = LineSum(wire, first_term, (got_c, out_c), kv_out.shape[0], dfirst.shape[2], keep_first)
    for chain in (out, qup, first):
        chain.clear()
    row_sum = RowSum(wire, send, kept, row_got, row_out, row_back, quarter)
    desk.arrive()
    out.step1()
    desk.more()
    in_weights = [
        pltpu.make_async_copy(q_down, weights.at[:, :part], weight_loads.at[0]),
        pltpu.make_async_copy(
            kv_proj.at[:, pl.ds(pl.multiple_of(wire.mp * kv_part, kv_part), kv_part)],
            weights.at[:, part:], weight_loads.at[1],
        ),
    ]
    for made in in_weights:
        made.start()
    desk.arrive()
    for z in range(4):
        side_sums[z] = terms_sum([(h1_theirs[m][z], dfirst[m]) for m in range(2)]).astype(LOW)
    side_first = wire.send(side_sums, side_got, wire.beside)
    for made in in_weights:
        made.wait()
    term = inner_cols(dfirst[...].reshape(2 * rows, dfirst.shape[2]), weights[...])
    for m in range(2):
        send[m] = term[m * rows + half : (m + 1) * rows].astype(LOW)
        kept[m] = term[m * rows : m * rows + half]
    row_sum.core.start()
    qup.step1()
    row_sum.pass_on()
    layer_share = Share(wire, layer_out, quarter)
    layer_share.begin(layer_own[...])
    out.step2()
    side_first.wait_recv()
    first.step1()
    qup.step2()
    dh1 = row_sum.result()
    gain1_sum = jnp.sum(jnp.sum(dh1 * n1[...], axis=0), axis=0, keepdims=True)
    back = dh1 * gain1[...]
    share = Share(wire, grad_tokens, quarter)
    share.begin(
        (dy[...] + inv1[...] * (back - n1[...] * mean_of(back * n1[...]))).astype(LOW)
    )
    w, r = gain1_sum.shape[1] // 8, gain_c_sum.shape[1] // 8
    for s in range(8):
        sums[s] = jnp.concatenate(
            [gain1_sum[:, s * w : (s + 1) * w], gain2_sum[:, s * w : (s + 1) * w],
             gain_c_sum[:, s * r : (s + 1) * r]], axis=1
        )
    core_sums = wire.send(sums, sums_core, wire.core)
    out.step3()
    core_sums.wait_recv()
    core_sums.wait_send()
    sums[...] = sums[...] + sums_core[...]
    cross_sums = wire.send(sums, sums_cross, wire.cross)
    qup.step3()
    first.step2()
    cross_sums.wait_recv()
    cross_sums.wait_send()
    sums[...] = sums[...] + sums_cross[...]
    side_of = lambda p, s: sums.at[2 * p + s]
    side_sends = [
        wire.send(side_of(p, 1 - wire.side), sums_side.at[p], wire.beside) for p in range(4)
    ]
    layer_share.forward()
    share.forward()
    first.step3()
    for made in side_sends:
        made.wait_recv()
        made.wait_send()
    line_sends = []
    for d in range(1, 4):
        for way, there in ((1, place + d <= 3), (-1, place - d >= 0)):
            index = 2 * (d - 1) + (way < 0)
            line_sends.append(
                (wire.copy(sums_line.at[6 + index], sums_line.at[index],
                           {"seq": wire.seq + 2 * way * d}), d, way, there)
            )

            @pl.when(there)
            def _(index=index, d=d, way=way):
                to = place + way * d
                sums_line[6 + index] = sums[2 * to + wire.side] + sums_side[to]
                line_sends[-1][0].start()

            @pl.when((place - way * d < 0) | (place - way * d > 3))
            def _(index=index):
                sums_line[index] = jnp.zeros(sums_line.shape[1:], F32)

    out.finish()
    desk.flush(grad_out)
    qup.finish()
    desk.flush(grad_qup)
    first.finish()
    cores = []
    size = kv_out.shape[0] // 4
    for k in range(4):
        rows_of = pl.ds(pl.multiple_of(wire.blocks[k] * size, size), size)
        if k:
            device = {"mp": wire.blocks[k]}
            cores.append(wire.send(kv_out.at[rows_of], kv_got.at[k], device))
        else:
            kv_got[0] = kv_out[rows_of]
    total = sums[2 * place + wire.side] + sums_side[place]
    for made, d, way, there in line_sends:
        pl.when((place - way * d >= 0) & (place - way * d <= 3))(made.wait_recv)
    for index in range(6):
        total = total + sums_line[index]
    gains[...] = total
    for made in cores:
        made.wait_recv()
    columns = kv_out.shape[1]
    for k in range(4):
        at = pl.ds(pl.multiple_of(wire.blocks[k] * columns, columns), columns)
        grad_kv[:, at] = kv_got[k]
    share.end()
    layer_share.end()
    for made in (side_first, *cores):
        made.wait_send()
    for made, d, way, there in line_sends:
        pl.when(there)(made.wait_send)
    row_sum.end()
    for chain in (out, qup, first):
        chain.settle()


def attend_one(
    scale, mp_blocks, c, gain, q_up, cos, sin, kv, key_ids, row_ids, row_starts, out_proj,
    qn, q, o, lse, send, keep, chat_out, inverse_out,
):
    rows = qn.shape[0]
    half, quarter = rows // 2, rows // 4
    part = c.shape[2]
    wide = q.shape[2]
    cut = lambda k, i: c[k, i * quarter : (i + 1) * quarter, :]
    pieces = [jnp.concatenate([cut(k, i ^ k) for i in range(4)], 0) for k in range(4)]
    latent = jnp.concatenate(pieces, 1).astype(F32)
    inverse = inverse_rms(latent)
    chat = latent * inverse
    inverse_out[...] = inverse[:quarter]
    for k in range(4):
        columns = pl.ds(pl.multiple_of(mp_blocks[k] * part, part), part)
        chat_out[:, columns] = chat[:quarter, k * part : (k + 1) * part]
        qn[:, columns] = (chat[:, k * part : (k + 1) * part] * gain[:, columns]).astype(LOW)
    bias = jnp.where((key_ids >= row_starts) & (key_ids <= row_ids), 0.0, NEG_LARGE)
    low = qn[...]
    for h in range(q.shape[0]):
        pre = dot(low, q_up[:, h * wide : (h + 1) * wide])
        q_h = (rotate(pre, cos, sin) * scale).astype(LOW)
        q[h] = q_h
        scores = inner_cols(q_h, kv[:, :wide]) + bias
        top = jnp.max(scores, axis=-1, keepdims=True)
        probs = jnp.exp(scores - top)
        total = jnp.sum(probs, axis=-1, keepdims=True)
        out = dot(probs.astype(LOW), kv[:, wide:]) / total
        o[:, h * wide : (h + 1) * wide] = out.astype(LOW)
        log_total = jnp.broadcast_to(top + jnp.log(total), (rows, 128))
        lse[h : h + 1, :] = jnp.transpose(log_total)[:1]
    keep[...] = dot(o[:half, :], out_proj[...])
    send[...] = dot(o[half:, :], out_proj[...]).astype(LOW)


def fore1_body(scale, desk, *refs):
    refs = list(refs)
    take = lambda n: [refs.pop(0) for _ in range(n)]
    tokens, cotangent, q_down, kv_proj, q_up, out_proj, w_down = take(7)
    lengths, gain1, gain_c, gain2, cosine, sine = take(6)
    h1_mine, h1_theirs, qn_mine, qn_theirs = (take(2) for _ in range(4))
    qs, os, lses, kvs, dz_got = (take(2) for _ in range(5))
    dhid, chat, inv_c, y_out, n2_out, inv2_out, n1_out, inv1_out, h2 = take(9)
    dz, x, down_w, kv_w, up_w, out_w, back_w, h1, c, qn, dz_theirs = take(11)
    send, kept, got, cross_out, cross_got = take(5)
    loads = take(1)[0]
    wire = Wire(*take(2))
    place, blocks = wire.place, wire.blocks
    rows = x.shape[1]
    half, quarter = rows // 2, rows // 4
    wide = kv_proj.shape[1] // 2

    started = []

    def load(source, target):
        made = pltpu.make_async_copy(source, target, loads.at[len(started)])
        made.start()
        started.append(made)
        return made

    def load_rows(source, target):
        return [
            load(source.at[pl.ds(pl.multiple_of(blocks[k] * quarter, quarter), quarter), :],
                 target.at[k * quarter : (k + 1) * quarter, :])
            for k in range(4)
        ]

    in_x = [load_rows(tokens.at[0], x.at[0])]
    in_kv = load(kv_proj, kv_w)
    in_x.append(load_rows(tokens.at[1], x.at[1]))
    in_down = load(q_down, down_w)
    in_dz = [load_rows(cotangent.at[m], dz.at[m]) for m in range(2)]
    in_back, in_up, in_out = load(w_down, back_w), load(q_up, up_w), load(out_proj, out_w)

    line_kv, side_kv, core_kv, cross_c, core_c = [], [], [], [], []
    for m in range(2):
        for d in range(1, 4):

            @pl.when(place < d)
            def _(m=m, d=d):
                kvs[m][0, :, d] = jnp.zeros(kvs[m].shape[1:2] + kvs[m].shape[3:], LOW)
                kvs[m][1, :, d] = jnp.zeros(kvs[m].shape[1:2] + kvs[m].shape[3:], LOW)

        own = kvs[m].at[0, 0, 0]
        line_kv.append([
            wire.copy(own, kvs[m].at[0, 0, d], {"seq": wire.seq + 2 * d}) for d in range(1, 4)
        ])
        side_kv.append([
            wire.copy(kvs[m].at[0, 0, d], kvs[m].at[0, 1, d], wire.beside) for d in range(4)
        ])
        core_kv.append([
            wire.copy(kvs[m].at[0, :, d], kvs[m].at[1, :, d], wire.core) for d in range(4)
        ])
        cross_c.append(wire.copy(c.at[m, 0], c.at[m, 1], wire.cross))
        core_c.append([
            wire.copy(c.at[m, 0], c.at[m, 2], wire.core),
            wire.copy(c.at[m, 1], c.at[m, 3], wire.core),
        ])
    wire.greet(4, 3)

    for m in range(2):
        cos, sin = cosine[m], sine[m]
        for made in in_x[m]:
            made.wait()
        if m == 0:
            in_kv.wait()
        values = x[m].astype(F32)
        inverse = inverse_rms(values)
        normed = values * inverse
        n1_out[m], inv1_out[m] = normed[:quarter], inverse[:quarter]
        low = (normed * gain1[...]).astype(LOW)
        h1[...] = low
        pair = dot(low[:half], kv_w[...])
        own = kvs[m].at[0, 0, 0]
        own[:, :wide] = rotate(pair[:, :wide], cos[:half], sin[:half]).astype(LOW)
        own[:, wide:] = pair[:, wide:].astype(LOW)
        for d in (3, 2, 1):
            pl.when(place + d <= 3)(line_kv[m][d - 1].start)
        side_kv[m][0].start()
        if m == 0:
            in_down.wait()
        c[m, 0] = dot(low, down_w[...]).astype(LOW)
        cross_c[m].start()
        core_c[m][0].start()
        side_columns(h1, h1_mine[m], h1_theirs[m], wire.side)
        desk.flush(h1_mine[m], h1_theirs[m])

    def pass_kv(m, d):
        @pl.when(place >= d)
        def _():
            line_kv[m][d - 1].wait_recv()
            side_kv[m][d].start()

    def pass_core(m, d):
        @pl.when(place >= d)
        def _():
            side_kv[m][d].wait_recv()
            core_kv[m][d].start()

    in_back.wait()
    for m in range(2):
        for made in in_dz[m]:
            made.wait()
    dhid[0] = inner_cols(dz[0], back_w[...])
    for d in (1, 2, 3):
        pass_kv(0, d)
    pass_core(0, 0)
    for m in range(2):
        cross_c[m].wait_recv()
        core_c[m][1].start()
    dhid[1] = inner_cols(dz[1], back_w[...])
    for d in (1, 2, 3):
        pass_kv(1, d)
    for m in range(2):
        for z in range(4):
            block = dz_theirs.shape[3]
            columns = pl.ds(pl.multiple_of((2 * z + 1 - wire.side) * block, block), block)
            dz_theirs[m, z] = dz[m, :half, columns]
    desk.flush(dhid, n1_out)
    for d in (1, 2, 3):
        pass_core(0, d)
    in_up.wait()
    in_out.wait()
    sums = [
        RowSum(wire, send.at[m : m + 1], kept.at[m : m + 1], got.at[m : m + 1],
               cross_out.at[m : m + 1], cross_got.at[m : m + 1], quarter)
        for m in range(2)
    ]
    shares = []

    def after_sum(m):
        value = x[m, :quarter, :].astype(F32) + sums[m].result()[0]
        inverse = inverse_rms(value)
        normed = value * inverse
        y_out[m], n2_out[m], inv2_out[m] = value, normed, inverse
        h2[m, :quarter, :] = (normed * gain2[...]).astype(LOW)
        spot = lambda k: h2.at[m, k * quarter : (k + 1) * quarter, :]
        shares.append((
            wire.send(spot(0), spot(1), wire.cross), wire.send(spot(0), spot(2), wire.core),
            wire.copy(spot(1), spot(3), wire.core),
        ))

    for m in range(2):
        if m == 1:
            for d in range(4):
                pass_core(1, d)
        for d in range(4):
            pl.when(place >= d)(core_kv[m][d].wait_recv)
        for made in core_c[m]:
            made.wait_recv()
        desk.flush(kvs[m])
        rows_at = row_places(wire, quarter, 0)
        attend_one(
            scale, blocks, c.at[m], gain_c, up_w, cosine[m], sine[m],
            kvs[m][...].reshape(2 * 2 * 4 * half, 2 * wide),
            key_places(wire, quarter, 4, 1, (0, 1)), rows_at,
            sequence_starts(lengths, m, rows_at), out_w, qn, qs[m], os[m], lses[m], send.at[m], kept.at[m],
            chat.at[m], inv_c.at[m],
        )
        sums[m].core.start()
        if m == 0:
            side_dz = wire.send(dz_theirs, dz_got[0], wire.beside)
        side_columns(qn, qn_mine[m], qn_theirs[m], wire.side)
        desk.flush(qs[m], os[m], qn_mine[m], qn_theirs[m])
        if m == 1:
            after_sum(0)
        sums[m].pass_on()
    after_sum(1)
    desk.flush(chat, y_out, n2_out)
    side_dz.wait_recv()
    core_dz = wire.send(dz_got[0], dz_got[1], wire.core)
    for near, _, far in shares:
        near.wait_recv()
        far.start()
    for _, first, far in shares:
        first.wait_recv()
        far.wait_recv()
    core_dz.wait_recv()
    for made in [side_dz, core_dz, *cross_c, *(a for p in core_c for a in p),
                 *(a for p in shares for a in p)]:
        made.wait_send()
    for m in range(2):
        sums[m].end()
        for d in range(4):

            @pl.when(place >= d)
            def _(m=m, d=d):
                side_kv[m][d].wait_send()
                core_kv[m][d].wait_send()

        for d in range(1, 4):
            pl.when(place + d <= 3)(line_kv[m][d - 1].wait_send)


def deliver_body(count, pieces, *refs):
    results, gains = refs[:count], refs[count]
    outs, rooms, sems = refs[count + 1 : -count - 1], refs[-count - 1 : -1], refs[-1]
    loads, stores = [], []
    for source, room, target in zip(results, rooms, outs):
        size = source.shape[-2] // pieces
        for i in range(pieces):
            cut = (slice(None),) * (len(source.shape) - 2) + (slice(i * size, (i + 1) * size),)
            at = len(loads)
            loads.append(pltpu.make_async_copy(source.at[cut], room.at[cut], sems.at[2 * at]))
            stores.append(pltpu.make_async_copy(room.at[cut], target.at[cut], sems.at[2 * at + 1]))
    for made in loads:
        made.start()
    at = 0
    for ref in outs[count:]:
        ref[...] = gains[0, at : at + ref.shape[0]]
        at += ref.shape[0]
    for load, store in zip(loads, stores):
        load.wait()
        store.start()
    for made in stores:
        made.wait()


def local(
    tokens,
    lengths,
    norm1_gain,
    q_down,
    latent_gain,
    q_up,
    kv_proj,
    out_proj,
    norm2_gain,
    w_gate,
    w_up,
    w_down,
    cotangent,
):
    micro, rows, width = tokens.shape
    seq = lax.axis_size("seq")
    line = seq // 2
    at = lax.axis_index("seq").astype(jnp.int32)
    me = lax.axis_index("mp").astype(jnp.int32)
    place, side = at // 2, at % 2
    ids = jnp.stack([me, side])
    quarter, half = rows // 4, rows // 2
    head_dim = kv_proj.shape[1] // 2
    heads = q_up.shape[1] // head_dim
    part = q_down.shape[1]
    rank = q_up.shape[0]
    hidden = w_gate.shape[1]
    kv_part = kv_proj.shape[1] // 4
    wide = width // seq
    scale = head_dim ** (-0.5)
    key_count = seq * rows
    beside = [(i, i ^ 1) for i in range(seq)]
    narrow = line == 4 and micro == 2 and key_count <= 2048 and not wide % 128

    def swap(index):
        return ((index & 1) << 1) | (index >> 1)

    def to_natural(array, axis):
        size = array.shape[axis] // 4
        return jnp.concatenate(
            [lax.dynamic_slice_in_dim(array, swap(me ^ b) * size, size, axis) for b in range(4)],
            axis,
        )

    def other(array):
        return lax.ppermute(array, "seq", beside)

    def sum_mp(send, keep):
        kept = keep + lax.ppermute(send, "mp", CORE).astype(F32)
        got = lax.ppermute(kept[..., quarter:, :].astype(LOW), "mp", CROSS)
        return kept[..., :quarter, :] + got.astype(F32)

    def gather_mp(piece):
        near = lax.ppermute(piece, "mp", CROSS)
        pair = jnp.concatenate([piece, near], -2)
        return piece, near, lax.ppermute(pair, "mp", CORE)

    def sides_shape(columns, their_rows, lead=()):
        if columns // seq % 128:
            return []
        return [
            whole((*lead, line, n, columns // seq), LOW) for n in (rows, their_rows)
        ]

    def split_sides(made, full, their_rows):
        if made:
            return made
        split = full.reshape(*full.shape[:-1], line, 2, full.shape[-1] // seq)
        mine, theirs = (
            jnp.moveaxis(lax.dynamic_index_in_dim(split, i, split.ndim - 2, keepdims=False), -2, -3)
            for i in (side, 1 - side)
        )
        return mine, theirs[..., :their_rows, :]

    def from_other(theirs):
        got = other(theirs)
        return got, lax.ppermute(got, "mp", CORE)

    def without_sides(body, count):
        return body if count else lambda *refs: body(*refs, None, None)

    def both_sides(mine, got):
        lefts, spans = [], []
        for array, first, count, partner in (
            (mine, 0, rows, 0), (got[0], 0, half, 1), (got[1], half, half, 1)
        ):
            stacked_array = not isinstance(array, list)
            for m in range(micro):
                spans.append((len(lefts) if not stacked_array else len(lefts), m if stacked_array else None,
                              m, partner, first, count))
                if not stacked_array:
                    lefts.append(array[m])
            if stacked_array:
                lefts.append(array)
        return lefts, spans

    class Chain:
        def __init__(self, lefts, rights, terms, shape, turned=False, from_side=None):
            self.args = [*lefts, *rights]
            self.spec = (terms, len(lefts), len(rights))
            self.shape, self.turned = shape, turned
            self.from_side = [] if from_side is None else [from_side]
            self.step, self.up, self.down = 0, None, None

        def block(self, index, added, after, last=False):
            turned = last and self.turned
            body = functools.partial(
                block_body, *self.spec, len(added), len(self.from_side), turned
            )
            shape = self.shape[::-1] if turned else self.shape
            return run(
                body, index.reshape(1), [*self.args, *added, *self.from_side],
                [whole(shape, F32 if last else LOW)], after, name="block",
            )[0]

        def advance(self, after):
            self.step += 1
            step = self.step
            goes_up = [(i, i + 2) for i in range(2 * step)]
            goes_down = [(seq - 1 - i, seq - 3 - i) for i in range(2 * step)]
            for_up, for_down = line - step + place, step - line + place
            if 2 * step < line + 1:
                which = jnp.where(
                    place <= step - 1, for_up, jnp.where(place >= line - step, for_down, 0)
                )
                term = self.block(which, [a for a in (self.up, self.down) if a is not None], after)
                if step == 1 and line > 3:
                    self.up = lax.ppermute(term, "seq", goes_up + goes_down)
                else:
                    self.up = lax.ppermute(term, "seq", goes_up)
                    self.down = lax.ppermute(term, "seq", goes_down)
                return [term]
            term_up = self.block(jnp.clip(for_up, 0, line - 1), [self.up], after)
            term_down = self.block(jnp.clip(for_down, 0, line - 1), [self.down], [term_up])
            self.up = lax.ppermute(term_up, "seq", goes_up)
            self.down = lax.ppermute(term_down, "seq", goes_down)
            return [term_down]

        def finish(self, after):
            while self.step < line - 1:
                after = self.advance(after)
            result = self.block(place, [self.up, self.down], after, last=True)
            return result, [result]

    quarter_rows = jnp.arange(quarter, dtype=jnp.int32)
    row_ids = at * rows + jnp.concatenate([(me ^ k) * quarter + quarter_rows for k in ORDER])
    key_ids = (
        ((place - jnp.arange(line, dtype=jnp.int32)[None, None, :, None, None]) * 2
         + (side ^ jnp.arange(2, dtype=jnp.int32)[None, :, None, None, None])) * rows
        + (me ^ (jnp.arange(2, dtype=jnp.int32)[:, None, None, None, None]
                 + 2 * jnp.arange(2, dtype=jnp.int32)[None, None, None, :, None])) * quarter
        + quarter_rows[None, None, None, None, :]
    ).reshape(key_count)

    gain1_row, gain2_row, gain_c_row = norm1_gain[None, :], norm2_gain[None, :], latent_gain[None, :]
    kv_cols = lax.dynamic_slice_in_dim(kv_proj, me * kv_part, kv_part, 1)
    first_weights = jnp.concatenate([q_down, kv_cols], axis=1)
    low = lambda *shape: pltpu.VMEM(shape, LOW)
    full = lambda *shape: pltpu.VMEM(shape, F32)
    near = lambda *arrays: [(1, a) for a in arrays]
    far = lambda *arrays: [(0, a) for a in arrays]
    columns = heads * head_dim
    side_rows = rank // seq
    first_columns = part + kv_part

    def narrow_layer():
        numbers = lambda array: [(2, array)]
        late = lambda *arrays: [(3, a) for a in arrays]
        later = lambda *arrays: [(4, a) for a in arrays]
        ends = jnp.cumsum(lengths, axis=1)
        first_end, second_end = ends[:, 0:1], ends[:, 1:2]
        places = row_ids[None, :] - jnp.where(
            row_ids >= second_end, second_end, jnp.where(row_ids >= first_end, first_end, 0)
        )
        freqs = BASE ** (-2.0 * jnp.arange(head_dim // 2, dtype=F32) / head_dim)
        angles = places.astype(F32)[:, :, None] * freqs
        cosine, sine = jnp.cos(angles), jnp.sin(angles)
        row_shape = whole((micro, quarter, width), F32)
        one_shape = whole((micro, quarter, 1), F32)
        side_shape = whole((micro, line, half, wide), LOW)
        args = far(tokens, cotangent, q_down, kv_proj, q_up, out_proj, w_down)
        args += numbers(lengths) + near(gain1_row, gain_c_row, gain2_row, cosine, sine)
        outs = late(*[whole((line, rows, wide), LOW)] * 4, *[whole((line, rows, side_rows), LOW)] * 4)
        outs += late(*[whole((heads, rows, head_dim), LOW)] * 2, *[whole((rows, columns), LOW)] * 2)
        outs += near(*[whole((heads, rows), F32)] * 2)
        outs += late(*[whole((2, 2, line, half, 2 * head_dim), LOW)] * 2)
        outs += far(*[side_shape] * 2)
        outs += late(
            whole((micro, rows, hidden), F32), whole((micro, quarter, rank), F32))
        outs += near(one_shape) + late(row_shape, row_shape) + near(one_shape) + late(row_shape)
        outs += near(one_shape) + late(whole((micro, rows, width), LOW))
        made = list(mesh_run(
            functools.partial(fore1_body, scale), args, outs,
            [low(micro, rows, width), low(micro, rows, width), low(width, part),
             low(width, 2 * head_dim),
             low(rank, columns), low(columns, width), low(hidden, width), low(rows, width),
             low(micro, 4, rows, part), low(rows, rank), low(micro, line, half, wide),
             low(micro, half, width), full(micro, half, width), low(micro, half, width),
             low(micro, quarter, width), low(micro, quarter, width),
             pltpu.SemaphoreType.DMA((24,))],
            4, "fore1", 60, 60,
        ))
        give = lambda n: [made.pop(0) for _ in range(n)]
        h1_mine, h1_theirs, qn_mine, qn_theirs = (give(2) for _ in range(4))
        qs, os, lses, kv, dz_got = (give(2) for _ in range(5))
        kv = [a.reshape(key_count, 2 * head_dim) for a in kv]
        dhid, chat, inv_c, y, n2, inv2, n1, inv1, h2 = give(9)

        ahead = hidden * 3 // 11 // 128 * 128
        args = far(w_gate, w_up, w_down, cotangent) + late(h2) + later(dhid, n2)
        args += near(inv2, gain2_row) + later(*dz_got, y)
        outs = near(whole((hidden, wide), F32)) + late(row_shape) + near(whole((1, width), F32))
        outs += late(whole((micro, rows, width), LOW), whole((micro, line, rows, wide), LOW), side_shape)
        outs += near(whole((micro, quarter, width), LOW))
        outs += late(*[whole((rows, hidden), LOW)] * 6, *[whole((line, rows, wide), LOW)] * 2)
        outs += far(*[whole((line, half, wide), LOW)] * 4, *[whole((rows, hidden), LOW)] * 2)
        made = list(mesh_run(
            functools.partial(back1_body, quarter), args, outs,
            [low(width, hidden), low(width, hidden), low(rows, hidden - ahead),
             low(rows, hidden - ahead), low(micro, line, half, wide),
             low(5, wide, hidden - ahead), low(2, wide, hidden - ahead),
             low(micro, half, width), full(micro, half, width), low(micro, half, width),
             low(micro, quarter, width), low(micro, quarter, width),
             pltpu.SemaphoreType.DMA((6,)), low(micro, half, width), low(micro, half, width),
             low(micro, half, width), low(micro, quarter, width), low(micro, quarter, width),
             low(5, 2 * wide, ahead), low(2, 2 * wide, ahead), full(2, wide, ahead),
             low(wide, ahead), low(wide, ahead), low(micro, rows, width),
             pltpu.SemaphoreType.DMA((8,))],
            1, "back1", 62, 40,
        ))
        grad_down, dy, gain2, dyl, dyl_mine, dyl_theirs, layer_own = give(7)
        hid, dg, du, h2_mine, h2_got, h2_far, dg_other = (give(2) for _ in range(7))

        args = numbers(lengths) + late(*dg, *dg_other, *du, *h2_mine, *h2_got, *h2_far)
        args += late(dyl, out_proj, q_up, *qs, *kv, *os) + near(*lses)
        args += late(cosine, sine, chat) + near(inv_c, gain_c_row) + far(dyl_theirs)
        args += late(*qn_theirs) + far(*os)
        outs = late(whole((wide, hidden), F32), whole((wide, hidden), F32))
        outs += near(whole((micro, rows, first_columns), LOW), whole((1, rank), F32))
        outs += late(whole((micro, rows, columns), LOW))
        outs += far(side_shape, side_shape, whole((line, side_rows, columns), LOW),
                    *[whole((rows, columns), LOW)] * 2)
        kv_low = lambda *lead: low(*lead, quarter, 2 * head_dim)
        key_half = key_count // 2
        (grad_gate, grad_up, dfirst, gain_c, dqp, dyl_got, dyl_far, qup_side,
         *o_other) = mesh_run(
            functools.partial(back2_body, quarter, scale), args, outs,
            [low(rows, hidden), low(rows, hidden), low(5, wide, hidden), low(2, wide, hidden),
             low(5, wide, hidden), low(2, wide, hidden), full(heads * rows, head_dim),
             low(micro, half, rank),
             full(micro, half, rank), low(micro, key_half, 2 * head_dim),
             low(micro, key_half, 2 * head_dim), low(micro, half, rank),
             low(micro, quarter, rank), low(micro, quarter, rank),
             low(micro, key_half, 2 * head_dim), kv_low(micro, 2 * line), kv_low(micro, 2 * line),
             kv_low(micro, line), kv_low(micro, line), kv_low(micro, 3), kv_low(micro, 3),
             full(micro, quarter, 2 * head_dim), low(micro, rows, rank + 2 * head_dim),
             low(line, side_rows, columns)],
            2, "back2", 62, 44,
        )

        args = later(dfirst) + far(q_down, kv_proj) + later(*h1_mine, *h1_theirs)
        args += late(*os, *o_other, dyl_mine, dyl_got, dyl_far)
        args += later(*qn_mine, dqp, qup_side, n1)
        args += near(inv1) + later(dy) + near(gain1_row, gain2, gain_c, layer_own)
        block = width // 4 // seq
        gain_columns = 2 * wide + side_rows
        outs = late(whole((columns, wide), F32), whole((side_rows, columns), F32))
        outs += near(whole((wide, part), F32), whole((block, 2 * head_dim), F32),
                    whole((micro, rows, width), LOW), whole((1, gain_columns), F32),
                    whole((micro, rows, width), LOW))
        grad_out, grad_qup, grad_qdown, grad_kv, input_grads, gains, layer_out = mesh_run(
            functools.partial(back3_body, quarter), args, outs,
            [low(5, wide, columns), low(2, wide, columns), low(5, side_rows, columns),
             low(2, side_rows, columns), low(5, wide, first_columns),
             low(2, wide, first_columns), low(line, wide, first_columns),
             low(line, wide, first_columns), low(micro, half, width), full(micro, half, width),
             low(micro, half, width), low(micro, quarter, width), low(micro, quarter, width),
             full(wide, kv_part), full(4, block, kv_part), full(seq, 1, gain_columns),
             full(seq, 1, gain_columns), full(seq, 1, gain_columns), full(line, 1, gain_columns),
             full(12, 1, gain_columns), low(width, first_columns), pltpu.SemaphoreType.DMA((2,))],
            3, "back3", 60, 44,
        )
        results = [layer_out, input_grads, grad_qdown, grad_qup, grad_kv, grad_out, grad_gate,
                   grad_up, grad_down]
        made = pl.pallas_call(
            functools.partial(deliver_body, len(results), 4),
            in_specs=[pl.BlockSpec(memory_space=pl.ANY)] * len(results) + [in_vmem()],
            out_specs=[pl.BlockSpec(memory_space=pl.ANY)] * len(results) + [in_vmem()] * 3,
            out_shape=[whole(a.shape, a.dtype) for a in results]
            + [whole((n,), F32) for n in (wide, wide, side_rows)],
            scratch_shapes=[pltpu.VMEM(a.shape, a.dtype) for a in results]
            + [pltpu.SemaphoreType.DMA((8 * len(results),))],
            compiler_params=pltpu.CompilerParams(vmem_limit_bytes=60 << 20),
            name="deliver",
        )(*results, gains)
        (layer_out, input_grads, grad_qdown, grad_qup, grad_kv, grad_out, grad_gate, grad_up,
         grad_down, grad_n1, grad_n2, grad_c) = made
        return (
            layer_out, input_grads, grad_n1, grad_qdown, grad_c, grad_qup, grad_kv, grad_out,
            grad_n2, grad_gate, grad_up, grad_down,
        )

    if narrow:
        return narrow_layer()

    both_rows = sides_shape(width, rows)
    half_rows = sides_shape(width, half)
    rank_sides = sides_shape(rank, rows)

    tables, starts, kv, c_part, h1_sides = [], [], [], [], []
    order = []
    for m in range(micro):
        _, places = documents(lengths[m], row_ids)
        starts.append(row_ids - places)
        tables.append(rotation(places, head_dim))
        c, packed, h1, *made = run(
            without_sides(functools.partial(first_body, m, quarter), len(both_rows)),
            ids,
            [tokens, gain1_row, q_down, kv_proj, *tables[m]],
            [whole((rows, part), LOW), whole((half, 2 * head_dim), LOW), whole((rows, width), LOW),
             *both_rows],
            order,
            name="first",
        )
        order = [c]
        blocks = [packed] + [
            lax.ppermute(packed, "seq", [(i, i + 2 * d) for i in range(seq - 2 * d)])
            for d in range(1, line)
        ]
        near = jnp.stack(blocks, 0)
        near = jnp.stack([near, other(near)], 0)
        kv.append(
            jnp.stack([near, lax.ppermute(near, "mp", CORE)], 0).reshape(key_count, 2 * head_dim)
        )
        c_part.append(c)
        h1_sides.append(split_sides(made, h1, rows))

    dhid, dz, *made = run(
        functools.partial(cotangent_body, micro, quarter),
        ids,
        [cotangent, w_down],
        [whole((micro, rows, hidden), F32), whole((micro, rows, width), LOW),
         *sides_shape(width, half, (micro,))],
        order,
        name="cotangent",
    )
    order = [dz]
    dz_mine, dz_theirs = split_sides(made, dz, half)
    dz_got = from_other(dz_theirs)

    qn_sides, qs, os, lses, sums, c_rows = [], [], [], [], [], []
    for m in range(micro):
        near = lax.ppermute(c_part[m], "mp", CROSS)
        swapped = jnp.concatenate(
            [near[quarter : 2 * quarter], near[:quarter], near[3 * quarter :],
             near[2 * quarter : 3 * quarter]], 0
        )
        far = lax.ppermute(jnp.concatenate([c_part[m], swapped], 1), "mp", CORE)
        qn, q, o, lse, send, keep, *made = run(
            without_sides(functools.partial(attend_body, scale), len(rank_sides)),
            ids,
            [c_part[m], near, far, gain_c_row, q_up, *tables[m], kv[m], key_ids[None, :],
             row_ids[:, None], starts[m][:, None], out_proj],
            [whole((rows, rank), LOW), whole((heads, rows, head_dim), LOW),
             whole((rows, heads * head_dim), LOW), whole((heads, rows), F32),
             whole((half, width), LOW), whole((half, width), F32), *rank_sides],
            order,
            name="attend",
        )
        order = [o]
        qn_sides.append(split_sides(made, qn, rows))
        qs.append(q)
        os.append(o)
        lses.append(lse)
        sums.append(sum_mp(send, keep))
        c_rows.append(
            jnp.concatenate([c_part[m][:quarter], swapped[:quarter], far[half : half + quarter]], 1)
        )

    h2_mine, h2_theirs, hid, dg, du, state = [], [], [], [], [], []
    for m in range(micro):
        x = lax.dynamic_slice_in_dim(tokens[m], me * quarter, quarter, 0).astype(F32)
        inv1 = inverse_rms(x)
        y = x + sums[m]
        inv2 = inverse_rms(y)
        n2 = y * inv2
        pieces = gather_mp((n2 * gain2_row).astype(LOW))
        h2, hid_m, dg_m, du_m, *made = run(
            without_sides(functools.partial(forward_body, m), len(half_rows)),
            ids,
            [*pieces, w_gate, w_up, dhid],
            [whole((rows, width), LOW), *[whole((rows, hidden), LOW)] * 3, *half_rows],
            order,
            name="forward",
        )
        order = [hid_m]
        mine, theirs = split_sides(made, h2, half)
        h2_mine.append(mine)
        h2_theirs.append(theirs)
        hid.append(hid_m)
        dg.append(dg_m)
        du.append(du_m)
        state.append(dict(x=x, n1=x * inv1, inv1=inv1, y=y, n2=n2, inv2=inv2, c=c_rows[m]))

    def stacked(name):
        return jnp.stack([st[name] for st in state], 0)

    def with_other(arrays):
        return [*arrays, *[other(a) for a in arrays]]

    def terms_of(spans):
        return [(a, lead, m + micro * partner, None, first, count)
                for a, lead, m, partner, first, count in spans]

    send, keep, ffn_send, ffn_keep = run(
        functools.partial(hidden_back_body, micro),
        ids,
        [*dg, *du, *hid, w_gate, w_up, w_down],
        [whole((micro, half, width), LOW), whole((micro, half, width), F32)] * 2,
        order,
        name="hidden_back",
    )
    lefts, spans = both_sides(dz_mine, dz_got)
    chain_down = Chain(lefts, with_other(hid), terms_of(spans), (wide, hidden), turned=True)
    lefts, spans = both_sides(h2_mine, [list(p) for p in zip(*[from_other(t) for t in h2_theirs])])
    chain_gate = Chain(lefts, with_other(dg), terms_of(spans), (wide, hidden))
    chain_up = Chain(lefts, with_other(du), terms_of(spans), (wide, hidden))

    order = chain_down.advance([send])
    dh2 = sum_mp(send, keep)
    y, n2, inv2, n1, inv1 = (stacked(k) for k in ("y", "n2", "inv2", "n1", "inv1"))
    dz_own = dz[:, :quarter].astype(F32)
    gain2 = jnp.sum(dh2 * n2, axis=(0, 1))
    dy = dz_own + norm_backward(dh2 * gain2_row, n2, inv2)
    for _ in range(2):
        order = chain_down.advance(order)
    order = chain_gate.advance(order)

    def attend_back(which, pieces):
        args = [*pieces, out_proj, q_up, key_ids[:, None]]
        for m in which:
            args += [qs[m], kv[m], os[m], lses[m], jnp.stack([row_ids, starts[m]], 0), *tables[m]]
        n = len(which)
        return run(
            functools.partial(attend_back_body, scale, n, min(1024, key_count // 2)),
            ids,
            args,
            [whole((n, rows, width), LOW), whole((n, rows, heads * head_dim), LOW),
             whole((n, half, rank), LOW), whole((n, half, rank), F32),
             whole((n, key_count // 2, 2 * head_dim), LOW),
             whole((n, key_count // 2, 2 * head_dim), F32), *sides_shape(width, half, (n,))],
            order,
            scratch=[pltpu.VMEM((heads, rows, head_dim), F32),
                     pltpu.VMEM((heads, rows, head_dim), LOW),
                     pltpu.VMEM((heads, 8, rows), F32)],
            name="attend_back",
            limit=56,
        )

    pieces = gather_mp(dy.astype(LOW))
    if key_count <= 2048:
        made = attend_back(range(micro), pieces)
    else:
        each = [attend_back([m], [p[m : m + 1] for p in pieces]) for m in range(micro)]
        made = [jnp.concatenate(parts, 0) for parts in zip(*each)]
    dyl, dqp, send, keep, kv_send, kv_keep, *made = made
    order = [send]
    dyl_mine, dyl_theirs = split_sides(made, dyl, half)
    lefts, spans = both_sides(dyl_mine, from_other(dyl_theirs))
    chain_out = Chain(lefts, with_other(os), terms_of(spans), (wide, heads * head_dim), turned=True)

    def side_sum(lefts, rights, shape, after):
        terms = [(m, None, 0, m, 0, rows) for m in range(micro)]
        (made,) = run(
            functools.partial(side_sum_body, terms, len(lefts)),
            ids,
            [*lefts, *rights],
            [whole((line, *shape), LOW)],
            after,
            name="side_sum",
        )
        return other(made), [made]

    def own_chain(side_pairs, right, shape, after):
        from_side, after = side_sum([p[1] for p in side_pairs], [right], shape, after)
        terms = [(m, None, 0, m, 0, rows) for m in range(micro)]
        return Chain([p[0] for p in side_pairs], [right], terms, shape, from_side=from_side), after

    shape = (rank // seq, heads * head_dim)
    chain_qup, order = own_chain(qn_sides, dqp, shape, order)
    order = chain_gate.advance(order)
    order = chain_up.advance(order)

    dqn = sum_mp(send, keep)
    c = stacked("c").astype(F32)
    inv_c = inverse_rms(c)
    chat = c * inv_c
    chat = to_natural(chat, 2)
    gain_c = jnp.sum(dqn * chat, axis=(0, 1))
    dc = norm_backward(dqn * gain_c_row, chat, inv_c).astype(LOW)

    dkv = kv_keep + lax.ppermute(kv_send, "mp", CORE).astype(F32)
    dkv = dkv.reshape(micro, 2, line, 2, quarter, 2 * head_dim)
    dkv = dkv[:, :, :, 0] + lax.ppermute(dkv[:, :, :, 1].astype(LOW), "mp", CROSS).astype(F32)
    dkv = dkv[:, 0] + other(dkv[:, 1].astype(LOW)).astype(F32)
    total = dkv[:, 0]
    for d in range(1, line):
        total = total + lax.ppermute(
            dkv[:, d].astype(LOW), "seq", [(i + 2 * d, i) for i in range(seq - 2 * d)]
        ).astype(F32)
    cosine = jnp.stack([t[0][:quarter] for t in tables], 0)
    sine = jnp.stack([t[1][:quarter] for t in tables], 0)
    dkv_low = jnp.concatenate(
        [unrotate(total[..., :head_dim], cosine, sine), total[..., head_dim:]], axis=-1
    ).astype(LOW)
    both = jnp.concatenate(gather_mp(jnp.concatenate([dc, dkv_low], -1)), -2)
    dfirst = jnp.concatenate(
        [lax.dynamic_slice_in_dim(both, me * part, part, 2),
         lax.dynamic_slice_in_dim(both, rank + me * kv_part, kv_part, 2)], -1
    )

    grad_down, order = chain_down.finish(order)
    order = chain_gate.advance(order)
    order = chain_up.advance(order)
    order = chain_out.advance(order)
    grad_gate, order = chain_gate.finish(order)
    order = chain_up.advance(order)
    order = chain_out.advance(order)
    grad_up, order = chain_up.finish(order)
    order = chain_qup.advance(order)
    order = chain_out.advance(order)
    chain_first, order = own_chain(h1_sides, dfirst, (wide, part + kv_part), order)
    order = chain_qup.advance(order)
    grad_out, order = chain_out.finish(order)
    order = chain_first.advance(order)
    order = chain_qup.advance(order)
    order = chain_first.advance(order)
    grad_qup, order = chain_qup.finish(order)
    order = chain_first.advance(order)
    grad_first, order = chain_first.finish(order)

    grad_qdown = grad_first[:, :part]
    kv_cols_grad = grad_first[:, part:]
    pieces = []
    for k in ORDER:
        size = kv_cols_grad.shape[0] // 4
        sent = lax.dynamic_slice_in_dim(kv_cols_grad, (me ^ k) * size, size, 0)
        pieces.append(lax.ppermute(sent, "mp", [(i, i ^ k) for i in range(4)]) if k else sent)
    grad_kv = to_natural(jnp.concatenate(pieces, 1), 1)

    def put_natural(pieces):
        return run(
            functools.partial(natural_body, micro, quarter),
            ids,
            pieces,
            [whole((micro, rows, width), LOW)],
            name="natural",
        )[0]

    part_sum = inner_cols(dfirst.reshape(micro * rows, -1), first_weights).reshape(micro, rows, width)
    dh1 = sum_mp(part_sum[:, half:].astype(LOW), part_sum[:, :half])
    gain1 = jnp.sum(dh1 * n1, axis=(0, 1))
    dx = (dy + norm_backward(dh1 * gain1_row, n1, inv1)).astype(LOW)
    input_grads = put_natural(gather_mp(dx))

    ffn = sum_mp(ffn_send, ffn_keep)
    layer_out = put_natural(gather_mp((y + ffn).astype(LOW)))

    gains = jnp.concatenate(
        [gain1.reshape(seq, -1), gain2.reshape(seq, -1), gain_c.reshape(seq, -1)], axis=1
    )
    gains = gains + lax.ppermute(gains, "mp", CORE)
    gains = gains + lax.ppermute(gains, "mp", CROSS)
    gain_sum = lax.dynamic_index_in_dim(gains, at, 0, keepdims=False)
    for k in range(1, seq):
        gain_sum = gain_sum + lax.ppermute(
            lax.dynamic_index_in_dim(gains, at ^ k, 0, keepdims=False),
            "seq",
            [(i, i ^ k) for i in range(seq)],
        )
    return (
        layer_out,
        input_grads,
        gain_sum[:wide],
        grad_qdown,
        gain_sum[2 * wide :],
        grad_qup,
        grad_kv,
        grad_out,
        gain_sum[wide : 2 * wide],
        grad_gate,
        grad_up,
        grad_down,
    )


def solution(mesh):
    placed = (
        P(None, "seq", None),
        P(),
        P(),
        P(None, "mp"),
        P(),
        P(None, "mp"),
        P(),
        P("mp", None),
        P(),
        P(None, "mp"),
        P(None, "mp"),
        P("mp", None),
        P(None, "seq", None),
    )
    return jax.shard_map(
        local,
        mesh=mesh,
        in_specs=placed,
        out_specs=(
            P(None, "seq", None),
            P(None, "seq", None),
            P("seq"),
            P("seq", "mp"),
            P("seq"),
            P("seq", "mp"),
            P(("seq", "mp"), None),
            P("mp", "seq"),
            P("seq"),
            P("seq", "mp"),
            P("seq", "mp"),
            P("mp", "seq"),
        ),
        check_vma=False,
    )
```

```python
import functools

import jax
import jax.numpy as jnp
from jax import lax
from jax.experimental import pallas as pl
from jax.experimental.pallas import tpu as pltpu
from jax.sharding import PartitionSpec as P

EPS = 1e-06
BASE = 10000.0
NEG_LARGE = -1e30
LOW = jnp.bfloat16
F32 = jnp.float32
ORDER = (0, 2, 1, 3)
CORE = [(i, i ^ 1) for i in range(4)]
CROSS = [(i, i ^ 2) for i in range(4)]


def inverse_rms(values):
    return lax.rsqrt(jnp.mean(values * values, axis=-1, keepdims=True) + EPS)


def norm_backward(grad_hat, normed, inverse):
    return inverse * (grad_hat - normed * jnp.mean(grad_hat * normed, axis=-1, keepdims=True))


def dot(left, right):
    return jnp.dot(left, right, preferred_element_type=F32)


def inner_rows(left, right):
    return lax.dot_general(left, right, (((0,), (0,)), ((), ())), preferred_element_type=F32)


def inner_cols(left, right):
    return lax.dot_general(left, right, (((1,), (1,)), ((), ())), preferred_element_type=F32)


def documents(lengths_row, rows):
    first_end = lengths_row[0]
    second_end = first_end + lengths_row[1]
    doc_ids = (rows >= first_end).astype(jnp.int32) + (rows >= second_end).astype(jnp.int32)
    starts = jnp.where(rows >= second_end, second_end, jnp.where(rows >= first_end, first_end, 0))
    return (doc_ids, rows - starts)


def rotation(positions, head_dim):
    half = head_dim // 2
    freqs = BASE ** (-2.0 * jnp.arange(half, dtype=F32) / head_dim)
    angles = positions.astype(F32)[:, None] * freqs[None, :]
    return (jnp.cos(angles), jnp.sin(angles))


def rotate(values, cosine, sine):
    half = values.shape[-1] // 2
    first = values[..., :half]
    second = values[..., half:]
    return jnp.concatenate(
        [first * cosine - second * sine, second * cosine + first * sine], axis=-1
    )


def unrotate(grads, cosine, sine):
    return rotate(grads, cosine, -sine)


def in_vmem():
    return pl.BlockSpec(memory_space=pltpu.VMEM)


def whole(shape, dtype):
    return jax.ShapeDtypeStruct(shape, dtype)


def run(body, ids, args, outs, after=(), scratch=(), name=None, limit=40):
    args, after = list(args), list(after)

    def without(*refs):
        body(*refs[: 1 + len(args)], *refs[1 + len(args) + len(after) :])

    return pl.pallas_call(
        without,
        grid_spec=pltpu.PrefetchScalarGridSpec(
            num_scalar_prefetch=1,
            grid=(1,),
            in_specs=[in_vmem()] * len(args) + [pl.BlockSpec(memory_space=pl.ANY)] * len(after),
            out_specs=[in_vmem()] * len(outs),
            scratch_shapes=list(scratch),
        ),
        out_shape=list(outs),
        cost_estimate=pl.CostEstimate(flops=1000, bytes_accessed=1000, transcendentals=0),
        compiler_params=pltpu.CompilerParams(vmem_limit_bytes=limit << 20),
        name=name,
    )(ids, *args, *after)


def side_columns(source, mine, theirs, side):
    line, _, wide = mine.shape
    rows = theirs.shape[1]
    for z in range(line):
        mine[z] = source[:, pl.ds(pl.multiple_of((2 * z + side) * wide, wide), wide)]
        theirs[z] = source[:rows, pl.ds(pl.multiple_of((2 * z + 1 - side) * wide, wide), wide)]


def first_body(m, quarter, ids, x_ref, gain, q_down, kv_proj, cos, sin, c, kv, h1, mine, theirs):
    blocks = [
        x_ref[m, pl.ds(pl.multiple_of((ids[0] ^ k) * quarter, quarter), quarter), :] for k in ORDER
    ]
    x = jnp.concatenate(blocks, 0).astype(F32)
    low = (x * inverse_rms(x) * gain[...]).astype(LOW)
    h1[...] = low
    half = 2 * quarter
    pair = dot(low[:half], kv_proj[...])
    wide = kv_proj.shape[1] // 2
    kv[:, :wide] = rotate(pair[:, :wide], cos[:half], sin[:half]).astype(LOW)
    kv[:, wide:] = pair[:, wide:].astype(LOW)
    c[...] = dot(low, q_down[...]).astype(LOW)
    if mine is not None:
        side_columns(h1, mine, theirs, ids[1])


def cotangent_body(micro, quarter, ids, z_ref, w_down, dhid, dz, *sides):
    for m in range(micro):
        blocks = [
            z_ref[m, pl.ds(pl.multiple_of((ids[0] ^ k) * quarter, quarter), quarter), :]
            for k in ORDER
        ]
        dz[m] = jnp.concatenate(blocks, 0)
        if sides:
            side_columns(dz.at[m], sides[0].at[m], sides[1].at[m], ids[1])
        dhid[m] = inner_cols(dz[m], w_down[...])


def attend_body(
    scale, ids, c0, c1, c2, gain, q_up, cos, sin, kv, key_ids, row_ids, row_starts, out_proj,
    qn, q, o, lse, send, keep, mine, theirs,
):
    rows = qn.shape[0]
    quarter = rows // 4
    part = c0.shape[1]
    wide = q.shape[2]
    got = c1[...]
    pair = jnp.concatenate(
        [got[quarter : 2 * quarter], got[:quarter], got[3 * quarter :], got[2 * quarter : 3 * quarter]],
        0,
    )
    far = jnp.concatenate([c2[2 * quarter :], c2[: 2 * quarter]], 0)
    c = jnp.concatenate([c0[...], pair, far], 1).astype(F32)
    chat = c * inverse_rms(c)
    for k, xor in enumerate(ORDER):
        columns = pl.ds(pl.multiple_of((ids[0] ^ xor) * part, part), part)
        qn[:, columns] = (chat[:, k * part : (k + 1) * part] * gain[:, columns]).astype(LOW)
    if mine is not None:
        side_columns(qn, mine, theirs, ids[1])
    bias = jnp.where(
        (key_ids[...] >= row_starts[...]) & (key_ids[...] <= row_ids[...]), 0.0, NEG_LARGE
    )
    low = qn[...]
    keys, values = kv[:, :wide], kv[:, wide:]
    for h in range(q.shape[0]):
        pre = dot(low, q_up[:, h * wide : (h + 1) * wide])
        q_h = (rotate(pre, cos[...], sin[...]) * scale).astype(LOW)
        q[h] = q_h
        scores = inner_cols(q_h, keys) + bias
        top = jnp.max(scores, axis=-1, keepdims=True)
        probs = jnp.exp(scores - top)
        total = jnp.sum(probs, axis=-1, keepdims=True)
        out = dot(probs.astype(LOW), values) / total
        o[:, h * wide : (h + 1) * wide] = out.astype(LOW)
        log_total = jnp.broadcast_to(top + jnp.log(total), (rows, 128))
        lse[h : h + 1, :] = jnp.transpose(log_total)[:1]
    half = 2 * quarter
    send[...] = dot(o[half:, :], out_proj[...]).astype(LOW)
    keep[...] = dot(o[:half, :], out_proj[...])


def forward_body(m, ids, a0, a1, a2, w_gate, w_up, dhid, h2, hid, dg, du, mine, theirs):
    h2[...] = jnp.concatenate([a0[...], a1[...], a2[...]], 0)
    if mine is not None:
        side_columns(h2, mine, theirs, ids[1])
    low = h2[...]
    g = dot(low, w_gate[...])
    u = dot(low, w_up[...])
    sig = jax.nn.sigmoid(g)
    swish = g * sig
    hid[...] = (swish * u).astype(LOW)
    back = dhid[m]
    dg[...] = (back * u * sig * (1.0 + g * (1.0 - sig))).astype(LOW)
    du[...] = (back * swish).astype(LOW)


def hidden_back_body(micro, ids, *refs):
    dgs, dus = refs[:micro], refs[micro : 2 * micro]
    hids = refs[2 * micro : 3 * micro]
    w_gate, w_up, w_down, send, keep, out_send, out_keep = refs[3 * micro :]
    half = send.shape[1]
    every = lambda parts: jnp.concatenate([part[...] for part in parts], 0)
    rows = 2 * half
    total = inner_cols(every(dgs), w_gate[...]) + inner_cols(every(dus), w_up[...])
    for m in range(micro):
        send[m] = total[m * rows + half : (m + 1) * rows].astype(LOW)
        keep[m] = total[m * rows : m * rows + half]
    total = dot(every(hids), w_down[...])
    for m in range(micro):
        out_send[m] = total[m * rows + half : (m + 1) * rows].astype(LOW)
        out_keep[m] = total[m * rows : m * rows + half]


def pick(ref, lead):
    return ref if lead is None else ref.at[lead]


def block_body(terms, lefts, rights, extra, from_side, turned, ids, *refs):
    left, refs = refs[:lefts], refs[lefts:]
    right, refs = refs[:rights], refs[rights:]
    added, out = refs[: extra + from_side], refs[-1]
    total = None
    for a, a_lead, b, b_lead, first, count in terms:
        rows = pick(right[b], b_lead)[first : first + count, :]
        term = inner_rows(pick(left[a], a_lead)[ids[0]], rows)
        total = term if total is None else total + term
    for i, ref in enumerate(added):
        total = total + (ref[ids[0]] if i >= extra else ref[...]).astype(F32)
    out[...] = jnp.transpose(total) if turned else total.astype(out.dtype)


def side_sum_body(terms, lefts, ids, *refs):
    left, right, out = refs[:lefts], refs[lefts:-1], refs[-1]
    for z in range(out.shape[0]):
        total = None
        for a, a_lead, b, b_lead, first, count in terms:
            rows = pick(right[b], b_lead)[first : first + count, :]
            term = inner_rows(pick(left[a], a_lead)[z], rows)
            total = term if total is None else total + term
        out[z] = total.astype(out.dtype)


def attend_back_body(
    scale, micro, chunk, ids, a0, a1, a2, out_proj, q_up, key_ids, *refs
):
    per = 7
    groups = [refs[m * per : (m + 1) * per] for m in range(micro)]
    dyl_out, dqp, send, keep, kv_send, kv_keep = refs[micro * per : micro * per + 6]
    dq_acc, do_acc, delta_acc = refs[-3:]
    sides = refs[micro * per + 6 : -3]
    for m in range(micro):
        q, kv, o, lse, row_ids, cos, sin = groups[m]
        heads, rows, wide = q.shape
        half_rows = rows // 2
        dyl = jnp.concatenate([a0[m], a1[m], a2[m]], 0)
        dyl_out[m] = dyl
        if sides:
            side_columns(dyl_out.at[m], sides[0].at[m], sides[1].at[m], ids[1])
        for h in range(heads):
            do = inner_cols(dyl, out_proj[h * wide : (h + 1) * wide, :]).astype(LOW)
            do_acc[h] = do
            delta = jnp.sum(
                do.astype(F32) * o[:, h * wide : (h + 1) * wide].astype(F32), axis=-1, keepdims=True
            )
            delta_acc[h] = jnp.transpose(jnp.broadcast_to(delta, (rows, 128)))[:8]
            dq_acc[h] = jnp.zeros((rows, wide), F32)
        count = kv.shape[0] // 2 // chunk
        for part, out in ((0, kv_keep), (1, kv_send)):

            def one(i, carry):
                base = pl.multiple_of((part * count + i) * chunk, chunk)
                keys = kv[pl.ds(base, chunk), :wide]
                values = kv[pl.ds(base, chunk), wide:]
                at = key_ids[pl.ds(base, chunk), :]
                bias = jnp.where((at >= row_ids[1:2, :]) & (at <= row_ids[0:1, :]), 0.0, NEG_LARGE)

                def head(h, sums):
                    dk, dv = sums
                    q_h, do_h = q[h], do_acc[h]
                    probs = jnp.exp(inner_cols(keys, q_h) + bias - lse[pl.ds(h, 1), :])
                    back = inner_cols(values, do_h) - delta_acc[h][:1]
                    ds = (probs * back).astype(LOW)
                    dv = dv + dot(probs.astype(LOW), do_h)
                    dk = dk + dot(ds, q_h)
                    dq_acc[h] = dq_acc[h] + inner_rows(ds, keys)
                    return dk, dv

                zero = jnp.zeros((chunk, wide), F32)
                dk, dv = lax.fori_loop(0, heads, head, (zero, zero))
                place = pl.ds(pl.multiple_of(i * chunk, chunk), chunk)
                out[m, place, :wide] = dk.astype(out.dtype)
                out[m, place, wide:] = dv.astype(out.dtype)
                return carry

            if count == 1:
                one(0, 0)
            else:
                lax.fori_loop(0, count, one, 0)
        for h in range(heads):
            dq = unrotate(dq_acc[h] * scale, cos[...], sin[...])
            dqp[m, :, h * wide : (h + 1) * wide] = dq.astype(LOW)
        low = dqp[m]
        send[m] = inner_cols(low[half_rows:], q_up[...]).astype(LOW)
        keep[m] = inner_cols(low[:half_rows], q_up[...])


def natural_body(micro, quarter, ids, a0, a1, a2, out):
    for m in range(micro):
        pieces = (a0[m], a1[m], a2[m, :quarter, :], a2[m, quarter:, :])
        for k, piece in zip(ORDER, pieces):
            out[m, pl.ds(pl.multiple_of((ids[0] ^ k) * quarter, quarter), quarter), :] = piece


class Wire:
    def __init__(self, sends, recvs):
        self.sends, self.recvs, self.used = sends, recvs, 0
        self.seq, self.mp = lax.axis_index("seq"), lax.axis_index("mp")
        self.place, self.side = self.seq // 2, self.seq % 2
        core, cross = self.mp % 2, self.mp // 2
        self.blocks = (
            self.mp, 2 * (1 - cross) + core, 2 * cross + 1 - core, 2 * (1 - cross) + 1 - core
        )
        self.core, self.cross = {"mp": self.blocks[2]}, {"mp": self.blocks[1]}
        self.beside = {"seq": self.seq + 1 - 2 * self.side}
        self.up, self.down = {"seq": self.seq + 2}, {"seq": self.seq - 2}

    def copy(self, source, target, device):
        at = self.used
        self.used += 1
        return pltpu.make_async_remote_copy(
            src_ref=source, dst_ref=target, send_sem=self.sends.at[at], recv_sem=self.recvs.at[at],
            device_id=device, device_id_type=pl.DeviceIdType.MESH,
        )

    def send(self, source, target, device):
        made = self.copy(source, target, device)
        made.start()
        return made

    def greet(self, line, far=1, diagonal=False):
        barrier = pltpu.get_barrier_semaphore()
        devices = [self.core, self.cross, self.beside]
        if diagonal:
            devices.append({"mp": self.blocks[3]})
        for device in devices:
            pl.semaphore_signal(barrier, 1, device_id=device, device_id_type=pl.DeviceIdType.MESH)
        for d in range(1, far + 1):
            for way, there in ((1, self.place < line - d), (-1, self.place >= d)):

                @pl.when(there)
                def _():
                    pl.semaphore_signal(
                        barrier, 1, device_id={"seq": self.seq + 2 * way * d},
                        device_id_type=pl.DeviceIdType.MESH,
                    )
        below, above = jnp.minimum(self.place, far), jnp.minimum(line - 1 - self.place, far)
        pl.semaphore_wait(barrier, len(devices) + below + above)


def along(pieces, axis):
    return pieces[0] if len(pieces) == 1 else jnp.concatenate(pieces, axis)


def pair_places(first, second, quarter, axis):
    shape = (2 * quarter, 1) if axis == 0 else (1, 2 * quarter)
    index = lax.broadcasted_iota(jnp.int32, shape, axis)
    return jnp.where(index < quarter, first * quarter + index, (second - 1) * quarter + index)


def row_places(wire, quarter, axis):
    b = wire.blocks
    pieces = [pair_places(b[i], b[i + 1], quarter, axis) for i in (0, 2)]
    return wire.seq * (4 * quarter) + along(pieces, axis)


def key_places(wire, quarter, line, axis, cores):
    pieces = []
    for core in cores:
        for side in (wire.side, 1 - wire.side):
            for d in range(line):
                base = ((wire.place - d) * 2 + side) * (4 * quarter)
                b = wire.blocks[2 * core : 2 * core + 2]
                pieces.append(base + pair_places(b[0], b[1], quarter, axis))
    return along(pieces, axis)


def sequence_starts(lengths, m, places):
    first_end = lengths[m, 0]
    second_end = first_end + lengths[m, 1]
    return jnp.where(
        places >= second_end, second_end, jnp.where(places >= first_end, first_end, 0)
    )


class LineSum:
    def __init__(self, wire, term, room, rows, columns, keep):
        got, out = room
        view = lambda ref, i: ref.at[i, :rows, :columns]
        self.place, self.term, self.keep = wire.place, term, keep
        self.got = [view(got, i) for i in range(5)]
        self.out = [view(out, i) for i in range(2)]
        one, two_up, two_down, three_up, three_down = self.got
        a, b = self.out
        self.one = wire.copy(a, one, wire.up), wire.copy(a, one, wire.down)
        self.two = wire.copy(b, two_up, wire.up), wire.copy(b, two_down, wire.down)
        self.three = wire.copy(a, three_up, wire.up), wire.copy(b, three_down, wire.down)

    def clear(self):
        place = self.place
        for ref, empty in zip(
            self.got, ((place == 0) | (place == 3),) * 3 + (place == 0, place == 3)
        ):

            @pl.when(empty)
            def _(ref=ref):
                ref[...] = jnp.zeros(ref.shape, ref.dtype)

    def step1(self):
        place = self.place

        @pl.when((place == 0) | (place == 3))
        def _():
            self.out[0][...] = self.term(3 - place).astype(LOW)

        pl.when(place == 0)(self.one[0].start)
        pl.when(place == 3)(self.one[1].start)

    def step2(self):
        place = self.place
        pl.when(place == 1)(self.one[0].wait_recv)
        pl.when(place == 2)(self.one[1].wait_recv)
        self.out[1][...] = (
            self.term((place + 2) % 4) + self.got[0][...].astype(F32)
        ).astype(LOW)
        pl.when(place <= 1)(self.two[0].start)
        pl.when(place >= 2)(self.two[1].start)

    def step3(self):
        place = self.place

        @pl.when((place == 1) | (place == 2))
        def _():
            self.two[0].wait_recv()
            self.two[1].wait_recv()

        pl.when(place == 0)(self.one[0].wait_send)
        pl.when(place == 3)(self.one[1].wait_send)

        @pl.when(place <= 2)
        def _():
            self.out[0][...] = (self.term(place + 1) + self.got[1][...].astype(F32)).astype(LOW)
            self.three[0].start()

        pl.when(place <= 1)(self.two[0].wait_send)
        pl.when(place >= 2)(self.two[1].wait_send)

        @pl.when(place >= 1)
        def _():
            self.out[1][...] = (self.term(place - 1) + self.got[2][...].astype(F32)).astype(LOW)
            self.three[1].start()

    def finish(self):
        place = self.place
        pl.when(place >= 1)(self.three[0].wait_recv)
        pl.when(place <= 2)(self.three[1].wait_recv)
        self.keep(
            self.term(place) + self.got[3][...].astype(F32) + self.got[4][...].astype(F32)
        )

    def settle(self):
        place = self.place
        pl.when(place <= 2)(self.three[0].wait_send)
        pl.when(place >= 1)(self.three[1].wait_send)


class Desk:
    def __init__(self, first, loads, stores):
        self.loads, self.stores, self.stored = loads, stores, []
        for _, made in first:
            made.start()
        self.waiting = list(first)

    def more(self):
        for _, made in self.loads:
            made.start()
        self.waiting += self.loads

    def arrive(self, *refs):
        rest = []
        for ref, made in self.waiting:
            if not refs or any(ref is other for other in refs):
                made.wait()
            else:
                rest.append((ref, made))
        self.waiting = rest

    def flush(self, *refs):
        rest = []
        for ref, made in self.stores:
            if not refs or any(ref is other for other in refs):
                made.start()
                self.stored.append(made)
            else:
                rest.append((ref, made))
        self.stores = rest

    def close(self):
        self.flush()
        for made in self.stored:
            made.wait()


SPACES = (pl.ANY, pltpu.VMEM, pltpu.SMEM, pl.ANY, pl.ANY)


def mesh_run(body, args, outs, scratch, number, name, limit, sends):
    late_in = [i for i, (kind, _) in enumerate(args) if kind >= 3]
    late_out = [i for i, (kind, _) in enumerate(outs) if kind == 3]

    def whole_body(*refs):
        refs = list(refs)
        take = lambda n: [refs.pop(0) for _ in range(n)]
        given, results, rooms_in, rooms_out = (
            take(len(args)), take(len(outs)), take(len(late_in)), take(len(late_out))
        )
        load_sems, store_sems = take(2)
        first, loads, stores = [], [], []
        for n, (i, room) in enumerate(zip(late_in, rooms_in)):
            made = pltpu.make_async_copy(given[i], room, load_sems.at[n])
            (first if args[i][0] == 3 else loads).append((room, made))
            given[i] = room
        for n, (i, room) in enumerate(zip(late_out, rooms_out)):
            stores.append((room, pltpu.make_async_copy(room, results[i], store_sems.at[n])))
            results[i] = room
        desk = Desk(first, loads, stores)
        body(desk, *given, *results, *refs)
        desk.close()

    room = lambda a: pltpu.VMEM(a.shape, a.dtype)
    return pl.pallas_call(
        whole_body,
        in_specs=[pl.BlockSpec(memory_space=SPACES[kind]) for kind, _ in args],
        out_specs=[pl.BlockSpec(memory_space=SPACES[kind]) for kind, _ in outs],
        out_shape=[shape for _, shape in outs],
        scratch_shapes=[
            *[room(args[i][1]) for i in late_in], *[room(outs[i][1]) for i in late_out],
            pltpu.SemaphoreType.DMA((max(1, len(late_in)),)),
            pltpu.SemaphoreType.DMA((max(1, len(late_out)),)),
            *scratch, pltpu.SemaphoreType.DMA((sends,)), pltpu.SemaphoreType.DMA((sends,)),
        ],
        cost_estimate=pl.CostEstimate(flops=1000, bytes_accessed=1000, transcendentals=0),
        compiler_params=pltpu.CompilerParams(
            collective_id=number, has_side_effects=True, vmem_limit_bytes=limit << 20
        ),
        name=name,
    )(*[array for _, array in args])


def attend_back_one(
    scale, keys_at, rows_at, starts, dyl, out_proj, q_up, q, kv, o, lse, cos, sin,
    dqp, send, keep, kv_send, kv_keep, dq_acc, between=None,
):
    heads, rows, wide = q.shape
    half_rows = rows // 2
    low = dyl[...]
    grads, deltas = [], []
    for h in range(heads):
        columns = slice(h * wide, (h + 1) * wide)
        do = inner_cols(low, out_proj[columns, :]).astype(LOW)
        grads.append(do)
        delta = jnp.sum(do.astype(F32) * o[:, columns].astype(F32), axis=-1, keepdims=True)
        deltas.append(jnp.transpose(jnp.broadcast_to(delta, (rows, 128)))[:1])
    do_all, delta_all = jnp.concatenate(grads, 0), jnp.concatenate(deltas, 1)
    q_all = q[...].reshape(heads * rows, wide)
    lse_all = jnp.concatenate([lse[h : h + 1, :] for h in range(heads)], 1)
    dq_acc[...] = jnp.zeros(dq_acc.shape, F32)
    count = kv.shape[0] // 2
    chunk = min(256, count)
    for part, out in ((1, kv_send), (0, kv_keep)):
        for first in range(0, count, chunk):
            span = slice(part * count + first, part * count + first + chunk)
            keys, values = kv[span, :wide], kv[span, wide:]
            at = keys_at[part][first : first + chunk]
            bias = jnp.where((at >= starts) & (at <= rows_at), 0.0, NEG_LARGE)
            scores = inner_cols(keys, q_all) + jnp.concatenate([bias] * heads, 1)
            probs = jnp.exp(scores - lse_all)
            ds = (probs * (inner_cols(values, do_all) - delta_all)).astype(LOW)
            spot = slice(first, first + chunk)
            out[spot, :wide] = dot(ds, q_all).astype(out.dtype)
            out[spot, wide:] = dot(probs.astype(LOW), do_all).astype(out.dtype)
            dq_acc[...] += inner_rows(ds, keys)
        if part and between is not None:
            between()
    for h in range(heads):
        dq = unrotate(dq_acc[h * rows : (h + 1) * rows, :] * scale, cos, sin)
        dqp[:, h * wide : (h + 1) * wide] = dq.astype(LOW)
    total = inner_cols(dqp[...], q_up[...])
    send[...] = total[half_rows:].astype(LOW)
    keep[...] = total[:half_rows]


def mean_of(values):
    return jnp.mean(values, axis=-1, keepdims=True)


def terms_sum(pairs):
    total = None
    for left, right in pairs:
        term = inner_rows(left, right)
        total = term if total is None else total + term
    return total


def back1_body(quarter, desk, *refs):
    refs = list(refs)
    take = lambda n: [refs.pop(0) for _ in range(n)]
    w_gate, w_up, w_down, cotangent, h2, dhid, n2, inv2, gain2, dz_got, dz_far, y = take(12)
    grad, dy, gain_sum, dyl, dyl_mine, dyl_theirs, layer_own = take(7)
    hid, dg, du, h2_mine = (take(2) for _ in range(4))
    h2_got, h2_far, dg_other = take(2), take(2), take(2)
    gate_w, up_w, hid_other0, hid_other1, h2_theirs, got, out = take(7)
    send, kept, core_got, cross_out, cross_got, loads = take(6)
    ffn_send, ffn_kept, ffn_got, ffn_out, ffn_back = take(5)
    early_got, early_out, early_sum, early_send, early_back, dz, row_loads = take(7)
    wire = Wire(*take(2))
    half, rows = 2 * quarter, 4 * quarter
    ahead = early_send.shape[1]
    block = early_send.shape[0]
    middle = ahead + (gate_w.shape[1] - ahead) // 2
    columns_of = [slice(0, ahead), slice(ahead, middle), slice(middle, gate_w.shape[1])]
    in_weights = []
    for i, columns in enumerate(columns_of):
        for j, (source, target) in enumerate(((w_gate, gate_w), (w_up, up_w))):
            in_weights.append(pltpu.make_async_copy(
                source.at[:, columns], target.at[:, columns], loads.at[2 * i + j]
            ))
    for made in in_weights[:2]:
        made.start()
    hid_other = (hid_other0, hid_other1)
    hid_all = (*(a.at[:, ahead:] for a in hid), *hid_other)

    def term(z):
        columns = pl.ds(pl.multiple_of((2 * z + wire.side) * block, block), block)
        return terms_sum(halves_terms(
            [dz[m, :, columns] for m in range(2)], [dz_got[m, z] for m in range(2)],
            [dz_far[m, z] for m in range(2)], hid_all, half))

    def early_term(z):
        columns = pl.ds(pl.multiple_of(z * 2 * block, 2 * block), 2 * block)
        return terms_sum([(dz[m, :, columns], hid[m][:, :ahead]) for m in range(2)])

    def keep(total):
        grad[ahead:, :] = jnp.transpose(total)

    def early_keep(total):
        early_sum[0], early_sum[1] = total[:block], total[block:]

    chain = LineSum(wire, term, (got, out), block, grad.shape[0] - ahead, keep)
    early = LineSum(wire, early_term, (early_got, early_out), 2 * block, ahead, early_keep)
    chain.clear()
    early.clear()
    wire.greet(4)
    desk.arrive(h2)
    for made in in_weights[2:]:
        made.start()
    desk.more()
    in_dz = []
    for m in range(2):
        for k in range(4):
            at = pl.ds(pl.multiple_of(wire.blocks[k] * quarter, quarter), quarter)
            in_dz.append(pltpu.make_async_copy(
                cotangent.at[m, at, :], dz.at[m, k * quarter : (k + 1) * quarter, :],
                row_loads.at[4 * m + k],
            ))
            in_dz[-1].start()
    for m in range(2):
        side_columns(h2.at[m], h2_mine[m], h2_theirs.at[m], wire.side)
    y_h2 = [wire.send(h2_theirs.at[m], h2_got[m], wire.beside) for m in range(2)]
    y_hid = []

    def columns_forward(m, i):
        columns = columns_of[i]
        if m == 0:
            for made in in_weights[2 * i : 2 * i + 2]:
                made.wait()
        g = dot(h2[m], gate_w[:, columns])
        u = dot(h2[m], up_w[:, columns])
        sig = jax.nn.sigmoid(g)
        swish = g * sig
        hid[m][:, columns] = (swish * u).astype(LOW)
        if i:
            there = hid_other[m].at[:, columns.start - ahead : columns.stop - ahead]
            y_hid.append(wire.send(hid[m].at[:, columns], there, wire.beside))
        if m == 0 and i == 0:
            desk.arrive()
        back = dhid[m, :, columns]
        dg[m][:, columns] = (back * u * sig * (1.0 + g * (1.0 - sig))).astype(LOW)
        du[m][:, columns] = (back * swish).astype(LOW)

    for m in range(2):
        columns_forward(m, 0)
    for made in in_dz:
        made.wait()
    early.step1()
    for m in range(2):
        columns_forward(m, 1)
        if m == 1:
            early.step2()
        columns_forward(m, 2)
        desk.flush(dg[m], du[m], hid[m], h2_mine[m])
    both = lambda pair: jnp.concatenate([pair[0][...], pair[1][...]], 0)
    total = inner_cols(both(dg), gate_w[...]) + inner_cols(both(du), up_w[...])
    for m in range(2):
        send[m] = total[m * rows + half : (m + 1) * rows].astype(LOW)
        kept[m] = total[m * rows : m * rows + half]
    sums = RowSum(wire, send, kept, core_got, cross_out, cross_got, quarter)
    sums.core.start()
    wide = gate_w.shape[1]
    rest = w_down.shape[1] - wide
    downs = [gate_w.at[:wide, :], up_w.at[:wide, :rest]]
    in_down = [
        pltpu.make_async_copy(w_down.at[:, :wide], downs[0], loads.at[0]),
        pltpu.make_async_copy(w_down.at[:, wide:], downs[1], loads.at[1]),
    ]
    for made in in_down:
        made.start()
    early.step3()
    sums.pass_on()
    for made in y_hid:
        made.wait_recv()
    y_next = y_h2 + [wire.send(dg[m], dg_other[m], wire.beside) for m in range(2)]
    chain.step1()
    for made in in_down:
        made.wait()
    low = both(hid)
    ffn_sum = RowSum(wire, ffn_send, ffn_kept, ffn_got, ffn_out, ffn_back, quarter)
    for columns, part in ((slice(0, wide), downs[0]), (slice(wide, None), downs[1])):
        total = dot(low, part[...])
        for m in range(2):
            ffn_send[m, :, columns] = total[m * rows + half : (m + 1) * rows].astype(LOW)
            ffn_kept[m, :, columns] = total[m * rows : m * rows + half].astype(LOW)
    ffn_sum.core.start()
    early.finish()
    early_send[...] = early_sum[1 - wire.side].astype(LOW)
    y_early = wire.send(early_send, early_back, wire.beside)
    dh2 = sums.result()
    gain_sum[...] = jnp.sum(jnp.sum(dh2 * n2[...], axis=0), axis=0, keepdims=True)
    back = dh2 * gain2[...]
    grad_y = dz[:, :quarter, :].astype(F32) + inv2[...] * (
        back - n2[...] * mean_of(back * n2[...])
    )
    dy[...] = grad_y
    dyl[:, :quarter, :] = grad_y.astype(LOW)
    cross_dyl = wire.send(dyl.at[:, :quarter, :], dyl.at[:, quarter:half, :], wire.cross)
    ffn_sum.pass_on()
    chain.step2()
    cross_dyl.wait_recv()
    core_dyl = wire.send(dyl.at[:, :half, :], dyl.at[:, half:, :], wire.core)
    core_h2 = []
    for i in range(2):
        y_next[i].wait_recv()
        core_h2.append(wire.send(h2_got[i], h2_far[i], wire.core))
    core_dyl.wait_recv()
    for m in range(2):
        side_columns(dyl.at[m], dyl_mine.at[m], dyl_theirs.at[m], wire.side)
    desk.flush(dy, dyl, dyl_mine, dyl_theirs)
    chain.step3()
    layer_own[...] = (y[...] + ffn_sum.result()).astype(LOW)
    y_early.wait_recv()
    grad[:ahead, :] = jnp.transpose(early_sum[wire.side] + early_back[...].astype(F32))
    for made in y_next[2:] + core_h2:
        made.wait_recv()
    chain.finish()
    for made in [*y_hid, cross_dyl, core_dyl, *y_next, *core_h2, y_early]:
        made.wait_send()
    sums.end()
    ffn_sum.end()
    early.settle()
    chain.settle()


class Share:
    def __init__(self, wire, out, quarter):
        spot = lambda block: out.at[:, pl.ds(pl.multiple_of(block * quarter, quarter), quarter), :]
        own, near = spot(wire.blocks[0]), spot(wire.blocks[1])
        self.own = own
        self.first = wire.copy(own, own, wire.cross)
        self.rest = wire.copy(own, own, wire.core), wire.copy(near, near, wire.core)

    def begin(self, value):
        self.own[...] = value
        self.first.start()
        self.rest[0].start()

    def forward(self):
        self.first.wait_recv()
        self.rest[1].start()

    def end(self):
        for made in self.rest:
            made.wait_recv()
        for made in (self.first, *self.rest):
            made.wait_send()


class RowSum:
    def __init__(self, wire, send, kept, got, cross_out, cross_got, quarter, parts=1):
        self.kept, self.got, self.quarter = kept, got, quarter
        self.out, self.back = cross_out, cross_got
        self.core = wire.copy(send, got, wire.core)
        size = quarter // parts
        self.spans = [slice(i * size, (i + 1) * size) for i in range(parts)]
        self.cross = [
            wire.copy(cross_out.at[:, span, :], cross_got.at[:, span, :], wire.cross)
            for span in self.spans
        ]

    def pass_on(self):
        self.core.wait_recv()
        for span, made in zip(self.spans, self.cross):
            rest = slice(self.quarter + span.start, self.quarter + span.stop)
            self.out[:, span, :] = (
                self.kept[:, rest, :] + self.got[:, rest, :].astype(F32)
            ).astype(LOW)
            made.start()

    def result(self, part=0):
        span = self.spans[part]
        self.cross[part].wait_recv()
        return (
            self.kept[:, span, :] + self.got[:, span, :].astype(F32)
            + self.back[:, span, :].astype(F32)
        )

    def end(self):
        self.core.wait_send()
        for made in self.cross:
            made.wait_send()


def halves_terms(mine, got, far, rights, half):
    pairs = [(mine[m], rights[m][...]) for m in range(2)]
    for m in range(2):
        pairs.append((got[m], rights[2 + m][:half, :]))
        pairs.append((far[m], rights[2 + m][half:, :]))
    return pairs


def back2_body(quarter, scale, desk, *refs):
    refs = list(refs)
    take = lambda n: [refs.pop(0) for _ in range(n)]
    (lengths,) = take(1)
    dg, dg_other, du, h2_mine, h2_got, h2_far = (take(2) for _ in range(6))
    dyl, out_proj, q_up = take(3)
    q, kv, o, lse = (take(2) for _ in range(4))
    cos, sin, chat, inv_c, gain_c, dyl_theirs = take(6)
    qn_theirs, os_far = take(2), take(2)
    grad_gate, grad_up, dfirst, gain_sum, dqp, dyl_got, dyl_far, qup_side = take(8)
    oo = take(2)
    du_other = take(2)
    got_a, out_a, got_b, out_b = take(4)
    dq_acc, dqn_send, dqn_keep, kv_send, kv_keep = take(5)
    dqn_got, dqn_out, dqn_back = take(3)
    kv_got, kv_out, kv_back, side_out, side_got, line_out, line_got, kv_own = take(8)
    both, side_sums = take(2)
    wire = Wire(*take(2))
    half, rows = 2 * quarter, 4 * quarter
    wide = kv_own.shape[2] // 2
    rank = chat.shape[2]
    place = wire.place

    y_du = [wire.copy(du[m], du_other[m], wire.beside) for m in range(2)]

    def chain(rights, grad, room):
        def term(z):
            return terms_sum(halves_terms(
                [a[z] for a in h2_mine], [a[z] for a in h2_got], [a[z] for a in h2_far], rights,
                half))

        def keep(total):
            grad[...] = total

        made = LineSum(wire, term, room, *grad.shape, keep)
        made.clear()
        return made

    gate = chain((*dg, *dg_other), grad_gate, (got_a, out_a))
    up = chain((*du, *du_other), grad_up, (got_b, out_b))
    dqn_sum, core_kv, cross_kv, side_kv, line_kv = [], [], [], [], []
    for m in range(2):
        one = lambda ref: ref.at[m : m + 1]
        dqn_sum.append(RowSum(wire, one(dqn_send), one(dqn_keep), one(dqn_got), one(dqn_out),
                              one(dqn_back), quarter))
        core_kv.append(wire.copy(kv_send.at[m], kv_got.at[m], wire.core))
        cross_kv.append(wire.copy(kv_out.at[m], kv_back.at[m], wire.cross))
        side_kv.append(wire.copy(side_out.at[m], side_got.at[m], wire.beside))
        line_kv.append([
            wire.copy(line_out.at[m, d - 1], line_got.at[m, d - 1], {"seq": wire.seq - 2 * d})
            for d in range(1, 4)
        ])
        for d in range(1, 4):

            @pl.when(place > 3 - d)
            def _(m=m, d=d):
                line_got[m, d - 1] = jnp.zeros(line_got.shape[2:], LOW)

    wire.greet(4, 3)
    desk.arrive(*du)
    for made in y_du:
        made.start()
    desk.arrive(*dg, *dg_other, *h2_mine, *h2_got, *h2_far)
    gate.step1()
    desk.arrive()

    def attend(m, between=None):
        rows_at = row_places(wire, quarter, 1)
        attend_back_one(
            scale, [key_places(wire, quarter, 4, 0, (core,)) for core in range(2)], rows_at,
            sequence_starts(lengths, m, rows_at), dyl.at[m], out_proj, q_up, q[m], kv[m], o[m],
            lse[m], cos[m], sin[m], dqp.at[m], dqn_send.at[m], dqn_keep.at[m], kv_send.at[m],
            kv_keep.at[m], dq_acc, between,
        )
        core_kv[m].start()
        dqn_sum[m].core.start()

    split = lambda ref, m: ref[m].reshape(8, 2, quarter, 2 * wide)

    def kv_cross(m):
        dqn_sum[m].pass_on()
        core_kv[m].wait_recv()
        kv_out[m] = (
            split(kv_keep, m)[:, 1].astype(F32) + split(kv_got, m)[:, 1].astype(F32)
        ).astype(LOW)
        cross_kv[m].start()

    def kv_sum(m, span):
        return (
            split(kv_keep, m)[span, 0].astype(F32) + split(kv_got, m)[span, 0].astype(F32)
            + kv_back[m, span].astype(F32)
        )

    def kv_side(m):
        cross_kv[m].wait_recv()
        side_out[m] = kv_sum(m, slice(4, 8)).astype(LOW)
        side_kv[m].start()

    def kv_line(m):
        side_kv[m].wait_recv()
        own = kv_sum(m, slice(0, 4)) + side_got[m].astype(F32)
        kv_own[m] = own[0]
        for d in range(1, 4):
            line_out[m, d - 1] = own[d].astype(LOW)
            pl.when(place >= d)(line_kv[m][d - 1].start)

    def latent(m):
        dqn = dqn_sum[m].result()[0]
        gain = jnp.sum(dqn * chat[m], axis=0, keepdims=True)
        gain_sum[...] = gain if m == 0 else gain_sum[...] + gain
        back = dqn * gain_c[...]
        both[m, :quarter, :rank] = (
            inv_c[m] * (back - chat[m] * mean_of(back * chat[m]))
        ).astype(LOW)

    y_late = []

    def start_up():
        for made in y_du:
            made.wait_recv()
        y_late.append(wire.send(dyl_theirs, dyl_got, wire.beside))
        y_late.extend(wire.send(os_far[m], oo[m], wire.beside) for m in range(2))
        up.step1()

    attend(0)
    kv_cross(0)
    gate.step2()
    attend(1, start_up)
    gate.step3()
    kv_cross(1)
    kv_side(0)
    latent(0)
    up.step2()
    latent(1)
    for z in range(4):
        side_sums[z] = terms_sum([(qn_theirs[m][z], dqp[m]) for m in range(2)]).astype(LOW)
    kv_side(1)
    side_qup = wire.send(side_sums, qup_side, wire.beside)
    side_dyl, *side_o = y_late
    desk.flush(dqp)
    kv_line(0)
    kv_line(1)
    gate.finish()
    desk.flush(grad_gate)
    for m in range(2):
        for d in range(1, 4):
            pl.when(place <= 3 - d)(line_kv[m][d - 1].wait_recv)
        total = kv_own[m]
        for d in range(1, 4):
            total = total + line_got[m, d - 1].astype(F32)
        both[m, :quarter, rank : rank + wide] = unrotate(
            total[:, :wide], cos[m, :quarter], sin[m, :quarter]
        ).astype(LOW)
        both[m, :quarter, rank + wide :] = total[:, wide:].astype(LOW)
    cross_both = wire.send(both.at[:, :quarter, :], both.at[:, quarter:half, :], wire.cross)
    up.step3()
    cross_both.wait_recv()
    core_both = wire.send(both.at[:, :half, :], both.at[:, half:, :], wire.core)
    side_dyl.wait_recv()
    core_dyl = wire.send(dyl_got, dyl_far, wire.core)
    core_both.wait_recv()
    part = rank // 4
    kv_part = wide // 2
    dfirst[:, :, :part] = both[:, :, pl.ds(pl.multiple_of(wire.mp * part, part), part)]
    dfirst[:, :, part:] = both[
        :, :, pl.ds(pl.multiple_of(rank + wire.mp * kv_part, kv_part), kv_part)
    ]
    up.finish()
    core_dyl.wait_recv()
    for made in (side_qup, *side_o):
        made.wait_recv()
    for made in [*y_du, *core_kv, *cross_kv, *side_kv, cross_both, core_both, side_dyl, core_dyl,
                 side_qup, *side_o]:
        made.wait_send()
    for m in range(2):
        dqn_sum[m].end()
        for d in range(1, 4):
            pl.when(place >= d)(line_kv[m][d - 1].wait_send)
    gate.settle()
    up.settle()


def back3_body(quarter, desk, *refs):
    refs = list(refs)
    take = lambda n: [refs.pop(0) for _ in range(n)]
    dfirst, q_down, kv_proj = take(3)
    h1_mine, h1_theirs, o, oo = (take(2) for _ in range(4))
    dyl_mine, dyl_got, dyl_far = take(3)
    qn_mine = take(2)
    dqp, qup_side, n1, inv1, dy, gain1, gain2_sum, gain_c_sum, layer_own = take(9)
    grad_out, grad_qup, grad_qdown, grad_kv, grad_tokens, gains, layer_out = take(7)
    got_a, out_a, got_b, out_b, got_c, out_c = take(6)
    side_sums, side_got = take(2)
    send, kept, row_got, row_out, row_back = take(5)
    kv_out, kv_got = take(2)
    sums, sums_core, sums_cross, sums_side, sums_line, weights, weight_loads = take(7)
    wire = Wire(*take(2))
    half, rows = 2 * quarter, 4 * quarter
    place = wire.place
    part, kv_part = grad_qdown.shape[1], kv_out.shape[1]
    wire.greet(4, 3, diagonal=True)


    def out_term(z):
        return terms_sum(halves_terms(
            [dyl_mine[m, z] for m in range(2)], [dyl_got[m, z] for m in range(2)],
            [dyl_far[m, z] for m in range(2)], (*o, *oo), half))

    def qup_term(z):
        return terms_sum([(qn_mine[m][z], dqp[m]) for m in range(2)]) + qup_side[z].astype(F32)

    def first_term(z):
        return terms_sum([(h1_mine[m][z], dfirst[m]) for m in range(2)]) + side_got[z].astype(F32)

    def keep_out(total):
        grad_out[...] = jnp.transpose(total)

    def keep_qup(total):
        grad_qup[...] = total

    def keep_first(total):
        grad_qdown[...] = total[:, :part]
        kv_out[...] = total[:, part:]

    out = LineSum(wire, out_term, (got_a, out_a), *grad_out.shape[::-1], keep_out)
    qup = LineSum(wire, qup_term, (got_b, out_b), *grad_qup.shape, keep_qup)
    first = LineSum(wire, first_term, (got_c, out_c), kv_out.shape[0], dfirst.shape[2], keep_first)
    for chain in (out, qup, first):
        chain.clear()
    row_sum = RowSum(wire, send, kept, row_got, row_out, row_back, quarter)
    desk.arrive()
    out.step1()
    desk.more()
    in_weights = [
        pltpu.make_async_copy(q_down, weights.at[:, :part], weight_loads.at[0]),
        pltpu.make_async_copy(
            kv_proj.at[:, pl.ds(pl.multiple_of(wire.mp * kv_part, kv_part), kv_part)],
            weights.at[:, part:], weight_loads.at[1],
        ),
    ]
    for made in in_weights:
        made.start()
    desk.arrive()
    for z in range(4):
        side_sums[z] = terms_sum([(h1_theirs[m][z], dfirst[m]) for m in range(2)]).astype(LOW)
    side_first = wire.send(side_sums, side_got, wire.beside)
    for made in in_weights:
        made.wait()
    term = inner_cols(dfirst[...].reshape(2 * rows, dfirst.shape[2]), weights[...])
    for m in range(2):
        send[m] = term[m * rows + half : (m + 1) * rows].astype(LOW)
        kept[m] = term[m * rows : m * rows + half]
    row_sum.core.start()
    qup.step1()
    row_sum.pass_on()
    layer_share = Share(wire, layer_out, quarter)
    layer_share.begin(layer_own[...])
    out.step2()
    side_first.wait_recv()
    first.step1()
    qup.step2()
    dh1 = row_sum.result()
    gain1_sum = jnp.sum(jnp.sum(dh1 * n1[...], axis=0), axis=0, keepdims=True)
    back = dh1 * gain1[...]
    share = Share(wire, grad_tokens, quarter)
    share.begin(
        (dy[...] + inv1[...] * (back - n1[...] * mean_of(back * n1[...]))).astype(LOW)
    )
    w, r = gain1_sum.shape[1] // 8, gain_c_sum.shape[1] // 8
    for s in range(8):
        sums[s] = jnp.concatenate(
            [gain1_sum[:, s * w : (s + 1) * w], gain2_sum[:, s * w : (s + 1) * w],
             gain_c_sum[:, s * r : (s + 1) * r]], axis=1
        )
    core_sums = wire.send(sums, sums_core, wire.core)
    out.step3()
    core_sums.wait_recv()
    core_sums.wait_send()
    sums[...] = sums[...] + sums_core[...]
    cross_sums = wire.send(sums, sums_cross, wire.cross)
    qup.step3()
    first.step2()
    cross_sums.wait_recv()
    cross_sums.wait_send()
    sums[...] = sums[...] + sums_cross[...]
    side_of = lambda p, s: sums.at[2 * p + s]
    side_sends = [
        wire.send(side_of(p, 1 - wire.side), sums_side.at[p], wire.beside) for p in range(4)
    ]
    layer_share.forward()
    share.forward()
    first.step3()
    for made in side_sends:
        made.wait_recv()
        made.wait_send()
    line_sends = []
    for d in range(1, 4):
        for way, there in ((1, place + d <= 3), (-1, place - d >= 0)):
            index = 2 * (d - 1) + (way < 0)
            line_sends.append(
                (wire.copy(sums_line.at[6 + index], sums_line.at[index],
                           {"seq": wire.seq + 2 * way * d}), d, way, there)
            )

            @pl.when(there)
            def _(index=index, d=d, way=way):
                to = place + way * d
                sums_line[6 + index] = sums[2 * to + wire.side] + sums_side[to]
                line_sends[-1][0].start()

            @pl.when((place - way * d < 0) | (place - way * d > 3))
            def _(index=index):
                sums_line[index] = jnp.zeros(sums_line.shape[1:], F32)

    share.end()
    layer_share.end()
    desk.flush(grad_tokens, layer_out)
    first.finish()
    cores = []
    size = kv_out.shape[0] // 4
    for k in range(4):
        rows_of = pl.ds(pl.multiple_of(wire.blocks[k] * size, size), size)
        if k:
            device = {"mp": wire.blocks[k]}
            cores.append(wire.send(kv_out.at[rows_of], kv_got.at[k], device))
        else:
            kv_got[0] = kv_out[rows_of]
    qup.finish()
    desk.flush(grad_qup)
    out.finish()
    desk.flush(grad_out)
    total = sums[2 * place + wire.side] + sums_side[place]
    for made, d, way, there in line_sends:
        pl.when((place - way * d >= 0) & (place - way * d <= 3))(made.wait_recv)
    for index in range(6):
        total = total + sums_line[index]
    gains[...] = total
    for made in cores:
        made.wait_recv()
    columns = kv_out.shape[1]
    for k in range(4):
        at = pl.ds(pl.multiple_of(wire.blocks[k] * columns, columns), columns)
        grad_kv[:, at] = kv_got[k]
    for made in (side_first, *cores):
        made.wait_send()
    for made, d, way, there in line_sends:
        pl.when(there)(made.wait_send)
    row_sum.end()
    for chain in (out, qup, first):
        chain.settle()


def attend_one(
    scale, mp_blocks, c, gain, q_up, cos, sin, kv, key_ids, row_ids, row_starts, out_proj,
    qn, q, o, lse, send, keep, chat_out, inverse_out,
):
    rows = qn.shape[0]
    half, quarter = rows // 2, rows // 4
    part = c.shape[2]
    wide = q.shape[2]
    cut = lambda k, i: c[k, i * quarter : (i + 1) * quarter, :]
    pieces = [jnp.concatenate([cut(k, i ^ k) for i in range(4)], 0) for k in range(4)]
    latent = jnp.concatenate(pieces, 1).astype(F32)
    inverse = inverse_rms(latent)
    chat = latent * inverse
    inverse_out[...] = inverse[:quarter]
    for k in range(4):
        columns = pl.ds(pl.multiple_of(mp_blocks[k] * part, part), part)
        chat_out[:, columns] = chat[:quarter, k * part : (k + 1) * part]
        qn[:, columns] = (chat[:, k * part : (k + 1) * part] * gain[:, columns]).astype(LOW)
    bias = jnp.where((key_ids >= row_starts) & (key_ids <= row_ids), 0.0, NEG_LARGE)
    low = qn[...]
    for h in range(q.shape[0]):
        pre = dot(low, q_up[:, h * wide : (h + 1) * wide])
        q_h = (rotate(pre, cos, sin) * scale).astype(LOW)
        q[h] = q_h
        scores = inner_cols(q_h, kv[:, :wide]) + bias
        top = jnp.max(scores, axis=-1, keepdims=True)
        probs = jnp.exp(scores - top)
        total = jnp.sum(probs, axis=-1, keepdims=True)
        out = dot(probs.astype(LOW), kv[:, wide:]) / total
        o[:, h * wide : (h + 1) * wide] = out.astype(LOW)
        log_total = jnp.broadcast_to(top + jnp.log(total), (rows, 128))
        lse[h : h + 1, :] = jnp.transpose(log_total)[:1]
    keep[...] = dot(o[:half, :], out_proj[...])
    send[...] = dot(o[half:, :], out_proj[...]).astype(LOW)


def fore1_body(scale, desk, *refs):
    refs = list(refs)
    take = lambda n: [refs.pop(0) for _ in range(n)]
    tokens, cotangent, q_down, kv_proj, q_up, out_proj, w_down = take(7)
    lengths, gain1, gain_c, gain2, cosine, sine = take(6)
    h1_mine, h1_theirs, qn_mine, qn_theirs = (take(2) for _ in range(4))
    qs, os, lses, kvs, dz_got = (take(2) for _ in range(5))
    dhid, chat, inv_c, y_out, n2_out, inv2_out, n1_out, inv1_out, h2 = take(9)
    dz, x, down_w, kv_w, up_w, out_w, back_w, h1, c, qn, dz_theirs = take(11)
    send, kept, got, cross_out, cross_got = take(5)
    loads = take(1)[0]
    wire = Wire(*take(2))
    place, blocks = wire.place, wire.blocks
    rows = x.shape[1]
    half, quarter = rows // 2, rows // 4
    wide = kv_proj.shape[1] // 2

    started = []

    def load(source, target):
        made = pltpu.make_async_copy(source, target, loads.at[len(started)])
        made.start()
        started.append(made)
        return made

    def load_rows(source, target):
        return [
            load(source.at[pl.ds(pl.multiple_of(blocks[k] * quarter, quarter), quarter), :],
                 target.at[k * quarter : (k + 1) * quarter, :])
            for k in range(4)
        ]

    in_x = [load_rows(tokens.at[0], x.at[0])]
    in_kv = load(kv_proj, kv_w)
    in_x.append(load_rows(tokens.at[1], x.at[1]))
    in_down = load(q_down, down_w)
    in_dz = [load_rows(cotangent.at[m], dz.at[m]) for m in range(2)]
    in_back, in_up, in_out = load(w_down, back_w), load(q_up, up_w), load(out_proj, out_w)

    line_kv, side_kv, core_kv, cross_c, core_c = [], [], [], [], []
    for m in range(2):
        for d in range(1, 4):

            @pl.when(place < d)
            def _(m=m, d=d):
                kvs[m][0, :, d] = jnp.zeros(kvs[m].shape[1:2] + kvs[m].shape[3:], LOW)
                kvs[m][1, :, d] = jnp.zeros(kvs[m].shape[1:2] + kvs[m].shape[3:], LOW)

        own = kvs[m].at[0, 0, 0]
        line_kv.append([
            wire.copy(own, kvs[m].at[0, 0, d], {"seq": wire.seq + 2 * d}) for d in range(1, 4)
        ])
        side_kv.append([
            wire.copy(kvs[m].at[0, 0, d], kvs[m].at[0, 1, d], wire.beside) for d in range(4)
        ])
        core_kv.append([
            wire.copy(kvs[m].at[0, :, d], kvs[m].at[1, :, d], wire.core) for d in range(4)
        ])
        cross_c.append(wire.copy(c.at[m, 0], c.at[m, 1], wire.cross))
        core_c.append([
            wire.copy(c.at[m, 0], c.at[m, 2], wire.core),
            wire.copy(c.at[m, 1], c.at[m, 3], wire.core),
        ])
    wire.greet(4, 3)

    for m in range(2):
        cos, sin = cosine[m], sine[m]
        for made in in_x[m]:
            made.wait()
        if m == 0:
            in_kv.wait()
        values = x[m].astype(F32)
        inverse = inverse_rms(values)
        normed = values * inverse
        n1_out[m], inv1_out[m] = normed[:quarter], inverse[:quarter]
        low = (normed * gain1[...]).astype(LOW)
        h1[...] = low
        pair = dot(low[:half], kv_w[...])
        own = kvs[m].at[0, 0, 0]
        own[:, :wide] = rotate(pair[:, :wide], cos[:half], sin[:half]).astype(LOW)
        own[:, wide:] = pair[:, wide:].astype(LOW)
        for d in (3, 2, 1):
            pl.when(place + d <= 3)(line_kv[m][d - 1].start)
        side_kv[m][0].start()
        if m == 0:
            in_down.wait()
        c[m, 0] = dot(low, down_w[...]).astype(LOW)
        cross_c[m].start()
        core_c[m][0].start()
        side_columns(h1, h1_mine[m], h1_theirs[m], wire.side)
        desk.flush(h1_mine[m], h1_theirs[m])

    def pass_kv(m, d):
        @pl.when(place >= d)
        def _():
            line_kv[m][d - 1].wait_recv()
            side_kv[m][d].start()

    def pass_core(m, d):
        @pl.when(place >= d)
        def _():
            side_kv[m][d].wait_recv()
            core_kv[m][d].start()

    in_back.wait()
    for m in range(2):
        for made in in_dz[m]:
            made.wait()
    dhid[0] = inner_cols(dz[0], back_w[...])
    for d in (1, 2, 3):
        pass_kv(0, d)
    pass_core(0, 0)
    for m in range(2):
        cross_c[m].wait_recv()
        core_c[m][1].start()
    dhid[1] = inner_cols(dz[1], back_w[...])
    for d in (1, 2, 3):
        pass_kv(1, d)
    for m in range(2):
        for z in range(4):
            block = dz_theirs.shape[3]
            columns = pl.ds(pl.multiple_of((2 * z + 1 - wire.side) * block, block), block)
            dz_theirs[m, z] = dz[m, :half, columns]
    desk.flush(dhid, n1_out)
    for d in (1, 2, 3):
        pass_core(0, d)
    in_up.wait()
    in_out.wait()
    sums = [
        RowSum(wire, send.at[m : m + 1], kept.at[m : m + 1], got.at[m : m + 1],
               cross_out.at[m : m + 1], cross_got.at[m : m + 1], quarter, 2)
        for m in range(2)
    ]
    shares = []

    def after_sum(m):
        for part, span in enumerate(sums[m].spans):
            value = x[m, span, :].astype(F32) + sums[m].result(part)[0]
            inverse = inverse_rms(value)
            normed = value * inverse
            y_out[m, span, :], n2_out[m, span, :], inv2_out[m, span, :] = value, normed, inverse
            h2[m, span, :] = (normed * gain2[...]).astype(LOW)
            spot = lambda k: h2.at[m, k * quarter + span.start : k * quarter + span.stop, :]
            shares.append((
                wire.send(spot(0), spot(1), wire.cross), wire.send(spot(0), spot(2), wire.core),
                wire.copy(spot(1), spot(3), wire.core),
            ))

    for m in range(2):
        if m == 1:
            for d in range(4):
                pass_core(1, d)
        for d in range(4):
            pl.when(place >= d)(core_kv[m][d].wait_recv)
        for made in core_c[m]:
            made.wait_recv()
        desk.flush(kvs[m])
        rows_at = row_places(wire, quarter, 0)
        attend_one(
            scale, blocks, c.at[m], gain_c, up_w, cosine[m], sine[m],
            kvs[m][...].reshape(2 * 2 * 4 * half, 2 * wide),
            key_places(wire, quarter, 4, 1, (0, 1)), rows_at,
            sequence_starts(lengths, m, rows_at), out_w, qn, qs[m], os[m], lses[m], send.at[m], kept.at[m],
            chat.at[m], inv_c.at[m],
        )
        sums[m].core.start()
        if m == 0:
            side_dz = wire.send(dz_theirs, dz_got[0], wire.beside)
        side_columns(qn, qn_mine[m], qn_theirs[m], wire.side)
        desk.flush(qs[m], os[m], qn_mine[m], qn_theirs[m])
        if m == 1:
            after_sum(0)
        sums[m].pass_on()
    after_sum(1)
    desk.flush(chat, y_out, n2_out)
    side_dz.wait_recv()
    core_dz = wire.send(dz_got[0], dz_got[1], wire.core)
    for near, _, far in shares:
        near.wait_recv()
        far.start()
    for _, first, far in shares:
        first.wait_recv()
        far.wait_recv()
    core_dz.wait_recv()
    for made in [side_dz, core_dz, *cross_c, *(a for p in core_c for a in p),
                 *(a for p in shares for a in p)]:
        made.wait_send()
    for m in range(2):
        sums[m].end()
        for d in range(4):

            @pl.when(place >= d)
            def _(m=m, d=d):
                side_kv[m][d].wait_send()
                core_kv[m][d].wait_send()

        for d in range(1, 4):
            pl.when(place + d <= 3)(line_kv[m][d - 1].wait_send)


def deliver_body(count, pieces, *refs):
    results, gains = refs[:count], refs[count]
    outs, rooms, sems = refs[count + 1 : -count - 1], refs[-count - 1 : -1], refs[-1]
    loads, stores = [], []
    for source, room, target in zip(results, rooms, outs):
        size = source.shape[-2] // pieces
        for i in range(pieces):
            cut = (slice(None),) * (len(source.shape) - 2) + (slice(i * size, (i + 1) * size),)
            at = len(loads)
            loads.append(pltpu.make_async_copy(source.at[cut], room.at[cut], sems.at[2 * at]))
            stores.append(pltpu.make_async_copy(room.at[cut], target.at[cut], sems.at[2 * at + 1]))
    for made in loads:
        made.start()
    at = 0
    for ref in outs[count:]:
        ref[...] = gains[0, at : at + ref.shape[0]]
        at += ref.shape[0]
    for load, store in zip(loads, stores):
        load.wait()
        store.start()
    for made in stores:
        made.wait()


def local(
    tokens,
    lengths,
    norm1_gain,
    q_down,
    latent_gain,
    q_up,
    kv_proj,
    out_proj,
    norm2_gain,
    w_gate,
    w_up,
    w_down,
    cotangent,
):
    micro, rows, width = tokens.shape
    seq = lax.axis_size("seq")
    line = seq // 2
    at = lax.axis_index("seq").astype(jnp.int32)
    me = lax.axis_index("mp").astype(jnp.int32)
    place, side = at // 2, at % 2
    ids = jnp.stack([me, side])
    quarter, half = rows // 4, rows // 2
    head_dim = kv_proj.shape[1] // 2
    heads = q_up.shape[1] // head_dim
    part = q_down.shape[1]
    rank = q_up.shape[0]
    hidden = w_gate.shape[1]
    kv_part = kv_proj.shape[1] // 4
    wide = width // seq
    scale = head_dim ** (-0.5)
    key_count = seq * rows
    beside = [(i, i ^ 1) for i in range(seq)]
    narrow = line == 4 and micro == 2 and key_count <= 2048 and not wide % 128

    def swap(index):
        return ((index & 1) << 1) | (index >> 1)

    def to_natural(array, axis):
        size = array.shape[axis] // 4
        return jnp.concatenate(
            [lax.dynamic_slice_in_dim(array, swap(me ^ b) * size, size, axis) for b in range(4)],
            axis,
        )

    def other(array):
        return lax.ppermute(array, "seq", beside)

    def sum_mp(send, keep):
        kept = keep + lax.ppermute(send, "mp", CORE).astype(F32)
        got = lax.ppermute(kept[..., quarter:, :].astype(LOW), "mp", CROSS)
        return kept[..., :quarter, :] + got.astype(F32)

    def gather_mp(piece):
        near = lax.ppermute(piece, "mp", CROSS)
        pair = jnp.concatenate([piece, near], -2)
        return piece, near, lax.ppermute(pair, "mp", CORE)

    def sides_shape(columns, their_rows, lead=()):
        if columns // seq % 128:
            return []
        return [
            whole((*lead, line, n, columns // seq), LOW) for n in (rows, their_rows)
        ]

    def split_sides(made, full, their_rows):
        if made:
            return made
        split = full.reshape(*full.shape[:-1], line, 2, full.shape[-1] // seq)
        mine, theirs = (
            jnp.moveaxis(lax.dynamic_index_in_dim(split, i, split.ndim - 2, keepdims=False), -2, -3)
            for i in (side, 1 - side)
        )
        return mine, theirs[..., :their_rows, :]

    def from_other(theirs):
        got = other(theirs)
        return got, lax.ppermute(got, "mp", CORE)

    def without_sides(body, count):
        return body if count else lambda *refs: body(*refs, None, None)

    def both_sides(mine, got):
        lefts, spans = [], []
        for array, first, count, partner in (
            (mine, 0, rows, 0), (got[0], 0, half, 1), (got[1], half, half, 1)
        ):
            stacked_array = not isinstance(array, list)
            for m in range(micro):
                spans.append((len(lefts) if not stacked_array else len(lefts), m if stacked_array else None,
                              m, partner, first, count))
                if not stacked_array:
                    lefts.append(array[m])
            if stacked_array:
                lefts.append(array)
        return lefts, spans

    class Chain:
        def __init__(self, lefts, rights, terms, shape, turned=False, from_side=None):
            self.args = [*lefts, *rights]
            self.spec = (terms, len(lefts), len(rights))
            self.shape, self.turned = shape, turned
            self.from_side = [] if from_side is None else [from_side]
            self.step, self.up, self.down = 0, None, None

        def block(self, index, added, after, last=False):
            turned = last and self.turned
            body = functools.partial(
                block_body, *self.spec, len(added), len(self.from_side), turned
            )
            shape = self.shape[::-1] if turned else self.shape
            return run(
                body, index.reshape(1), [*self.args, *added, *self.from_side],
                [whole(shape, F32 if last else LOW)], after, name="block",
            )[0]

        def advance(self, after):
            self.step += 1
            step = self.step
            goes_up = [(i, i + 2) for i in range(2 * step)]
            goes_down = [(seq - 1 - i, seq - 3 - i) for i in range(2 * step)]
            for_up, for_down = line - step + place, step - line + place
            if 2 * step < line + 1:
                which = jnp.where(
                    place <= step - 1, for_up, jnp.where(place >= line - step, for_down, 0)
                )
                term = self.block(which, [a for a in (self.up, self.down) if a is not None], after)
                if step == 1 and line > 3:
                    self.up = lax.ppermute(term, "seq", goes_up + goes_down)
                else:
                    self.up = lax.ppermute(term, "seq", goes_up)
                    self.down = lax.ppermute(term, "seq", goes_down)
                return [term]
            term_up = self.block(jnp.clip(for_up, 0, line - 1), [self.up], after)
            term_down = self.block(jnp.clip(for_down, 0, line - 1), [self.down], [term_up])
            self.up = lax.ppermute(term_up, "seq", goes_up)
            self.down = lax.ppermute(term_down, "seq", goes_down)
            return [term_down]

        def finish(self, after):
            while self.step < line - 1:
                after = self.advance(after)
            result = self.block(place, [self.up, self.down], after, last=True)
            return result, [result]

    quarter_rows = jnp.arange(quarter, dtype=jnp.int32)
    row_ids = at * rows + jnp.concatenate([(me ^ k) * quarter + quarter_rows for k in ORDER])
    key_ids = (
        ((place - jnp.arange(line, dtype=jnp.int32)[None, None, :, None, None]) * 2
         + (side ^ jnp.arange(2, dtype=jnp.int32)[None, :, None, None, None])) * rows
        + (me ^ (jnp.arange(2, dtype=jnp.int32)[:, None, None, None, None]
                 + 2 * jnp.arange(2, dtype=jnp.int32)[None, None, None, :, None])) * quarter
        + quarter_rows[None, None, None, None, :]
    ).reshape(key_count)

    gain1_row, gain2_row, gain_c_row = norm1_gain[None, :], norm2_gain[None, :], latent_gain[None, :]
    kv_cols = lax.dynamic_slice_in_dim(kv_proj, me * kv_part, kv_part, 1)
    first_weights = jnp.concatenate([q_down, kv_cols], axis=1)
    low = lambda *shape: pltpu.VMEM(shape, LOW)
    full = lambda *shape: pltpu.VMEM(shape, F32)
    near = lambda *arrays: [(1, a) for a in arrays]
    far = lambda *arrays: [(0, a) for a in arrays]
    columns = heads * head_dim
    side_rows = rank // seq
    first_columns = part + kv_part

    def narrow_layer():
        numbers = lambda array: [(2, array)]
        late = lambda *arrays: [(3, a) for a in arrays]
        later = lambda *arrays: [(4, a) for a in arrays]
        first_end = lengths[:, 0:1]
        second_end = first_end + lengths[:, 1:2]
        places = row_ids[None, :] - jnp.where(
            row_ids >= second_end, second_end, jnp.where(row_ids >= first_end, first_end, 0)
        )
        freqs = BASE ** (-2.0 * jnp.arange(head_dim // 2, dtype=F32) / head_dim)
        angles = places.astype(F32)[:, :, None] * freqs
        cosine, sine = jnp.cos(angles), jnp.sin(angles)
        row_shape = whole((micro, quarter, width), F32)
        one_shape = whole((micro, quarter, 1), F32)
        side_shape = whole((micro, line, half, wide), LOW)
        args = far(tokens, cotangent, q_down, kv_proj, q_up, out_proj, w_down)
        args += numbers(lengths) + near(gain1_row, gain_c_row, gain2_row, cosine, sine)
        outs = late(*[whole((line, rows, wide), LOW)] * 4, *[whole((line, rows, side_rows), LOW)] * 4)
        outs += late(*[whole((heads, rows, head_dim), LOW)] * 2, *[whole((rows, columns), LOW)] * 2)
        outs += near(*[whole((heads, rows), F32)] * 2)
        outs += late(*[whole((2, 2, line, half, 2 * head_dim), LOW)] * 2)
        outs += far(*[side_shape] * 2)
        outs += late(
            whole((micro, rows, hidden), F32), whole((micro, quarter, rank), F32))
        outs += near(one_shape) + late(row_shape, row_shape) + near(one_shape) + late(row_shape)
        outs += near(one_shape) + late(whole((micro, rows, width), LOW))
        made = list(mesh_run(
            functools.partial(fore1_body, scale), args, outs,
            [low(micro, rows, width), low(micro, rows, width), low(width, part),
             low(width, 2 * head_dim),
             low(rank, columns), low(columns, width), low(hidden, width), low(rows, width),
             low(micro, 4, rows, part), low(rows, rank), low(micro, line, half, wide),
             low(micro, half, width), full(micro, half, width), low(micro, half, width),
             low(micro, quarter, width), low(micro, quarter, width),
             pltpu.SemaphoreType.DMA((24,))],
            4, "fore1", 60, 72,
        ))
        give = lambda n: [made.pop(0) for _ in range(n)]
        h1_mine, h1_theirs, qn_mine, qn_theirs = (give(2) for _ in range(4))
        qs, os, lses, kv, dz_got = (give(2) for _ in range(5))
        kv = [a.reshape(key_count, 2 * head_dim) for a in kv]
        dhid, chat, inv_c, y, n2, inv2, n1, inv1, h2 = give(9)

        ahead = hidden * 3 // 11 // 128 * 128
        args = far(w_gate, w_up, w_down, cotangent) + late(h2) + later(dhid, n2)
        args += near(inv2, gain2_row) + later(*dz_got, y)
        outs = near(whole((hidden, wide), F32)) + late(row_shape) + near(whole((1, width), F32))
        outs += late(whole((micro, rows, width), LOW), whole((micro, line, rows, wide), LOW), side_shape)
        outs += near(whole((micro, quarter, width), LOW))
        outs += late(*[whole((rows, hidden), LOW)] * 6, *[whole((line, rows, wide), LOW)] * 2)
        outs += far(*[whole((line, half, wide), LOW)] * 4, *[whole((rows, hidden), LOW)] * 2)
        made = list(mesh_run(
            functools.partial(back1_body, quarter), args, outs,
            [low(width, hidden), low(width, hidden), low(rows, hidden - ahead),
             low(rows, hidden - ahead), low(micro, line, half, wide),
             low(5, wide, hidden - ahead), low(2, wide, hidden - ahead),
             low(micro, half, width), full(micro, half, width), low(micro, half, width),
             low(micro, quarter, width), low(micro, quarter, width),
             pltpu.SemaphoreType.DMA((6,)), low(micro, half, width), low(micro, half, width),
             low(micro, half, width), low(micro, quarter, width), low(micro, quarter, width),
             low(5, 2 * wide, ahead), low(2, 2 * wide, ahead), full(2, wide, ahead),
             low(wide, ahead), low(wide, ahead), low(micro, rows, width),
             pltpu.SemaphoreType.DMA((8,))],
            1, "back1", 62, 40,
        ))
        grad_down, dy, gain2, dyl, dyl_mine, dyl_theirs, layer_own = give(7)
        hid, dg, du, h2_mine, h2_got, h2_far, dg_other = (give(2) for _ in range(7))

        args = numbers(lengths) + late(*dg, *dg_other, *du, *h2_mine, *h2_got, *h2_far)
        args += late(dyl, out_proj, q_up, *qs, *kv, *os) + near(*lses)
        args += late(cosine, sine, chat) + near(inv_c, gain_c_row) + far(dyl_theirs)
        args += late(*qn_theirs) + far(*os)
        outs = late(whole((wide, hidden), F32), whole((wide, hidden), F32))
        outs += near(whole((micro, rows, first_columns), LOW), whole((1, rank), F32))
        outs += late(whole((micro, rows, columns), LOW))
        outs += far(side_shape, side_shape, whole((line, side_rows, columns), LOW),
                    *[whole((rows, columns), LOW)] * 2)
        kv_low = lambda *lead: low(*lead, quarter, 2 * head_dim)
        key_half = key_count // 2
        (grad_gate, grad_up, dfirst, gain_c, dqp, dyl_got, dyl_far, qup_side,
         *o_other) = mesh_run(
            functools.partial(back2_body, quarter, scale), args, outs,
            [low(rows, hidden), low(rows, hidden), low(5, wide, hidden), low(2, wide, hidden),
             low(5, wide, hidden), low(2, wide, hidden), full(heads * rows, head_dim),
             low(micro, half, rank),
             full(micro, half, rank), low(micro, key_half, 2 * head_dim),
             low(micro, key_half, 2 * head_dim), low(micro, half, rank),
             low(micro, quarter, rank), low(micro, quarter, rank),
             low(micro, key_half, 2 * head_dim), kv_low(micro, 2 * line), kv_low(micro, 2 * line),
             kv_low(micro, line), kv_low(micro, line), kv_low(micro, 3), kv_low(micro, 3),
             full(micro, quarter, 2 * head_dim), low(micro, rows, rank + 2 * head_dim),
             low(line, side_rows, columns)],
            2, "back2", 62, 44,
        )

        args = later(dfirst) + far(q_down, kv_proj) + later(*h1_mine, *h1_theirs)
        args += late(*os, *o_other, dyl_mine, dyl_got, dyl_far)
        args += later(*qn_mine, dqp, qup_side, n1)
        args += near(inv1) + later(dy) + near(gain1_row, gain2, gain_c, layer_own)
        block = width // 4 // seq
        gain_columns = 2 * wide + side_rows
        outs = late(whole((columns, wide), F32), whole((side_rows, columns), F32))
        outs += near(whole((wide, part), F32), whole((block, 2 * head_dim), F32))
        outs += late(whole((micro, rows, width), LOW)) + near(whole((1, gain_columns), F32))
        outs += late(whole((micro, rows, width), LOW))
        grad_out, grad_qup, grad_qdown, grad_kv, input_grads, gains, layer_out = mesh_run(
            functools.partial(back3_body, quarter), args, outs,
            [low(5, wide, columns), low(2, wide, columns), low(5, side_rows, columns),
             low(2, side_rows, columns), low(5, wide, first_columns),
             low(2, wide, first_columns), low(line, wide, first_columns),
             low(line, wide, first_columns), low(micro, half, width), full(micro, half, width),
             low(micro, half, width), low(micro, quarter, width), low(micro, quarter, width),
             full(wide, kv_part), full(4, block, kv_part), full(seq, 1, gain_columns),
             full(seq, 1, gain_columns), full(seq, 1, gain_columns), full(line, 1, gain_columns),
             full(12, 1, gain_columns), low(width, first_columns), pltpu.SemaphoreType.DMA((2,))],
            3, "back3", 60, 44,
        )
        results = [layer_out, input_grads, grad_qdown, grad_qup, grad_kv, grad_out, grad_gate,
                   grad_up, grad_down]
        made = pl.pallas_call(
            functools.partial(deliver_body, len(results), 4),
            in_specs=[pl.BlockSpec(memory_space=pl.ANY)] * len(results) + [in_vmem()],
            out_specs=[pl.BlockSpec(memory_space=pl.ANY)] * len(results) + [in_vmem()] * 3,
            out_shape=[whole(a.shape, a.dtype) for a in results]
            + [whole((n,), F32) for n in (wide, wide, side_rows)],
            scratch_shapes=[pltpu.VMEM(a.shape, a.dtype) for a in results]
            + [pltpu.SemaphoreType.DMA((8 * len(results),))],
            compiler_params=pltpu.CompilerParams(vmem_limit_bytes=60 << 20),
            name="deliver",
        )(*results, gains)
        (layer_out, input_grads, grad_qdown, grad_qup, grad_kv, grad_out, grad_gate, grad_up,
         grad_down, grad_n1, grad_n2, grad_c) = made
        return (
            layer_out, input_grads, grad_n1, grad_qdown, grad_c, grad_qup, grad_kv, grad_out,
            grad_n2, grad_gate, grad_up, grad_down,
        )

    if narrow:
        return narrow_layer()

    both_rows = sides_shape(width, rows)
    half_rows = sides_shape(width, half)
    rank_sides = sides_shape(rank, rows)

    tables, starts, kv, c_part, h1_sides = [], [], [], [], []
    order = []
    for m in range(micro):
        _, places = documents(lengths[m], row_ids)
        starts.append(row_ids - places)
        tables.append(rotation(places, head_dim))
        c, packed, h1, *made = run(
            without_sides(functools.partial(first_body, m, quarter), len(both_rows)),
            ids,
            [tokens, gain1_row, q_down, kv_proj, *tables[m]],
            [whole((rows, part), LOW), whole((half, 2 * head_dim), LOW), whole((rows, width), LOW),
             *both_rows],
            order,
            name="first",
        )
        order = [c]
        blocks = [packed] + [
            lax.ppermute(packed, "seq", [(i, i + 2 * d) for i in range(seq - 2 * d)])
            for d in range(1, line)
        ]
        near = jnp.stack(blocks, 0)
        near = jnp.stack([near, other(near)], 0)
        kv.append(
            jnp.stack([near, lax.ppermute(near, "mp", CORE)], 0).reshape(key_count, 2 * head_dim)
        )
        c_part.append(c)
        h1_sides.append(split_sides(made, h1, rows))

    dhid, dz, *made = run(
        functools.partial(cotangent_body, micro, quarter),
        ids,
        [cotangent, w_down],
        [whole((micro, rows, hidden), F32), whole((micro, rows, width), LOW),
         *sides_shape(width, half, (micro,))],
        order,
        name="cotangent",
    )
    order = [dz]
    dz_mine, dz_theirs = split_sides(made, dz, half)
    dz_got = from_other(dz_theirs)

    qn_sides, qs, os, lses, sums, c_rows = [], [], [], [], [], []
    for m in range(micro):
        near = lax.ppermute(c_part[m], "mp", CROSS)
        swapped = jnp.concatenate(
            [near[quarter : 2 * quarter], near[:quarter], near[3 * quarter :],
             near[2 * quarter : 3 * quarter]], 0
        )
        far = lax.ppermute(jnp.concatenate([c_part[m], swapped], 1), "mp", CORE)
        qn, q, o, lse, send, keep, *made = run(
            without_sides(functools.partial(attend_body, scale), len(rank_sides)),
            ids,
            [c_part[m], near, far, gain_c_row, q_up, *tables[m], kv[m], key_ids[None, :],
             row_ids[:, None], starts[m][:, None], out_proj],
            [whole((rows, rank), LOW), whole((heads, rows, head_dim), LOW),
             whole((rows, heads * head_dim), LOW), whole((heads, rows), F32),
             whole((half, width), LOW), whole((half, width), F32), *rank_sides],
            order,
            name="attend",
        )
        order = [o]
        qn_sides.append(split_sides(made, qn, rows))
        qs.append(q)
        os.append(o)
        lses.append(lse)
        sums.append(sum_mp(send, keep))
        c_rows.append(
            jnp.concatenate([c_part[m][:quarter], swapped[:quarter], far[half : half + quarter]], 1)
        )

    h2_mine, h2_theirs, hid, dg, du, state = [], [], [], [], [], []
    for m in range(micro):
        x = lax.dynamic_slice_in_dim(tokens[m], me * quarter, quarter, 0).astype(F32)
        inv1 = inverse_rms(x)
        y = x + sums[m]
        inv2 = inverse_rms(y)
        n2 = y * inv2
        pieces = gather_mp((n2 * gain2_row).astype(LOW))
        h2, hid_m, dg_m, du_m, *made = run(
            without_sides(functools.partial(forward_body, m), len(half_rows)),
            ids,
            [*pieces, w_gate, w_up, dhid],
            [whole((rows, width), LOW), *[whole((rows, hidden), LOW)] * 3, *half_rows],
            order,
            name="forward",
        )
        order = [hid_m]
        mine, theirs = split_sides(made, h2, half)
        h2_mine.append(mine)
        h2_theirs.append(theirs)
        hid.append(hid_m)
        dg.append(dg_m)
        du.append(du_m)
        state.append(dict(x=x, n1=x * inv1, inv1=inv1, y=y, n2=n2, inv2=inv2, c=c_rows[m]))

    def stacked(name):
        return jnp.stack([st[name] for st in state], 0)

    def with_other(arrays):
        return [*arrays, *[other(a) for a in arrays]]

    def terms_of(spans):
        return [(a, lead, m + micro * partner, None, first, count)
                for a, lead, m, partner, first, count in spans]

    send, keep, ffn_send, ffn_keep = run(
        functools.partial(hidden_back_body, micro),
        ids,
        [*dg, *du, *hid, w_gate, w_up, w_down],
        [whole((micro, half, width), LOW), whole((micro, half, width), F32)] * 2,
        order,
        name="hidden_back",
    )
    lefts, spans = both_sides(dz_mine, dz_got)
    chain_down = Chain(lefts, with_other(hid), terms_of(spans), (wide, hidden), turned=True)
    lefts, spans = both_sides(h2_mine, [list(p) for p in zip(*[from_other(t) for t in h2_theirs])])
    chain_gate = Chain(lefts, with_other(dg), terms_of(spans), (wide, hidden))
    chain_up = Chain(lefts, with_other(du), terms_of(spans), (wide, hidden))

    order = chain_down.advance([send])
    dh2 = sum_mp(send, keep)
    y, n2, inv2, n1, inv1 = (stacked(k) for k in ("y", "n2", "inv2", "n1", "inv1"))
    dz_own = dz[:, :quarter].astype(F32)
    gain2 = jnp.sum(dh2 * n2, axis=(0, 1))
    dy = dz_own + norm_backward(dh2 * gain2_row, n2, inv2)
    for _ in range(2):
        order = chain_down.advance(order)
    order = chain_gate.advance(order)

    def attend_back(which, pieces):
        args = [*pieces, out_proj, q_up, key_ids[:, None]]
        for m in which:
            args += [qs[m], kv[m], os[m], lses[m], jnp.stack([row_ids, starts[m]], 0), *tables[m]]
        n = len(which)
        return run(
            functools.partial(attend_back_body, scale, n, min(1024, key_count // 2)),
            ids,
            args,
            [whole((n, rows, width), LOW), whole((n, rows, heads * head_dim), LOW),
             whole((n, half, rank), LOW), whole((n, half, rank), F32),
             whole((n, key_count // 2, 2 * head_dim), LOW),
             whole((n, key_count // 2, 2 * head_dim), F32), *sides_shape(width, half, (n,))],
            order,
            scratch=[pltpu.VMEM((heads, rows, head_dim), F32),
                     pltpu.VMEM((heads, rows, head_dim), LOW),
                     pltpu.VMEM((heads, 8, rows), F32)],
            name="attend_back",
            limit=56,
        )

    pieces = gather_mp(dy.astype(LOW))
    if key_count <= 2048:
        made = attend_back(range(micro), pieces)
    else:
        each = [attend_back([m], [p[m : m + 1] for p in pieces]) for m in range(micro)]
        made = [jnp.concatenate(parts, 0) for parts in zip(*each)]
    dyl, dqp, send, keep, kv_send, kv_keep, *made = made
    order = [send]
    dyl_mine, dyl_theirs = split_sides(made, dyl, half)
    lefts, spans = both_sides(dyl_mine, from_other(dyl_theirs))
    chain_out = Chain(lefts, with_other(os), terms_of(spans), (wide, heads * head_dim), turned=True)

    def side_sum(lefts, rights, shape, after):
        terms = [(m, None, 0, m, 0, rows) for m in range(micro)]
        (made,) = run(
            functools.partial(side_sum_body, terms, len(lefts)),
            ids,
            [*lefts, *rights],
            [whole((line, *shape), LOW)],
            after,
            name="side_sum",
        )
        return other(made), [made]

    def own_chain(side_pairs, right, shape, after):
        from_side, after = side_sum([p[1] for p in side_pairs], [right], shape, after)
        terms = [(m, None, 0, m, 0, rows) for m in range(micro)]
        return Chain([p[0] for p in side_pairs], [right], terms, shape, from_side=from_side), after

    shape = (rank // seq, heads * head_dim)
    chain_qup, order = own_chain(qn_sides, dqp, shape, order)
    order = chain_gate.advance(order)
    order = chain_up.advance(order)

    dqn = sum_mp(send, keep)
    c = stacked("c").astype(F32)
    inv_c = inverse_rms(c)
    chat = c * inv_c
    chat = to_natural(chat, 2)
    gain_c = jnp.sum(dqn * chat, axis=(0, 1))
    dc = norm_backward(dqn * gain_c_row, chat, inv_c).astype(LOW)

    dkv = kv_keep + lax.ppermute(kv_send, "mp", CORE).astype(F32)
    dkv = dkv.reshape(micro, 2, line, 2, quarter, 2 * head_dim)
    dkv = dkv[:, :, :, 0] + lax.ppermute(dkv[:, :, :, 1].astype(LOW), "mp", CROSS).astype(F32)
    dkv = dkv[:, 0] + other(dkv[:, 1].astype(LOW)).astype(F32)
    total = dkv[:, 0]
    for d in range(1, line):
        total = total + lax.ppermute(
            dkv[:, d].astype(LOW), "seq", [(i + 2 * d, i) for i in range(seq - 2 * d)]
        ).astype(F32)
    cosine = jnp.stack([t[0][:quarter] for t in tables], 0)
    sine = jnp.stack([t[1][:quarter] for t in tables], 0)
    dkv_low = jnp.concatenate(
        [unrotate(total[..., :head_dim], cosine, sine), total[..., head_dim:]], axis=-1
    ).astype(LOW)
    both = jnp.concatenate(gather_mp(jnp.concatenate([dc, dkv_low], -1)), -2)
    dfirst = jnp.concatenate(
        [lax.dynamic_slice_in_dim(both, me * part, part, 2),
         lax.dynamic_slice_in_dim(both, rank + me * kv_part, kv_part, 2)], -1
    )

    grad_down, order = chain_down.finish(order)
    order = chain_gate.advance(order)
    order = chain_up.advance(order)
    order = chain_out.advance(order)
    grad_gate, order = chain_gate.finish(order)
    order = chain_up.advance(order)
    order = chain_out.advance(order)
    grad_up, order = chain_up.finish(order)
    order = chain_qup.advance(order)
    order = chain_out.advance(order)
    chain_first, order = own_chain(h1_sides, dfirst, (wide, part + kv_part), order)
    order = chain_qup.advance(order)
    grad_out, order = chain_out.finish(order)
    order = chain_first.advance(order)
    order = chain_qup.advance(order)
    order = chain_first.advance(order)
    grad_qup, order = chain_qup.finish(order)
    order = chain_first.advance(order)
    grad_first, order = chain_first.finish(order)

    grad_qdown = grad_first[:, :part]
    kv_cols_grad = grad_first[:, part:]
    pieces = []
    for k in ORDER:
        size = kv_cols_grad.shape[0] // 4
        sent = lax.dynamic_slice_in_dim(kv_cols_grad, (me ^ k) * size, size, 0)
        pieces.append(lax.ppermute(sent, "mp", [(i, i ^ k) for i in range(4)]) if k else sent)
    grad_kv = to_natural(jnp.concatenate(pieces, 1), 1)

    def put_natural(pieces):
        return run(
            functools.partial(natural_body, micro, quarter),
            ids,
            pieces,
            [whole((micro, rows, width), LOW)],
            name="natural",
        )[0]

    part_sum = inner_cols(dfirst.reshape(micro * rows, -1), first_weights).reshape(micro, rows, width)
    dh1 = sum_mp(part_sum[:, half:].astype(LOW), part_sum[:, :half])
    gain1 = jnp.sum(dh1 * n1, axis=(0, 1))
    dx = (dy + norm_backward(dh1 * gain1_row, n1, inv1)).astype(LOW)
    input_grads = put_natural(gather_mp(dx))

    ffn = sum_mp(ffn_send, ffn_keep)
    layer_out = put_natural(gather_mp((y + ffn).astype(LOW)))

    gains = jnp.concatenate(
        [gain1.reshape(seq, -1), gain2.reshape(seq, -1), gain_c.reshape(seq, -1)], axis=1
    )
    gains = gains + lax.ppermute(gains, "mp", CORE)
    gains = gains + lax.ppermute(gains, "mp", CROSS)
    gain_sum = lax.dynamic_index_in_dim(gains, at, 0, keepdims=False)
    for k in range(1, seq):
        gain_sum = gain_sum + lax.ppermute(
            lax.dynamic_index_in_dim(gains, at ^ k, 0, keepdims=False),
            "seq",
            [(i, i ^ k) for i in range(seq)],
        )
    return (
        layer_out,
        input_grads,
        gain_sum[:wide],
        grad_qdown,
        gain_sum[2 * wide :],
        grad_qup,
        grad_kv,
        grad_out,
        gain_sum[wide : 2 * wide],
        grad_gate,
        grad_up,
        grad_down,
    )


def solution(mesh):
    placed = (
        P(None, "seq", None),
        P(),
        P(),
        P(None, "mp"),
        P(),
        P(None, "mp"),
        P(),
        P("mp", None),
        P(),
        P(None, "mp"),
        P(None, "mp"),
        P("mp", None),
        P(None, "seq", None),
    )
    return jax.shard_map(
        local,
        mesh=mesh,
        in_specs=placed,
        out_specs=(
            P(None, "seq", None),
            P(None, "seq", None),
            P("seq"),
            P("seq", "mp"),
            P("seq"),
            P("seq", "mp"),
            P(("seq", "mp"), None),
            P("mp", "seq"),
            P("seq"),
            P("seq", "mp"),
            P("seq", "mp"),
            P("mp", "seq"),
        ),
        check_vma=False,
    )
```

```python
import functools

import jax
import jax.numpy as jnp
from jax import lax
from jax.experimental import pallas as pl
from jax.experimental.pallas import tpu as pltpu
from jax.sharding import PartitionSpec as P

EPS = 1e-06
BASE = 10000.0
NEG_LARGE = -1e30
LOW = jnp.bfloat16
F32 = jnp.float32
ORDER = (0, 2, 1, 3)
CORE = [(i, i ^ 1) for i in range(4)]
CROSS = [(i, i ^ 2) for i in range(4)]


def inverse_rms(values):
    return lax.rsqrt(jnp.mean(values * values, axis=-1, keepdims=True) + EPS)


def norm_backward(grad_hat, normed, inverse):
    return inverse * (grad_hat - normed * jnp.mean(grad_hat * normed, axis=-1, keepdims=True))


def dot(left, right):
    return jnp.dot(left, right, preferred_element_type=F32)


def inner_rows(left, right):
    return lax.dot_general(left, right, (((0,), (0,)), ((), ())), preferred_element_type=F32)


def inner_cols(left, right):
    return lax.dot_general(left, right, (((1,), (1,)), ((), ())), preferred_element_type=F32)


def documents(lengths_row, rows):
    first_end = lengths_row[0]
    second_end = first_end + lengths_row[1]
    doc_ids = (rows >= first_end).astype(jnp.int32) + (rows >= second_end).astype(jnp.int32)
    starts = jnp.where(rows >= second_end, second_end, jnp.where(rows >= first_end, first_end, 0))
    return (doc_ids, rows - starts)


def rotation(positions, head_dim):
    half = head_dim // 2
    freqs = BASE ** (-2.0 * jnp.arange(half, dtype=F32) / head_dim)
    angles = positions.astype(F32)[:, None] * freqs[None, :]
    return (jnp.cos(angles), jnp.sin(angles))


def rotate(values, cosine, sine):
    half = values.shape[-1] // 2
    first = values[..., :half]
    second = values[..., half:]
    return jnp.concatenate(
        [first * cosine - second * sine, second * cosine + first * sine], axis=-1
    )


def unrotate(grads, cosine, sine):
    return rotate(grads, cosine, -sine)


def in_vmem():
    return pl.BlockSpec(memory_space=pltpu.VMEM)


def whole(shape, dtype):
    return jax.ShapeDtypeStruct(shape, dtype)


def run(body, ids, args, outs, after=(), scratch=(), name=None, limit=40):
    args, after = list(args), list(after)

    def without(*refs):
        body(*refs[: 1 + len(args)], *refs[1 + len(args) + len(after) :])

    return pl.pallas_call(
        without,
        grid_spec=pltpu.PrefetchScalarGridSpec(
            num_scalar_prefetch=1,
            grid=(1,),
            in_specs=[in_vmem()] * len(args) + [pl.BlockSpec(memory_space=pl.ANY)] * len(after),
            out_specs=[in_vmem()] * len(outs),
            scratch_shapes=list(scratch),
        ),
        out_shape=list(outs),
        cost_estimate=pl.CostEstimate(flops=1000, bytes_accessed=1000, transcendentals=0),
        compiler_params=pltpu.CompilerParams(vmem_limit_bytes=limit << 20),
        name=name,
    )(ids, *args, *after)


def side_columns(source, mine, theirs, side):
    line, _, wide = mine.shape
    rows = theirs.shape[1]
    for z in range(line):
        mine[z] = source[:, pl.ds(pl.multiple_of((2 * z + side) * wide, wide), wide)]
        theirs[z] = source[:rows, pl.ds(pl.multiple_of((2 * z + 1 - side) * wide, wide), wide)]


def first_body(m, quarter, ids, x_ref, gain, q_down, kv_proj, cos, sin, c, kv, h1, mine, theirs):
    blocks = [
        x_ref[m, pl.ds(pl.multiple_of((ids[0] ^ k) * quarter, quarter), quarter), :] for k in ORDER
    ]
    x = jnp.concatenate(blocks, 0).astype(F32)
    low = (x * inverse_rms(x) * gain[...]).astype(LOW)
    h1[...] = low
    half = 2 * quarter
    pair = dot(low[:half], kv_proj[...])
    wide = kv_proj.shape[1] // 2
    kv[:, :wide] = rotate(pair[:, :wide], cos[:half], sin[:half]).astype(LOW)
    kv[:, wide:] = pair[:, wide:].astype(LOW)
    c[...] = dot(low, q_down[...]).astype(LOW)
    if mine is not None:
        side_columns(h1, mine, theirs, ids[1])


def cotangent_body(micro, quarter, ids, z_ref, w_down, dhid, dz, *sides):
    for m in range(micro):
        blocks = [
            z_ref[m, pl.ds(pl.multiple_of((ids[0] ^ k) * quarter, quarter), quarter), :]
            for k in ORDER
        ]
        dz[m] = jnp.concatenate(blocks, 0)
        if sides:
            side_columns(dz.at[m], sides[0].at[m], sides[1].at[m], ids[1])
        dhid[m] = inner_cols(dz[m], w_down[...])


def attend_body(
    scale, ids, c0, c1, c2, gain, q_up, cos, sin, kv, key_ids, row_ids, row_starts, out_proj,
    qn, q, o, lse, send, keep, mine, theirs,
):
    rows = qn.shape[0]
    quarter = rows // 4
    part = c0.shape[1]
    wide = q.shape[2]
    got = c1[...]
    pair = jnp.concatenate(
        [got[quarter : 2 * quarter], got[:quarter], got[3 * quarter :], got[2 * quarter : 3 * quarter]],
        0,
    )
    far = jnp.concatenate([c2[2 * quarter :], c2[: 2 * quarter]], 0)
    c = jnp.concatenate([c0[...], pair, far], 1).astype(F32)
    chat = c * inverse_rms(c)
    for k, xor in enumerate(ORDER):
        columns = pl.ds(pl.multiple_of((ids[0] ^ xor) * part, part), part)
        qn[:, columns] = (chat[:, k * part : (k + 1) * part] * gain[:, columns]).astype(LOW)
    if mine is not None:
        side_columns(qn, mine, theirs, ids[1])
    bias = jnp.where(
        (key_ids[...] >= row_starts[...]) & (key_ids[...] <= row_ids[...]), 0.0, NEG_LARGE
    )
    low = qn[...]
    keys, values = kv[:, :wide], kv[:, wide:]
    for h in range(q.shape[0]):
        pre = dot(low, q_up[:, h * wide : (h + 1) * wide])
        q_h = (rotate(pre, cos[...], sin[...]) * scale).astype(LOW)
        q[h] = q_h
        scores = inner_cols(q_h, keys) + bias
        top = jnp.max(scores, axis=-1, keepdims=True)
        probs = jnp.exp(scores - top)
        total = jnp.sum(probs, axis=-1, keepdims=True)
        out = dot(probs.astype(LOW), values) / total
        o[:, h * wide : (h + 1) * wide] = out.astype(LOW)
        log_total = jnp.broadcast_to(top + jnp.log(total), (rows, 128))
        lse[h : h + 1, :] = jnp.transpose(log_total)[:1]
    half = 2 * quarter
    send[...] = dot(o[half:, :], out_proj[...]).astype(LOW)
    keep[...] = dot(o[:half, :], out_proj[...])


def forward_body(m, ids, a0, a1, a2, w_gate, w_up, dhid, h2, hid, dg, du, mine, theirs):
    h2[...] = jnp.concatenate([a0[...], a1[...], a2[...]], 0)
    if mine is not None:
        side_columns(h2, mine, theirs, ids[1])
    low = h2[...]
    g = dot(low, w_gate[...])
    u = dot(low, w_up[...])
    sig = jax.nn.sigmoid(g)
    swish = g * sig
    hid[...] = (swish * u).astype(LOW)
    back = dhid[m]
    dg[...] = (back * u * sig * (1.0 + g * (1.0 - sig))).astype(LOW)
    du[...] = (back * swish).astype(LOW)


def hidden_back_body(micro, ids, *refs):
    dgs, dus = refs[:micro], refs[micro : 2 * micro]
    hids = refs[2 * micro : 3 * micro]
    w_gate, w_up, w_down, send, keep, out_send, out_keep = refs[3 * micro :]
    half = send.shape[1]
    every = lambda parts: jnp.concatenate([part[...] for part in parts], 0)
    rows = 2 * half
    total = inner_cols(every(dgs), w_gate[...]) + inner_cols(every(dus), w_up[...])
    for m in range(micro):
        send[m] = total[m * rows + half : (m + 1) * rows].astype(LOW)
        keep[m] = total[m * rows : m * rows + half]
    total = dot(every(hids), w_down[...])
    for m in range(micro):
        out_send[m] = total[m * rows + half : (m + 1) * rows].astype(LOW)
        out_keep[m] = total[m * rows : m * rows + half]


def pick(ref, lead):
    return ref if lead is None else ref.at[lead]


def block_body(terms, lefts, rights, extra, from_side, turned, ids, *refs):
    left, refs = refs[:lefts], refs[lefts:]
    right, refs = refs[:rights], refs[rights:]
    added, out = refs[: extra + from_side], refs[-1]
    total = None
    for a, a_lead, b, b_lead, first, count in terms:
        rows = pick(right[b], b_lead)[first : first + count, :]
        term = inner_rows(pick(left[a], a_lead)[ids[0]], rows)
        total = term if total is None else total + term
    for i, ref in enumerate(added):
        total = total + (ref[ids[0]] if i >= extra else ref[...]).astype(F32)
    out[...] = jnp.transpose(total) if turned else total.astype(out.dtype)


def side_sum_body(terms, lefts, ids, *refs):
    left, right, out = refs[:lefts], refs[lefts:-1], refs[-1]
    for z in range(out.shape[0]):
        total = None
        for a, a_lead, b, b_lead, first, count in terms:
            rows = pick(right[b], b_lead)[first : first + count, :]
            term = inner_rows(pick(left[a], a_lead)[z], rows)
            total = term if total is None else total + term
        out[z] = total.astype(out.dtype)


def attend_back_body(
    scale, micro, chunk, ids, a0, a1, a2, out_proj, q_up, key_ids, *refs
):
    per = 7
    groups = [refs[m * per : (m + 1) * per] for m in range(micro)]
    dyl_out, dqp, send, keep, kv_send, kv_keep = refs[micro * per : micro * per + 6]
    dq_acc, do_acc, delta_acc = refs[-3:]
    sides = refs[micro * per + 6 : -3]
    for m in range(micro):
        q, kv, o, lse, row_ids, cos, sin = groups[m]
        heads, rows, wide = q.shape
        half_rows = rows // 2
        dyl = jnp.concatenate([a0[m], a1[m], a2[m]], 0)
        dyl_out[m] = dyl
        if sides:
            side_columns(dyl_out.at[m], sides[0].at[m], sides[1].at[m], ids[1])
        for h in range(heads):
            do = inner_cols(dyl, out_proj[h * wide : (h + 1) * wide, :]).astype(LOW)
            do_acc[h] = do
            delta = jnp.sum(
                do.astype(F32) * o[:, h * wide : (h + 1) * wide].astype(F32), axis=-1, keepdims=True
            )
            delta_acc[h] = jnp.transpose(jnp.broadcast_to(delta, (rows, 128)))[:8]
            dq_acc[h] = jnp.zeros((rows, wide), F32)
        count = kv.shape[0] // 2 // chunk
        for part, out in ((0, kv_keep), (1, kv_send)):

            def one(i, carry):
                base = pl.multiple_of((part * count + i) * chunk, chunk)
                keys = kv[pl.ds(base, chunk), :wide]
                values = kv[pl.ds(base, chunk), wide:]
                at = key_ids[pl.ds(base, chunk), :]
                bias = jnp.where((at >= row_ids[1:2, :]) & (at <= row_ids[0:1, :]), 0.0, NEG_LARGE)

                def head(h, sums):
                    dk, dv = sums
                    q_h, do_h = q[h], do_acc[h]
                    probs = jnp.exp(inner_cols(keys, q_h) + bias - lse[pl.ds(h, 1), :])
                    back = inner_cols(values, do_h) - delta_acc[h][:1]
                    ds = (probs * back).astype(LOW)
                    dv = dv + dot(probs.astype(LOW), do_h)
                    dk = dk + dot(ds, q_h)
                    dq_acc[h] = dq_acc[h] + inner_rows(ds, keys)
                    return dk, dv

                zero = jnp.zeros((chunk, wide), F32)
                dk, dv = lax.fori_loop(0, heads, head, (zero, zero))
                place = pl.ds(pl.multiple_of(i * chunk, chunk), chunk)
                out[m, place, :wide] = dk.astype(out.dtype)
                out[m, place, wide:] = dv.astype(out.dtype)
                return carry

            if count == 1:
                one(0, 0)
            else:
                lax.fori_loop(0, count, one, 0)
        for h in range(heads):
            dq = unrotate(dq_acc[h] * scale, cos[...], sin[...])
            dqp[m, :, h * wide : (h + 1) * wide] = dq.astype(LOW)
        low = dqp[m]
        send[m] = inner_cols(low[half_rows:], q_up[...]).astype(LOW)
        keep[m] = inner_cols(low[:half_rows], q_up[...])


def natural_body(micro, quarter, ids, a0, a1, a2, out):
    for m in range(micro):
        pieces = (a0[m], a1[m], a2[m, :quarter, :], a2[m, quarter:, :])
        for k, piece in zip(ORDER, pieces):
            out[m, pl.ds(pl.multiple_of((ids[0] ^ k) * quarter, quarter), quarter), :] = piece


class Wire:
    def __init__(self, sends, recvs):
        self.sends, self.recvs, self.used = sends, recvs, 0
        self.seq, self.mp = lax.axis_index("seq"), lax.axis_index("mp")
        self.place, self.side = self.seq // 2, self.seq % 2
        core, cross = self.mp % 2, self.mp // 2
        self.blocks = (
            self.mp, 2 * (1 - cross) + core, 2 * cross + 1 - core, 2 * (1 - cross) + 1 - core
        )
        self.core, self.cross = {"mp": self.blocks[2]}, {"mp": self.blocks[1]}
        self.beside = {"seq": self.seq + 1 - 2 * self.side}
        self.up, self.down = {"seq": self.seq + 2}, {"seq": self.seq - 2}

    def copy(self, source, target, device):
        at = self.used
        self.used += 1
        return pltpu.make_async_remote_copy(
            src_ref=source, dst_ref=target, send_sem=self.sends.at[at], recv_sem=self.recvs.at[at],
            device_id=device, device_id_type=pl.DeviceIdType.MESH,
        )

    def send(self, source, target, device):
        made = self.copy(source, target, device)
        made.start()
        return made

    def greet(self, line, far=1, diagonal=False):
        barrier = pltpu.get_barrier_semaphore()
        devices = [self.core, self.cross, self.beside]
        if diagonal:
            devices.append({"mp": self.blocks[3]})
        for device in devices:
            pl.semaphore_signal(barrier, 1, device_id=device, device_id_type=pl.DeviceIdType.MESH)
        for d in range(1, far + 1):
            for way, there in ((1, self.place < line - d), (-1, self.place >= d)):

                @pl.when(there)
                def _():
                    pl.semaphore_signal(
                        barrier, 1, device_id={"seq": self.seq + 2 * way * d},
                        device_id_type=pl.DeviceIdType.MESH,
                    )
        below, above = jnp.minimum(self.place, far), jnp.minimum(line - 1 - self.place, far)
        pl.semaphore_wait(barrier, len(devices) + below + above)


def along(pieces, axis):
    return pieces[0] if len(pieces) == 1 else jnp.concatenate(pieces, axis)


def pair_places(first, second, quarter, axis):
    shape = (2 * quarter, 1) if axis == 0 else (1, 2 * quarter)
    index = lax.broadcasted_iota(jnp.int32, shape, axis)
    return jnp.where(index < quarter, first * quarter + index, (second - 1) * quarter + index)


def row_places(wire, quarter, axis):
    b = wire.blocks
    pieces = [pair_places(b[i], b[i + 1], quarter, axis) for i in (0, 2)]
    return wire.seq * (4 * quarter) + along(pieces, axis)


def key_places(wire, quarter, line, axis, cores):
    pieces = []
    for core in cores:
        for side in (wire.side, 1 - wire.side):
            for d in range(line):
                base = ((wire.place - d) * 2 + side) * (4 * quarter)
                b = wire.blocks[2 * core : 2 * core + 2]
                pieces.append(base + pair_places(b[0], b[1], quarter, axis))
    return along(pieces, axis)


def sequence_starts(lengths, m, places):
    first_end = lengths[m, 0]
    second_end = first_end + lengths[m, 1]
    return jnp.where(
        places >= second_end, second_end, jnp.where(places >= first_end, first_end, 0)
    )


class LineSum:
    def __init__(self, wire, term, room, rows, columns, keep):
        got, out = room
        view = lambda ref, i: ref.at[i, :rows, :columns]
        self.place, self.term, self.keep = wire.place, term, keep
        self.got = [view(got, i) for i in range(5)]
        self.out = [view(out, i) for i in range(2)]
        one, two_up, two_down, three_up, three_down = self.got
        a, b = self.out
        self.one = wire.copy(a, one, wire.up), wire.copy(a, one, wire.down)
        self.two = wire.copy(b, two_up, wire.up), wire.copy(b, two_down, wire.down)
        self.three = wire.copy(a, three_up, wire.up), wire.copy(b, three_down, wire.down)

    def clear(self):
        place = self.place
        for ref, empty in zip(
            self.got, ((place == 0) | (place == 3),) * 3 + (place == 0, place == 3)
        ):

            @pl.when(empty)
            def _(ref=ref):
                ref[...] = jnp.zeros(ref.shape, ref.dtype)

    def step1(self):
        place = self.place

        @pl.when((place == 0) | (place == 3))
        def _():
            self.out[0][...] = self.term(3 - place).astype(LOW)

        pl.when(place == 0)(self.one[0].start)
        pl.when(place == 3)(self.one[1].start)

    def step2(self):
        place = self.place
        pl.when(place == 1)(self.one[0].wait_recv)
        pl.when(place == 2)(self.one[1].wait_recv)
        self.out[1][...] = (
            self.term((place + 2) % 4) + self.got[0][...].astype(F32)
        ).astype(LOW)
        pl.when(place <= 1)(self.two[0].start)
        pl.when(place >= 2)(self.two[1].start)

    def step3(self):
        place = self.place

        @pl.when((place == 1) | (place == 2))
        def _():
            self.two[0].wait_recv()
            self.two[1].wait_recv()

        pl.when(place == 0)(self.one[0].wait_send)
        pl.when(place == 3)(self.one[1].wait_send)

        @pl.when(place <= 2)
        def _():
            self.out[0][...] = (self.term(place + 1) + self.got[1][...].astype(F32)).astype(LOW)
            self.three[0].start()

        pl.when(place <= 1)(self.two[0].wait_send)
        pl.when(place >= 2)(self.two[1].wait_send)

        @pl.when(place >= 1)
        def _():
            self.out[1][...] = (self.term(place - 1) + self.got[2][...].astype(F32)).astype(LOW)
            self.three[1].start()

    def finish(self):
        place = self.place
        pl.when(place >= 1)(self.three[0].wait_recv)
        pl.when(place <= 2)(self.three[1].wait_recv)
        self.keep(
            self.term(place) + self.got[3][...].astype(F32) + self.got[4][...].astype(F32)
        )

    def settle(self):
        place = self.place
        pl.when(place <= 2)(self.three[0].wait_send)
        pl.when(place >= 1)(self.three[1].wait_send)


class Desk:
    def __init__(self, first, loads, stores):
        self.loads, self.stores, self.stored = loads, stores, []
        for _, made in first:
            made.start()
        self.waiting = list(first)

    def more(self):
        for _, made in self.loads:
            made.start()
        self.waiting += self.loads

    def arrive(self, *refs):
        rest = []
        for ref, made in self.waiting:
            if not refs or any(ref is other for other in refs):
                made.wait()
            else:
                rest.append((ref, made))
        self.waiting = rest

    def flush(self, *refs):
        rest = []
        for ref, made in self.stores:
            if not refs or any(ref is other for other in refs):
                made.start()
                self.stored.append(made)
            else:
                rest.append((ref, made))
        self.stores = rest

    def close(self):
        self.flush()
        for made in self.stored:
            made.wait()


SPACES = (pl.ANY, pltpu.VMEM, pltpu.SMEM, pl.ANY, pl.ANY)


def mesh_run(body, args, outs, scratch, number, name, limit, sends):
    late_in = [i for i, (kind, _) in enumerate(args) if kind >= 3]
    late_out = [i for i, (kind, _) in enumerate(outs) if kind == 3]

    def whole_body(*refs):
        refs = list(refs)
        take = lambda n: [refs.pop(0) for _ in range(n)]
        given, results, rooms_in, rooms_out = (
            take(len(args)), take(len(outs)), take(len(late_in)), take(len(late_out))
        )
        load_sems, store_sems = take(2)
        first, loads, stores = [], [], []
        for n, (i, room) in enumerate(zip(late_in, rooms_in)):
            made = pltpu.make_async_copy(given[i], room, load_sems.at[n])
            (first if args[i][0] == 3 else loads).append((room, made))
            given[i] = room
        for n, (i, room) in enumerate(zip(late_out, rooms_out)):
            stores.append((room, pltpu.make_async_copy(room, results[i], store_sems.at[n])))
            results[i] = room
        desk = Desk(first, loads, stores)
        body(desk, *given, *results, *refs)
        desk.close()

    room = lambda a: pltpu.VMEM(a.shape, a.dtype)
    return pl.pallas_call(
        whole_body,
        in_specs=[pl.BlockSpec(memory_space=SPACES[kind]) for kind, _ in args],
        out_specs=[pl.BlockSpec(memory_space=SPACES[kind]) for kind, _ in outs],
        out_shape=[shape for _, shape in outs],
        scratch_shapes=[
            *[room(args[i][1]) for i in late_in], *[room(outs[i][1]) for i in late_out],
            pltpu.SemaphoreType.DMA((max(1, len(late_in)),)),
            pltpu.SemaphoreType.DMA((max(1, len(late_out)),)),
            *scratch, pltpu.SemaphoreType.DMA((sends,)), pltpu.SemaphoreType.DMA((sends,)),
        ],
        cost_estimate=pl.CostEstimate(flops=1000, bytes_accessed=1000, transcendentals=0),
        compiler_params=pltpu.CompilerParams(
            collective_id=number, has_side_effects=True, vmem_limit_bytes=limit << 20
        ),
        name=name,
    )(*[array for _, array in args])


def attend_back_one(
    scale, keys_at, rows_at, starts, dyl, out_proj, q_up, q, kv, o, lse, cos, sin,
    dqp, send, keep, kv_send, kv_keep, dq_acc, between=None,
):
    heads, rows, wide = q.shape
    half_rows = rows // 2
    low = dyl[...]
    grads, deltas = [], []
    for h in range(heads):
        columns = slice(h * wide, (h + 1) * wide)
        do = inner_cols(low, out_proj[columns, :]).astype(LOW)
        grads.append(do)
        delta = jnp.sum(do.astype(F32) * o[:, columns].astype(F32), axis=-1, keepdims=True)
        deltas.append(jnp.transpose(jnp.broadcast_to(delta, (rows, 128)))[:1])
    do_all, delta_all = jnp.concatenate(grads, 0), jnp.concatenate(deltas, 1)
    q_all = q[...].reshape(heads * rows, wide)
    lse_all = jnp.concatenate([lse[h : h + 1, :] for h in range(heads)], 1)
    dq_acc[...] = jnp.zeros(dq_acc.shape, F32)
    count = kv.shape[0] // 2
    chunk = min(256, count)
    for part, out in ((1, kv_send), (0, kv_keep)):
        for first in range(0, count, chunk):
            span = slice(part * count + first, part * count + first + chunk)
            keys, values = kv[span, :wide], kv[span, wide:]
            at = keys_at[part][first : first + chunk]
            bias = jnp.where((at >= starts) & (at <= rows_at), 0.0, NEG_LARGE)
            scores = inner_cols(keys, q_all) + jnp.concatenate([bias] * heads, 1)
            probs = jnp.exp(scores - lse_all)
            ds = (probs * (inner_cols(values, do_all) - delta_all)).astype(LOW)
            spot = slice(first, first + chunk)
            out[spot, :wide] = dot(ds, q_all).astype(out.dtype)
            out[spot, wide:] = dot(probs.astype(LOW), do_all).astype(out.dtype)
            dq_acc[...] += inner_rows(ds, keys)
        if part and between is not None:
            between()
    for h in range(heads):
        dq = unrotate(dq_acc[h * rows : (h + 1) * rows, :] * scale, cos, sin)
        dqp[:, h * wide : (h + 1) * wide] = dq.astype(LOW)
    total = inner_cols(dqp[...], q_up[...])
    send[...] = total[half_rows:].astype(LOW)
    keep[...] = total[:half_rows]


def mean_of(values):
    return jnp.mean(values, axis=-1, keepdims=True)


def terms_sum(pairs):
    total = None
    for left, right in pairs:
        term = inner_rows(left, right)
        total = term if total is None else total + term
    return total


def back1_body(quarter, desk, *refs):
    refs = list(refs)
    take = lambda n: [refs.pop(0) for _ in range(n)]
    w_gate, w_up, w_down, cotangent, h2, dhid, n2, inv2, gain2, dz_got, dz_far, y = take(12)
    grad, dy, gain_sum, dyl, dyl_mine, dyl_theirs, layer_own = take(7)
    hid, dg, du, h2_mine = (take(2) for _ in range(4))
    h2_got, h2_far, dg_other = take(2), take(2), take(2)
    gate_w, up_w, hid_other0, hid_other1, h2_theirs, got, out = take(7)
    send, kept, core_got, cross_out, cross_got, loads = take(6)
    ffn_send, ffn_kept, ffn_got, ffn_out, ffn_back = take(5)
    early_got, early_out, early_sum, early_send, early_back, dz, row_loads = take(7)
    wire = Wire(*take(2))
    half, rows = 2 * quarter, 4 * quarter
    ahead = early_send.shape[1]
    block = early_send.shape[0]
    middle = ahead + (gate_w.shape[1] - ahead) // 2
    columns_of = [slice(0, ahead), slice(ahead, middle), slice(middle, gate_w.shape[1])]
    in_weights = []
    for i, columns in enumerate(columns_of):
        for j, (source, target) in enumerate(((w_gate, gate_w), (w_up, up_w))):
            in_weights.append(pltpu.make_async_copy(
                source.at[:, columns], target.at[:, columns], loads.at[2 * i + j]
            ))
    for made in in_weights[:2]:
        made.start()
    hid_other = (hid_other0, hid_other1)
    hid_all = (*(a.at[:, ahead:] for a in hid), *hid_other)

    def term(z):
        columns = pl.ds(pl.multiple_of((2 * z + wire.side) * block, block), block)
        return terms_sum(halves_terms(
            [dz[m, :, columns] for m in range(2)], [dz_got[m, z] for m in range(2)],
            [dz_far[m, z] for m in range(2)], hid_all, half))

    def early_term(z):
        columns = pl.ds(pl.multiple_of(z * 2 * block, 2 * block), 2 * block)
        return terms_sum([(dz[m, :, columns], hid[m][:, :ahead]) for m in range(2)])

    def keep(total):
        grad[ahead:, :] = jnp.transpose(total)

    def early_keep(total):
        early_sum[0], early_sum[1] = total[:block], total[block:]

    chain = LineSum(wire, term, (got, out), block, grad.shape[0] - ahead, keep)
    early = LineSum(wire, early_term, (early_got, early_out), 2 * block, ahead, early_keep)
    chain.clear()
    early.clear()
    wire.greet(4)
    desk.arrive(h2)
    for made in in_weights[2:]:
        made.start()
    desk.more()
    in_dz = []
    for m in range(2):
        for k in range(4):
            at = pl.ds(pl.multiple_of(wire.blocks[k] * quarter, quarter), quarter)
            in_dz.append(pltpu.make_async_copy(
                cotangent.at[m, at, :], dz.at[m, k * quarter : (k + 1) * quarter, :],
                row_loads.at[4 * m + k],
            ))
            in_dz[-1].start()
    for m in range(2):
        side_columns(h2.at[m], h2_mine[m], h2_theirs.at[m], wire.side)
    y_h2 = [wire.send(h2_theirs.at[m], h2_got[m], wire.beside) for m in range(2)]
    y_hid = []

    def columns_forward(m, i):
        columns = columns_of[i]
        if m == 0:
            for made in in_weights[2 * i : 2 * i + 2]:
                made.wait()
        g = dot(h2[m], gate_w[:, columns])
        u = dot(h2[m], up_w[:, columns])
        sig = jax.nn.sigmoid(g)
        swish = g * sig
        hid[m][:, columns] = (swish * u).astype(LOW)
        if i:
            there = hid_other[m].at[:, columns.start - ahead : columns.stop - ahead]
            y_hid.append(wire.send(hid[m].at[:, columns], there, wire.beside))
        if m == 0 and i == 0:
            desk.arrive()
        back = dhid[m, :, columns]
        dg[m][:, columns] = (back * u * sig * (1.0 + g * (1.0 - sig))).astype(LOW)
        du[m][:, columns] = (back * swish).astype(LOW)

    for m in range(2):
        columns_forward(m, 0)
    for made in in_dz:
        made.wait()
    early.step1()
    for m in range(2):
        columns_forward(m, 1)
        if m == 1:
            early.step2()
        columns_forward(m, 2)
        desk.flush(dg[m], du[m], hid[m], h2_mine[m])
    both = lambda pair: jnp.concatenate([pair[0][...], pair[1][...]], 0)
    total = inner_cols(both(dg), gate_w[...]) + inner_cols(both(du), up_w[...])
    for m in range(2):
        send[m] = total[m * rows + half : (m + 1) * rows].astype(LOW)
        kept[m] = total[m * rows : m * rows + half]
    sums = RowSum(wire, send, kept, core_got, cross_out, cross_got, quarter)
    sums.core.start()
    wide = gate_w.shape[1]
    rest = w_down.shape[1] - wide
    downs = [gate_w.at[:wide, :], up_w.at[:wide, :rest]]
    in_down = [
        pltpu.make_async_copy(w_down.at[:, :wide], downs[0], loads.at[0]),
        pltpu.make_async_copy(w_down.at[:, wide:], downs[1], loads.at[1]),
    ]
    for made in in_down:
        made.start()
    early.step3()
    sums.pass_on()
    for made in y_hid:
        made.wait_recv()
    y_next = y_h2 + [wire.send(dg[m], dg_other[m], wire.beside) for m in range(2)]
    chain.step1()
    for made in in_down:
        made.wait()
    low = both(hid)
    ffn_sum = RowSum(wire, ffn_send, ffn_kept, ffn_got, ffn_out, ffn_back, quarter)
    for columns, part in ((slice(0, wide), downs[0]), (slice(wide, None), downs[1])):
        total = dot(low, part[...])
        for m in range(2):
            ffn_send[m, :, columns] = total[m * rows + half : (m + 1) * rows].astype(LOW)
            ffn_kept[m, :, columns] = total[m * rows : m * rows + half].astype(LOW)
    ffn_sum.core.start()
    early.finish()
    early_send[...] = early_sum[1 - wire.side].astype(LOW)
    y_early = wire.send(early_send, early_back, wire.beside)
    dh2 = sums.result()
    gain_sum[...] = jnp.sum(jnp.sum(dh2 * n2[...], axis=0), axis=0, keepdims=True)
    back = dh2 * gain2[...]
    grad_y = dz[:, :quarter, :].astype(F32) + inv2[...] * (
        back - n2[...] * mean_of(back * n2[...])
    )
    dy[...] = grad_y
    dyl[:, :quarter, :] = grad_y.astype(LOW)
    cross_dyl = wire.send(dyl.at[:, :quarter, :], dyl.at[:, quarter:half, :], wire.cross)
    ffn_sum.pass_on()
    chain.step2()
    cross_dyl.wait_recv()
    core_dyl = wire.send(dyl.at[:, :half, :], dyl.at[:, half:, :], wire.core)
    core_h2 = []
    for i in range(2):
        y_next[i].wait_recv()
        core_h2.append(wire.send(h2_got[i], h2_far[i], wire.core))
    core_dyl.wait_recv()
    for m in range(2):
        side_columns(dyl.at[m], dyl_mine.at[m], dyl_theirs.at[m], wire.side)
    desk.flush(dy, dyl, dyl_mine, dyl_theirs)
    chain.step3()
    layer_own[...] = (y[...] + ffn_sum.result()).astype(LOW)
    y_early.wait_recv()
    grad[:ahead, :] = jnp.transpose(early_sum[wire.side] + early_back[...].astype(F32))
    for made in y_next[2:] + core_h2:
        made.wait_recv()
    chain.finish()
    for made in [*y_hid, cross_dyl, core_dyl, *y_next, *core_h2, y_early]:
        made.wait_send()
    sums.end()
    ffn_sum.end()
    early.settle()
    chain.settle()


class Share:
    def __init__(self, wire, out, quarter):
        spot = lambda block: out.at[:, pl.ds(pl.multiple_of(block * quarter, quarter), quarter), :]
        own, near = spot(wire.blocks[0]), spot(wire.blocks[1])
        self.own = own
        self.first = wire.copy(own, own, wire.cross)
        self.rest = wire.copy(own, own, wire.core), wire.copy(near, near, wire.core)

    def begin(self, value):
        self.own[...] = value
        self.first.start()
        self.rest[0].start()

    def forward(self):
        self.first.wait_recv()
        self.rest[1].start()

    def end(self):
        for made in self.rest:
            made.wait_recv()
        for made in (self.first, *self.rest):
            made.wait_send()


class RowSum:
    def __init__(self, wire, send, kept, got, cross_out, cross_got, quarter, parts=1):
        self.kept, self.got, self.quarter = kept, got, quarter
        self.out, self.back = cross_out, cross_got
        self.core = wire.copy(send, got, wire.core)
        size = quarter // parts
        self.spans = [slice(i * size, (i + 1) * size) for i in range(parts)]
        self.cross = [
            wire.copy(cross_out.at[:, span, :], cross_got.at[:, span, :], wire.cross)
            for span in self.spans
        ]

    def pass_on(self):
        self.core.wait_recv()
        for span, made in zip(self.spans, self.cross):
            rest = slice(self.quarter + span.start, self.quarter + span.stop)
            self.out[:, span, :] = (
                self.kept[:, rest, :] + self.got[:, rest, :].astype(F32)
            ).astype(LOW)
            made.start()

    def result(self, part=0):
        span = self.spans[part]
        self.cross[part].wait_recv()
        return (
            self.kept[:, span, :] + self.got[:, span, :].astype(F32)
            + self.back[:, span, :].astype(F32)
        )

    def end(self):
        self.core.wait_send()
        for made in self.cross:
            made.wait_send()


def halves_terms(mine, got, far, rights, half):
    pairs = [(mine[m], rights[m][...]) for m in range(2)]
    for m in range(2):
        pairs.append((got[m], rights[2 + m][:half, :]))
        pairs.append((far[m], rights[2 + m][half:, :]))
    return pairs


def back2_body(quarter, scale, desk, *refs):
    refs = list(refs)
    take = lambda n: [refs.pop(0) for _ in range(n)]
    (lengths,) = take(1)
    dg, dg_other, du, h2_mine, h2_got, h2_far = (take(2) for _ in range(6))
    dyl, out_proj, q_up = take(3)
    q, kv, o, lse = (take(2) for _ in range(4))
    cos, sin, chat, inv_c, gain_c, dyl_theirs = take(6)
    qn_theirs, os_far = take(2), take(2)
    grad_gate, grad_up, dfirst, gain_sum, dqp, dyl_got, dyl_far, qup_side = take(8)
    oo = take(2)
    du_other = take(2)
    got_a, out_a, got_b, out_b = take(4)
    dq_acc, dqn_send, dqn_keep, kv_send, kv_keep = take(5)
    dqn_got, dqn_out, dqn_back = take(3)
    kv_got, kv_out, kv_back, side_out, side_got, line_out, line_got, kv_own = take(8)
    both, side_sums = take(2)
    wire = Wire(*take(2))
    half, rows = 2 * quarter, 4 * quarter
    wide = kv_own.shape[2] // 2
    rank = chat.shape[2]
    place = wire.place

    y_du = [wire.copy(du[m], du_other[m], wire.beside) for m in range(2)]

    def chain(rights, grad, room):
        def term(z):
            return terms_sum(halves_terms(
                [a[z] for a in h2_mine], [a[z] for a in h2_got], [a[z] for a in h2_far], rights,
                half))

        def keep(total):
            grad[...] = total

        made = LineSum(wire, term, room, *grad.shape, keep)
        made.clear()
        return made

    gate = chain((*dg, *dg_other), grad_gate, (got_a, out_a))
    up = chain((*du, *du_other), grad_up, (got_b, out_b))
    dqn_sum, core_kv, cross_kv, side_kv, line_kv = [], [], [], [], []
    for m in range(2):
        one = lambda ref: ref.at[m : m + 1]
        dqn_sum.append(RowSum(wire, one(dqn_send), one(dqn_keep), one(dqn_got), one(dqn_out),
                              one(dqn_back), quarter))
        core_kv.append(wire.copy(kv_send.at[m], kv_got.at[m], wire.core))
        cross_kv.append(wire.copy(kv_out.at[m], kv_back.at[m], wire.cross))
        side_kv.append(wire.copy(side_out.at[m], side_got.at[m], wire.beside))
        line_kv.append([
            wire.copy(line_out.at[m, d - 1], line_got.at[m, d - 1], {"seq": wire.seq - 2 * d})
            for d in range(1, 4)
        ])
        for d in range(1, 4):

            @pl.when(place > 3 - d)
            def _(m=m, d=d):
                line_got[m, d - 1] = jnp.zeros(line_got.shape[2:], LOW)

    wire.greet(4, 3)
    desk.arrive(*du)
    for made in y_du:
        made.start()
    desk.arrive(*dg, *dg_other, *h2_mine, *h2_got, *h2_far)
    gate.step1()
    desk.arrive()

    def attend(m, between=None):
        rows_at = row_places(wire, quarter, 1)
        attend_back_one(
            scale, [key_places(wire, quarter, 4, 0, (core,)) for core in range(2)], rows_at,
            sequence_starts(lengths, m, rows_at), dyl.at[m], out_proj, q_up, q[m], kv[m], o[m],
            lse[m], cos[m], sin[m], dqp.at[m], dqn_send.at[m], dqn_keep.at[m], kv_send.at[m],
            kv_keep.at[m], dq_acc, between,
        )
        core_kv[m].start()
        dqn_sum[m].core.start()

    split = lambda ref, m: ref[m].reshape(8, 2, quarter, 2 * wide)

    def kv_cross(m):
        dqn_sum[m].pass_on()
        core_kv[m].wait_recv()
        kv_out[m] = (
            split(kv_keep, m)[:, 1].astype(F32) + split(kv_got, m)[:, 1].astype(F32)
        ).astype(LOW)
        cross_kv[m].start()

    def kv_sum(m, span):
        return (
            split(kv_keep, m)[span, 0].astype(F32) + split(kv_got, m)[span, 0].astype(F32)
            + kv_back[m, span].astype(F32)
        )

    def kv_side(m):
        cross_kv[m].wait_recv()
        side_out[m] = kv_sum(m, slice(4, 8)).astype(LOW)
        side_kv[m].start()

    def kv_line(m):
        side_kv[m].wait_recv()
        own = kv_sum(m, slice(0, 4)) + side_got[m].astype(F32)
        kv_own[m] = own[0]
        for d in range(1, 4):
            line_out[m, d - 1] = own[d].astype(LOW)
            pl.when(place >= d)(line_kv[m][d - 1].start)

    def latent(m):
        dqn = dqn_sum[m].result()[0]
        gain = jnp.sum(dqn * chat[m], axis=0, keepdims=True)
        gain_sum[...] = gain if m == 0 else gain_sum[...] + gain
        back = dqn * gain_c[...]
        both[m, :quarter, :rank] = (
            inv_c[m] * (back - chat[m] * mean_of(back * chat[m]))
        ).astype(LOW)

    y_late = []

    def start_up():
        for made in y_du:
            made.wait_recv()
        y_late.append(wire.send(dyl_theirs, dyl_got, wire.beside))
        y_late.extend(wire.send(os_far[m], oo[m], wire.beside) for m in range(2))
        up.step1()

    attend(0)
    kv_cross(0)
    gate.step2()
    attend(1, start_up)
    gate.step3()
    kv_cross(1)
    kv_side(0)
    latent(0)
    up.step2()
    latent(1)
    for z in range(4):
        side_sums[z] = terms_sum([(qn_theirs[m][z], dqp[m]) for m in range(2)]).astype(LOW)
    kv_side(1)
    side_qup = wire.send(side_sums, qup_side, wire.beside)
    side_dyl, *side_o = y_late
    desk.flush(dqp)
    kv_line(0)
    kv_line(1)
    gate.finish()
    desk.flush(grad_gate)
    for m in range(2):
        for d in range(1, 4):
            pl.when(place <= 3 - d)(line_kv[m][d - 1].wait_recv)
        total = kv_own[m]
        for d in range(1, 4):
            total = total + line_got[m, d - 1].astype(F32)
        both[m, :quarter, rank : rank + wide] = unrotate(
            total[:, :wide], cos[m, :quarter], sin[m, :quarter]
        ).astype(LOW)
        both[m, :quarter, rank + wide :] = total[:, wide:].astype(LOW)
    cross_both = wire.send(both.at[:, :quarter, :], both.at[:, quarter:half, :], wire.cross)
    up.step3()
    cross_both.wait_recv()
    core_both = wire.send(both.at[:, :half, :], both.at[:, half:, :], wire.core)
    side_dyl.wait_recv()
    core_dyl = wire.send(dyl_got, dyl_far, wire.core)
    core_both.wait_recv()
    part = rank // 4
    kv_part = wide // 2
    dfirst[:, :, :part] = both[:, :, pl.ds(pl.multiple_of(wire.mp * part, part), part)]
    dfirst[:, :, part:] = both[
        :, :, pl.ds(pl.multiple_of(rank + wire.mp * kv_part, kv_part), kv_part)
    ]
    up.finish()
    core_dyl.wait_recv()
    for made in (side_qup, *side_o):
        made.wait_recv()
    for made in [*y_du, *core_kv, *cross_kv, *side_kv, cross_both, core_both, side_dyl, core_dyl,
                 side_qup, *side_o]:
        made.wait_send()
    for m in range(2):
        dqn_sum[m].end()
        for d in range(1, 4):
            pl.when(place >= d)(line_kv[m][d - 1].wait_send)
    gate.settle()
    up.settle()


def back3_body(quarter, desk, *refs):
    refs = list(refs)
    take = lambda n: [refs.pop(0) for _ in range(n)]
    dfirst, q_down, kv_proj = take(3)
    h1_mine, h1_theirs, o, oo = (take(2) for _ in range(4))
    dyl_mine, dyl_got, dyl_far = take(3)
    qn_mine = take(2)
    dqp, qup_side, n1, inv1, dy, gain1, gain2_sum, gain_c_sum, layer_own = take(9)
    grad_out, grad_qup, grad_qdown, grad_kv, grad_tokens, gains, layer_out = take(7)
    got_a, out_a, got_b, out_b, got_c, out_c = take(6)
    side_sums, side_got = take(2)
    send, kept, row_got, row_out, row_back = take(5)
    kv_out, kv_got = take(2)
    sums, sums_core, sums_cross, sums_side, sums_line, weights, weight_loads = take(7)
    wire = Wire(*take(2))
    half, rows = 2 * quarter, 4 * quarter
    place = wire.place
    part, kv_part = grad_qdown.shape[1], kv_out.shape[1]
    wire.greet(4, 3, diagonal=True)


    def out_term(z):
        return terms_sum(halves_terms(
            [dyl_mine[m, z] for m in range(2)], [dyl_got[m, z] for m in range(2)],
            [dyl_far[m, z] for m in range(2)], (*o, *oo), half))

    def qup_term(z):
        return terms_sum([(qn_mine[m][z], dqp[m]) for m in range(2)]) + qup_side[z].astype(F32)

    def first_term(z):
        return terms_sum([(h1_mine[m][z], dfirst[m]) for m in range(2)]) + side_got[z].astype(F32)

    def keep_out(total):
        grad_out[...] = jnp.transpose(total)

    def keep_qup(total):
        grad_qup[...] = total

    def keep_first(total):
        grad_qdown[...] = total[:, :part]
        kv_out[...] = total[:, part:]

    out = LineSum(wire, out_term, (got_a, out_a), *grad_out.shape[::-1], keep_out)
    qup = LineSum(wire, qup_term, (got_b, out_b), *grad_qup.shape, keep_qup)
    first = LineSum(wire, first_term, (got_c, out_c), kv_out.shape[0], dfirst.shape[2], keep_first)
    for chain in (out, qup, first):
        chain.clear()
    row_sum = RowSum(wire, send, kept, row_got, row_out, row_back, quarter)
    desk.arrive()
    out.step1()
    desk.more()
    in_weights = [
        pltpu.make_async_copy(q_down, weights.at[:, :part], weight_loads.at[0]),
        pltpu.make_async_copy(
            kv_proj.at[:, pl.ds(pl.multiple_of(wire.mp * kv_part, kv_part), kv_part)],
            weights.at[:, part:], weight_loads.at[1],
        ),
    ]
    for made in in_weights:
        made.start()
    desk.arrive()
    for z in range(4):
        side_sums[z] = terms_sum([(h1_theirs[m][z], dfirst[m]) for m in range(2)]).astype(LOW)
    side_first = wire.send(side_sums, side_got, wire.beside)
    for made in in_weights:
        made.wait()
    term = inner_cols(dfirst[...].reshape(2 * rows, dfirst.shape[2]), weights[...])
    for m in range(2):
        send[m] = term[m * rows + half : (m + 1) * rows].astype(LOW)
        kept[m] = term[m * rows : m * rows + half]
    row_sum.core.start()
    qup.step1()
    row_sum.pass_on()
    layer_share = Share(wire, layer_out, quarter)
    layer_share.begin(layer_own[...])
    out.step2()
    side_first.wait_recv()
    first.step1()
    qup.step2()
    dh1 = row_sum.result()
    gain1_sum = jnp.sum(jnp.sum(dh1 * n1[...], axis=0), axis=0, keepdims=True)
    back = dh1 * gain1[...]
    share = Share(wire, grad_tokens, quarter)
    share.begin(
        (dy[...] + inv1[...] * (back - n1[...] * mean_of(back * n1[...]))).astype(LOW)
    )
    w, r = gain1_sum.shape[1] // 8, gain_c_sum.shape[1] // 8
    for s in range(8):
        sums[s] = jnp.concatenate(
            [gain1_sum[:, s * w : (s + 1) * w], gain2_sum[:, s * w : (s + 1) * w],
             gain_c_sum[:, s * r : (s + 1) * r]], axis=1
        )
    core_sums = wire.send(sums, sums_core, wire.core)
    out.step3()
    core_sums.wait_recv()
    core_sums.wait_send()
    sums[...] = sums[...] + sums_core[...]
    cross_sums = wire.send(sums, sums_cross, wire.cross)
    qup.step3()
    first.step2()
    cross_sums.wait_recv()
    cross_sums.wait_send()
    sums[...] = sums[...] + sums_cross[...]
    side_of = lambda p, s: sums.at[2 * p + s]
    side_sends = [
        wire.send(side_of(p, 1 - wire.side), sums_side.at[p], wire.beside) for p in range(4)
    ]
    layer_share.forward()
    share.forward()
    first.step3()
    for made in side_sends:
        made.wait_recv()
        made.wait_send()
    line_sends = []
    for d in range(1, 4):
        for way, there in ((1, place + d <= 3), (-1, place - d >= 0)):
            index = 2 * (d - 1) + (way < 0)
            line_sends.append(
                (wire.copy(sums_line.at[6 + index], sums_line.at[index],
                           {"seq": wire.seq + 2 * way * d}), d, way, there)
            )

            @pl.when(there)
            def _(index=index, d=d, way=way):
                to = place + way * d
                sums_line[6 + index] = sums[2 * to + wire.side] + sums_side[to]
                line_sends[-1][0].start()

            @pl.when((place - way * d < 0) | (place - way * d > 3))
            def _(index=index):
                sums_line[index] = jnp.zeros(sums_line.shape[1:], F32)

    share.end()
    layer_share.end()
    desk.flush(grad_tokens, layer_out)
    first.finish()
    cores = []
    size = kv_out.shape[0] // 4
    for k in range(4):
        rows_of = pl.ds(pl.multiple_of(wire.blocks[k] * size, size), size)
        if k:
            device = {"mp": wire.blocks[k]}
            cores.append(wire.send(kv_out.at[rows_of], kv_got.at[k], device))
        else:
            kv_got[0] = kv_out[rows_of]
    qup.finish()
    desk.flush(grad_qup)
    out.finish()
    desk.flush(grad_out)
    total = sums[2 * place + wire.side] + sums_side[place]
    for made, d, way, there in line_sends:
        pl.when((place - way * d >= 0) & (place - way * d <= 3))(made.wait_recv)
    for index in range(6):
        total = total + sums_line[index]
    gains[...] = total
    for made in cores:
        made.wait_recv()
    columns = kv_out.shape[1]
    for k in range(4):
        at = pl.ds(pl.multiple_of(wire.blocks[k] * columns, columns), columns)
        grad_kv[:, at] = kv_got[k]
    for made in (side_first, *cores):
        made.wait_send()
    for made, d, way, there in line_sends:
        pl.when(there)(made.wait_send)
    row_sum.end()
    for chain in (out, qup, first):
        chain.settle()


def attend_one(
    scale, mp_blocks, c, gain, q_up, cos, sin, kv, key_ids, row_ids, row_starts, out_proj,
    qn, q, o, lse, send, keep, chat_out, inverse_out,
):
    rows = qn.shape[0]
    half, quarter = rows // 2, rows // 4
    part = c.shape[2]
    wide = q.shape[2]
    cut = lambda k, i: c[k, i * quarter : (i + 1) * quarter, :]
    pieces = [jnp.concatenate([cut(k, i ^ k) for i in range(4)], 0) for k in range(4)]
    latent = jnp.concatenate(pieces, 1).astype(F32)
    inverse = inverse_rms(latent)
    chat = latent * inverse
    inverse_out[...] = inverse[:quarter]
    for k in range(4):
        columns = pl.ds(pl.multiple_of(mp_blocks[k] * part, part), part)
        chat_out[:, columns] = chat[:quarter, k * part : (k + 1) * part]
        qn[:, columns] = (chat[:, k * part : (k + 1) * part] * gain[:, columns]).astype(LOW)
    bias = jnp.where((key_ids >= row_starts) & (key_ids <= row_ids), 0.0, NEG_LARGE)
    low = qn[...]
    for h in range(q.shape[0]):
        pre = dot(low, q_up[:, h * wide : (h + 1) * wide])
        q_h = (rotate(pre, cos, sin) * scale).astype(LOW)
        q[h] = q_h
        scores = inner_cols(q_h, kv[:, :wide]) + bias
        top = jnp.max(scores, axis=-1, keepdims=True)
        probs = jnp.exp(scores - top)
        total = jnp.sum(probs, axis=-1, keepdims=True)
        out = dot(probs.astype(LOW), kv[:, wide:]) / total
        o[:, h * wide : (h + 1) * wide] = out.astype(LOW)
        log_total = jnp.broadcast_to(top + jnp.log(total), (rows, 128))
        lse[h : h + 1, :] = jnp.transpose(log_total)[:1]
    keep[...] = dot(o[:half, :], out_proj[...])
    send[...] = dot(o[half:, :], out_proj[...]).astype(LOW)


def fore1_body(scale, desk, *refs):
    refs = list(refs)
    take = lambda n: [refs.pop(0) for _ in range(n)]
    tokens, cotangent, q_down, kv_proj, q_up, out_proj, w_down = take(7)
    lengths, gain1, gain_c, gain2, cosine, sine = take(6)
    h1_mine, h1_theirs, qn_mine, qn_theirs = (take(2) for _ in range(4))
    qs, os, lses, kvs, dz_got = (take(2) for _ in range(5))
    dhid, chat, inv_c, y_out, n2_out, inv2_out, n1_out, inv1_out, h2 = take(9)
    dz, x, down_w, kv_w, up_w, out_w, back_w, h1, c, qn, dz_theirs = take(11)
    send, kept, got, cross_out, cross_got = take(5)
    loads = take(1)[0]
    wire = Wire(*take(2))
    place, blocks = wire.place, wire.blocks
    rows = x.shape[1]
    half, quarter = rows // 2, rows // 4
    wide = kv_proj.shape[1] // 2

    started = []

    def load(source, target):
        made = pltpu.make_async_copy(source, target, loads.at[len(started)])
        made.start()
        started.append(made)
        return made

    def load_rows(source, target):
        return [
            load(source.at[pl.ds(pl.multiple_of(blocks[k] * quarter, quarter), quarter), :],
                 target.at[k * quarter : (k + 1) * quarter, :])
            for k in range(4)
        ]

    in_x = [load_rows(tokens.at[0], x.at[0])]
    in_kv = load(kv_proj, kv_w)
    in_x.append(load_rows(tokens.at[1], x.at[1]))
    in_down = load(q_down, down_w)
    in_dz = [load_rows(cotangent.at[m], dz.at[m]) for m in range(2)]
    in_back, in_up, in_out = load(w_down, back_w), load(q_up, up_w), load(out_proj, out_w)

    line_kv, side_kv, cross_kv, core_kv, cross_c, core_c = [], [], [], [], [], []
    for m in range(2):
        for d in range(1, 4):

            @pl.when(place < d)
            def _(m=m, d=d):
                kvs[m][0, :, d] = jnp.zeros(kvs[m].shape[1:2] + kvs[m].shape[3:], LOW)
                kvs[m][1, :, d] = jnp.zeros(kvs[m].shape[1:2] + kvs[m].shape[3:], LOW)

        own = kvs[m].at[0, 0, 0]
        near, there = slice(0, quarter), slice(quarter, half)
        line_kv.append([
            wire.copy(own.at[near], kvs[m].at[0, 0, d, near], {"seq": wire.seq + 2 * d})
            for d in range(1, 4)
        ])
        side_kv.append([wire.copy(own, kvs[m].at[0, 1, 0], wire.beside)] + [
            wire.copy(kvs[m].at[0, 0, d, near], kvs[m].at[0, 1, d, near], wire.beside)
            for d in range(1, 4)
        ])
        cross_kv.append([None] + [
            wire.copy(kvs[m].at[0, :, d, near], kvs[m].at[0, :, d, there], wire.cross)
            for d in range(1, 4)
        ])
        core_kv.append([
            wire.copy(kvs[m].at[0, :, d], kvs[m].at[1, :, d], wire.core) for d in range(4)
        ])
        cross_c.append(wire.copy(c.at[m, 0], c.at[m, 1], wire.cross))
        core_c.append([
            wire.copy(c.at[m, 0], c.at[m, 2], wire.core),
            wire.copy(c.at[m, 1], c.at[m, 3], wire.core),
        ])
    wire.greet(4, 3)

    for m in range(2):
        cos, sin = cosine[m], sine[m]
        for made in in_x[m]:
            made.wait()
        if m == 0:
            in_kv.wait()
        values = x[m].astype(F32)
        inverse = inverse_rms(values)
        normed = values * inverse
        n1_out[m], inv1_out[m] = normed[:quarter], inverse[:quarter]
        low = (normed * gain1[...]).astype(LOW)
        h1[...] = low
        pair = dot(low[:half], kv_w[...])
        own = kvs[m].at[0, 0, 0]
        own[:, :wide] = rotate(pair[:, :wide], cos[:half], sin[:half]).astype(LOW)
        own[:, wide:] = pair[:, wide:].astype(LOW)
        for d in (3, 2, 1):
            pl.when(place + d <= 3)(line_kv[m][d - 1].start)
        side_kv[m][0].start()
        if m == 0:
            in_down.wait()
        c[m, 0] = dot(low, down_w[...]).astype(LOW)
        cross_c[m].start()
        core_c[m][0].start()
        side_columns(h1, h1_mine[m], h1_theirs[m], wire.side)
        desk.flush(h1_mine[m], h1_theirs[m])

    def pass_kv(m, d):
        @pl.when(place >= d)
        def _():
            line_kv[m][d - 1].wait_recv()
            side_kv[m][d].start()

    def pass_cross(m, d):
        @pl.when(place >= d)
        def _():
            side_kv[m][d].wait_recv()
            cross_kv[m][d].start()

    def pass_core(m, d):
        @pl.when(place >= d)
        def _():
            (cross_kv if d else side_kv)[m][d].wait_recv()
            core_kv[m][d].start()

    in_back.wait()
    for m in range(2):
        for made in in_dz[m]:
            made.wait()
    dhid[0] = inner_cols(dz[0], back_w[...])
    for d in (1, 2, 3):
        pass_kv(0, d)
    for m in range(2):
        cross_c[m].wait_recv()
        core_c[m][1].start()
    for d in (1, 2, 3):
        pass_cross(0, d)
    dhid[1] = inner_cols(dz[1], back_w[...])
    for d in (1, 2, 3):
        pass_kv(1, d)
    for m in range(2):
        for z in range(4):
            block = dz_theirs.shape[3]
            columns = pl.ds(pl.multiple_of((2 * z + 1 - wire.side) * block, block), block)
            dz_theirs[m, z] = dz[m, :half, columns]
    desk.flush(dhid, n1_out)
    for d in range(4):
        pass_core(0, d)
    for d in (1, 2, 3):
        pass_cross(1, d)
    in_up.wait()
    in_out.wait()
    sums = [
        RowSum(wire, send.at[m : m + 1], kept.at[m : m + 1], got.at[m : m + 1],
               cross_out.at[m : m + 1], cross_got.at[m : m + 1], quarter, 2)
        for m in range(2)
    ]
    shares = []

    def after_sum(m):
        for part, span in enumerate(sums[m].spans):
            value = x[m, span, :].astype(F32) + sums[m].result(part)[0]
            inverse = inverse_rms(value)
            normed = value * inverse
            y_out[m, span, :], n2_out[m, span, :], inv2_out[m, span, :] = value, normed, inverse
            h2[m, span, :] = (normed * gain2[...]).astype(LOW)
            spot = lambda k: h2.at[m, k * quarter + span.start : k * quarter + span.stop, :]
            shares.append((
                wire.send(spot(0), spot(1), wire.cross), wire.send(spot(0), spot(2), wire.core),
                wire.copy(spot(1), spot(3), wire.core),
            ))

    for m in range(2):
        if m == 1:
            for d in range(4):
                pass_core(1, d)
        for d in range(4):
            pl.when(place >= d)(core_kv[m][d].wait_recv)
        for made in core_c[m]:
            made.wait_recv()
        desk.flush(kvs[m])
        rows_at = row_places(wire, quarter, 0)
        attend_one(
            scale, blocks, c.at[m], gain_c, up_w, cosine[m], sine[m],
            kvs[m][...].reshape(2 * 2 * 4 * half, 2 * wide),
            key_places(wire, quarter, 4, 1, (0, 1)), rows_at,
            sequence_starts(lengths, m, rows_at), out_w, qn, qs[m], os[m], lses[m], send.at[m], kept.at[m],
            chat.at[m], inv_c.at[m],
        )
        sums[m].core.start()
        if m == 0:
            side_dz = wire.send(dz_theirs, dz_got[0], wire.beside)
        side_columns(qn, qn_mine[m], qn_theirs[m], wire.side)
        desk.flush(qs[m], os[m], qn_mine[m], qn_theirs[m])
        if m == 1:
            after_sum(0)
        sums[m].pass_on()
    after_sum(1)
    desk.flush(chat, y_out, n2_out)
    side_dz.wait_recv()
    core_dz = wire.send(dz_got[0], dz_got[1], wire.core)
    for near, _, far in shares:
        near.wait_recv()
        far.start()
    for _, first, far in shares:
        first.wait_recv()
        far.wait_recv()
    core_dz.wait_recv()
    for made in [side_dz, core_dz, *cross_c, *(a for p in core_c for a in p),
                 *(a for p in shares for a in p)]:
        made.wait_send()
    for m in range(2):
        sums[m].end()
        for d in range(4):

            @pl.when(place >= d)
            def _(m=m, d=d):
                side_kv[m][d].wait_send()
                if d:
                    cross_kv[m][d].wait_send()
                core_kv[m][d].wait_send()

        for d in range(1, 4):
            pl.when(place + d <= 3)(line_kv[m][d - 1].wait_send)


def deliver_body(count, pieces, *refs):
    results, gains = refs[:count], refs[count]
    outs, rooms, sems = refs[count + 1 : -count - 1], refs[-count - 1 : -1], refs[-1]
    loads, stores = [], []
    for source, room, target in zip(results, rooms, outs):
        size = source.shape[-2] // pieces
        for i in range(pieces):
            cut = (slice(None),) * (len(source.shape) - 2) + (slice(i * size, (i + 1) * size),)
            at = len(loads)
            loads.append(pltpu.make_async_copy(source.at[cut], room.at[cut], sems.at[2 * at]))
            stores.append(pltpu.make_async_copy(room.at[cut], target.at[cut], sems.at[2 * at + 1]))
    for made in loads:
        made.start()
    at = 0
    for ref in outs[count:]:
        ref[...] = gains[0, at : at + ref.shape[0]]
        at += ref.shape[0]
    for load, store in zip(loads, stores):
        load.wait()
        store.start()
    for made in stores:
        made.wait()


def local(
    tokens,
    lengths,
    norm1_gain,
    q_down,
    latent_gain,
    q_up,
    kv_proj,
    out_proj,
    norm2_gain,
    w_gate,
    w_up,
    w_down,
    cotangent,
):
    micro, rows, width = tokens.shape
    seq = lax.axis_size("seq")
    line = seq // 2
    at = lax.axis_index("seq").astype(jnp.int32)
    me = lax.axis_index("mp").astype(jnp.int32)
    place, side = at // 2, at % 2
    ids = jnp.stack([me, side])
    quarter, half = rows // 4, rows // 2
    head_dim = kv_proj.shape[1] // 2
    heads = q_up.shape[1] // head_dim
    part = q_down.shape[1]
    rank = q_up.shape[0]
    hidden = w_gate.shape[1]
    kv_part = kv_proj.shape[1] // 4
    wide = width // seq
    scale = head_dim ** (-0.5)
    key_count = seq * rows
    beside = [(i, i ^ 1) for i in range(seq)]
    narrow = line == 4 and micro == 2 and key_count <= 2048 and not wide % 128

    def swap(index):
        return ((index & 1) << 1) | (index >> 1)

    def to_natural(array, axis):
        size = array.shape[axis] // 4
        return jnp.concatenate(
            [lax.dynamic_slice_in_dim(array, swap(me ^ b) * size, size, axis) for b in range(4)],
            axis,
        )

    def other(array):
        return lax.ppermute(array, "seq", beside)

    def sum_mp(send, keep):
        kept = keep + lax.ppermute(send, "mp", CORE).astype(F32)
        got = lax.ppermute(kept[..., quarter:, :].astype(LOW), "mp", CROSS)
        return kept[..., :quarter, :] + got.astype(F32)

    def gather_mp(piece):
        near = lax.ppermute(piece, "mp", CROSS)
        pair = jnp.concatenate([piece, near], -2)
        return piece, near, lax.ppermute(pair, "mp", CORE)

    def sides_shape(columns, their_rows, lead=()):
        if columns // seq % 128:
            return []
        return [
            whole((*lead, line, n, columns // seq), LOW) for n in (rows, their_rows)
        ]

    def split_sides(made, full, their_rows):
        if made:
            return made
        split = full.reshape(*full.shape[:-1], line, 2, full.shape[-1] // seq)
        mine, theirs = (
            jnp.moveaxis(lax.dynamic_index_in_dim(split, i, split.ndim - 2, keepdims=False), -2, -3)
            for i in (side, 1 - side)
        )
        return mine, theirs[..., :their_rows, :]

    def from_other(theirs):
        got = other(theirs)
        return got, lax.ppermute(got, "mp", CORE)

    def without_sides(body, count):
        return body if count else lambda *refs: body(*refs, None, None)

    def both_sides(mine, got):
        lefts, spans = [], []
        for array, first, count, partner in (
            (mine, 0, rows, 0), (got[0], 0, half, 1), (got[1], half, half, 1)
        ):
            stacked_array = not isinstance(array, list)
            for m in range(micro):
                spans.append((len(lefts) if not stacked_array else len(lefts), m if stacked_array else None,
                              m, partner, first, count))
                if not stacked_array:
                    lefts.append(array[m])
            if stacked_array:
                lefts.append(array)
        return lefts, spans

    class Chain:
        def __init__(self, lefts, rights, terms, shape, turned=False, from_side=None):
            self.args = [*lefts, *rights]
            self.spec = (terms, len(lefts), len(rights))
            self.shape, self.turned = shape, turned
            self.from_side = [] if from_side is None else [from_side]
            self.step, self.up, self.down = 0, None, None

        def block(self, index, added, after, last=False):
            turned = last and self.turned
            body = functools.partial(
                block_body, *self.spec, len(added), len(self.from_side), turned
            )
            shape = self.shape[::-1] if turned else self.shape
            return run(
                body, index.reshape(1), [*self.args, *added, *self.from_side],
                [whole(shape, F32 if last else LOW)], after, name="block",
            )[0]

        def advance(self, after):
            self.step += 1
            step = self.step
            goes_up = [(i, i + 2) for i in range(2 * step)]
            goes_down = [(seq - 1 - i, seq - 3 - i) for i in range(2 * step)]
            for_up, for_down = line - step + place, step - line + place
            if 2 * step < line + 1:
                which = jnp.where(
                    place <= step - 1, for_up, jnp.where(place >= line - step, for_down, 0)
                )
                term = self.block(which, [a for a in (self.up, self.down) if a is not None], after)
                if step == 1 and line > 3:
                    self.up = lax.ppermute(term, "seq", goes_up + goes_down)
                else:
                    self.up = lax.ppermute(term, "seq", goes_up)
                    self.down = lax.ppermute(term, "seq", goes_down)
                return [term]
            term_up = self.block(jnp.clip(for_up, 0, line - 1), [self.up], after)
            term_down = self.block(jnp.clip(for_down, 0, line - 1), [self.down], [term_up])
            self.up = lax.ppermute(term_up, "seq", goes_up)
            self.down = lax.ppermute(term_down, "seq", goes_down)
            return [term_down]

        def finish(self, after):
            while self.step < line - 1:
                after = self.advance(after)
            result = self.block(place, [self.up, self.down], after, last=True)
            return result, [result]

    quarter_rows = jnp.arange(quarter, dtype=jnp.int32)
    row_ids = at * rows + jnp.concatenate([(me ^ k) * quarter + quarter_rows for k in ORDER])
    key_ids = (
        ((place - jnp.arange(line, dtype=jnp.int32)[None, None, :, None, None]) * 2
         + (side ^ jnp.arange(2, dtype=jnp.int32)[None, :, None, None, None])) * rows
        + (me ^ (jnp.arange(2, dtype=jnp.int32)[:, None, None, None, None]
                 + 2 * jnp.arange(2, dtype=jnp.int32)[None, None, None, :, None])) * quarter
        + quarter_rows[None, None, None, None, :]
    ).reshape(key_count)

    gain1_row, gain2_row, gain_c_row = norm1_gain[None, :], norm2_gain[None, :], latent_gain[None, :]
    kv_cols = lax.dynamic_slice_in_dim(kv_proj, me * kv_part, kv_part, 1)
    first_weights = jnp.concatenate([q_down, kv_cols], axis=1)
    low = lambda *shape: pltpu.VMEM(shape, LOW)
    full = lambda *shape: pltpu.VMEM(shape, F32)
    near = lambda *arrays: [(1, a) for a in arrays]
    far = lambda *arrays: [(0, a) for a in arrays]
    columns = heads * head_dim
    side_rows = rank // seq
    first_columns = part + kv_part

    def narrow_layer():
        numbers = lambda array: [(2, array)]
        late = lambda *arrays: [(3, a) for a in arrays]
        later = lambda *arrays: [(4, a) for a in arrays]
        first_end = lengths[:, 0:1]
        second_end = first_end + lengths[:, 1:2]
        places = row_ids[None, :] - jnp.where(
            row_ids >= second_end, second_end, jnp.where(row_ids >= first_end, first_end, 0)
        )
        freqs = BASE ** (-2.0 * jnp.arange(head_dim // 2, dtype=F32) / head_dim)
        angles = places.astype(F32)[:, :, None] * freqs
        cosine, sine = jnp.cos(angles), jnp.sin(angles)
        row_shape = whole((micro, quarter, width), F32)
        one_shape = whole((micro, quarter, 1), F32)
        side_shape = whole((micro, line, half, wide), LOW)
        args = far(tokens, cotangent, q_down, kv_proj, q_up, out_proj, w_down)
        args += numbers(lengths) + near(gain1_row, gain_c_row, gain2_row, cosine, sine)
        outs = late(*[whole((line, rows, wide), LOW)] * 4, *[whole((line, rows, side_rows), LOW)] * 4)
        outs += late(*[whole((heads, rows, head_dim), LOW)] * 2, *[whole((rows, columns), LOW)] * 2)
        outs += near(*[whole((heads, rows), F32)] * 2)
        outs += late(*[whole((2, 2, line, half, 2 * head_dim), LOW)] * 2)
        outs += far(*[side_shape] * 2)
        outs += late(
            whole((micro, rows, hidden), F32), whole((micro, quarter, rank), F32))
        outs += near(one_shape) + late(row_shape, row_shape) + near(one_shape) + late(row_shape)
        outs += near(one_shape) + late(whole((micro, rows, width), LOW))
        made = list(mesh_run(
            functools.partial(fore1_body, scale), args, outs,
            [low(micro, rows, width), low(micro, rows, width), low(width, part),
             low(width, 2 * head_dim),
             low(rank, columns), low(columns, width), low(hidden, width), low(rows, width),
             low(micro, 4, rows, part), low(rows, rank), low(micro, line, half, wide),
             low(micro, half, width), full(micro, half, width), low(micro, half, width),
             low(micro, quarter, width), low(micro, quarter, width),
             pltpu.SemaphoreType.DMA((24,))],
            4, "fore1", 60, 84,
        ))
        give = lambda n: [made.pop(0) for _ in range(n)]
        h1_mine, h1_theirs, qn_mine, qn_theirs = (give(2) for _ in range(4))
        qs, os, lses, kv, dz_got = (give(2) for _ in range(5))
        kv = [a.reshape(key_count, 2 * head_dim) for a in kv]
        dhid, chat, inv_c, y, n2, inv2, n1, inv1, h2 = give(9)

        ahead = hidden * 3 // 11 // 128 * 128
        args = far(w_gate, w_up, w_down, cotangent) + late(h2) + later(dhid, n2)
        args += near(inv2, gain2_row) + later(*dz_got, y)
        outs = near(whole((hidden, wide), F32)) + late(row_shape) + near(whole((1, width), F32))
        outs += late(whole((micro, rows, width), LOW), whole((micro, line, rows, wide), LOW), side_shape)
        outs += near(whole((micro, quarter, width), LOW))
        outs += late(*[whole((rows, hidden), LOW)] * 6, *[whole((line, rows, wide), LOW)] * 2)
        outs += far(*[whole((line, half, wide), LOW)] * 4, *[whole((rows, hidden), LOW)] * 2)
        made = list(mesh_run(
            functools.partial(back1_body, quarter), args, outs,
            [low(width, hidden), low(width, hidden), low(rows, hidden - ahead),
             low(rows, hidden - ahead), low(micro, line, half, wide),
             low(5, wide, hidden - ahead), low(2, wide, hidden - ahead),
             low(micro, half, width), full(micro, half, width), low(micro, half, width),
             low(micro, quarter, width), low(micro, quarter, width),
             pltpu.SemaphoreType.DMA((6,)), low(micro, half, width), low(micro, half, width),
             low(micro, half, width), low(micro, quarter, width), low(micro, quarter, width),
             low(5, 2 * wide, ahead), low(2, 2 * wide, ahead), full(2, wide, ahead),
             low(wide, ahead), low(wide, ahead), low(micro, rows, width),
             pltpu.SemaphoreType.DMA((8,))],
            1, "back1", 62, 40,
        ))
        grad_down, dy, gain2, dyl, dyl_mine, dyl_theirs, layer_own = give(7)
        hid, dg, du, h2_mine, h2_got, h2_far, dg_other = (give(2) for _ in range(7))

        args = numbers(lengths) + late(*dg, *dg_other, *du, *h2_mine, *h2_got, *h2_far)
        args += late(dyl, out_proj, q_up, *qs, *kv, *os) + near(*lses)
        args += late(cosine, sine, chat) + near(inv_c, gain_c_row) + far(dyl_theirs)
        args += late(*qn_theirs) + far(*os)
        outs = late(whole((wide, hidden), F32), whole((wide, hidden), F32))
        outs += near(whole((micro, rows, first_columns), LOW), whole((1, rank), F32))
        outs += late(whole((micro, rows, columns), LOW))
        outs += far(side_shape, side_shape, whole((line, side_rows, columns), LOW),
                    *[whole((rows, columns), LOW)] * 2)
        kv_low = lambda *lead: low(*lead, quarter, 2 * head_dim)
        key_half = key_count // 2
        (grad_gate, grad_up, dfirst, gain_c, dqp, dyl_got, dyl_far, qup_side,
         *o_other) = mesh_run(
            functools.partial(back2_body, quarter, scale), args, outs,
            [low(rows, hidden), low(rows, hidden), low(5, wide, hidden), low(2, wide, hidden),
             low(5, wide, hidden), low(2, wide, hidden), full(heads * rows, head_dim),
             low(micro, half, rank),
             full(micro, half, rank), low(micro, key_half, 2 * head_dim),
             low(micro, key_half, 2 * head_dim), low(micro, half, rank),
             low(micro, quarter, rank), low(micro, quarter, rank),
             low(micro, key_half, 2 * head_dim), kv_low(micro, 2 * line), kv_low(micro, 2 * line),
             kv_low(micro, line), kv_low(micro, line), kv_low(micro, 3), kv_low(micro, 3),
             full(micro, quarter, 2 * head_dim), low(micro, rows, rank + 2 * head_dim),
             low(line, side_rows, columns)],
            2, "back2", 62, 44,
        )

        args = later(dfirst) + far(q_down, kv_proj) + later(*h1_mine, *h1_theirs)
        args += late(*os, *o_other, dyl_mine, dyl_got, dyl_far)
        args += later(*qn_mine, dqp, qup_side, n1)
        args += near(inv1) + later(dy) + near(gain1_row, gain2, gain_c, layer_own)
        block = width // 4 // seq
        gain_columns = 2 * wide + side_rows
        outs = late(whole((columns, wide), F32), whole((side_rows, columns), F32))
        outs += near(whole((wide, part), F32), whole((block, 2 * head_dim), F32))
        outs += late(whole((micro, rows, width), LOW)) + near(whole((1, gain_columns), F32))
        outs += late(whole((micro, rows, width), LOW))
        grad_out, grad_qup, grad_qdown, grad_kv, input_grads, gains, layer_out = mesh_run(
            functools.partial(back3_body, quarter), args, outs,
            [low(5, wide, columns), low(2, wide, columns), low(5, side_rows, columns),
             low(2, side_rows, columns), low(5, wide, first_columns),
             low(2, wide, first_columns), low(line, wide, first_columns),
             low(line, wide, first_columns), low(micro, half, width), full(micro, half, width),
             low(micro, half, width), low(micro, quarter, width), low(micro, quarter, width),
             full(wide, kv_part), full(4, block, kv_part), full(seq, 1, gain_columns),
             full(seq, 1, gain_columns), full(seq, 1, gain_columns), full(line, 1, gain_columns),
             full(12, 1, gain_columns), low(width, first_columns), pltpu.SemaphoreType.DMA((2,))],
            3, "back3", 60, 44,
        )
        results = [layer_out, input_grads, grad_qdown, grad_qup, grad_kv, grad_out, grad_gate,
                   grad_up, grad_down]
        made = pl.pallas_call(
            functools.partial(deliver_body, len(results), 4),
            in_specs=[pl.BlockSpec(memory_space=pl.ANY)] * len(results) + [in_vmem()],
            out_specs=[pl.BlockSpec(memory_space=pl.ANY)] * len(results) + [in_vmem()] * 3,
            out_shape=[whole(a.shape, a.dtype) for a in results]
            + [whole((n,), F32) for n in (wide, wide, side_rows)],
            scratch_shapes=[pltpu.VMEM(a.shape, a.dtype) for a in results]
            + [pltpu.SemaphoreType.DMA((8 * len(results),))],
            compiler_params=pltpu.CompilerParams(vmem_limit_bytes=60 << 20),
            name="deliver",
        )(*results, gains)
        (layer_out, input_grads, grad_qdown, grad_qup, grad_kv, grad_out, grad_gate, grad_up,
         grad_down, grad_n1, grad_n2, grad_c) = made
        return (
            layer_out, input_grads, grad_n1, grad_qdown, grad_c, grad_qup, grad_kv, grad_out,
            grad_n2, grad_gate, grad_up, grad_down,
        )

    if narrow:
        return narrow_layer()

    both_rows = sides_shape(width, rows)
    half_rows = sides_shape(width, half)
    rank_sides = sides_shape(rank, rows)

    tables, starts, kv, c_part, h1_sides = [], [], [], [], []
    order = []
    for m in range(micro):
        _, places = documents(lengths[m], row_ids)
        starts.append(row_ids - places)
        tables.append(rotation(places, head_dim))
        c, packed, h1, *made = run(
            without_sides(functools.partial(first_body, m, quarter), len(both_rows)),
            ids,
            [tokens, gain1_row, q_down, kv_proj, *tables[m]],
            [whole((rows, part), LOW), whole((half, 2 * head_dim), LOW), whole((rows, width), LOW),
             *both_rows],
            order,
            name="first",
        )
        order = [c]
        blocks = [packed] + [
            lax.ppermute(packed, "seq", [(i, i + 2 * d) for i in range(seq - 2 * d)])
            for d in range(1, line)
        ]
        near = jnp.stack(blocks, 0)
        near = jnp.stack([near, other(near)], 0)
        kv.append(
            jnp.stack([near, lax.ppermute(near, "mp", CORE)], 0).reshape(key_count, 2 * head_dim)
        )
        c_part.append(c)
        h1_sides.append(split_sides(made, h1, rows))

    dhid, dz, *made = run(
        functools.partial(cotangent_body, micro, quarter),
        ids,
        [cotangent, w_down],
        [whole((micro, rows, hidden), F32), whole((micro, rows, width), LOW),
         *sides_shape(width, half, (micro,))],
        order,
        name="cotangent",
    )
    order = [dz]
    dz_mine, dz_theirs = split_sides(made, dz, half)
    dz_got = from_other(dz_theirs)

    qn_sides, qs, os, lses, sums, c_rows = [], [], [], [], [], []
    for m in range(micro):
        near = lax.ppermute(c_part[m], "mp", CROSS)
        swapped = jnp.concatenate(
            [near[quarter : 2 * quarter], near[:quarter], near[3 * quarter :],
             near[2 * quarter : 3 * quarter]], 0
        )
        far = lax.ppermute(jnp.concatenate([c_part[m], swapped], 1), "mp", CORE)
        qn, q, o, lse, send, keep, *made = run(
            without_sides(functools.partial(attend_body, scale), len(rank_sides)),
            ids,
            [c_part[m], near, far, gain_c_row, q_up, *tables[m], kv[m], key_ids[None, :],
             row_ids[:, None], starts[m][:, None], out_proj],
            [whole((rows, rank), LOW), whole((heads, rows, head_dim), LOW),
             whole((rows, heads * head_dim), LOW), whole((heads, rows), F32),
             whole((half, width), LOW), whole((half, width), F32), *rank_sides],
            order,
            name="attend",
        )
        order = [o]
        qn_sides.append(split_sides(made, qn, rows))
        qs.append(q)
        os.append(o)
        lses.append(lse)
        sums.append(sum_mp(send, keep))
        c_rows.append(
            jnp.concatenate([c_part[m][:quarter], swapped[:quarter], far[half : half + quarter]], 1)
        )

    h2_mine, h2_theirs, hid, dg, du, state = [], [], [], [], [], []
    for m in range(micro):
        x = lax.dynamic_slice_in_dim(tokens[m], me * quarter, quarter, 0).astype(F32)
        inv1 = inverse_rms(x)
        y = x + sums[m]
        inv2 = inverse_rms(y)
        n2 = y * inv2
        pieces = gather_mp((n2 * gain2_row).astype(LOW))
        h2, hid_m, dg_m, du_m, *made = run(
            without_sides(functools.partial(forward_body, m), len(half_rows)),
            ids,
            [*pieces, w_gate, w_up, dhid],
            [whole((rows, width), LOW), *[whole((rows, hidden), LOW)] * 3, *half_rows],
            order,
            name="forward",
        )
        order = [hid_m]
        mine, theirs = split_sides(made, h2, half)
        h2_mine.append(mine)
        h2_theirs.append(theirs)
        hid.append(hid_m)
        dg.append(dg_m)
        du.append(du_m)
        state.append(dict(x=x, n1=x * inv1, inv1=inv1, y=y, n2=n2, inv2=inv2, c=c_rows[m]))

    def stacked(name):
        return jnp.stack([st[name] for st in state], 0)

    def with_other(arrays):
        return [*arrays, *[other(a) for a in arrays]]

    def terms_of(spans):
        return [(a, lead, m + micro * partner, None, first, count)
                for a, lead, m, partner, first, count in spans]

    send, keep, ffn_send, ffn_keep = run(
        functools.partial(hidden_back_body, micro),
        ids,
        [*dg, *du, *hid, w_gate, w_up, w_down],
        [whole((micro, half, width), LOW), whole((micro, half, width), F32)] * 2,
        order,
        name="hidden_back",
    )
    lefts, spans = both_sides(dz_mine, dz_got)
    chain_down = Chain(lefts, with_other(hid), terms_of(spans), (wide, hidden), turned=True)
    lefts, spans = both_sides(h2_mine, [list(p) for p in zip(*[from_other(t) for t in h2_theirs])])
    chain_gate = Chain(lefts, with_other(dg), terms_of(spans), (wide, hidden))
    chain_up = Chain(lefts, with_other(du), terms_of(spans), (wide, hidden))

    order = chain_down.advance([send])
    dh2 = sum_mp(send, keep)
    y, n2, inv2, n1, inv1 = (stacked(k) for k in ("y", "n2", "inv2", "n1", "inv1"))
    dz_own = dz[:, :quarter].astype(F32)
    gain2 = jnp.sum(dh2 * n2, axis=(0, 1))
    dy = dz_own + norm_backward(dh2 * gain2_row, n2, inv2)
    for _ in range(2):
        order = chain_down.advance(order)
    order = chain_gate.advance(order)

    def attend_back(which, pieces):
        args = [*pieces, out_proj, q_up, key_ids[:, None]]
        for m in which:
            args += [qs[m], kv[m], os[m], lses[m], jnp.stack([row_ids, starts[m]], 0), *tables[m]]
        n = len(which)
        return run(
            functools.partial(attend_back_body, scale, n, min(1024, key_count // 2)),
            ids,
            args,
            [whole((n, rows, width), LOW), whole((n, rows, heads * head_dim), LOW),
             whole((n, half, rank), LOW), whole((n, half, rank), F32),
             whole((n, key_count // 2, 2 * head_dim), LOW),
             whole((n, key_count // 2, 2 * head_dim), F32), *sides_shape(width, half, (n,))],
            order,
            scratch=[pltpu.VMEM((heads, rows, head_dim), F32),
                     pltpu.VMEM((heads, rows, head_dim), LOW),
                     pltpu.VMEM((heads, 8, rows), F32)],
            name="attend_back",
            limit=56,
        )

    pieces = gather_mp(dy.astype(LOW))
    if key_count <= 2048:
        made = attend_back(range(micro), pieces)
    else:
        each = [attend_back([m], [p[m : m + 1] for p in pieces]) for m in range(micro)]
        made = [jnp.concatenate(parts, 0) for parts in zip(*each)]
    dyl, dqp, send, keep, kv_send, kv_keep, *made = made
    order = [send]
    dyl_mine, dyl_theirs = split_sides(made, dyl, half)
    lefts, spans = both_sides(dyl_mine, from_other(dyl_theirs))
    chain_out = Chain(lefts, with_other(os), terms_of(spans), (wide, heads * head_dim), turned=True)

    def side_sum(lefts, rights, shape, after):
        terms = [(m, None, 0, m, 0, rows) for m in range(micro)]
        (made,) = run(
            functools.partial(side_sum_body, terms, len(lefts)),
            ids,
            [*lefts, *rights],
            [whole((line, *shape), LOW)],
            after,
            name="side_sum",
        )
        return other(made), [made]

    def own_chain(side_pairs, right, shape, after):
        from_side, after = side_sum([p[1] for p in side_pairs], [right], shape, after)
        terms = [(m, None, 0, m, 0, rows) for m in range(micro)]
        return Chain([p[0] for p in side_pairs], [right], terms, shape, from_side=from_side), after

    shape = (rank // seq, heads * head_dim)
    chain_qup, order = own_chain(qn_sides, dqp, shape, order)
    order = chain_gate.advance(order)
    order = chain_up.advance(order)

    dqn = sum_mp(send, keep)
    c = stacked("c").astype(F32)
    inv_c = inverse_rms(c)
    chat = c * inv_c
    chat = to_natural(chat, 2)
    gain_c = jnp.sum(dqn * chat, axis=(0, 1))
    dc = norm_backward(dqn * gain_c_row, chat, inv_c).astype(LOW)

    dkv = kv_keep + lax.ppermute(kv_send, "mp", CORE).astype(F32)
    dkv = dkv.reshape(micro, 2, line, 2, quarter, 2 * head_dim)
    dkv = dkv[:, :, :, 0] + lax.ppermute(dkv[:, :, :, 1].astype(LOW), "mp", CROSS).astype(F32)
    dkv = dkv[:, 0] + other(dkv[:, 1].astype(LOW)).astype(F32)
    total = dkv[:, 0]
    for d in range(1, line):
        total = total + lax.ppermute(
            dkv[:, d].astype(LOW), "seq", [(i + 2 * d, i) for i in range(seq - 2 * d)]
        ).astype(F32)
    cosine = jnp.stack([t[0][:quarter] for t in tables], 0)
    sine = jnp.stack([t[1][:quarter] for t in tables], 0)
    dkv_low = jnp.concatenate(
        [unrotate(total[..., :head_dim], cosine, sine), total[..., head_dim:]], axis=-1
    ).astype(LOW)
    both = jnp.concatenate(gather_mp(jnp.concatenate([dc, dkv_low], -1)), -2)
    dfirst = jnp.concatenate(
        [lax.dynamic_slice_in_dim(both, me * part, part, 2),
         lax.dynamic_slice_in_dim(both, rank + me * kv_part, kv_part, 2)], -1
    )

    grad_down, order = chain_down.finish(order)
    order = chain_gate.advance(order)
    order = chain_up.advance(order)
    order = chain_out.advance(order)
    grad_gate, order = chain_gate.finish(order)
    order = chain_up.advance(order)
    order = chain_out.advance(order)
    grad_up, order = chain_up.finish(order)
    order = chain_qup.advance(order)
    order = chain_out.advance(order)
    chain_first, order = own_chain(h1_sides, dfirst, (wide, part + kv_part), order)
    order = chain_qup.advance(order)
    grad_out, order = chain_out.finish(order)
    order = chain_first.advance(order)
    order = chain_qup.advance(order)
    order = chain_first.advance(order)
    grad_qup, order = chain_qup.finish(order)
    order = chain_first.advance(order)
    grad_first, order = chain_first.finish(order)

    grad_qdown = grad_first[:, :part]
    kv_cols_grad = grad_first[:, part:]
    pieces = []
    for k in ORDER:
        size = kv_cols_grad.shape[0] // 4
        sent = lax.dynamic_slice_in_dim(kv_cols_grad, (me ^ k) * size, size, 0)
        pieces.append(lax.ppermute(sent, "mp", [(i, i ^ k) for i in range(4)]) if k else sent)
    grad_kv = to_natural(jnp.concatenate(pieces, 1), 1)

    def put_natural(pieces):
        return run(
            functools.partial(natural_body, micro, quarter),
            ids,
            pieces,
            [whole((micro, rows, width), LOW)],
            name="natural",
        )[0]

    part_sum = inner_cols(dfirst.reshape(micro * rows, -1), first_weights).reshape(micro, rows, width)
    dh1 = sum_mp(part_sum[:, half:].astype(LOW), part_sum[:, :half])
    gain1 = jnp.sum(dh1 * n1, axis=(0, 1))
    dx = (dy + norm_backward(dh1 * gain1_row, n1, inv1)).astype(LOW)
    input_grads = put_natural(gather_mp(dx))

    ffn = sum_mp(ffn_send, ffn_keep)
    layer_out = put_natural(gather_mp((y + ffn).astype(LOW)))

    gains = jnp.concatenate(
        [gain1.reshape(seq, -1), gain2.reshape(seq, -1), gain_c.reshape(seq, -1)], axis=1
    )
    gains = gains + lax.ppermute(gains, "mp", CORE)
    gains = gains + lax.ppermute(gains, "mp", CROSS)
    gain_sum = lax.dynamic_index_in_dim(gains, at, 0, keepdims=False)
    for k in range(1, seq):
        gain_sum = gain_sum + lax.ppermute(
            lax.dynamic_index_in_dim(gains, at ^ k, 0, keepdims=False),
            "seq",
            [(i, i ^ k) for i in range(seq)],
        )
    return (
        layer_out,
        input_grads,
        gain_sum[:wide],
        grad_qdown,
        gain_sum[2 * wide :],
        grad_qup,
        grad_kv,
        grad_out,
        gain_sum[wide : 2 * wide],
        grad_gate,
        grad_up,
        grad_down,
    )


def solution(mesh):
    placed = (
        P(None, "seq", None),
        P(),
        P(),
        P(None, "mp"),
        P(),
        P(None, "mp"),
        P(),
        P("mp", None),
        P(),
        P(None, "mp"),
        P(None, "mp"),
        P("mp", None),
        P(None, "seq", None),
    )
    return jax.shard_map(
        local,
        mesh=mesh,
        in_specs=placed,
        out_specs=(
            P(None, "seq", None),
            P(None, "seq", None),
            P("seq"),
            P("seq", "mp"),
            P("seq"),
            P("seq", "mp"),
            P(("seq", "mp"), None),
            P("mp", "seq"),
            P("seq"),
            P("seq", "mp"),
            P("seq", "mp"),
            P("mp", "seq"),
        ),
        check_vma=False,
    )
```

```python
import functools

import jax
import jax.numpy as jnp
from jax import lax
from jax.experimental import pallas as pl
from jax.experimental.pallas import tpu as pltpu
from jax.sharding import PartitionSpec as P

EPS = 1e-06
BASE = 10000.0
NEG_LARGE = -1e30
LOW = jnp.bfloat16
F32 = jnp.float32
ORDER = (0, 2, 1, 3)
CORE = [(i, i ^ 1) for i in range(4)]
CROSS = [(i, i ^ 2) for i in range(4)]


def inverse_rms(values):
    return lax.rsqrt(jnp.mean(values * values, axis=-1, keepdims=True) + EPS)


def norm_backward(grad_hat, normed, inverse):
    return inverse * (grad_hat - normed * jnp.mean(grad_hat * normed, axis=-1, keepdims=True))


def dot(left, right):
    return jnp.dot(left, right, preferred_element_type=F32)


def inner_rows(left, right):
    return lax.dot_general(left, right, (((0,), (0,)), ((), ())), preferred_element_type=F32)


def inner_cols(left, right):
    return lax.dot_general(left, right, (((1,), (1,)), ((), ())), preferred_element_type=F32)


def documents(lengths_row, rows):
    first_end = lengths_row[0]
    second_end = first_end + lengths_row[1]
    doc_ids = (rows >= first_end).astype(jnp.int32) + (rows >= second_end).astype(jnp.int32)
    starts = jnp.where(rows >= second_end, second_end, jnp.where(rows >= first_end, first_end, 0))
    return (doc_ids, rows - starts)


def rotation(positions, head_dim):
    half = head_dim // 2
    freqs = BASE ** (-2.0 * jnp.arange(half, dtype=F32) / head_dim)
    angles = positions.astype(F32)[:, None] * freqs[None, :]
    return (jnp.cos(angles), jnp.sin(angles))


def rotate(values, cosine, sine):
    half = values.shape[-1] // 2
    first = values[..., :half]
    second = values[..., half:]
    return jnp.concatenate(
        [first * cosine - second * sine, second * cosine + first * sine], axis=-1
    )


def unrotate(grads, cosine, sine):
    return rotate(grads, cosine, -sine)


def in_vmem():
    return pl.BlockSpec(memory_space=pltpu.VMEM)


def whole(shape, dtype):
    return jax.ShapeDtypeStruct(shape, dtype)


def run(body, ids, args, outs, after=(), scratch=(), name=None, limit=40):
    args, after = list(args), list(after)

    def without(*refs):
        body(*refs[: 1 + len(args)], *refs[1 + len(args) + len(after) :])

    return pl.pallas_call(
        without,
        grid_spec=pltpu.PrefetchScalarGridSpec(
            num_scalar_prefetch=1,
            grid=(1,),
            in_specs=[in_vmem()] * len(args) + [pl.BlockSpec(memory_space=pl.ANY)] * len(after),
            out_specs=[in_vmem()] * len(outs),
            scratch_shapes=list(scratch),
        ),
        out_shape=list(outs),
        cost_estimate=pl.CostEstimate(flops=1000, bytes_accessed=1000, transcendentals=0),
        compiler_params=pltpu.CompilerParams(vmem_limit_bytes=limit << 20),
        name=name,
    )(ids, *args, *after)


def side_columns(source, mine, theirs, side):
    line, _, wide = mine.shape
    rows = theirs.shape[1]
    for z in range(line):
        mine[z] = source[:, pl.ds(pl.multiple_of((2 * z + side) * wide, wide), wide)]
        theirs[z] = source[:rows, pl.ds(pl.multiple_of((2 * z + 1 - side) * wide, wide), wide)]


def first_body(m, quarter, ids, x_ref, gain, q_down, kv_proj, cos, sin, c, kv, h1, mine, theirs):
    blocks = [
        x_ref[m, pl.ds(pl.multiple_of((ids[0] ^ k) * quarter, quarter), quarter), :] for k in ORDER
    ]
    x = jnp.concatenate(blocks, 0).astype(F32)
    low = (x * inverse_rms(x) * gain[...]).astype(LOW)
    h1[...] = low
    half = 2 * quarter
    pair = dot(low[:half], kv_proj[...])
    wide = kv_proj.shape[1] // 2
    kv[:, :wide] = rotate(pair[:, :wide], cos[:half], sin[:half]).astype(LOW)
    kv[:, wide:] = pair[:, wide:].astype(LOW)
    c[...] = dot(low, q_down[...]).astype(LOW)
    if mine is not None:
        side_columns(h1, mine, theirs, ids[1])


def cotangent_body(micro, quarter, ids, z_ref, w_down, dhid, dz, *sides):
    for m in range(micro):
        blocks = [
            z_ref[m, pl.ds(pl.multiple_of((ids[0] ^ k) * quarter, quarter), quarter), :]
            for k in ORDER
        ]
        dz[m] = jnp.concatenate(blocks, 0)
        if sides:
            side_columns(dz.at[m], sides[0].at[m], sides[1].at[m], ids[1])
        dhid[m] = inner_cols(dz[m], w_down[...])


def attend_body(
    scale, ids, c0, c1, c2, gain, q_up, cos, sin, kv, key_ids, row_ids, row_starts, out_proj,
    qn, q, o, lse, send, keep, mine, theirs,
):
    rows = qn.shape[0]
    quarter = rows // 4
    part = c0.shape[1]
    wide = q.shape[2]
    got = c1[...]
    pair = jnp.concatenate(
        [got[quarter : 2 * quarter], got[:quarter], got[3 * quarter :], got[2 * quarter : 3 * quarter]],
        0,
    )
    far = jnp.concatenate([c2[2 * quarter :], c2[: 2 * quarter]], 0)
    c = jnp.concatenate([c0[...], pair, far], 1).astype(F32)
    chat = c * inverse_rms(c)
    for k, xor in enumerate(ORDER):
        columns = pl.ds(pl.multiple_of((ids[0] ^ xor) * part, part), part)
        qn[:, columns] = (chat[:, k * part : (k + 1) * part] * gain[:, columns]).astype(LOW)
    if mine is not None:
        side_columns(qn, mine, theirs, ids[1])
    bias = jnp.where(
        (key_ids[...] >= row_starts[...]) & (key_ids[...] <= row_ids[...]), 0.0, NEG_LARGE
    )
    low = qn[...]
    keys, values = kv[:, :wide], kv[:, wide:]
    for h in range(q.shape[0]):
        pre = dot(low, q_up[:, h * wide : (h + 1) * wide])
        q_h = (rotate(pre, cos[...], sin[...]) * scale).astype(LOW)
        q[h] = q_h
        scores = inner_cols(q_h, keys) + bias
        top = jnp.max(scores, axis=-1, keepdims=True)
        probs = jnp.exp(scores - top)
        total = jnp.sum(probs, axis=-1, keepdims=True)
        out = dot(probs.astype(LOW), values) / total
        o[:, h * wide : (h + 1) * wide] = out.astype(LOW)
        log_total = jnp.broadcast_to(top + jnp.log(total), (rows, 128))
        lse[h : h + 1, :] = jnp.transpose(log_total)[:1]
    half = 2 * quarter
    send[...] = dot(o[half:, :], out_proj[...]).astype(LOW)
    keep[...] = dot(o[:half, :], out_proj[...])


def forward_body(m, ids, a0, a1, a2, w_gate, w_up, dhid, h2, hid, dg, du, mine, theirs):
    h2[...] = jnp.concatenate([a0[...], a1[...], a2[...]], 0)
    if mine is not None:
        side_columns(h2, mine, theirs, ids[1])
    low = h2[...]
    g = dot(low, w_gate[...])
    u = dot(low, w_up[...])
    sig = jax.nn.sigmoid(g)
    swish = g * sig
    hid[...] = (swish * u).astype(LOW)
    back = dhid[m]
    dg[...] = (back * u * sig * (1.0 + g * (1.0 - sig))).astype(LOW)
    du[...] = (back * swish).astype(LOW)


def hidden_back_body(micro, ids, *refs):
    dgs, dus = refs[:micro], refs[micro : 2 * micro]
    hids = refs[2 * micro : 3 * micro]
    w_gate, w_up, w_down, send, keep, out_send, out_keep = refs[3 * micro :]
    half = send.shape[1]
    every = lambda parts: jnp.concatenate([part[...] for part in parts], 0)
    rows = 2 * half
    total = inner_cols(every(dgs), w_gate[...]) + inner_cols(every(dus), w_up[...])
    for m in range(micro):
        send[m] = total[m * rows + half : (m + 1) * rows].astype(LOW)
        keep[m] = total[m * rows : m * rows + half]
    total = dot(every(hids), w_down[...])
    for m in range(micro):
        out_send[m] = total[m * rows + half : (m + 1) * rows].astype(LOW)
        out_keep[m] = total[m * rows : m * rows + half]


def pick(ref, lead):
    return ref if lead is None else ref.at[lead]


def block_body(terms, lefts, rights, extra, from_side, turned, ids, *refs):
    left, refs = refs[:lefts], refs[lefts:]
    right, refs = refs[:rights], refs[rights:]
    added, out = refs[: extra + from_side], refs[-1]
    total = None
    for a, a_lead, b, b_lead, first, count in terms:
        rows = pick(right[b], b_lead)[first : first + count, :]
        term = inner_rows(pick(left[a], a_lead)[ids[0]], rows)
        total = term if total is None else total + term
    for i, ref in enumerate(added):
        total = total + (ref[ids[0]] if i >= extra else ref[...]).astype(F32)
    out[...] = jnp.transpose(total) if turned else total.astype(out.dtype)


def side_sum_body(terms, lefts, ids, *refs):
    left, right, out = refs[:lefts], refs[lefts:-1], refs[-1]
    for z in range(out.shape[0]):
        total = None
        for a, a_lead, b, b_lead, first, count in terms:
            rows = pick(right[b], b_lead)[first : first + count, :]
            term = inner_rows(pick(left[a], a_lead)[z], rows)
            total = term if total is None else total + term
        out[z] = total.astype(out.dtype)


def attend_back_body(
    scale, micro, chunk, ids, a0, a1, a2, out_proj, q_up, key_ids, *refs
):
    per = 7
    groups = [refs[m * per : (m + 1) * per] for m in range(micro)]
    dyl_out, dqp, send, keep, kv_send, kv_keep = refs[micro * per : micro * per + 6]
    dq_acc, do_acc, delta_acc = refs[-3:]
    sides = refs[micro * per + 6 : -3]
    for m in range(micro):
        q, kv, o, lse, row_ids, cos, sin = groups[m]
        heads, rows, wide = q.shape
        half_rows = rows // 2
        dyl = jnp.concatenate([a0[m], a1[m], a2[m]], 0)
        dyl_out[m] = dyl
        if sides:
            side_columns(dyl_out.at[m], sides[0].at[m], sides[1].at[m], ids[1])
        for h in range(heads):
            do = inner_cols(dyl, out_proj[h * wide : (h + 1) * wide, :]).astype(LOW)
            do_acc[h] = do
            delta = jnp.sum(
                do.astype(F32) * o[:, h * wide : (h + 1) * wide].astype(F32), axis=-1, keepdims=True
            )
            delta_acc[h] = jnp.transpose(jnp.broadcast_to(delta, (rows, 128)))[:8]
            dq_acc[h] = jnp.zeros((rows, wide), F32)
        count = kv.shape[0] // 2 // chunk
        for part, out in ((0, kv_keep), (1, kv_send)):

            def one(i, carry):
                base = pl.multiple_of((part * count + i) * chunk, chunk)
                keys = kv[pl.ds(base, chunk), :wide]
                values = kv[pl.ds(base, chunk), wide:]
                at = key_ids[pl.ds(base, chunk), :]
                bias = jnp.where((at >= row_ids[1:2, :]) & (at <= row_ids[0:1, :]), 0.0, NEG_LARGE)

                def head(h, sums):
                    dk, dv = sums
                    q_h, do_h = q[h], do_acc[h]
                    probs = jnp.exp(inner_cols(keys, q_h) + bias - lse[pl.ds(h, 1), :])
                    back = inner_cols(values, do_h) - delta_acc[h][:1]
                    ds = (probs * back).astype(LOW)
                    dv = dv + dot(probs.astype(LOW), do_h)
                    dk = dk + dot(ds, q_h)
                    dq_acc[h] = dq_acc[h] + inner_rows(ds, keys)
                    return dk, dv

                zero = jnp.zeros((chunk, wide), F32)
                dk, dv = lax.fori_loop(0, heads, head, (zero, zero))
                place = pl.ds(pl.multiple_of(i * chunk, chunk), chunk)
                out[m, place, :wide] = dk.astype(out.dtype)
                out[m, place, wide:] = dv.astype(out.dtype)
                return carry

            if count == 1:
                one(0, 0)
            else:
                lax.fori_loop(0, count, one, 0)
        for h in range(heads):
            dq = unrotate(dq_acc[h] * scale, cos[...], sin[...])
            dqp[m, :, h * wide : (h + 1) * wide] = dq.astype(LOW)
        low = dqp[m]
        send[m] = inner_cols(low[half_rows:], q_up[...]).astype(LOW)
        keep[m] = inner_cols(low[:half_rows], q_up[...])


def natural_body(micro, quarter, ids, a0, a1, a2, out):
    for m in range(micro):
        pieces = (a0[m], a1[m], a2[m, :quarter, :], a2[m, quarter:, :])
        for k, piece in zip(ORDER, pieces):
            out[m, pl.ds(pl.multiple_of((ids[0] ^ k) * quarter, quarter), quarter), :] = piece


class Wire:
    def __init__(self, sends, recvs):
        self.sends, self.recvs, self.used = sends, recvs, 0
        self.seq, self.mp = lax.axis_index("seq"), lax.axis_index("mp")
        self.place, self.side = self.seq // 2, self.seq % 2
        core, cross = self.mp % 2, self.mp // 2
        self.blocks = (
            self.mp, 2 * (1 - cross) + core, 2 * cross + 1 - core, 2 * (1 - cross) + 1 - core
        )
        self.core, self.cross = {"mp": self.blocks[2]}, {"mp": self.blocks[1]}
        self.beside = {"seq": self.seq + 1 - 2 * self.side}
        self.up, self.down = self.along(1), self.along(-1)

    def along(self, far):
        return {"seq": 2 * ((self.place + far + 4) % 4) + self.side}

    def copy(self, source, target, device):
        at = self.used
        self.used += 1
        return pltpu.make_async_remote_copy(
            src_ref=source, dst_ref=target, send_sem=self.sends.at[at], recv_sem=self.recvs.at[at],
            device_id=device, device_id_type=pl.DeviceIdType.MESH,
        )

    def send(self, source, target, device):
        made = self.copy(source, target, device)
        made.start()
        return made

    def greet(self, line, far=1, diagonal=False):
        barrier = pltpu.get_barrier_semaphore()
        devices = [self.core, self.cross, self.beside]
        if diagonal:
            devices.append({"mp": self.blocks[3]})
        for device in devices:
            pl.semaphore_signal(barrier, 1, device_id=device, device_id_type=pl.DeviceIdType.MESH)
        for d in range(1, far + 1):
            for way, there in ((1, self.place < line - d), (-1, self.place >= d)):

                @pl.when(there)
                def _():
                    pl.semaphore_signal(
                        barrier, 1, device_id={"seq": self.seq + 2 * way * d},
                        device_id_type=pl.DeviceIdType.MESH,
                    )
        below, above = jnp.minimum(self.place, far), jnp.minimum(line - 1 - self.place, far)
        pl.semaphore_wait(barrier, len(devices) + below + above)


def along(pieces, axis):
    return pieces[0] if len(pieces) == 1 else jnp.concatenate(pieces, axis)


def pair_places(first, second, quarter, axis):
    shape = (2 * quarter, 1) if axis == 0 else (1, 2 * quarter)
    index = lax.broadcasted_iota(jnp.int32, shape, axis)
    return jnp.where(index < quarter, first * quarter + index, (second - 1) * quarter + index)


def row_places(wire, quarter, axis):
    b = wire.blocks
    pieces = [pair_places(b[i], b[i + 1], quarter, axis) for i in (0, 2)]
    return wire.seq * (4 * quarter) + along(pieces, axis)


def key_places(wire, quarter, line, axis, cores):
    pieces = []
    for core in cores:
        for side in (wire.side, 1 - wire.side):
            for d in range(line):
                base = ((wire.place - d) * 2 + side) * (4 * quarter)
                b = wire.blocks[2 * core : 2 * core + 2]
                pieces.append(base + pair_places(b[0], b[1], quarter, axis))
    return along(pieces, axis)


def sequence_starts(lengths, m, places):
    first_end = lengths[m, 0]
    second_end = first_end + lengths[m, 1]
    return jnp.where(
        places >= second_end, second_end, jnp.where(places >= first_end, first_end, 0)
    )


class LineSum:
    def __init__(self, wire, term, room, rows, columns, keep):
        got, out = room
        view = lambda ref, i: ref.at[i, :rows, :columns]
        self.place, self.term, self.keep = wire.place, term, keep
        self.got = [view(got, i) for i in range(5)]
        self.out = [view(out, i) for i in range(2)]
        one, two_up, two_down, three_up, three_down = self.got
        a, b = self.out
        self.one = wire.copy(a, one, wire.up), wire.copy(a, one, wire.down)
        self.two = wire.copy(b, two_up, wire.up), wire.copy(b, two_down, wire.down)
        self.three = wire.copy(a, three_up, wire.up), wire.copy(b, three_down, wire.down)

    def clear(self):
        place = self.place
        for ref, empty in zip(
            self.got, ((place == 0) | (place == 3),) * 3 + (place == 0, place == 3)
        ):

            @pl.when(empty)
            def _(ref=ref):
                ref[...] = jnp.zeros(ref.shape, ref.dtype)

    def step1(self):
        place = self.place

        @pl.when((place == 0) | (place == 3))
        def _():
            self.out[0][...] = self.term(3 - place).astype(LOW)

        pl.when(place == 0)(self.one[0].start)
        pl.when(place == 3)(self.one[1].start)

    def step2(self):
        place = self.place
        pl.when(place == 1)(self.one[0].wait_recv)
        pl.when(place == 2)(self.one[1].wait_recv)
        self.out[1][...] = (
            self.term((place + 2) % 4) + self.got[0][...].astype(F32)
        ).astype(LOW)
        pl.when(place <= 1)(self.two[0].start)
        pl.when(place >= 2)(self.two[1].start)

    def step3(self):
        place = self.place

        @pl.when((place == 1) | (place == 2))
        def _():
            self.two[0].wait_recv()
            self.two[1].wait_recv()

        pl.when(place == 0)(self.one[0].wait_send)
        pl.when(place == 3)(self.one[1].wait_send)

        @pl.when(place <= 2)
        def _():
            self.out[0][...] = (self.term(place + 1) + self.got[1][...].astype(F32)).astype(LOW)
            self.three[0].start()

        pl.when(place <= 1)(self.two[0].wait_send)
        pl.when(place >= 2)(self.two[1].wait_send)

        @pl.when(place >= 1)
        def _():
            self.out[1][...] = (self.term(place - 1) + self.got[2][...].astype(F32)).astype(LOW)
            self.three[1].start()

    def finish(self):
        place = self.place
        pl.when(place >= 1)(self.three[0].wait_recv)
        pl.when(place <= 2)(self.three[1].wait_recv)
        self.keep(
            self.term(place) + self.got[3][...].astype(F32) + self.got[4][...].astype(F32)
        )

    def settle(self):
        place = self.place
        pl.when(place <= 2)(self.three[0].wait_send)
        pl.when(place >= 1)(self.three[1].wait_send)


class Desk:
    def __init__(self, first, loads, stores):
        self.loads, self.stores, self.stored = loads, stores, []
        for _, made in first:
            made.start()
        self.waiting = list(first)

    def more(self):
        for _, made in self.loads:
            made.start()
        self.waiting += self.loads

    def arrive(self, *refs):
        rest = []
        for ref, made in self.waiting:
            if not refs or any(ref is other for other in refs):
                made.wait()
            else:
                rest.append((ref, made))
        self.waiting = rest

    def flush(self, *refs):
        rest = []
        for ref, made in self.stores:
            if not refs or any(ref is other for other in refs):
                made.start()
                self.stored.append(made)
            else:
                rest.append((ref, made))
        self.stores = rest

    def close(self):
        self.flush()
        for made in self.stored:
            made.wait()


SPACES = (pl.ANY, pltpu.VMEM, pltpu.SMEM, pl.ANY, pl.ANY)


def mesh_run(body, args, outs, scratch, number, name, limit, sends):
    late_in = [i for i, (kind, _) in enumerate(args) if kind >= 3]
    late_out = [i for i, (kind, _) in enumerate(outs) if kind == 3]

    def whole_body(*refs):
        refs = list(refs)
        take = lambda n: [refs.pop(0) for _ in range(n)]
        given, results, rooms_in, rooms_out = (
            take(len(args)), take(len(outs)), take(len(late_in)), take(len(late_out))
        )
        load_sems, store_sems = take(2)
        first, loads, stores = [], [], []
        for n, (i, room) in enumerate(zip(late_in, rooms_in)):
            made = pltpu.make_async_copy(given[i], room, load_sems.at[n])
            (first if args[i][0] == 3 else loads).append((room, made))
            given[i] = room
        for n, (i, room) in enumerate(zip(late_out, rooms_out)):
            stores.append((room, pltpu.make_async_copy(room, results[i], store_sems.at[n])))
            results[i] = room
        desk = Desk(first, loads, stores)
        body(desk, *given, *results, *refs)
        desk.close()

    room = lambda a: pltpu.VMEM(a.shape, a.dtype)
    return pl.pallas_call(
        whole_body,
        in_specs=[pl.BlockSpec(memory_space=SPACES[kind]) for kind, _ in args],
        out_specs=[pl.BlockSpec(memory_space=SPACES[kind]) for kind, _ in outs],
        out_shape=[shape for _, shape in outs],
        scratch_shapes=[
            *[room(args[i][1]) for i in late_in], *[room(outs[i][1]) for i in late_out],
            pltpu.SemaphoreType.DMA((max(1, len(late_in)),)),
            pltpu.SemaphoreType.DMA((max(1, len(late_out)),)),
            *scratch, pltpu.SemaphoreType.DMA((sends,)), pltpu.SemaphoreType.DMA((sends,)),
        ],
        cost_estimate=pl.CostEstimate(flops=1000, bytes_accessed=1000, transcendentals=0),
        compiler_params=pltpu.CompilerParams(
            collective_id=number, has_side_effects=True, vmem_limit_bytes=limit << 20
        ),
        name=name,
    )(*[array for _, array in args])


def attend_back_one(
    scale, keys_at, rows_at, starts, dyl, out_proj, q_up, q, kv, o, lse, cos, sin,
    dqp, send, keep, kv_send, kv_keep, dq_acc, between=None,
):
    heads, rows, wide = q.shape
    half_rows = rows // 2
    low = dyl[...]
    grads, deltas = [], []
    for h in range(heads):
        columns = slice(h * wide, (h + 1) * wide)
        do = inner_cols(low, out_proj[columns, :]).astype(LOW)
        grads.append(do)
        delta = jnp.sum(do.astype(F32) * o[:, columns].astype(F32), axis=-1, keepdims=True)
        deltas.append(jnp.transpose(jnp.broadcast_to(delta, (rows, 128)))[:1])
    do_all, delta_all = jnp.concatenate(grads, 0), jnp.concatenate(deltas, 1)
    q_all = q[...].reshape(heads * rows, wide)
    lse_all = jnp.concatenate([lse[h : h + 1, :] for h in range(heads)], 1)
    dq_acc[...] = jnp.zeros(dq_acc.shape, F32)
    count = kv.shape[0] // 2
    chunk = min(256, count)
    for part, out in ((1, kv_send), (0, kv_keep)):
        for first in range(0, count, chunk):
            span = slice(part * count + first, part * count + first + chunk)
            keys, values = kv[span, :wide], kv[span, wide:]
            at = keys_at[part][first : first + chunk]
            bias = jnp.where((at >= starts) & (at <= rows_at), 0.0, NEG_LARGE)
            scores = inner_cols(keys, q_all) + jnp.concatenate([bias] * heads, 1)
            probs = jnp.exp(scores - lse_all)
            ds = (probs * (inner_cols(values, do_all) - delta_all)).astype(LOW)
            spot = slice(first, first + chunk)
            out[spot, :wide] = dot(ds, q_all).astype(out.dtype)
            out[spot, wide:] = dot(probs.astype(LOW), do_all).astype(out.dtype)
            dq_acc[...] += inner_rows(ds, keys)
        if part and between is not None:
            between()
    for h in range(heads):
        dq = unrotate(dq_acc[h * rows : (h + 1) * rows, :] * scale, cos, sin)
        dqp[:, h * wide : (h + 1) * wide] = dq.astype(LOW)
    total = inner_cols(dqp[...], q_up[...])
    send[...] = total[half_rows:].astype(LOW)
    keep[...] = total[:half_rows]


def mean_of(values):
    return jnp.mean(values, axis=-1, keepdims=True)


def terms_sum(pairs):
    total = None
    for left, right in pairs:
        term = inner_rows(left, right)
        total = term if total is None else total + term
    return total


def back1_body(quarter, desk, *refs):
    refs = list(refs)
    take = lambda n: [refs.pop(0) for _ in range(n)]
    w_gate, w_up, w_down, cotangent, h2, dhid, n2, inv2, gain2, dz_got, dz_far, y = take(12)
    grad, dy, gain_sum, dyl, dyl_mine, dyl_theirs, layer_own = take(7)
    hid, dg, du, h2_mine = (take(2) for _ in range(4))
    h2_got, h2_far, dg_other = take(2), take(2), take(2)
    gate_w, up_w, hid_other0, hid_other1, h2_theirs, got, out = take(7)
    send, kept, core_got, cross_out, cross_got, loads = take(6)
    ffn_send, ffn_kept, ffn_got, ffn_out, ffn_back = take(5)
    early_got, early_out, early_sum, early_send, early_back, dz, row_loads = take(7)
    wire = Wire(*take(2))
    half, rows = 2 * quarter, 4 * quarter
    ahead = early_send.shape[1]
    block = early_send.shape[0]
    middle = ahead + (gate_w.shape[1] - ahead) // 2
    columns_of = [slice(0, ahead), slice(ahead, middle), slice(middle, gate_w.shape[1])]
    in_weights = []
    for i, columns in enumerate(columns_of):
        for j, (source, target) in enumerate(((w_gate, gate_w), (w_up, up_w))):
            in_weights.append(pltpu.make_async_copy(
                source.at[:, columns], target.at[:, columns], loads.at[2 * i + j]
            ))
    for made in in_weights[:2]:
        made.start()
    hid_other = (hid_other0, hid_other1)
    hid_all = (*(a.at[:, ahead:] for a in hid), *hid_other)

    def term(z):
        columns = pl.ds(pl.multiple_of((2 * z + wire.side) * block, block), block)
        return terms_sum(halves_terms(
            [dz[m, :, columns] for m in range(2)], [dz_got[m, z] for m in range(2)],
            [dz_far[m, z] for m in range(2)], hid_all, half))

    def early_term(z):
        columns = pl.ds(pl.multiple_of(z * 2 * block, 2 * block), 2 * block)
        return terms_sum([(dz[m, :, columns], hid[m][:, :ahead]) for m in range(2)])

    def keep(total):
        grad[ahead:, :] = jnp.transpose(total)

    def early_keep(total):
        early_sum[0], early_sum[1] = total[:block], total[block:]

    chain = LineSum(wire, term, (got, out), block, grad.shape[0] - ahead, keep)
    early = LineSum(wire, early_term, (early_got, early_out), 2 * block, ahead, early_keep)
    chain.clear()
    early.clear()
    wire.greet(4)
    desk.arrive(h2)
    for made in in_weights[2:]:
        made.start()
    desk.more()
    in_dz = []
    for m in range(2):
        for k in range(4):
            at = pl.ds(pl.multiple_of(wire.blocks[k] * quarter, quarter), quarter)
            in_dz.append(pltpu.make_async_copy(
                cotangent.at[m, at, :], dz.at[m, k * quarter : (k + 1) * quarter, :],
                row_loads.at[4 * m + k],
            ))
            in_dz[-1].start()
    for m in range(2):
        side_columns(h2.at[m], h2_mine[m], h2_theirs.at[m], wire.side)
    y_h2 = [wire.send(h2_theirs.at[m], h2_got[m], wire.beside) for m in range(2)]
    y_hid = []

    def columns_forward(m, i):
        columns = columns_of[i]
        if m == 0:
            for made in in_weights[2 * i : 2 * i + 2]:
                made.wait()
        g = dot(h2[m], gate_w[:, columns])
        u = dot(h2[m], up_w[:, columns])
        sig = jax.nn.sigmoid(g)
        swish = g * sig
        hid[m][:, columns] = (swish * u).astype(LOW)
        if i:
            there = hid_other[m].at[:, columns.start - ahead : columns.stop - ahead]
            y_hid.append(wire.send(hid[m].at[:, columns], there, wire.beside))
        if m == 0 and i == 0:
            desk.arrive()
        back = dhid[m, :, columns]
        dg[m][:, columns] = (back * u * sig * (1.0 + g * (1.0 - sig))).astype(LOW)
        du[m][:, columns] = (back * swish).astype(LOW)

    for m in range(2):
        columns_forward(m, 0)
    for made in in_dz:
        made.wait()
    early.step1()
    for m in range(2):
        columns_forward(m, 1)
        if m == 1:
            early.step2()
        columns_forward(m, 2)
        desk.flush(dg[m], du[m], hid[m], h2_mine[m])
    both = lambda pair: jnp.concatenate([pair[0][...], pair[1][...]], 0)
    total = inner_cols(both(dg), gate_w[...]) + inner_cols(both(du), up_w[...])
    for m in range(2):
        send[m] = total[m * rows + half : (m + 1) * rows].astype(LOW)
        kept[m] = total[m * rows : m * rows + half]
    sums = RowSum(wire, send, kept, core_got, cross_out, cross_got, quarter)
    sums.core.start()
    wide = gate_w.shape[1]
    rest = w_down.shape[1] - wide
    downs = [gate_w.at[:wide, :], up_w.at[:wide, :rest]]
    in_down = [
        pltpu.make_async_copy(w_down.at[:, :wide], downs[0], loads.at[0]),
        pltpu.make_async_copy(w_down.at[:, wide:], downs[1], loads.at[1]),
    ]
    for made in in_down:
        made.start()
    early.step3()
    sums.pass_on()
    for made in y_hid:
        made.wait_recv()
    y_next = y_h2 + [wire.send(dg[m], dg_other[m], wire.beside) for m in range(2)]
    chain.step1()
    for made in in_down:
        made.wait()
    low = both(hid)
    ffn_sum = RowSum(wire, ffn_send, ffn_kept, ffn_got, ffn_out, ffn_back, quarter)
    for columns, part in ((slice(0, wide), downs[0]), (slice(wide, None), downs[1])):
        total = dot(low, part[...])
        for m in range(2):
            ffn_send[m, :, columns] = total[m * rows + half : (m + 1) * rows].astype(LOW)
            ffn_kept[m, :, columns] = total[m * rows : m * rows + half].astype(LOW)
    ffn_sum.core.start()
    early.finish()
    early_send[...] = early_sum[1 - wire.side].astype(LOW)
    y_early = wire.send(early_send, early_back, wire.beside)
    dh2 = sums.result()
    gain_sum[...] = jnp.sum(jnp.sum(dh2 * n2[...], axis=0), axis=0, keepdims=True)
    back = dh2 * gain2[...]
    grad_y = dz[:, :quarter, :].astype(F32) + inv2[...] * (
        back - n2[...] * mean_of(back * n2[...])
    )
    dy[...] = grad_y
    dyl[:, :quarter, :] = grad_y.astype(LOW)
    cross_dyl = wire.send(dyl.at[:, :quarter, :], dyl.at[:, quarter:half, :], wire.cross)
    ffn_sum.pass_on()
    chain.step2()
    cross_dyl.wait_recv()
    core_dyl = wire.send(dyl.at[:, :half, :], dyl.at[:, half:, :], wire.core)
    core_h2 = []
    for i in range(2):
        y_next[i].wait_recv()
        core_h2.append(wire.send(h2_got[i], h2_far[i], wire.core))
    core_dyl.wait_recv()
    for m in range(2):
        side_columns(dyl.at[m], dyl_mine.at[m], dyl_theirs.at[m], wire.side)
    desk.flush(dy, dyl, dyl_mine, dyl_theirs)
    chain.step3()
    layer_own[...] = (y[...] + ffn_sum.result()).astype(LOW)
    y_early.wait_recv()
    grad[:ahead, :] = jnp.transpose(early_sum[wire.side] + early_back[...].astype(F32))
    for made in y_next[2:] + core_h2:
        made.wait_recv()
    chain.finish()
    for made in [*y_hid, cross_dyl, core_dyl, *y_next, *core_h2, y_early]:
        made.wait_send()
    sums.end()
    ffn_sum.end()
    early.settle()
    chain.settle()


class Share:
    def __init__(self, wire, out, quarter):
        spot = lambda block: out.at[:, pl.ds(pl.multiple_of(block * quarter, quarter), quarter), :]
        own, near = spot(wire.blocks[0]), spot(wire.blocks[1])
        self.own = own
        self.first = wire.copy(own, own, wire.cross)
        self.rest = wire.copy(own, own, wire.core), wire.copy(near, near, wire.core)

    def begin(self, value):
        self.own[...] = value
        self.first.start()
        self.rest[0].start()

    def forward(self):
        self.first.wait_recv()
        self.rest[1].start()

    def end(self):
        for made in self.rest:
            made.wait_recv()
        for made in (self.first, *self.rest):
            made.wait_send()


class RowSum:
    def __init__(self, wire, send, kept, got, cross_out, cross_got, quarter, parts=1):
        self.kept, self.got, self.quarter = kept, got, quarter
        self.out, self.back = cross_out, cross_got
        self.core = wire.copy(send, got, wire.core)
        size = quarter // parts
        self.spans = [slice(i * size, (i + 1) * size) for i in range(parts)]
        self.cross = [
            wire.copy(cross_out.at[:, span, :], cross_got.at[:, span, :], wire.cross)
            for span in self.spans
        ]

    def pass_on(self):
        self.core.wait_recv()
        for span, made in zip(self.spans, self.cross):
            rest = slice(self.quarter + span.start, self.quarter + span.stop)
            self.out[:, span, :] = (
                self.kept[:, rest, :] + self.got[:, rest, :].astype(F32)
            ).astype(LOW)
            made.start()

    def result(self, part=0):
        span = self.spans[part]
        self.cross[part].wait_recv()
        return (
            self.kept[:, span, :] + self.got[:, span, :].astype(F32)
            + self.back[:, span, :].astype(F32)
        )

    def end(self):
        self.core.wait_send()
        for made in self.cross:
            made.wait_send()


def halves_terms(mine, got, far, rights, half):
    pairs = [(mine[m], rights[m][...]) for m in range(2)]
    for m in range(2):
        pairs.append((got[m], rights[2 + m][:half, :]))
        pairs.append((far[m], rights[2 + m][half:, :]))
    return pairs


def back2_body(quarter, scale, desk, *refs):
    refs = list(refs)
    take = lambda n: [refs.pop(0) for _ in range(n)]
    (lengths,) = take(1)
    dg, dg_other, du, h2_mine, h2_got, h2_far = (take(2) for _ in range(6))
    dyl, out_proj, q_up = take(3)
    q, kv, o, lse = (take(2) for _ in range(4))
    cos, sin, chat, inv_c, gain_c, dyl_theirs = take(6)
    qn_theirs, os_far = take(2), take(2)
    grad_gate, grad_up, dfirst, gain_sum, dqp, dyl_got, dyl_far, qup_side = take(8)
    oo = take(2)
    du_other = take(2)
    got_a, out_a, got_b, out_b = take(4)
    dq_acc, dqn_send, dqn_keep, kv_send, kv_keep = take(5)
    dqn_got, dqn_out, dqn_back = take(3)
    kv_got, kv_out, kv_back, side_out, side_got, line_out, line_got, kv_own = take(8)
    both, side_sums = take(2)
    wire = Wire(*take(2))
    half, rows = 2 * quarter, 4 * quarter
    wide = kv_own.shape[2] // 2
    rank = chat.shape[2]
    place = wire.place

    y_du = [wire.copy(du[m], du_other[m], wire.beside) for m in range(2)]

    def chain(rights, grad, room):
        def term(z):
            return terms_sum(halves_terms(
                [a[z] for a in h2_mine], [a[z] for a in h2_got], [a[z] for a in h2_far], rights,
                half))

        def keep(total):
            grad[...] = total

        made = LineSum(wire, term, room, *grad.shape, keep)
        made.clear()
        return made

    gate = chain((*dg, *dg_other), grad_gate, (got_a, out_a))
    up = chain((*du, *du_other), grad_up, (got_b, out_b))
    dqn_sum, core_kv, cross_kv, side_kv, line_kv = [], [], [], [], []
    for m in range(2):
        one = lambda ref: ref.at[m : m + 1]
        dqn_sum.append(RowSum(wire, one(dqn_send), one(dqn_keep), one(dqn_got), one(dqn_out),
                              one(dqn_back), quarter))
        core_kv.append(wire.copy(kv_send.at[m], kv_got.at[m], wire.core))
        cross_kv.append(wire.copy(kv_out.at[m], kv_back.at[m], wire.cross))
        side_kv.append(wire.copy(side_out.at[m], side_got.at[m], wire.beside))
        line_kv.append([
            wire.copy(line_out.at[m, d - 1], line_got.at[m, d - 1], wire.along(-d))
            for d in range(1, 4)
        ])
        for d in range(1, 4):

            @pl.when(place > 3 - d)
            def _(m=m, d=d):
                line_got[m, d - 1] = jnp.zeros(line_got.shape[2:], LOW)

    wire.greet(4, 3)
    desk.arrive(*du)
    for made in y_du:
        made.start()
    desk.arrive(*dg, *dg_other, *h2_mine, *h2_got, *h2_far)
    gate.step1()
    desk.arrive()

    def attend(m, between=None):
        rows_at = row_places(wire, quarter, 1)
        attend_back_one(
            scale, [key_places(wire, quarter, 4, 0, (core,)) for core in range(2)], rows_at,
            sequence_starts(lengths, m, rows_at), dyl.at[m], out_proj, q_up, q[m], kv[m], o[m],
            lse[m], cos[m], sin[m], dqp.at[m], dqn_send.at[m], dqn_keep.at[m], kv_send.at[m],
            kv_keep.at[m], dq_acc, between,
        )
        core_kv[m].start()
        dqn_sum[m].core.start()

    split = lambda ref, m: ref[m].reshape(8, 2, quarter, 2 * wide)

    def kv_cross(m):
        dqn_sum[m].pass_on()
        core_kv[m].wait_recv()
        kv_out[m] = (
            split(kv_keep, m)[:, 1].astype(F32) + split(kv_got, m)[:, 1].astype(F32)
        ).astype(LOW)
        cross_kv[m].start()

    def kv_sum(m, span):
        return (
            split(kv_keep, m)[span, 0].astype(F32) + split(kv_got, m)[span, 0].astype(F32)
            + kv_back[m, span].astype(F32)
        )

    def kv_side(m):
        cross_kv[m].wait_recv()
        side_out[m] = kv_sum(m, slice(4, 8)).astype(LOW)
        side_kv[m].start()

    def kv_line(m):
        side_kv[m].wait_recv()
        own = kv_sum(m, slice(0, 4)) + side_got[m].astype(F32)
        kv_own[m] = own[0]
        for d in range(1, 4):
            line_out[m, d - 1] = own[d].astype(LOW)
            pl.when(place >= d)(line_kv[m][d - 1].start)

    def latent(m):
        dqn = dqn_sum[m].result()[0]
        gain = jnp.sum(dqn * chat[m], axis=0, keepdims=True)
        gain_sum[...] = gain if m == 0 else gain_sum[...] + gain
        back = dqn * gain_c[...]
        both[m, :quarter, :rank] = (
            inv_c[m] * (back - chat[m] * mean_of(back * chat[m]))
        ).astype(LOW)

    y_late = []

    def start_up():
        for made in y_du:
            made.wait_recv()
        y_late.append(wire.send(dyl_theirs, dyl_got, wire.beside))
        y_late.extend(wire.send(os_far[m], oo[m], wire.beside) for m in range(2))
        up.step1()

    attend(0)
    kv_cross(0)
    gate.step2()
    attend(1, start_up)
    gate.step3()
    kv_cross(1)
    kv_side(0)
    latent(0)
    up.step2()
    latent(1)
    for z in range(4):
        side_sums[z] = terms_sum([(qn_theirs[m][z], dqp[m]) for m in range(2)]).astype(LOW)
    kv_side(1)
    side_qup = wire.send(side_sums, qup_side, wire.beside)
    side_dyl, *side_o = y_late
    desk.flush(dqp)
    kv_line(0)
    kv_line(1)
    gate.finish()
    desk.flush(grad_gate)
    for m in range(2):
        for d in range(1, 4):
            pl.when(place <= 3 - d)(line_kv[m][d - 1].wait_recv)
        total = kv_own[m]
        for d in range(1, 4):
            total = total + line_got[m, d - 1].astype(F32)
        both[m, :quarter, rank : rank + wide] = unrotate(
            total[:, :wide], cos[m, :quarter], sin[m, :quarter]
        ).astype(LOW)
        both[m, :quarter, rank + wide :] = total[:, wide:].astype(LOW)
    cross_both = wire.send(both.at[:, :quarter, :], both.at[:, quarter:half, :], wire.cross)
    up.step3()
    cross_both.wait_recv()
    core_both = wire.send(both.at[:, :half, :], both.at[:, half:, :], wire.core)
    side_dyl.wait_recv()
    core_dyl = wire.send(dyl_got, dyl_far, wire.core)
    core_both.wait_recv()
    part = rank // 4
    kv_part = wide // 2
    dfirst[:, :, :part] = both[:, :, pl.ds(pl.multiple_of(wire.mp * part, part), part)]
    dfirst[:, :, part:] = both[
        :, :, pl.ds(pl.multiple_of(rank + wire.mp * kv_part, kv_part), kv_part)
    ]
    up.finish()
    core_dyl.wait_recv()
    for made in (side_qup, *side_o):
        made.wait_recv()
    for made in [*y_du, *core_kv, *cross_kv, *side_kv, cross_both, core_both, side_dyl, core_dyl,
                 side_qup, *side_o]:
        made.wait_send()
    for m in range(2):
        dqn_sum[m].end()
        for d in range(1, 4):
            pl.when(place >= d)(line_kv[m][d - 1].wait_send)
    gate.settle()
    up.settle()


def back3_body(quarter, desk, *refs):
    refs = list(refs)
    take = lambda n: [refs.pop(0) for _ in range(n)]
    dfirst, q_down, kv_proj = take(3)
    h1_mine, h1_theirs, o, oo = (take(2) for _ in range(4))
    dyl_mine, dyl_got, dyl_far = take(3)
    qn_mine = take(2)
    dqp, qup_side, n1, inv1, dy, gain1, gain2_sum, gain_c_sum, layer_own = take(9)
    grad_out, grad_qup, grad_qdown, grad_kv, grad_tokens, gains, layer_out = take(7)
    got_a, out_a, got_b, out_b, got_c, out_c = take(6)
    side_sums, side_got = take(2)
    send, kept, row_got, row_out, row_back = take(5)
    kv_out, kv_got = take(2)
    sums, sums_core, sums_cross, sums_side, sums_line, weights, weight_loads = take(7)
    wire = Wire(*take(2))
    half, rows = 2 * quarter, 4 * quarter
    place = wire.place
    part, kv_part = grad_qdown.shape[1], kv_out.shape[1]
    wire.greet(4, 3, diagonal=True)


    def out_term(z):
        return terms_sum(halves_terms(
            [dyl_mine[m, z] for m in range(2)], [dyl_got[m, z] for m in range(2)],
            [dyl_far[m, z] for m in range(2)], (*o, *oo), half))

    def qup_term(z):
        return terms_sum([(qn_mine[m][z], dqp[m]) for m in range(2)]) + qup_side[z].astype(F32)

    def first_term(z):
        return terms_sum([(h1_mine[m][z], dfirst[m]) for m in range(2)]) + side_got[z].astype(F32)

    def keep_out(total):
        grad_out[...] = jnp.transpose(total)

    def keep_qup(total):
        grad_qup[...] = total

    def keep_first(total):
        grad_qdown[...] = total[:, :part]
        kv_out[...] = total[:, part:]

    out = LineSum(wire, out_term, (got_a, out_a), *grad_out.shape[::-1], keep_out)
    qup = LineSum(wire, qup_term, (got_b, out_b), *grad_qup.shape, keep_qup)
    first = LineSum(wire, first_term, (got_c, out_c), kv_out.shape[0], dfirst.shape[2], keep_first)
    for chain in (out, qup, first):
        chain.clear()
    row_sum = RowSum(wire, send, kept, row_got, row_out, row_back, quarter)
    desk.arrive()
    out.step1()
    desk.more()
    in_weights = [
        pltpu.make_async_copy(q_down, weights.at[:, :part], weight_loads.at[0]),
        pltpu.make_async_copy(
            kv_proj.at[:, pl.ds(pl.multiple_of(wire.mp * kv_part, kv_part), kv_part)],
            weights.at[:, part:], weight_loads.at[1],
        ),
    ]
    for made in in_weights:
        made.start()
    desk.arrive()
    for z in range(4):
        side_sums[z] = terms_sum([(h1_theirs[m][z], dfirst[m]) for m in range(2)]).astype(LOW)
    side_first = wire.send(side_sums, side_got, wire.beside)
    for made in in_weights:
        made.wait()
    term = inner_cols(dfirst[...].reshape(2 * rows, dfirst.shape[2]), weights[...])
    for m in range(2):
        send[m] = term[m * rows + half : (m + 1) * rows].astype(LOW)
        kept[m] = term[m * rows : m * rows + half]
    row_sum.core.start()
    qup.step1()
    row_sum.pass_on()
    layer_share = Share(wire, layer_out, quarter)
    layer_share.begin(layer_own[...])
    out.step2()
    side_first.wait_recv()
    first.step1()
    qup.step2()
    dh1 = row_sum.result()
    gain1_sum = jnp.sum(jnp.sum(dh1 * n1[...], axis=0), axis=0, keepdims=True)
    back = dh1 * gain1[...]
    share = Share(wire, grad_tokens, quarter)
    share.begin(
        (dy[...] + inv1[...] * (back - n1[...] * mean_of(back * n1[...]))).astype(LOW)
    )
    w, r = gain1_sum.shape[1] // 8, gain_c_sum.shape[1] // 8
    for s in range(8):
        sums[s] = jnp.concatenate(
            [gain1_sum[:, s * w : (s + 1) * w], gain2_sum[:, s * w : (s + 1) * w],
             gain_c_sum[:, s * r : (s + 1) * r]], axis=1
        )
    core_sums = wire.send(sums, sums_core, wire.core)
    out.step3()
    core_sums.wait_recv()
    core_sums.wait_send()
    sums[...] = sums[...] + sums_core[...]
    cross_sums = wire.send(sums, sums_cross, wire.cross)
    qup.step3()
    first.step2()
    cross_sums.wait_recv()
    cross_sums.wait_send()
    sums[...] = sums[...] + sums_cross[...]
    side_of = lambda p, s: sums.at[2 * p + s]
    side_sends = [
        wire.send(side_of(p, 1 - wire.side), sums_side.at[p], wire.beside) for p in range(4)
    ]
    layer_share.forward()
    share.forward()
    first.step3()
    for made in side_sends:
        made.wait_recv()
        made.wait_send()
    line_sends = []
    for d in range(1, 4):
        for way, there in ((1, place + d <= 3), (-1, place - d >= 0)):
            index = 2 * (d - 1) + (way < 0)
            line_sends.append(
                (wire.copy(sums_line.at[6 + index], sums_line.at[index],
                           wire.along(way * d)), d, way, there)
            )

            @pl.when(there)
            def _(index=index, d=d, way=way):
                to = place + way * d
                sums_line[6 + index] = sums[2 * to + wire.side] + sums_side[to]
                line_sends[-1][0].start()

            @pl.when((place - way * d < 0) | (place - way * d > 3))
            def _(index=index):
                sums_line[index] = jnp.zeros(sums_line.shape[1:], F32)

    share.end()
    layer_share.end()
    desk.flush(grad_tokens, layer_out)
    first.finish()
    cores = []
    size = kv_out.shape[0] // 4
    for k in range(4):
        rows_of = pl.ds(pl.multiple_of(wire.blocks[k] * size, size), size)
        if k:
            device = {"mp": wire.blocks[k]}
            cores.append(wire.send(kv_out.at[rows_of], kv_got.at[k], device))
        else:
            kv_got[0] = kv_out[rows_of]
    qup.finish()
    desk.flush(grad_qup)
    out.finish()
    desk.flush(grad_out)
    total = sums[2 * place + wire.side] + sums_side[place]
    for made, d, way, there in line_sends:
        pl.when((place - way * d >= 0) & (place - way * d <= 3))(made.wait_recv)
    for index in range(6):
        total = total + sums_line[index]
    gains[...] = total
    for made in cores:
        made.wait_recv()
    columns = kv_out.shape[1]
    for k in range(4):
        at = pl.ds(pl.multiple_of(wire.blocks[k] * columns, columns), columns)
        grad_kv[:, at] = kv_got[k]
    for made in (side_first, *cores):
        made.wait_send()
    for made, d, way, there in line_sends:
        pl.when(there)(made.wait_send)
    row_sum.end()
    for chain in (out, qup, first):
        chain.settle()


def attend_one(
    scale, mp_blocks, c, gain, q_up, cos, sin, kv, key_ids, row_ids, row_starts, out_proj,
    qn, q, o, lse, send, keep, chat_out, inverse_out,
):
    rows = qn.shape[0]
    half, quarter = rows // 2, rows // 4
    part = c.shape[2]
    wide = q.shape[2]
    cut = lambda k, i: c[k, i * quarter : (i + 1) * quarter, :]
    pieces = [jnp.concatenate([cut(k, i ^ k) for i in range(4)], 0) for k in range(4)]
    latent = jnp.concatenate(pieces, 1).astype(F32)
    inverse = inverse_rms(latent)
    chat = latent * inverse
    inverse_out[...] = inverse[:quarter]
    for k in range(4):
        columns = pl.ds(pl.multiple_of(mp_blocks[k] * part, part), part)
        chat_out[:, columns] = chat[:quarter, k * part : (k + 1) * part]
        qn[:, columns] = (chat[:, k * part : (k + 1) * part] * gain[:, columns]).astype(LOW)
    bias = jnp.where((key_ids >= row_starts) & (key_ids <= row_ids), 0.0, NEG_LARGE)
    low = qn[...]
    for h in range(q.shape[0]):
        pre = dot(low, q_up[:, h * wide : (h + 1) * wide])
        q_h = (rotate(pre, cos, sin) * scale).astype(LOW)
        q[h] = q_h
        scores = inner_cols(q_h, kv[:, :wide]) + bias
        top = jnp.max(scores, axis=-1, keepdims=True)
        probs = jnp.exp(scores - top)
        total = jnp.sum(probs, axis=-1, keepdims=True)
        out = dot(probs.astype(LOW), kv[:, wide:]) / total
        o[:, h * wide : (h + 1) * wide] = out.astype(LOW)
        log_total = jnp.broadcast_to(top + jnp.log(total), (rows, 128))
        lse[h : h + 1, :] = jnp.transpose(log_total)[:1]
    keep[...] = dot(o[:half, :], out_proj[...])
    send[...] = dot(o[half:, :], out_proj[...]).astype(LOW)


def fore1_body(scale, desk, *refs):
    refs = list(refs)
    take = lambda n: [refs.pop(0) for _ in range(n)]
    tokens, cotangent, q_down, kv_proj, q_up, out_proj, w_down = take(7)
    lengths, gain1, gain_c, gain2, cosine, sine = take(6)
    h1_mine, h1_theirs, qn_mine, qn_theirs = (take(2) for _ in range(4))
    qs, os, lses, kvs, dz_got = (take(2) for _ in range(5))
    dhid, chat, inv_c, y_out, n2_out, inv2_out, n1_out, inv1_out, h2 = take(9)
    dz, x, down_w, kv_w, up_w, out_w, back_w, h1, c, qn, dz_theirs = take(11)
    send, kept, got, cross_out, cross_got = take(5)
    loads = take(1)[0]
    wire = Wire(*take(2))
    place, blocks = wire.place, wire.blocks
    rows = x.shape[1]
    half, quarter = rows // 2, rows // 4
    wide = kv_proj.shape[1] // 2

    started = []

    def load(source, target):
        made = pltpu.make_async_copy(source, target, loads.at[len(started)])
        made.start()
        started.append(made)
        return made

    def load_rows(source, target):
        return [
            load(source.at[pl.ds(pl.multiple_of(blocks[k] * quarter, quarter), quarter), :],
                 target.at[k * quarter : (k + 1) * quarter, :])
            for k in range(4)
        ]

    in_x = [load_rows(tokens.at[0], x.at[0])]
    in_kv = load(kv_proj, kv_w)
    in_x.append(load_rows(tokens.at[1], x.at[1]))
    in_down = load(q_down, down_w)
    in_dz = [load_rows(cotangent.at[m], dz.at[m]) for m in range(2)]
    in_back, in_up, in_out = load(w_down, back_w), load(q_up, up_w), load(out_proj, out_w)

    line_kv, side_kv, cross_kv, core_kv, cross_c, core_c = [], [], [], [], [], []
    for m in range(2):
        for d in range(1, 4):

            @pl.when(place < d)
            def _(m=m, d=d):
                kvs[m][0, :, d] = jnp.zeros(kvs[m].shape[1:2] + kvs[m].shape[3:], LOW)
                kvs[m][1, :, d] = jnp.zeros(kvs[m].shape[1:2] + kvs[m].shape[3:], LOW)

        own = kvs[m].at[0, 0, 0]
        near, there = slice(0, quarter), slice(quarter, half)
        line_kv.append([
            wire.copy(own.at[near], kvs[m].at[0, 0, d, near], wire.along(d))
            for d in range(1, 4)
        ])
        side_kv.append([wire.copy(own, kvs[m].at[0, 1, 0], wire.beside)] + [
            wire.copy(kvs[m].at[0, 0, d, near], kvs[m].at[0, 1, d, near], wire.beside)
            for d in range(1, 4)
        ])
        cross_kv.append([None] + [
            wire.copy(kvs[m].at[0, :, d, near], kvs[m].at[0, :, d, there], wire.cross)
            for d in range(1, 4)
        ])
        core_kv.append([
            wire.copy(kvs[m].at[0, :, d], kvs[m].at[1, :, d], wire.core) for d in range(4)
        ])
        cross_c.append(wire.copy(c.at[m, 0], c.at[m, 1], wire.cross))
        core_c.append([
            wire.copy(c.at[m, 0], c.at[m, 2], wire.core),
            wire.copy(c.at[m, 1], c.at[m, 3], wire.core),
        ])
    wire.greet(4, 3)

    for m in range(2):
        cos, sin = cosine[m], sine[m]
        for made in in_x[m]:
            made.wait()
        if m == 0:
            in_kv.wait()
        values = x[m].astype(F32)
        inverse = inverse_rms(values)
        normed = values * inverse
        n1_out[m], inv1_out[m] = normed[:quarter], inverse[:quarter]
        low = (normed * gain1[...]).astype(LOW)
        h1[...] = low
        pair = dot(low[:half], kv_w[...])
        own = kvs[m].at[0, 0, 0]
        own[:, :wide] = rotate(pair[:, :wide], cos[:half], sin[:half]).astype(LOW)
        own[:, wide:] = pair[:, wide:].astype(LOW)
        for d in (3, 2, 1):
            pl.when(place + d <= 3)(line_kv[m][d - 1].start)
        side_kv[m][0].start()
        if m == 0:
            in_down.wait()
        c[m, 0] = dot(low, down_w[...]).astype(LOW)
        cross_c[m].start()
        core_c[m][0].start()
        side_columns(h1, h1_mine[m], h1_theirs[m], wire.side)
        desk.flush(h1_mine[m], h1_theirs[m])

    def pass_kv(m, d):
        @pl.when(place >= d)
        def _():
            line_kv[m][d - 1].wait_recv()
            side_kv[m][d].start()

    def pass_cross(m, d):
        @pl.when(place >= d)
        def _():
            side_kv[m][d].wait_recv()
            cross_kv[m][d].start()

    def pass_core(m, d):
        @pl.when(place >= d)
        def _():
            (cross_kv if d else side_kv)[m][d].wait_recv()
            core_kv[m][d].start()

    in_back.wait()
    for m in range(2):
        for made in in_dz[m]:
            made.wait()
    dhid[0] = inner_cols(dz[0], back_w[...])
    for d in (1, 2, 3):
        pass_kv(0, d)
    for m in range(2):
        cross_c[m].wait_recv()
        core_c[m][1].start()
    for d in (1, 2, 3):
        pass_cross(0, d)
    dhid[1] = inner_cols(dz[1], back_w[...])
    for d in (1, 2, 3):
        pass_kv(1, d)
    for m in range(2):
        for z in range(4):
            block = dz_theirs.shape[3]
            columns = pl.ds(pl.multiple_of((2 * z + 1 - wire.side) * block, block), block)
            dz_theirs[m, z] = dz[m, :half, columns]
    desk.flush(dhid, n1_out)
    for d in range(4):
        pass_core(0, d)
    for d in (1, 2, 3):
        pass_cross(1, d)
    in_up.wait()
    in_out.wait()
    sums = [
        RowSum(wire, send.at[m : m + 1], kept.at[m : m + 1], got.at[m : m + 1],
               cross_out.at[m : m + 1], cross_got.at[m : m + 1], quarter, 2)
        for m in range(2)
    ]
    shares = []

    def after_sum(m):
        for part, span in enumerate(sums[m].spans):
            value = x[m, span, :].astype(F32) + sums[m].result(part)[0]
            inverse = inverse_rms(value)
            normed = value * inverse
            y_out[m, span, :], n2_out[m, span, :], inv2_out[m, span, :] = value, normed, inverse
            h2[m, span, :] = (normed * gain2[...]).astype(LOW)
            spot = lambda k: h2.at[m, k * quarter + span.start : k * quarter + span.stop, :]
            shares.append((
                wire.send(spot(0), spot(1), wire.cross), wire.send(spot(0), spot(2), wire.core),
                wire.copy(spot(1), spot(3), wire.core),
            ))

    for m in range(2):
        if m == 1:
            for d in range(4):
                pass_core(1, d)
        for d in range(4):
            pl.when(place >= d)(core_kv[m][d].wait_recv)
        for made in core_c[m]:
            made.wait_recv()
        desk.flush(kvs[m])
        rows_at = row_places(wire, quarter, 0)
        attend_one(
            scale, blocks, c.at[m], gain_c, up_w, cosine[m], sine[m],
            kvs[m][...].reshape(2 * 2 * 4 * half, 2 * wide),
            key_places(wire, quarter, 4, 1, (0, 1)), rows_at,
            sequence_starts(lengths, m, rows_at), out_w, qn, qs[m], os[m], lses[m], send.at[m], kept.at[m],
            chat.at[m], inv_c.at[m],
        )
        sums[m].core.start()
        if m == 0:
            side_dz = wire.send(dz_theirs, dz_got[0], wire.beside)
        side_columns(qn, qn_mine[m], qn_theirs[m], wire.side)
        desk.flush(qs[m], os[m], qn_mine[m], qn_theirs[m])
        if m == 1:
            after_sum(0)
        sums[m].pass_on()
    after_sum(1)
    desk.flush(chat, y_out, n2_out)
    side_dz.wait_recv()
    core_dz = wire.send(dz_got[0], dz_got[1], wire.core)
    for near, _, far in shares:
        near.wait_recv()
        far.start()
    for _, first, far in shares:
        first.wait_recv()
        far.wait_recv()
    core_dz.wait_recv()
    for made in [side_dz, core_dz, *cross_c, *(a for p in core_c for a in p),
                 *(a for p in shares for a in p)]:
        made.wait_send()
    for m in range(2):
        sums[m].end()
        for d in range(4):

            @pl.when(place >= d)
            def _(m=m, d=d):
                side_kv[m][d].wait_send()
                if d:
                    cross_kv[m][d].wait_send()
                core_kv[m][d].wait_send()

        for d in range(1, 4):
            pl.when(place + d <= 3)(line_kv[m][d - 1].wait_send)


def deliver_body(count, pieces, *refs):
    results, gains = refs[:count], refs[count]
    outs, rooms, sems = refs[count + 1 : -count - 1], refs[-count - 1 : -1], refs[-1]
    loads, stores = [], []
    for source, room, target in zip(results, rooms, outs):
        size = source.shape[-2] // pieces
        for i in range(pieces):
            cut = (slice(None),) * (len(source.shape) - 2) + (slice(i * size, (i + 1) * size),)
            at = len(loads)
            loads.append(pltpu.make_async_copy(source.at[cut], room.at[cut], sems.at[2 * at]))
            stores.append(pltpu.make_async_copy(room.at[cut], target.at[cut], sems.at[2 * at + 1]))
    for made in loads:
        made.start()
    at = 0
    for ref in outs[count:]:
        ref[...] = gains[0, at : at + ref.shape[0]]
        at += ref.shape[0]
    for load, store in zip(loads, stores):
        load.wait()
        store.start()
    for made in stores:
        made.wait()


def local(
    tokens,
    lengths,
    norm1_gain,
    q_down,
    latent_gain,
    q_up,
    kv_proj,
    out_proj,
    norm2_gain,
    w_gate,
    w_up,
    w_down,
    cotangent,
):
    micro, rows, width = tokens.shape
    seq = lax.axis_size("seq")
    line = seq // 2
    at = lax.axis_index("seq").astype(jnp.int32)
    me = lax.axis_index("mp").astype(jnp.int32)
    place, side = at // 2, at % 2
    ids = jnp.stack([me, side])
    quarter, half = rows // 4, rows // 2
    head_dim = kv_proj.shape[1] // 2
    heads = q_up.shape[1] // head_dim
    part = q_down.shape[1]
    rank = q_up.shape[0]
    hidden = w_gate.shape[1]
    kv_part = kv_proj.shape[1] // 4
    wide = width // seq
    scale = head_dim ** (-0.5)
    key_count = seq * rows
    beside = [(i, i ^ 1) for i in range(seq)]
    narrow = line == 4 and micro == 2 and key_count <= 2048 and not wide % 128

    def swap(index):
        return ((index & 1) << 1) | (index >> 1)

    def to_natural(array, axis):
        size = array.shape[axis] // 4
        return jnp.concatenate(
            [lax.dynamic_slice_in_dim(array, swap(me ^ b) * size, size, axis) for b in range(4)],
            axis,
        )

    def other(array):
        return lax.ppermute(array, "seq", beside)

    def sum_mp(send, keep):
        kept = keep + lax.ppermute(send, "mp", CORE).astype(F32)
        got = lax.ppermute(kept[..., quarter:, :].astype(LOW), "mp", CROSS)
        return kept[..., :quarter, :] + got.astype(F32)

    def gather_mp(piece):
        near = lax.ppermute(piece, "mp", CROSS)
        pair = jnp.concatenate([piece, near], -2)
        return piece, near, lax.ppermute(pair, "mp", CORE)

    def sides_shape(columns, their_rows, lead=()):
        if columns // seq % 128:
            return []
        return [
            whole((*lead, line, n, columns // seq), LOW) for n in (rows, their_rows)
        ]

    def split_sides(made, full, their_rows):
        if made:
            return made
        split = full.reshape(*full.shape[:-1], line, 2, full.shape[-1] // seq)
        mine, theirs = (
            jnp.moveaxis(lax.dynamic_index_in_dim(split, i, split.ndim - 2, keepdims=False), -2, -3)
            for i in (side, 1 - side)
        )
        return mine, theirs[..., :their_rows, :]

    def from_other(theirs):
        got = other(theirs)
        return got, lax.ppermute(got, "mp", CORE)

    def without_sides(body, count):
        return body if count else lambda *refs: body(*refs, None, None)

    def both_sides(mine, got):
        lefts, spans = [], []
        for array, first, count, partner in (
            (mine, 0, rows, 0), (got[0], 0, half, 1), (got[1], half, half, 1)
        ):
            stacked_array = not isinstance(array, list)
            for m in range(micro):
                spans.append((len(lefts) if not stacked_array else len(lefts), m if stacked_array else None,
                              m, partner, first, count))
                if not stacked_array:
                    lefts.append(array[m])
            if stacked_array:
                lefts.append(array)
        return lefts, spans

    class Chain:
        def __init__(self, lefts, rights, terms, shape, turned=False, from_side=None):
            self.args = [*lefts, *rights]
            self.spec = (terms, len(lefts), len(rights))
            self.shape, self.turned = shape, turned
            self.from_side = [] if from_side is None else [from_side]
            self.step, self.up, self.down = 0, None, None

        def block(self, index, added, after, last=False):
            turned = last and self.turned
            body = functools.partial(
                block_body, *self.spec, len(added), len(self.from_side), turned
            )
            shape = self.shape[::-1] if turned else self.shape
            return run(
                body, index.reshape(1), [*self.args, *added, *self.from_side],
                [whole(shape, F32 if last else LOW)], after, name="block",
            )[0]

        def advance(self, after):
            self.step += 1
            step = self.step
            goes_up = [(i, i + 2) for i in range(2 * step)]
            goes_down = [(seq - 1 - i, seq - 3 - i) for i in range(2 * step)]
            for_up, for_down = line - step + place, step - line + place
            if 2 * step < line + 1:
                which = jnp.where(
                    place <= step - 1, for_up, jnp.where(place >= line - step, for_down, 0)
                )
                term = self.block(which, [a for a in (self.up, self.down) if a is not None], after)
                if step == 1 and line > 3:
                    self.up = lax.ppermute(term, "seq", goes_up + goes_down)
                else:
                    self.up = lax.ppermute(term, "seq", goes_up)
                    self.down = lax.ppermute(term, "seq", goes_down)
                return [term]
            term_up = self.block(jnp.clip(for_up, 0, line - 1), [self.up], after)
            term_down = self.block(jnp.clip(for_down, 0, line - 1), [self.down], [term_up])
            self.up = lax.ppermute(term_up, "seq", goes_up)
            self.down = lax.ppermute(term_down, "seq", goes_down)
            return [term_down]

        def finish(self, after):
            while self.step < line - 1:
                after = self.advance(after)
            result = self.block(place, [self.up, self.down], after, last=True)
            return result, [result]

    quarter_rows = jnp.arange(quarter, dtype=jnp.int32)
    row_ids = at * rows + jnp.concatenate([(me ^ k) * quarter + quarter_rows for k in ORDER])
    key_ids = (
        ((place - jnp.arange(line, dtype=jnp.int32)[None, None, :, None, None]) * 2
         + (side ^ jnp.arange(2, dtype=jnp.int32)[None, :, None, None, None])) * rows
        + (me ^ (jnp.arange(2, dtype=jnp.int32)[:, None, None, None, None]
                 + 2 * jnp.arange(2, dtype=jnp.int32)[None, None, None, :, None])) * quarter
        + quarter_rows[None, None, None, None, :]
    ).reshape(key_count)

    gain1_row, gain2_row, gain_c_row = norm1_gain[None, :], norm2_gain[None, :], latent_gain[None, :]
    kv_cols = lax.dynamic_slice_in_dim(kv_proj, me * kv_part, kv_part, 1)
    first_weights = jnp.concatenate([q_down, kv_cols], axis=1)
    low = lambda *shape: pltpu.VMEM(shape, LOW)
    full = lambda *shape: pltpu.VMEM(shape, F32)
    near = lambda *arrays: [(1, a) for a in arrays]
    far = lambda *arrays: [(0, a) for a in arrays]
    columns = heads * head_dim
    side_rows = rank // seq
    first_columns = part + kv_part

    def narrow_layer():
        numbers = lambda array: [(2, array)]
        late = lambda *arrays: [(3, a) for a in arrays]
        later = lambda *arrays: [(4, a) for a in arrays]
        first_end = lengths[:, 0:1]
        second_end = first_end + lengths[:, 1:2]
        places = row_ids[None, :] - jnp.where(
            row_ids >= second_end, second_end, jnp.where(row_ids >= first_end, first_end, 0)
        )
        freqs = BASE ** (-2.0 * jnp.arange(head_dim // 2, dtype=F32) / head_dim)
        angles = places.astype(F32)[:, :, None] * freqs
        cosine, sine = jnp.cos(angles), jnp.sin(angles)
        row_shape = whole((micro, quarter, width), F32)
        one_shape = whole((micro, quarter, 1), F32)
        side_shape = whole((micro, line, half, wide), LOW)
        args = far(tokens, cotangent, q_down, kv_proj, q_up, out_proj, w_down)
        args += numbers(lengths) + near(gain1_row, gain_c_row, gain2_row, cosine, sine)
        outs = late(*[whole((line, rows, wide), LOW)] * 4, *[whole((line, rows, side_rows), LOW)] * 4)
        outs += late(*[whole((heads, rows, head_dim), LOW)] * 2, *[whole((rows, columns), LOW)] * 2)
        outs += near(*[whole((heads, rows), F32)] * 2)
        outs += late(*[whole((2, 2, line, half, 2 * head_dim), LOW)] * 2)
        outs += far(*[side_shape] * 2)
        outs += late(
            whole((micro, rows, hidden), F32), whole((micro, quarter, rank), F32))
        outs += near(one_shape) + late(row_shape, row_shape) + near(one_shape) + late(row_shape)
        outs += near(one_shape) + late(whole((micro, rows, width), LOW))
        made = list(mesh_run(
            functools.partial(fore1_body, scale), args, outs,
            [low(micro, rows, width), low(micro, rows, width), low(width, part),
             low(width, 2 * head_dim),
             low(rank, columns), low(columns, width), low(hidden, width), low(rows, width),
             low(micro, 4, rows, part), low(rows, rank), low(micro, line, half, wide),
             low(micro, half, width), full(micro, half, width), low(micro, half, width),
             low(micro, quarter, width), low(micro, quarter, width),
             pltpu.SemaphoreType.DMA((24,))],
            4, "fore1", 60, 84,
        ))
        give = lambda n: [made.pop(0) for _ in range(n)]
        h1_mine, h1_theirs, qn_mine, qn_theirs = (give(2) for _ in range(4))
        qs, os, lses, kv, dz_got = (give(2) for _ in range(5))
        kv = [a.reshape(key_count, 2 * head_dim) for a in kv]
        dhid, chat, inv_c, y, n2, inv2, n1, inv1, h2 = give(9)

        ahead = hidden * 3 // 11 // 128 * 128
        args = far(w_gate, w_up, w_down, cotangent) + late(h2) + later(dhid, n2)
        args += near(inv2, gain2_row) + later(*dz_got, y)
        outs = near(whole((hidden, wide), F32)) + late(row_shape) + near(whole((1, width), F32))
        outs += late(whole((micro, rows, width), LOW), whole((micro, line, rows, wide), LOW), side_shape)
        outs += near(whole((micro, quarter, width), LOW))
        outs += late(*[whole((rows, hidden), LOW)] * 6, *[whole((line, rows, wide), LOW)] * 2)
        outs += far(*[whole((line, half, wide), LOW)] * 4, *[whole((rows, hidden), LOW)] * 2)
        made = list(mesh_run(
            functools.partial(back1_body, quarter), args, outs,
            [low(width, hidden), low(width, hidden), low(rows, hidden - ahead),
             low(rows, hidden - ahead), low(micro, line, half, wide),
             low(5, wide, hidden - ahead), low(2, wide, hidden - ahead),
             low(micro, half, width), full(micro, half, width), low(micro, half, width),
             low(micro, quarter, width), low(micro, quarter, width),
             pltpu.SemaphoreType.DMA((6,)), low(micro, half, width), low(micro, half, width),
             low(micro, half, width), low(micro, quarter, width), low(micro, quarter, width),
             low(5, 2 * wide, ahead), low(2, 2 * wide, ahead), full(2, wide, ahead),
             low(wide, ahead), low(wide, ahead), low(micro, rows, width),
             pltpu.SemaphoreType.DMA((8,))],
            1, "back1", 62, 40,
        ))
        grad_down, dy, gain2, dyl, dyl_mine, dyl_theirs, layer_own = give(7)
        hid, dg, du, h2_mine, h2_got, h2_far, dg_other = (give(2) for _ in range(7))

        args = numbers(lengths) + late(*dg, *dg_other, *du, *h2_mine, *h2_got, *h2_far)
        args += late(dyl, out_proj, q_up, *qs, *kv, *os) + near(*lses)
        args += late(cosine, sine, chat) + near(inv_c, gain_c_row) + far(dyl_theirs)
        args += late(*qn_theirs) + far(*os)
        outs = late(whole((wide, hidden), F32), whole((wide, hidden), F32))
        outs += near(whole((micro, rows, first_columns), LOW), whole((1, rank), F32))
        outs += late(whole((micro, rows, columns), LOW))
        outs += far(side_shape, side_shape, whole((line, side_rows, columns), LOW),
                    *[whole((rows, columns), LOW)] * 2)
        kv_low = lambda *lead: low(*lead, quarter, 2 * head_dim)
        key_half = key_count // 2
        (grad_gate, grad_up, dfirst, gain_c, dqp, dyl_got, dyl_far, qup_side,
         *o_other) = mesh_run(
            functools.partial(back2_body, quarter, scale), args, outs,
            [low(rows, hidden), low(rows, hidden), low(5, wide, hidden), low(2, wide, hidden),
             low(5, wide, hidden), low(2, wide, hidden), full(heads * rows, head_dim),
             low(micro, half, rank),
             full(micro, half, rank), low(micro, key_half, 2 * head_dim),
             low(micro, key_half, 2 * head_dim), low(micro, half, rank),
             low(micro, quarter, rank), low(micro, quarter, rank),
             low(micro, key_half, 2 * head_dim), kv_low(micro, 2 * line), kv_low(micro, 2 * line),
             kv_low(micro, line), kv_low(micro, line), kv_low(micro, 3), kv_low(micro, 3),
             full(micro, quarter, 2 * head_dim), low(micro, rows, rank + 2 * head_dim),
             low(line, side_rows, columns)],
            2, "back2", 62, 44,
        )

        args = later(dfirst) + far(q_down, kv_proj) + later(*h1_mine, *h1_theirs)
        args += late(*os, *o_other, dyl_mine, dyl_got, dyl_far)
        args += later(*qn_mine, dqp, qup_side, n1)
        args += near(inv1) + later(dy) + near(gain1_row, gain2, gain_c, layer_own)
        block = width // 4 // seq
        gain_columns = 2 * wide + side_rows
        outs = late(whole((columns, wide), F32), whole((side_rows, columns), F32))
        outs += near(whole((wide, part), F32), whole((block, 2 * head_dim), F32))
        outs += late(whole((micro, rows, width), LOW)) + near(whole((1, gain_columns), F32))
        outs += late(whole((micro, rows, width), LOW))
        grad_out, grad_qup, grad_qdown, grad_kv, input_grads, gains, layer_out = mesh_run(
            functools.partial(back3_body, quarter), args, outs,
            [low(5, wide, columns), low(2, wide, columns), low(5, side_rows, columns),
             low(2, side_rows, columns), low(5, wide, first_columns),
             low(2, wide, first_columns), low(line, wide, first_columns),
             low(line, wide, first_columns), low(micro, half, width), full(micro, half, width),
             low(micro, half, width), low(micro, quarter, width), low(micro, quarter, width),
             full(wide, kv_part), full(4, block, kv_part), full(seq, 1, gain_columns),
             full(seq, 1, gain_columns), full(seq, 1, gain_columns), full(line, 1, gain_columns),
             full(12, 1, gain_columns), low(width, first_columns), pltpu.SemaphoreType.DMA((2,))],
            3, "back3", 60, 44,
        )
        results = [layer_out, input_grads, grad_qdown, grad_qup, grad_kv, grad_out, grad_gate,
                   grad_up, grad_down]
        made = pl.pallas_call(
            functools.partial(deliver_body, len(results), 4),
            in_specs=[pl.BlockSpec(memory_space=pl.ANY)] * len(results) + [in_vmem()],
            out_specs=[pl.BlockSpec(memory_space=pl.ANY)] * len(results) + [in_vmem()] * 3,
            out_shape=[whole(a.shape, a.dtype) for a in results]
            + [whole((n,), F32) for n in (wide, wide, side_rows)],
            scratch_shapes=[pltpu.VMEM(a.shape, a.dtype) for a in results]
            + [pltpu.SemaphoreType.DMA((8 * len(results),))],
            compiler_params=pltpu.CompilerParams(vmem_limit_bytes=60 << 20),
            name="deliver",
        )(*results, gains)
        (layer_out, input_grads, grad_qdown, grad_qup, grad_kv, grad_out, grad_gate, grad_up,
         grad_down, grad_n1, grad_n2, grad_c) = made
        return (
            layer_out, input_grads, grad_n1, grad_qdown, grad_c, grad_qup, grad_kv, grad_out,
            grad_n2, grad_gate, grad_up, grad_down,
        )

    if narrow:
        return narrow_layer()

    both_rows = sides_shape(width, rows)
    half_rows = sides_shape(width, half)
    rank_sides = sides_shape(rank, rows)

    tables, starts, kv, c_part, h1_sides = [], [], [], [], []
    order = []
    for m in range(micro):
        _, places = documents(lengths[m], row_ids)
        starts.append(row_ids - places)
        tables.append(rotation(places, head_dim))
        c, packed, h1, *made = run(
            without_sides(functools.partial(first_body, m, quarter), len(both_rows)),
            ids,
            [tokens, gain1_row, q_down, kv_proj, *tables[m]],
            [whole((rows, part), LOW), whole((half, 2 * head_dim), LOW), whole((rows, width), LOW),
             *both_rows],
            order,
            name="first",
        )
        order = [c]
        blocks = [packed] + [
            lax.ppermute(packed, "seq", [(i, i + 2 * d) for i in range(seq - 2 * d)])
            for d in range(1, line)
        ]
        near = jnp.stack(blocks, 0)
        near = jnp.stack([near, other(near)], 0)
        kv.append(
            jnp.stack([near, lax.ppermute(near, "mp", CORE)], 0).reshape(key_count, 2 * head_dim)
        )
        c_part.append(c)
        h1_sides.append(split_sides(made, h1, rows))

    dhid, dz, *made = run(
        functools.partial(cotangent_body, micro, quarter),
        ids,
        [cotangent, w_down],
        [whole((micro, rows, hidden), F32), whole((micro, rows, width), LOW),
         *sides_shape(width, half, (micro,))],
        order,
        name="cotangent",
    )
    order = [dz]
    dz_mine, dz_theirs = split_sides(made, dz, half)
    dz_got = from_other(dz_theirs)

    qn_sides, qs, os, lses, sums, c_rows = [], [], [], [], [], []
    for m in range(micro):
        near = lax.ppermute(c_part[m], "mp", CROSS)
        swapped = jnp.concatenate(
            [near[quarter : 2 * quarter], near[:quarter], near[3 * quarter :],
             near[2 * quarter : 3 * quarter]], 0
        )
        far = lax.ppermute(jnp.concatenate([c_part[m], swapped], 1), "mp", CORE)
        qn, q, o, lse, send, keep, *made = run(
            without_sides(functools.partial(attend_body, scale), len(rank_sides)),
            ids,
            [c_part[m], near, far, gain_c_row, q_up, *tables[m], kv[m], key_ids[None, :],
             row_ids[:, None], starts[m][:, None], out_proj],
            [whole((rows, rank), LOW), whole((heads, rows, head_dim), LOW),
             whole((rows, heads * head_dim), LOW), whole((heads, rows), F32),
             whole((half, width), LOW), whole((half, width), F32), *rank_sides],
            order,
            name="attend",
        )
        order = [o]
        qn_sides.append(split_sides(made, qn, rows))
        qs.append(q)
        os.append(o)
        lses.append(lse)
        sums.append(sum_mp(send, keep))
        c_rows.append(
            jnp.concatenate([c_part[m][:quarter], swapped[:quarter], far[half : half + quarter]], 1)
        )

    h2_mine, h2_theirs, hid, dg, du, state = [], [], [], [], [], []
    for m in range(micro):
        x = lax.dynamic_slice_in_dim(tokens[m], me * quarter, quarter, 0).astype(F32)
        inv1 = inverse_rms(x)
        y = x + sums[m]
        inv2 = inverse_rms(y)
        n2 = y * inv2
        pieces = gather_mp((n2 * gain2_row).astype(LOW))
        h2, hid_m, dg_m, du_m, *made = run(
            without_sides(functools.partial(forward_body, m), len(half_rows)),
            ids,
            [*pieces, w_gate, w_up, dhid],
            [whole((rows, width), LOW), *[whole((rows, hidden), LOW)] * 3, *half_rows],
            order,
            name="forward",
        )
        order = [hid_m]
        mine, theirs = split_sides(made, h2, half)
        h2_mine.append(mine)
        h2_theirs.append(theirs)
        hid.append(hid_m)
        dg.append(dg_m)
        du.append(du_m)
        state.append(dict(x=x, n1=x * inv1, inv1=inv1, y=y, n2=n2, inv2=inv2, c=c_rows[m]))

    def stacked(name):
        return jnp.stack([st[name] for st in state], 0)

    def with_other(arrays):
        return [*arrays, *[other(a) for a in arrays]]

    def terms_of(spans):
        return [(a, lead, m + micro * partner, None, first, count)
                for a, lead, m, partner, first, count in spans]

    send, keep, ffn_send, ffn_keep = run(
        functools.partial(hidden_back_body, micro),
        ids,
        [*dg, *du, *hid, w_gate, w_up, w_down],
        [whole((micro, half, width), LOW), whole((micro, half, width), F32)] * 2,
        order,
        name="hidden_back",
    )
    lefts, spans = both_sides(dz_mine, dz_got)
    chain_down = Chain(lefts, with_other(hid), terms_of(spans), (wide, hidden), turned=True)
    lefts, spans = both_sides(h2_mine, [list(p) for p in zip(*[from_other(t) for t in h2_theirs])])
    chain_gate = Chain(lefts, with_other(dg), terms_of(spans), (wide, hidden))
    chain_up = Chain(lefts, with_other(du), terms_of(spans), (wide, hidden))

    order = chain_down.advance([send])
    dh2 = sum_mp(send, keep)
    y, n2, inv2, n1, inv1 = (stacked(k) for k in ("y", "n2", "inv2", "n1", "inv1"))
    dz_own = dz[:, :quarter].astype(F32)
    gain2 = jnp.sum(dh2 * n2, axis=(0, 1))
    dy = dz_own + norm_backward(dh2 * gain2_row, n2, inv2)
    for _ in range(2):
        order = chain_down.advance(order)
    order = chain_gate.advance(order)

    def attend_back(which, pieces):
        args = [*pieces, out_proj, q_up, key_ids[:, None]]
        for m in which:
            args += [qs[m], kv[m], os[m], lses[m], jnp.stack([row_ids, starts[m]], 0), *tables[m]]
        n = len(which)
        return run(
            functools.partial(attend_back_body, scale, n, min(1024, key_count // 2)),
            ids,
            args,
            [whole((n, rows, width), LOW), whole((n, rows, heads * head_dim), LOW),
             whole((n, half, rank), LOW), whole((n, half, rank), F32),
             whole((n, key_count // 2, 2 * head_dim), LOW),
             whole((n, key_count // 2, 2 * head_dim), F32), *sides_shape(width, half, (n,))],
            order,
            scratch=[pltpu.VMEM((heads, rows, head_dim), F32),
                     pltpu.VMEM((heads, rows, head_dim), LOW),
                     pltpu.VMEM((heads, 8, rows), F32)],
            name="attend_back",
            limit=56,
        )

    pieces = gather_mp(dy.astype(LOW))
    if key_count <= 2048:
        made = attend_back(range(micro), pieces)
    else:
        each = [attend_back([m], [p[m : m + 1] for p in pieces]) for m in range(micro)]
        made = [jnp.concatenate(parts, 0) for parts in zip(*each)]
    dyl, dqp, send, keep, kv_send, kv_keep, *made = made
    order = [send]
    dyl_mine, dyl_theirs = split_sides(made, dyl, half)
    lefts, spans = both_sides(dyl_mine, from_other(dyl_theirs))
    chain_out = Chain(lefts, with_other(os), terms_of(spans), (wide, heads * head_dim), turned=True)

    def side_sum(lefts, rights, shape, after):
        terms = [(m, None, 0, m, 0, rows) for m in range(micro)]
        (made,) = run(
            functools.partial(side_sum_body, terms, len(lefts)),
            ids,
            [*lefts, *rights],
            [whole((line, *shape), LOW)],
            after,
            name="side_sum",
        )
        return other(made), [made]

    def own_chain(side_pairs, right, shape, after):
        from_side, after = side_sum([p[1] for p in side_pairs], [right], shape, after)
        terms = [(m, None, 0, m, 0, rows) for m in range(micro)]
        return Chain([p[0] for p in side_pairs], [right], terms, shape, from_side=from_side), after

    shape = (rank // seq, heads * head_dim)
    chain_qup, order = own_chain(qn_sides, dqp, shape, order)
    order = chain_gate.advance(order)
    order = chain_up.advance(order)

    dqn = sum_mp(send, keep)
    c = stacked("c").astype(F32)
    inv_c = inverse_rms(c)
    chat = c * inv_c
    chat = to_natural(chat, 2)
    gain_c = jnp.sum(dqn * chat, axis=(0, 1))
    dc = norm_backward(dqn * gain_c_row, chat, inv_c).astype(LOW)

    dkv = kv_keep + lax.ppermute(kv_send, "mp", CORE).astype(F32)
    dkv = dkv.reshape(micro, 2, line, 2, quarter, 2 * head_dim)
    dkv = dkv[:, :, :, 0] + lax.ppermute(dkv[:, :, :, 1].astype(LOW), "mp", CROSS).astype(F32)
    dkv = dkv[:, 0] + other(dkv[:, 1].astype(LOW)).astype(F32)
    total = dkv[:, 0]
    for d in range(1, line):
        total = total + lax.ppermute(
            dkv[:, d].astype(LOW), "seq", [(i + 2 * d, i) for i in range(seq - 2 * d)]
        ).astype(F32)
    cosine = jnp.stack([t[0][:quarter] for t in tables], 0)
    sine = jnp.stack([t[1][:quarter] for t in tables], 0)
    dkv_low = jnp.concatenate(
        [unrotate(total[..., :head_dim], cosine, sine), total[..., head_dim:]], axis=-1
    ).astype(LOW)
    both = jnp.concatenate(gather_mp(jnp.concatenate([dc, dkv_low], -1)), -2)
    dfirst = jnp.concatenate(
        [lax.dynamic_slice_in_dim(both, me * part, part, 2),
         lax.dynamic_slice_in_dim(both, rank + me * kv_part, kv_part, 2)], -1
    )

    grad_down, order = chain_down.finish(order)
    order = chain_gate.advance(order)
    order = chain_up.advance(order)
    order = chain_out.advance(order)
    grad_gate, order = chain_gate.finish(order)
    order = chain_up.advance(order)
    order = chain_out.advance(order)
    grad_up, order = chain_up.finish(order)
    order = chain_qup.advance(order)
    order = chain_out.advance(order)
    chain_first, order = own_chain(h1_sides, dfirst, (wide, part + kv_part), order)
    order = chain_qup.advance(order)
    grad_out, order = chain_out.finish(order)
    order = chain_first.advance(order)
    order = chain_qup.advance(order)
    order = chain_first.advance(order)
    grad_qup, order = chain_qup.finish(order)
    order = chain_first.advance(order)
    grad_first, order = chain_first.finish(order)

    grad_qdown = grad_first[:, :part]
    kv_cols_grad = grad_first[:, part:]
    pieces = []
    for k in ORDER:
        size = kv_cols_grad.shape[0] // 4
        sent = lax.dynamic_slice_in_dim(kv_cols_grad, (me ^ k) * size, size, 0)
        pieces.append(lax.ppermute(sent, "mp", [(i, i ^ k) for i in range(4)]) if k else sent)
    grad_kv = to_natural(jnp.concatenate(pieces, 1), 1)

    def put_natural(pieces):
        return run(
            functools.partial(natural_body, micro, quarter),
            ids,
            pieces,
            [whole((micro, rows, width), LOW)],
            name="natural",
        )[0]

    part_sum = inner_cols(dfirst.reshape(micro * rows, -1), first_weights).reshape(micro, rows, width)
    dh1 = sum_mp(part_sum[:, half:].astype(LOW), part_sum[:, :half])
    gain1 = jnp.sum(dh1 * n1, axis=(0, 1))
    dx = (dy + norm_backward(dh1 * gain1_row, n1, inv1)).astype(LOW)
    input_grads = put_natural(gather_mp(dx))

    ffn = sum_mp(ffn_send, ffn_keep)
    layer_out = put_natural(gather_mp((y + ffn).astype(LOW)))

    gains = jnp.concatenate(
        [gain1.reshape(seq, -1), gain2.reshape(seq, -1), gain_c.reshape(seq, -1)], axis=1
    )
    gains = gains + lax.ppermute(gains, "mp", CORE)
    gains = gains + lax.ppermute(gains, "mp", CROSS)
    gain_sum = lax.dynamic_index_in_dim(gains, at, 0, keepdims=False)
    for k in range(1, seq):
        gain_sum = gain_sum + lax.ppermute(
            lax.dynamic_index_in_dim(gains, at ^ k, 0, keepdims=False),
            "seq",
            [(i, i ^ k) for i in range(seq)],
        )
    return (
        layer_out,
        input_grads,
        gain_sum[:wide],
        grad_qdown,
        gain_sum[2 * wide :],
        grad_qup,
        grad_kv,
        grad_out,
        gain_sum[wide : 2 * wide],
        grad_gate,
        grad_up,
        grad_down,
    )


def solution(mesh):
    placed = (
        P(None, "seq", None),
        P(),
        P(),
        P(None, "mp"),
        P(),
        P(None, "mp"),
        P(),
        P("mp", None),
        P(),
        P(None, "mp"),
        P(None, "mp"),
        P("mp", None),
        P(None, "seq", None),
    )
    return jax.shard_map(
        local,
        mesh=mesh,
        in_specs=placed,
        out_specs=(
            P(None, "seq", None),
            P(None, "seq", None),
            P("seq"),
            P("seq", "mp"),
            P("seq"),
            P("seq", "mp"),
            P(("seq", "mp"), None),
            P("mp", "seq"),
            P("seq"),
            P("seq", "mp"),
            P("seq", "mp"),
            P("mp", "seq"),
        ),
        check_vma=False,
    )
```
